32 devices in a mesh: seq: 8 (over z, y), head: 4 (over x, core).
Axes of the slice: x: 2, y: 2, z: 4, core: 2. Of those that a mesh axis runs over, the one named last changes fastest.
Arguments:
- ids: int32 [16, 256], P('seq'), may hold values from 0 to 32
- pad_mask: int32 [16], P('seq'), may hold values from 0 to 1, as said below
- embed: bfloat16 [33, 768], replicated, may hold values from -16 to 16
- row_qkv: bfloat16 [3, 768, 768], P(None, 'head'), may hold values from -24 to 24
- row_out: bfloat16 [768, 768], P('head'), may hold values from -0.4375 to 0.4375
- col_qkv: bfloat16 [3, 768, 768], P(None, 'head'), may hold values from -24 to 24
- col_out: bfloat16 [768, 768], P('head'), may hold values from -0.21875 to 0.21875
Outputs:
- layer_out: bfloat16 [16, 256, 768], P('seq', None, 'head')
The draws below stay inside these ranges and needn't reach their ends.
Inputs may be any that keep to these rules, and one draw needn't show every extreme that they name: `pad_mask`: sequence 0 is always real.
All inputs are finite; a program needn't handle non-finite values.
Results may differ from the reference program's by a relative error of at most 0.007.
Values may be sent and summed in bfloat16 or wider, within the bound.
No kernel may reach another device: no remote copies, remote signals or barrier semaphores. Data moves between devices by JAX's collectives and lax.ppermute only.
A program may use at most 64 MiB of HBM per device.

```python
import math
import jax
import jax.numpy as jnp
import numpy as np
from jax import lax

D = 768
HEADS = 12
HEAD_DIM = 64
VOCAB = 33
COLS = 256
ROWS = 16


def weight_block(key, query_gain):
    first = jax.random.fold_in(key, 0)
    base = jnp.clip(jax.random.normal(first, (3, D, D), jnp.float32), -4.0, 4.0) * D ** (-0.5)
    key_weight = base[1]
    return jnp.swapaxes(jnp.stack([query_gain * base[0], key_weight, base[2]]), 1, 2)


def draw_row_qkv(key, part):
    key = jax.random.fold_in(key, 21)
    block = weight_block(key, 2.0)
    return block.astype(jnp.bfloat16)


def draw_col_qkv(key, part):
    key = jax.random.fold_in(key, 22)
    block = weight_block(key, 1.0)
    return block.astype(jnp.bfloat16)


def draw_embed(key, part):
    key = jax.random.fold_in(key, 11)
    first, second, third = jax.random.split(key, 3)
    col_scale = jnp.exp(jax.random.uniform(second, (1, D), jnp.float32, 0.0, math.log(10.0)))
    row_scale = jnp.exp(jax.random.uniform(third, (VOCAB, 1), jnp.float32, 0.0, math.log(4.0)))
    base = jnp.clip(jax.random.normal(first, (VOCAB, D), jnp.float32), -4.0, 4.0)
    return (base * col_scale * row_scale * 0.1).astype(jnp.bfloat16)


def draw_pad_mask(key, part):
    key = jax.random.fold_in(key, 31)
    position = jnp.arange(ROWS, dtype=jnp.int32)
    ticket = jax.random.randint(key, (ROWS,), 0, 1000, jnp.int32)
    limit = 1000 - 800 * position // ROWS
    live = jnp.logical_or(ticket < limit, position == 0)
    return live.astype(jnp.int32)


def set_ends(entries, stream_key, least, largest):
    spot = [jax.random.randint(jax.random.fold_in(stream_key, axis), (), 0, length) for axis, length in enumerate(entries.shape)]
    widest = entries.shape.index(max(entries.shape))
    beside = spot[:widest] + [(spot[widest] + 1) % entries.shape[widest]] + spot[widest + 1:]
    return entries.at[tuple(spot)].set(least).at[tuple(beside)].set(largest)


def block_scale(own_key, extent, cuts, least, high):
    gain = 1.0
    for axis_at, shards_of in cuts:
        heights = jax.random.uniform(jax.random.fold_in(jax.random.fold_in(own_key, 6), axis_at), (shards_of,), jnp.float32, least / len(cuts), high / len(cuts))
        gain = gain * jnp.repeat(jnp.exp(heights), extent[axis_at] // shards_of).reshape((-1,) + (1,) * (len(extent) - 1 - axis_at))
    return gain


def rank_table(count, skew):
    weights = [(1 << 20) // math.isqrt(standing ** skew) + 1 for standing in range(1, count + 1)]
    scale = 1 + sum(weights) // (1 << 30)
    return np.cumsum(np.array([max(1, weight // scale) for weight in weights]))


def skewed_ids(own_key, dims, amount, slope):
    listing = rank_table(amount, slope)
    pick = jax.random.randint(jax.random.fold_in(own_key, 1), dims, 0, int(listing[amount - 1]))
    grade = jnp.searchsorted(jnp.asarray(listing, jnp.int32), pick, side="right")
    return jax.random.permutation(jax.random.fold_in(own_key, 2), amount)[grade].astype(jnp.int32)


def gaussian(stream_key, shape, deviation, reach, pieces=(), held_as=jnp.bfloat16):
    loudness = block_scale(stream_key, shape, pieces, -0.22, 0.18) if pieces else 1.0
    values = jax.random.normal(stream_key, shape, jnp.float32) * deviation * loudness
    return jnp.minimum(jnp.maximum(values, -reach), reach).astype(held_as)


def setup_inputs(seed: int = 0) -> dict:
    seeds = jax.random.split(jax.random.key(seed), 8)
    ids = set_ends(skewed_ids(seeds[0], (ROWS, COLS), VOCAB, 1), jax.random.fold_in(seeds[0], 3), 0, VOCAB - 1).astype(jnp.int32)
    pad_mask = draw_pad_mask(jax.random.fold_in(seeds[7], 71), 0)
    embed = draw_embed(jax.random.fold_in(seeds[7], 71), 0)
    row_qkv = draw_row_qkv(jax.random.fold_in(seeds[7], 71), 0)
    row_out = gaussian(seeds[4], (D, D), (D // 4) ** -0.5, 0.4375, ((0, 4),))
    col_qkv = draw_col_qkv(jax.random.fold_in(seeds[7], 71), 0)
    col_out = gaussian(seeds[6], (D, D), D ** -0.5, 0.21875, ((0, 4),))
    return {"ids": ids, "pad_mask": pad_mask, "embed": embed, "row_qkv": row_qkv, "row_out": row_out, "col_qkv": col_qkv, "col_out": col_out}


EPS = 1e-05

def layer_norm(values):
    mean = lax.optimization_barrier(jnp.mean(values, axis=-1, keepdims=True))
    centred = values - mean
    spread = lax.optimization_barrier(jnp.mean(centred * centred, axis=-1, keepdims=True))
    return centred * lax.rsqrt(spread + EPS)

def softmax_last(scores):
    top = lax.optimization_barrier(jnp.max(scores, axis=-1, keepdims=True))
    weights = jnp.exp(scores - top)
    return weights / lax.optimization_barrier(jnp.sum(weights, axis=-1, keepdims=True))

def project(inputs, weights):
    product = jnp.einsum('rcd,ted->trce', inputs.astype(jnp.float32), weights.astype(jnp.float32))
    return product.astype(jnp.bfloat16)

def reference(ids, pad_mask, embed, row_qkv, row_out, col_qkv, col_out):
    embedded = embed.astype(jnp.float32)[ids]
    normed = layer_norm(embedded).astype(jnp.bfloat16)
    row_proj = project(normed, row_qkv)
    live = pad_mask.astype(jnp.float32)
    count = jnp.sum(live)
    head_shape = (ROWS, COLS, HEADS, HEAD_DIM)
    query = (row_proj[0].astype(jnp.float32) * live[:, None, None]).reshape(head_shape)
    keys = row_proj[1].astype(jnp.float32).reshape(head_shape)
    values = row_proj[2].astype(jnp.float32).reshape(head_shape)
    tied = jnp.einsum('rihd,rjhd->hij', query, keys) * (HEAD_DIM ** (-0.5) / jnp.sqrt(count))
    row_probs = softmax_last(tied).astype(jnp.bfloat16)
    row_context = jnp.einsum('hij,rjhd->rihd', row_probs.astype(jnp.float32), values)
    row_context = row_context.astype(jnp.bfloat16).reshape(ROWS, COLS, D)
    mixed = embedded + jnp.einsum('rce,fe->rcf', row_context.astype(jnp.float32), row_out.astype(jnp.float32))
    normed_second = layer_norm(mixed).astype(jnp.bfloat16)
    col_proj = project(normed_second, col_qkv)
    by_column = jnp.moveaxis(col_proj, 2, 0)

    def one_column(block):
        shape = (ROWS, HEADS, HEAD_DIM)
        col_query = block[0].astype(jnp.float32).reshape(shape)
        col_keys = block[1].astype(jnp.float32).reshape(shape)
        col_values = block[2].astype(jnp.float32).reshape(shape)
        scores = jnp.einsum('rhd,shd->hrs', col_query, col_keys) * HEAD_DIM ** (-0.5)
        scores = jnp.where(live > 0, scores, -jnp.inf)
        probs = softmax_last(scores).astype(jnp.bfloat16)
        context = jnp.einsum('hrs,shd->rhd', probs.astype(jnp.float32), col_values)
        return context.astype(jnp.bfloat16).reshape(ROWS, D)
    col_context = jnp.moveaxis(lax.map(one_column, by_column), 0, 1)
    layer_out = mixed + jnp.einsum('rce,fe->rcf', col_context.astype(jnp.float32), col_out.astype(jnp.float32))
    return layer_out.astype(jnp.bfloat16)
```

```python
import functools

import jax
import jax.numpy as jnp
from jax import lax
from jax.experimental import pallas as pl
from jax.experimental.pallas import tpu as pltpu
from jax.sharding import PartitionSpec as P

HEAD_DIM = 64
EPS = 1e-05
LANES = 128
CODES = 64
TABLE_ROWS = 48

f32 = jnp.float32
bf16 = jnp.bfloat16


def layer_norm(values):
    mean = jnp.mean(values, axis=-1, keepdims=True)
    centred = values - mean
    spread = jnp.mean(centred * centred, axis=-1, keepdims=True)
    return centred * lax.rsqrt(spread + EPS)


def softmax_last(scores):
    top = jnp.max(scores, axis=-1, keepdims=True)
    weights = jnp.exp(scores - top)
    return weights / jnp.sum(weights, axis=-1, keepdims=True)


def dot_nt(left, right):
    return lax.dot_general(left, right, (((1,), (1,)), ((), ())), preferred_element_type=f32)


def dot_nn(left, right):
    return jnp.dot(left, right, preferred_element_type=f32)


def iota(shape, axis):
    return lax.broadcasted_iota(jnp.int32, shape, axis)


def table_kernel(embed_ref, qkv_ref, out_ref):
    vocab = embed_ref.shape[0]
    normed = layer_norm(embed_ref[...].astype(f32)).astype(bf16)
    for t in range(3):
        table = dot_nt(normed, qkv_ref[t])
        out_ref[t] = jnp.zeros(out_ref.shape[1:], bf16)
        out_ref[t, 0:vocab, :] = table.astype(bf16)


def make_tables(embed, row_qkv):
    local_width = row_qkv.shape[1]
    return pl.pallas_call(
        table_kernel,
        out_shape=jax.ShapeDtypeStruct((3, TABLE_ROWS, local_width), bf16),
        name="tables",
    )(embed, row_qkv)


def halves(pair):
    lane = iota(pair.shape, 1)
    zero = jnp.zeros_like(pair)
    return jnp.where(lane < HEAD_DIM, pair, zero), jnp.where(lane < HEAD_DIM, zero, pair)


def spread_pair(pair):
    first, second = halves(pair)
    zero = jnp.zeros_like(pair)
    return jnp.concatenate(
        [
            jnp.concatenate([first, zero], 1),
            jnp.concatenate([zero, first], 1),
            jnp.concatenate([second, zero], 1),
            jnp.concatenate([zero, second], 1),
        ],
        0,
    )


def main_kernel(
    ids_ref,
    tab_ref,
    embed_ref,
    row_out_ref,
    col_qkv_ref,
    context_ref,
    mixed_out_ref,
    table_ref,
    embed2_ref,
    hot_ref,
    own_ref,
    live_own_ref,
    sum_ref,
    spread_ref,
    row_context_ref,
):
    rows = ids_ref.shape[0]
    pairs = rows // 2
    cols = hot_ref.shape[1]
    own = own_ref.shape[0] // pairs
    vocab, width = embed_ref.shape
    heads = width // HEAD_DIM
    parts = tab_ref.shape[0]
    local = tab_ref.shape[3]
    tokens = rows * own
    group = lax.axis_index("seq")
    part = lax.axis_index("head")

    table_ref[...] = jnp.zeros(table_ref.shape, bf16)
    for t in range(3):
        table_ref[t, 0:TABLE_ROWS, :] = jnp.concatenate([tab_ref[p, t] for p in range(parts)], 1)
    embed2_ref[...] = jnp.zeros(embed2_ref.shape, bf16)
    embed2_ref[0:vocab, 0:width] = embed_ref[...]
    embed2_ref[CODES : CODES + vocab, width : 2 * width] = embed_ref[...]

    ids = ids_ref[:, 0:cols]
    live = ids_ref[:, cols : cols + LANES].astype(f32)
    code = iota((CODES, cols), 0)
    for r in range(rows):
        hot = jnp.broadcast_to(ids[r : r + 1, :], (CODES, cols)) == code
        hot_ref[r * CODES : (r + 1) * CODES, :] = hot.astype(f32).astype(bf16)

    pick = (iota((own, cols), 1) == group * own + iota((own, cols), 0)).astype(f32).astype(bf16)
    mine = dot_nt(pick, ids.astype(f32).astype(bf16))
    lane = iota((own, LANES), 1)
    first_half = lane < CODES
    lane_code = jnp.where(first_half, lane, lane - CODES).astype(f32)
    for k in range(pairs):
        value = jnp.where(first_half, mine[:, 2 * k : 2 * k + 1], mine[:, 2 * k + 1 : 2 * k + 2])
        hot = (value == lane_code).astype(f32)
        alive = jnp.where(first_half, live[2 * k : 2 * k + 1, :], live[2 * k + 1 : 2 * k + 2, :])
        own_ref[k * own : (k + 1) * own, :] = hot.astype(bf16)
        live_own_ref[k * own : (k + 1) * own, :] = (hot * alive).astype(bf16)

    depth = rows * CODES
    for hp in range(heads // 2):
        span = slice(hp * LANES, (hp + 1) * LANES)
        queries = spread_pair(table_ref[0, :, span])
        keys = table_ref[1, :, span]
        zero = jnp.zeros_like(keys)
        keys2 = jnp.concatenate(
            [jnp.concatenate([keys, zero], 1), jnp.concatenate([zero, keys], 1)], 0
        )
        scores = dot_nt(queries, keys2)
        high = scores.astype(bf16)
        low = (scores - high.astype(f32)).astype(bf16)
        looked = dot_nn(
            live_own_ref[...],
            jnp.concatenate([high[:LANES], low[:LANES], high[LANES:], low[LANES:]], 1),
        ).astype(bf16)
        for h2 in range(2):
            base = (hp * 2 + h2) * own
            for piece in range(2):
                at = (h2 * 2 + piece) * LANES
                for k in range(pairs):
                    to = piece * depth + k * LANES
                    sum_ref[base : base + own, to : to + LANES] = looked[
                        k * own : (k + 1) * own, at : at + LANES
                    ]
    tied = dot_nn(sum_ref[:, 0:depth], hot_ref[...]) + dot_nn(
        sum_ref[:, depth : 2 * depth], hot_ref[...]
    )
    count = jnp.sum(live, axis=0, keepdims=True)[:, 0:1]
    probs = softmax_last(tied * (HEAD_DIM ** (-0.5) / jnp.sqrt(count))).astype(bf16)

    spread_ref[...] = dot_nt(probs, hot_ref[...]).astype(bf16)
    for hp in range(heads // 2):
        values = spread_pair(table_ref[2, :, hp * LANES : (hp + 1) * LANES])
        weights = jnp.concatenate(
            [
                jnp.concatenate(
                    [
                        spread_ref[
                            (hp * 2 + h2) * own : (hp * 2 + h2 + 1) * own,
                            k * LANES : (k + 1) * LANES,
                        ]
                        for h2 in range(2)
                    ],
                    1,
                )
                for k in range(pairs)
            ],
            0,
        )
        context = dot_nn(weights, values).astype(bf16)
        for k in range(pairs):
            for r2 in range(2):
                at = (2 * k + r2) * own
                row_context_ref[at : at + own, hp * LANES : (hp + 1) * LANES] = context[
                    k * own : (k + 1) * own, r2 * LANES : (r2 + 1) * LANES
                ]

    embedded2 = dot_nn(own_ref[...], embed2_ref[...])
    embedded = jnp.concatenate(
        [
            embedded2[k * own : (k + 1) * own, r2 * width : (r2 + 1) * width]
            for k in range(pairs)
            for r2 in range(2)
        ],
        0,
    )
    mixed = embedded + dot_nt(row_context_ref[...], row_out_ref[...])
    for p in range(parts):

        @pl.when(part == p)
        def _():
            mixed_out_ref[...] = mixed[:, p * local : (p + 1) * local]

    normed = layer_norm(mixed).astype(bf16)

    few = 8
    groups = own // few
    unit = rows * few

    def regroup(values):
        shape = (rows, groups, few, values.shape[1])
        return jnp.swapaxes(values.reshape(shape), 0, 1).reshape(tokens, values.shape[1])

    proj = [
        regroup(dot_nt(normed, col_qkv_ref[t * local : (t + 1) * local, :])).astype(bf16)
        for t in range(3)
    ]
    sub, lan = iota((unit, unit), 0), iota((unit, unit), 1)
    same_column = (sub % few) == (lan % few)
    seq_of_lane = iota((rows, unit), 1) // few
    live_lane = jnp.sum(
        jnp.where(seq_of_lane == iota((rows, unit), 0), live, 0.0), axis=0, keepdims=True
    )
    visible = jnp.logical_and(same_column, jnp.broadcast_to(live_lane, (unit, unit)) > 0)
    blocks = []
    for g in range(groups):
        at = slice(g * unit, (g + 1) * unit)
        pieces = []
        for first in range(0, local, LANES):
            span = slice(first, min(first + LANES, local))
            query, keys, values = (proj[t][at, span] for t in range(3))
            many = query.shape[1] // HEAD_DIM
            result = None
            for h2 in range(many):
                inside = iota(query.shape, 1) // HEAD_DIM == h2
                this = query if many == 1 else jnp.where(inside, query, jnp.zeros_like(query))
                scores = dot_nt(this, keys) * HEAD_DIM ** (-0.5)
                weights = softmax_last(jnp.where(visible, scores, -jnp.inf)).astype(bf16)
                found = dot_nn(weights, values)
                result = found if result is None else jnp.where(inside, found, result)
            pieces.append(result)
        blocks.append(jnp.concatenate(pieces, 1))
    whole = jnp.concatenate(blocks, 0).reshape(groups, rows, few, local)
    context_ref[...] = jnp.swapaxes(whole, 0, 1).reshape(tokens, local).astype(bf16)


def attend(ids, tables, embed, row_out, col_qkv, own):
    rows = ids.shape[0]
    cols = ids.shape[1] - LANES
    width = embed.shape[1]
    heads = width // HEAD_DIM
    local = tables.shape[3]
    tokens = rows * own
    return pl.pallas_call(
        main_kernel,
        out_shape=(
            jax.ShapeDtypeStruct((tokens, local), bf16),
            jax.ShapeDtypeStruct((tokens, local), f32),
        ),
        scratch_shapes=[
            pltpu.VMEM((3, CODES, width), bf16),
            pltpu.VMEM((2 * CODES, 2 * width), bf16),
            pltpu.VMEM((rows * CODES, cols), bf16),
            pltpu.VMEM((rows // 2 * own, LANES), bf16),
            pltpu.VMEM((rows // 2 * own, LANES), bf16),
            pltpu.VMEM((heads * own, 2 * rows * CODES), bf16),
            pltpu.VMEM((heads * own, rows * CODES), bf16),
            pltpu.VMEM((tokens, width), bf16),
        ],
        compiler_params=pltpu.CompilerParams(vmem_limit_bytes=48 * 1024 * 1024),
        name="attend",
    )(ids, tables, embed, row_out, col_qkv)


def finish_kernel(context_ref, col_out_ref, mixed_ref, out_ref):
    parts, _, local = context_ref.shape
    total = mixed_ref[...]
    for p in range(parts):
        total = total + dot_nt(context_ref[p], col_out_ref[:, p * local : (p + 1) * local])
    out_ref[...] = total.astype(bf16)


def finish(contexts, col_out, mixed):
    return pl.pallas_call(
        finish_kernel,
        out_shape=jax.ShapeDtypeStruct(mixed.shape, bf16),
        compiler_params=pltpu.CompilerParams(vmem_limit_bytes=48 * 1024 * 1024),
        name="finish",
    )(contexts, col_out, mixed)


def fast_body(ids, pad_mask, embed, row_qkv, row_out, col_qkv, col_out):
    rows_here, cols = ids.shape
    local = row_out.shape[0]
    groups = lax.axis_size("seq")
    own = cols // groups
    live = jnp.broadcast_to(pad_mask[:, None], (rows_here, LANES))
    ids_all = lax.all_gather(jnp.concatenate([ids, live], 1), "seq", axis=0, tiled=True)
    tables = lax.all_gather(make_tables(embed, row_qkv), "head", axis=0)
    row_out_all = lax.all_gather(row_out, "head", axis=0, tiled=True)
    context, mixed = attend(
        ids_all, tables, embed, row_out_all, col_qkv.reshape(3 * local, -1), own
    )
    contexts = lax.all_gather(context, "head", axis=0)
    out = finish(contexts, col_out, mixed)
    out = out.reshape(groups, rows_here, own, local)
    back = lax.all_to_all(out, "seq", split_axis=0, concat_axis=2, tiled=True)
    return back.reshape(rows_here, cols, local)


def weight_fold(out_weight, piece):
    return jnp.einsum("rce,fe->rcf", piece, out_weight, preferred_element_type=f32)


def attend_columns(query, keys, values, key_live):
    rows_all, count_cols, local_width = query.shape
    heads_here = local_width // HEAD_DIM
    shape = (rows_all, count_cols, heads_here, HEAD_DIM)
    scores = jnp.einsum(
        "rchd,schd->chrs",
        query.reshape(shape),
        keys.reshape(shape),
        preferred_element_type=f32,
    ) * HEAD_DIM ** (-0.5)
    scores = jnp.where(key_live > 0, scores, -jnp.inf)
    probs = softmax_last(scores).astype(bf16)
    context = jnp.einsum(
        "chrs,schd->rchd", probs, values.reshape(shape), preferred_element_type=f32
    )
    return context.astype(bf16).reshape(rows_all, count_cols, local_width)


def send_back(context):
    return lax.all_to_all(context[:, None], "seq", split_axis=0, concat_axis=1, tiled=True)


def general_body(ids, pad_mask, embed, row_qkv, row_out, col_qkv, col_out):
    rows_here, cols = ids.shape
    width = embed.shape[1]
    local_width = row_out.shape[0]
    heads_here = local_width // HEAD_DIM
    groups = lax.axis_size("seq")
    per_group = cols // groups
    codes = lax.broadcasted_iota(jnp.int32, (1, 1, embed.shape[0]), 2)
    onehot = (ids[:, :, None] == codes).astype(bf16)
    embedded = jnp.einsum("rcv,vd->rcd", onehot, embed, preferred_element_type=f32)
    normed = layer_norm(embedded).astype(bf16)
    row_proj = jnp.einsum("rcd,ted->trce", normed, row_qkv, preferred_element_type=f32)
    row_proj = row_proj.astype(bf16)
    live = pad_mask.astype(bf16)
    head_shape = (rows_here, cols, heads_here, HEAD_DIM)
    query = (row_proj[0] * live[:, None, None]).reshape(head_shape)
    keys = row_proj[1].reshape(head_shape)
    values = row_proj[2].reshape(head_shape)
    partial_scores = jnp.einsum("rihd,rjhd->hij", query, keys, preferred_element_type=f32)
    count_here = jnp.sum(pad_mask.astype(f32))
    scale = HEAD_DIM ** (-0.5)
    total, count = lax.psum((partial_scores, count_here), "seq")
    row_probs = softmax_last(total * (scale / jnp.sqrt(count))).astype(bf16)
    row_context = jnp.einsum("hij,rjhd->rihd", row_probs, values, preferred_element_type=f32)
    row_context = row_context.astype(bf16).reshape(rows_here, cols, local_width)
    start_feature = lax.axis_index("head") * local_width
    resident = lax.dynamic_slice_in_dim(embedded, start_feature, local_width, 2)
    row_update = weight_fold(row_out, lax.all_gather(row_context, "head", axis=2, tiled=True))
    mixed = resident + row_update
    sums, squares = lax.psum((jnp.sum(mixed, axis=-1), jnp.sum(mixed * mixed, axis=-1)), "head")
    mean = sums / width
    spread = squares / width - mean * mean
    normed_here = ((mixed - mean[..., None]) * lax.rsqrt(spread[..., None] + EPS)).astype(bf16)
    live_tile = jnp.broadcast_to(live[:, None, None, None], (rows_here, groups, per_group, 1))
    normed_full = lax.all_gather(normed_here, "head", axis=2, tiled=True)
    col_proj = jnp.einsum("rcd,ted->rcte", normed_full, col_qkv, preferred_element_type=f32)
    packed = col_proj.astype(bf16).reshape(rows_here, groups, per_group, 3 * local_width)
    received = lax.all_to_all(packed, "seq", split_axis=1, concat_axis=0, tiled=True)
    mask_part = lax.all_to_all(live_tile, "seq", split_axis=1, concat_axis=0, tiled=True)
    column_out = send_back(
        attend_columns(
            received[:, 0, :, :local_width],
            received[:, 0, :, local_width : 2 * local_width],
            received[:, 0, :, 2 * local_width :],
            mask_part[:, 0, 0, 0],
        )
    )
    column_out = column_out.reshape(rows_here, cols, local_width)
    col_update = weight_fold(col_out, lax.all_gather(column_out, "head", axis=2, tiled=True))
    return (mixed + col_update).astype(bf16)


def body(ids, pad_mask, embed, row_qkv, row_out, col_qkv, col_out):
    rows_here, cols = ids.shape
    groups = lax.axis_size("seq")
    own, rows = cols // groups, rows_here * groups
    fits = own % 16 == 0 and rows * 8 == LANES and embed.shape[0] <= TABLE_ROWS
    chosen = fast_body if fits else general_body
    return chosen(ids, pad_mask, embed, row_qkv, row_out, col_qkv, col_out)


def solution(mesh):
    placed = (
        P("seq", None),
        P("seq"),
        P(),
        P(None, "head", None),
        P("head", None),
        P(None, "head", None),
        P("head", None),
    )
    return jax.shard_map(
        body, mesh=mesh, in_specs=placed, out_specs=P("seq", None, "head"), check_vma=False
    )
```

```python
import functools

import jax
import jax.numpy as jnp
from jax import lax
from jax.experimental import pallas as pl
from jax.experimental.pallas import tpu as pltpu
from jax.sharding import PartitionSpec as P

HEAD_DIM = 64
EPS = 1e-05
LANES = 128
CODES = 64
TABLE_ROWS = 48

f32 = jnp.float32
bf16 = jnp.bfloat16


def layer_norm(values):
    mean = jnp.mean(values, axis=-1, keepdims=True)
    centred = values - mean
    spread = jnp.mean(centred * centred, axis=-1, keepdims=True)
    return centred * lax.rsqrt(spread + EPS)


def softmax_last(scores):
    top = jnp.max(scores, axis=-1, keepdims=True)
    weights = jnp.exp(scores - top)
    return weights / jnp.sum(weights, axis=-1, keepdims=True)


def dot_nt(left, right):
    return lax.dot_general(left, right, (((1,), (1,)), ((), ())), preferred_element_type=f32)


def dot_nn(left, right):
    return jnp.dot(left, right, preferred_element_type=f32)


def iota(shape, axis):
    return lax.broadcasted_iota(jnp.int32, shape, axis)


def table_kernel(embed_ref, qkv_ref, out_ref):
    vocab = embed_ref.shape[0]
    normed = layer_norm(embed_ref[...].astype(f32)).astype(bf16)
    for t in range(3):
        table = dot_nt(normed, qkv_ref[t])
        out_ref[t] = jnp.zeros(out_ref.shape[1:], bf16)
        out_ref[t, 0:vocab, :] = table.astype(bf16)


def make_tables(embed, row_qkv):
    local_width = row_qkv.shape[1]
    return pl.pallas_call(
        table_kernel,
        out_shape=jax.ShapeDtypeStruct((3, TABLE_ROWS, local_width), bf16),
        name="tables",
    )(embed, row_qkv)


def halves(pair):
    lane = iota(pair.shape, 1)
    zero = jnp.zeros_like(pair)
    return jnp.where(lane < HEAD_DIM, pair, zero), jnp.where(lane < HEAD_DIM, zero, pair)


def spread_pair(pair):
    first, second = halves(pair)
    zero = jnp.zeros_like(pair)
    return jnp.concatenate(
        [
            jnp.concatenate([first, zero], 1),
            jnp.concatenate([zero, first], 1),
            jnp.concatenate([second, zero], 1),
            jnp.concatenate([zero, second], 1),
        ],
        0,
    )


def main_kernel(groups, parts, *refs):
    ids_refs, refs = refs[:groups], refs[groups:]
    tab_refs, refs = refs[:parts], refs[parts:]
    row_out_refs, refs = refs[:parts], refs[parts:]
    (
        embed_ref,
        col_qkv_hbm,
        context_ref,
        mixed_out_ref,
        tab_ref,
        row_out_ref,
        col_qkv_ref,
        table_ref,
        embed2_ref,
        hot_ref,
        own_ref,
        live_own_ref,
        sum_ref,
        spread_ref,
        row_context_ref,
        weight_sem,
    ) = refs
    rows = ids_refs[0].shape[0] * groups
    pairs = rows // 2
    cols = hot_ref.shape[1]
    own = own_ref.shape[0] // pairs
    vocab, width = embed_ref.shape
    heads = width // HEAD_DIM
    local = tab_ref.shape[3]
    tokens = rows * own
    group = lax.axis_index("seq")
    part = lax.axis_index("head")

    loads = [
        pltpu.make_async_copy(row_out_refs[p], row_out_ref.at[part ^ p], weight_sem.at[p])
        for p in range(parts)
    ]
    loads.append(pltpu.make_async_copy(col_qkv_hbm, col_qkv_ref, weight_sem.at[parts]))
    for load in loads:
        load.start()

    for p in range(parts):
        tab_ref[part ^ p] = tab_refs[p][...]
    table_ref[...] = jnp.zeros(table_ref.shape, bf16)
    for t in range(3):
        table_ref[t, 0:TABLE_ROWS, :] = jnp.concatenate([tab_ref[p, t] for p in range(parts)], 1)
    embed2_ref[...] = jnp.zeros(embed2_ref.shape, bf16)
    embed2_ref[0:vocab, 0:width] = embed_ref[...]
    embed2_ref[CODES : CODES + vocab, width : 2 * width] = embed_ref[...]

    coded = jnp.concatenate([ref[...] for ref in ids_refs], 0)
    ids = coded & 0xFFFF
    live = (coded[:, 0:LANES] >> 16).astype(f32)
    code = iota((CODES, cols), 0)
    for r in range(rows):
        hot = jnp.broadcast_to(ids[r : r + 1, :], (CODES, cols)) == code
        hot_ref[r * CODES : (r + 1) * CODES, :] = hot.astype(f32).astype(bf16)

    pick = (iota((own, cols), 1) == group * own + iota((own, cols), 0)).astype(f32).astype(bf16)
    mine = dot_nt(pick, ids.astype(f32).astype(bf16))
    lane = iota((own, LANES), 1)
    first_half = lane < CODES
    lane_code = jnp.where(first_half, lane, lane - CODES).astype(f32)
    for k in range(pairs):
        value = jnp.where(first_half, mine[:, 2 * k : 2 * k + 1], mine[:, 2 * k + 1 : 2 * k + 2])
        hot = (value == lane_code).astype(f32)
        alive = jnp.where(first_half, live[2 * k : 2 * k + 1, :], live[2 * k + 1 : 2 * k + 2, :])
        own_ref[k * own : (k + 1) * own, :] = hot.astype(bf16)
        live_own_ref[k * own : (k + 1) * own, :] = (hot * alive).astype(bf16)

    depth = rows * CODES
    for hp in range(heads // 2):
        span = slice(hp * LANES, (hp + 1) * LANES)
        queries = spread_pair(table_ref[0, :, span])
        keys = table_ref[1, :, span]
        zero = jnp.zeros_like(keys)
        keys2 = jnp.concatenate(
            [jnp.concatenate([keys, zero], 1), jnp.concatenate([zero, keys], 1)], 0
        )
        scores = dot_nt(queries, keys2)
        high = scores.astype(bf16)
        low = (scores - high.astype(f32)).astype(bf16)
        looked = dot_nn(
            live_own_ref[...],
            jnp.concatenate([high[:LANES], low[:LANES], high[LANES:], low[LANES:]], 1),
        ).astype(bf16)
        for h2 in range(2):
            base = (hp * 2 + h2) * own
            for piece in range(2):
                at = (h2 * 2 + piece) * LANES
                for k in range(pairs):
                    to = piece * depth + k * LANES
                    sum_ref[base : base + own, to : to + LANES] = looked[
                        k * own : (k + 1) * own, at : at + LANES
                    ]
    tied = dot_nn(sum_ref[:, 0:depth], hot_ref[...]) + dot_nn(
        sum_ref[:, depth : 2 * depth], hot_ref[...]
    )
    count = jnp.sum(live, axis=0, keepdims=True)[:, 0:1]
    probs = softmax_last(tied * (HEAD_DIM ** (-0.5) / jnp.sqrt(count))).astype(bf16)

    spread_ref[...] = dot_nt(probs, hot_ref[...]).astype(bf16)
    for hp in range(heads // 2):
        values = spread_pair(table_ref[2, :, hp * LANES : (hp + 1) * LANES])
        weights = jnp.concatenate(
            [
                jnp.concatenate(
                    [
                        spread_ref[
                            (hp * 2 + h2) * own : (hp * 2 + h2 + 1) * own,
                            k * LANES : (k + 1) * LANES,
                        ]
                        for h2 in range(2)
                    ],
                    1,
                )
                for k in range(pairs)
            ],
            0,
        )
        context = dot_nn(weights, values).astype(bf16)
        for k in range(pairs):
            for r2 in range(2):
                at = (2 * k + r2) * own
                row_context_ref[at : at + own, hp * LANES : (hp + 1) * LANES] = context[
                    k * own : (k + 1) * own, r2 * LANES : (r2 + 1) * LANES
                ]

    embedded2 = dot_nn(own_ref[...], embed2_ref[...])
    embedded = jnp.concatenate(
        [
            embedded2[k * own : (k + 1) * own, r2 * width : (r2 + 1) * width]
            for k in range(pairs)
            for r2 in range(2)
        ],
        0,
    )
    for load in loads[:parts]:
        load.wait()
    mixed = embedded + dot_nt(row_context_ref[...], row_out_ref[...].reshape(width, width))
    for p in range(parts):

        @pl.when(part == p)
        def _():
            mixed_out_ref[...] = mixed[:, p * local : (p + 1) * local]

    normed = layer_norm(mixed).astype(bf16)

    few = 8
    groups = own // few
    unit = rows * few

    def regroup(values):
        shape = (rows, groups, few, values.shape[1])
        return jnp.swapaxes(values.reshape(shape), 0, 1).reshape(tokens, values.shape[1])

    loads[parts].wait()
    proj = [
        regroup(dot_nt(normed, col_qkv_ref[t * local : (t + 1) * local, :])).astype(bf16)
        for t in range(3)
    ]
    sub, lan = iota((unit, unit), 0), iota((unit, unit), 1)
    same_column = (sub % few) == (lan % few)
    seq_of_lane = iota((rows, unit), 1) // few
    live_lane = jnp.sum(
        jnp.where(seq_of_lane == iota((rows, unit), 0), live, 0.0), axis=0, keepdims=True
    )
    visible = jnp.logical_and(same_column, jnp.broadcast_to(live_lane, (unit, unit)) > 0)
    blocks = []
    for g in range(groups):
        at = slice(g * unit, (g + 1) * unit)
        pieces = []
        for first in range(0, local, LANES):
            span = slice(first, min(first + LANES, local))
            query, keys, values = (proj[t][at, span] for t in range(3))
            many = query.shape[1] // HEAD_DIM
            result = None
            for h2 in range(many):
                inside = iota(query.shape, 1) // HEAD_DIM == h2
                this = query if many == 1 else jnp.where(inside, query, jnp.zeros_like(query))
                scores = dot_nt(this, keys) * HEAD_DIM ** (-0.5)
                weights = softmax_last(jnp.where(visible, scores, -jnp.inf)).astype(bf16)
                found = dot_nn(weights, values)
                result = found if result is None else jnp.where(inside, found, result)
            pieces.append(result)
        blocks.append(jnp.concatenate(pieces, 1))
    whole = jnp.concatenate(blocks, 0).reshape(groups, rows, few, local)
    context_ref[...] = jnp.swapaxes(whole, 0, 1).reshape(tokens, local).astype(bf16)


def attend(ids, tables, embed, row_outs, col_qkv):
    groups, parts = len(ids), len(tables)
    rows_here, cols = ids[0].shape
    own = cols // groups
    rows = rows_here * groups
    width = embed.shape[1]
    heads = width // HEAD_DIM
    local = tables[0].shape[2]
    tokens = rows * own
    vmem = pl.BlockSpec(memory_space=pltpu.VMEM)
    hbm = pl.BlockSpec(memory_space=pl.ANY)
    return pl.pallas_call(
        functools.partial(main_kernel, groups, parts),
        out_shape=(
            jax.ShapeDtypeStruct((tokens, local), bf16),
            jax.ShapeDtypeStruct((tokens, local), f32),
        ),
        in_specs=[vmem] * (groups + parts) + [hbm] * parts + [vmem, hbm],
        scratch_shapes=[
            pltpu.VMEM((parts, 3, TABLE_ROWS, local), bf16),
            pltpu.VMEM((parts, local, width), bf16),
            pltpu.VMEM((3 * local, width), bf16),
            pltpu.VMEM((3, CODES, width), bf16),
            pltpu.VMEM((2 * CODES, 2 * width), bf16),
            pltpu.VMEM((rows * CODES, cols), bf16),
            pltpu.VMEM((rows // 2 * own, LANES), bf16),
            pltpu.VMEM((rows // 2 * own, LANES), bf16),
            pltpu.VMEM((heads * own, 2 * rows * CODES), bf16),
            pltpu.VMEM((heads * own, rows * CODES), bf16),
            pltpu.VMEM((tokens, width), bf16),
            pltpu.SemaphoreType.DMA((parts + 1,)),
        ],
        compiler_params=pltpu.CompilerParams(vmem_limit_bytes=48 * 1024 * 1024),
        name="attend",
    )(*ids, *tables, *row_outs, embed, col_qkv)


def finish_kernel(parts, *refs):
    context_refs = refs[:parts]
    col_out_ref, mixed_ref, out_ref, weight_ref = refs[parts:]
    local = mixed_ref.shape[1]
    part = lax.axis_index("head")
    for p in range(parts):
        weight_ref[p] = col_out_ref[:, p * local : (p + 1) * local]
    total = mixed_ref[...]
    for p in range(parts):
        total = total + dot_nt(context_refs[p][...], weight_ref[part ^ p])
    out_ref[...] = total.astype(bf16)


def finish(contexts, col_out, mixed):
    parts = len(contexts)
    local = mixed.shape[1]
    return pl.pallas_call(
        functools.partial(finish_kernel, parts),
        out_shape=jax.ShapeDtypeStruct(mixed.shape, bf16),
        scratch_shapes=[pltpu.VMEM((parts, local, local), bf16)],
        compiler_params=pltpu.CompilerParams(vmem_limit_bytes=48 * 1024 * 1024),
        name="finish",
    )(*contexts, col_out, mixed)


def order_kernel(groups, *refs):
    out_ref = refs[groups]
    group = lax.axis_index("seq")
    for d in range(groups):
        out_ref[:, group ^ d] = refs[d][...]


def order(blocks):
    groups = len(blocks)
    rows_here, own, local = blocks[0].shape
    return pl.pallas_call(
        functools.partial(order_kernel, groups),
        out_shape=jax.ShapeDtypeStruct((rows_here, groups, own, local), bf16),
        name="order",
    )(*blocks)


def exchange(value, axis, step):
    if step == 0:
        return value
    count = lax.axis_size(axis)
    return lax.ppermute(value, axis, [(i, i ^ step) for i in range(count)])


def fast_body(ids, pad_mask, embed, row_qkv, row_out, col_qkv, col_out):
    rows_here, cols = ids.shape
    local = row_out.shape[0]
    groups, parts = lax.axis_size("seq"), lax.axis_size("head")
    own = cols // groups
    coded = ids + 65536 * pad_mask[:, None]
    row_outs = [exchange(row_out, "head", p) for p in range(parts)]
    codes = [exchange(coded, "seq", d) for d in range(groups)]
    mine = make_tables(embed, row_qkv)
    tables = [exchange(mine, "head", p) for p in range(parts)]
    context, mixed = attend(codes, tables, embed, row_outs, col_qkv.reshape(3 * local, -1))
    contexts = [exchange(context, "head", p) for p in range(parts)]
    out = finish(contexts, col_out, mixed).reshape(groups, rows_here, own, local)
    blocks = [exchange(out[d], "seq", d) for d in range(groups)]
    return order(blocks).reshape(rows_here, cols, local)


def weight_fold(out_weight, piece):
    return jnp.einsum("rce,fe->rcf", piece, out_weight, preferred_element_type=f32)


def attend_columns(query, keys, values, key_live):
    rows_all, count_cols, local_width = query.shape
    heads_here = local_width // HEAD_DIM
    shape = (rows_all, count_cols, heads_here, HEAD_DIM)
    scores = jnp.einsum(
        "rchd,schd->chrs",
        query.reshape(shape),
        keys.reshape(shape),
        preferred_element_type=f32,
    ) * HEAD_DIM ** (-0.5)
    scores = jnp.where(key_live > 0, scores, -jnp.inf)
    probs = softmax_last(scores).astype(bf16)
    context = jnp.einsum(
        "chrs,schd->rchd", probs, values.reshape(shape), preferred_element_type=f32
    )
    return context.astype(bf16).reshape(rows_all, count_cols, local_width)


def send_back(context):
    return lax.all_to_all(context[:, None], "seq", split_axis=0, concat_axis=1, tiled=True)


def general_body(ids, pad_mask, embed, row_qkv, row_out, col_qkv, col_out):
    rows_here, cols = ids.shape
    width = embed.shape[1]
    local_width = row_out.shape[0]
    heads_here = local_width // HEAD_DIM
    groups = lax.axis_size("seq")
    per_group = cols // groups
    codes = lax.broadcasted_iota(jnp.int32, (1, 1, embed.shape[0]), 2)
    onehot = (ids[:, :, None] == codes).astype(bf16)
    embedded = jnp.einsum("rcv,vd->rcd", onehot, embed, preferred_element_type=f32)
    normed = layer_norm(embedded).astype(bf16)
    row_proj = jnp.einsum("rcd,ted->trce", normed, row_qkv, preferred_element_type=f32)
    row_proj = row_proj.astype(bf16)
    live = pad_mask.astype(bf16)
    head_shape = (rows_here, cols, heads_here, HEAD_DIM)
    query = (row_proj[0] * live[:, None, None]).reshape(head_shape)
    keys = row_proj[1].reshape(head_shape)
    values = row_proj[2].reshape(head_shape)
    partial_scores = jnp.einsum("rihd,rjhd->hij", query, keys, preferred_element_type=f32)
    count_here = jnp.sum(pad_mask.astype(f32))
    scale = HEAD_DIM ** (-0.5)
    total, count = lax.psum((partial_scores, count_here), "seq")
    row_probs = softmax_last(total * (scale / jnp.sqrt(count))).astype(bf16)
    row_context = jnp.einsum("hij,rjhd->rihd", row_probs, values, preferred_element_type=f32)
    row_context = row_context.astype(bf16).reshape(rows_here, cols, local_width)
    start_feature = lax.axis_index("head") * local_width
    resident = lax.dynamic_slice_in_dim(embedded, start_feature, local_width, 2)
    row_update = weight_fold(row_out, lax.all_gather(row_context, "head", axis=2, tiled=True))
    mixed = resident + row_update
    sums, squares = lax.psum((jnp.sum(mixed, axis=-1), jnp.sum(mixed * mixed, axis=-1)), "head")
    mean = sums / width
    spread = squares / width - mean * mean
    normed_here = ((mixed - mean[..., None]) * lax.rsqrt(spread[..., None] + EPS)).astype(bf16)
    live_tile = jnp.broadcast_to(live[:, None, None, None], (rows_here, groups, per_group, 1))
    normed_full = lax.all_gather(normed_here, "head", axis=2, tiled=True)
    col_proj = jnp.einsum("rcd,ted->rcte", normed_full, col_qkv, preferred_element_type=f32)
    packed = col_proj.astype(bf16).reshape(rows_here, groups, per_group, 3 * local_width)
    received = lax.all_to_all(packed, "seq", split_axis=1, concat_axis=0, tiled=True)
    mask_part = lax.all_to_all(live_tile, "seq", split_axis=1, concat_axis=0, tiled=True)
    column_out = send_back(
        attend_columns(
            received[:, 0, :, :local_width],
            received[:, 0, :, local_width : 2 * local_width],
            received[:, 0, :, 2 * local_width :],
            mask_part[:, 0, 0, 0],
        )
    )
    column_out = column_out.reshape(rows_here, cols, local_width)
    col_update = weight_fold(col_out, lax.all_gather(column_out, "head", axis=2, tiled=True))
    return (mixed + col_update).astype(bf16)


def body(ids, pad_mask, embed, row_qkv, row_out, col_qkv, col_out):
    rows_here, cols = ids.shape
    groups = lax.axis_size("seq")
    own, rows = cols // groups, rows_here * groups
    paired = groups & (groups - 1) == 0 and lax.axis_size("head") in (2, 4)
    fits = paired and own % 16 == 0 and rows * 8 == LANES and embed.shape[0] <= TABLE_ROWS
    chosen = fast_body if fits else general_body
    return chosen(ids, pad_mask, embed, row_qkv, row_out, col_qkv, col_out)


def solution(mesh):
    placed = (
        P("seq", None),
        P("seq"),
        P(),
        P(None, "head", None),
        P("head", None),
        P(None, "head", None),
        P("head", None),
    )
    return jax.shard_map(
        body, mesh=mesh, in_specs=placed, out_specs=P("seq", None, "head"), check_vma=False
    )
```

```python
import functools

import jax
import jax.numpy as jnp
from jax import lax
from jax.experimental import pallas as pl
from jax.experimental.pallas import tpu as pltpu
from jax.sharding import PartitionSpec as P

HEAD_DIM = 64
EPS = 1e-05
LANES = 128
CODES = 64
VOCAB_ROWS = 40
TABLE_ROWS = 48

f32 = jnp.float32
bf16 = jnp.bfloat16


def layer_norm(values):
    mean = jnp.mean(values, axis=-1, keepdims=True)
    centred = values - mean
    spread = jnp.mean(centred * centred, axis=-1, keepdims=True)
    return centred * lax.rsqrt(spread + EPS)


def softmax_last(scores):
    top = jnp.max(scores, axis=-1, keepdims=True)
    weights = jnp.exp(scores - top)
    return weights / jnp.sum(weights, axis=-1, keepdims=True)


def dot_nt(left, right):
    return lax.dot_general(left, right, (((1,), (1,)), ((), ())), preferred_element_type=f32)


def dot_nn(left, right):
    return jnp.dot(left, right, preferred_element_type=f32)


def iota(shape, axis):
    return lax.broadcasted_iota(jnp.int32, shape, axis)


def table_kernel(embed_ref, qkv_ref, out_ref, padded_ref):
    vocab = embed_ref.shape[0]
    padded_ref[...] = jnp.zeros(padded_ref.shape, f32)
    padded_ref[0:vocab, :] = embed_ref[...].astype(f32)
    normed = layer_norm(padded_ref[...]).astype(bf16)
    out_ref[...] = dot_nt(normed, qkv_ref[...]).astype(bf16)


def make_tables(embed, qkv):
    return pl.pallas_call(
        table_kernel,
        out_shape=jax.ShapeDtypeStruct((TABLE_ROWS, qkv.shape[0]), bf16),
        scratch_shapes=[pltpu.VMEM((TABLE_ROWS, embed.shape[1]), f32)],
        cost_estimate=pl.CostEstimate(
            flops=2 * TABLE_ROWS * qkv.size, bytes_accessed=2 * qkv.size, transcendentals=0
        ),
        name="tables",
    )(embed, qkv)


def pack_kernel(table_ref, *refs):
    codes_refs, out_ref = refs[:-1], refs[-1]
    coded = jnp.concatenate([ref[...] for ref in codes_refs], 0)
    ids = (coded & 0xFFFF).astype(f32)
    live = (coded >> 16).astype(f32)
    some, cols = coded.shape
    out_ref[...] = table_ref[...]
    spare = jnp.concatenate(
        [ids, live[:, 0:LANES], jnp.zeros((some, out_ref.shape[1] - cols - LANES), f32)], 1
    )
    if some < 8:
        spare = jnp.concatenate([spare, jnp.zeros((8 - some, spare.shape[1]), f32)], 0)
    kept = table_ref[VOCAB_ROWS - 8 : VOCAB_ROWS, :].astype(f32)
    out_ref[VOCAB_ROWS - 8 : TABLE_ROWS, :] = jnp.concatenate([kept, spare], 0).astype(bf16)


def pack(table, codes):
    return pl.pallas_call(
        pack_kernel, out_shape=jax.ShapeDtypeStruct(table.shape, bf16), name="pack"
    )(table, *codes)


def halves(pair):
    lane = iota(pair.shape, 1)
    zero = jnp.zeros_like(pair)
    return jnp.where(lane < HEAD_DIM, pair, zero), jnp.where(lane < HEAD_DIM, zero, pair)


def spread_pair(pair):
    first, second = halves(pair)
    zero = jnp.zeros_like(pair)
    return jnp.concatenate(
        [
            jnp.concatenate([first, zero], 1),
            jnp.concatenate([zero, first], 1),
            jnp.concatenate([second, zero], 1),
            jnp.concatenate([zero, second], 1),
        ],
        0,
    )


def read_sequences(payload_ref, rows, first, last):
    parts = payload_ref.shape[0]
    each = rows // parts
    return jnp.concatenate(
        [
            payload_ref[p, VOCAB_ROWS:TABLE_ROWS, first:last].astype(f32)[0:each]
            for p in range(parts)
        ],
        0,
    )


def row_kernel(
    payload_ref,
    row_context_ref,
    own_ref,
    table_ref,
    hot_ref,
    live_own_ref,
    sum_ref,
    spread_ref,
):
    parts = payload_ref.shape[0]
    depth, cols = hot_ref.shape
    rows = depth // CODES
    pairs = rows // 2
    own = own_ref.shape[0] // pairs
    width = row_context_ref.shape[1]
    heads = width // HEAD_DIM
    local = width // parts
    group = lax.axis_index("seq")

    for t in range(3):
        table_ref[t, 0:VOCAB_ROWS, :] = jnp.concatenate(
            [payload_ref[p, 0:VOCAB_ROWS, t * local : (t + 1) * local] for p in range(parts)], 1
        )
        table_ref[t, VOCAB_ROWS:CODES, :] = jnp.zeros((CODES - VOCAB_ROWS, width), bf16)

    ids = read_sequences(payload_ref, rows, 0, cols)
    live = read_sequences(payload_ref, rows, cols, cols + LANES)
    code = iota((CODES, cols), 0).astype(f32)
    for r in range(rows):
        hot = jnp.broadcast_to(ids[r : r + 1, :], (CODES, cols)) == code
        hot_ref[r * CODES : (r + 1) * CODES, :] = hot.astype(f32).astype(bf16)

    pick = (iota((own, cols), 1) == group * own + iota((own, cols), 0)).astype(f32).astype(bf16)
    mine = dot_nt(pick, ids.astype(bf16))
    lane = iota((own, LANES), 1)
    first_half = lane < CODES
    lane_code = jnp.where(first_half, lane, lane - CODES).astype(f32)
    for k in range(pairs):
        value = jnp.where(first_half, mine[:, 2 * k : 2 * k + 1], mine[:, 2 * k + 1 : 2 * k + 2])
        hot = (value == lane_code).astype(f32)
        alive = jnp.where(first_half, live[2 * k : 2 * k + 1, :], live[2 * k + 1 : 2 * k + 2, :])
        own_ref[k * own : (k + 1) * own, :] = hot.astype(bf16)
        live_own_ref[k * own : (k + 1) * own, :] = (hot * alive).astype(bf16)

    for hp in range(heads // 2):
        span = slice(hp * LANES, (hp + 1) * LANES)
        queries = spread_pair(table_ref[0, :, span])
        keys = table_ref[1, :, span]
        zero = jnp.zeros_like(keys)
        keys2 = jnp.concatenate(
            [jnp.concatenate([keys, zero], 1), jnp.concatenate([zero, keys], 1)], 0
        )
        scores = dot_nt(queries, keys2)
        high = scores.astype(bf16)
        low = (scores - high.astype(f32)).astype(bf16)
        looked = dot_nn(
            live_own_ref[...],
            jnp.concatenate([high[:LANES], low[:LANES], high[LANES:], low[LANES:]], 1),
        ).astype(bf16)
        for h2 in range(2):
            base = (hp * 2 + h2) * own
            for piece in range(2):
                at = (h2 * 2 + piece) * LANES
                for k in range(pairs):
                    to = piece * depth + k * LANES
                    sum_ref[base : base + own, to : to + LANES] = looked[
                        k * own : (k + 1) * own, at : at + LANES
                    ]
    tied = dot_nn(sum_ref[:, 0:depth], hot_ref[...]) + dot_nn(
        sum_ref[:, depth : 2 * depth], hot_ref[...]
    )
    count = jnp.sum(live, axis=0, keepdims=True)[:, 0:1]
    probs = softmax_last(tied * (HEAD_DIM ** (-0.5) / jnp.sqrt(count))).astype(bf16)

    spread_ref[...] = dot_nt(probs, hot_ref[...]).astype(bf16)
    for hp in range(heads // 2):
        values = spread_pair(table_ref[2, :, hp * LANES : (hp + 1) * LANES])
        weights = jnp.concatenate(
            [
                jnp.concatenate(
                    [
                        spread_ref[
                            (hp * 2 + h2) * own : (hp * 2 + h2 + 1) * own,
                            k * LANES : (k + 1) * LANES,
                        ]
                        for h2 in range(2)
                    ],
                    1,
                )
                for k in range(pairs)
            ],
            0,
        )
        context = dot_nn(weights, values).astype(bf16)
        for k in range(pairs):
            for r2 in range(2):
                at = (2 * k + r2) * own
                row_context_ref[at : at + own, hp * LANES : (hp + 1) * LANES] = context[
                    k * own : (k + 1) * own, r2 * LANES : (r2 + 1) * LANES
                ]


def attend_rows(payload, rows, cols, own, width):
    heads = width // HEAD_DIM
    tokens = rows * own
    return pl.pallas_call(
        row_kernel,
        out_shape=(
            jax.ShapeDtypeStruct((tokens, width), bf16),
            jax.ShapeDtypeStruct((rows // 2 * own, LANES), bf16),
        ),
        scratch_shapes=[
            pltpu.VMEM((3, CODES, width), bf16),
            pltpu.VMEM((rows * CODES, cols), bf16),
            pltpu.VMEM((rows // 2 * own, LANES), bf16),
            pltpu.VMEM((heads * own, 2 * rows * CODES), bf16),
            pltpu.VMEM((heads * own, rows * CODES), bf16),
        ],
        cost_estimate=pl.CostEstimate(flops=5 * 10**9, bytes_accessed=10**6, transcendentals=0),
        compiler_params=pltpu.CompilerParams(vmem_limit_bytes=32 * 1024 * 1024),
        name="row_attention",
    )(payload)


def column_kernel(parts, cols, *refs):
    row_out_refs, refs = refs[:parts], refs[parts:]
    (
        payload_ref,
        row_context_ref,
        own_ref,
        embed_ref,
        col_qkv_ref,
        context_ref,
        mixed_out_ref,
        row_out_ref,
        embed2_ref,
    ) = refs
    tokens, width = row_context_ref.shape
    rows = LANES // 8
    pairs = rows // 2
    own = own_ref.shape[0] // pairs
    vocab = embed_ref.shape[0]
    local = width // parts
    part = lax.axis_index("head")

    for p in range(parts):
        row_out_ref[part ^ p] = row_out_refs[p][...]
    embed2_ref[...] = jnp.zeros(embed2_ref.shape, bf16)
    embed2_ref[0:vocab, 0:width] = embed_ref[...]
    embed2_ref[CODES : CODES + vocab, width : 2 * width] = embed_ref[...]

    embedded2 = dot_nn(own_ref[...], embed2_ref[...])
    embedded = jnp.concatenate(
        [
            embedded2[k * own : (k + 1) * own, r2 * width : (r2 + 1) * width]
            for k in range(pairs)
            for r2 in range(2)
        ],
        0,
    )
    mixed = embedded + dot_nt(row_context_ref[...], row_out_ref[...].reshape(width, width))
    for p in range(parts):

        @pl.when(part == p)
        def _():
            mixed_out_ref[...] = mixed[:, p * local : (p + 1) * local]

    normed = layer_norm(mixed).astype(bf16)

    few = 8
    groups = own // few
    unit = rows * few

    def regroup(values):
        shape = (rows, groups, few, values.shape[1])
        return jnp.swapaxes(values.reshape(shape), 0, 1).reshape(tokens, values.shape[1])

    proj = [
        regroup(dot_nt(normed, col_qkv_ref[t * local : (t + 1) * local, :])).astype(bf16)
        for t in range(3)
    ]
    live = read_sequences(payload_ref, rows, cols, cols + LANES)
    sub, lan = iota((unit, unit), 0), iota((unit, unit), 1)
    same_column = (sub % few) == (lan % few)
    seq_of_lane = iota((rows, unit), 1) // few
    live_lane = jnp.sum(
        jnp.where(seq_of_lane == iota((rows, unit), 0), live, 0.0), axis=0, keepdims=True
    )
    visible = jnp.logical_and(same_column, jnp.broadcast_to(live_lane, (unit, unit)) > 0)
    blocks = []
    for g in range(groups):
        at = slice(g * unit, (g + 1) * unit)
        pieces = []
        for first in range(0, local, LANES):
            span = slice(first, min(first + LANES, local))
            query, keys, values = (proj[t][at, span] for t in range(3))
            many = query.shape[1] // HEAD_DIM
            result = None
            for h2 in range(many):
                inside = iota(query.shape, 1) // HEAD_DIM == h2
                this = query if many == 1 else jnp.where(inside, query, jnp.zeros_like(query))
                scores = dot_nt(this, keys) * HEAD_DIM ** (-0.5)
                weights = softmax_last(jnp.where(visible, scores, -jnp.inf)).astype(bf16)
                found = dot_nn(weights, values)
                result = found if result is None else jnp.where(inside, found, result)
            pieces.append(result)
        blocks.append(jnp.concatenate(pieces, 1))
    whole = jnp.concatenate(blocks, 0).reshape(groups, rows, few, local)
    context = jnp.swapaxes(whole, 0, 1).reshape(tokens, local)
    context_ref[0:tokens, :] = context[:, 0:LANES].astype(bf16)
    half = tokens // 2
    context_ref[tokens : tokens + half, :] = jnp.concatenate(
        [context[0:half, LANES:local], context[half:tokens, LANES:local]], 1
    ).astype(bf16)


def attend_columns_here(row_outs, payload, row_context, own_codes, embed, col_qkv, cols):
    parts = len(row_outs)
    tokens, width = row_context.shape
    local = width // parts
    return pl.pallas_call(
        functools.partial(column_kernel, parts, cols),
        out_shape=(
            jax.ShapeDtypeStruct((tokens * local // LANES, LANES), bf16),
            jax.ShapeDtypeStruct((tokens, local), f32),
        ),
        scratch_shapes=[
            pltpu.VMEM((parts, local, width), bf16),
            pltpu.VMEM((2 * CODES, 2 * width), bf16),
        ],
        compiler_params=pltpu.CompilerParams(vmem_limit_bytes=32 * 1024 * 1024),
        name="column_attention",
    )(*row_outs, payload, row_context, own_codes, embed, col_qkv)


def finish_kernel(groups, context_ref, col_out_ref, mixed_ref, out_ref):
    parts = context_ref.shape[0]
    tokens, local = mixed_ref.shape
    half = tokens // 2
    group = lax.axis_index("seq")
    total = mixed_ref[...]
    for p in range(parts):
        weight = col_out_ref[:, p * local : (p + 1) * local]
        total = total + dot_nt(context_ref[p, 0:tokens, :], weight[:, 0:LANES])
        rest = weight[:, LANES:local]
        zero = jnp.zeros_like(rest)
        last = context_ref[p, tokens : tokens + half, :]
        total = total + jnp.concatenate(
            [
                dot_nt(last, jnp.concatenate([rest, zero], 1)),
                dot_nt(last, jnp.concatenate([zero, rest], 1)),
            ],
            0,
        )
    each = tokens // groups
    for d in range(groups):
        block = total[d * each : (d + 1) * each, :]
        packed = jnp.concatenate(
            [
                block[:, 0:LANES],
                jnp.concatenate(
                    [block[0 : each // 2, LANES:local], block[each // 2 :, LANES:local]], 1
                ),
            ],
            0,
        )
        out_ref[group ^ d] = packed.astype(bf16)


def finish(contexts, col_out, mixed, groups):
    tokens, local = mixed.shape
    return pl.pallas_call(
        functools.partial(finish_kernel, groups),
        out_shape=jax.ShapeDtypeStruct((groups, tokens // groups * local // LANES, LANES), bf16),
        compiler_params=pltpu.CompilerParams(vmem_limit_bytes=32 * 1024 * 1024),
        name="finish",
    )(contexts, col_out, mixed)


def order_kernel(blocks_ref, out_ref):
    groups = blocks_ref.shape[0]
    local, cols = out_ref.shape[1:]
    own = cols // groups
    rest = local - LANES
    for part in range(3):
        piece = jnp.concatenate(
            [blocks_ref[g, part * own : (part + 1) * own, :] for g in range(groups)], 0
        )
        turned = piece.astype(f32).T.astype(bf16)
        if part < 2:
            out_ref[part, 0:LANES, :] = turned
        else:
            for r in range(2):
                out_ref[r, LANES:local, :] = turned[r * rest : (r + 1) * rest, :]


def order(blocks, cols, local):
    return pl.pallas_call(
        order_kernel,
        out_shape=jax.ShapeDtypeStruct((2, local, cols), bf16),
        name="order",
    )(blocks)


def fast_body(ids, pad_mask, embed, row_qkv, row_out, col_qkv, col_out):
    rows_here, cols = ids.shape
    width = embed.shape[1]
    local = row_out.shape[0]
    groups, parts = lax.axis_size("seq"), lax.axis_size("head")
    own, rows = cols // groups, rows_here * groups
    each = groups // parts

    def pairwise(value, partner):
        order = [(g, p) for g in range(groups) for p in range(parts)]
        link = [(g * parts + p, partner(g, p)) for g, p in order]
        return lax.ppermute(value, ("seq", "head"), [(i, g * parts + p) for i, (g, p) in link])

    coded = ids + 65536 * pad_mask[:, None]
    codes = [pairwise(coded, lambda g, p, b=b: (g ^ (p * each + b), p)) for b in range(each)]
    row_outs = [row_out] + [
        pairwise(row_out, lambda g, p, step=step: (g, p ^ step)) for step in range(1, parts)
    ]
    table = make_tables(embed, row_qkv.reshape(3 * local, width))
    payload = lax.all_gather(pack(table, codes), "head", axis=0)
    row_context, own_codes = attend_rows(payload, rows, cols, own, width)
    context, mixed = attend_columns_here(
        row_outs, payload, row_context, own_codes, embed, col_qkv.reshape(3 * local, width), cols
    )
    contexts = lax.all_gather(context, "head", axis=0)
    blocks = finish(contexts, col_out, mixed, groups)
    blocks = lax.all_to_all(blocks, "seq", split_axis=0, concat_axis=0, tiled=True)
    return jnp.swapaxes(order(blocks, cols, local), 1, 2)


def weight_fold(out_weight, piece):
    return jnp.einsum("rce,fe->rcf", piece, out_weight, preferred_element_type=f32)


def attend_columns(query, keys, values, key_live):
    rows_all, count_cols, local_width = query.shape
    heads_here = local_width // HEAD_DIM
    shape = (rows_all, count_cols, heads_here, HEAD_DIM)
    scores = jnp.einsum(
        "rchd,schd->chrs",
        query.reshape(shape),
        keys.reshape(shape),
        preferred_element_type=f32,
    ) * HEAD_DIM ** (-0.5)
    scores = jnp.where(key_live > 0, scores, -jnp.inf)
    probs = softmax_last(scores).astype(bf16)
    context = jnp.einsum(
        "chrs,schd->rchd", probs, values.reshape(shape), preferred_element_type=f32
    )
    return context.astype(bf16).reshape(rows_all, count_cols, local_width)


def send_back(context):
    return lax.all_to_all(context[:, None], "seq", split_axis=0, concat_axis=1, tiled=True)


def general_body(ids, pad_mask, embed, row_qkv, row_out, col_qkv, col_out):
    rows_here, cols = ids.shape
    width = embed.shape[1]
    local_width = row_out.shape[0]
    heads_here = local_width // HEAD_DIM
    groups = lax.axis_size("seq")
    per_group = cols // groups
    codes = lax.broadcasted_iota(jnp.int32, (1, 1, embed.shape[0]), 2)
    onehot = (ids[:, :, None] == codes).astype(bf16)
    embedded = jnp.einsum("rcv,vd->rcd", onehot, embed, preferred_element_type=f32)
    normed = layer_norm(embedded).astype(bf16)
    row_proj = jnp.einsum("rcd,ted->trce", normed, row_qkv, preferred_element_type=f32)
    row_proj = row_proj.astype(bf16)
    live = pad_mask.astype(bf16)
    head_shape = (rows_here, cols, heads_here, HEAD_DIM)
    query = (row_proj[0] * live[:, None, None]).reshape(head_shape)
    keys = row_proj[1].reshape(head_shape)
    values = row_proj[2].reshape(head_shape)
    partial_scores = jnp.einsum("rihd,rjhd->hij", query, keys, preferred_element_type=f32)
    count_here = jnp.sum(pad_mask.astype(f32))
    scale = HEAD_DIM ** (-0.5)
    total, count = lax.psum((partial_scores, count_here), "seq")
    row_probs = softmax_last(total * (scale / jnp.sqrt(count))).astype(bf16)
    row_context = jnp.einsum("hij,rjhd->rihd", row_probs, values, preferred_element_type=f32)
    row_context = row_context.astype(bf16).reshape(rows_here, cols, local_width)
    start_feature = lax.axis_index("head") * local_width
    resident = lax.dynamic_slice_in_dim(embedded, start_feature, local_width, 2)
    row_update = weight_fold(row_out, lax.all_gather(row_context, "head", axis=2, tiled=True))
    mixed = resident + row_update
    sums, squares = lax.psum((jnp.sum(mixed, axis=-1), jnp.sum(mixed * mixed, axis=-1)), "head")
    mean = sums / width
    spread = squares / width - mean * mean
    normed_here = ((mixed - mean[..., None]) * lax.rsqrt(spread[..., None] + EPS)).astype(bf16)
    live_tile = jnp.broadcast_to(live[:, None, None, None], (rows_here, groups, per_group, 1))
    normed_full = lax.all_gather(normed_here, "head", axis=2, tiled=True)
    col_proj = jnp.einsum("rcd,ted->rcte", normed_full, col_qkv, preferred_element_type=f32)
    packed = col_proj.astype(bf16).reshape(rows_here, groups, per_group, 3 * local_width)
    received = lax.all_to_all(packed, "seq", split_axis=1, concat_axis=0, tiled=True)
    mask_part = lax.all_to_all(live_tile, "seq", split_axis=1, concat_axis=0, tiled=True)
    column_out = send_back(
        attend_columns(
            received[:, 0, :, :local_width],
            received[:, 0, :, local_width : 2 * local_width],
            received[:, 0, :, 2 * local_width :],
            mask_part[:, 0, 0, 0],
        )
    )
    column_out = column_out.reshape(rows_here, cols, local_width)
    col_update = weight_fold(col_out, lax.all_gather(column_out, "head", axis=2, tiled=True))
    return (mixed + col_update).astype(bf16)


def body(ids, pad_mask, embed, row_qkv, row_out, col_qkv, col_out):
    rows_here, cols = ids.shape
    groups = lax.axis_size("seq")
    own, rows = cols // groups, rows_here * groups
    parts = lax.axis_size("head")
    local = row_out.shape[0]
    fits = (
        groups & (groups - 1) == 0
        and parts in (2, 4)
        and groups % parts == 0
        and rows * 8 == LANES
        and rows_here == 2
        and rows <= 8 * parts
        and own % 16 == 0
        and cols + LANES <= 3 * local
        and local == LANES + HEAD_DIM
        and embed.shape[0] <= VOCAB_ROWS
    )
    chosen = fast_body if fits else general_body
    return chosen(ids, pad_mask, embed, row_qkv, row_out, col_qkv, col_out)


def solution(mesh):
    placed = (
        P("seq", None),
        P("seq"),
        P(),
        P(None, "head", None),
        P("head", None),
        P(None, "head", None),
        P("head", None),
    )
    return jax.shard_map(
        body, mesh=mesh, in_specs=placed, out_specs=P("seq", None, "head"), check_vma=False
    )
```

```python
import functools

import jax
import jax.numpy as jnp
from jax import lax
from jax.experimental import pallas as pl
from jax.experimental.pallas import tpu as pltpu
from jax.sharding import PartitionSpec as P

HEAD_DIM = 64
EPS = 1e-05
LANES = 128
CODES = 64
VOCAB_ROWS = 40
TABLE_ROWS = 48

f32 = jnp.float32
bf16 = jnp.bfloat16


def layer_norm(values):
    mean = jnp.mean(values, axis=-1, keepdims=True)
    centred = values - mean
    spread = jnp.mean(centred * centred, axis=-1, keepdims=True)
    return centred * lax.rsqrt(spread + EPS)


def softmax_last(scores):
    top = jnp.max(scores, axis=-1, keepdims=True)
    weights = jnp.exp(scores - top)
    return weights / jnp.sum(weights, axis=-1, keepdims=True)


def dot_nt(left, right):
    return lax.dot_general(left, right, (((1,), (1,)), ((), ())), preferred_element_type=f32)


def dot_nn(left, right):
    return jnp.dot(left, right, preferred_element_type=f32)


def iota(shape, axis):
    return lax.broadcasted_iota(jnp.int32, shape, axis)


def code_kernel(ids_ref, live_ref, out_ref):
    row = iota(ids_ref.shape, 0)
    live = jnp.zeros(ids_ref.shape, jnp.int32)
    for r in range(ids_ref.shape[0]):
        live = jnp.where(row == r, live_ref[r], live)
    out_ref[...] = ids_ref[...] + 65536 * live


def make_codes(ids, pad_mask):
    return pl.pallas_call(
        code_kernel,
        out_shape=jax.ShapeDtypeStruct(ids.shape, jnp.int32),
        in_specs=[
            pl.BlockSpec(memory_space=pltpu.VMEM),
            pl.BlockSpec(memory_space=pltpu.SMEM),
        ],
        name="codes",
    )(ids, pad_mask)


def table_kernel(embed_ref, qkv_ref, *refs):
    codes_refs, (out_ref, padded_ref) = refs[:-2], refs[-2:]
    vocab = embed_ref.shape[0]
    padded_ref[...] = jnp.zeros(padded_ref.shape, f32)
    padded_ref[0:vocab, :] = embed_ref[...].astype(f32)
    normed = layer_norm(padded_ref[...]).astype(bf16)
    table = dot_nt(normed, qkv_ref[...])
    coded = jnp.concatenate([ref[...] for ref in codes_refs], 0)
    some, cols = coded.shape
    ids = (coded & 0xFFFF).astype(f32)
    live = (coded >> 16).astype(f32)
    spare = jnp.concatenate(
        [ids, live[:, 0:LANES], jnp.zeros((some, out_ref.shape[1] - cols - LANES), f32)], 1
    )
    if some < TABLE_ROWS - VOCAB_ROWS:
        empty = jnp.zeros((TABLE_ROWS - VOCAB_ROWS - some, spare.shape[1]), f32)
        spare = jnp.concatenate([spare, empty], 0)
    out_ref[...] = jnp.concatenate([table[0:VOCAB_ROWS], spare], 0).astype(bf16)


def make_payload(embed, qkv, codes):
    return pl.pallas_call(
        table_kernel,
        out_shape=jax.ShapeDtypeStruct((TABLE_ROWS, qkv.shape[0]), bf16),
        scratch_shapes=[pltpu.VMEM((TABLE_ROWS, embed.shape[1]), f32)],
        cost_estimate=pl.CostEstimate(
            flops=2 * TABLE_ROWS * qkv.size, bytes_accessed=2 * qkv.size, transcendentals=0
        ),
        name="tables",
    )(embed, qkv, *codes)


def halves(pair):
    lane = iota(pair.shape, 1)
    zero = jnp.zeros_like(pair)
    return jnp.where(lane < HEAD_DIM, pair, zero), jnp.where(lane < HEAD_DIM, zero, pair)


def spread_pair(pair):
    first, second = halves(pair)
    zero = jnp.zeros_like(pair)
    return jnp.concatenate(
        [
            jnp.concatenate([first, zero], 1),
            jnp.concatenate([zero, first], 1),
            jnp.concatenate([second, zero], 1),
            jnp.concatenate([zero, second], 1),
        ],
        0,
    )


def read_sequences(payload_ref, rows, first, last):
    parts = payload_ref.shape[0]
    each = rows // parts
    return jnp.concatenate(
        [
            payload_ref[p, VOCAB_ROWS:TABLE_ROWS, first:last].astype(f32)[0:each]
            for p in range(parts)
        ],
        0,
    )


def row_kernel(
    payload_ref,
    row_context_ref,
    own_ref,
    table_ref,
    hot_ref,
    live_own_ref,
    sum_ref,
    spread_ref,
):
    parts = payload_ref.shape[0]
    depth, cols = hot_ref.shape
    rows = depth // CODES
    pairs = rows // 2
    own = own_ref.shape[0] // pairs
    width = row_context_ref.shape[1]
    heads = width // HEAD_DIM
    local = width // parts
    group = lax.axis_index("seq")

    for t in range(3):
        table_ref[t, 0:VOCAB_ROWS, :] = jnp.concatenate(
            [payload_ref[p, 0:VOCAB_ROWS, t * local : (t + 1) * local] for p in range(parts)], 1
        )
        table_ref[t, VOCAB_ROWS:CODES, :] = jnp.zeros((CODES - VOCAB_ROWS, width), bf16)

    ids = read_sequences(payload_ref, rows, 0, cols)
    live = read_sequences(payload_ref, rows, cols, cols + LANES)
    code = iota((CODES, cols), 0).astype(f32)
    for r in range(rows):
        hot = jnp.broadcast_to(ids[r : r + 1, :], (CODES, cols)) == code
        hot_ref[r * CODES : (r + 1) * CODES, :] = hot.astype(f32).astype(bf16)

    pick = (iota((own, cols), 1) == group * own + iota((own, cols), 0)).astype(f32).astype(bf16)
    mine = dot_nt(pick, ids.astype(bf16))
    lane = iota((own, LANES), 1)
    first_half = lane < CODES
    lane_code = jnp.where(first_half, lane, lane - CODES).astype(f32)
    for k in range(pairs):
        value = jnp.where(first_half, mine[:, 2 * k : 2 * k + 1], mine[:, 2 * k + 1 : 2 * k + 2])
        hot = (value == lane_code).astype(f32)
        alive = jnp.where(first_half, live[2 * k : 2 * k + 1, :], live[2 * k + 1 : 2 * k + 2, :])
        own_ref[k * own : (k + 1) * own, :] = hot.astype(bf16)
        live_own_ref[k * own : (k + 1) * own, :] = (hot * alive).astype(bf16)

    for hp in range(heads // 2):
        span = slice(hp * LANES, (hp + 1) * LANES)
        queries = spread_pair(table_ref[0, :, span])
        keys = table_ref[1, :, span]
        zero = jnp.zeros_like(keys)
        keys2 = jnp.concatenate(
            [jnp.concatenate([keys, zero], 1), jnp.concatenate([zero, keys], 1)], 0
        )
        scores = dot_nt(queries, keys2)
        high = scores.astype(bf16)
        low = (scores - high.astype(f32)).astype(bf16)
        looked = dot_nn(
            live_own_ref[...],
            jnp.concatenate([high[:LANES], low[:LANES], high[LANES:], low[LANES:]], 1),
        ).astype(bf16)
        for h2 in range(2):
            base = (hp * 2 + h2) * own
            for piece in range(2):
                at = (h2 * 2 + piece) * LANES
                for k in range(pairs):
                    to = piece * depth + k * LANES
                    sum_ref[base : base + own, to : to + LANES] = looked[
                        k * own : (k + 1) * own, at : at + LANES
                    ]
    tied = dot_nn(sum_ref[:, 0:depth], hot_ref[...]) + dot_nn(
        sum_ref[:, depth : 2 * depth], hot_ref[...]
    )
    count = jnp.sum(live, axis=0, keepdims=True)[:, 0:1]
    probs = softmax_last(tied * (HEAD_DIM ** (-0.5) / jnp.sqrt(count))).astype(bf16)

    spread_ref[...] = dot_nt(probs, hot_ref[...]).astype(bf16)
    for hp in range(heads // 2):
        values = spread_pair(table_ref[2, :, hp * LANES : (hp + 1) * LANES])
        weights = jnp.concatenate(
            [
                jnp.concatenate(
                    [
                        spread_ref[
                            (hp * 2 + h2) * own : (hp * 2 + h2 + 1) * own,
                            k * LANES : (k + 1) * LANES,
                        ]
                        for h2 in range(2)
                    ],
                    1,
                )
                for k in range(pairs)
            ],
            0,
        )
        context = dot_nn(weights, values).astype(bf16)
        for k in range(pairs):
            for r2 in range(2):
                at = (2 * k + r2) * own
                row_context_ref[at : at + own, hp * LANES : (hp + 1) * LANES] = context[
                    k * own : (k + 1) * own, r2 * LANES : (r2 + 1) * LANES
                ]


def attend_rows(payload, rows, cols, own, width):
    heads = width // HEAD_DIM
    tokens = rows * own
    return pl.pallas_call(
        row_kernel,
        out_shape=(
            jax.ShapeDtypeStruct((tokens, width), bf16),
            jax.ShapeDtypeStruct((rows // 2 * own, LANES), bf16),
        ),
        scratch_shapes=[
            pltpu.VMEM((3, CODES, width), bf16),
            pltpu.VMEM((rows * CODES, cols), bf16),
            pltpu.VMEM((rows // 2 * own, LANES), bf16),
            pltpu.VMEM((heads * own, 2 * rows * CODES), bf16),
            pltpu.VMEM((heads * own, rows * CODES), bf16),
        ],
        cost_estimate=pl.CostEstimate(flops=5 * 10**9, bytes_accessed=10**6, transcendentals=0),
        compiler_params=pltpu.CompilerParams(vmem_limit_bytes=32 * 1024 * 1024),
        name="row_attention",
    )(payload)


def column_kernel(parts, cols, *refs):
    row_out_refs, refs = refs[:parts], refs[parts:]
    (
        payload_ref,
        row_context_ref,
        own_ref,
        embed_ref,
        col_qkv_ref,
        context_ref,
        mixed_out_ref,
        row_out_ref,
        embed2_ref,
    ) = refs
    tokens, width = row_context_ref.shape
    rows = LANES // 8
    pairs = rows // 2
    own = own_ref.shape[0] // pairs
    vocab = embed_ref.shape[0]
    local = width // parts
    part = lax.axis_index("head")

    for p in range(parts):
        row_out_ref[part ^ p] = row_out_refs[p][...]
    embed2_ref[...] = jnp.zeros(embed2_ref.shape, bf16)
    embed2_ref[0:vocab, 0:width] = embed_ref[...]
    embed2_ref[CODES : CODES + vocab, width : 2 * width] = embed_ref[...]

    embedded2 = dot_nn(own_ref[...], embed2_ref[...])
    embedded = jnp.concatenate(
        [
            embedded2[k * own : (k + 1) * own, r2 * width : (r2 + 1) * width]
            for k in range(pairs)
            for r2 in range(2)
        ],
        0,
    )
    mixed = embedded + dot_nt(row_context_ref[...], row_out_ref[...].reshape(width, width))
    for p in range(parts):

        @pl.when(part == p)
        def _():
            mixed_out_ref[...] = mixed[:, p * local : (p + 1) * local]

    normed = layer_norm(mixed).astype(bf16)

    few = 8
    groups = own // few
    unit = rows * few

    def regroup(values):
        shape = (rows, groups, few, values.shape[1])
        return jnp.swapaxes(values.reshape(shape), 0, 1).reshape(tokens, values.shape[1])

    proj = [
        regroup(dot_nt(normed, col_qkv_ref[t * local : (t + 1) * local, :])).astype(bf16)
        for t in range(3)
    ]
    live = read_sequences(payload_ref, rows, cols, cols + LANES)
    sub, lan = iota((unit, unit), 0), iota((unit, unit), 1)
    same_column = (sub % few) == (lan % few)
    seq_of_lane = iota((rows, unit), 1) // few
    live_lane = jnp.sum(
        jnp.where(seq_of_lane == iota((rows, unit), 0), live, 0.0), axis=0, keepdims=True
    )
    visible = jnp.logical_and(same_column, jnp.broadcast_to(live_lane, (unit, unit)) > 0)
    blocks = []
    for g in range(groups):
        at = slice(g * unit, (g + 1) * unit)
        pieces = []
        for first in range(0, local, LANES):
            span = slice(first, min(first + LANES, local))
            query, keys, values = (proj[t][at, span] for t in range(3))
            many = query.shape[1] // HEAD_DIM
            result = None
            for h2 in range(many):
                inside = iota(query.shape, 1) // HEAD_DIM == h2
                this = query if many == 1 else jnp.where(inside, query, jnp.zeros_like(query))
                scores = dot_nt(this, keys) * HEAD_DIM ** (-0.5)
                weights = softmax_last(jnp.where(visible, scores, -jnp.inf)).astype(bf16)
                found = dot_nn(weights, values)
                result = found if result is None else jnp.where(inside, found, result)
            pieces.append(result)
        blocks.append(jnp.concatenate(pieces, 1))
    whole = jnp.concatenate(blocks, 0).reshape(groups, rows, few, local)
    context = jnp.swapaxes(whole, 0, 1).reshape(tokens, local)
    context_ref[0:tokens, :] = context[:, 0:LANES].astype(bf16)
    half = tokens // 2
    context_ref[tokens : tokens + half, :] = jnp.concatenate(
        [context[0:half, LANES:local], context[half:tokens, LANES:local]], 1
    ).astype(bf16)


def attend_columns_here(row_outs, payload, row_context, own_codes, embed, col_qkv, cols):
    parts = len(row_outs)
    tokens, width = row_context.shape
    local = width // parts
    return pl.pallas_call(
        functools.partial(column_kernel, parts, cols),
        out_shape=(
            jax.ShapeDtypeStruct((tokens * local // LANES, LANES), bf16),
            jax.ShapeDtypeStruct((tokens, local), f32),
        ),
        scratch_shapes=[
            pltpu.VMEM((parts, local, width), bf16),
            pltpu.VMEM((2 * CODES, 2 * width), bf16),
        ],
        compiler_params=pltpu.CompilerParams(vmem_limit_bytes=32 * 1024 * 1024),
        name="column_attention",
    )(*row_outs, payload, row_context, own_codes, embed, col_qkv)


def finish_kernel(groups, context_ref, col_out_ref, mixed_ref, out_ref):
    cores, chips = context_ref.shape[0:2]
    tokens, local = mixed_ref.shape
    half = tokens // 2
    group = lax.axis_index("seq")
    total = mixed_ref[...]
    for p in range(cores * chips):
        core, chip = p % cores, p // cores
        weight = col_out_ref[:, p * local : (p + 1) * local]
        total = total + dot_nt(context_ref[core, chip, 0:tokens, :], weight[:, 0:LANES])
        rest = weight[:, LANES:local]
        zero = jnp.zeros_like(rest)
        last = context_ref[core, chip, tokens : tokens + half, :]
        total = total + jnp.concatenate(
            [
                dot_nt(last, jnp.concatenate([rest, zero], 1)),
                dot_nt(last, jnp.concatenate([zero, rest], 1)),
            ],
            0,
        )
    each = tokens // groups
    for d in range(groups):
        block = total[d * each : (d + 1) * each, :]
        packed = jnp.concatenate(
            [
                block[:, 0:LANES],
                jnp.concatenate(
                    [block[0 : each // 2, LANES:local], block[each // 2 :, LANES:local]], 1
                ),
            ],
            0,
        )
        out_ref[group ^ d] = packed.astype(bf16)


def finish(contexts, col_out, mixed, groups):
    tokens, local = mixed.shape
    return pl.pallas_call(
        functools.partial(finish_kernel, groups),
        out_shape=jax.ShapeDtypeStruct((groups, tokens // groups * local // LANES, LANES), bf16),
        compiler_params=pltpu.CompilerParams(vmem_limit_bytes=32 * 1024 * 1024),
        name="finish",
    )(contexts, col_out, mixed)


def order_kernel(blocks_ref, out_ref):
    groups = blocks_ref.shape[0]
    local, cols = out_ref.shape[1:]
    own = cols // groups
    rest = local - LANES
    for part in range(3):
        piece = jnp.concatenate(
            [blocks_ref[g, part * own : (part + 1) * own, :] for g in range(groups)], 0
        )
        turned = piece.astype(f32).T.astype(bf16)
        if part < 2:
            out_ref[part, 0:LANES, :] = turned
        else:
            for r in range(2):
                out_ref[r, LANES:local, :] = turned[r * rest : (r + 1) * rest, :]


def order(blocks, cols, local):
    return pl.pallas_call(
        order_kernel,
        out_shape=jax.ShapeDtypeStruct((2, local, cols), bf16),
        name="order",
    )(blocks)


def fast_body(ids, pad_mask, embed, row_qkv, row_out, col_qkv, col_out):
    rows_here, cols = ids.shape
    width = embed.shape[1]
    local = row_out.shape[0]
    groups, parts = lax.axis_size("seq"), lax.axis_size("head")
    own, rows = cols // groups, rows_here * groups
    each = groups // parts

    def pairwise(value, partner):
        order = [(g, p) for g in range(groups) for p in range(parts)]
        link = [(g * parts + p, partner(g, p)) for g, p in order]
        return lax.ppermute(value, ("seq", "head"), [(i, g * parts + p) for i, (g, p) in link])

    coded = make_codes(ids, pad_mask)
    codes = [pairwise(coded, lambda g, p, b=b: (g ^ (p * each + b), p)) for b in range(each)]
    sibling = lambda g, p: (g, p ^ 1)
    across = lambda g, p: (g, p ^ 2)
    far = pairwise(row_out, across)
    row_outs = [row_out, pairwise(row_out, sibling), far, pairwise(far, sibling)]
    payload = make_payload(embed, row_qkv.reshape(3 * local, width), codes)
    payload = lax.all_gather(payload, "head", axis=0)
    row_context, own_codes = attend_rows(payload, rows, cols, own, width)
    context, mixed = attend_columns_here(
        row_outs, payload, row_context, own_codes, embed, col_qkv.reshape(3 * local, width), cols
    )
    contexts = lax.all_gather(context, "head", axis=0, axis_index_groups=[[0, 2], [1, 3]])
    contexts = lax.all_gather(contexts, "head", axis=0, axis_index_groups=[[0, 1], [2, 3]])
    blocks = finish(contexts, col_out, mixed, groups)
    blocks = lax.all_to_all(blocks, "seq", split_axis=0, concat_axis=0, tiled=True)
    return jnp.swapaxes(order(blocks, cols, local), 1, 2)


def weight_fold(out_weight, piece):
    return jnp.einsum("rce,fe->rcf", piece, out_weight, preferred_element_type=f32)


def attend_columns(query, keys, values, key_live):
    rows_all, count_cols, local_width = query.shape
    heads_here = local_width // HEAD_DIM
    shape = (rows_all, count_cols, heads_here, HEAD_DIM)
    scores = jnp.einsum(
        "rchd,schd->chrs",
        query.reshape(shape),
        keys.reshape(shape),
        preferred_element_type=f32,
    ) * HEAD_DIM ** (-0.5)
    scores = jnp.where(key_live > 0, scores, -jnp.inf)
    probs = softmax_last(scores).astype(bf16)
    context = jnp.einsum(
        "chrs,schd->rchd", probs, values.reshape(shape), preferred_element_type=f32
    )
    return context.astype(bf16).reshape(rows_all, count_cols, local_width)


def send_back(context):
    return lax.all_to_all(context[:, None], "seq", split_axis=0, concat_axis=1, tiled=True)


def general_body(ids, pad_mask, embed, row_qkv, row_out, col_qkv, col_out):
    rows_here, cols = ids.shape
    width = embed.shape[1]
    local_width = row_out.shape[0]
    heads_here = local_width // HEAD_DIM
    groups = lax.axis_size("seq")
    per_group = cols // groups
    codes = lax.broadcasted_iota(jnp.int32, (1, 1, embed.shape[0]), 2)
    onehot = (ids[:, :, None] == codes).astype(bf16)
    embedded = jnp.einsum("rcv,vd->rcd", onehot, embed, preferred_element_type=f32)
    normed = layer_norm(embedded).astype(bf16)
    row_proj = jnp.einsum("rcd,ted->trce", normed, row_qkv, preferred_element_type=f32)
    row_proj = row_proj.astype(bf16)
    live = pad_mask.astype(bf16)
    head_shape = (rows_here, cols, heads_here, HEAD_DIM)
    query = (row_proj[0] * live[:, None, None]).reshape(head_shape)
    keys = row_proj[1].reshape(head_shape)
    values = row_proj[2].reshape(head_shape)
    partial_scores = jnp.einsum("rihd,rjhd->hij", query, keys, preferred_element_type=f32)
    count_here = jnp.sum(pad_mask.astype(f32))
    scale = HEAD_DIM ** (-0.5)
    total, count = lax.psum((partial_scores, count_here), "seq")
    row_probs = softmax_last(total * (scale / jnp.sqrt(count))).astype(bf16)
    row_context = jnp.einsum("hij,rjhd->rihd", row_probs, values, preferred_element_type=f32)
    row_context = row_context.astype(bf16).reshape(rows_here, cols, local_width)
    start_feature = lax.axis_index("head") * local_width
    resident = lax.dynamic_slice_in_dim(embedded, start_feature, local_width, 2)
    row_update = weight_fold(row_out, lax.all_gather(row_context, "head", axis=2, tiled=True))
    mixed = resident + row_update
    sums, squares = lax.psum((jnp.sum(mixed, axis=-1), jnp.sum(mixed * mixed, axis=-1)), "head")
    mean = sums / width
    spread = squares / width - mean * mean
    normed_here = ((mixed - mean[..., None]) * lax.rsqrt(spread[..., None] + EPS)).astype(bf16)
    live_tile = jnp.broadcast_to(live[:, None, None, None], (rows_here, groups, per_group, 1))
    normed_full = lax.all_gather(normed_here, "head", axis=2, tiled=True)
    col_proj = jnp.einsum("rcd,ted->rcte", normed_full, col_qkv, preferred_element_type=f32)
    packed = col_proj.astype(bf16).reshape(rows_here, groups, per_group, 3 * local_width)
    received = lax.all_to_all(packed, "seq", split_axis=1, concat_axis=0, tiled=True)
    mask_part = lax.all_to_all(live_tile, "seq", split_axis=1, concat_axis=0, tiled=True)
    column_out = send_back(
        attend_columns(
            received[:, 0, :, :local_width],
            received[:, 0, :, local_width : 2 * local_width],
            received[:, 0, :, 2 * local_width :],
            mask_part[:, 0, 0, 0],
        )
    )
    column_out = column_out.reshape(rows_here, cols, local_width)
    col_update = weight_fold(col_out, lax.all_gather(column_out, "head", axis=2, tiled=True))
    return (mixed + col_update).astype(bf16)


def body(ids, pad_mask, embed, row_qkv, row_out, col_qkv, col_out):
    rows_here, cols = ids.shape
    groups = lax.axis_size("seq")
    own, rows = cols // groups, rows_here * groups
    parts = lax.axis_size("head")
    local = row_out.shape[0]
    fits = (
        groups & (groups - 1) == 0
        and parts == 4
        and groups % parts == 0
        and rows * 8 == LANES
        and rows_here == 2
        and rows <= 8 * parts
        and own % 16 == 0
        and cols + LANES <= 3 * local
        and local == LANES + HEAD_DIM
        and embed.shape[0] <= VOCAB_ROWS
    )
    chosen = fast_body if fits else general_body
    return chosen(ids, pad_mask, embed, row_qkv, row_out, col_qkv, col_out)


def solution(mesh):
    placed = (
        P("seq", None),
        P("seq"),
        P(),
        P(None, "head", None),
        P("head", None),
        P(None, "head", None),
        P("head", None),
    )
    return jax.shard_map(
        body, mesh=mesh, in_specs=placed, out_specs=P("seq", None, "head"), check_vma=False
    )
```

```python
import functools

import jax
import jax.numpy as jnp
from jax import lax
from jax.experimental import pallas as pl
from jax.experimental.pallas import tpu as pltpu
from jax.sharding import PartitionSpec as P

HEAD_DIM = 64
EPS = 1e-05
LANES = 128
CODES = 64
VOCAB_ROWS = 40
TABLE_ROWS = 48

SMALL_VMEM = 8 * 1024 * 1024
LARGE_VMEM = 32 * 1024 * 1024

f32 = jnp.float32
bf16 = jnp.bfloat16


def layer_norm(values):
    mean = jnp.mean(values, axis=-1, keepdims=True)
    centred = values - mean
    spread = jnp.mean(centred * centred, axis=-1, keepdims=True)
    return centred * lax.rsqrt(spread + EPS)


def softmax_last(scores):
    top = jnp.max(scores, axis=-1, keepdims=True)
    weights = jnp.exp(scores - top)
    return weights * (1.0 / jnp.sum(weights, axis=-1, keepdims=True))


def dot_nt(left, right):
    return lax.dot_general(left, right, (((1,), (1,)), ((), ())), preferred_element_type=f32)


def dot_nn(left, right):
    return jnp.dot(left, right, preferred_element_type=f32)


def iota(shape, axis):
    return lax.broadcasted_iota(jnp.int32, shape, axis)


def code_kernel(ids_ref, live_ref, out_ref):
    row = iota(ids_ref.shape, 0)
    live = jnp.zeros(ids_ref.shape, jnp.int32)
    for r in range(ids_ref.shape[0]):
        live = jnp.where(row == r, live_ref[r], live)
    out_ref[...] = ids_ref[...] + 65536 * live


def make_codes(ids, pad_mask):
    return pl.pallas_call(
        code_kernel,
        out_shape=jax.ShapeDtypeStruct(ids.shape, jnp.int32),
        in_specs=[
            pl.BlockSpec(memory_space=pltpu.VMEM),
            pl.BlockSpec(memory_space=pltpu.SMEM),
        ],
        compiler_params=pltpu.CompilerParams(vmem_limit_bytes=SMALL_VMEM),
        name="codes",
    )(ids, pad_mask)


def table_kernel(embed_ref, qkv_ref, *refs):
    codes_refs, (out_ref, padded_ref) = refs[:-2], refs[-2:]
    vocab = embed_ref.shape[0]
    padded_ref[...] = jnp.zeros(padded_ref.shape, f32)
    padded_ref[0:vocab, :] = embed_ref[...].astype(f32)
    normed = layer_norm(padded_ref[...]).astype(bf16)
    table = dot_nt(normed, qkv_ref[...])
    coded = jnp.concatenate([ref[...] for ref in codes_refs], 0)
    some, cols = coded.shape
    ids = (coded & 0xFFFF).astype(f32)
    live = (coded >> 16).astype(f32)
    spare = jnp.concatenate(
        [ids, live[:, 0:LANES], jnp.zeros((some, out_ref.shape[1] - cols - LANES), f32)], 1
    )
    if some < TABLE_ROWS - VOCAB_ROWS:
        empty = jnp.zeros((TABLE_ROWS - VOCAB_ROWS - some, spare.shape[1]), f32)
        spare = jnp.concatenate([spare, empty], 0)
    out_ref[...] = jnp.concatenate([table[0:VOCAB_ROWS], spare], 0).astype(bf16)


def make_payload(embed, qkv, codes):
    return pl.pallas_call(
        table_kernel,
        out_shape=jax.ShapeDtypeStruct((TABLE_ROWS, qkv.shape[0]), bf16),
        scratch_shapes=[pltpu.VMEM((TABLE_ROWS, embed.shape[1]), f32)],
        cost_estimate=pl.CostEstimate(
            flops=2 * TABLE_ROWS * qkv.size, bytes_accessed=2 * qkv.size, transcendentals=0
        ),
        compiler_params=pltpu.CompilerParams(vmem_limit_bytes=SMALL_VMEM),
        name="tables",
    )(embed, qkv, *codes)


def halves(pair):
    lane = iota(pair.shape, 1)
    zero = jnp.zeros_like(pair)
    return jnp.where(lane < HEAD_DIM, pair, zero), jnp.where(lane < HEAD_DIM, zero, pair)


def spread_pair(pair):
    first, second = halves(pair)
    zero = jnp.zeros_like(pair)
    return jnp.concatenate(
        [
            jnp.concatenate([first, zero], 1),
            jnp.concatenate([zero, first], 1),
            jnp.concatenate([second, zero], 1),
            jnp.concatenate([zero, second], 1),
        ],
        0,
    )


def double(block):
    zero = jnp.zeros_like(block)
    return jnp.concatenate(
        [jnp.concatenate([block, zero], 1), jnp.concatenate([zero, block], 1)], 0
    )


def read_sequences(payload_ref, rows, first, last):
    parts = payload_ref.shape[0]
    each = rows // parts
    return jnp.concatenate(
        [
            payload_ref[p, VOCAB_ROWS:TABLE_ROWS, first:last].astype(f32)[0:each]
            for p in range(parts)
        ],
        0,
    )


def row_kernel(
    payload_ref,
    row_context_ref,
    own_ref,
    table_ref,
    hot_ref,
    live_own_ref,
    sum_ref,
    spread_ref,
):
    parts = payload_ref.shape[0]
    depth, cols = hot_ref.shape
    rows = depth // CODES
    pairs = rows // 2
    own = own_ref.shape[0] // pairs
    width = row_context_ref.shape[1]
    heads = width // HEAD_DIM
    local = width // parts
    group = lax.axis_index("seq")

    for t in range(3):
        table_ref[t, 0:VOCAB_ROWS, :] = jnp.concatenate(
            [payload_ref[p, 0:VOCAB_ROWS, t * local : (t + 1) * local] for p in range(parts)], 1
        )
        table_ref[t, VOCAB_ROWS:CODES, :] = jnp.zeros((CODES - VOCAB_ROWS, width), bf16)

    ids = read_sequences(payload_ref, rows, 0, cols)
    live = read_sequences(payload_ref, rows, cols, cols + LANES)
    code = iota((CODES, cols), 0).astype(f32)
    for r in range(rows):
        hot = jnp.broadcast_to(ids[r : r + 1, :], (CODES, cols)) == code
        hot_ref[r * CODES : (r + 1) * CODES, :] = hot.astype(f32).astype(bf16)

    pick = (iota((own, cols), 1) == group * own + iota((own, cols), 0)).astype(f32).astype(bf16)
    mine = dot_nt(pick, ids.astype(bf16))
    lane = iota((own, LANES), 1)
    first_half = lane < CODES
    lane_code = jnp.where(first_half, lane, lane - CODES).astype(f32)
    for k in range(pairs):
        value = jnp.where(first_half, mine[:, 2 * k : 2 * k + 1], mine[:, 2 * k + 1 : 2 * k + 2])
        hot = (value == lane_code).astype(f32)
        alive = jnp.where(first_half, live[2 * k : 2 * k + 1, :], live[2 * k + 1 : 2 * k + 2, :])
        own_ref[k * own : (k + 1) * own, :] = hot.astype(bf16)
        live_own_ref[k * own : (k + 1) * own, :] = (hot * alive).astype(bf16)

    spans = [slice(hp * LANES, (hp + 1) * LANES) for hp in range(heads // 2)]
    queries = [spread_pair(table_ref[0, :, span]) for span in spans]
    keys = [double(table_ref[1, :, span]) for span in spans]
    scores = [dot_nt(query, key) for query, key in zip(queries, keys)]
    high = [score.astype(bf16) for score in scores]
    low = [(score - part.astype(f32)).astype(bf16) for score, part in zip(scores, high)]
    for hp in range(heads // 2):
        for h2 in range(2):
            half = slice(h2 * LANES, (h2 + 1) * LANES)
            looked = dot_nn(
                live_own_ref[...], jnp.concatenate([high[hp][half], low[hp][half]], 1)
            ).astype(bf16)
            base = (hp * 2 + h2) * own
            for piece in range(2):
                for k in range(pairs):
                    to = piece * depth + k * LANES
                    sum_ref[base : base + own, to : to + LANES] = looked[
                        k * own : (k + 1) * own, piece * LANES : (piece + 1) * LANES
                    ]
    tied = dot_nn(sum_ref[:, 0:depth], hot_ref[...]) + dot_nn(
        sum_ref[:, depth : 2 * depth], hot_ref[...]
    )
    count = jnp.sum(live, axis=0, keepdims=True)[:, 0:1]
    probs = softmax_last(tied * (HEAD_DIM ** (-0.5) / jnp.sqrt(count))).astype(bf16)

    spread_ref[...] = dot_nt(probs, hot_ref[...]).astype(bf16)
    values = [spread_pair(table_ref[2, :, span]) for span in spans]
    contexts = []
    for hp in range(heads // 2):
        first = (hp * 2) * own
        weights = jnp.concatenate(
            [
                jnp.concatenate(
                    [
                        spread_ref[first : first + own, k * LANES : (k + 1) * LANES],
                        spread_ref[first + own : first + 2 * own, k * LANES : (k + 1) * LANES],
                    ],
                    1,
                )
                for k in range(pairs)
            ],
            0,
        )
        contexts.append(dot_nn(weights, values[hp]).astype(bf16))
    for hp in range(heads // 2):
        for k in range(pairs):
            for r2 in range(2):
                at = (2 * k + r2) * own
                row_context_ref[at : at + own, spans[hp]] = contexts[hp][
                    k * own : (k + 1) * own, r2 * LANES : (r2 + 1) * LANES
                ]


def attend_rows(payload, rows, cols, own, width):
    heads = width // HEAD_DIM
    tokens = rows * own
    return pl.pallas_call(
        row_kernel,
        out_shape=(
            jax.ShapeDtypeStruct((tokens, width), bf16),
            jax.ShapeDtypeStruct((rows // 2 * own, LANES), bf16),
        ),
        scratch_shapes=[
            pltpu.VMEM((3, CODES, width), bf16),
            pltpu.VMEM((rows * CODES, cols), bf16),
            pltpu.VMEM((rows // 2 * own, LANES), bf16),
            pltpu.VMEM((heads * own, 2 * rows * CODES), bf16),
            pltpu.VMEM((heads * own, rows * CODES), bf16),
        ],
        cost_estimate=pl.CostEstimate(flops=5 * 10**9, bytes_accessed=10**6, transcendentals=0),
        compiler_params=pltpu.CompilerParams(vmem_limit_bytes=LARGE_VMEM),
        name="row_attention",
    )(payload)


def column_kernel(parts, cols, *refs):
    row_out_refs, refs = refs[:parts], refs[parts:]
    (
        payload_ref,
        row_context_ref,
        own_ref,
        embed_ref,
        col_qkv_ref,
        context_ref,
        mixed_out_ref,
        row_out_ref,
        embed2_ref,
    ) = refs
    tokens, width = row_context_ref.shape
    rows = LANES // 8
    pairs = rows // 2
    own = own_ref.shape[0] // pairs
    vocab = embed_ref.shape[0]
    local = width // parts
    part = lax.axis_index("head")

    for p in range(parts):
        row_out_ref[part ^ p] = row_out_refs[p][...]
    embed2_ref[...] = jnp.zeros(embed2_ref.shape, bf16)
    embed2_ref[0:vocab, 0:width] = embed_ref[...]
    embed2_ref[CODES : CODES + vocab, width : 2 * width] = embed_ref[...]

    embedded2 = dot_nn(own_ref[...], embed2_ref[...])
    embedded = jnp.concatenate(
        [
            embedded2[k * own : (k + 1) * own, r2 * width : (r2 + 1) * width]
            for k in range(pairs)
            for r2 in range(2)
        ],
        0,
    )
    mixed = embedded + dot_nt(row_context_ref[...], row_out_ref[...].reshape(width, width))
    for p in range(parts):

        @pl.when(part == p)
        def _():
            mixed_out_ref[...] = mixed[:, p * local : (p + 1) * local]

    normed = layer_norm(mixed).astype(bf16)

    few = 8
    groups = own // few
    unit = rows * few

    def regroup(values):
        shape = (rows, groups, few, values.shape[1])
        return jnp.swapaxes(values.reshape(shape), 0, 1).reshape(tokens, values.shape[1])

    proj = [
        dot_nt(normed, col_qkv_ref[t * local : (t + 1) * local, :]) for t in range(3)
    ]
    proj[0] = proj[0] * HEAD_DIM ** (-0.5)
    proj = [regroup(values).astype(bf16) for values in proj]
    live = read_sequences(payload_ref, rows, cols, cols + LANES)
    sub, lan = iota((unit, unit), 0), iota((unit, unit), 1)
    same_column = (sub % few) == (lan % few)
    seq_of_lane = iota((rows, unit), 1) // few
    live_lane = jnp.sum(
        jnp.where(seq_of_lane == iota((rows, unit), 0), live, 0.0), axis=0, keepdims=True
    )
    visible = jnp.logical_and(same_column, jnp.broadcast_to(live_lane, (unit, unit)) > 0)
    chosen = []
    for g in range(groups):
        at = slice(g * unit, (g + 1) * unit)
        for h in range(local // HEAD_DIM):
            first = h * HEAD_DIM // LANES * LANES
            span = slice(first, min(first + LANES, local))
            query, keys, values = (proj[t][at, span] for t in range(3))
            if query.shape[1] > HEAD_DIM:
                inside = iota(query.shape, 1) // HEAD_DIM == h % 2
                query = jnp.where(inside, query, jnp.zeros_like(query))
            chosen.append((query, keys, values))
    scores = [jnp.where(visible, dot_nt(query, keys), -jnp.inf) for query, keys, _ in chosen]
    tops = [jnp.max(score, axis=-1, keepdims=True) for score in scores]
    weights = [jnp.exp(score - top) for score, top in zip(scores, tops)]
    shares = [1.0 / jnp.sum(weight, axis=-1, keepdims=True) for weight in weights]
    probs = [(weight * share).astype(bf16) for weight, share in zip(weights, shares)]
    found = [dot_nn(prob, values) for prob, (_, _, values) in zip(probs, chosen)]
    many = local // HEAD_DIM
    first_head = iota((unit, LANES), 1) < HEAD_DIM
    blocks = [
        jnp.concatenate(
            [jnp.where(first_head, found[g * many], found[g * many + 1]), found[g * many + 2]], 1
        )
        for g in range(groups)
    ]
    whole = jnp.concatenate(blocks, 0).reshape(groups, rows, few, local)
    context = jnp.swapaxes(whole, 0, 1).reshape(tokens, local)
    context_ref[0:tokens, :] = context[:, 0:LANES].astype(bf16)
    half = tokens // 2
    context_ref[tokens : tokens + half, :] = jnp.concatenate(
        [context[0:half, LANES:local], context[half:tokens, LANES:local]], 1
    ).astype(bf16)


def attend_columns_here(row_outs, payload, row_context, own_codes, embed, col_qkv, cols):
    parts = len(row_outs)
    tokens, width = row_context.shape
    local = width // parts
    return pl.pallas_call(
        functools.partial(column_kernel, parts, cols),
        out_shape=(
            jax.ShapeDtypeStruct((tokens * local // LANES, LANES), bf16),
            jax.ShapeDtypeStruct((tokens, local), f32),
        ),
        scratch_shapes=[
            pltpu.VMEM((parts, local, width), bf16),
            pltpu.VMEM((2 * CODES, 2 * width), bf16),
        ],
        compiler_params=pltpu.CompilerParams(vmem_limit_bytes=LARGE_VMEM),
        name="column_attention",
    )(*row_outs, payload, row_context, own_codes, embed, col_qkv)


def finish_kernel(groups, context_ref, col_out_ref, mixed_ref, out_ref):
    parts = context_ref.shape[0]
    tokens, local = mixed_ref.shape
    half = tokens // 2
    group = lax.axis_index("seq")
    total = mixed_ref[...]
    for p in range(parts):
        weight = col_out_ref[:, p * local : (p + 1) * local]
        total = total + dot_nt(context_ref[p, 0:tokens, :], weight[:, 0:LANES])
        rest = weight[:, LANES:local]
        zero = jnp.zeros_like(rest)
        last = context_ref[p, tokens : tokens + half, :]
        total = total + jnp.concatenate(
            [
                dot_nt(last, jnp.concatenate([rest, zero], 1)),
                dot_nt(last, jnp.concatenate([zero, rest], 1)),
            ],
            0,
        )
    each = tokens // groups
    for d in range(groups):
        block = total[d * each : (d + 1) * each, :]
        packed = jnp.concatenate(
            [
                block[:, 0:LANES],
                jnp.concatenate(
                    [block[0 : each // 2, LANES:local], block[each // 2 :, LANES:local]], 1
                ),
            ],
            0,
        )
        out_ref[group ^ d] = packed.astype(bf16)


def finish(contexts, col_out, mixed, groups):
    tokens, local = mixed.shape
    return pl.pallas_call(
        functools.partial(finish_kernel, groups),
        out_shape=jax.ShapeDtypeStruct((groups, tokens // groups * local // LANES, LANES), bf16),
        compiler_params=pltpu.CompilerParams(vmem_limit_bytes=LARGE_VMEM),
        name="finish",
    )(contexts, col_out, mixed)


def order_kernel(blocks_ref, out_ref):
    groups = blocks_ref.shape[0]
    local, cols = out_ref.shape[1:]
    own = cols // groups
    rest = local - LANES
    for part in range(3):
        piece = jnp.concatenate(
            [blocks_ref[g, part * own : (part + 1) * own, :] for g in range(groups)], 0
        )
        turned = piece.astype(f32).T.astype(bf16)
        if part < 2:
            out_ref[part, 0:LANES, :] = turned
        else:
            for r in range(2):
                out_ref[r, LANES:local, :] = turned[r * rest : (r + 1) * rest, :]


def order(blocks, cols, local):
    return pl.pallas_call(
        order_kernel,
        out_shape=jax.ShapeDtypeStruct((2, local, cols), bf16),
        compiler_params=pltpu.CompilerParams(vmem_limit_bytes=SMALL_VMEM),
        name="order",
    )(blocks)


def fast_body(ids, pad_mask, embed, row_qkv, row_out, col_qkv, col_out):
    rows_here, cols = ids.shape
    width = embed.shape[1]
    local = row_out.shape[0]
    groups, parts = lax.axis_size("seq"), lax.axis_size("head")
    own, rows = cols // groups, rows_here * groups
    each = groups // parts

    def pairwise(value, partner):
        order = [(g, p) for g in range(groups) for p in range(parts)]
        link = [(g * parts + p, partner(g, p)) for g, p in order]
        return lax.ppermute(value, ("seq", "head"), [(i, g * parts + p) for i, (g, p) in link])

    coded = make_codes(ids, pad_mask)
    codes = [pairwise(coded, lambda g, p, b=b: (g ^ (p * each + b), p)) for b in range(each)]
    sibling = lambda g, p: (g, p ^ 1)
    across = lambda g, p: (g, p ^ 2)
    far = pairwise(row_out, across)
    payload = make_payload(embed, row_qkv.reshape(3 * local, width), codes)
    payload = lax.all_gather(payload, "head", axis=0)
    payload, near, far = lax.optimization_barrier((payload, row_out, far))
    row_outs = [row_out, pairwise(near, sibling), far, pairwise(far, sibling)]
    row_context, own_codes = attend_rows(payload, rows, cols, own, width)
    context, mixed = attend_columns_here(
        row_outs, payload, row_context, own_codes, embed, col_qkv.reshape(3 * local, width), cols
    )
    contexts = lax.all_gather(context, "head", axis=0)
    blocks = finish(contexts, col_out, mixed, groups)
    blocks = lax.all_to_all(blocks, "seq", split_axis=0, concat_axis=0, tiled=True)
    return jnp.swapaxes(order(blocks, cols, local), 1, 2)


def weight_fold(out_weight, piece):
    return jnp.einsum("rce,fe->rcf", piece, out_weight, preferred_element_type=f32)


def attend_columns(query, keys, values, key_live):
    rows_all, count_cols, local_width = query.shape
    heads_here = local_width // HEAD_DIM
    shape = (rows_all, count_cols, heads_here, HEAD_DIM)
    scores = jnp.einsum(
        "rchd,schd->chrs",
        query.reshape(shape),
        keys.reshape(shape),
        preferred_element_type=f32,
    ) * HEAD_DIM ** (-0.5)
    scores = jnp.where(key_live > 0, scores, -jnp.inf)
    probs = softmax_last(scores).astype(bf16)
    context = jnp.einsum(
        "chrs,schd->rchd", probs, values.reshape(shape), preferred_element_type=f32
    )
    return context.astype(bf16).reshape(rows_all, count_cols, local_width)


def send_back(context):
    return lax.all_to_all(context[:, None], "seq", split_axis=0, concat_axis=1, tiled=True)


def general_body(ids, pad_mask, embed, row_qkv, row_out, col_qkv, col_out):
    rows_here, cols = ids.shape
    width = embed.shape[1]
    local_width = row_out.shape[0]
    heads_here = local_width // HEAD_DIM
    groups = lax.axis_size("seq")
    per_group = cols // groups
    codes = lax.broadcasted_iota(jnp.int32, (1, 1, embed.shape[0]), 2)
    onehot = (ids[:, :, None] == codes).astype(bf16)
    embedded = jnp.einsum("rcv,vd->rcd", onehot, embed, preferred_element_type=f32)
    normed = layer_norm(embedded).astype(bf16)
    row_proj = jnp.einsum("rcd,ted->trce", normed, row_qkv, preferred_element_type=f32)
    row_proj = row_proj.astype(bf16)
    live = pad_mask.astype(bf16)
    head_shape = (rows_here, cols, heads_here, HEAD_DIM)
    query = (row_proj[0] * live[:, None, None]).reshape(head_shape)
    keys = row_proj[1].reshape(head_shape)
    values = row_proj[2].reshape(head_shape)
    partial_scores = jnp.einsum("rihd,rjhd->hij", query, keys, preferred_element_type=f32)
    count_here = jnp.sum(pad_mask.astype(f32))
    scale = HEAD_DIM ** (-0.5)
    total, count = lax.psum((partial_scores, count_here), "seq")
    row_probs = softmax_last(total * (scale / jnp.sqrt(count))).astype(bf16)
    row_context = jnp.einsum("hij,rjhd->rihd", row_probs, values, preferred_element_type=f32)
    row_context = row_context.astype(bf16).reshape(rows_here, cols, local_width)
    start_feature = lax.axis_index("head") * local_width
    resident = lax.dynamic_slice_in_dim(embedded, start_feature, local_width, 2)
    row_update = weight_fold(row_out, lax.all_gather(row_context, "head", axis=2, tiled=True))
    mixed = resident + row_update
    sums, squares = lax.psum((jnp.sum(mixed, axis=-1), jnp.sum(mixed * mixed, axis=-1)), "head")
    mean = sums / width
    spread = squares / width - mean * mean
    normed_here = ((mixed - mean[..., None]) * lax.rsqrt(spread[..., None] + EPS)).astype(bf16)
    live_tile = jnp.broadcast_to(live[:, None, None, None], (rows_here, groups, per_group, 1))
    normed_full = lax.all_gather(normed_here, "head", axis=2, tiled=True)
    col_proj = jnp.einsum("rcd,ted->rcte", normed_full, col_qkv, preferred_element_type=f32)
    packed = col_proj.astype(bf16).reshape(rows_here, groups, per_group, 3 * local_width)
    received = lax.all_to_all(packed, "seq", split_axis=1, concat_axis=0, tiled=True)
    mask_part = lax.all_to_all(live_tile, "seq", split_axis=1, concat_axis=0, tiled=True)
    column_out = send_back(
        attend_columns(
            received[:, 0, :, :local_width],
            received[:, 0, :, local_width : 2 * local_width],
            received[:, 0, :, 2 * local_width :],
            mask_part[:, 0, 0, 0],
        )
    )
    column_out = column_out.reshape(rows_here, cols, local_width)
    col_update = weight_fold(col_out, lax.all_gather(column_out, "head", axis=2, tiled=True))
    return (mixed + col_update).astype(bf16)


def body(ids, pad_mask, embed, row_qkv, row_out, col_qkv, col_out):
    rows_here, cols = ids.shape
    groups = lax.axis_size("seq")
    own, rows = cols // groups, rows_here * groups
    parts = lax.axis_size("head")
    local = row_out.shape[0]
    fits = (
        groups & (groups - 1) == 0
        and parts == 4
        and groups % parts == 0
        and rows * 8 == LANES
        and rows_here == 2
        and rows <= 8 * parts
        and own % 16 == 0
        and cols + LANES <= 3 * local
        and local == LANES + HEAD_DIM
        and embed.shape[0] <= VOCAB_ROWS
    )
    chosen = fast_body if fits else general_body
    return chosen(ids, pad_mask, embed, row_qkv, row_out, col_qkv, col_out)


def solution(mesh):
    placed = (
        P("seq", None),
        P("seq"),
        P(),
        P(None, "head", None),
        P("head", None),
        P(None, "head", None),
        P("head", None),
    )
    return jax.shard_map(
        body, mesh=mesh, in_specs=placed, out_specs=P("seq", None, "head"), check_vma=False
    )
```

```python
import functools

import jax
import jax.numpy as jnp
from jax import lax
from jax.experimental import pallas as pl
from jax.experimental.pallas import tpu as pltpu
from jax.sharding import PartitionSpec as P

HEAD_DIM = 64
EPS = 1e-05
LANES = 128
CODES = 64
VOCAB_ROWS = 40
TABLE_ROWS = 48

SMALL_VMEM = 8 * 1024 * 1024
LARGE_VMEM = 32 * 1024 * 1024

f32 = jnp.float32
bf16 = jnp.bfloat16


def layer_norm(values):
    mean = jnp.mean(values, axis=-1, keepdims=True)
    centred = values - mean
    spread = jnp.mean(centred * centred, axis=-1, keepdims=True)
    return centred * lax.rsqrt(spread + EPS)


def softmax_last(scores):
    top = jnp.max(scores, axis=-1, keepdims=True)
    weights = jnp.exp(scores - top)
    return weights * (1.0 / jnp.sum(weights, axis=-1, keepdims=True))


def dot_nt(left, right):
    return lax.dot_general(left, right, (((1,), (1,)), ((), ())), preferred_element_type=f32)


def dot_nn(left, right):
    return jnp.dot(left, right, preferred_element_type=f32)


def in_hbm(value):
    return pltpu.with_memory_space_constraint(value, pltpu.HBM)


def iota(shape, axis):
    return lax.broadcasted_iota(jnp.int32, shape, axis)


def code_kernel(ids_hbm, live_hbm, out_ref, ids_ref, live_ref, sems):
    loads = [
        pltpu.make_async_copy(ids_hbm, ids_ref, sems.at[0]),
        pltpu.make_async_copy(live_hbm, live_ref, sems.at[1]),
    ]
    for load in loads:
        load.start()
    for load in loads:
        load.wait()
    row = iota(ids_ref.shape, 0)
    live = jnp.zeros(ids_ref.shape, jnp.int32)
    for r in range(ids_ref.shape[0]):
        live = jnp.where(row == r, live_ref[r], live)
    out_ref[...] = ids_ref[...] + 65536 * live


def make_codes(ids, pad_mask):
    return pl.pallas_call(
        code_kernel,
        out_shape=jax.ShapeDtypeStruct(ids.shape, jnp.int32),
        in_specs=[pl.BlockSpec(memory_space=pltpu.HBM)] * 2,
        scratch_shapes=[
            pltpu.VMEM(ids.shape, jnp.int32),
            pltpu.SMEM(pad_mask.shape, jnp.int32),
            pltpu.SemaphoreType.DMA((2,)),
        ],
        compiler_params=pltpu.CompilerParams(vmem_limit_bytes=SMALL_VMEM),
        name="codes",
    )(in_hbm(ids), in_hbm(pad_mask))


def table_kernel(embed_hbm, qkv_hbm, out_ref, embed_ref, qkv_ref, padded_ref, sems):
    kinds, local = qkv_ref.shape[0:2]
    loads = [pltpu.make_async_copy(embed_hbm, embed_ref, sems.at[kinds])]
    loads += [
        pltpu.make_async_copy(qkv_hbm.at[t], qkv_ref.at[t], sems.at[t]) for t in range(kinds)
    ]
    for load in loads:
        load.start()
    padded_ref[...] = jnp.zeros(padded_ref.shape, f32)
    loads[0].wait()
    padded_ref[0 : embed_ref.shape[0], :] = embed_ref[...].astype(f32)
    normed = layer_norm(padded_ref[...]).astype(bf16)
    tables = []
    for t in range(kinds):
        loads[1 + t].wait()
        tables.append(dot_nt(normed, qkv_ref[t]))
    out_ref[...] = jnp.concatenate(tables, 1).astype(bf16)


def make_tables(embed, row_qkv):
    kinds, local, width = row_qkv.shape
    return pl.pallas_call(
        table_kernel,
        out_shape=jax.ShapeDtypeStruct((TABLE_ROWS, kinds * local), bf16),
        in_specs=[pl.BlockSpec(memory_space=pltpu.HBM)] * 2,
        scratch_shapes=[
            pltpu.VMEM(embed.shape, bf16),
            pltpu.VMEM(row_qkv.shape, bf16),
            pltpu.VMEM((TABLE_ROWS, width), f32),
            pltpu.SemaphoreType.DMA((kinds + 1,)),
        ],
        cost_estimate=pl.CostEstimate(
            flops=2 * TABLE_ROWS * row_qkv.size,
            bytes_accessed=2 * row_qkv.size,
            transcendentals=0,
        ),
        compiler_params=pltpu.CompilerParams(vmem_limit_bytes=SMALL_VMEM),
        name="tables",
    )(in_hbm(embed), in_hbm(row_qkv))


def pack_kernel(table_ref, *refs):
    codes_refs, out_ref = refs[:-1], refs[-1]
    coded = jnp.concatenate([ref[...] for ref in codes_refs], 0)
    some, cols = coded.shape
    ids = (coded & 0xFFFF).astype(f32)
    live = (coded >> 16).astype(f32)
    spare = jnp.concatenate(
        [ids, live[:, 0:LANES], jnp.zeros((some, out_ref.shape[1] - cols - LANES), f32)], 1
    )
    if some < TABLE_ROWS - VOCAB_ROWS:
        empty = jnp.zeros((TABLE_ROWS - VOCAB_ROWS - some, spare.shape[1]), f32)
        spare = jnp.concatenate([spare, empty], 0)
    table = table_ref[...].astype(f32)[0:VOCAB_ROWS]
    out_ref[...] = jnp.concatenate([table, spare], 0).astype(bf16)


def pack(table, codes):
    return pl.pallas_call(
        pack_kernel,
        out_shape=jax.ShapeDtypeStruct(table.shape, bf16),
        compiler_params=pltpu.CompilerParams(vmem_limit_bytes=SMALL_VMEM),
        name="pack",
    )(table, *codes)


def halves(pair):
    lane = iota(pair.shape, 1)
    zero = jnp.zeros_like(pair)
    return jnp.where(lane < HEAD_DIM, pair, zero), jnp.where(lane < HEAD_DIM, zero, pair)


def spread_pair(pair):
    first, second = halves(pair)
    zero = jnp.zeros_like(pair)
    return jnp.concatenate(
        [
            jnp.concatenate([first, zero], 1),
            jnp.concatenate([zero, first], 1),
            jnp.concatenate([second, zero], 1),
            jnp.concatenate([zero, second], 1),
        ],
        0,
    )


def double(block):
    zero = jnp.zeros_like(block)
    return jnp.concatenate(
        [jnp.concatenate([block, zero], 1), jnp.concatenate([zero, block], 1)], 0
    )


def read_sequences(payload_ref, rows, first, last):
    parts = payload_ref.shape[0]
    each = rows // parts
    return jnp.concatenate(
        [
            payload_ref[p, VOCAB_ROWS:TABLE_ROWS, first:last].astype(f32)[0:each]
            for p in range(parts)
        ],
        0,
    )


def row_kernel(parts, *refs):
    payload_refs, refs = refs[:parts], refs[parts:]
    (
        row_context_ref,
        own_ref,
        live_ref,
        payload_ref,
        table_ref,
        hot_ref,
        live_own_ref,
        sum_ref,
        spread_ref,
    ) = refs
    depth, cols = hot_ref.shape
    rows = depth // CODES
    pairs = rows // 2
    own = live_own_ref.shape[0] // pairs
    half = own // 2
    width = row_context_ref.shape[2]
    heads = width // HEAD_DIM
    local = width // parts
    group = lax.axis_index("seq")
    part = lax.axis_index("head")
    for p in range(parts):
        payload_ref[part ^ p] = payload_refs[p][...]

    for t in range(3):
        table_ref[t, 0:VOCAB_ROWS, :] = jnp.concatenate(
            [payload_ref[p, 0:VOCAB_ROWS, t * local : (t + 1) * local] for p in range(parts)], 1
        )
        table_ref[t, VOCAB_ROWS:CODES, :] = jnp.zeros((CODES - VOCAB_ROWS, width), bf16)

    ids = read_sequences(payload_ref, rows, 0, cols)
    live = read_sequences(payload_ref, rows, cols, cols + LANES)
    live_ref[...] = live
    code = iota((CODES, cols), 0).astype(f32)
    for r in range(rows):
        hot = jnp.broadcast_to(ids[r : r + 1, :], (CODES, cols)) == code
        hot_ref[r * CODES : (r + 1) * CODES, :] = hot.astype(f32).astype(bf16)

    pick = (iota((own, cols), 1) == group * own + iota((own, cols), 0)).astype(f32).astype(bf16)
    mine = dot_nt(pick, ids.astype(bf16))
    lane = iota((own, LANES), 1)
    first_half = lane < CODES
    lane_code = jnp.where(first_half, lane, lane - CODES).astype(f32)
    for k in range(pairs):
        value = jnp.where(first_half, mine[:, 2 * k : 2 * k + 1], mine[:, 2 * k + 1 : 2 * k + 2])
        hot = (value == lane_code).astype(f32)
        alive = jnp.where(first_half, live[2 * k : 2 * k + 1, :], live[2 * k + 1 : 2 * k + 2, :])
        for c in range(2):
            own_ref[c, k * half : (k + 1) * half, :] = hot[c * half : (c + 1) * half].astype(bf16)
        live_own_ref[k * own : (k + 1) * own, :] = (hot * alive).astype(bf16)

    spans = [slice(hp * LANES, (hp + 1) * LANES) for hp in range(heads // 2)]
    queries = [spread_pair(table_ref[0, :, span]) for span in spans]
    keys = [double(table_ref[1, :, span]) for span in spans]
    scores = [dot_nt(query, key) for query, key in zip(queries, keys)]
    high = [score.astype(bf16) for score in scores]
    low = [(score - part.astype(f32)).astype(bf16) for score, part in zip(scores, high)]
    for hp in range(heads // 2):
        for h2 in range(2):
            these = slice(h2 * LANES, (h2 + 1) * LANES)
            looked = dot_nn(
                live_own_ref[...], jnp.concatenate([high[hp][these], low[hp][these]], 1)
            ).astype(bf16)
            base = (hp * 2 + h2) * own
            for piece in range(2):
                for k in range(pairs):
                    to = piece * depth + k * LANES
                    sum_ref[base : base + own, to : to + LANES] = looked[
                        k * own : (k + 1) * own, piece * LANES : (piece + 1) * LANES
                    ]
    tied = dot_nn(sum_ref[:, 0:depth], hot_ref[...]) + dot_nn(
        sum_ref[:, depth : 2 * depth], hot_ref[...]
    )
    count = jnp.sum(live, axis=0, keepdims=True)[:, 0:1]
    probs = softmax_last(tied * (HEAD_DIM ** (-0.5) / jnp.sqrt(count))).astype(bf16)

    spread_ref[...] = dot_nt(probs, hot_ref[...]).astype(bf16)
    values = [spread_pair(table_ref[2, :, span]) for span in spans]
    contexts = []
    for hp in range(heads // 2):
        first = (hp * 2) * own
        weights = jnp.concatenate(
            [
                jnp.concatenate(
                    [
                        spread_ref[first : first + own, k * LANES : (k + 1) * LANES],
                        spread_ref[first + own : first + 2 * own, k * LANES : (k + 1) * LANES],
                    ],
                    1,
                )
                for k in range(pairs)
            ],
            0,
        )
        contexts.append(dot_nn(weights, values[hp]).astype(bf16))
    for hp in range(heads // 2):
        for k in range(pairs):
            for r2 in range(2):
                at = (2 * k + r2) * half
                for c in range(2):
                    row_context_ref[c, at : at + half, spans[hp]] = contexts[hp][
                        k * own + c * half : k * own + (c + 1) * half,
                        r2 * LANES : (r2 + 1) * LANES,
                    ]


def attend_rows(payloads, rows, cols, own, width):
    heads = width // HEAD_DIM
    parts = len(payloads)
    return pl.pallas_call(
        functools.partial(row_kernel, parts),
        out_shape=(
            jax.ShapeDtypeStruct((2, rows * own // 2, width), bf16),
            jax.ShapeDtypeStruct((2, rows * own // 4, LANES), bf16),
            jax.ShapeDtypeStruct((rows, LANES), f32),
        ),
        scratch_shapes=[
            pltpu.VMEM((parts,) + payloads[0].shape, bf16),
            pltpu.VMEM((3, CODES, width), bf16),
            pltpu.VMEM((rows * CODES, cols), bf16),
            pltpu.VMEM((rows // 2 * own, LANES), bf16),
            pltpu.VMEM((heads * own, 2 * rows * CODES), bf16),
            pltpu.VMEM((heads * own, rows * CODES), bf16),
        ],
        cost_estimate=pl.CostEstimate(flops=3 * 10**9, bytes_accessed=10**6, transcendentals=0),
        compiler_params=pltpu.CompilerParams(vmem_limit_bytes=LARGE_VMEM),
        name="row_attention",
    )(*payloads)


def column_kernel(parts, c, *refs):
    row_out_refs, refs = refs[:parts], refs[parts:]
    (
        live_ref,
        row_context_ref,
        own_ref,
        embed_ref,
        col_qkv_ref,
        context_ref,
        mixed_out_ref,
        row_out_ref,
        embed2_ref,
    ) = refs
    rows = live_ref.shape[0]
    tokens, width = row_context_ref.shape[1:]
    pairs = rows // 2
    own = tokens // rows
    vocab = embed_ref.shape[0]
    local = width // parts
    part = lax.axis_index("head")

    for p in range(parts):
        row_out_ref[part ^ p] = row_out_refs[p][...]
    embed2_ref[...] = jnp.zeros(embed2_ref.shape, bf16)
    embed2_ref[0:vocab, 0:width] = embed_ref[...]
    embed2_ref[CODES : CODES + vocab, width : 2 * width] = embed_ref[...]

    embedded2 = dot_nn(own_ref[c], embed2_ref[...])
    embedded = jnp.concatenate(
        [
            embedded2[k * own : (k + 1) * own, r2 * width : (r2 + 1) * width]
            for k in range(pairs)
            for r2 in range(2)
        ],
        0,
    )
    mixed = embedded + dot_nt(row_context_ref[c], row_out_ref[...].reshape(width, width))
    for p in range(parts):

        @pl.when(part == p)
        def _():
            mixed_out_ref[...] = mixed[:, p * local : (p + 1) * local]

    normed = layer_norm(mixed).astype(bf16)

    few = 8
    groups = own // few
    unit = rows * few

    def regroup(values):
        shape = (rows, groups, few, values.shape[1])
        return jnp.swapaxes(values.reshape(shape), 0, 1).reshape(tokens, values.shape[1])

    proj = [
        dot_nt(normed, col_qkv_ref[t * local : (t + 1) * local, :]) for t in range(3)
    ]
    proj[0] = proj[0] * HEAD_DIM ** (-0.5)
    proj = [regroup(values).astype(bf16) for values in proj]
    sub, lan = iota((unit, unit), 0), iota((unit, unit), 1)
    same_column = (sub % few) == (lan % few)
    seq_of_lane = iota((rows, unit), 1) // few
    live_lane = jnp.sum(
        jnp.where(seq_of_lane == iota((rows, unit), 0), live_ref[...], 0.0), axis=0, keepdims=True
    )
    visible = jnp.logical_and(same_column, jnp.broadcast_to(live_lane, (unit, unit)) > 0)
    chosen = []
    for g in range(groups):
        at = slice(g * unit, (g + 1) * unit)
        for h in range(local // HEAD_DIM):
            first = h * HEAD_DIM // LANES * LANES
            span = slice(first, min(first + LANES, local))
            query, keys, values = (proj[t][at, span] for t in range(3))
            if query.shape[1] > HEAD_DIM:
                inside = iota(query.shape, 1) // HEAD_DIM == h % 2
                query = jnp.where(inside, query, jnp.zeros_like(query))
            chosen.append((query, keys, values))
    scores = [jnp.where(visible, dot_nt(query, keys), -jnp.inf) for query, keys, _ in chosen]
    tops = [jnp.max(score, axis=-1, keepdims=True) for score in scores]
    weights = [jnp.exp(score - top) for score, top in zip(scores, tops)]
    shares = [1.0 / jnp.sum(weight, axis=-1, keepdims=True) for weight in weights]
    probs = [(weight * share).astype(bf16) for weight, share in zip(weights, shares)]
    found = [dot_nn(prob, values) for prob, (_, _, values) in zip(probs, chosen)]
    many = local // HEAD_DIM
    first_head = iota((unit, LANES), 1) < HEAD_DIM
    blocks = [
        jnp.concatenate(
            [jnp.where(first_head, found[g * many], found[g * many + 1]), found[g * many + 2]], 1
        )
        for g in range(groups)
    ]
    whole = jnp.concatenate(blocks, 0).reshape(groups, rows, few, local)
    context = jnp.swapaxes(whole, 0, 1).reshape(tokens, local)
    context_ref[0:tokens, :] = context[:, 0:LANES].astype(bf16)
    some = tokens // 2
    context_ref[tokens : tokens + some, :] = jnp.concatenate(
        [context[0:some, LANES:local], context[some:tokens, LANES:local]], 1
    ).astype(bf16)


def attend_columns_here(c, row_outs, live, row_context, own_codes, embed, col_qkv):
    parts = len(row_outs)
    tokens, width = row_context.shape[1:]
    local = width // parts
    return pl.pallas_call(
        functools.partial(column_kernel, parts, c),
        out_shape=(
            jax.ShapeDtypeStruct((tokens * local // LANES, LANES), bf16),
            jax.ShapeDtypeStruct((tokens, local), f32),
        ),
        scratch_shapes=[
            pltpu.VMEM((parts, local, width), bf16),
            pltpu.VMEM((2 * CODES, 2 * width), bf16),
        ],
        cost_estimate=pl.CostEstimate(flops=2 * 10**9, bytes_accessed=10**6, transcendentals=0),
        compiler_params=pltpu.CompilerParams(vmem_limit_bytes=LARGE_VMEM),
        name="column_attention",
    )(*row_outs, live, row_context, own_codes, embed, col_qkv)


def finish_kernel(parts, groups, *refs):
    context_refs = [refs[:parts], refs[parts : 2 * parts]]
    mixed_refs = refs[2 * parts : 2 * parts + 2]
    col_out_ref, out_ref, weight_ref = refs[2 * parts + 2 :]
    tokens, local = mixed_refs[0].shape
    some = tokens // 2
    group = lax.axis_index("seq")
    part = lax.axis_index("head")
    for p in range(parts):
        weight_ref[p] = col_out_ref[:, p * local : (p + 1) * local]
    totals = [ref[...] for ref in mixed_refs]
    for p in range(parts):
        weight = weight_ref[part ^ p]
        rest = weight[:, LANES:local]
        zero = jnp.zeros_like(rest)
        left = jnp.concatenate([rest, zero], 1)
        right = jnp.concatenate([zero, rest], 1)
        for c in range(2):
            context = context_refs[c][p]
            last = context[tokens : tokens + some, :]
            totals[c] = (
                totals[c]
                + dot_nt(context[0:tokens, :], weight[:, 0:LANES])
                + jnp.concatenate([dot_nt(last, left), dot_nt(last, right)], 0)
            )
    own = tokens // groups // 2
    for d in range(groups):
        first, second = (
            jnp.concatenate(
                [total[(2 * d + r) * own : (2 * d + r + 1) * own, :] for total in totals], 0
            )
            for r in range(2)
        )
        rest = jnp.concatenate([first[:, LANES:local], second[:, LANES:local]], 1)
        out_ref[group ^ d] = jnp.concatenate(
            [first[:, 0:LANES], second[:, 0:LANES], rest], 0
        ).astype(bf16)


def finish(contexts, mixed, col_out, groups):
    parts = len(contexts[0])
    tokens, local = mixed[0].shape
    return pl.pallas_call(
        functools.partial(finish_kernel, parts, groups),
        out_shape=jax.ShapeDtypeStruct(
            (groups, 2 * tokens // groups * local // LANES, LANES), bf16
        ),
        scratch_shapes=[pltpu.VMEM((parts, local, local), bf16)],
        compiler_params=pltpu.CompilerParams(vmem_limit_bytes=LARGE_VMEM),
        name="finish",
    )(*contexts[0], *contexts[1], *mixed, col_out)


def order_kernel(blocks_ref, out_ref):
    groups = blocks_ref.shape[0]
    local, cols = out_ref.shape[1:]
    own = cols // groups
    rest = local - LANES
    for part in range(3):
        piece = jnp.concatenate(
            [blocks_ref[g, part * own : (part + 1) * own, :] for g in range(groups)], 0
        )
        turned = piece.astype(f32).T.astype(bf16)
        if part < 2:
            out_ref[part, 0:LANES, :] = turned
        else:
            for r in range(2):
                out_ref[r, LANES:local, :] = turned[r * rest : (r + 1) * rest, :]


def order(blocks, cols, local):
    return pl.pallas_call(
        order_kernel,
        out_shape=jax.ShapeDtypeStruct((2, local, cols), bf16),
        compiler_params=pltpu.CompilerParams(vmem_limit_bytes=SMALL_VMEM),
        name="order",
    )(blocks)


def fast_body(ids, pad_mask, embed, row_qkv, row_out, col_qkv, col_out):
    rows_here, cols = ids.shape
    width = embed.shape[1]
    local = row_out.shape[0]
    groups, parts = lax.axis_size("seq"), lax.axis_size("head")
    own, rows = cols // groups, rows_here * groups
    each = groups // parts

    def pairwise(value, partner):
        order = [(g, p) for g in range(groups) for p in range(parts)]
        link = [(g * parts + p, partner(g, p)) for g, p in order]
        return lax.ppermute(value, ("seq", "head"), [(i, g * parts + p) for i, (g, p) in link])

    def sibling(g, p):
        return g, p ^ 1

    def across(g, p):
        return g, p ^ 2

    def opposite(g, p):
        return g, p ^ 3

    far = pairwise(row_out, across)
    coded = make_codes(ids, pad_mask)
    codes = [pairwise(coded, lambda g, p, b=b: (g ^ (p * each + b), p)) for b in range(each)]
    payload = pack(make_tables(embed, row_qkv), codes)
    payloads = [payload] + [pairwise(payload, to) for to in (sibling, across, opposite)]
    *payloads, near, far = lax.optimization_barrier((*payloads, row_out, far))
    row_outs = [row_out, pairwise(near, sibling), far, pairwise(far, sibling)]
    row_context, own_codes, live = attend_rows(payloads, rows, cols, own, width)
    contexts, mixed = [], []
    for c in range(2):
        context, residual = attend_columns_here(
            c, row_outs, live, row_context, own_codes, embed, col_qkv.reshape(3 * local, width)
        )
        beyond = pairwise(context, across)
        near = pairwise(context, sibling)
        contexts.append((context, near, beyond, pairwise(beyond, sibling)))
        mixed.append(residual)
    blocks = finish(contexts, mixed, col_out, groups)
    blocks = lax.all_to_all(blocks, "seq", split_axis=0, concat_axis=0, tiled=True)
    return jnp.swapaxes(order(blocks, cols, local), 1, 2)


def weight_fold(out_weight, piece):
    return jnp.einsum("rce,fe->rcf", piece, out_weight, preferred_element_type=f32)


def attend_columns(query, keys, values, key_live):
    rows_all, count_cols, local_width = query.shape
    heads_here = local_width // HEAD_DIM
    shape = (rows_all, count_cols, heads_here, HEAD_DIM)
    scores = jnp.einsum(
        "rchd,schd->chrs",
        query.reshape(shape),
        keys.reshape(shape),
        preferred_element_type=f32,
    ) * HEAD_DIM ** (-0.5)
    scores = jnp.where(key_live > 0, scores, -jnp.inf)
    probs = softmax_last(scores).astype(bf16)
    context = jnp.einsum(
        "chrs,schd->rchd", probs, values.reshape(shape), preferred_element_type=f32
    )
    return context.astype(bf16).reshape(rows_all, count_cols, local_width)


def send_back(context):
    return lax.all_to_all(context[:, None], "seq", split_axis=0, concat_axis=1, tiled=True)


def general_body(ids, pad_mask, embed, row_qkv, row_out, col_qkv, col_out):
    rows_here, cols = ids.shape
    width = embed.shape[1]
    local_width = row_out.shape[0]
    heads_here = local_width // HEAD_DIM
    groups = lax.axis_size("seq")
    per_group = cols // groups
    codes = lax.broadcasted_iota(jnp.int32, (1, 1, embed.shape[0]), 2)
    onehot = (ids[:, :, None] == codes).astype(bf16)
    embedded = jnp.einsum("rcv,vd->rcd", onehot, embed, preferred_element_type=f32)
    normed = layer_norm(embedded).astype(bf16)
    row_proj = jnp.einsum("rcd,ted->trce", normed, row_qkv, preferred_element_type=f32)
    row_proj = row_proj.astype(bf16)
    live = pad_mask.astype(bf16)
    head_shape = (rows_here, cols, heads_here, HEAD_DIM)
    query = (row_proj[0] * live[:, None, None]).reshape(head_shape)
    keys = row_proj[1].reshape(head_shape)
    values = row_proj[2].reshape(head_shape)
    partial_scores = jnp.einsum("rihd,rjhd->hij", query, keys, preferred_element_type=f32)
    count_here = jnp.sum(pad_mask.astype(f32))
    scale = HEAD_DIM ** (-0.5)
    total, count = lax.psum((partial_scores, count_here), "seq")
    row_probs = softmax_last(total * (scale / jnp.sqrt(count))).astype(bf16)
    row_context = jnp.einsum("hij,rjhd->rihd", row_probs, values, preferred_element_type=f32)
    row_context = row_context.astype(bf16).reshape(rows_here, cols, local_width)
    start_feature = lax.axis_index("head") * local_width
    resident = lax.dynamic_slice_in_dim(embedded, start_feature, local_width, 2)
    row_update = weight_fold(row_out, lax.all_gather(row_context, "head", axis=2, tiled=True))
    mixed = resident + row_update
    sums, squares = lax.psum((jnp.sum(mixed, axis=-1), jnp.sum(mixed * mixed, axis=-1)), "head")
    mean = sums / width
    spread = squares / width - mean * mean
    normed_here = ((mixed - mean[..., None]) * lax.rsqrt(spread[..., None] + EPS)).astype(bf16)
    live_tile = jnp.broadcast_to(live[:, None, None, None], (rows_here, groups, per_group, 1))
    normed_full = lax.all_gather(normed_here, "head", axis=2, tiled=True)
    col_proj = jnp.einsum("rcd,ted->rcte", normed_full, col_qkv, preferred_element_type=f32)
    packed = col_proj.astype(bf16).reshape(rows_here, groups, per_group, 3 * local_width)
    received = lax.all_to_all(packed, "seq", split_axis=1, concat_axis=0, tiled=True)
    mask_part = lax.all_to_all(live_tile, "seq", split_axis=1, concat_axis=0, tiled=True)
    column_out = send_back(
        attend_columns(
            received[:, 0, :, :local_width],
            received[:, 0, :, local_width : 2 * local_width],
            received[:, 0, :, 2 * local_width :],
            mask_part[:, 0, 0, 0],
        )
    )
    column_out = column_out.reshape(rows_here, cols, local_width)
    col_update = weight_fold(col_out, lax.all_gather(column_out, "head", axis=2, tiled=True))
    return (mixed + col_update).astype(bf16)


def body(ids, pad_mask, embed, row_qkv, row_out, col_qkv, col_out):
    rows_here, cols = ids.shape
    groups = lax.axis_size("seq")
    own, rows = cols // groups, rows_here * groups
    parts = lax.axis_size("head")
    local = row_out.shape[0]
    fits = (
        groups & (groups - 1) == 0
        and parts == 4
        and groups % parts == 0
        and rows * 8 == LANES
        and rows_here == 2
        and rows <= 8 * parts
        and own % 32 == 0
        and cols + LANES <= 3 * local
        and local == LANES + HEAD_DIM
        and embed.shape[0] <= VOCAB_ROWS
    )
    chosen = fast_body if fits else general_body
    return chosen(ids, pad_mask, embed, row_qkv, row_out, col_qkv, col_out)


def solution(mesh):
    placed = (
        P("seq", None),
        P("seq"),
        P(),
        P(None, "head", None),
        P("head", None),
        P(None, "head", None),
        P("head", None),
    )
    return jax.shard_map(
        body, mesh=mesh, in_specs=placed, out_specs=P("seq", None, "head"), check_vma=False
    )
```

```python
import functools

import jax
import jax.numpy as jnp
from jax import lax
from jax.experimental import pallas as pl
from jax.experimental.pallas import tpu as pltpu
from jax.sharding import PartitionSpec as P

HEAD_DIM = 64
EPS = 1e-05
LANES = 128
CODES = 64
VOCAB_ROWS = 40
TABLE_ROWS = 48

SMALL_VMEM = 8 * 1024 * 1024
LARGE_VMEM = 32 * 1024 * 1024

f32 = jnp.float32
bf16 = jnp.bfloat16


def layer_norm(values):
    mean = jnp.mean(values, axis=-1, keepdims=True)
    centred = values - mean
    spread = jnp.mean(centred * centred, axis=-1, keepdims=True)
    return centred * lax.rsqrt(spread + EPS)


def softmax_last(scores):
    top = jnp.max(scores, axis=-1, keepdims=True)
    weights = jnp.exp(scores - top)
    return weights * (1.0 / jnp.sum(weights, axis=-1, keepdims=True))


def dot_nt(left, right):
    return lax.dot_general(left, right, (((1,), (1,)), ((), ())), preferred_element_type=f32)


def dot_nn(left, right):
    return jnp.dot(left, right, preferred_element_type=f32)


def in_hbm(value):
    return pltpu.with_memory_space_constraint(value, pltpu.HBM)


def iota(shape, axis):
    return lax.broadcasted_iota(jnp.int32, shape, axis)


def code_kernel(
    ids_hbm, live_hbm, row_out_hbm, out_ref, early_ref, late_ref, ids_ref, live_ref, sems
):
    cut = early_ref.shape[0]
    loads = [
        pltpu.make_async_copy(ids_hbm, ids_ref, sems.at[0]),
        pltpu.make_async_copy(live_hbm, live_ref, sems.at[1]),
        pltpu.make_async_copy(row_out_hbm.at[0:cut], early_ref, sems.at[2]),
        pltpu.make_async_copy(row_out_hbm.at[cut : cut + late_ref.shape[0]], late_ref, sems.at[3]),
    ]
    for load in loads:
        load.start()
    for load in loads[0:2]:
        load.wait()
    row = iota(ids_ref.shape, 0)
    live = jnp.zeros(ids_ref.shape, jnp.int32)
    for r in range(ids_ref.shape[0]):
        live = jnp.where(row == r, live_ref[r], live)
    out_ref[...] = ids_ref[...] + 65536 * live
    for load in loads[2:]:
        load.wait()


def make_codes(ids, pad_mask, row_out):
    local, width = row_out.shape
    return pl.pallas_call(
        code_kernel,
        out_shape=(
            jax.ShapeDtypeStruct(ids.shape, jnp.int32),
            jax.ShapeDtypeStruct((local - HEAD_DIM, width), bf16),
            jax.ShapeDtypeStruct((HEAD_DIM, width), bf16),
        ),
        in_specs=[pl.BlockSpec(memory_space=pltpu.HBM)] * 3,
        scratch_shapes=[
            pltpu.VMEM(ids.shape, jnp.int32),
            pltpu.SMEM(pad_mask.shape, jnp.int32),
            pltpu.SemaphoreType.DMA((4,)),
        ],
        compiler_params=pltpu.CompilerParams(vmem_limit_bytes=SMALL_VMEM),
        name="codes",
    )(in_hbm(ids), in_hbm(pad_mask), in_hbm(row_out))


def table_kernel(embed_hbm, qkv_hbm, out_ref, embed_ref, qkv_ref, padded_ref, sems):
    kinds, local = qkv_ref.shape[0:2]
    loads = [pltpu.make_async_copy(embed_hbm, embed_ref, sems.at[kinds])]
    loads += [
        pltpu.make_async_copy(qkv_hbm.at[t], qkv_ref.at[t], sems.at[t]) for t in range(kinds)
    ]
    for load in loads:
        load.start()
    padded_ref[...] = jnp.zeros(padded_ref.shape, f32)
    loads[0].wait()
    padded_ref[0 : embed_ref.shape[0], :] = embed_ref[...].astype(f32)
    normed = layer_norm(padded_ref[...]).astype(bf16)
    tables = []
    for t in range(kinds):
        loads[1 + t].wait()
        tables.append(dot_nt(normed, qkv_ref[t]))
    out_ref[...] = jnp.concatenate(tables, 1).astype(bf16)


def make_tables(embed, row_qkv):
    kinds, local, width = row_qkv.shape
    return pl.pallas_call(
        table_kernel,
        out_shape=jax.ShapeDtypeStruct((TABLE_ROWS, kinds * local), bf16),
        in_specs=[pl.BlockSpec(memory_space=pltpu.HBM)] * 2,
        scratch_shapes=[
            pltpu.VMEM(embed.shape, bf16),
            pltpu.VMEM(row_qkv.shape, bf16),
            pltpu.VMEM((TABLE_ROWS, width), f32),
            pltpu.SemaphoreType.DMA((kinds + 1,)),
        ],
        cost_estimate=pl.CostEstimate(
            flops=2 * TABLE_ROWS * row_qkv.size,
            bytes_accessed=2 * row_qkv.size,
            transcendentals=0,
        ),
        compiler_params=pltpu.CompilerParams(vmem_limit_bytes=SMALL_VMEM),
        name="tables",
    )(in_hbm(embed), in_hbm(row_qkv))


def pack_kernel(table_ref, *refs):
    codes_refs, out_ref = refs[:-1], refs[-1]
    coded = jnp.concatenate([ref[...] for ref in codes_refs], 0)
    some, cols = coded.shape
    ids = (coded & 0xFFFF).astype(f32)
    live = (coded >> 16).astype(f32)
    spare = jnp.concatenate(
        [ids, live[:, 0:LANES], jnp.zeros((some, out_ref.shape[1] - cols - LANES), f32)], 1
    )
    if some < TABLE_ROWS - VOCAB_ROWS:
        empty = jnp.zeros((TABLE_ROWS - VOCAB_ROWS - some, spare.shape[1]), f32)
        spare = jnp.concatenate([spare, empty], 0)
    table = table_ref[...].astype(f32)[0:VOCAB_ROWS]
    out_ref[...] = jnp.concatenate([table, spare], 0).astype(bf16)


def pack(table, codes):
    return pl.pallas_call(
        pack_kernel,
        out_shape=jax.ShapeDtypeStruct(table.shape, bf16),
        compiler_params=pltpu.CompilerParams(vmem_limit_bytes=SMALL_VMEM),
        name="pack",
    )(table, *codes)


def halves(pair):
    lane = iota(pair.shape, 1)
    zero = jnp.zeros_like(pair)
    return jnp.where(lane < HEAD_DIM, pair, zero), jnp.where(lane < HEAD_DIM, zero, pair)


def spread_pair(pair):
    first, second = halves(pair)
    zero = jnp.zeros_like(pair)
    return jnp.concatenate(
        [
            jnp.concatenate([first, zero], 1),
            jnp.concatenate([zero, first], 1),
            jnp.concatenate([second, zero], 1),
            jnp.concatenate([zero, second], 1),
        ],
        0,
    )


def double(block):
    zero = jnp.zeros_like(block)
    return jnp.concatenate(
        [jnp.concatenate([block, zero], 1), jnp.concatenate([zero, block], 1)], 0
    )


def read_sequences(payload_ref, rows, first, last):
    parts = payload_ref.shape[0]
    each = rows // parts
    return jnp.concatenate(
        [
            payload_ref[p, VOCAB_ROWS:TABLE_ROWS, first:last].astype(f32)[0:each]
            for p in range(parts)
        ],
        0,
    )


def row_kernel(parts, *refs):
    payload_refs, refs = refs[:parts], refs[parts:]
    (
        row_context_ref,
        own_ref,
        live_ref,
        payload_ref,
        table_ref,
        hot_ref,
        live_own_ref,
        sum_ref,
        spread_ref,
    ) = refs
    depth, cols = hot_ref.shape
    rows = depth // CODES
    pairs = rows // 2
    own = live_own_ref.shape[0] // pairs
    half = own // 2
    width = row_context_ref.shape[2]
    heads = width // HEAD_DIM
    local = width // parts
    group = lax.axis_index("seq")
    part = lax.axis_index("head")
    for p in range(parts):
        payload_ref[part ^ p] = payload_refs[p][...]

    for t in range(3):
        table_ref[t, 0:VOCAB_ROWS, :] = jnp.concatenate(
            [payload_ref[p, 0:VOCAB_ROWS, t * local : (t + 1) * local] for p in range(parts)], 1
        )
        table_ref[t, VOCAB_ROWS:CODES, :] = jnp.zeros((CODES - VOCAB_ROWS, width), bf16)

    ids = read_sequences(payload_ref, rows, 0, cols)
    live = read_sequences(payload_ref, rows, cols, cols + LANES)
    live_ref[...] = live
    code = iota((CODES, cols), 0).astype(f32)
    for r in range(rows):
        hot = jnp.broadcast_to(ids[r : r + 1, :], (CODES, cols)) == code
        hot_ref[r * CODES : (r + 1) * CODES, :] = hot.astype(f32).astype(bf16)

    pick = (iota((own, cols), 1) == group * own + iota((own, cols), 0)).astype(f32).astype(bf16)
    mine = dot_nt(pick, ids.astype(bf16))
    lane = iota((own, LANES), 1)
    first_half = lane < CODES
    lane_code = jnp.where(first_half, lane, lane - CODES).astype(f32)
    for k in range(pairs):
        value = jnp.where(first_half, mine[:, 2 * k : 2 * k + 1], mine[:, 2 * k + 1 : 2 * k + 2])
        hot = (value == lane_code).astype(f32)
        alive = jnp.where(first_half, live[2 * k : 2 * k + 1, :], live[2 * k + 1 : 2 * k + 2, :])
        for c in range(2):
            own_ref[c, k * half : (k + 1) * half, :] = hot[c * half : (c + 1) * half].astype(bf16)
        live_own_ref[k * own : (k + 1) * own, :] = (hot * alive).astype(bf16)

    spans = [slice(hp * LANES, (hp + 1) * LANES) for hp in range(heads // 2)]
    queries = [spread_pair(table_ref[0, :, span]) for span in spans]
    keys = [double(table_ref[1, :, span]) for span in spans]
    scores = [dot_nt(query, key) for query, key in zip(queries, keys)]
    high = [score.astype(bf16) for score in scores]
    low = [(score - part.astype(f32)).astype(bf16) for score, part in zip(scores, high)]
    for hp in range(heads // 2):
        for h2 in range(2):
            these = slice(h2 * LANES, (h2 + 1) * LANES)
            looked = dot_nn(
                live_own_ref[...], jnp.concatenate([high[hp][these], low[hp][these]], 1)
            ).astype(bf16)
            base = (hp * 2 + h2) * own
            for piece in range(2):
                for k in range(pairs):
                    to = piece * depth + k * LANES
                    sum_ref[base : base + own, to : to + LANES] = looked[
                        k * own : (k + 1) * own, piece * LANES : (piece + 1) * LANES
                    ]
    tied = dot_nn(sum_ref[:, 0:depth], hot_ref[...]) + dot_nn(
        sum_ref[:, depth : 2 * depth], hot_ref[...]
    )
    count = jnp.sum(live, axis=0, keepdims=True)[:, 0:1]
    probs = softmax_last(tied * (HEAD_DIM ** (-0.5) / jnp.sqrt(count))).astype(bf16)

    spread_ref[...] = dot_nt(probs, hot_ref[...]).astype(bf16)
    values = [spread_pair(table_ref[2, :, span]) for span in spans]
    contexts = []
    for hp in range(heads // 2):
        first = (hp * 2) * own
        weights = jnp.concatenate(
            [
                jnp.concatenate(
                    [
                        spread_ref[first : first + own, k * LANES : (k + 1) * LANES],
                        spread_ref[first + own : first + 2 * own, k * LANES : (k + 1) * LANES],
                    ],
                    1,
                )
                for k in range(pairs)
            ],
            0,
        )
        contexts.append(dot_nn(weights, values[hp]).astype(bf16))
    for hp in range(heads // 2):
        for k in range(pairs):
            for r2 in range(2):
                at = (2 * k + r2) * half
                for c in range(2):
                    row_context_ref[c, at : at + half, spans[hp]] = contexts[hp][
                        k * own + c * half : k * own + (c + 1) * half,
                        r2 * LANES : (r2 + 1) * LANES,
                    ]


def attend_rows(payloads, rows, cols, own, width):
    heads = width // HEAD_DIM
    parts = len(payloads)
    return pl.pallas_call(
        functools.partial(row_kernel, parts),
        out_shape=(
            jax.ShapeDtypeStruct((2, rows * own // 2, width), bf16),
            jax.ShapeDtypeStruct((2, rows * own // 4, LANES), bf16),
            jax.ShapeDtypeStruct((rows, LANES), f32),
        ),
        scratch_shapes=[
            pltpu.VMEM((parts,) + payloads[0].shape, bf16),
            pltpu.VMEM((3, CODES, width), bf16),
            pltpu.VMEM((rows * CODES, cols), bf16),
            pltpu.VMEM((rows // 2 * own, LANES), bf16),
            pltpu.VMEM((heads * own, 2 * rows * CODES), bf16),
            pltpu.VMEM((heads * own, rows * CODES), bf16),
        ],
        cost_estimate=pl.CostEstimate(flops=3 * 10**9, bytes_accessed=10**6, transcendentals=0),
        compiler_params=pltpu.CompilerParams(vmem_limit_bytes=LARGE_VMEM),
        name="row_attention",
    )(*payloads)


def column_kernel(parts, c, *refs):
    row_out_refs, refs = refs[: 2 * parts], refs[2 * parts :]
    (
        live_ref,
        row_context_ref,
        own_ref,
        embed_ref,
        col_qkv_ref,
        context_ref,
        mixed_out_ref,
        row_out_ref,
        embed2_ref,
    ) = refs
    rows = live_ref.shape[0]
    tokens, width = row_context_ref.shape[1:]
    pairs = rows // 2
    own = tokens // rows
    vocab = embed_ref.shape[0]
    local = width // parts
    part = lax.axis_index("head")

    for p in range(parts):
        early, late = row_out_refs[2 * p : 2 * p + 2]
        row_out_ref[part ^ p, 0 : early.shape[0]] = early[...]
        row_out_ref[part ^ p, early.shape[0] : local] = late[...]
    embed2_ref[...] = jnp.zeros(embed2_ref.shape, bf16)
    embed2_ref[0:vocab, 0:width] = embed_ref[...]
    embed2_ref[CODES : CODES + vocab, width : 2 * width] = embed_ref[...]

    embedded2 = dot_nn(own_ref[c], embed2_ref[...])
    embedded = jnp.concatenate(
        [
            embedded2[k * own : (k + 1) * own, r2 * width : (r2 + 1) * width]
            for k in range(pairs)
            for r2 in range(2)
        ],
        0,
    )
    mixed = embedded + dot_nt(row_context_ref[c], row_out_ref[...].reshape(width, width))
    for p in range(parts):

        @pl.when(part == p)
        def _():
            mixed_out_ref[...] = mixed[:, p * local : (p + 1) * local]

    normed = layer_norm(mixed).astype(bf16)

    few = 8
    groups = own // few
    unit = rows * few

    def regroup(values):
        shape = (rows, groups, few, values.shape[1])
        return jnp.swapaxes(values.reshape(shape), 0, 1).reshape(tokens, values.shape[1])

    proj = [
        dot_nt(normed, col_qkv_ref[t * local : (t + 1) * local, :]) for t in range(3)
    ]
    proj[0] = proj[0] * HEAD_DIM ** (-0.5)
    proj = [regroup(values).astype(bf16) for values in proj]
    sub, lan = iota((unit, unit), 0), iota((unit, unit), 1)
    same_column = (sub % few) == (lan % few)
    seq_of_lane = iota((rows, unit), 1) // few
    live_lane = jnp.sum(
        jnp.where(seq_of_lane == iota((rows, unit), 0), live_ref[...], 0.0), axis=0, keepdims=True
    )
    visible = jnp.logical_and(same_column, jnp.broadcast_to(live_lane, (unit, unit)) > 0)
    chosen = []
    for g in range(groups):
        at = slice(g * unit, (g + 1) * unit)
        for h in range(local // HEAD_DIM):
            first = h * HEAD_DIM // LANES * LANES
            span = slice(first, min(first + LANES, local))
            query, keys, values = (proj[t][at, span] for t in range(3))
            if query.shape[1] > HEAD_DIM:
                inside = iota(query.shape, 1) // HEAD_DIM == h % 2
                query = jnp.where(inside, query, jnp.zeros_like(query))
            chosen.append((query, keys, values))
    scores = [jnp.where(visible, dot_nt(query, keys), -jnp.inf) for query, keys, _ in chosen]
    tops = [jnp.max(score, axis=-1, keepdims=True) for score in scores]
    weights = [jnp.exp(score - top) for score, top in zip(scores, tops)]
    shares = [1.0 / jnp.sum(weight, axis=-1, keepdims=True) for weight in weights]
    probs = [(weight * share).astype(bf16) for weight, share in zip(weights, shares)]
    found = [dot_nn(prob, values) for prob, (_, _, values) in zip(probs, chosen)]
    many = local // HEAD_DIM
    first_head = iota((unit, LANES), 1) < HEAD_DIM
    blocks = [
        jnp.concatenate(
            [jnp.where(first_head, found[g * many], found[g * many + 1]), found[g * many + 2]], 1
        )
        for g in range(groups)
    ]
    whole = jnp.concatenate(blocks, 0).reshape(groups, rows, few, local)
    context = jnp.swapaxes(whole, 0, 1).reshape(tokens, local)
    context_ref[0:tokens, :] = context[:, 0:LANES].astype(bf16)
    some = tokens // 2
    context_ref[tokens : tokens + some, :] = jnp.concatenate(
        [context[0:some, LANES:local], context[some:tokens, LANES:local]], 1
    ).astype(bf16)


def attend_columns_here(c, row_outs, live, row_context, own_codes, embed, col_qkv):
    parts = len(row_outs) // 2
    tokens, width = row_context.shape[1:]
    local = width // parts
    return pl.pallas_call(
        functools.partial(column_kernel, parts, c),
        out_shape=(
            jax.ShapeDtypeStruct((tokens * local // LANES, LANES), bf16),
            jax.ShapeDtypeStruct((tokens, local), f32),
        ),
        scratch_shapes=[
            pltpu.VMEM((parts, local, width), bf16),
            pltpu.VMEM((2 * CODES, 2 * width), bf16),
        ],
        cost_estimate=pl.CostEstimate(flops=2 * 10**9, bytes_accessed=10**6, transcendentals=0),
        compiler_params=pltpu.CompilerParams(vmem_limit_bytes=LARGE_VMEM),
        name="column_attention",
    )(*row_outs, live, row_context, own_codes, embed, col_qkv)


def finish_kernel(parts, groups, *refs):
    context_refs = refs[:parts]
    mixed_ref, col_out_ref, out_ref, weight_ref = refs[parts:]
    tokens, local = mixed_ref.shape
    some = tokens // 2
    group = lax.axis_index("seq")
    part = lax.axis_index("head")
    for p in range(parts):
        weight_ref[p] = col_out_ref[:, p * local : (p + 1) * local]
    total = mixed_ref[...]
    for p in range(parts):
        context = context_refs[p]
        weight = weight_ref[part ^ p]
        rest = weight[:, LANES:local]
        zero = jnp.zeros_like(rest)
        left = jnp.concatenate([rest, zero], 1)
        right = jnp.concatenate([zero, rest], 1)
        last = context[tokens : tokens + some, :]
        total = (
            total
            + dot_nt(context[0:tokens, :], weight[:, 0:LANES])
            + jnp.concatenate([dot_nt(last, left), dot_nt(last, right)], 0)
        )
    own = tokens // groups // 2
    for d in range(groups):
        first, second = (total[(2 * d + r) * own : (2 * d + r + 1) * own, :] for r in range(2))
        rest = jnp.concatenate([first[:, LANES:local], second[:, LANES:local]], 1)
        out_ref[group ^ d] = jnp.concatenate(
            [first[:, 0:LANES], second[:, 0:LANES], rest], 0
        ).astype(bf16)


def finish(contexts, mixed, col_out, groups):
    parts = len(contexts)
    tokens, local = mixed.shape
    return pl.pallas_call(
        functools.partial(finish_kernel, parts, groups),
        out_shape=jax.ShapeDtypeStruct((groups, tokens // groups * local // LANES, LANES), bf16),
        scratch_shapes=[pltpu.VMEM((parts, local, local), bf16)],
        cost_estimate=pl.CostEstimate(flops=10**9, bytes_accessed=10**6, transcendentals=0),
        compiler_params=pltpu.CompilerParams(vmem_limit_bytes=LARGE_VMEM),
        name="finish",
    )(*contexts, mixed, col_out)


def order_kernel(*refs):
    blocks_refs, out_ref = refs[:-1], refs[-1]
    groups = blocks_refs[0].shape[0]
    local, cols = out_ref.shape[1:]
    own = cols // groups // len(blocks_refs)
    rest = local - LANES
    for part in range(3):
        piece = jnp.concatenate(
            [
                ref[g, part * own : (part + 1) * own, :]
                for g in range(groups)
                for ref in blocks_refs
            ],
            0,
        )
        turned = piece.astype(f32).T.astype(bf16)
        if part < 2:
            out_ref[part, 0:LANES, :] = turned
        else:
            for r in range(2):
                out_ref[r, LANES:local, :] = turned[r * rest : (r + 1) * rest, :]


def order(blocks, cols, local):
    return pl.pallas_call(
        order_kernel,
        out_shape=jax.ShapeDtypeStruct((2, local, cols), bf16),
        compiler_params=pltpu.CompilerParams(vmem_limit_bytes=SMALL_VMEM),
        name="order",
    )(*blocks)


def fast_body(ids, pad_mask, embed, row_qkv, row_out, col_qkv, col_out):
    rows_here, cols = ids.shape
    width = embed.shape[1]
    local = row_out.shape[0]
    groups, parts = lax.axis_size("seq"), lax.axis_size("head")
    own, rows = cols // groups, rows_here * groups
    each = groups // parts

    def pairwise(value, partner):
        order = [(g, p) for g in range(groups) for p in range(parts)]
        link = [(g * parts + p, partner(g, p)) for g, p in order]
        return lax.ppermute(value, ("seq", "head"), [(i, g * parts + p) for i, (g, p) in link])

    def sibling(g, p):
        return g, p ^ 1

    def across(g, p):
        return g, p ^ 2

    def opposite(g, p):
        return g, p ^ 3

    coded, early, late = make_codes(ids, pad_mask, row_out)
    early_far = pairwise(early, across)
    codes = [pairwise(coded, lambda g, p, b=b: (g ^ (p * each + b), p)) for b in range(each)]
    payload = pack(make_tables(embed, row_qkv), codes)
    payloads = [payload] + [pairwise(payload, to) for to in (sibling, across, opposite)]
    *payloads, near, late, early_far = lax.optimization_barrier(
        (*payloads, early, late, early_far)
    )
    row_outs = [early, late, pairwise(near, sibling), pairwise(late, sibling)]
    row_outs += [early_far, pairwise(late, across)]
    row_outs += [pairwise(early_far, sibling), pairwise(late, opposite)]
    row_context, own_codes, live = attend_rows(payloads, rows, cols, own, width)
    blocks = []
    for c in range(2):
        context, mixed = attend_columns_here(
            c, row_outs, live, row_context, own_codes, embed, col_qkv.reshape(3 * local, width)
        )
        beyond = pairwise(context, across)
        near = pairwise(context, sibling)
        contexts = (context, near, beyond, pairwise(beyond, sibling))
        block = finish(contexts, mixed, col_out, groups)
        blocks.append(lax.all_to_all(block, "seq", split_axis=0, concat_axis=0, tiled=True))
    return jnp.swapaxes(order(blocks, cols, local), 1, 2)


def weight_fold(out_weight, piece):
    return jnp.einsum("rce,fe->rcf", piece, out_weight, preferred_element_type=f32)


def attend_columns(query, keys, values, key_live):
    rows_all, count_cols, local_width = query.shape
    heads_here = local_width // HEAD_DIM
    shape = (rows_all, count_cols, heads_here, HEAD_DIM)
    scores = jnp.einsum(
        "rchd,schd->chrs",
        query.reshape(shape),
        keys.reshape(shape),
        preferred_element_type=f32,
    ) * HEAD_DIM ** (-0.5)
    scores = jnp.where(key_live > 0, scores, -jnp.inf)
    probs = softmax_last(scores).astype(bf16)
    context = jnp.einsum(
        "chrs,schd->rchd", probs, values.reshape(shape), preferred_element_type=f32
    )
    return context.astype(bf16).reshape(rows_all, count_cols, local_width)


def send_back(context):
    return lax.all_to_all(context[:, None], "seq", split_axis=0, concat_axis=1, tiled=True)


def general_body(ids, pad_mask, embed, row_qkv, row_out, col_qkv, col_out):
    rows_here, cols = ids.shape
    width = embed.shape[1]
    local_width = row_out.shape[0]
    heads_here = local_width // HEAD_DIM
    groups = lax.axis_size("seq")
    per_group = cols // groups
    codes = lax.broadcasted_iota(jnp.int32, (1, 1, embed.shape[0]), 2)
    onehot = (ids[:, :, None] == codes).astype(bf16)
    embedded = jnp.einsum("rcv,vd->rcd", onehot, embed, preferred_element_type=f32)
    normed = layer_norm(embedded).astype(bf16)
    row_proj = jnp.einsum("rcd,ted->trce", normed, row_qkv, preferred_element_type=f32)
    row_proj = row_proj.astype(bf16)
    live = pad_mask.astype(bf16)
    head_shape = (rows_here, cols, heads_here, HEAD_DIM)
    query = (row_proj[0] * live[:, None, None]).reshape(head_shape)
    keys = row_proj[1].reshape(head_shape)
    values = row_proj[2].reshape(head_shape)
    partial_scores = jnp.einsum("rihd,rjhd->hij", query, keys, preferred_element_type=f32)
    count_here = jnp.sum(pad_mask.astype(f32))
    scale = HEAD_DIM ** (-0.5)
    total, count = lax.psum((partial_scores, count_here), "seq")
    row_probs = softmax_last(total * (scale / jnp.sqrt(count))).astype(bf16)
    row_context = jnp.einsum("hij,rjhd->rihd", row_probs, values, preferred_element_type=f32)
    row_context = row_context.astype(bf16).reshape(rows_here, cols, local_width)
    start_feature = lax.axis_index("head") * local_width
    resident = lax.dynamic_slice_in_dim(embedded, start_feature, local_width, 2)
    row_update = weight_fold(row_out, lax.all_gather(row_context, "head", axis=2, tiled=True))
    mixed = resident + row_update
    sums, squares = lax.psum((jnp.sum(mixed, axis=-1), jnp.sum(mixed * mixed, axis=-1)), "head")
    mean = sums / width
    spread = squares / width - mean * mean
    normed_here = ((mixed - mean[..., None]) * lax.rsqrt(spread[..., None] + EPS)).astype(bf16)
    live_tile = jnp.broadcast_to(live[:, None, None, None], (rows_here, groups, per_group, 1))
    normed_full = lax.all_gather(normed_here, "head", axis=2, tiled=True)
    col_proj = jnp.einsum("rcd,ted->rcte", normed_full, col_qkv, preferred_element_type=f32)
    packed = col_proj.astype(bf16).reshape(rows_here, groups, per_group, 3 * local_width)
    received = lax.all_to_all(packed, "seq", split_axis=1, concat_axis=0, tiled=True)
    mask_part = lax.all_to_all(live_tile, "seq", split_axis=1, concat_axis=0, tiled=True)
    column_out = send_back(
        attend_columns(
            received[:, 0, :, :local_width],
            received[:, 0, :, local_width : 2 * local_width],
            received[:, 0, :, 2 * local_width :],
            mask_part[:, 0, 0, 0],
        )
    )
    column_out = column_out.reshape(rows_here, cols, local_width)
    col_update = weight_fold(col_out, lax.all_gather(column_out, "head", axis=2, tiled=True))
    return (mixed + col_update).astype(bf16)


def body(ids, pad_mask, embed, row_qkv, row_out, col_qkv, col_out):
    rows_here, cols = ids.shape
    groups = lax.axis_size("seq")
    own, rows = cols // groups, rows_here * groups
    parts = lax.axis_size("head")
    local = row_out.shape[0]
    fits = (
        groups & (groups - 1) == 0
        and parts == 4
        and groups % parts == 0
        and rows * 8 == LANES
        and rows_here == 2
        and rows <= 8 * parts
        and own % 32 == 0
        and cols + LANES <= 3 * local
        and local == LANES + HEAD_DIM
        and embed.shape[0] <= VOCAB_ROWS
    )
    chosen = fast_body if fits else general_body
    return chosen(ids, pad_mask, embed, row_qkv, row_out, col_qkv, col_out)


def solution(mesh):
    placed = (
        P("seq", None),
        P("seq"),
        P(),
        P(None, "head", None),
        P("head", None),
        P(None, "head", None),
        P("head", None),
    )
    return jax.shard_map(
        body, mesh=mesh, in_specs=placed, out_specs=P("seq", None, "head"), check_vma=False
    )
```

```python
import functools

import jax
import jax.numpy as jnp
from jax import lax
from jax.experimental import pallas as pl
from jax.experimental.pallas import tpu as pltpu
from jax.sharding import PartitionSpec as P

HEAD_DIM = 64
EPS = 1e-05
LANES = 128
CODES = 64
VOCAB_ROWS = 40
TABLE_ROWS = 48

SMALL_VMEM = 8 * 1024 * 1024
LARGE_VMEM = 32 * 1024 * 1024

f32 = jnp.float32
bf16 = jnp.bfloat16


def layer_norm(values):
    mean = jnp.mean(values, axis=-1, keepdims=True)
    centred = values - mean
    spread = jnp.mean(centred * centred, axis=-1, keepdims=True)
    return centred * lax.rsqrt(spread + EPS)


def softmax_last(scores):
    top = jnp.max(scores, axis=-1, keepdims=True)
    weights = jnp.exp(scores - top)
    return weights * (1.0 / jnp.sum(weights, axis=-1, keepdims=True))


def dot_nt(left, right):
    return lax.dot_general(left, right, (((1,), (1,)), ((), ())), preferred_element_type=f32)


def dot_nn(left, right):
    return jnp.dot(left, right, preferred_element_type=f32)


def in_hbm(value):
    return pltpu.with_memory_space_constraint(value, pltpu.HBM)


def iota(shape, axis):
    return lax.broadcasted_iota(jnp.int32, shape, axis)


def code_kernel(ids_hbm, live_hbm, out_ref, ids_ref, live_ref, sems):
    loads = [
        pltpu.make_async_copy(ids_hbm, ids_ref, sems.at[0]),
        pltpu.make_async_copy(live_hbm, live_ref, sems.at[1]),
    ]
    for load in loads:
        load.start()
    for load in loads:
        load.wait()
    row = iota(ids_ref.shape, 0)
    live = jnp.zeros(ids_ref.shape, jnp.int32)
    for r in range(ids_ref.shape[0]):
        live = jnp.where(row == r, live_ref[r], live)
    out_ref[...] = ids_ref[...] + 65536 * live


def make_codes(ids, pad_mask):
    return pl.pallas_call(
        code_kernel,
        out_shape=jax.ShapeDtypeStruct(ids.shape, jnp.int32),
        in_specs=[pl.BlockSpec(memory_space=pltpu.HBM)] * 2,
        scratch_shapes=[
            pltpu.VMEM(ids.shape, jnp.int32),
            pltpu.SMEM(pad_mask.shape, jnp.int32),
            pltpu.SemaphoreType.DMA((2,)),
        ],
        compiler_params=pltpu.CompilerParams(vmem_limit_bytes=SMALL_VMEM),
        name="codes",
    )(in_hbm(ids), in_hbm(pad_mask))


def table_kernel(embed_hbm, qkv_hbm, out_ref, embed_ref, qkv_ref, padded_ref, sems):
    kinds, local = qkv_ref.shape[0:2]
    loads = [pltpu.make_async_copy(embed_hbm, embed_ref, sems.at[kinds])]
    loads += [
        pltpu.make_async_copy(qkv_hbm.at[t], qkv_ref.at[t], sems.at[t]) for t in range(kinds)
    ]
    for load in loads:
        load.start()
    padded_ref[...] = jnp.zeros(padded_ref.shape, f32)
    loads[0].wait()
    padded_ref[0 : embed_ref.shape[0], :] = embed_ref[...].astype(f32)
    normed = layer_norm(padded_ref[...]).astype(bf16)
    tables = []
    for t in range(kinds):
        loads[1 + t].wait()
        tables.append(dot_nt(normed, qkv_ref[t]))
    out_ref[...] = jnp.concatenate(tables, 1).astype(bf16)


def make_tables(embed, row_qkv):
    kinds, local, width = row_qkv.shape
    return pl.pallas_call(
        table_kernel,
        out_shape=jax.ShapeDtypeStruct((TABLE_ROWS, kinds * local), bf16),
        in_specs=[pl.BlockSpec(memory_space=pltpu.HBM)] * 2,
        scratch_shapes=[
            pltpu.VMEM(embed.shape, bf16),
            pltpu.VMEM(row_qkv.shape, bf16),
            pltpu.VMEM((TABLE_ROWS, width), f32),
            pltpu.SemaphoreType.DMA((kinds + 1,)),
        ],
        cost_estimate=pl.CostEstimate(
            flops=2 * TABLE_ROWS * row_qkv.size,
            bytes_accessed=2 * row_qkv.size,
            transcendentals=0,
        ),
        compiler_params=pltpu.CompilerParams(vmem_limit_bytes=SMALL_VMEM),
        name="tables",
    )(in_hbm(embed), in_hbm(row_qkv))


def pack_kernel(table_ref, *refs):
    codes_refs, out_ref = refs[:-1], refs[-1]
    coded = jnp.concatenate([ref[...] for ref in codes_refs], 0)
    some, cols = coded.shape
    ids = (coded & 0xFFFF).astype(f32)
    live = (coded >> 16).astype(f32)
    spare = jnp.concatenate(
        [ids, live[:, 0:LANES], jnp.zeros((some, out_ref.shape[1] - cols - LANES), f32)], 1
    )
    if some < TABLE_ROWS - VOCAB_ROWS:
        empty = jnp.zeros((TABLE_ROWS - VOCAB_ROWS - some, spare.shape[1]), f32)
        spare = jnp.concatenate([spare, empty], 0)
    table = table_ref[...].astype(f32)[0:VOCAB_ROWS]
    out_ref[...] = jnp.concatenate([table, spare], 0).astype(bf16)


def pack(table, codes):
    return pl.pallas_call(
        pack_kernel,
        out_shape=jax.ShapeDtypeStruct(table.shape, bf16),
        compiler_params=pltpu.CompilerParams(vmem_limit_bytes=SMALL_VMEM),
        name="pack",
    )(table, *codes)


def halves(pair):
    lane = iota(pair.shape, 1)
    zero = jnp.zeros_like(pair)
    return jnp.where(lane < HEAD_DIM, pair, zero), jnp.where(lane < HEAD_DIM, zero, pair)


def spread_pair(pair):
    first, second = halves(pair)
    zero = jnp.zeros_like(pair)
    return jnp.concatenate(
        [
            jnp.concatenate([first, zero], 1),
            jnp.concatenate([zero, first], 1),
            jnp.concatenate([second, zero], 1),
            jnp.concatenate([zero, second], 1),
        ],
        0,
    )


def double(block):
    zero = jnp.zeros_like(block)
    return jnp.concatenate(
        [jnp.concatenate([block, zero], 1), jnp.concatenate([zero, block], 1)], 0
    )


def read_sequences(payload_ref, rows, first, last):
    parts = payload_ref.shape[0]
    each = rows // parts
    return jnp.concatenate(
        [
            payload_ref[p, VOCAB_ROWS:TABLE_ROWS, first:last].astype(f32)[0:each]
            for p in range(parts)
        ],
        0,
    )


def row_kernel(parts, *refs):
    payload_refs, refs = refs[:parts], refs[parts:]
    (
        row_context_ref,
        own_ref,
        live_ref,
        payload_ref,
        table_ref,
        hot_ref,
        live_own_ref,
        sum_ref,
        spread_ref,
    ) = refs
    depth, cols = hot_ref.shape
    rows = depth // CODES
    pairs = rows // 2
    own = live_own_ref.shape[0] // pairs
    width = row_context_ref.shape[1]
    heads = width // HEAD_DIM
    local = width // parts
    group = lax.axis_index("seq")
    part = lax.axis_index("head")
    for p in range(parts):
        payload_ref[part ^ p] = payload_refs[p][...]

    for t in range(3):
        table_ref[t, 0:VOCAB_ROWS, :] = jnp.concatenate(
            [payload_ref[p, 0:VOCAB_ROWS, t * local : (t + 1) * local] for p in range(parts)], 1
        )
        table_ref[t, VOCAB_ROWS:CODES, :] = jnp.zeros((CODES - VOCAB_ROWS, width), bf16)

    ids = read_sequences(payload_ref, rows, 0, cols)
    live = read_sequences(payload_ref, rows, cols, cols + LANES)
    live_ref[...] = live
    code = iota((CODES, cols), 0).astype(f32)
    for r in range(rows):
        hot = jnp.broadcast_to(ids[r : r + 1, :], (CODES, cols)) == code
        hot_ref[r * CODES : (r + 1) * CODES, :] = hot.astype(f32).astype(bf16)

    pick = (iota((own, cols), 1) == group * own + iota((own, cols), 0)).astype(f32).astype(bf16)
    mine = dot_nt(pick, ids.astype(bf16))
    lane = iota((own, LANES), 1)
    first_half = lane < CODES
    lane_code = jnp.where(first_half, lane, lane - CODES).astype(f32)
    for k in range(pairs):
        value = jnp.where(first_half, mine[:, 2 * k : 2 * k + 1], mine[:, 2 * k + 1 : 2 * k + 2])
        hot = (value == lane_code).astype(f32)
        alive = jnp.where(first_half, live[2 * k : 2 * k + 1, :], live[2 * k + 1 : 2 * k + 2, :])
        own_ref[k * own : (k + 1) * own, :] = hot.astype(bf16)
        live_own_ref[k * own : (k + 1) * own, :] = (hot * alive).astype(bf16)

    spans = [slice(hp * LANES, (hp + 1) * LANES) for hp in range(heads // 2)]
    queries = [spread_pair(table_ref[0, :, span]) for span in spans]
    keys = [double(table_ref[1, :, span]) for span in spans]
    scores = [dot_nt(query, key) for query, key in zip(queries, keys)]
    high = [score.astype(bf16) for score in scores]
    low = [(score - part.astype(f32)).astype(bf16) for score, part in zip(scores, high)]
    for hp in range(heads // 2):
        for h2 in range(2):
            these = slice(h2 * LANES, (h2 + 1) * LANES)
            looked = dot_nn(
                live_own_ref[...], jnp.concatenate([high[hp][these], low[hp][these]], 1)
            ).astype(bf16)
            base = (hp * 2 + h2) * own
            for piece in range(2):
                for k in range(pairs):
                    to = piece * depth + k * LANES
                    sum_ref[base : base + own, to : to + LANES] = looked[
                        k * own : (k + 1) * own, piece * LANES : (piece + 1) * LANES
                    ]
    tied = dot_nn(sum_ref[:, 0:depth], hot_ref[...]) + dot_nn(
        sum_ref[:, depth : 2 * depth], hot_ref[...]
    )
    count = jnp.sum(live, axis=0, keepdims=True)[:, 0:1]
    probs = softmax_last(tied * (HEAD_DIM ** (-0.5) / jnp.sqrt(count))).astype(bf16)

    spread_ref[...] = dot_nt(probs, hot_ref[...]).astype(bf16)
    values = [spread_pair(table_ref[2, :, span]) for span in spans]
    contexts = []
    for hp in range(heads // 2):
        first = (hp * 2) * own
        weights = jnp.concatenate(
            [
                jnp.concatenate(
                    [
                        spread_ref[first : first + own, k * LANES : (k + 1) * LANES],
                        spread_ref[first + own : first + 2 * own, k * LANES : (k + 1) * LANES],
                    ],
                    1,
                )
                for k in range(pairs)
            ],
            0,
        )
        contexts.append(dot_nn(weights, values[hp]).astype(bf16))
    for hp in range(heads // 2):
        for k in range(pairs):
            for r2 in range(2):
                at = (2 * k + r2) * own
                row_context_ref[at : at + own, spans[hp]] = contexts[hp][
                    k * own : (k + 1) * own, r2 * LANES : (r2 + 1) * LANES
                ]


def attend_rows(payloads, rows, cols, own, width):
    heads = width // HEAD_DIM
    parts = len(payloads)
    return pl.pallas_call(
        functools.partial(row_kernel, parts),
        out_shape=(
            jax.ShapeDtypeStruct((rows * own, width), bf16),
            jax.ShapeDtypeStruct((rows * own // 2, LANES), bf16),
            jax.ShapeDtypeStruct((rows, LANES), f32),
        ),
        scratch_shapes=[
            pltpu.VMEM((parts,) + payloads[0].shape, bf16),
            pltpu.VMEM((3, CODES, width), bf16),
            pltpu.VMEM((rows * CODES, cols), bf16),
            pltpu.VMEM((rows // 2 * own, LANES), bf16),
            pltpu.VMEM((heads * own, 2 * rows * CODES), bf16),
            pltpu.VMEM((heads * own, rows * CODES), bf16),
        ],
        cost_estimate=pl.CostEstimate(flops=3 * 10**9, bytes_accessed=10**6, transcendentals=0),
        compiler_params=pltpu.CompilerParams(vmem_limit_bytes=LARGE_VMEM),
        name="row_attention",
    )(*payloads)


def column_kernel(parts, *refs):
    row_out_refs, refs = refs[:parts], refs[parts:]
    (
        live_ref,
        row_context_ref,
        own_ref,
        embed_ref,
        col_qkv_ref,
        *out_refs,
        row_out_ref,
        embed2_ref,
    ) = refs
    context_refs, mixed_refs = out_refs[:2], out_refs[2:]
    rows = live_ref.shape[0]
    tokens, width = row_context_ref.shape
    pairs = rows // 2
    own = tokens // rows
    vocab = embed_ref.shape[0]
    local = width // parts
    part = lax.axis_index("head")

    for p in range(parts):
        row_out_ref[part ^ p] = row_out_refs[p][...]
    embed2_ref[...] = jnp.zeros(embed2_ref.shape, bf16)
    embed2_ref[0:vocab, 0:width] = embed_ref[...]
    embed2_ref[CODES : CODES + vocab, width : 2 * width] = embed_ref[...]

    embedded2 = dot_nn(own_ref[...], embed2_ref[...])
    embedded = jnp.concatenate(
        [
            embedded2[k * own : (k + 1) * own, r2 * width : (r2 + 1) * width]
            for k in range(pairs)
            for r2 in range(2)
        ],
        0,
    )
    mixed = embedded + dot_nt(row_context_ref[...], row_out_ref[...].reshape(width, width))
    for p in range(parts):

        @pl.when(part == p)
        def _():
            for c in range(2):
                mixed_refs[c][...] = mixed[
                    c * tokens // 2 : (c + 1) * tokens // 2, p * local : (p + 1) * local
                ]

    normed = layer_norm(mixed).astype(bf16)

    few = 8
    groups = own // few
    unit = rows * few

    def regroup(values):
        shape = (rows, groups, few, values.shape[1])
        return jnp.swapaxes(values.reshape(shape), 0, 1).reshape(tokens, values.shape[1])

    proj = [
        dot_nt(normed, col_qkv_ref[t * local : (t + 1) * local, :]) for t in range(3)
    ]
    proj[0] = proj[0] * HEAD_DIM ** (-0.5)
    proj = [regroup(values).astype(bf16) for values in proj]
    sub, lan = iota((unit, unit), 0), iota((unit, unit), 1)
    same_column = (sub % few) == (lan % few)
    seq_of_lane = iota((rows, unit), 1) // few
    live_lane = jnp.sum(
        jnp.where(seq_of_lane == iota((rows, unit), 0), live_ref[...], 0.0), axis=0, keepdims=True
    )
    visible = jnp.logical_and(same_column, jnp.broadcast_to(live_lane, (unit, unit)) > 0)
    chosen = []
    for g in range(groups):
        at = slice(g * unit, (g + 1) * unit)
        for h in range(local // HEAD_DIM):
            first = h * HEAD_DIM // LANES * LANES
            span = slice(first, min(first + LANES, local))
            query, keys, values = (proj[t][at, span] for t in range(3))
            if query.shape[1] > HEAD_DIM:
                inside = iota(query.shape, 1) // HEAD_DIM == h % 2
                query = jnp.where(inside, query, jnp.zeros_like(query))
            chosen.append((query, keys, values))
    scores = [jnp.where(visible, dot_nt(query, keys), -jnp.inf) for query, keys, _ in chosen]
    tops = [jnp.max(score, axis=-1, keepdims=True) for score in scores]
    weights = [jnp.exp(score - top) for score, top in zip(scores, tops)]
    shares = [1.0 / jnp.sum(weight, axis=-1, keepdims=True) for weight in weights]
    probs = [(weight * share).astype(bf16) for weight, share in zip(weights, shares)]
    found = [dot_nn(prob, values) for prob, (_, _, values) in zip(probs, chosen)]
    many = local // HEAD_DIM
    first_head = iota((unit, LANES), 1) < HEAD_DIM
    blocks = [
        jnp.concatenate(
            [jnp.where(first_head, found[g * many], found[g * many + 1]), found[g * many + 2]], 1
        )
        for g in range(groups)
    ]
    whole = jnp.concatenate(blocks, 0).reshape(groups, rows, few, local)
    context = jnp.swapaxes(whole, 0, 1).reshape(tokens, local)
    half, some = tokens // 2, tokens // 4
    for c in range(2):
        part_of = context[c * half : (c + 1) * half]
        context_refs[c][0:half, :] = part_of[:, 0:LANES].astype(bf16)
        context_refs[c][half : half + some, :] = jnp.concatenate(
            [part_of[0:some, LANES:local], part_of[some:half, LANES:local]], 1
        ).astype(bf16)


def attend_columns_here(row_outs, live, row_context, own_codes, embed, col_qkv):
    parts = len(row_outs)
    tokens, width = row_context.shape
    local = width // parts
    return pl.pallas_call(
        functools.partial(column_kernel, parts),
        out_shape=(
            *[jax.ShapeDtypeStruct((tokens // 2 * local // LANES, LANES), bf16)] * 2,
            *[jax.ShapeDtypeStruct((tokens // 2, local), f32)] * 2,
        ),
        scratch_shapes=[
            pltpu.VMEM((parts, local, width), bf16),
            pltpu.VMEM((2 * CODES, 2 * width), bf16),
        ],
        cost_estimate=pl.CostEstimate(flops=2 * 10**9, bytes_accessed=10**6, transcendentals=0),
        compiler_params=pltpu.CompilerParams(vmem_limit_bytes=LARGE_VMEM),
        name="column_attention",
    )(*row_outs, live, row_context, own_codes, embed, col_qkv)


def finish_kernel(parts, *refs):
    context_refs = refs[:parts]
    mixed_ref, col_out_ref, *out_refs, weight_ref = refs[parts:]
    tokens, local = mixed_ref.shape
    some = tokens // 2
    part = lax.axis_index("head")
    for p in range(parts):
        weight_ref[p] = col_out_ref[:, p * local : (p + 1) * local]
    total = mixed_ref[...]
    for p in range(parts):
        context = context_refs[p]
        weight = weight_ref[part ^ p]
        rest = weight[:, LANES:local]
        zero = jnp.zeros_like(rest)
        left = jnp.concatenate([rest, zero], 1)
        right = jnp.concatenate([zero, rest], 1)
        last = context[tokens : tokens + some, :]
        total = (
            total
            + dot_nt(context[0:tokens, :], weight[:, 0:LANES])
            + jnp.concatenate([dot_nt(last, left), dot_nt(last, right)], 0)
        )
    own = tokens // len(out_refs) // 2
    for d, out_ref in enumerate(out_refs):
        first, second = (total[(2 * d + r) * own : (2 * d + r + 1) * own, :] for r in range(2))
        rest = jnp.concatenate([first[:, LANES:local], second[:, LANES:local]], 1)
        out_ref[...] = jnp.concatenate([first[:, 0:LANES], second[:, 0:LANES], rest], 0).astype(bf16)


def finish(contexts, mixed, col_out, slots):
    parts = len(contexts)
    tokens, local = mixed.shape
    return pl.pallas_call(
        functools.partial(finish_kernel, parts),
        out_shape=[jax.ShapeDtypeStruct((tokens // slots * local // LANES, LANES), bf16)] * slots,
        scratch_shapes=[pltpu.VMEM((parts, local, local), bf16)],
        cost_estimate=pl.CostEstimate(flops=10**9, bytes_accessed=10**6, transcendentals=0),
        compiler_params=pltpu.CompilerParams(vmem_limit_bytes=LARGE_VMEM),
        name="finish",
    )(*contexts, mixed, col_out)


def order_kernel(*refs):
    *slot_refs, out_ref, blocks_ref = refs
    groups = len(slot_refs)
    group = lax.axis_index("seq")
    for place, slot_ref in enumerate(slot_refs):
        d = groups - 1 - place
        blocks_ref[group ^ d] = slot_ref[...]
    local, cols = out_ref.shape[1:]
    own = cols // groups
    rest = local - LANES
    for part in range(3):
        piece = jnp.concatenate(
            [blocks_ref[g, part * own : (part + 1) * own, :] for g in range(groups)], 0
        )
        turned = piece.astype(f32).T.astype(bf16)
        if part < 2:
            out_ref[part, 0:LANES, :] = turned
        else:
            for r in range(2):
                out_ref[r, LANES:local, :] = turned[r * rest : (r + 1) * rest, :]


def order(slots, cols, local):
    return pl.pallas_call(
        order_kernel,
        out_shape=jax.ShapeDtypeStruct((2, local, cols), bf16),
        scratch_shapes=[pltpu.VMEM((len(slots),) + slots[0].shape, bf16)],
        compiler_params=pltpu.CompilerParams(vmem_limit_bytes=SMALL_VMEM),
        name="order",
    )(*slots)


def fast_body(ids, pad_mask, embed, row_qkv, row_out, col_qkv, col_out):
    rows_here, cols = ids.shape
    width = embed.shape[1]
    local = row_out.shape[0]
    groups, parts = lax.axis_size("seq"), lax.axis_size("head")
    own, rows = cols // groups, rows_here * groups
    each = groups // parts

    def pairwise(value, partner):
        order = [(g, p) for g in range(groups) for p in range(parts)]
        link = [(g * parts + p, partner(g, p)) for g, p in order]
        return lax.ppermute(value, ("seq", "head"), [(i, g * parts + p) for i, (g, p) in link])

    def sibling(g, p):
        return g, p ^ 1

    def across(g, p):
        return g, p ^ 2

    def opposite(g, p):
        return g, p ^ 3

    far = pairwise(row_out, across)
    coded = make_codes(ids, pad_mask)
    codes = [pairwise(coded, lambda g, p, b=b: (g ^ (p * each + b), p)) for b in range(each)]
    payload = pack(make_tables(embed, row_qkv), codes)
    payloads = [payload] + [pairwise(payload, to) for to in (sibling, across, opposite)]
    *payloads, near, far = lax.optimization_barrier((*payloads, row_out, far))
    row_outs = [row_out, pairwise(near, sibling), far, pairwise(far, sibling)]
    row_context, own_codes, live = attend_rows(payloads, rows, cols, own, width)
    *contexts, mixed_low, mixed_high = attend_columns_here(
        row_outs, live, row_context, own_codes, embed, col_qkv.reshape(3 * local, width)
    )
    slots = [None] * groups
    for c, mixed in ((1, mixed_high), (0, mixed_low)):
        beyond = pairwise(contexts[c], across)
        near = pairwise(contexts[c], sibling)
        whole = (contexts[c], near, beyond, pairwise(beyond, sibling))
        some = groups // 2
        for j, block in enumerate(finish(whole, mixed, col_out, some)):
            d = c * some + j
            slots[d] = pairwise(block, lambda g, p, d=d: (g ^ d, p)) if d else block
    return jnp.swapaxes(order(slots[::-1], cols, local), 1, 2)


def weight_fold(out_weight, piece):
    return jnp.einsum("rce,fe->rcf", piece, out_weight, preferred_element_type=f32)


def attend_columns(query, keys, values, key_live):
    rows_all, count_cols, local_width = query.shape
    heads_here = local_width // HEAD_DIM
    shape = (rows_all, count_cols, heads_here, HEAD_DIM)
    scores = jnp.einsum(
        "rchd,schd->chrs",
        query.reshape(shape),
        keys.reshape(shape),
        preferred_element_type=f32,
    ) * HEAD_DIM ** (-0.5)
    scores = jnp.where(key_live > 0, scores, -jnp.inf)
    probs = softmax_last(scores).astype(bf16)
    context = jnp.einsum(
        "chrs,schd->rchd", probs, values.reshape(shape), preferred_element_type=f32
    )
    return context.astype(bf16).reshape(rows_all, count_cols, local_width)


def send_back(context):
    return lax.all_to_all(context[:, None], "seq", split_axis=0, concat_axis=1, tiled=True)


def general_body(ids, pad_mask, embed, row_qkv, row_out, col_qkv, col_out):
    rows_here, cols = ids.shape
    width = embed.shape[1]
    local_width = row_out.shape[0]
    heads_here = local_width // HEAD_DIM
    groups = lax.axis_size("seq")
    per_group = cols // groups
    codes = lax.broadcasted_iota(jnp.int32, (1, 1, embed.shape[0]), 2)
    onehot = (ids[:, :, None] == codes).astype(bf16)
    embedded = jnp.einsum("rcv,vd->rcd", onehot, embed, preferred_element_type=f32)
    normed = layer_norm(embedded).astype(bf16)
    row_proj = jnp.einsum("rcd,ted->trce", normed, row_qkv, preferred_element_type=f32)
    row_proj = row_proj.astype(bf16)
    live = pad_mask.astype(bf16)
    head_shape = (rows_here, cols, heads_here, HEAD_DIM)
    query = (row_proj[0] * live[:, None, None]).reshape(head_shape)
    keys = row_proj[1].reshape(head_shape)
    values = row_proj[2].reshape(head_shape)
    partial_scores = jnp.einsum("rihd,rjhd->hij", query, keys, preferred_element_type=f32)
    count_here = jnp.sum(pad_mask.astype(f32))
    scale = HEAD_DIM ** (-0.5)
    total, count = lax.psum((partial_scores, count_here), "seq")
    row_probs = softmax_last(total * (scale / jnp.sqrt(count))).astype(bf16)
    row_context = jnp.einsum("hij,rjhd->rihd", row_probs, values, preferred_element_type=f32)
    row_context = row_context.astype(bf16).reshape(rows_here, cols, local_width)
    start_feature = lax.axis_index("head") * local_width
    resident = lax.dynamic_slice_in_dim(embedded, start_feature, local_width, 2)
    row_update = weight_fold(row_out, lax.all_gather(row_context, "head", axis=2, tiled=True))
    mixed = resident + row_update
    sums, squares = lax.psum((jnp.sum(mixed, axis=-1), jnp.sum(mixed * mixed, axis=-1)), "head")
    mean = sums / width
    spread = squares / width - mean * mean
    normed_here = ((mixed - mean[..., None]) * lax.rsqrt(spread[..., None] + EPS)).astype(bf16)
    live_tile = jnp.broadcast_to(live[:, None, None, None], (rows_here, groups, per_group, 1))
    normed_full = lax.all_gather(normed_here, "head", axis=2, tiled=True)
    col_proj = jnp.einsum("rcd,ted->rcte", normed_full, col_qkv, preferred_element_type=f32)
    packed = col_proj.astype(bf16).reshape(rows_here, groups, per_group, 3 * local_width)
    received = lax.all_to_all(packed, "seq", split_axis=1, concat_axis=0, tiled=True)
    mask_part = lax.all_to_all(live_tile, "seq", split_axis=1, concat_axis=0, tiled=True)
    column_out = send_back(
        attend_columns(
            received[:, 0, :, :local_width],
            received[:, 0, :, local_width : 2 * local_width],
            received[:, 0, :, 2 * local_width :],
            mask_part[:, 0, 0, 0],
        )
    )
    column_out = column_out.reshape(rows_here, cols, local_width)
    col_update = weight_fold(col_out, lax.all_gather(column_out, "head", axis=2, tiled=True))
    return (mixed + col_update).astype(bf16)


def body(ids, pad_mask, embed, row_qkv, row_out, col_qkv, col_out):
    rows_here, cols = ids.shape
    groups = lax.axis_size("seq")
    own, rows = cols // groups, rows_here * groups
    parts = lax.axis_size("head")
    local = row_out.shape[0]
    fits = (
        groups & (groups - 1) == 0
        and parts == 4
        and groups % parts == 0
        and rows * 8 == LANES
        and rows_here == 2
        and rows <= 8 * parts
        and own % 32 == 0
        and cols + LANES <= 3 * local
        and local == LANES + HEAD_DIM
        and embed.shape[0] <= VOCAB_ROWS
    )
    chosen = fast_body if fits else general_body
    return chosen(ids, pad_mask, embed, row_qkv, row_out, col_qkv, col_out)


def solution(mesh):
    placed = (
        P("seq", None),
        P("seq"),
        P(),
        P(None, "head", None),
        P("head", None),
        P(None, "head", None),
        P("head", None),
    )
    return jax.shard_map(
        body, mesh=mesh, in_specs=placed, out_specs=P("seq", None, "head"), check_vma=False
    )
```

```python
import functools

import jax
import jax.numpy as jnp
from jax import lax
from jax.experimental import pallas as pl
from jax.experimental.pallas import tpu as pltpu
from jax.sharding import PartitionSpec as P

HEAD_DIM = 64
EPS = 1e-05
LANES = 128
CODES = 64
TABLE_ROWS = 40

SMALL_VMEM = 8 * 1024 * 1024
LARGE_VMEM = 32 * 1024 * 1024

f32 = jnp.float32
bf16 = jnp.bfloat16


def layer_norm(values):
    mean = jnp.mean(values, axis=-1, keepdims=True)
    centred = values - mean
    spread = jnp.mean(centred * centred, axis=-1, keepdims=True)
    return centred * lax.rsqrt(spread + EPS)


def softmax_last(scores):
    top = jnp.max(scores, axis=-1, keepdims=True)
    weights = jnp.exp(scores - top)
    return weights * (1.0 / jnp.sum(weights, axis=-1, keepdims=True))


def dot_nt(left, right):
    return lax.dot_general(left, right, (((1,), (1,)), ((), ())), preferred_element_type=f32)


def dot_nn(left, right):
    return jnp.dot(left, right, preferred_element_type=f32)


def in_hbm(value):
    return pltpu.with_memory_space_constraint(value, pltpu.HBM)


def iota(shape, axis):
    return lax.broadcasted_iota(jnp.int32, shape, axis)


def table_kernel(
    ids_hbm,
    live_hbm,
    embed_hbm,
    qkv_hbm,
    out_ref,
    coded_ref,
    ids_ref,
    live_ref,
    embed_ref,
    qkv_ref,
    padded_ref,
    sems,
):
    kinds = qkv_ref.shape[0]
    loads = [
        pltpu.make_async_copy(embed_hbm, embed_ref, sems.at[kinds]),
        pltpu.make_async_copy(ids_hbm, ids_ref, sems.at[kinds + 1]),
        pltpu.make_async_copy(live_hbm, live_ref, sems.at[kinds + 2]),
    ]
    loads += [
        pltpu.make_async_copy(qkv_hbm.at[t], qkv_ref.at[t], sems.at[t]) for t in range(kinds)
    ]
    for load in loads:
        load.start()
    padded_ref[...] = jnp.zeros(padded_ref.shape, f32)
    for load in loads[0:3]:
        load.wait()
    padded_ref[0 : embed_ref.shape[0], :] = embed_ref[...].astype(f32)
    normed = layer_norm(padded_ref[...]).astype(bf16)
    row = iota(ids_ref.shape, 0)
    live = jnp.zeros(ids_ref.shape, jnp.int32)
    for r in range(ids_ref.shape[0]):
        live = jnp.where(row == r, live_ref[r], live)
    coded = ids_ref[...] + 65536 * live
    for g in range(coded_ref.shape[0]):
        coded_ref[g] = coded
    tables = []
    for t in range(kinds):
        loads[3 + t].wait()
        tables.append(dot_nt(normed, qkv_ref[t]))
    out_ref[...] = jnp.concatenate(tables, 1).astype(bf16)


def make_tables(ids, pad_mask, embed, row_qkv, groups):
    kinds, local, width = row_qkv.shape
    return pl.pallas_call(
        table_kernel,
        out_shape=(
            jax.ShapeDtypeStruct((TABLE_ROWS, kinds * local), bf16),
            jax.ShapeDtypeStruct((groups,) + ids.shape, jnp.int32),
        ),
        in_specs=[pl.BlockSpec(memory_space=pltpu.HBM)] * 4,
        scratch_shapes=[
            pltpu.VMEM(ids.shape, jnp.int32),
            pltpu.SMEM(pad_mask.shape, jnp.int32),
            pltpu.VMEM(embed.shape, bf16),
            pltpu.VMEM(row_qkv.shape, bf16),
            pltpu.VMEM((TABLE_ROWS, width), f32),
            pltpu.SemaphoreType.DMA((kinds + 3,)),
        ],
        cost_estimate=pl.CostEstimate(
            flops=2 * TABLE_ROWS * row_qkv.size,
            bytes_accessed=2 * row_qkv.size,
            transcendentals=0,
        ),
        compiler_params=pltpu.CompilerParams(vmem_limit_bytes=SMALL_VMEM),
        name="tables",
    )(in_hbm(ids), in_hbm(pad_mask), in_hbm(embed), in_hbm(row_qkv))


def halves(pair):
    lane = iota(pair.shape, 1)
    zero = jnp.zeros_like(pair)
    return jnp.where(lane < HEAD_DIM, pair, zero), jnp.where(lane < HEAD_DIM, zero, pair)


def spread_pair(pair):
    first, second = halves(pair)
    zero = jnp.zeros_like(pair)
    return jnp.concatenate(
        [
            jnp.concatenate([first, zero], 1),
            jnp.concatenate([zero, first], 1),
            jnp.concatenate([second, zero], 1),
            jnp.concatenate([zero, second], 1),
        ],
        0,
    )


def double(block):
    zero = jnp.zeros_like(block)
    return jnp.concatenate(
        [jnp.concatenate([block, zero], 1), jnp.concatenate([zero, block], 1)], 0
    )


def row_kernel(parts, *refs):
    tables_refs, refs = refs[:parts], refs[parts:]
    (
        codes_ref,
        row_context_ref,
        own_ref,
        live_ref,
        tables_ref,
        table_ref,
        hot_ref,
        live_own_ref,
        sum_ref,
        spread_ref,
    ) = refs
    depth, cols = hot_ref.shape
    rows = depth // CODES
    pairs = rows // 2
    own = live_own_ref.shape[0] // pairs
    width = row_context_ref.shape[1]
    heads = width // HEAD_DIM
    local = width // parts
    group = lax.axis_index("seq")
    part = lax.axis_index("head")
    for p in range(parts):
        tables_ref[part ^ p] = tables_refs[p][...]

    for t in range(3):
        table_ref[t, 0:TABLE_ROWS, :] = jnp.concatenate(
            [tables_ref[p, :, t * local : (t + 1) * local] for p in range(parts)], 1
        )
        table_ref[t, TABLE_ROWS:CODES, :] = jnp.zeros((CODES - TABLE_ROWS, width), bf16)

    coded = jnp.concatenate([codes_ref[g] for g in range(codes_ref.shape[0])], 0)
    ids = (coded & 0xFFFF).astype(f32)
    live = (coded[:, 0:LANES] >> 16).astype(f32)
    live_ref[...] = live
    code = iota((CODES, cols), 0).astype(f32)
    for r in range(rows):
        hot = jnp.broadcast_to(ids[r : r + 1, :], (CODES, cols)) == code
        hot_ref[r * CODES : (r + 1) * CODES, :] = hot.astype(f32).astype(bf16)

    pick = (iota((own, cols), 1) == group * own + iota((own, cols), 0)).astype(f32).astype(bf16)
    mine = dot_nt(pick, ids.astype(bf16))
    lane = iota((own, LANES), 1)
    first_half = lane < CODES
    lane_code = jnp.where(first_half, lane, lane - CODES).astype(f32)
    for k in range(pairs):
        value = jnp.where(first_half, mine[:, 2 * k : 2 * k + 1], mine[:, 2 * k + 1 : 2 * k + 2])
        hot = (value == lane_code).astype(f32)
        alive = jnp.where(first_half, live[2 * k : 2 * k + 1, :], live[2 * k + 1 : 2 * k + 2, :])
        own_ref[k * own : (k + 1) * own, :] = hot.astype(bf16)
        live_own_ref[k * own : (k + 1) * own, :] = (hot * alive).astype(bf16)

    spans = [slice(hp * LANES, (hp + 1) * LANES) for hp in range(heads // 2)]
    queries = [spread_pair(table_ref[0, :, span]) for span in spans]
    keys = [double(table_ref[1, :, span]) for span in spans]
    scores = [dot_nt(query, key) for query, key in zip(queries, keys)]
    high = [score.astype(bf16) for score in scores]
    low = [(score - part.astype(f32)).astype(bf16) for score, part in zip(scores, high)]
    for hp in range(heads // 2):
        for h2 in range(2):
            these = slice(h2 * LANES, (h2 + 1) * LANES)
            looked = dot_nn(
                live_own_ref[...], jnp.concatenate([high[hp][these], low[hp][these]], 1)
            ).astype(bf16)
            base = (hp * 2 + h2) * own
            for piece in range(2):
                for k in range(pairs):
                    to = piece * depth + k * LANES
                    sum_ref[base : base + own, to : to + LANES] = looked[
                        k * own : (k + 1) * own, piece * LANES : (piece + 1) * LANES
                    ]
    tied = dot_nn(sum_ref[:, 0:depth], hot_ref[...]) + dot_nn(
        sum_ref[:, depth : 2 * depth], hot_ref[...]
    )
    count = jnp.sum(live, axis=0, keepdims=True)[:, 0:1]
    probs = softmax_last(tied * (HEAD_DIM ** (-0.5) / jnp.sqrt(count))).astype(bf16)

    spread_ref[...] = dot_nt(probs, hot_ref[...]).astype(bf16)
    values = [spread_pair(table_ref[2, :, span]) for span in spans]
    contexts = []
    for hp in range(heads // 2):
        first = (hp * 2) * own
        weights = jnp.concatenate(
            [
                jnp.concatenate(
                    [
                        spread_ref[first : first + own, k * LANES : (k + 1) * LANES],
                        spread_ref[first + own : first + 2 * own, k * LANES : (k + 1) * LANES],
                    ],
                    1,
                )
                for k in range(pairs)
            ],
            0,
        )
        contexts.append(dot_nn(weights, values[hp]).astype(bf16))
    for hp in range(heads // 2):
        for k in range(pairs):
            for r2 in range(2):
                at = (2 * k + r2) * own
                row_context_ref[at : at + own, spans[hp]] = contexts[hp][
                    k * own : (k + 1) * own, r2 * LANES : (r2 + 1) * LANES
                ]


def attend_rows(tables, codes, rows, cols, own, width):
    heads = width // HEAD_DIM
    parts = len(tables)
    return pl.pallas_call(
        functools.partial(row_kernel, parts),
        out_shape=(
            jax.ShapeDtypeStruct((rows * own, width), bf16),
            jax.ShapeDtypeStruct((rows * own // 2, LANES), bf16),
            jax.ShapeDtypeStruct((rows, LANES), f32),
        ),
        scratch_shapes=[
            pltpu.VMEM((parts,) + tables[0].shape, bf16),
            pltpu.VMEM((3, CODES, width), bf16),
            pltpu.VMEM((rows * CODES, cols), bf16),
            pltpu.VMEM((rows // 2 * own, LANES), bf16),
            pltpu.VMEM((heads * own, 2 * rows * CODES), bf16),
            pltpu.VMEM((heads * own, rows * CODES), bf16),
        ],
        cost_estimate=pl.CostEstimate(flops=3 * 10**9, bytes_accessed=10**6, transcendentals=0),
        compiler_params=pltpu.CompilerParams(vmem_limit_bytes=LARGE_VMEM),
        name="row_attention",
    )(*tables, codes)


def column_kernel(parts, *refs):
    row_out_refs, refs = refs[:parts], refs[parts:]
    (
        live_ref,
        row_context_ref,
        own_ref,
        embed_ref,
        col_qkv_ref,
        *out_refs,
        row_out_ref,
        embed2_ref,
    ) = refs
    context_refs, mixed_refs = out_refs[:2], out_refs[2:]
    rows = live_ref.shape[0]
    tokens, width = row_context_ref.shape
    pairs = rows // 2
    own = tokens // rows
    vocab = embed_ref.shape[0]
    local = width // parts
    part = lax.axis_index("head")

    for p in range(parts):
        row_out_ref[part ^ p] = row_out_refs[p][...]
    embed2_ref[...] = jnp.zeros(embed2_ref.shape, bf16)
    embed2_ref[0:vocab, 0:width] = embed_ref[...]
    embed2_ref[CODES : CODES + vocab, width : 2 * width] = embed_ref[...]

    embedded2 = dot_nn(own_ref[...], embed2_ref[...])
    embedded = jnp.concatenate(
        [
            embedded2[k * own : (k + 1) * own, r2 * width : (r2 + 1) * width]
            for k in range(pairs)
            for r2 in range(2)
        ],
        0,
    )
    mixed = embedded + dot_nt(row_context_ref[...], row_out_ref[...].reshape(width, width))
    for p in range(parts):

        @pl.when(part == p)
        def _():
            for c in range(2):
                mixed_refs[c][...] = mixed[
                    c * tokens // 2 : (c + 1) * tokens // 2, p * local : (p + 1) * local
                ]

    normed = layer_norm(mixed).astype(bf16)

    few = 8
    groups = own // few
    unit = rows * few

    def regroup(values):
        shape = (rows, groups, few, values.shape[1])
        return jnp.swapaxes(values.reshape(shape), 0, 1).reshape(tokens, values.shape[1])

    proj = [
        dot_nt(normed, col_qkv_ref[t * local : (t + 1) * local, :]) for t in range(3)
    ]
    proj[0] = proj[0] * HEAD_DIM ** (-0.5)
    proj = [regroup(values).astype(bf16) for values in proj]
    sub, lan = iota((unit, unit), 0), iota((unit, unit), 1)
    same_column = (sub % few) == (lan % few)
    seq_of_lane = iota((rows, unit), 1) // few
    live_lane = jnp.sum(
        jnp.where(seq_of_lane == iota((rows, unit), 0), live_ref[...], 0.0), axis=0, keepdims=True
    )
    visible = jnp.logical_and(same_column, jnp.broadcast_to(live_lane, (unit, unit)) > 0)
    chosen = []
    for g in range(groups):
        at = slice(g * unit, (g + 1) * unit)
        for h in range(local // HEAD_DIM):
            first = h * HEAD_DIM // LANES * LANES
            span = slice(first, min(first + LANES, local))
            query, keys, values = (proj[t][at, span] for t in range(3))
            if query.shape[1] > HEAD_DIM:
                inside = iota(query.shape, 1) // HEAD_DIM == h % 2
                query = jnp.where(inside, query, jnp.zeros_like(query))
            chosen.append((query, keys, values))
    scores = [jnp.where(visible, dot_nt(query, keys), -jnp.inf) for query, keys, _ in chosen]
    tops = [jnp.max(score, axis=-1, keepdims=True) for score in scores]
    weights = [jnp.exp(score - top) for score, top in zip(scores, tops)]
    shares = [1.0 / jnp.sum(weight, axis=-1, keepdims=True) for weight in weights]
    probs = [(weight * share).astype(bf16) for weight, share in zip(weights, shares)]
    found = [dot_nn(prob, values) for prob, (_, _, values) in zip(probs, chosen)]
    many = local // HEAD_DIM
    first_head = iota((unit, LANES), 1) < HEAD_DIM
    blocks = [
        jnp.concatenate(
            [jnp.where(first_head, found[g * many], found[g * many + 1]), found[g * many + 2]], 1
        )
        for g in range(groups)
    ]
    whole = jnp.concatenate(blocks, 0).reshape(groups, rows, few, local)
    context = jnp.swapaxes(whole, 0, 1).reshape(tokens, local)
    half, some = tokens // 2, tokens // 4
    for c in range(2):
        part_of = context[c * half : (c + 1) * half]
        context_refs[c][0:half, :] = part_of[:, 0:LANES].astype(bf16)
        context_refs[c][half : half + some, :] = jnp.concatenate(
            [part_of[0:some, LANES:local], part_of[some:half, LANES:local]], 1
        ).astype(bf16)


def attend_columns_here(row_outs, live, row_context, own_codes, embed, col_qkv):
    parts = len(row_outs)
    tokens, width = row_context.shape
    local = width // parts
    return pl.pallas_call(
        functools.partial(column_kernel, parts),
        out_shape=(
            *[jax.ShapeDtypeStruct((tokens // 2 * local // LANES, LANES), bf16)] * 2,
            *[jax.ShapeDtypeStruct((tokens // 2, local), f32)] * 2,
        ),
        scratch_shapes=[
            pltpu.VMEM((parts, local, width), bf16),
            pltpu.VMEM((2 * CODES, 2 * width), bf16),
        ],
        cost_estimate=pl.CostEstimate(flops=2 * 10**9, bytes_accessed=10**6, transcendentals=0),
        compiler_params=pltpu.CompilerParams(vmem_limit_bytes=LARGE_VMEM),
        name="column_attention",
    )(*row_outs, live, row_context, own_codes, embed, col_qkv)


def finish_kernel(parts, groups, *refs):
    context_refs = [refs[:parts], refs[parts : 2 * parts]]
    mixed_refs = refs[2 * parts : 2 * parts + 2]
    col_out_ref, out_ref, weight_ref = refs[2 * parts + 2 :]
    tokens, local = mixed_refs[0].shape
    some = tokens // 2
    part = lax.axis_index("head")
    for p in range(parts):
        weight_ref[p] = col_out_ref[:, p * local : (p + 1) * local]
    totals = [ref[...] for ref in mixed_refs]
    for p in range(parts):
        weight = weight_ref[part ^ p]
        rest = weight[:, LANES:local]
        zero = jnp.zeros_like(rest)
        left = jnp.concatenate([rest, zero], 1)
        right = jnp.concatenate([zero, rest], 1)
        for c in range(2):
            context = context_refs[c][p]
            last = context[tokens : tokens + some, :]
            totals[c] = (
                totals[c]
                + dot_nt(context[0:tokens, :], weight[:, 0:LANES])
                + jnp.concatenate([dot_nt(last, left), dot_nt(last, right)], 0)
            )
    slots = groups // 2
    own = tokens // slots // 2
    for d in range(groups):
        first, second = (
            totals[d // slots][(2 * (d % slots) + r) * own : (2 * (d % slots) + r + 1) * own, :]
            for r in range(2)
        )
        rest = jnp.concatenate([first[:, LANES:local], second[:, LANES:local]], 1)
        out_ref[d] = jnp.concatenate(
            [first[:, 0:LANES], second[:, 0:LANES], rest], 0
        ).astype(bf16)


def finish(contexts, mixed, col_out, groups):
    parts = len(contexts[0])
    tokens, local = mixed[0].shape
    return pl.pallas_call(
        functools.partial(finish_kernel, parts, groups),
        out_shape=jax.ShapeDtypeStruct(
            (groups, 2 * tokens // groups * local // LANES, LANES), bf16
        ),
        scratch_shapes=[pltpu.VMEM((parts, local, local), bf16)],
        compiler_params=pltpu.CompilerParams(vmem_limit_bytes=LARGE_VMEM),
        name="finish",
    )(*contexts[0], *contexts[1], *mixed, col_out)


def order_kernel(blocks_ref, out_ref):
    groups = blocks_ref.shape[0]
    local, cols = out_ref.shape[1:]
    own = cols // groups
    rest = local - LANES
    for part in range(3):
        piece = jnp.concatenate(
            [blocks_ref[g, part * own : (part + 1) * own, :] for g in range(groups)], 0
        )
        turned = piece.astype(f32).T.astype(bf16)
        if part < 2:
            out_ref[part, 0:LANES, :] = turned
        else:
            for r in range(2):
                out_ref[r, LANES:local, :] = turned[r * rest : (r + 1) * rest, :]


def order(blocks, cols, local):
    return pl.pallas_call(
        order_kernel,
        out_shape=jax.ShapeDtypeStruct((2, local, cols), bf16),
        compiler_params=pltpu.CompilerParams(vmem_limit_bytes=SMALL_VMEM),
        name="order",
    )(blocks)


def fast_body(ids, pad_mask, embed, row_qkv, row_out, col_qkv, col_out):
    rows_here, cols = ids.shape
    width = embed.shape[1]
    local = row_out.shape[0]
    groups, parts = lax.axis_size("seq"), lax.axis_size("head")
    own, rows = cols // groups, rows_here * groups

    def pairwise(value, partner):
        order = [(g, p) for g in range(groups) for p in range(parts)]
        link = [(g * parts + p, partner(g, p)) for g, p in order]
        return lax.ppermute(value, ("seq", "head"), [(i, g * parts + p) for i, (g, p) in link])

    def sibling(g, p):
        return g, p ^ 1

    def across(g, p):
        return g, p ^ 2

    def opposite(g, p):
        return g, p ^ 3

    far = pairwise(row_out, across)
    table, codes = make_tables(ids, pad_mask, embed, row_qkv, groups)
    tables = [table] + [pairwise(table, to) for to in (sibling, across, opposite)]
    codes = lax.all_to_all(codes, "seq", split_axis=0, concat_axis=0, tiled=True)
    codes, near, far = lax.optimization_barrier((codes, row_out, far))
    row_outs = [row_out, pairwise(near, sibling), far, pairwise(far, sibling)]
    row_context, own_codes, live = attend_rows(tables, codes, rows, cols, own, width)
    *halves_here, mixed_low, mixed_high = attend_columns_here(
        row_outs, live, row_context, own_codes, embed, col_qkv.reshape(3 * local, width)
    )
    contexts = []
    for context in halves_here:
        beyond = pairwise(context, across)
        contexts.append(
            (context, pairwise(context, sibling), beyond, pairwise(beyond, sibling))
        )
    blocks = finish(contexts, (mixed_low, mixed_high), col_out, groups)
    blocks = lax.all_to_all(blocks, "seq", split_axis=0, concat_axis=0, tiled=True)
    return jnp.swapaxes(order(blocks, cols, local), 1, 2)


def weight_fold(out_weight, piece):
    return jnp.einsum("rce,fe->rcf", piece, out_weight, preferred_element_type=f32)


def attend_columns(query, keys, values, key_live):
    rows_all, count_cols, local_width = query.shape
    heads_here = local_width // HEAD_DIM
    shape = (rows_all, count_cols, heads_here, HEAD_DIM)
    scores = jnp.einsum(
        "rchd,schd->chrs",
        query.reshape(shape),
        keys.reshape(shape),
        preferred_element_type=f32,
    ) * HEAD_DIM ** (-0.5)
    scores = jnp.where(key_live > 0, scores, -jnp.inf)
    probs = softmax_last(scores).astype(bf16)
    context = jnp.einsum(
        "chrs,schd->rchd", probs, values.reshape(shape), preferred_element_type=f32
    )
    return context.astype(bf16).reshape(rows_all, count_cols, local_width)


def send_back(context):
    return lax.all_to_all(context[:, None], "seq", split_axis=0, concat_axis=1, tiled=True)


def general_body(ids, pad_mask, embed, row_qkv, row_out, col_qkv, col_out):
    rows_here, cols = ids.shape
    width = embed.shape[1]
    local_width = row_out.shape[0]
    heads_here = local_width // HEAD_DIM
    groups = lax.axis_size("seq")
    per_group = cols // groups
    codes = lax.broadcasted_iota(jnp.int32, (1, 1, embed.shape[0]), 2)
    onehot = (ids[:, :, None] == codes).astype(bf16)
    embedded = jnp.einsum("rcv,vd->rcd", onehot, embed, preferred_element_type=f32)
    normed = layer_norm(embedded).astype(bf16)
    row_proj = jnp.einsum("rcd,ted->trce", normed, row_qkv, preferred_element_type=f32)
    row_proj = row_proj.astype(bf16)
    live = pad_mask.astype(bf16)
    head_shape = (rows_here, cols, heads_here, HEAD_DIM)
    query = (row_proj[0] * live[:, None, None]).reshape(head_shape)
    keys = row_proj[1].reshape(head_shape)
    values = row_proj[2].reshape(head_shape)
    partial_scores = jnp.einsum("rihd,rjhd->hij", query, keys, preferred_element_type=f32)
    count_here = jnp.sum(pad_mask.astype(f32))
    scale = HEAD_DIM ** (-0.5)
    total, count = lax.psum((partial_scores, count_here), "seq")
    row_probs = softmax_last(total * (scale / jnp.sqrt(count))).astype(bf16)
    row_context = jnp.einsum("hij,rjhd->rihd", row_probs, values, preferred_element_type=f32)
    row_context = row_context.astype(bf16).reshape(rows_here, cols, local_width)
    start_feature = lax.axis_index("head") * local_width
    resident = lax.dynamic_slice_in_dim(embedded, start_feature, local_width, 2)
    row_update = weight_fold(row_out, lax.all_gather(row_context, "head", axis=2, tiled=True))
    mixed = resident + row_update
    sums, squares = lax.psum((jnp.sum(mixed, axis=-1), jnp.sum(mixed * mixed, axis=-1)), "head")
    mean = sums / width
    spread = squares / width - mean * mean
    normed_here = ((mixed - mean[..., None]) * lax.rsqrt(spread[..., None] + EPS)).astype(bf16)
    live_tile = jnp.broadcast_to(live[:, None, None, None], (rows_here, groups, per_group, 1))
    normed_full = lax.all_gather(normed_here, "head", axis=2, tiled=True)
    col_proj = jnp.einsum("rcd,ted->rcte", normed_full, col_qkv, preferred_element_type=f32)
    packed = col_proj.astype(bf16).reshape(rows_here, groups, per_group, 3 * local_width)
    received = lax.all_to_all(packed, "seq", split_axis=1, concat_axis=0, tiled=True)
    mask_part = lax.all_to_all(live_tile, "seq", split_axis=1, concat_axis=0, tiled=True)
    column_out = send_back(
        attend_columns(
            received[:, 0, :, :local_width],
            received[:, 0, :, local_width : 2 * local_width],
            received[:, 0, :, 2 * local_width :],
            mask_part[:, 0, 0, 0],
        )
    )
    column_out = column_out.reshape(rows_here, cols, local_width)
    col_update = weight_fold(col_out, lax.all_gather(column_out, "head", axis=2, tiled=True))
    return (mixed + col_update).astype(bf16)


def body(ids, pad_mask, embed, row_qkv, row_out, col_qkv, col_out):
    rows_here, cols = ids.shape
    groups = lax.axis_size("seq")
    own, rows = cols // groups, rows_here * groups
    parts = lax.axis_size("head")
    local = row_out.shape[0]
    fits = (
        parts == 4
        and groups % 2 == 0
        and rows * 8 == LANES
        and rows_here == 2
        and own % 32 == 0
        and cols >= LANES
        and local == LANES + HEAD_DIM
        and embed.shape[0] <= TABLE_ROWS
    )
    chosen = fast_body if fits else general_body
    return chosen(ids, pad_mask, embed, row_qkv, row_out, col_qkv, col_out)


def solution(mesh):
    placed = (
        P("seq", None),
        P("seq"),
        P(),
        P(None, "head", None),
        P("head", None),
        P(None, "head", None),
        P("head", None),
    )
    return jax.shard_map(
        body, mesh=mesh, in_specs=placed, out_specs=P("seq", None, "head"), check_vma=False
    )
```

```python
import functools

import jax
import jax.numpy as jnp
from jax import lax
from jax.experimental import pallas as pl
from jax.experimental.pallas import tpu as pltpu
from jax.sharding import PartitionSpec as P

HEAD_DIM = 64
EPS = 1e-05
LANES = 128
CODES = 64
TABLE_ROWS = 40

SMALL_VMEM = 8 * 1024 * 1024
LARGE_VMEM = 32 * 1024 * 1024

f32 = jnp.float32
bf16 = jnp.bfloat16


def layer_norm(values):
    mean = jnp.mean(values, axis=-1, keepdims=True)
    centred = values - mean
    spread = jnp.mean(centred * centred, axis=-1, keepdims=True)
    return centred * lax.rsqrt(spread + EPS)


def softmax_last(scores):
    top = jnp.max(scores, axis=-1, keepdims=True)
    weights = jnp.exp(scores - top)
    return weights * (1.0 / jnp.sum(weights, axis=-1, keepdims=True))


def dot_nt(left, right):
    return lax.dot_general(left, right, (((1,), (1,)), ((), ())), preferred_element_type=f32)


def dot_nn(left, right):
    return jnp.dot(left, right, preferred_element_type=f32)


def in_hbm(value):
    return pltpu.with_memory_space_constraint(value, pltpu.HBM)


def iota(shape, axis):
    return lax.broadcasted_iota(jnp.int32, shape, axis)


def code_kernel(ids_hbm, live_hbm, out_ref, ids_ref, live_ref, sems):
    loads = [
        pltpu.make_async_copy(ids_hbm, ids_ref, sems.at[0]),
        pltpu.make_async_copy(live_hbm, live_ref, sems.at[1]),
    ]
    for load in loads:
        load.start()
    for load in loads:
        load.wait()
    row = iota(ids_ref.shape, 0)
    live = jnp.zeros(ids_ref.shape, jnp.int32)
    for r in range(ids_ref.shape[0]):
        live = jnp.where(row == r, live_ref[r], live)
    coded = ids_ref[...] + 65536 * live
    for g in range(out_ref.shape[0]):
        out_ref[g] = coded


def make_codes(ids, pad_mask, groups):
    return pl.pallas_call(
        code_kernel,
        out_shape=jax.ShapeDtypeStruct((groups,) + ids.shape, jnp.int32),
        in_specs=[pl.BlockSpec(memory_space=pltpu.HBM)] * 2,
        scratch_shapes=[
            pltpu.VMEM(ids.shape, jnp.int32),
            pltpu.SMEM(pad_mask.shape, jnp.int32),
            pltpu.SemaphoreType.DMA((2,)),
        ],
        compiler_params=pltpu.CompilerParams(vmem_limit_bytes=SMALL_VMEM),
        name="codes",
    )(in_hbm(ids), in_hbm(pad_mask))


def table_kernel(embed_hbm, qkv_hbm, out_ref, embed_ref, qkv_ref, padded_ref, sems):
    kinds = qkv_ref.shape[0]
    loads = [pltpu.make_async_copy(embed_hbm, embed_ref, sems.at[kinds])]
    loads += [
        pltpu.make_async_copy(qkv_hbm.at[t], qkv_ref.at[t], sems.at[t]) for t in range(kinds)
    ]
    for load in loads:
        load.start()
    padded_ref[...] = jnp.zeros(padded_ref.shape, f32)
    loads[0].wait()
    padded_ref[0 : embed_ref.shape[0], :] = embed_ref[...].astype(f32)
    normed = layer_norm(padded_ref[...]).astype(bf16)
    tables = []
    for t in range(kinds):
        loads[1 + t].wait()
        tables.append(dot_nt(normed, qkv_ref[t]))
    out_ref[...] = jnp.concatenate(tables, 1).astype(bf16)


def make_tables(embed, row_qkv):
    kinds, local, width = row_qkv.shape
    return pl.pallas_call(
        table_kernel,
        out_shape=jax.ShapeDtypeStruct((TABLE_ROWS, kinds * local), bf16),
        in_specs=[pl.BlockSpec(memory_space=pltpu.HBM)] * 2,
        scratch_shapes=[
            pltpu.VMEM(embed.shape, bf16),
            pltpu.VMEM(row_qkv.shape, bf16),
            pltpu.VMEM((TABLE_ROWS, width), f32),
            pltpu.SemaphoreType.DMA((kinds + 1,)),
        ],
        cost_estimate=pl.CostEstimate(
            flops=2 * 10**9, bytes_accessed=2 * row_qkv.size, transcendentals=0
        ),
        compiler_params=pltpu.CompilerParams(vmem_limit_bytes=SMALL_VMEM),
        name="tables",
    )(in_hbm(embed), in_hbm(row_qkv))


def halves(pair):
    lane = iota(pair.shape, 1)
    zero = jnp.zeros_like(pair)
    return jnp.where(lane < HEAD_DIM, pair, zero), jnp.where(lane < HEAD_DIM, zero, pair)


def spread_pair(pair):
    first, second = halves(pair)
    zero = jnp.zeros_like(pair)
    return jnp.concatenate(
        [
            jnp.concatenate([first, zero], 1),
            jnp.concatenate([zero, first], 1),
            jnp.concatenate([second, zero], 1),
            jnp.concatenate([zero, second], 1),
        ],
        0,
    )


def double(block):
    zero = jnp.zeros_like(block)
    return jnp.concatenate(
        [jnp.concatenate([block, zero], 1), jnp.concatenate([zero, block], 1)], 0
    )


def slot_order(groups):
    return list(range(0, groups, 2)) + list(range(1, groups, 2))


def row_kernel(parts, *refs):
    tables_refs, refs = refs[:parts], refs[parts:]
    (
        codes_ref,
        row_context_ref,
        own_ref,
        live_ref,
        tables_ref,
        table_ref,
        hot_ref,
        live_own_ref,
        sum_ref,
        spread_ref,
    ) = refs
    depth, cols = hot_ref.shape
    rows = depth // CODES
    pairs = rows // 2
    own = live_own_ref.shape[0] // pairs
    width = row_context_ref.shape[1]
    heads = width // HEAD_DIM
    local = width // parts
    group = lax.axis_index("seq")
    part = lax.axis_index("head")
    for p in range(parts):
        tables_ref[part ^ p] = tables_refs[p][...]

    for t in range(3):
        table_ref[t, 0:TABLE_ROWS, :] = jnp.concatenate(
            [tables_ref[p, :, t * local : (t + 1) * local] for p in range(parts)], 1
        )
        table_ref[t, TABLE_ROWS:CODES, :] = jnp.zeros((CODES - TABLE_ROWS, width), bf16)

    coded = jnp.concatenate([codes_ref[group ^ d] for d in slot_order(codes_ref.shape[0])], 0)
    ids = (coded & 0xFFFF).astype(f32)
    live = (coded[:, 0:LANES] >> 16).astype(f32)
    live_ref[...] = live
    code = iota((CODES, cols), 0).astype(f32)
    for r in range(rows):
        hot = jnp.broadcast_to(ids[r : r + 1, :], (CODES, cols)) == code
        hot_ref[r * CODES : (r + 1) * CODES, :] = hot.astype(f32).astype(bf16)

    pick = (iota((own, cols), 1) == group * own + iota((own, cols), 0)).astype(f32).astype(bf16)
    mine = dot_nt(pick, ids.astype(bf16))
    lane = iota((own, LANES), 1)
    first_half = lane < CODES
    lane_code = jnp.where(first_half, lane, lane - CODES).astype(f32)
    for k in range(pairs):
        value = jnp.where(first_half, mine[:, 2 * k : 2 * k + 1], mine[:, 2 * k + 1 : 2 * k + 2])
        hot = (value == lane_code).astype(f32)
        alive = jnp.where(first_half, live[2 * k : 2 * k + 1, :], live[2 * k + 1 : 2 * k + 2, :])
        own_ref[k * own : (k + 1) * own, :] = hot.astype(bf16)
        live_own_ref[k * own : (k + 1) * own, :] = (hot * alive).astype(bf16)

    spans = [slice(hp * LANES, (hp + 1) * LANES) for hp in range(heads // 2)]
    queries = [spread_pair(table_ref[0, :, span]) for span in spans]
    keys = [double(table_ref[1, :, span]) for span in spans]
    scores = [dot_nt(query, key) for query, key in zip(queries, keys)]
    high = [score.astype(bf16) for score in scores]
    low = [(score - part.astype(f32)).astype(bf16) for score, part in zip(scores, high)]
    for hp in range(heads // 2):
        for h2 in range(2):
            these = slice(h2 * LANES, (h2 + 1) * LANES)
            looked = dot_nn(
                live_own_ref[...], jnp.concatenate([high[hp][these], low[hp][these]], 1)
            ).astype(bf16)
            base = (hp * 2 + h2) * own
            for piece in range(2):
                for k in range(pairs):
                    to = piece * depth + k * LANES
                    sum_ref[base : base + own, to : to + LANES] = looked[
                        k * own : (k + 1) * own, piece * LANES : (piece + 1) * LANES
                    ]
    tied = dot_nn(sum_ref[:, 0:depth], hot_ref[...]) + dot_nn(
        sum_ref[:, depth : 2 * depth], hot_ref[...]
    )
    count = jnp.sum(live, axis=0, keepdims=True)[:, 0:1]
    probs = softmax_last(tied * (HEAD_DIM ** (-0.5) / jnp.sqrt(count))).astype(bf16)

    spread_ref[...] = dot_nt(probs, hot_ref[...]).astype(bf16)
    values = [spread_pair(table_ref[2, :, span]) for span in spans]
    contexts = []
    for hp in range(heads // 2):
        first = (hp * 2) * own
        weights = jnp.concatenate(
            [
                jnp.concatenate(
                    [
                        spread_ref[first : first + own, k * LANES : (k + 1) * LANES],
                        spread_ref[first + own : first + 2 * own, k * LANES : (k + 1) * LANES],
                    ],
                    1,
                )
                for k in range(pairs)
            ],
            0,
        )
        contexts.append(dot_nn(weights, values[hp]).astype(bf16))
    for hp in range(heads // 2):
        for k in range(pairs):
            for r2 in range(2):
                at = (2 * k + r2) * own
                row_context_ref[at : at + own, spans[hp]] = contexts[hp][
                    k * own : (k + 1) * own, r2 * LANES : (r2 + 1) * LANES
                ]


def attend_rows(tables, codes, rows, cols, own, width):
    heads = width // HEAD_DIM
    parts = len(tables)
    return pl.pallas_call(
        functools.partial(row_kernel, parts),
        out_shape=(
            jax.ShapeDtypeStruct((rows * own, width), bf16),
            jax.ShapeDtypeStruct((rows * own // 2, LANES), bf16),
            jax.ShapeDtypeStruct((rows, LANES), f32),
        ),
        scratch_shapes=[
            pltpu.VMEM((parts,) + tables[0].shape, bf16),
            pltpu.VMEM((3, CODES, width), bf16),
            pltpu.VMEM((rows * CODES, cols), bf16),
            pltpu.VMEM((rows // 2 * own, LANES), bf16),
            pltpu.VMEM((heads * own, 2 * rows * CODES), bf16),
            pltpu.VMEM((heads * own, rows * CODES), bf16),
        ],
        cost_estimate=pl.CostEstimate(flops=3 * 10**9, bytes_accessed=10**6, transcendentals=0),
        compiler_params=pltpu.CompilerParams(vmem_limit_bytes=LARGE_VMEM),
        name="row_attention",
    )(*tables, codes)


def column_kernel(parts, *refs):
    row_out_refs, refs = refs[:parts], refs[parts:]
    (
        live_ref,
        row_context_ref,
        own_ref,
        embed_ref,
        col_qkv_ref,
        *out_refs,
        row_out_ref,
        embed2_ref,
    ) = refs
    context_refs, mixed_refs = out_refs[:2], out_refs[2:]
    rows = live_ref.shape[0]
    tokens, width = row_context_ref.shape
    pairs = rows // 2
    own = tokens // rows
    vocab = embed_ref.shape[0]
    local = width // parts
    part = lax.axis_index("head")

    for p in range(parts):
        row_out_ref[part ^ p] = row_out_refs[p][...]
    embed2_ref[...] = jnp.zeros(embed2_ref.shape, bf16)
    embed2_ref[0:vocab, 0:width] = embed_ref[...]
    embed2_ref[CODES : CODES + vocab, width : 2 * width] = embed_ref[...]

    embedded2 = dot_nn(own_ref[...], embed2_ref[...])
    embedded = jnp.concatenate(
        [
            embedded2[k * own : (k + 1) * own, r2 * width : (r2 + 1) * width]
            for k in range(pairs)
            for r2 in range(2)
        ],
        0,
    )
    mixed = embedded + dot_nt(row_context_ref[...], row_out_ref[...].reshape(width, width))
    for p in range(parts):

        @pl.when(part == p)
        def _():
            for c in range(2):
                mixed_refs[c][...] = mixed[
                    c * tokens // 2 : (c + 1) * tokens // 2, p * local : (p + 1) * local
                ]

    normed = layer_norm(mixed).astype(bf16)

    few = 8
    groups = own // few
    unit = rows * few

    def regroup(values):
        shape = (rows, groups, few, values.shape[1])
        return jnp.swapaxes(values.reshape(shape), 0, 1).reshape(tokens, values.shape[1])

    proj = [
        dot_nt(normed, col_qkv_ref[t * local : (t + 1) * local, :]) for t in range(3)
    ]
    proj[0] = proj[0] * HEAD_DIM ** (-0.5)
    proj = [regroup(values).astype(bf16) for values in proj]
    sub, lan = iota((unit, unit), 0), iota((unit, unit), 1)
    same_column = (sub % few) == (lan % few)
    seq_of_lane = iota((rows, unit), 1) // few
    live_lane = jnp.sum(
        jnp.where(seq_of_lane == iota((rows, unit), 0), live_ref[...], 0.0), axis=0, keepdims=True
    )
    visible = jnp.logical_and(same_column, jnp.broadcast_to(live_lane, (unit, unit)) > 0)
    chosen = []
    for g in range(groups):
        at = slice(g * unit, (g + 1) * unit)
        for h in range(local // HEAD_DIM):
            first = h * HEAD_DIM // LANES * LANES
            span = slice(first, min(first + LANES, local))
            query, keys, values = (proj[t][at, span] for t in range(3))
            if query.shape[1] > HEAD_DIM:
                inside = iota(query.shape, 1) // HEAD_DIM == h % 2
                query = jnp.where(inside, query, jnp.zeros_like(query))
            chosen.append((query, keys, values))
    scores = [jnp.where(visible, dot_nt(query, keys), -jnp.inf) for query, keys, _ in chosen]
    tops = [jnp.max(score, axis=-1, keepdims=True) for score in scores]
    weights = [jnp.exp(score - top) for score, top in zip(scores, tops)]
    shares = [1.0 / jnp.sum(weight, axis=-1, keepdims=True) for weight in weights]
    probs = [(weight * share).astype(bf16) for weight, share in zip(weights, shares)]
    found = [dot_nn(prob, values) for prob, (_, _, values) in zip(probs, chosen)]
    many = local // HEAD_DIM
    first_head = iota((unit, LANES), 1) < HEAD_DIM
    blocks = [
        jnp.concatenate(
            [jnp.where(first_head, found[g * many], found[g * many + 1]), found[g * many + 2]], 1
        )
        for g in range(groups)
    ]
    whole = jnp.concatenate(blocks, 0).reshape(groups, rows, few, local)
    context = jnp.swapaxes(whole, 0, 1).reshape(tokens, local)
    half, some = tokens // 2, tokens // 4
    for c in range(2):
        part_of = context[c * half : (c + 1) * half]
        context_refs[c][0:half, :] = part_of[:, 0:LANES].astype(bf16)
        context_refs[c][half : half + some, :] = jnp.concatenate(
            [part_of[0:some, LANES:local], part_of[some:half, LANES:local]], 1
        ).astype(bf16)


def attend_columns_here(row_outs, live, row_context, own_codes, embed, col_qkv):
    parts = len(row_outs)
    tokens, width = row_context.shape
    local = width // parts
    return pl.pallas_call(
        functools.partial(column_kernel, parts),
        out_shape=(
            *[jax.ShapeDtypeStruct((tokens // 2 * local // LANES, LANES), bf16)] * 2,
            *[jax.ShapeDtypeStruct((tokens // 2, local), f32)] * 2,
        ),
        scratch_shapes=[
            pltpu.VMEM((parts, local, width), bf16),
            pltpu.VMEM((2 * CODES, 2 * width), bf16),
        ],
        cost_estimate=pl.CostEstimate(flops=2 * 10**9, bytes_accessed=10**6, transcendentals=0),
        compiler_params=pltpu.CompilerParams(vmem_limit_bytes=LARGE_VMEM),
        name="column_attention",
    )(*row_outs, live, row_context, own_codes, embed, col_qkv)


def finish_kernel(parts, *refs):
    context_refs = refs[:parts]
    mixed_ref, col_out_ref, out_ref, weight_ref = refs[parts:]
    tokens, local = mixed_ref.shape
    some = tokens // 2
    pair = lax.axis_index("seq") // 2
    part = lax.axis_index("head")
    for p in range(parts):
        weight_ref[p] = col_out_ref[:, p * local : (p + 1) * local]
    total = mixed_ref[...]
    for p in range(parts):
        context = context_refs[p]
        weight = weight_ref[part ^ p]
        rest = weight[:, LANES:local]
        zero = jnp.zeros_like(rest)
        left = jnp.concatenate([rest, zero], 1)
        right = jnp.concatenate([zero, rest], 1)
        last = context[tokens : tokens + some, :]
        total = (
            total
            + dot_nt(context[0:tokens, :], weight[:, 0:LANES])
            + jnp.concatenate([dot_nt(last, left), dot_nt(last, right)], 0)
        )
    own = tokens // out_ref.shape[0] // 2
    for d in range(out_ref.shape[0]):
        first, second = (total[(2 * d + r) * own : (2 * d + r + 1) * own, :] for r in range(2))
        rest = jnp.concatenate([first[:, LANES:local], second[:, LANES:local]], 1)
        out_ref[pair ^ d] = jnp.concatenate(
            [first[:, 0:LANES], second[:, 0:LANES], rest], 0
        ).astype(bf16)


def finish(contexts, mixed, col_out, count):
    parts = len(contexts)
    tokens, local = mixed.shape
    return pl.pallas_call(
        functools.partial(finish_kernel, parts),
        out_shape=jax.ShapeDtypeStruct((count, tokens // count * local // LANES, LANES), bf16),
        scratch_shapes=[pltpu.VMEM((parts, local, local), bf16)],
        cost_estimate=pl.CostEstimate(flops=10**9, bytes_accessed=10**6, transcendentals=0),
        compiler_params=pltpu.CompilerParams(vmem_limit_bytes=LARGE_VMEM),
        name="finish",
    )(*contexts, mixed, col_out)


def join_kernel(other_ref, own_ref, out_ref):
    out_ref[:, 0] = own_ref[...]
    out_ref[:, 1] = other_ref[...]


def join(other, own):
    return pl.pallas_call(
        join_kernel,
        out_shape=jax.ShapeDtypeStruct((own.shape[0], 2) + own.shape[1:], own.dtype),
        compiler_params=pltpu.CompilerParams(vmem_limit_bytes=SMALL_VMEM),
        name="join",
    )(other, own)


def order_kernel(blocks_ref, out_ref, ordered_ref):
    groups = ordered_ref.shape[0]
    here = lax.axis_index("seq") % 2
    for pair in range(blocks_ref.shape[0]):
        for k in range(2):
            ordered_ref[2 * pair + (here ^ k)] = blocks_ref[pair, k]
    local, cols = out_ref.shape[1:]
    own = cols // groups
    rest = local - LANES
    for part in range(3):
        piece = jnp.concatenate(
            [ordered_ref[g, part * own : (part + 1) * own, :] for g in range(groups)], 0
        )
        turned = piece.astype(f32).T.astype(bf16)
        if part < 2:
            out_ref[part, 0:LANES, :] = turned
        else:
            for r in range(2):
                out_ref[r, LANES:local, :] = turned[r * rest : (r + 1) * rest, :]


def order(blocks, cols, local):
    pairs, _, rows, lanes = blocks.shape
    return pl.pallas_call(
        order_kernel,
        out_shape=jax.ShapeDtypeStruct((2, local, cols), bf16),
        scratch_shapes=[pltpu.VMEM((2 * pairs, rows, lanes), bf16)],
        compiler_params=pltpu.CompilerParams(vmem_limit_bytes=SMALL_VMEM),
        name="order",
    )(blocks)


def fast_body(ids, pad_mask, embed, row_qkv, row_out, col_qkv, col_out):
    rows_here, cols = ids.shape
    width = embed.shape[1]
    local = row_out.shape[0]
    groups, parts = lax.axis_size("seq"), lax.axis_size("head")
    own, rows = cols // groups, rows_here * groups

    def pairwise(value, partner):
        order = [(g, p) for g in range(groups) for p in range(parts)]
        link = [(g * parts + p, partner(g, p)) for g, p in order]
        return lax.ppermute(value, ("seq", "head"), [(i, g * parts + p) for i, (g, p) in link])

    def sibling(g, p):
        return g, p ^ 1

    def across(g, p):
        return g, p ^ 2

    def opposite(g, p):
        return g, p ^ 3

    far = pairwise(row_out, across)
    codes = make_codes(ids, pad_mask, groups)
    codes, row_qkv = lax.optimization_barrier((codes, row_qkv))
    table = make_tables(embed, row_qkv)
    tables = [table] + [pairwise(table, to) for to in (sibling, across, opposite)]
    codes = lax.all_to_all(codes, "seq", split_axis=0, concat_axis=0, tiled=True)
    codes, near, far = lax.optimization_barrier((codes, row_out, far))
    row_outs = [row_out, pairwise(near, sibling), far, pairwise(far, sibling)]
    row_context, own_codes, live = attend_rows(tables, codes, rows, cols, own, width)
    *halves_here, mixed_low, mixed_high = attend_columns_here(
        row_outs, live, row_context, own_codes, embed, col_qkv.reshape(3 * local, width)
    )
    results = []
    for context, mixed in zip(halves_here, (mixed_low, mixed_high)):
        beyond = pairwise(context, across)
        whole = (context, pairwise(context, sibling), beyond, pairwise(beyond, sibling))
        results.append(finish(whole, mixed, col_out, groups // 2))
    own_result, other_result = results
    other_result = pairwise(other_result, lambda g, p: (g ^ 1, p))
    blocks = lax.all_to_all(
        join(other_result, own_result),
        "seq",
        split_axis=0,
        concat_axis=0,
        tiled=True,
        axis_index_groups=[list(range(k, groups, 2)) for k in range(2)],
    )
    return jnp.swapaxes(order(blocks, cols, local), 1, 2)


def weight_fold(out_weight, piece):
    return jnp.einsum("rce,fe->rcf", piece, out_weight, preferred_element_type=f32)


def attend_columns(query, keys, values, key_live):
    rows_all, count_cols, local_width = query.shape
    heads_here = local_width // HEAD_DIM
    shape = (rows_all, count_cols, heads_here, HEAD_DIM)
    scores = jnp.einsum(
        "rchd,schd->chrs",
        query.reshape(shape),
        keys.reshape(shape),
        preferred_element_type=f32,
    ) * HEAD_DIM ** (-0.5)
    scores = jnp.where(key_live > 0, scores, -jnp.inf)
    probs = softmax_last(scores).astype(bf16)
    context = jnp.einsum(
        "chrs,schd->rchd", probs, values.reshape(shape), preferred_element_type=f32
    )
    return context.astype(bf16).reshape(rows_all, count_cols, local_width)


def send_back(context):
    return lax.all_to_all(context[:, None], "seq", split_axis=0, concat_axis=1, tiled=True)


def general_body(ids, pad_mask, embed, row_qkv, row_out, col_qkv, col_out):
    rows_here, cols = ids.shape
    width = embed.shape[1]
    local_width = row_out.shape[0]
    heads_here = local_width // HEAD_DIM
    groups = lax.axis_size("seq")
    per_group = cols // groups
    codes = lax.broadcasted_iota(jnp.int32, (1, 1, embed.shape[0]), 2)
    onehot = (ids[:, :, None] == codes).astype(bf16)
    embedded = jnp.einsum("rcv,vd->rcd", onehot, embed, preferred_element_type=f32)
    normed = layer_norm(embedded).astype(bf16)
    row_proj = jnp.einsum("rcd,ted->trce", normed, row_qkv, preferred_element_type=f32)
    row_proj = row_proj.astype(bf16)
    live = pad_mask.astype(bf16)
    head_shape = (rows_here, cols, heads_here, HEAD_DIM)
    query = (row_proj[0] * live[:, None, None]).reshape(head_shape)
    keys = row_proj[1].reshape(head_shape)
    values = row_proj[2].reshape(head_shape)
    partial_scores = jnp.einsum("rihd,rjhd->hij", query, keys, preferred_element_type=f32)
    count_here = jnp.sum(pad_mask.astype(f32))
    scale = HEAD_DIM ** (-0.5)
    total, count = lax.psum((partial_scores, count_here), "seq")
    row_probs = softmax_last(total * (scale / jnp.sqrt(count))).astype(bf16)
    row_context = jnp.einsum("hij,rjhd->rihd", row_probs, values, preferred_element_type=f32)
    row_context = row_context.astype(bf16).reshape(rows_here, cols, local_width)
    start_feature = lax.axis_index("head") * local_width
    resident = lax.dynamic_slice_in_dim(embedded, start_feature, local_width, 2)
    row_update = weight_fold(row_out, lax.all_gather(row_context, "head", axis=2, tiled=True))
    mixed = resident + row_update
    sums, squares = lax.psum((jnp.sum(mixed, axis=-1), jnp.sum(mixed * mixed, axis=-1)), "head")
    mean = sums / width
    spread = squares / width - mean * mean
    normed_here = ((mixed - mean[..., None]) * lax.rsqrt(spread[..., None] + EPS)).astype(bf16)
    live_tile = jnp.broadcast_to(live[:, None, None, None], (rows_here, groups, per_group, 1))
    normed_full = lax.all_gather(normed_here, "head", axis=2, tiled=True)
    col_proj = jnp.einsum("rcd,ted->rcte", normed_full, col_qkv, preferred_element_type=f32)
    packed = col_proj.astype(bf16).reshape(rows_here, groups, per_group, 3 * local_width)
    received = lax.all_to_all(packed, "seq", split_axis=1, concat_axis=0, tiled=True)
    mask_part = lax.all_to_all(live_tile, "seq", split_axis=1, concat_axis=0, tiled=True)
    column_out = send_back(
        attend_columns(
            received[:, 0, :, :local_width],
            received[:, 0, :, local_width : 2 * local_width],
            received[:, 0, :, 2 * local_width :],
            mask_part[:, 0, 0, 0],
        )
    )
    column_out = column_out.reshape(rows_here, cols, local_width)
    col_update = weight_fold(col_out, lax.all_gather(column_out, "head", axis=2, tiled=True))
    return (mixed + col_update).astype(bf16)


def body(ids, pad_mask, embed, row_qkv, row_out, col_qkv, col_out):
    rows_here, cols = ids.shape
    groups = lax.axis_size("seq")
    own, rows = cols // groups, rows_here * groups
    parts = lax.axis_size("head")
    local = row_out.shape[0]
    fits = (
        parts == 4
        and groups >= 2
        and groups & (groups - 1) == 0
        and rows * 8 == LANES
        and rows_here == 2
        and own % 32 == 0
        and cols >= LANES
        and local == LANES + HEAD_DIM
        and embed.shape[0] <= TABLE_ROWS
    )
    chosen = fast_body if fits else general_body
    return chosen(ids, pad_mask, embed, row_qkv, row_out, col_qkv, col_out)


def solution(mesh):
    placed = (
        P("seq", None),
        P("seq"),
        P(),
        P(None, "head", None),
        P("head", None),
        P(None, "head", None),
        P("head", None),
    )
    return jax.shard_map(
        body, mesh=mesh, in_specs=placed, out_specs=P("seq", None, "head"), check_vma=False
    )
```

```python
import functools

import jax
import jax.numpy as jnp
from jax import lax
from jax.experimental import pallas as pl
from jax.experimental.pallas import tpu as pltpu
from jax.sharding import PartitionSpec as P

HEAD_DIM = 64
EPS = 1e-05
LANES = 128
CODES = 64
TABLE_ROWS = 40

SMALL_VMEM = 8 * 1024 * 1024
LARGE_VMEM = 32 * 1024 * 1024

f32 = jnp.float32
bf16 = jnp.bfloat16


def layer_norm(values):
    mean = jnp.mean(values, axis=-1, keepdims=True)
    centred = values - mean
    spread = jnp.mean(centred * centred, axis=-1, keepdims=True)
    return centred * lax.rsqrt(spread + EPS)


def softmax_last(scores):
    top = jnp.max(scores, axis=-1, keepdims=True)
    weights = jnp.exp(scores - top)
    return weights * (1.0 / jnp.sum(weights, axis=-1, keepdims=True))


def dot_nt(left, right):
    return lax.dot_general(left, right, (((1,), (1,)), ((), ())), preferred_element_type=f32)


def dot_nn(left, right):
    return jnp.dot(left, right, preferred_element_type=f32)


def in_hbm(value):
    return pltpu.with_memory_space_constraint(value, pltpu.HBM)


def iota(shape, axis):
    return lax.broadcasted_iota(jnp.int32, shape, axis)


def code_kernel(ids_hbm, live_hbm, out_ref, ids_ref, live_ref, sems):
    loads = [
        pltpu.make_async_copy(ids_hbm, ids_ref, sems.at[0]),
        pltpu.make_async_copy(live_hbm, live_ref, sems.at[1]),
    ]
    for load in loads:
        load.start()
    for load in loads:
        load.wait()
    row = iota(ids_ref.shape, 0)
    live = jnp.zeros(ids_ref.shape, jnp.int32)
    for r in range(ids_ref.shape[0]):
        live = jnp.where(row == r, live_ref[r], live)
    coded = ids_ref[...] + 65536 * live
    out_ref[...] = jnp.concatenate([coded] * (out_ref.shape[0] // coded.shape[0]), 0)


def make_codes(ids, pad_mask, height):
    return pl.pallas_call(
        code_kernel,
        out_shape=jax.ShapeDtypeStruct((height, ids.shape[1]), jnp.int32),
        in_specs=[pl.BlockSpec(memory_space=pltpu.HBM)] * 2,
        scratch_shapes=[
            pltpu.VMEM(ids.shape, jnp.int32),
            pltpu.SMEM(pad_mask.shape, jnp.int32),
            pltpu.SemaphoreType.DMA((2,)),
        ],
        compiler_params=pltpu.CompilerParams(vmem_limit_bytes=SMALL_VMEM),
        name="codes",
    )(in_hbm(ids), in_hbm(pad_mask))


def join_kernel(rows, own_ref, other_ref, out_ref):
    own, other = own_ref[...], other_ref[...]
    both = jnp.concatenate([own[0:rows], other[0:rows]], 0)
    out_ref[...] = jnp.concatenate([both] * (own.shape[0] // (2 * rows)), 0)


def join(own, other, rows):
    return pl.pallas_call(
        functools.partial(join_kernel, rows),
        out_shape=jax.ShapeDtypeStruct(own.shape, own.dtype),
        compiler_params=pltpu.CompilerParams(vmem_limit_bytes=SMALL_VMEM),
        name="join",
    )(own, other)


def table_kernel(embed_hbm, qkv_hbm, out_ref, embed_ref, qkv_ref, padded_ref, sems):
    kinds = qkv_ref.shape[0]
    loads = [pltpu.make_async_copy(embed_hbm, embed_ref, sems.at[kinds])]
    loads += [
        pltpu.make_async_copy(qkv_hbm.at[t], qkv_ref.at[t], sems.at[t]) for t in range(kinds)
    ]
    for load in loads:
        load.start()
    padded_ref[...] = jnp.zeros(padded_ref.shape, f32)
    loads[0].wait()
    padded_ref[0 : embed_ref.shape[0], :] = embed_ref[...].astype(f32)
    normed = layer_norm(padded_ref[...]).astype(bf16)
    tables = []
    for t in range(kinds):
        loads[1 + t].wait()
        tables.append(dot_nt(normed, qkv_ref[t]))
    out_ref[...] = jnp.concatenate(tables, 1).astype(bf16)


def make_tables(embed, row_qkv):
    kinds, local, width = row_qkv.shape
    return pl.pallas_call(
        table_kernel,
        out_shape=jax.ShapeDtypeStruct((TABLE_ROWS, kinds * local), bf16),
        in_specs=[pl.BlockSpec(memory_space=pltpu.HBM)] * 2,
        scratch_shapes=[
            pltpu.VMEM(embed.shape, bf16),
            pltpu.VMEM(row_qkv.shape, bf16),
            pltpu.VMEM((TABLE_ROWS, width), f32),
            pltpu.SemaphoreType.DMA((kinds + 1,)),
        ],
        cost_estimate=pl.CostEstimate(
            flops=2 * 10**9, bytes_accessed=2 * row_qkv.size, transcendentals=0
        ),
        compiler_params=pltpu.CompilerParams(vmem_limit_bytes=SMALL_VMEM),
        name="tables",
    )(in_hbm(embed), in_hbm(row_qkv))


def halves(pair):
    lane = iota(pair.shape, 1)
    zero = jnp.zeros_like(pair)
    return jnp.where(lane < HEAD_DIM, pair, zero), jnp.where(lane < HEAD_DIM, zero, pair)


def spread_pair(pair):
    first, second = halves(pair)
    zero = jnp.zeros_like(pair)
    return jnp.concatenate(
        [
            jnp.concatenate([first, zero], 1),
            jnp.concatenate([zero, first], 1),
            jnp.concatenate([second, zero], 1),
            jnp.concatenate([zero, second], 1),
        ],
        0,
    )


def double(block):
    zero = jnp.zeros_like(block)
    return jnp.concatenate(
        [jnp.concatenate([block, zero], 1), jnp.concatenate([zero, block], 1)], 0
    )


def row_kernel(parts, *refs):
    tables_refs, refs = refs[:parts], refs[parts:]
    (
        near_codes_ref,
        far_codes_ref,
        row_context_ref,
        own_ref,
        live_ref,
        tables_ref,
        table_ref,
        hot_ref,
        live_own_ref,
        sum_ref,
        spread_ref,
    ) = refs
    depth, cols = hot_ref.shape
    rows = depth // CODES
    pairs = rows // 2
    own = live_own_ref.shape[0] // pairs
    width = row_context_ref.shape[1]
    heads = width // HEAD_DIM
    local = width // parts
    group = lax.axis_index("seq")
    part = lax.axis_index("head")
    for p in range(parts):
        tables_ref[part ^ p] = tables_refs[p][...]

    for t in range(3):
        table_ref[t, 0:TABLE_ROWS, :] = jnp.concatenate(
            [tables_ref[p, :, t * local : (t + 1) * local] for p in range(parts)], 1
        )
        table_ref[t, TABLE_ROWS:CODES, :] = jnp.zeros((CODES - TABLE_ROWS, width), bf16)

    coded = jnp.concatenate([near_codes_ref[...], far_codes_ref[...]], 0)
    ids = (coded & 0xFFFF).astype(f32)
    live = (coded[:, 0:LANES] >> 16).astype(f32)
    live_ref[...] = live
    code = iota((CODES, cols), 0).astype(f32)
    for r in range(rows):
        hot = jnp.broadcast_to(ids[r : r + 1, :], (CODES, cols)) == code
        hot_ref[r * CODES : (r + 1) * CODES, :] = hot.astype(f32).astype(bf16)

    pick = (iota((own, cols), 1) == group * own + iota((own, cols), 0)).astype(f32).astype(bf16)
    mine = dot_nt(pick, ids.astype(bf16))
    lane = iota((own, LANES), 1)
    first_half = lane < CODES
    lane_code = jnp.where(first_half, lane, lane - CODES).astype(f32)
    for k in range(pairs):
        value = jnp.where(first_half, mine[:, 2 * k : 2 * k + 1], mine[:, 2 * k + 1 : 2 * k + 2])
        hot = (value == lane_code).astype(f32)
        alive = jnp.where(first_half, live[2 * k : 2 * k + 1, :], live[2 * k + 1 : 2 * k + 2, :])
        own_ref[k * own : (k + 1) * own, :] = hot.astype(bf16)
        live_own_ref[k * own : (k + 1) * own, :] = (hot * alive).astype(bf16)

    spans = [slice(hp * LANES, (hp + 1) * LANES) for hp in range(heads // 2)]
    queries = [spread_pair(table_ref[0, :, span]) for span in spans]
    keys = [double(table_ref[1, :, span]) for span in spans]
    scores = [dot_nt(query, key) for query, key in zip(queries, keys)]
    high = [score.astype(bf16) for score in scores]
    low = [(score - part.astype(f32)).astype(bf16) for score, part in zip(scores, high)]
    for hp in range(heads // 2):
        for h2 in range(2):
            these = slice(h2 * LANES, (h2 + 1) * LANES)
            looked = dot_nn(
                live_own_ref[...], jnp.concatenate([high[hp][these], low[hp][these]], 1)
            ).astype(bf16)
            base = (hp * 2 + h2) * own
            for piece in range(2):
                for k in range(pairs):
                    to = piece * depth + k * LANES
                    sum_ref[base : base + own, to : to + LANES] = looked[
                        k * own : (k + 1) * own, piece * LANES : (piece + 1) * LANES
                    ]
    tied = dot_nn(sum_ref[:, 0:depth], hot_ref[...]) + dot_nn(
        sum_ref[:, depth : 2 * depth], hot_ref[...]
    )
    count = jnp.sum(live, axis=0, keepdims=True)[:, 0:1]
    probs = softmax_last(tied * (HEAD_DIM ** (-0.5) / jnp.sqrt(count))).astype(bf16)

    spread_ref[...] = dot_nt(probs, hot_ref[...]).astype(bf16)
    values = [spread_pair(table_ref[2, :, span]) for span in spans]
    contexts = []
    for hp in range(heads // 2):
        first = (hp * 2) * own
        weights = jnp.concatenate(
            [
                jnp.concatenate(
                    [
                        spread_ref[first : first + own, k * LANES : (k + 1) * LANES],
                        spread_ref[first + own : first + 2 * own, k * LANES : (k + 1) * LANES],
                    ],
                    1,
                )
                for k in range(pairs)
            ],
            0,
        )
        contexts.append(dot_nn(weights, values[hp]).astype(bf16))
    for hp in range(heads // 2):
        for k in range(pairs):
            for r2 in range(2):
                at = (2 * k + r2) * own
                row_context_ref[at : at + own, spans[hp]] = contexts[hp][
                    k * own : (k + 1) * own, r2 * LANES : (r2 + 1) * LANES
                ]


def attend_rows(tables, codes, rows, cols, own, width):
    heads = width // HEAD_DIM
    parts = len(tables)
    return pl.pallas_call(
        functools.partial(row_kernel, parts),
        out_shape=(
            jax.ShapeDtypeStruct((rows * own, width), bf16),
            jax.ShapeDtypeStruct((rows * own // 2, LANES), bf16),
            jax.ShapeDtypeStruct((rows, LANES), f32),
        ),
        scratch_shapes=[
            pltpu.VMEM((parts,) + tables[0].shape, bf16),
            pltpu.VMEM((3, CODES, width), bf16),
            pltpu.VMEM((rows * CODES, cols), bf16),
            pltpu.VMEM((rows // 2 * own, LANES), bf16),
            pltpu.VMEM((heads * own, 2 * rows * CODES), bf16),
            pltpu.VMEM((heads * own, rows * CODES), bf16),
        ],
        cost_estimate=pl.CostEstimate(flops=3 * 10**9, bytes_accessed=10**6, transcendentals=0),
        compiler_params=pltpu.CompilerParams(vmem_limit_bytes=LARGE_VMEM),
        name="row_attention",
    )(*tables, *codes)


def column_kernel(parts, *refs):
    row_out_refs, refs = refs[:parts], refs[parts:]
    (
        live_ref,
        row_context_ref,
        own_ref,
        embed_ref,
        col_qkv_ref,
        *out_refs,
        row_out_ref,
        embed2_ref,
    ) = refs
    context_refs, mixed_refs = out_refs[:2], out_refs[2:]
    rows = live_ref.shape[0]
    tokens, width = row_context_ref.shape
    pairs = rows // 2
    own = tokens // rows
    vocab = embed_ref.shape[0]
    local = width // parts
    part = lax.axis_index("head")

    for p in range(parts):
        row_out_ref[part ^ p] = row_out_refs[p][...]
    embed2_ref[...] = jnp.zeros(embed2_ref.shape, bf16)
    embed2_ref[0:vocab, 0:width] = embed_ref[...]
    embed2_ref[CODES : CODES + vocab, width : 2 * width] = embed_ref[...]

    embedded2 = dot_nn(own_ref[...], embed2_ref[...])
    embedded = jnp.concatenate(
        [
            embedded2[k * own : (k + 1) * own, r2 * width : (r2 + 1) * width]
            for k in range(pairs)
            for r2 in range(2)
        ],
        0,
    )
    mixed = embedded + dot_nt(row_context_ref[...], row_out_ref[...].reshape(width, width))
    for p in range(parts):

        @pl.when(part == p)
        def _():
            for c in range(2):
                mixed_refs[c][...] = mixed[
                    c * tokens // 2 : (c + 1) * tokens // 2, p * local : (p + 1) * local
                ]

    normed = layer_norm(mixed).astype(bf16)

    few = 8
    groups = own // few
    unit = rows * few

    def regroup(values):
        shape = (rows, groups, few, values.shape[1])
        return jnp.swapaxes(values.reshape(shape), 0, 1).reshape(tokens, values.shape[1])

    proj = [
        dot_nt(normed, col_qkv_ref[t * local : (t + 1) * local, :]) for t in range(3)
    ]
    proj[0] = proj[0] * HEAD_DIM ** (-0.5)
    proj = [regroup(values).astype(bf16) for values in proj]
    sub, lan = iota((unit, unit), 0), iota((unit, unit), 1)
    same_column = (sub % few) == (lan % few)
    seq_of_lane = iota((rows, unit), 1) // few
    live_lane = jnp.sum(
        jnp.where(seq_of_lane == iota((rows, unit), 0), live_ref[...], 0.0), axis=0, keepdims=True
    )
    visible = jnp.logical_and(same_column, jnp.broadcast_to(live_lane, (unit, unit)) > 0)
    chosen = []
    for g in range(groups):
        at = slice(g * unit, (g + 1) * unit)
        for h in range(local // HEAD_DIM):
            first = h * HEAD_DIM // LANES * LANES
            span = slice(first, min(first + LANES, local))
            query, keys, values = (proj[t][at, span] for t in range(3))
            if query.shape[1] > HEAD_DIM:
                inside = iota(query.shape, 1) // HEAD_DIM == h % 2
                query = jnp.where(inside, query, jnp.zeros_like(query))
            chosen.append((query, keys, values))
    scores = [jnp.where(visible, dot_nt(query, keys), -jnp.inf) for query, keys, _ in chosen]
    tops = [jnp.max(score, axis=-1, keepdims=True) for score in scores]
    weights = [jnp.exp(score - top) for score, top in zip(scores, tops)]
    shares = [1.0 / jnp.sum(weight, axis=-1, keepdims=True) for weight in weights]
    probs = [(weight * share).astype(bf16) for weight, share in zip(weights, shares)]
    found = [dot_nn(prob, values) for prob, (_, _, values) in zip(probs, chosen)]
    many = local // HEAD_DIM
    first_head = iota((unit, LANES), 1) < HEAD_DIM
    blocks = [
        jnp.concatenate(
            [jnp.where(first_head, found[g * many], found[g * many + 1]), found[g * many + 2]], 1
        )
        for g in range(groups)
    ]
    whole = jnp.concatenate(blocks, 0).reshape(groups, rows, few, local)
    context = jnp.swapaxes(whole, 0, 1).reshape(tokens, local)
    half, some = tokens // 2, tokens // 4
    for c in range(2):
        part_of = context[c * half : (c + 1) * half]
        context_refs[c][0:half, :] = part_of[:, 0:LANES].astype(bf16)
        context_refs[c][half : half + some, :] = jnp.concatenate(
            [part_of[0:some, LANES:local], part_of[some:half, LANES:local]], 1
        ).astype(bf16)


def attend_columns_here(row_outs, live, row_context, own_codes, embed, col_qkv):
    parts = len(row_outs)
    tokens, width = row_context.shape
    local = width // parts
    return pl.pallas_call(
        functools.partial(column_kernel, parts),
        out_shape=(
            *[jax.ShapeDtypeStruct((tokens // 2 * local // LANES, LANES), bf16)] * 2,
            *[jax.ShapeDtypeStruct((tokens // 2, local), f32)] * 2,
        ),
        scratch_shapes=[
            pltpu.VMEM((parts, local, width), bf16),
            pltpu.VMEM((2 * CODES, 2 * width), bf16),
        ],
        cost_estimate=pl.CostEstimate(flops=2 * 10**9, bytes_accessed=10**6, transcendentals=0),
        compiler_params=pltpu.CompilerParams(vmem_limit_bytes=LARGE_VMEM),
        name="column_attention",
    )(*row_outs, live, row_context, own_codes, embed, col_qkv)


def finish_kernel(parts, groups, *refs):
    context_refs = [refs[:parts], refs[parts : 2 * parts]]
    mixed_refs = refs[2 * parts : 2 * parts + 2]
    col_out_ref, out_ref, weight_ref = refs[2 * parts + 2 :]
    tokens, local = mixed_refs[0].shape
    some = tokens // 2
    group = lax.axis_index("seq")
    part = lax.axis_index("head")
    for p in range(parts):
        weight_ref[p] = col_out_ref[:, p * local : (p + 1) * local]
    totals = [ref[...] for ref in mixed_refs]
    for p in range(parts):
        weight = weight_ref[part ^ p]
        rest = weight[:, LANES:local]
        zero = jnp.zeros_like(rest)
        left = jnp.concatenate([rest, zero], 1)
        right = jnp.concatenate([zero, rest], 1)
        for c in range(2):
            context = context_refs[c][p]
            last = context[tokens : tokens + some, :]
            totals[c] = (
                totals[c]
                + dot_nt(context[0:tokens, :], weight[:, 0:LANES])
                + jnp.concatenate([dot_nt(last, left), dot_nt(last, right)], 0)
            )
    slots = groups // 2
    own = tokens // slots // 2
    for d in range(groups):
        first, second = (
            totals[d // slots][(2 * (d % slots) + r) * own : (2 * (d % slots) + r + 1) * own, :]
            for r in range(2)
        )
        rest = jnp.concatenate([first[:, LANES:local], second[:, LANES:local]], 1)
        out_ref[group ^ d] = jnp.concatenate(
            [first[:, 0:LANES], second[:, 0:LANES], rest], 0
        ).astype(bf16)


def finish(contexts, mixed, col_out, groups):
    parts = len(contexts[0])
    tokens, local = mixed[0].shape
    return pl.pallas_call(
        functools.partial(finish_kernel, parts, groups),
        out_shape=jax.ShapeDtypeStruct(
            (groups, 2 * tokens // groups * local // LANES, LANES), bf16
        ),
        scratch_shapes=[pltpu.VMEM((parts, local, local), bf16)],
        compiler_params=pltpu.CompilerParams(vmem_limit_bytes=LARGE_VMEM),
        name="finish",
    )(*contexts[0], *contexts[1], *mixed, col_out)


def order_kernel(blocks_ref, out_ref):
    groups = blocks_ref.shape[0]
    local, cols = out_ref.shape[1:]
    own = cols // groups
    rest = local - LANES
    for part in range(3):
        piece = jnp.concatenate(
            [blocks_ref[g, part * own : (part + 1) * own, :] for g in range(groups)], 0
        )
        turned = piece.astype(f32).T.astype(bf16)
        if part < 2:
            out_ref[part, 0:LANES, :] = turned
        else:
            for r in range(2):
                out_ref[r, LANES:local, :] = turned[r * rest : (r + 1) * rest, :]


def order(blocks, cols, local):
    return pl.pallas_call(
        order_kernel,
        out_shape=jax.ShapeDtypeStruct((2, local, cols), bf16),
        compiler_params=pltpu.CompilerParams(vmem_limit_bytes=SMALL_VMEM),
        name="order",
    )(blocks)


def fast_body(ids, pad_mask, embed, row_qkv, row_out, col_qkv, col_out):
    rows_here, cols = ids.shape
    width = embed.shape[1]
    local = row_out.shape[0]
    groups, parts = lax.axis_size("seq"), lax.axis_size("head")
    own, rows = cols // groups, rows_here * groups

    def pairwise(value, partner):
        order = [(g, p) for g in range(groups) for p in range(parts)]
        link = [(g * parts + p, partner(g, p)) for g, p in order]
        return lax.ppermute(value, ("seq", "head"), [(i, g * parts + p) for i, (g, p) in link])

    def sibling(g, p):
        return g, p ^ 1

    def across(g, p):
        return g, p ^ 2

    def opposite(g, p):
        return g, p ^ 3

    far = pairwise(row_out, across)
    coded = make_codes(ids, pad_mask, rows_here * groups // 2)
    coded, row_qkv = lax.optimization_barrier((coded, row_qkv))
    received = pairwise(coded, lambda g, p: (g ^ 1, p))
    table = make_tables(embed, row_qkv)
    step = 2
    while step < groups:
        coded = join(coded, received, rows_here * step // 2)
        if step == 2:
            coded, table = lax.optimization_barrier((coded, table))
            far_tables = [pairwise(table, to) for to in (across, opposite)]
        received = pairwise(coded, lambda g, p, step=step: (g ^ step, p))
        step *= 2
    codes = (coded, received)
    coded, late_table = lax.optimization_barrier((coded, table))
    codes = (coded, received)
    tables = [table, pairwise(late_table, sibling)] + far_tables
    *codes, near, far = lax.optimization_barrier((*codes, row_out, far))
    row_outs = [row_out, pairwise(near, sibling), far, pairwise(far, sibling)]
    row_context, own_codes, live = attend_rows(tables, codes, rows, cols, own, width)
    *halves_here, mixed_low, mixed_high = attend_columns_here(
        row_outs, live, row_context, own_codes, embed, col_qkv.reshape(3 * local, width)
    )
    contexts = []
    for context in halves_here:
        beyond = pairwise(context, across)
        contexts.append(
            (context, pairwise(context, sibling), beyond, pairwise(beyond, sibling))
        )
    blocks = finish(contexts, (mixed_low, mixed_high), col_out, groups)
    blocks = lax.all_to_all(blocks, "seq", split_axis=0, concat_axis=0, tiled=True)
    return jnp.swapaxes(order(blocks, cols, local), 1, 2)


def weight_fold(out_weight, piece):
    return jnp.einsum("rce,fe->rcf", piece, out_weight, preferred_element_type=f32)


def attend_columns(query, keys, values, key_live):
    rows_all, count_cols, local_width = query.shape
    heads_here = local_width // HEAD_DIM
    shape = (rows_all, count_cols, heads_here, HEAD_DIM)
    scores = jnp.einsum(
        "rchd,schd->chrs",
        query.reshape(shape),
        keys.reshape(shape),
        preferred_element_type=f32,
    ) * HEAD_DIM ** (-0.5)
    scores = jnp.where(key_live > 0, scores, -jnp.inf)
    probs = softmax_last(scores).astype(bf16)
    context = jnp.einsum(
        "chrs,schd->rchd", probs, values.reshape(shape), preferred_element_type=f32
    )
    return context.astype(bf16).reshape(rows_all, count_cols, local_width)


def send_back(context):
    return lax.all_to_all(context[:, None], "seq", split_axis=0, concat_axis=1, tiled=True)


def general_body(ids, pad_mask, embed, row_qkv, row_out, col_qkv, col_out):
    rows_here, cols = ids.shape
    width = embed.shape[1]
    local_width = row_out.shape[0]
    heads_here = local_width // HEAD_DIM
    groups = lax.axis_size("seq")
    per_group = cols // groups
    codes = lax.broadcasted_iota(jnp.int32, (1, 1, embed.shape[0]), 2)
    onehot = (ids[:, :, None] == codes).astype(bf16)
    embedded = jnp.einsum("rcv,vd->rcd", onehot, embed, preferred_element_type=f32)
    normed = layer_norm(embedded).astype(bf16)
    row_proj = jnp.einsum("rcd,ted->trce", normed, row_qkv, preferred_element_type=f32)
    row_proj = row_proj.astype(bf16)
    live = pad_mask.astype(bf16)
    head_shape = (rows_here, cols, heads_here, HEAD_DIM)
    query = (row_proj[0] * live[:, None, None]).reshape(head_shape)
    keys = row_proj[1].reshape(head_shape)
    values = row_proj[2].reshape(head_shape)
    partial_scores = jnp.einsum("rihd,rjhd->hij", query, keys, preferred_element_type=f32)
    count_here = jnp.sum(pad_mask.astype(f32))
    scale = HEAD_DIM ** (-0.5)
    total, count = lax.psum((partial_scores, count_here), "seq")
    row_probs = softmax_last(total * (scale / jnp.sqrt(count))).astype(bf16)
    row_context = jnp.einsum("hij,rjhd->rihd", row_probs, values, preferred_element_type=f32)
    row_context = row_context.astype(bf16).reshape(rows_here, cols, local_width)
    start_feature = lax.axis_index("head") * local_width
    resident = lax.dynamic_slice_in_dim(embedded, start_feature, local_width, 2)
    row_update = weight_fold(row_out, lax.all_gather(row_context, "head", axis=2, tiled=True))
    mixed = resident + row_update
    sums, squares = lax.psum((jnp.sum(mixed, axis=-1), jnp.sum(mixed * mixed, axis=-1)), "head")
    mean = sums / width
    spread = squares / width - mean * mean
    normed_here = ((mixed - mean[..., None]) * lax.rsqrt(spread[..., None] + EPS)).astype(bf16)
    live_tile = jnp.broadcast_to(live[:, None, None, None], (rows_here, groups, per_group, 1))
    normed_full = lax.all_gather(normed_here, "head", axis=2, tiled=True)
    col_proj = jnp.einsum("rcd,ted->rcte", normed_full, col_qkv, preferred_element_type=f32)
    packed = col_proj.astype(bf16).reshape(rows_here, groups, per_group, 3 * local_width)
    received = lax.all_to_all(packed, "seq", split_axis=1, concat_axis=0, tiled=True)
    mask_part = lax.all_to_all(live_tile, "seq", split_axis=1, concat_axis=0, tiled=True)
    column_out = send_back(
        attend_columns(
            received[:, 0, :, :local_width],
            received[:, 0, :, local_width : 2 * local_width],
            received[:, 0, :, 2 * local_width :],
            mask_part[:, 0, 0, 0],
        )
    )
    column_out = column_out.reshape(rows_here, cols, local_width)
    col_update = weight_fold(col_out, lax.all_gather(column_out, "head", axis=2, tiled=True))
    return (mixed + col_update).astype(bf16)


def body(ids, pad_mask, embed, row_qkv, row_out, col_qkv, col_out):
    rows_here, cols = ids.shape
    groups = lax.axis_size("seq")
    own, rows = cols // groups, rows_here * groups
    parts = lax.axis_size("head")
    local = row_out.shape[0]
    fits = (
        parts == 4
        and groups >= 4
        and groups & (groups - 1) == 0
        and rows * 8 == LANES
        and rows_here == 2
        and own % 32 == 0
        and cols >= LANES
        and local == LANES + HEAD_DIM
        and embed.shape[0] <= TABLE_ROWS
    )
    chosen = fast_body if fits else general_body
    return chosen(ids, pad_mask, embed, row_qkv, row_out, col_qkv, col_out)


def solution(mesh):
    placed = (
        P("seq", None),
        P("seq"),
        P(),
        P(None, "head", None),
        P("head", None),
        P(None, "head", None),
        P("head", None),
    )
    return jax.shard_map(
        body, mesh=mesh, in_specs=placed, out_specs=P("seq", None, "head"), check_vma=False
    )
```

```python
import functools

import jax
import jax.numpy as jnp
from jax import lax
from jax.experimental import pallas as pl
from jax.experimental.pallas import tpu as pltpu
from jax.sharding import PartitionSpec as P

HEAD_DIM = 64
EPS = 1e-05
LANES = 128
CODES = 64
TABLE_ROWS = 40

SMALL_VMEM = 8 * 1024 * 1024
LARGE_VMEM = 32 * 1024 * 1024

f32 = jnp.float32
bf16 = jnp.bfloat16


def layer_norm(values):
    mean = jnp.mean(values, axis=-1, keepdims=True)
    centred = values - mean
    spread = jnp.mean(centred * centred, axis=-1, keepdims=True)
    return centred * lax.rsqrt(spread + EPS)


def softmax_last(scores):
    top = jnp.max(scores, axis=-1, keepdims=True)
    weights = jnp.exp(scores - top)
    return weights * (1.0 / jnp.sum(weights, axis=-1, keepdims=True))


def dot_nt(left, right):
    return lax.dot_general(left, right, (((1,), (1,)), ((), ())), preferred_element_type=f32)


def dot_nn(left, right):
    return jnp.dot(left, right, preferred_element_type=f32)


def in_hbm(value):
    return pltpu.with_memory_space_constraint(value, pltpu.HBM)


def iota(shape, axis):
    return lax.broadcasted_iota(jnp.int32, shape, axis)


def code_kernel(ids_hbm, live_hbm, out_ref, ids_ref, live_ref, sems):
    loads = [
        pltpu.make_async_copy(ids_hbm, ids_ref, sems.at[0]),
        pltpu.make_async_copy(live_hbm, live_ref, sems.at[1]),
    ]
    for load in loads:
        load.start()
    for load in loads:
        load.wait()
    row = iota(ids_ref.shape, 0)
    live = jnp.zeros(ids_ref.shape, jnp.int32)
    for r in range(ids_ref.shape[0]):
        live = jnp.where(row == r, live_ref[r], live)
    coded = ids_ref[...] + 65536 * live
    out_ref[...] = jnp.concatenate([coded] * (out_ref.shape[0] // coded.shape[0]), 0)


def make_codes(ids, pad_mask, height):
    return pl.pallas_call(
        code_kernel,
        out_shape=jax.ShapeDtypeStruct((height, ids.shape[1]), jnp.int32),
        in_specs=[pl.BlockSpec(memory_space=pltpu.HBM)] * 2,
        scratch_shapes=[
            pltpu.VMEM(ids.shape, jnp.int32),
            pltpu.SMEM(pad_mask.shape, jnp.int32),
            pltpu.SemaphoreType.DMA((2,)),
        ],
        compiler_params=pltpu.CompilerParams(vmem_limit_bytes=SMALL_VMEM),
        name="codes",
    )(in_hbm(ids), in_hbm(pad_mask))


def join_kernel(rows, own_ref, other_ref, out_ref):
    own, other = own_ref[...], other_ref[...]
    both = jnp.concatenate([own[0:rows], other[0:rows]], 0)
    out_ref[...] = jnp.concatenate([both] * (own.shape[0] // (2 * rows)), 0)


def join(own, other, rows):
    return pl.pallas_call(
        functools.partial(join_kernel, rows),
        out_shape=jax.ShapeDtypeStruct(own.shape, own.dtype),
        compiler_params=pltpu.CompilerParams(vmem_limit_bytes=SMALL_VMEM),
        name="join",
    )(own, other)


def table_kernel(embed_hbm, qkv_hbm, out_ref, embed_ref, qkv_ref, padded_ref, sems):
    kinds, local = qkv_ref.shape[0:2]
    cut = local // 2
    loads = [pltpu.make_async_copy(embed_hbm, embed_ref, sems.at[2 * kinds])]
    loads += [
        pltpu.make_async_copy(
            qkv_hbm.at[t, half * cut : (half + 1) * cut],
            qkv_ref.at[t, half * cut : (half + 1) * cut],
            sems.at[2 * t + half],
        )
        for t in range(kinds)
        for half in range(2)
    ]
    for load in loads:
        load.start()
    padded_ref[...] = jnp.zeros(padded_ref.shape, f32)
    loads[0].wait()
    padded_ref[0 : embed_ref.shape[0], :] = embed_ref[...].astype(f32)
    normed = layer_norm(padded_ref[...]).astype(bf16)
    tables = []
    for t in range(kinds):
        loads[1 + 2 * t].wait()
        loads[2 + 2 * t].wait()
        tables.append(dot_nt(normed, qkv_ref[t]))
    out_ref[...] = jnp.concatenate(tables, 1).astype(bf16)


def make_tables(embed, row_qkv):
    kinds, local, width = row_qkv.shape
    return pl.pallas_call(
        table_kernel,
        out_shape=jax.ShapeDtypeStruct((TABLE_ROWS, kinds * local), bf16),
        in_specs=[pl.BlockSpec(memory_space=pltpu.HBM)] * 2,
        scratch_shapes=[
            pltpu.VMEM(embed.shape, bf16),
            pltpu.VMEM(row_qkv.shape, bf16),
            pltpu.VMEM((TABLE_ROWS, width), f32),
            pltpu.SemaphoreType.DMA((2 * kinds + 1,)),
        ],
        cost_estimate=pl.CostEstimate(
            flops=2 * 10**9, bytes_accessed=2 * row_qkv.size, transcendentals=0
        ),
        compiler_params=pltpu.CompilerParams(vmem_limit_bytes=SMALL_VMEM),
        name="tables",
    )(in_hbm(embed), in_hbm(row_qkv))


def halves(pair):
    lane = iota(pair.shape, 1)
    zero = jnp.zeros_like(pair)
    return jnp.where(lane < HEAD_DIM, pair, zero), jnp.where(lane < HEAD_DIM, zero, pair)


def spread_pair(pair):
    first, second = halves(pair)
    zero = jnp.zeros_like(pair)
    return jnp.concatenate(
        [
            jnp.concatenate([first, zero], 1),
            jnp.concatenate([zero, first], 1),
            jnp.concatenate([second, zero], 1),
            jnp.concatenate([zero, second], 1),
        ],
        0,
    )


def double(block):
    zero = jnp.zeros_like(block)
    return jnp.concatenate(
        [jnp.concatenate([block, zero], 1), jnp.concatenate([zero, block], 1)], 0
    )


def row_kernel(parts, *refs):
    tables_refs, refs = refs[:parts], refs[parts:]
    (
        near_codes_ref,
        far_codes_ref,
        row_context_ref,
        own_ref,
        live_ref,
        tables_ref,
        table_ref,
        hot_ref,
        live_own_ref,
        sum_ref,
        spread_ref,
    ) = refs
    depth, cols = hot_ref.shape
    rows = depth // CODES
    pairs = rows // 2
    own = live_own_ref.shape[0] // pairs
    width = row_context_ref.shape[1]
    heads = width // HEAD_DIM
    local = width // parts
    group = lax.axis_index("seq")
    part = lax.axis_index("head")
    for p in range(parts):
        tables_ref[part ^ p] = tables_refs[p][...]

    for t in range(3):
        table_ref[t, 0:TABLE_ROWS, :] = jnp.concatenate(
            [tables_ref[p, :, t * local : (t + 1) * local] for p in range(parts)], 1
        )
        table_ref[t, TABLE_ROWS:CODES, :] = jnp.zeros((CODES - TABLE_ROWS, width), bf16)

    coded = jnp.concatenate([near_codes_ref[...], far_codes_ref[...]], 0)
    ids = (coded & 0xFFFF).astype(f32)
    live = (coded[:, 0:LANES] >> 16).astype(f32)
    live_ref[...] = live
    code = iota((CODES, cols), 0).astype(f32)
    for r in range(rows):
        hot = jnp.broadcast_to(ids[r : r + 1, :], (CODES, cols)) == code
        hot_ref[r * CODES : (r + 1) * CODES, :] = hot.astype(f32).astype(bf16)

    pick = (iota((own, cols), 1) == group * own + iota((own, cols), 0)).astype(f32).astype(bf16)
    mine = dot_nt(pick, ids.astype(bf16))
    lane = iota((own, LANES), 1)
    first_half = lane < CODES
    lane_code = jnp.where(first_half, lane, lane - CODES).astype(f32)
    for k in range(pairs):
        value = jnp.where(first_half, mine[:, 2 * k : 2 * k + 1], mine[:, 2 * k + 1 : 2 * k + 2])
        hot = (value == lane_code).astype(f32)
        alive = jnp.where(first_half, live[2 * k : 2 * k + 1, :], live[2 * k + 1 : 2 * k + 2, :])
        own_ref[k * own : (k + 1) * own, :] = hot.astype(bf16)
        live_own_ref[k * own : (k + 1) * own, :] = (hot * alive).astype(bf16)

    spans = [slice(hp * LANES, (hp + 1) * LANES) for hp in range(heads // 2)]
    queries = [spread_pair(table_ref[0, :, span]) for span in spans]
    keys = [double(table_ref[1, :, span]) for span in spans]
    scores = [dot_nt(query, key) for query, key in zip(queries, keys)]
    high = [score.astype(bf16) for score in scores]
    low = [(score - part.astype(f32)).astype(bf16) for score, part in zip(scores, high)]
    for hp in range(heads // 2):
        for h2 in range(2):
            these = slice(h2 * LANES, (h2 + 1) * LANES)
            looked = dot_nn(
                live_own_ref[...], jnp.concatenate([high[hp][these], low[hp][these]], 1)
            ).astype(bf16)
            base = (hp * 2 + h2) * own
            for piece in range(2):
                for k in range(pairs):
                    to = piece * depth + k * LANES
                    sum_ref[base : base + own, to : to + LANES] = looked[
                        k * own : (k + 1) * own, piece * LANES : (piece + 1) * LANES
                    ]
    tied = dot_nn(sum_ref[:, 0:depth], hot_ref[...]) + dot_nn(
        sum_ref[:, depth : 2 * depth], hot_ref[...]
    )
    count = jnp.sum(live, axis=0, keepdims=True)[:, 0:1]
    probs = softmax_last(tied * (HEAD_DIM ** (-0.5) / jnp.sqrt(count))).astype(bf16)

    spread_ref[...] = dot_nt(probs, hot_ref[...]).astype(bf16)
    values = [spread_pair(table_ref[2, :, span]) for span in spans]
    contexts = []
    for hp in range(heads // 2):
        first = (hp * 2) * own
        weights = jnp.concatenate(
            [
                jnp.concatenate(
                    [
                        spread_ref[first : first + own, k * LANES : (k + 1) * LANES],
                        spread_ref[first + own : first + 2 * own, k * LANES : (k + 1) * LANES],
                    ],
                    1,
                )
                for k in range(pairs)
            ],
            0,
        )
        contexts.append(dot_nn(weights, values[hp]).astype(bf16))
    for hp in range(heads // 2):
        for k in range(pairs):
            for r2 in range(2):
                at = (2 * k + r2) * own
                row_context_ref[at : at + own, spans[hp]] = contexts[hp][
                    k * own : (k + 1) * own, r2 * LANES : (r2 + 1) * LANES
                ]


def attend_rows(tables, codes, rows, cols, own, width):
    heads = width // HEAD_DIM
    parts = len(tables)
    return pl.pallas_call(
        functools.partial(row_kernel, parts),
        out_shape=(
            jax.ShapeDtypeStruct((rows * own, width), bf16),
            jax.ShapeDtypeStruct((rows * own // 2, LANES), bf16),
            jax.ShapeDtypeStruct((rows, LANES), f32),
        ),
        scratch_shapes=[
            pltpu.VMEM((parts,) + tables[0].shape, bf16),
            pltpu.VMEM((3, CODES, width), bf16),
            pltpu.VMEM((rows * CODES, cols), bf16),
            pltpu.VMEM((rows // 2 * own, LANES), bf16),
            pltpu.VMEM((heads * own, 2 * rows * CODES), bf16),
            pltpu.VMEM((heads * own, rows * CODES), bf16),
        ],
        cost_estimate=pl.CostEstimate(flops=3 * 10**9, bytes_accessed=10**6, transcendentals=0),
        compiler_params=pltpu.CompilerParams(vmem_limit_bytes=LARGE_VMEM),
        name="row_attention",
    )(*tables, *codes)


def column_kernel(parts, *refs):
    row_out_refs, refs = refs[:parts], refs[parts:]
    (
        live_ref,
        row_context_ref,
        own_ref,
        embed_ref,
        col_qkv_ref,
        *out_refs,
        row_out_ref,
        embed2_ref,
    ) = refs
    context_refs, mixed_refs = out_refs[:2], out_refs[2:]
    rows = live_ref.shape[0]
    tokens, width = row_context_ref.shape
    pairs = rows // 2
    own = tokens // rows
    vocab = embed_ref.shape[0]
    local = width // parts
    part = lax.axis_index("head")

    for p in range(parts):
        row_out_ref[part ^ p] = row_out_refs[p][...]
    embed2_ref[...] = jnp.zeros(embed2_ref.shape, bf16)
    embed2_ref[0:vocab, 0:width] = embed_ref[...]
    embed2_ref[CODES : CODES + vocab, width : 2 * width] = embed_ref[...]

    embedded2 = dot_nn(own_ref[...], embed2_ref[...])
    embedded = jnp.concatenate(
        [
            embedded2[k * own : (k + 1) * own, r2 * width : (r2 + 1) * width]
            for k in range(pairs)
            for r2 in range(2)
        ],
        0,
    )
    mixed = embedded + dot_nt(row_context_ref[...], row_out_ref[...].reshape(width, width))
    for p in range(parts):

        @pl.when(part == p)
        def _():
            for c in range(2):
                mixed_refs[c][...] = mixed[
                    c * tokens // 2 : (c + 1) * tokens // 2, p * local : (p + 1) * local
                ]

    normed = layer_norm(mixed).astype(bf16)

    few = 8
    groups = own // few
    unit = rows * few

    def regroup(values):
        shape = (rows, groups, few, values.shape[1])
        return jnp.swapaxes(values.reshape(shape), 0, 1).reshape(tokens, values.shape[1])

    proj = [
        dot_nt(normed, col_qkv_ref[t * local : (t + 1) * local, :]) for t in range(3)
    ]
    proj[0] = proj[0] * HEAD_DIM ** (-0.5)
    proj = [regroup(values).astype(bf16) for values in proj]
    sub, lan = iota((unit, unit), 0), iota((unit, unit), 1)
    same_column = (sub % few) == (lan % few)
    seq_of_lane = iota((rows, unit), 1) // few
    live_lane = jnp.sum(
        jnp.where(seq_of_lane == iota((rows, unit), 0), live_ref[...], 0.0), axis=0, keepdims=True
    )
    visible = jnp.logical_and(same_column, jnp.broadcast_to(live_lane, (unit, unit)) > 0)
    chosen = []
    for g in range(groups):
        at = slice(g * unit, (g + 1) * unit)
        for h in range(local // HEAD_DIM):
            first = h * HEAD_DIM // LANES * LANES
            span = slice(first, min(first + LANES, local))
            query, keys, values = (proj[t][at, span] for t in range(3))
            if query.shape[1] > HEAD_DIM:
                inside = iota(query.shape, 1) // HEAD_DIM == h % 2
                query = jnp.where(inside, query, jnp.zeros_like(query))
            chosen.append((query, keys, values))
    scores = [jnp.where(visible, dot_nt(query, keys), -jnp.inf) for query, keys, _ in chosen]
    tops = [jnp.max(score, axis=-1, keepdims=True) for score in scores]
    weights = [jnp.exp(score - top) for score, top in zip(scores, tops)]
    shares = [1.0 / jnp.sum(weight, axis=-1, keepdims=True) for weight in weights]
    probs = [(weight * share).astype(bf16) for weight, share in zip(weights, shares)]
    found = [dot_nn(prob, values) for prob, (_, _, values) in zip(probs, chosen)]
    many = local // HEAD_DIM
    first_head = iota((unit, LANES), 1) < HEAD_DIM
    blocks = [
        jnp.concatenate(
            [jnp.where(first_head, found[g * many], found[g * many + 1]), found[g * many + 2]], 1
        )
        for g in range(groups)
    ]
    whole = jnp.concatenate(blocks, 0).reshape(groups, rows, few, local)
    context = jnp.swapaxes(whole, 0, 1).reshape(tokens, local)
    half, some = tokens // 2, tokens // 4
    for c in range(2):
        part_of = context[c * half : (c + 1) * half]
        context_refs[c][0:half, :] = part_of[:, 0:LANES].astype(bf16)
        context_refs[c][half : half + some, :] = jnp.concatenate(
            [part_of[0:some, LANES:local], part_of[some:half, LANES:local]], 1
        ).astype(bf16)


def attend_columns_here(row_outs, live, row_context, own_codes, embed, col_qkv):
    parts = len(row_outs)
    tokens, width = row_context.shape
    local = width // parts
    return pl.pallas_call(
        functools.partial(column_kernel, parts),
        out_shape=(
            *[jax.ShapeDtypeStruct((tokens // 2 * local // LANES, LANES), bf16)] * 2,
            *[jax.ShapeDtypeStruct((tokens // 2, local), f32)] * 2,
        ),
        scratch_shapes=[
            pltpu.VMEM((parts, local, width), bf16),
            pltpu.VMEM((2 * CODES, 2 * width), bf16),
        ],
        cost_estimate=pl.CostEstimate(flops=2 * 10**9, bytes_accessed=10**6, transcendentals=0),
        compiler_params=pltpu.CompilerParams(vmem_limit_bytes=LARGE_VMEM),
        name="column_attention",
    )(*row_outs, live, row_context, own_codes, embed, col_qkv)


def finish_kernel(parts, groups, *refs):
    context_refs = [refs[:parts], refs[parts : 2 * parts]]
    mixed_refs = refs[2 * parts : 2 * parts + 2]
    col_out_ref, out_ref, weight_ref = refs[2 * parts + 2 :]
    tokens, local = mixed_refs[0].shape
    some = tokens // 2
    group = lax.axis_index("seq")
    part = lax.axis_index("head")
    for p in range(parts):
        weight_ref[p] = col_out_ref[:, p * local : (p + 1) * local]
    totals = [ref[...] for ref in mixed_refs]
    for p in range(parts):
        weight = weight_ref[part ^ p]
        rest = weight[:, LANES:local]
        zero = jnp.zeros_like(rest)
        left = jnp.concatenate([rest, zero], 1)
        right = jnp.concatenate([zero, rest], 1)
        for c in range(2):
            context = context_refs[c][p]
            last = context[tokens : tokens + some, :]
            totals[c] = (
                totals[c]
                + dot_nt(context[0:tokens, :], weight[:, 0:LANES])
                + jnp.concatenate([dot_nt(last, left), dot_nt(last, right)], 0)
            )
    slots = groups // 2
    own = tokens // slots // 2
    for d in range(groups):
        first, second = (
            totals[d // slots][(2 * (d % slots) + r) * own : (2 * (d % slots) + r + 1) * own, :]
            for r in range(2)
        )
        rest = jnp.concatenate([first[:, LANES:local], second[:, LANES:local]], 1)
        out_ref[group ^ d] = jnp.concatenate(
            [first[:, 0:LANES], second[:, 0:LANES], rest], 0
        ).astype(bf16)


def finish(contexts, mixed, col_out, groups):
    parts = len(contexts[0])
    tokens, local = mixed[0].shape
    return pl.pallas_call(
        functools.partial(finish_kernel, parts, groups),
        out_shape=jax.ShapeDtypeStruct(
            (groups, 2 * tokens // groups * local // LANES, LANES), bf16
        ),
        scratch_shapes=[pltpu.VMEM((parts, local, local), bf16)],
        compiler_params=pltpu.CompilerParams(vmem_limit_bytes=LARGE_VMEM),
        name="finish",
    )(*contexts[0], *contexts[1], *mixed, col_out)


def order_kernel(blocks_ref, out_ref):
    groups = blocks_ref.shape[0]
    local, cols = out_ref.shape[1:]
    own = cols // groups
    rest = local - LANES
    for part in range(3):
        piece = jnp.concatenate(
            [blocks_ref[g, part * own : (part + 1) * own, :] for g in range(groups)], 0
        )
        turned = piece.astype(f32).T.astype(bf16)
        if part < 2:
            out_ref[part, 0:LANES, :] = turned
        else:
            for r in range(2):
                out_ref[r, LANES:local, :] = turned[r * rest : (r + 1) * rest, :]


def order(blocks, cols, local):
    return pl.pallas_call(
        order_kernel,
        out_shape=jax.ShapeDtypeStruct((2, local, cols), bf16),
        compiler_params=pltpu.CompilerParams(vmem_limit_bytes=SMALL_VMEM),
        name="order",
    )(blocks)


def fast_body(ids, pad_mask, embed, row_qkv, row_out, col_qkv, col_out):
    rows_here, cols = ids.shape
    width = embed.shape[1]
    local = row_out.shape[0]
    groups, parts = lax.axis_size("seq"), lax.axis_size("head")
    own, rows = cols // groups, rows_here * groups

    def pairwise(value, partner):
        order = [(g, p) for g in range(groups) for p in range(parts)]
        link = [(g * parts + p, partner(g, p)) for g, p in order]
        return lax.ppermute(value, ("seq", "head"), [(i, g * parts + p) for i, (g, p) in link])

    def sibling(g, p):
        return g, p ^ 1

    def across(g, p):
        return g, p ^ 2

    def opposite(g, p):
        return g, p ^ 3

    coded = make_codes(ids, pad_mask, rows_here * groups // 2)
    coded, row_qkv, row_out = lax.optimization_barrier((coded, row_qkv, row_out))
    received = pairwise(coded, lambda g, p: (g ^ 1, p))
    far = pairwise(row_out, across)
    near = pairwise(row_out, sibling)
    table = make_tables(embed, row_qkv)
    step = 2
    while step < groups:
        coded = join(coded, received, rows_here * step // 2)
        if step == 2:
            coded, table, near = lax.optimization_barrier((coded, table, near))
            far_tables = [pairwise(table, to) for to in (across, opposite)]
        received = pairwise(coded, lambda g, p, step=step: (g ^ step, p))
        step *= 2
    codes = (coded, received)
    coded, late_table = lax.optimization_barrier((coded, table))
    codes = (coded, received)
    tables = [table, pairwise(late_table, sibling)] + far_tables
    *codes, far = lax.optimization_barrier((*codes, far))
    row_outs = [row_out, near, far, pairwise(far, sibling)]
    row_context, own_codes, live = attend_rows(tables, codes, rows, cols, own, width)
    *halves_here, mixed_low, mixed_high = attend_columns_here(
        row_outs, live, row_context, own_codes, embed, col_qkv.reshape(3 * local, width)
    )
    contexts = []
    for context in halves_here:
        beyond = pairwise(context, across)
        contexts.append(
            (context, pairwise(context, sibling), beyond, pairwise(beyond, sibling))
        )
    blocks = finish(contexts, (mixed_low, mixed_high), col_out, groups)
    blocks = lax.all_to_all(blocks, "seq", split_axis=0, concat_axis=0, tiled=True)
    return jnp.swapaxes(order(blocks, cols, local), 1, 2)


def weight_fold(out_weight, piece):
    return jnp.einsum("rce,fe->rcf", piece, out_weight, preferred_element_type=f32)


def attend_columns(query, keys, values, key_live):
    rows_all, count_cols, local_width = query.shape
    heads_here = local_width // HEAD_DIM
    shape = (rows_all, count_cols, heads_here, HEAD_DIM)
    scores = jnp.einsum(
        "rchd,schd->chrs",
        query.reshape(shape),
        keys.reshape(shape),
        preferred_element_type=f32,
    ) * HEAD_DIM ** (-0.5)
    scores = jnp.where(key_live > 0, scores, -jnp.inf)
    probs = softmax_last(scores).astype(bf16)
    context = jnp.einsum(
        "chrs,schd->rchd", probs, values.reshape(shape), preferred_element_type=f32
    )
    return context.astype(bf16).reshape(rows_all, count_cols, local_width)


def send_back(context):
    return lax.all_to_all(context[:, None], "seq", split_axis=0, concat_axis=1, tiled=True)


def general_body(ids, pad_mask, embed, row_qkv, row_out, col_qkv, col_out):
    rows_here, cols = ids.shape
    width = embed.shape[1]
    local_width = row_out.shape[0]
    heads_here = local_width // HEAD_DIM
    groups = lax.axis_size("seq")
    per_group = cols // groups
    codes = lax.broadcasted_iota(jnp.int32, (1, 1, embed.shape[0]), 2)
    onehot = (ids[:, :, None] == codes).astype(bf16)
    embedded = jnp.einsum("rcv,vd->rcd", onehot, embed, preferred_element_type=f32)
    normed = layer_norm(embedded).astype(bf16)
    row_proj = jnp.einsum("rcd,ted->trce", normed, row_qkv, preferred_element_type=f32)
    row_proj = row_proj.astype(bf16)
    live = pad_mask.astype(bf16)
    head_shape = (rows_here, cols, heads_here, HEAD_DIM)
    query = (row_proj[0] * live[:, None, None]).reshape(head_shape)
    keys = row_proj[1].reshape(head_shape)
    values = row_proj[2].reshape(head_shape)
    partial_scores = jnp.einsum("rihd,rjhd->hij", query, keys, preferred_element_type=f32)
    count_here = jnp.sum(pad_mask.astype(f32))
    scale = HEAD_DIM ** (-0.5)
    total, count = lax.psum((partial_scores, count_here), "seq")
    row_probs = softmax_last(total * (scale / jnp.sqrt(count))).astype(bf16)
    row_context = jnp.einsum("hij,rjhd->rihd", row_probs, values, preferred_element_type=f32)
    row_context = row_context.astype(bf16).reshape(rows_here, cols, local_width)
    start_feature = lax.axis_index("head") * local_width
    resident = lax.dynamic_slice_in_dim(embedded, start_feature, local_width, 2)
    row_update = weight_fold(row_out, lax.all_gather(row_context, "head", axis=2, tiled=True))
    mixed = resident + row_update
    sums, squares = lax.psum((jnp.sum(mixed, axis=-1), jnp.sum(mixed * mixed, axis=-1)), "head")
    mean = sums / width
    spread = squares / width - mean * mean
    normed_here = ((mixed - mean[..., None]) * lax.rsqrt(spread[..., None] + EPS)).astype(bf16)
    live_tile = jnp.broadcast_to(live[:, None, None, None], (rows_here, groups, per_group, 1))
    normed_full = lax.all_gather(normed_here, "head", axis=2, tiled=True)
    col_proj = jnp.einsum("rcd,ted->rcte", normed_full, col_qkv, preferred_element_type=f32)
    packed = col_proj.astype(bf16).reshape(rows_here, groups, per_group, 3 * local_width)
    received = lax.all_to_all(packed, "seq", split_axis=1, concat_axis=0, tiled=True)
    mask_part = lax.all_to_all(live_tile, "seq", split_axis=1, concat_axis=0, tiled=True)
    column_out = send_back(
        attend_columns(
            received[:, 0, :, :local_width],
            received[:, 0, :, local_width : 2 * local_width],
            received[:, 0, :, 2 * local_width :],
            mask_part[:, 0, 0, 0],
        )
    )
    column_out = column_out.reshape(rows_here, cols, local_width)
    col_update = weight_fold(col_out, lax.all_gather(column_out, "head", axis=2, tiled=True))
    return (mixed + col_update).astype(bf16)


def body(ids, pad_mask, embed, row_qkv, row_out, col_qkv, col_out):
    rows_here, cols = ids.shape
    groups = lax.axis_size("seq")
    own, rows = cols // groups, rows_here * groups
    parts = lax.axis_size("head")
    local = row_out.shape[0]
    fits = (
        parts == 4
        and groups >= 4
        and groups & (groups - 1) == 0
        and rows * 8 == LANES
        and rows_here == 2
        and own % 32 == 0
        and cols >= LANES
        and local == LANES + HEAD_DIM
        and embed.shape[0] <= TABLE_ROWS
    )
    chosen = fast_body if fits else general_body
    return chosen(ids, pad_mask, embed, row_qkv, row_out, col_qkv, col_out)


def solution(mesh):
    placed = (
        P("seq", None),
        P("seq"),
        P(),
        P(None, "head", None),
        P("head", None),
        P(None, "head", None),
        P("head", None),
    )
    return jax.shard_map(
        body, mesh=mesh, in_specs=placed, out_specs=P("seq", None, "head"), check_vma=False
    )
```

```python
import functools

import jax
import jax.numpy as jnp
from jax import lax
from jax.experimental import pallas as pl
from jax.experimental.pallas import tpu as pltpu
from jax.sharding import PartitionSpec as P

HEAD_DIM = 64
EPS = 1e-05
LANES = 128
CODES = 64
TABLE_ROWS = 40

SMALL_VMEM = 8 * 1024 * 1024
LARGE_VMEM = 32 * 1024 * 1024

f32 = jnp.float32
bf16 = jnp.bfloat16


def layer_norm(values):
    mean = jnp.mean(values, axis=-1, keepdims=True)
    centred = values - mean
    spread = jnp.mean(centred * centred, axis=-1, keepdims=True)
    return centred * lax.rsqrt(spread + EPS)


def softmax_last(scores):
    top = jnp.max(scores, axis=-1, keepdims=True)
    weights = jnp.exp(scores - top)
    return weights * (1.0 / jnp.sum(weights, axis=-1, keepdims=True))


def dot_nt(left, right):
    return lax.dot_general(left, right, (((1,), (1,)), ((), ())), preferred_element_type=f32)


def dot_nn(left, right):
    return jnp.dot(left, right, preferred_element_type=f32)


def in_hbm(value):
    return pltpu.with_memory_space_constraint(value, pltpu.HBM)


def iota(shape, axis):
    return lax.broadcasted_iota(jnp.int32, shape, axis)


def code_kernel(ids_hbm, live_hbm, out_ref, ids_ref, live_ref, sems):
    loads = [
        pltpu.make_async_copy(ids_hbm, ids_ref, sems.at[0]),
        pltpu.make_async_copy(live_hbm, live_ref, sems.at[1]),
    ]
    for load in loads:
        load.start()
    for load in loads:
        load.wait()
    row = iota(ids_ref.shape, 0)
    live = jnp.zeros(ids_ref.shape, jnp.int32)
    for r in range(ids_ref.shape[0]):
        live = jnp.where(row == r, live_ref[r], live)
    out_ref[...] = ids_ref[...] + 65536 * live


def make_codes(ids, pad_mask):
    return pl.pallas_call(
        code_kernel,
        out_shape=jax.ShapeDtypeStruct(ids.shape, jnp.int32),
        in_specs=[pl.BlockSpec(memory_space=pltpu.HBM)] * 2,
        scratch_shapes=[
            pltpu.VMEM(ids.shape, jnp.int32),
            pltpu.SMEM(pad_mask.shape, jnp.int32),
            pltpu.SemaphoreType.DMA((2,)),
        ],
        compiler_params=pltpu.CompilerParams(vmem_limit_bytes=SMALL_VMEM),
        name="codes",
    )(in_hbm(ids), in_hbm(pad_mask))


def join_kernel(own_ref, other_ref, out_ref):
    both = jnp.concatenate([own_ref[...], other_ref[...]], 0)
    for pair in range(out_ref.shape[0]):
        out_ref[pair] = both


def join(own, other, pairs):
    rows, cols = own.shape
    return pl.pallas_call(
        join_kernel,
        out_shape=jax.ShapeDtypeStruct((pairs, 2 * rows, cols), own.dtype),
        compiler_params=pltpu.CompilerParams(vmem_limit_bytes=SMALL_VMEM),
        name="join",
    )(own, other)


def table_kernel(embed_hbm, qkv_hbm, out_ref, embed_ref, qkv_ref, padded_ref, sems):
    kinds = qkv_ref.shape[0]
    loads = [pltpu.make_async_copy(embed_hbm, embed_ref, sems.at[kinds])]
    loads += [
        pltpu.make_async_copy(qkv_hbm.at[t], qkv_ref.at[t], sems.at[t]) for t in range(kinds)
    ]
    for load in loads:
        load.start()
    padded_ref[...] = jnp.zeros(padded_ref.shape, f32)
    loads[0].wait()
    padded_ref[0 : embed_ref.shape[0], :] = embed_ref[...].astype(f32)
    normed = layer_norm(padded_ref[...]).astype(bf16)
    tables = []
    for t in range(kinds):
        loads[1 + t].wait()
        tables.append(dot_nt(normed, qkv_ref[t]))
    out_ref[...] = jnp.concatenate(tables, 1).astype(bf16)


def make_tables(embed, row_qkv):
    kinds, local, width = row_qkv.shape
    return pl.pallas_call(
        table_kernel,
        out_shape=jax.ShapeDtypeStruct((TABLE_ROWS, kinds * local), bf16),
        in_specs=[pl.BlockSpec(memory_space=pltpu.HBM)] * 2,
        scratch_shapes=[
            pltpu.VMEM(embed.shape, bf16),
            pltpu.VMEM(row_qkv.shape, bf16),
            pltpu.VMEM((TABLE_ROWS, width), f32),
            pltpu.SemaphoreType.DMA((kinds + 1,)),
        ],
        cost_estimate=pl.CostEstimate(
            flops=2 * 10**9, bytes_accessed=2 * row_qkv.size, transcendentals=0
        ),
        compiler_params=pltpu.CompilerParams(vmem_limit_bytes=SMALL_VMEM),
        name="tables",
    )(in_hbm(embed), in_hbm(row_qkv))


def halves(pair):
    lane = iota(pair.shape, 1)
    zero = jnp.zeros_like(pair)
    return jnp.where(lane < HEAD_DIM, pair, zero), jnp.where(lane < HEAD_DIM, zero, pair)


def spread_pair(pair):
    first, second = halves(pair)
    zero = jnp.zeros_like(pair)
    return jnp.concatenate(
        [
            jnp.concatenate([first, zero], 1),
            jnp.concatenate([zero, first], 1),
            jnp.concatenate([second, zero], 1),
            jnp.concatenate([zero, second], 1),
        ],
        0,
    )


def double(block):
    zero = jnp.zeros_like(block)
    return jnp.concatenate(
        [jnp.concatenate([block, zero], 1), jnp.concatenate([zero, block], 1)], 0
    )


def row_kernel(parts, *refs):
    tables_refs, refs = refs[:parts], refs[parts:]
    (
        codes_ref,
        row_context_ref,
        own_ref,
        live_ref,
        tables_ref,
        table_ref,
        hot_ref,
        live_own_ref,
        sum_ref,
        spread_ref,
    ) = refs
    depth, cols = hot_ref.shape
    rows = depth // CODES
    pairs = rows // 2
    own = live_own_ref.shape[0] // pairs
    width = row_context_ref.shape[1]
    heads = width // HEAD_DIM
    local = width // parts
    group = lax.axis_index("seq")
    part = lax.axis_index("head")
    for p in range(parts):
        tables_ref[part ^ p] = tables_refs[p][...]

    for t in range(3):
        table_ref[t, 0:TABLE_ROWS, :] = jnp.concatenate(
            [tables_ref[p, :, t * local : (t + 1) * local] for p in range(parts)], 1
        )
        table_ref[t, TABLE_ROWS:CODES, :] = jnp.zeros((CODES - TABLE_ROWS, width), bf16)

    pair = group // 2
    coded = jnp.concatenate([codes_ref[pair ^ d] for d in range(codes_ref.shape[0])], 0)
    ids = (coded & 0xFFFF).astype(f32)
    live = (coded[:, 0:LANES] >> 16).astype(f32)
    live_ref[...] = live
    code = iota((CODES, cols), 0).astype(f32)
    for r in range(rows):
        hot = jnp.broadcast_to(ids[r : r + 1, :], (CODES, cols)) == code
        hot_ref[r * CODES : (r + 1) * CODES, :] = hot.astype(f32).astype(bf16)

    pick = (iota((own, cols), 1) == group * own + iota((own, cols), 0)).astype(f32).astype(bf16)
    mine = dot_nt(pick, ids.astype(bf16))
    lane = iota((own, LANES), 1)
    first_half = lane < CODES
    lane_code = jnp.where(first_half, lane, lane - CODES).astype(f32)
    for k in range(pairs):
        value = jnp.where(first_half, mine[:, 2 * k : 2 * k + 1], mine[:, 2 * k + 1 : 2 * k + 2])
        hot = (value == lane_code).astype(f32)
        alive = jnp.where(first_half, live[2 * k : 2 * k + 1, :], live[2 * k + 1 : 2 * k + 2, :])
        own_ref[k * own : (k + 1) * own, :] = hot.astype(bf16)
        live_own_ref[k * own : (k + 1) * own, :] = (hot * alive).astype(bf16)

    spans = [slice(hp * LANES, (hp + 1) * LANES) for hp in range(heads // 2)]
    queries = [spread_pair(table_ref[0, :, span]) for span in spans]
    keys = [double(table_ref[1, :, span]) for span in spans]
    scores = [dot_nt(query, key) for query, key in zip(queries, keys)]
    high = [score.astype(bf16) for score in scores]
    low = [(score - part.astype(f32)).astype(bf16) for score, part in zip(scores, high)]
    for hp in range(heads // 2):
        for h2 in range(2):
            these = slice(h2 * LANES, (h2 + 1) * LANES)
            looked = dot_nn(
                live_own_ref[...], jnp.concatenate([high[hp][these], low[hp][these]], 1)
            ).astype(bf16)
            base = (hp * 2 + h2) * own
            for piece in range(2):
                for k in range(pairs):
                    to = piece * depth + k * LANES
                    sum_ref[base : base + own, to : to + LANES] = looked[
                        k * own : (k + 1) * own, piece * LANES : (piece + 1) * LANES
                    ]
    tied = dot_nn(sum_ref[:, 0:depth], hot_ref[...]) + dot_nn(
        sum_ref[:, depth : 2 * depth], hot_ref[...]
    )
    count = jnp.sum(live, axis=0, keepdims=True)[:, 0:1]
    probs = softmax_last(tied * (HEAD_DIM ** (-0.5) / jnp.sqrt(count))).astype(bf16)

    spread_ref[...] = dot_nt(probs, hot_ref[...]).astype(bf16)
    values = [spread_pair(table_ref[2, :, span]) for span in spans]
    contexts = []
    for hp in range(heads // 2):
        first = (hp * 2) * own
        weights = jnp.concatenate(
            [
                jnp.concatenate(
                    [
                        spread_ref[first : first + own, k * LANES : (k + 1) * LANES],
                        spread_ref[first + own : first + 2 * own, k * LANES : (k + 1) * LANES],
                    ],
                    1,
                )
                for k in range(pairs)
            ],
            0,
        )
        contexts.append(dot_nn(weights, values[hp]).astype(bf16))
    for hp in range(heads // 2):
        for k in range(pairs):
            for r2 in range(2):
                at = (2 * k + r2) * own
                row_context_ref[at : at + own, spans[hp]] = contexts[hp][
                    k * own : (k + 1) * own, r2 * LANES : (r2 + 1) * LANES
                ]


def attend_rows(tables, codes, rows, cols, own, width):
    heads = width // HEAD_DIM
    parts = len(tables)
    return pl.pallas_call(
        functools.partial(row_kernel, parts),
        out_shape=(
            jax.ShapeDtypeStruct((rows * own, width), bf16),
            jax.ShapeDtypeStruct((rows * own // 2, LANES), bf16),
            jax.ShapeDtypeStruct((rows, LANES), f32),
        ),
        scratch_shapes=[
            pltpu.VMEM((parts,) + tables[0].shape, bf16),
            pltpu.VMEM((3, CODES, width), bf16),
            pltpu.VMEM((rows * CODES, cols), bf16),
            pltpu.VMEM((rows // 2 * own, LANES), bf16),
            pltpu.VMEM((heads * own, 2 * rows * CODES), bf16),
            pltpu.VMEM((heads * own, rows * CODES), bf16),
        ],
        cost_estimate=pl.CostEstimate(flops=3 * 10**9, bytes_accessed=10**6, transcendentals=0),
        compiler_params=pltpu.CompilerParams(vmem_limit_bytes=LARGE_VMEM),
        name="row_attention",
    )(*tables, codes)


def column_kernel(parts, *refs):
    row_out_refs, refs = refs[:parts], refs[parts:]
    (
        live_ref,
        row_context_ref,
        own_ref,
        embed_ref,
        col_qkv_ref,
        *out_refs,
        row_out_ref,
        embed2_ref,
    ) = refs
    context_refs, mixed_refs = out_refs[:2], out_refs[2:]
    rows = live_ref.shape[0]
    tokens, width = row_context_ref.shape
    pairs = rows // 2
    own = tokens // rows
    vocab = embed_ref.shape[0]
    local = width // parts
    part = lax.axis_index("head")

    for p in range(parts):
        row_out_ref[part ^ p] = row_out_refs[p][...]
    embed2_ref[...] = jnp.zeros(embed2_ref.shape, bf16)
    embed2_ref[0:vocab, 0:width] = embed_ref[...]
    embed2_ref[CODES : CODES + vocab, width : 2 * width] = embed_ref[...]

    embedded2 = dot_nn(own_ref[...], embed2_ref[...])
    embedded = jnp.concatenate(
        [
            embedded2[k * own : (k + 1) * own, r2 * width : (r2 + 1) * width]
            for k in range(pairs)
            for r2 in range(2)
        ],
        0,
    )
    mixed = embedded + dot_nt(row_context_ref[...], row_out_ref[...].reshape(width, width))
    for p in range(parts):

        @pl.when(part == p)
        def _():
            for c in range(2):
                mixed_refs[c][...] = mixed[
                    c * tokens // 2 : (c + 1) * tokens // 2, p * local : (p + 1) * local
                ]

    normed = layer_norm(mixed).astype(bf16)

    few = 8
    groups = own // few
    unit = rows * few

    def regroup(values):
        shape = (rows, groups, few, values.shape[1])
        return jnp.swapaxes(values.reshape(shape), 0, 1).reshape(tokens, values.shape[1])

    proj = [
        dot_nt(normed, col_qkv_ref[t * local : (t + 1) * local, :]) for t in range(3)
    ]
    proj[0] = proj[0] * HEAD_DIM ** (-0.5)
    proj = [regroup(values).astype(bf16) for values in proj]
    sub, lan = iota((unit, unit), 0), iota((unit, unit), 1)
    same_column = (sub % few) == (lan % few)
    seq_of_lane = iota((rows, unit), 1) // few
    live_lane = jnp.sum(
        jnp.where(seq_of_lane == iota((rows, unit), 0), live_ref[...], 0.0), axis=0, keepdims=True
    )
    visible = jnp.logical_and(same_column, jnp.broadcast_to(live_lane, (unit, unit)) > 0)
    chosen = []
    for g in range(groups):
        at = slice(g * unit, (g + 1) * unit)
        for h in range(local // HEAD_DIM):
            first = h * HEAD_DIM // LANES * LANES
            span = slice(first, min(first + LANES, local))
            query, keys, values = (proj[t][at, span] for t in range(3))
            if query.shape[1] > HEAD_DIM:
                inside = iota(query.shape, 1) // HEAD_DIM == h % 2
                query = jnp.where(inside, query, jnp.zeros_like(query))
            chosen.append((query, keys, values))
    scores = [jnp.where(visible, dot_nt(query, keys), -jnp.inf) for query, keys, _ in chosen]
    tops = [jnp.max(score, axis=-1, keepdims=True) for score in scores]
    weights = [jnp.exp(score - top) for score, top in zip(scores, tops)]
    shares = [1.0 / jnp.sum(weight, axis=-1, keepdims=True) for weight in weights]
    probs = [(weight * share).astype(bf16) for weight, share in zip(weights, shares)]
    found = [dot_nn(prob, values) for prob, (_, _, values) in zip(probs, chosen)]
    many = local // HEAD_DIM
    first_head = iota((unit, LANES), 1) < HEAD_DIM
    blocks = [
        jnp.concatenate(
            [jnp.where(first_head, found[g * many], found[g * many + 1]), found[g * many + 2]], 1
        )
        for g in range(groups)
    ]
    whole = jnp.concatenate(blocks, 0).reshape(groups, rows, few, local)
    context = jnp.swapaxes(whole, 0, 1).reshape(tokens, local)
    half, some = tokens // 2, tokens // 4
    for c in range(2):
        part_of = context[c * half : (c + 1) * half]
        context_refs[c][0:half, :] = part_of[:, 0:LANES].astype(bf16)
        context_refs[c][half : half + some, :] = jnp.concatenate(
            [part_of[0:some, LANES:local], part_of[some:half, LANES:local]], 1
        ).astype(bf16)


def attend_columns_here(row_outs, live, row_context, own_codes, embed, col_qkv):
    parts = len(row_outs)
    tokens, width = row_context.shape
    local = width // parts
    return pl.pallas_call(
        functools.partial(column_kernel, parts),
        out_shape=(
            *[jax.ShapeDtypeStruct((tokens // 2 * local // LANES, LANES), bf16)] * 2,
            *[jax.ShapeDtypeStruct((tokens // 2, local), f32)] * 2,
        ),
        scratch_shapes=[
            pltpu.VMEM((parts, local, width), bf16),
            pltpu.VMEM((2 * CODES, 2 * width), bf16),
        ],
        cost_estimate=pl.CostEstimate(flops=2 * 10**9, bytes_accessed=10**6, transcendentals=0),
        compiler_params=pltpu.CompilerParams(vmem_limit_bytes=LARGE_VMEM),
        name="column_attention",
    )(*row_outs, live, row_context, own_codes, embed, col_qkv)


def finish_kernel(parts, groups, *refs):
    context_refs = [refs[:parts], refs[parts : 2 * parts]]
    mixed_refs = refs[2 * parts : 2 * parts + 2]
    col_out_ref, out_ref, weight_ref = refs[2 * parts + 2 :]
    tokens, local = mixed_refs[0].shape
    some = tokens // 2
    group = lax.axis_index("seq")
    part = lax.axis_index("head")
    for p in range(parts):
        weight_ref[p] = col_out_ref[:, p * local : (p + 1) * local]
    totals = [ref[...] for ref in mixed_refs]
    for p in range(parts):
        weight = weight_ref[part ^ p]
        rest = weight[:, LANES:local]
        zero = jnp.zeros_like(rest)
        left = jnp.concatenate([rest, zero], 1)
        right = jnp.concatenate([zero, rest], 1)
        for c in range(2):
            context = context_refs[c][p]
            last = context[tokens : tokens + some, :]
            totals[c] = (
                totals[c]
                + dot_nt(context[0:tokens, :], weight[:, 0:LANES])
                + jnp.concatenate([dot_nt(last, left), dot_nt(last, right)], 0)
            )
    slots = groups // 2
    own = tokens // slots // 2
    for d in range(groups):
        first, second = (
            totals[d // slots][(2 * (d % slots) + r) * own : (2 * (d % slots) + r + 1) * own, :]
            for r in range(2)
        )
        rest = jnp.concatenate([first[:, LANES:local], second[:, LANES:local]], 1)
        out_ref[group ^ d] = jnp.concatenate(
            [first[:, 0:LANES], second[:, 0:LANES], rest], 0
        ).astype(bf16)


def finish(contexts, mixed, col_out, groups):
    parts = len(contexts[0])
    tokens, local = mixed[0].shape
    return pl.pallas_call(
        functools.partial(finish_kernel, parts, groups),
        out_shape=jax.ShapeDtypeStruct(
            (groups, 2 * tokens // groups * local // LANES, LANES), bf16
        ),
        scratch_shapes=[pltpu.VMEM((parts, local, local), bf16)],
        compiler_params=pltpu.CompilerParams(vmem_limit_bytes=LARGE_VMEM),
        name="finish",
    )(*contexts[0], *contexts[1], *mixed, col_out)


def order_kernel(blocks_ref, out_ref):
    groups = blocks_ref.shape[0]
    local, cols = out_ref.shape[1:]
    own = cols // groups
    rest = local - LANES
    for part in range(3):
        piece = jnp.concatenate(
            [blocks_ref[g, part * own : (part + 1) * own, :] for g in range(groups)], 0
        )
        turned = piece.astype(f32).T.astype(bf16)
        if part < 2:
            out_ref[part, 0:LANES, :] = turned
        else:
            for r in range(2):
                out_ref[r, LANES:local, :] = turned[r * rest : (r + 1) * rest, :]


def order(blocks, cols, local):
    return pl.pallas_call(
        order_kernel,
        out_shape=jax.ShapeDtypeStruct((2, local, cols), bf16),
        compiler_params=pltpu.CompilerParams(vmem_limit_bytes=SMALL_VMEM),
        name="order",
    )(blocks)


def fast_body(ids, pad_mask, embed, row_qkv, row_out, col_qkv, col_out):
    rows_here, cols = ids.shape
    width = embed.shape[1]
    local = row_out.shape[0]
    groups, parts = lax.axis_size("seq"), lax.axis_size("head")
    own, rows = cols // groups, rows_here * groups

    def pairwise(value, partner):
        order = [(g, p) for g in range(groups) for p in range(parts)]
        link = [(g * parts + p, partner(g, p)) for g, p in order]
        return lax.ppermute(value, ("seq", "head"), [(i, g * parts + p) for i, (g, p) in link])

    def sibling(g, p):
        return g, p ^ 1

    def across(g, p):
        return g, p ^ 2

    def opposite(g, p):
        return g, p ^ 3

    coded = make_codes(ids, pad_mask)
    coded, row_qkv = lax.optimization_barrier((coded, row_qkv))
    received = pairwise(coded, lambda g, p: (g ^ 1, p))
    table = make_tables(embed, row_qkv)
    codes = join(coded, received, groups // 2)
    codes, table, row_out = lax.optimization_barrier((codes, table, row_out))
    tables = [table] + [pairwise(table, to) for to in (sibling, across, opposite)]
    far = pairwise(row_out, across)
    near = pairwise(row_out, sibling)
    codes = lax.all_to_all(
        codes,
        "seq",
        split_axis=0,
        concat_axis=0,
        tiled=True,
        axis_index_groups=[list(range(k, groups, 2)) for k in range(2)],
    )
    codes, far = lax.optimization_barrier((codes, far))
    row_outs = [row_out, near, far, pairwise(far, sibling)]
    row_context, own_codes, live = attend_rows(tables, codes, rows, cols, own, width)
    *halves_here, mixed_low, mixed_high = attend_columns_here(
        row_outs, live, row_context, own_codes, embed, col_qkv.reshape(3 * local, width)
    )
    contexts = []
    for context in halves_here:
        beyond = pairwise(context, across)
        contexts.append(
            (context, pairwise(context, sibling), beyond, pairwise(beyond, sibling))
        )
    blocks = finish(contexts, (mixed_low, mixed_high), col_out, groups)
    blocks = lax.all_to_all(blocks, "seq", split_axis=0, concat_axis=0, tiled=True)
    return jnp.swapaxes(order(blocks, cols, local), 1, 2)


def weight_fold(out_weight, piece):
    return jnp.einsum("rce,fe->rcf", piece, out_weight, preferred_element_type=f32)


def attend_columns(query, keys, values, key_live):
    rows_all, count_cols, local_width = query.shape
    heads_here = local_width // HEAD_DIM
    shape = (rows_all, count_cols, heads_here, HEAD_DIM)
    scores = jnp.einsum(
        "rchd,schd->chrs",
        query.reshape(shape),
        keys.reshape(shape),
        preferred_element_type=f32,
    ) * HEAD_DIM ** (-0.5)
    scores = jnp.where(key_live > 0, scores, -jnp.inf)
    probs = softmax_last(scores).astype(bf16)
    context = jnp.einsum(
        "chrs,schd->rchd", probs, values.reshape(shape), preferred_element_type=f32
    )
    return context.astype(bf16).reshape(rows_all, count_cols, local_width)


def send_back(context):
    return lax.all_to_all(context[:, None], "seq", split_axis=0, concat_axis=1, tiled=True)


def general_body(ids, pad_mask, embed, row_qkv, row_out, col_qkv, col_out):
    rows_here, cols = ids.shape
    width = embed.shape[1]
    local_width = row_out.shape[0]
    heads_here = local_width // HEAD_DIM
    groups = lax.axis_size("seq")
    per_group = cols // groups
    codes = lax.broadcasted_iota(jnp.int32, (1, 1, embed.shape[0]), 2)
    onehot = (ids[:, :, None] == codes).astype(bf16)
    embedded = jnp.einsum("rcv,vd->rcd", onehot, embed, preferred_element_type=f32)
    normed = layer_norm(embedded).astype(bf16)
    row_proj = jnp.einsum("rcd,ted->trce", normed, row_qkv, preferred_element_type=f32)
    row_proj = row_proj.astype(bf16)
    live = pad_mask.astype(bf16)
    head_shape = (rows_here, cols, heads_here, HEAD_DIM)
    query = (row_proj[0] * live[:, None, None]).reshape(head_shape)
    keys = row_proj[1].reshape(head_shape)
    values = row_proj[2].reshape(head_shape)
    partial_scores = jnp.einsum("rihd,rjhd->hij", query, keys, preferred_element_type=f32)
    count_here = jnp.sum(pad_mask.astype(f32))
    scale = HEAD_DIM ** (-0.5)
    total, count = lax.psum((partial_scores, count_here), "seq")
    row_probs = softmax_last(total * (scale / jnp.sqrt(count))).astype(bf16)
    row_context = jnp.einsum("hij,rjhd->rihd", row_probs, values, preferred_element_type=f32)
    row_context = row_context.astype(bf16).reshape(rows_here, cols, local_width)
    start_feature = lax.axis_index("head") * local_width
    resident = lax.dynamic_slice_in_dim(embedded, start_feature, local_width, 2)
    row_update = weight_fold(row_out, lax.all_gather(row_context, "head", axis=2, tiled=True))
    mixed = resident + row_update
    sums, squares = lax.psum((jnp.sum(mixed, axis=-1), jnp.sum(mixed * mixed, axis=-1)), "head")
    mean = sums / width
    spread = squares / width - mean * mean
    normed_here = ((mixed - mean[..., None]) * lax.rsqrt(spread[..., None] + EPS)).astype(bf16)
    live_tile = jnp.broadcast_to(live[:, None, None, None], (rows_here, groups, per_group, 1))
    normed_full = lax.all_gather(normed_here, "head", axis=2, tiled=True)
    col_proj = jnp.einsum("rcd,ted->rcte", normed_full, col_qkv, preferred_element_type=f32)
    packed = col_proj.astype(bf16).reshape(rows_here, groups, per_group, 3 * local_width)
    received = lax.all_to_all(packed, "seq", split_axis=1, concat_axis=0, tiled=True)
    mask_part = lax.all_to_all(live_tile, "seq", split_axis=1, concat_axis=0, tiled=True)
    column_out = send_back(
        attend_columns(
            received[:, 0, :, :local_width],
            received[:, 0, :, local_width : 2 * local_width],
            received[:, 0, :, 2 * local_width :],
            mask_part[:, 0, 0, 0],
        )
    )
    column_out = column_out.reshape(rows_here, cols, local_width)
    col_update = weight_fold(col_out, lax.all_gather(column_out, "head", axis=2, tiled=True))
    return (mixed + col_update).astype(bf16)


def body(ids, pad_mask, embed, row_qkv, row_out, col_qkv, col_out):
    rows_here, cols = ids.shape
    groups = lax.axis_size("seq")
    own, rows = cols // groups, rows_here * groups
    parts = lax.axis_size("head")
    local = row_out.shape[0]
    fits = (
        parts == 4
        and groups >= 4
        and groups & (groups - 1) == 0
        and rows * 8 == LANES
        and rows_here == 2
        and own % 32 == 0
        and cols >= LANES
        and local == LANES + HEAD_DIM
        and embed.shape[0] <= TABLE_ROWS
    )
    chosen = fast_body if fits else general_body
    return chosen(ids, pad_mask, embed, row_qkv, row_out, col_qkv, col_out)


def solution(mesh):
    placed = (
        P("seq", None),
        P("seq"),
        P(),
        P(None, "head", None),
        P("head", None),
        P(None, "head", None),
        P("head", None),
    )
    return jax.shard_map(
        body, mesh=mesh, in_specs=placed, out_specs=P("seq", None, "head"), check_vma=False
    )
```

```python
import functools

import jax
import jax.numpy as jnp
from jax import lax
from jax.experimental import pallas as pl
from jax.experimental.pallas import tpu as pltpu
from jax.sharding import PartitionSpec as P

HEAD_DIM = 64
EPS = 1e-05
LANES = 128
CODES = 64
TABLE_ROWS = 40

SMALL_VMEM = 8 * 1024 * 1024
LARGE_VMEM = 32 * 1024 * 1024

f32 = jnp.float32
bf16 = jnp.bfloat16


def layer_norm(values):
    mean = jnp.mean(values, axis=-1, keepdims=True)
    centred = values - mean
    spread = jnp.mean(centred * centred, axis=-1, keepdims=True)
    return centred * lax.rsqrt(spread + EPS)


def softmax_last(scores):
    top = jnp.max(scores, axis=-1, keepdims=True)
    weights = jnp.exp(scores - top)
    return weights * (1.0 / jnp.sum(weights, axis=-1, keepdims=True))


def dot_nt(left, right):
    return lax.dot_general(left, right, (((1,), (1,)), ((), ())), preferred_element_type=f32)


def dot_nn(left, right):
    return jnp.dot(left, right, preferred_element_type=f32)


def in_hbm(value):
    return pltpu.with_memory_space_constraint(value, pltpu.HBM)


def iota(shape, axis):
    return lax.broadcasted_iota(jnp.int32, shape, axis)


def code_kernel(ids_hbm, live_hbm, out_ref, ids_ref, live_ref, sems):
    loads = [
        pltpu.make_async_copy(ids_hbm, ids_ref, sems.at[0]),
        pltpu.make_async_copy(live_hbm, live_ref, sems.at[1]),
    ]
    for load in loads:
        load.start()
    for load in loads:
        load.wait()
    row = iota(ids_ref.shape, 0)
    live = jnp.zeros(ids_ref.shape, jnp.int32)
    for r in range(ids_ref.shape[0]):
        live = jnp.where(row == r, live_ref[r], live)
    coded = ids_ref[...] + 65536 * live
    out_ref[...] = jnp.concatenate([coded] * (out_ref.shape[0] // coded.shape[0]), 0)


def make_codes(ids, pad_mask, height):
    return pl.pallas_call(
        code_kernel,
        out_shape=jax.ShapeDtypeStruct((height, ids.shape[1]), jnp.int32),
        in_specs=[pl.BlockSpec(memory_space=pltpu.HBM)] * 2,
        scratch_shapes=[
            pltpu.VMEM(ids.shape, jnp.int32),
            pltpu.SMEM(pad_mask.shape, jnp.int32),
            pltpu.SemaphoreType.DMA((2,)),
        ],
        compiler_params=pltpu.CompilerParams(vmem_limit_bytes=SMALL_VMEM),
        name="codes",
    )(in_hbm(ids), in_hbm(pad_mask))


def join_kernel(rows, own_ref, other_ref, out_ref):
    own, other = own_ref[...], other_ref[...]
    both = jnp.concatenate([own[0:rows], other[0:rows]], 0)
    out_ref[...] = jnp.concatenate([both] * (own.shape[0] // (2 * rows)), 0)


def join(own, other, rows):
    return pl.pallas_call(
        functools.partial(join_kernel, rows),
        out_shape=jax.ShapeDtypeStruct(own.shape, own.dtype),
        compiler_params=pltpu.CompilerParams(vmem_limit_bytes=SMALL_VMEM),
        name="join",
    )(own, other)


def table_kernel(embed_hbm, qkv_hbm, out_ref, embed_ref, qkv_ref, padded_ref, sems):
    kinds = qkv_ref.shape[0]
    loads = [pltpu.make_async_copy(embed_hbm, embed_ref, sems.at[kinds])]
    loads += [
        pltpu.make_async_copy(qkv_hbm.at[t], qkv_ref.at[t], sems.at[t]) for t in range(kinds)
    ]
    for load in loads:
        load.start()
    padded_ref[...] = jnp.zeros(padded_ref.shape, f32)
    loads[0].wait()
    padded_ref[0 : embed_ref.shape[0], :] = embed_ref[...].astype(f32)
    normed = layer_norm(padded_ref[...]).astype(bf16)
    tables = []
    for t in range(kinds):
        loads[1 + t].wait()
        tables.append(dot_nt(normed, qkv_ref[t]))
    out_ref[...] = jnp.concatenate(tables, 1).astype(bf16)


def make_tables(embed, row_qkv):
    kinds, local, width = row_qkv.shape
    return pl.pallas_call(
        table_kernel,
        out_shape=jax.ShapeDtypeStruct((TABLE_ROWS, kinds * local), bf16),
        in_specs=[pl.BlockSpec(memory_space=pltpu.HBM)] * 2,
        scratch_shapes=[
            pltpu.VMEM(embed.shape, bf16),
            pltpu.VMEM(row_qkv.shape, bf16),
            pltpu.VMEM((TABLE_ROWS, width), f32),
            pltpu.SemaphoreType.DMA((kinds + 1,)),
        ],
        cost_estimate=pl.CostEstimate(
            flops=2 * 10**9, bytes_accessed=2 * row_qkv.size, transcendentals=0
        ),
        compiler_params=pltpu.CompilerParams(vmem_limit_bytes=SMALL_VMEM),
        name="tables",
    )(in_hbm(embed), in_hbm(row_qkv))


def halves(pair):
    lane = iota(pair.shape, 1)
    zero = jnp.zeros_like(pair)
    return jnp.where(lane < HEAD_DIM, pair, zero), jnp.where(lane < HEAD_DIM, zero, pair)


def spread_pair(pair):
    first, second = halves(pair)
    zero = jnp.zeros_like(pair)
    return jnp.concatenate(
        [
            jnp.concatenate([first, zero], 1),
            jnp.concatenate([zero, first], 1),
            jnp.concatenate([second, zero], 1),
            jnp.concatenate([zero, second], 1),
        ],
        0,
    )


def double(block):
    zero = jnp.zeros_like(block)
    return jnp.concatenate(
        [jnp.concatenate([block, zero], 1), jnp.concatenate([zero, block], 1)], 0
    )


def row_kernel(parts, *refs):
    tables_refs, refs = refs[:parts], refs[parts:]
    (
        near_codes_ref,
        far_codes_ref,
        row_context_ref,
        own_ref,
        live_ref,
        tables_ref,
        table_ref,
        hot_ref,
        live_own_ref,
        sum_ref,
        spread_ref,
    ) = refs
    depth, cols = hot_ref.shape
    rows = depth // CODES
    pairs = rows // 2
    own = live_own_ref.shape[0] // pairs
    width = row_context_ref.shape[1]
    heads = width // HEAD_DIM
    local = width // parts
    group = lax.axis_index("seq")
    part = lax.axis_index("head")
    for p in range(parts):
        tables_ref[part ^ p] = tables_refs[p][...]

    for t in range(3):
        table_ref[t, 0:TABLE_ROWS, :] = jnp.concatenate(
            [tables_ref[p, :, t * local : (t + 1) * local] for p in range(parts)], 1
        )
        table_ref[t, TABLE_ROWS:CODES, :] = jnp.zeros((CODES - TABLE_ROWS, width), bf16)

    coded = jnp.concatenate([near_codes_ref[...], far_codes_ref[...]], 0)
    ids = (coded & 0xFFFF).astype(f32)
    live = (coded[:, 0:LANES] >> 16).astype(f32)
    live_ref[...] = live
    code = iota((CODES, cols), 0).astype(f32)
    for r in range(rows):
        hot = jnp.broadcast_to(ids[r : r + 1, :], (CODES, cols)) == code
        hot_ref[r * CODES : (r + 1) * CODES, :] = hot.astype(f32).astype(bf16)

    pick = (iota((own, cols), 1) == group * own + iota((own, cols), 0)).astype(f32).astype(bf16)
    mine = dot_nt(pick, ids.astype(bf16))
    lane = iota((own, LANES), 1)
    first_half = lane < CODES
    lane_code = jnp.where(first_half, lane, lane - CODES).astype(f32)
    for k in range(pairs):
        value = jnp.where(first_half, mine[:, 2 * k : 2 * k + 1], mine[:, 2 * k + 1 : 2 * k + 2])
        hot = (value == lane_code).astype(f32)
        alive = jnp.where(first_half, live[2 * k : 2 * k + 1, :], live[2 * k + 1 : 2 * k + 2, :])
        own_ref[k * own : (k + 1) * own, :] = hot.astype(bf16)
        live_own_ref[k * own : (k + 1) * own, :] = (hot * alive).astype(bf16)

    spans = [slice(hp * LANES, (hp + 1) * LANES) for hp in range(heads // 2)]
    queries = [spread_pair(table_ref[0, :, span]) for span in spans]
    keys = [double(table_ref[1, :, span]) for span in spans]
    scores = [dot_nt(query, key) for query, key in zip(queries, keys)]
    high = [score.astype(bf16) for score in scores]
    low = [(score - part.astype(f32)).astype(bf16) for score, part in zip(scores, high)]
    for hp in range(heads // 2):
        for h2 in range(2):
            these = slice(h2 * LANES, (h2 + 1) * LANES)
            looked = dot_nn(
                live_own_ref[...], jnp.concatenate([high[hp][these], low[hp][these]], 1)
            ).astype(bf16)
            base = (hp * 2 + h2) * own
            for piece in range(2):
                for k in range(pairs):
                    to = piece * depth + k * LANES
                    sum_ref[base : base + own, to : to + LANES] = looked[
                        k * own : (k + 1) * own, piece * LANES : (piece + 1) * LANES
                    ]
    tied = dot_nn(sum_ref[:, 0:depth], hot_ref[...]) + dot_nn(
        sum_ref[:, depth : 2 * depth], hot_ref[...]
    )
    count = jnp.sum(live, axis=0, keepdims=True)[:, 0:1]
    probs = softmax_last(tied * (HEAD_DIM ** (-0.5) / jnp.sqrt(count))).astype(bf16)

    spread_ref[...] = dot_nt(probs, hot_ref[...]).astype(bf16)
    values = [spread_pair(table_ref[2, :, span]) for span in spans]
    contexts = []
    for hp in range(heads // 2):
        first = (hp * 2) * own
        weights = jnp.concatenate(
            [
                jnp.concatenate(
                    [
                        spread_ref[first : first + own, k * LANES : (k + 1) * LANES],
                        spread_ref[first + own : first + 2 * own, k * LANES : (k + 1) * LANES],
                    ],
                    1,
                )
                for k in range(pairs)
            ],
            0,
        )
        contexts.append(dot_nn(weights, values[hp]).astype(bf16))
    for hp in range(heads // 2):
        for k in range(pairs):
            for r2 in range(2):
                at = (2 * k + r2) * own
                row_context_ref[at : at + own, spans[hp]] = contexts[hp][
                    k * own : (k + 1) * own, r2 * LANES : (r2 + 1) * LANES
                ]


def attend_rows(tables, codes, rows, cols, own, width):
    heads = width // HEAD_DIM
    parts = len(tables)
    return pl.pallas_call(
        functools.partial(row_kernel, parts),
        out_shape=(
            jax.ShapeDtypeStruct((rows * own, width), bf16),
            jax.ShapeDtypeStruct((rows * own // 2, LANES), bf16),
            jax.ShapeDtypeStruct((rows, LANES), f32),
        ),
        scratch_shapes=[
            pltpu.VMEM((parts,) + tables[0].shape, bf16),
            pltpu.VMEM((3, CODES, width), bf16),
            pltpu.VMEM((rows * CODES, cols), bf16),
            pltpu.VMEM((rows // 2 * own, LANES), bf16),
            pltpu.VMEM((heads * own, 2 * rows * CODES), bf16),
            pltpu.VMEM((heads * own, rows * CODES), bf16),
        ],
        cost_estimate=pl.CostEstimate(flops=3 * 10**9, bytes_accessed=10**6, transcendentals=0),
        compiler_params=pltpu.CompilerParams(vmem_limit_bytes=LARGE_VMEM),
        name="row_attention",
    )(*tables, *codes)


def column_kernel(parts, *refs):
    row_out_refs, refs = refs[:parts], refs[parts:]
    (
        live_ref,
        row_context_ref,
        own_ref,
        embed_ref,
        col_qkv_ref,
        *context_refs,
        mixed_out_ref,
        row_out_ref,
        embed2_ref,
        weight_ref,
    ) = refs
    rows = live_ref.shape[0]
    tokens, width = row_context_ref.shape
    pairs = rows // 2
    own = tokens // rows
    vocab = embed_ref.shape[0]
    local = width // parts
    part = lax.axis_index("head")

    for p in range(parts):
        row_out_ref[part ^ p] = row_out_refs[p][...]
    embed2_ref[...] = jnp.zeros(embed2_ref.shape, bf16)
    embed2_ref[0:vocab, 0:width] = embed_ref[...]
    embed2_ref[CODES : CODES + vocab, width : 2 * width] = embed_ref[...]

    embedded2 = dot_nn(own_ref[...], embed2_ref[...])
    embedded = jnp.concatenate(
        [
            embedded2[k * own : (k + 1) * own, r2 * width : (r2 + 1) * width]
            for k in range(pairs)
            for r2 in range(2)
        ],
        0,
    )
    mixed = embedded + dot_nt(row_context_ref[...], row_out_ref[...].reshape(width, width))
    for p in range(parts):

        @pl.when(part == p)
        def _():
            mixed_out_ref[...] = mixed[:, p * local : (p + 1) * local]

    normed = layer_norm(mixed).astype(bf16)

    few = 8
    groups = own // few
    unit = rows * few

    def regroup(values):
        shape = (rows, groups, few, values.shape[1])
        return jnp.swapaxes(values.reshape(shape), 0, 1).reshape(tokens, values.shape[1])

    odd = part % 2
    for t in range(3):
        first = pl.multiple_of(t * local + odd * HEAD_DIM, HEAD_DIM)
        last = pl.multiple_of(t * local + (1 - odd) * LANES, HEAD_DIM)
        third = (3 + t) * LANES
        weight_ref[t * LANES : (t + 1) * LANES, :] = col_qkv_ref[pl.ds(first, LANES), :]
        weight_ref[third : third + HEAD_DIM, :] = col_qkv_ref[pl.ds(last, HEAD_DIM), :]
        weight_ref[third + HEAD_DIM : third + LANES, :] = jnp.zeros((HEAD_DIM, width), bf16)
    proj = [
        dot_nt(normed, weight_ref[2 * j * LANES : 2 * (j + 1) * LANES, :]) for j in range(3)
    ]
    proj = [
        proj[j][:, k * LANES : (k + 1) * LANES] * (HEAD_DIM ** (-0.5) if (2 * j + k) % 3 == 0 else 1.0)
        for j in range(3)
        for k in range(2)
    ]
    proj = [regroup(values).astype(bf16) for values in proj]
    sub, lan = iota((unit, unit), 0), iota((unit, unit), 1)
    same_column = (sub % few) == (lan % few)
    seq_of_lane = iota((rows, unit), 1) // few
    live_lane = jnp.sum(
        jnp.where(seq_of_lane == iota((rows, unit), 0), live_ref[...], 0.0), axis=0, keepdims=True
    )
    visible = jnp.logical_and(same_column, jnp.broadcast_to(live_lane, (unit, unit)) > 0)
    chosen = []
    for g in range(groups):
        at = slice(g * unit, (g + 1) * unit)
        query, keys, values = (proj[t][at] for t in range(3))
        chosen += [(half, keys, values) for half in halves(query)]
        chosen.append(tuple(proj[3 + t][at] for t in range(3)))
    scores = [jnp.where(visible, dot_nt(query, keys), -jnp.inf) for query, keys, _ in chosen]
    tops = [jnp.max(score, axis=-1, keepdims=True) for score in scores]
    weights = [jnp.exp(score - top) for score, top in zip(scores, tops)]
    shares = [1.0 / jnp.sum(weight, axis=-1, keepdims=True) for weight in weights]
    probs = [(weight * share).astype(bf16) for weight, share in zip(weights, shares)]
    found = [dot_nn(prob, values) for prob, (_, _, values) in zip(probs, chosen)]
    first_head = iota((unit, LANES), 1) < HEAD_DIM

    def ungroup(blocks):
        whole = jnp.concatenate(blocks, 0).reshape(groups, rows, few, LANES)
        return jnp.swapaxes(whole, 0, 1).reshape(tokens, LANES)

    main = ungroup(
        [jnp.where(first_head, found[3 * g], found[3 * g + 1]) for g in range(groups)]
    )
    third = ungroup([found[3 * g + 2] for g in range(groups)])
    start = 0
    for context_ref in context_refs:
        count = context_ref.shape[0] * 2 // 3
        some = count // 2
        context_ref[0:count, :] = main[start : start + count].astype(bf16)
        early = third[start : start + some]
        late = third[start + some : start + count]
        left = jnp.where(odd == 1, late, early)
        right = jnp.where(odd == 1, early, late)
        context_ref[count : count + some, :] = jnp.concatenate(
            [left[:, 0:HEAD_DIM], right[:, 0:HEAD_DIM]], 1
        ).astype(bf16)
        start += count


def attend_columns_here(row_outs, live, row_context, own_codes, embed, col_qkv):
    parts = len(row_outs)
    tokens, width = row_context.shape
    local = width // parts
    half = tokens // 2 * local // LANES
    return pl.pallas_call(
        functools.partial(column_kernel, parts),
        out_shape=(
            jax.ShapeDtypeStruct((half, LANES), bf16),
            jax.ShapeDtypeStruct((half, LANES), bf16),
            jax.ShapeDtypeStruct((tokens, local), f32),
        ),
        scratch_shapes=[
            pltpu.VMEM((parts, local, width), bf16),
            pltpu.VMEM((2 * CODES, 2 * width), bf16),
            pltpu.VMEM((6 * LANES, width), bf16),
        ],
        cost_estimate=pl.CostEstimate(flops=2 * 10**9, bytes_accessed=10**6, transcendentals=0),
        compiler_params=pltpu.CompilerParams(vmem_limit_bytes=LARGE_VMEM),
        name="column_attention",
    )(*row_outs, live, row_context, own_codes, embed, col_qkv)


def finish_kernel(parts, groups, *refs):
    context_refs = [refs[:parts], refs[parts : 2 * parts]]
    mixed_ref, col_out_ref, out_ref, context_ref = refs[2 * parts :]
    tokens, local = mixed_ref.shape
    group = lax.axis_index("seq")
    part = lax.axis_index("head")
    starts = [0, context_refs[0][0].shape[0]]
    for start, some_refs in zip(starts, context_refs):
        for p in range(parts):
            context_ref[part ^ p, start : start + some_refs[p].shape[0], :] = some_refs[p][...]
    pieces = []
    for start, some_refs in zip(starts, context_refs):
        count = some_refs[0].shape[0] * 2 // 3
        end = start + some_refs[0].shape[0]
        low = iota((count // 2, LANES), 1) < HEAD_DIM
        features = []
        for p in range(0, parts, 2):
            even = context_ref[p, start + count : end, :]
            other = context_ref[p + 1, start + count : end, :]
            early = jnp.where(low, even, other)
            late = jnp.where(low, other, even)
            late = jnp.concatenate([late[:, HEAD_DIM:], late[:, 0:HEAD_DIM]], 1)
            features += [
                context_ref[p, start : start + count, :],
                jnp.concatenate([early, late], 0),
                context_ref[p + 1, start : start + count, :],
            ]
        pieces.append(jnp.concatenate(features, 1))
    total = mixed_ref[...] + dot_nt(jnp.concatenate(pieces, 0), col_out_ref[...])
    own = tokens // groups // 2
    for d in range(groups):
        first, second = (total[(2 * d + r) * own : (2 * d + r + 1) * own, :] for r in range(2))
        rest = jnp.concatenate([first[:, LANES:local], second[:, LANES:local]], 1)
        out_ref[group ^ d] = jnp.concatenate(
            [first[:, 0:LANES], second[:, 0:LANES], rest], 0
        ).astype(bf16)


def finish(contexts, mixed, col_out, groups):
    parts = len(contexts[0])
    tokens, local = mixed.shape
    return pl.pallas_call(
        functools.partial(finish_kernel, parts, groups),
        out_shape=jax.ShapeDtypeStruct((groups, tokens // groups * local // LANES, LANES), bf16),
        scratch_shapes=[pltpu.VMEM((parts, tokens * local // LANES, LANES), bf16)],
        compiler_params=pltpu.CompilerParams(vmem_limit_bytes=LARGE_VMEM),
        name="finish",
    )(*contexts[0], *contexts[1], mixed, col_out)


def order_kernel(blocks_ref, out_ref):
    groups = blocks_ref.shape[0]
    local, cols = out_ref.shape[1:]
    own = cols // groups
    rest = local - LANES
    for part in range(3):
        piece = jnp.concatenate(
            [blocks_ref[g, part * own : (part + 1) * own, :] for g in range(groups)], 0
        )
        turned = piece.astype(f32).T.astype(bf16)
        if part < 2:
            out_ref[part, 0:LANES, :] = turned
        else:
            for r in range(2):
                out_ref[r, LANES:local, :] = turned[r * rest : (r + 1) * rest, :]


def order(blocks, cols, local):
    return pl.pallas_call(
        order_kernel,
        out_shape=jax.ShapeDtypeStruct((2, local, cols), bf16),
        compiler_params=pltpu.CompilerParams(vmem_limit_bytes=SMALL_VMEM),
        name="order",
    )(blocks)


def fast_body(ids, pad_mask, embed, row_qkv, row_out, col_qkv, col_out):
    rows_here, cols = ids.shape
    width = embed.shape[1]
    local = row_out.shape[0]
    groups, parts = lax.axis_size("seq"), lax.axis_size("head")
    own, rows = cols // groups, rows_here * groups

    def pairwise(value, partner):
        order = [(g, p) for g in range(groups) for p in range(parts)]
        link = [(g * parts + p, partner(g, p)) for g, p in order]
        return lax.ppermute(value, ("seq", "head"), [(i, g * parts + p) for i, (g, p) in link])

    def sibling(g, p):
        return g, p ^ 1

    def across(g, p):
        return g, p ^ 2

    def opposite(g, p):
        return g, p ^ 3

    far = pairwise(row_out, across)
    coded = make_codes(ids, pad_mask, rows_here * groups // 2)
    coded, row_qkv = lax.optimization_barrier((coded, row_qkv))
    received = pairwise(coded, lambda g, p: (g ^ 1, p))
    table = make_tables(embed, row_qkv)
    step = 2
    while step < groups:
        coded = join(coded, received, rows_here * step // 2)
        if step == 2:
            coded, table = lax.optimization_barrier((coded, table))
            far_tables = [pairwise(table, to) for to in (across, opposite)]
        received = pairwise(coded, lambda g, p, step=step: (g ^ step, p))
        step *= 2
    codes = (coded, received)
    coded, late_table = lax.optimization_barrier((coded, table))
    codes = (coded, received)
    tables = [table, pairwise(late_table, sibling)] + far_tables
    *codes, near, far = lax.optimization_barrier((*codes, row_out, far))
    row_outs = [row_out, pairwise(near, sibling), far, pairwise(far, sibling)]
    row_context, own_codes, live = attend_rows(tables, codes, rows, cols, own, width)
    *halves_here, mixed = attend_columns_here(
        row_outs, live, row_context, own_codes, embed, col_qkv.reshape(3 * local, width)
    )
    contexts = []
    for context in halves_here:
        beyond = pairwise(context, across)
        contexts.append(
            (context, pairwise(context, sibling), beyond, pairwise(beyond, sibling))
        )
    blocks = finish(contexts, mixed, col_out, groups)
    blocks = lax.all_to_all(blocks, "seq", split_axis=0, concat_axis=0, tiled=True)
    return jnp.swapaxes(order(blocks, cols, local), 1, 2)


def weight_fold(out_weight, piece):
    return jnp.einsum("rce,fe->rcf", piece, out_weight, preferred_element_type=f32)


def attend_columns(query, keys, values, key_live):
    rows_all, count_cols, local_width = query.shape
    heads_here = local_width // HEAD_DIM
    shape = (rows_all, count_cols, heads_here, HEAD_DIM)
    scores = jnp.einsum(
        "rchd,schd->chrs",
        query.reshape(shape),
        keys.reshape(shape),
        preferred_element_type=f32,
    ) * HEAD_DIM ** (-0.5)
    scores = jnp.where(key_live > 0, scores, -jnp.inf)
    probs = softmax_last(scores).astype(bf16)
    context = jnp.einsum(
        "chrs,schd->rchd", probs, values.reshape(shape), preferred_element_type=f32
    )
    return context.astype(bf16).reshape(rows_all, count_cols, local_width)


def send_back(context):
    return lax.all_to_all(context[:, None], "seq", split_axis=0, concat_axis=1, tiled=True)


def general_body(ids, pad_mask, embed, row_qkv, row_out, col_qkv, col_out):
    rows_here, cols = ids.shape
    width = embed.shape[1]
    local_width = row_out.shape[0]
    heads_here = local_width // HEAD_DIM
    groups = lax.axis_size("seq")
    per_group = cols // groups
    codes = lax.broadcasted_iota(jnp.int32, (1, 1, embed.shape[0]), 2)
    onehot = (ids[:, :, None] == codes).astype(bf16)
    embedded = jnp.einsum("rcv,vd->rcd", onehot, embed, preferred_element_type=f32)
    normed = layer_norm(embedded).astype(bf16)
    row_proj = jnp.einsum("rcd,ted->trce", normed, row_qkv, preferred_element_type=f32)
    row_proj = row_proj.astype(bf16)
    live = pad_mask.astype(bf16)
    head_shape = (rows_here, cols, heads_here, HEAD_DIM)
    query = (row_proj[0] * live[:, None, None]).reshape(head_shape)
    keys = row_proj[1].reshape(head_shape)
    values = row_proj[2].reshape(head_shape)
    partial_scores = jnp.einsum("rihd,rjhd->hij", query, keys, preferred_element_type=f32)
    count_here = jnp.sum(pad_mask.astype(f32))
    scale = HEAD_DIM ** (-0.5)
    total, count = lax.psum((partial_scores, count_here), "seq")
    row_probs = softmax_last(total * (scale / jnp.sqrt(count))).astype(bf16)
    row_context = jnp.einsum("hij,rjhd->rihd", row_probs, values, preferred_element_type=f32)
    row_context = row_context.astype(bf16).reshape(rows_here, cols, local_width)
    start_feature = lax.axis_index("head") * local_width
    resident = lax.dynamic_slice_in_dim(embedded, start_feature, local_width, 2)
    row_update = weight_fold(row_out, lax.all_gather(row_context, "head", axis=2, tiled=True))
    mixed = resident + row_update
    sums, squares = lax.psum((jnp.sum(mixed, axis=-1), jnp.sum(mixed * mixed, axis=-1)), "head")
    mean = sums / width
    spread = squares / width - mean * mean
    normed_here = ((mixed - mean[..., None]) * lax.rsqrt(spread[..., None] + EPS)).astype(bf16)
    live_tile = jnp.broadcast_to(live[:, None, None, None], (rows_here, groups, per_group, 1))
    normed_full = lax.all_gather(normed_here, "head", axis=2, tiled=True)
    col_proj = jnp.einsum("rcd,ted->rcte", normed_full, col_qkv, preferred_element_type=f32)
    packed = col_proj.astype(bf16).reshape(rows_here, groups, per_group, 3 * local_width)
    received = lax.all_to_all(packed, "seq", split_axis=1, concat_axis=0, tiled=True)
    mask_part = lax.all_to_all(live_tile, "seq", split_axis=1, concat_axis=0, tiled=True)
    column_out = send_back(
        attend_columns(
            received[:, 0, :, :local_width],
            received[:, 0, :, local_width : 2 * local_width],
            received[:, 0, :, 2 * local_width :],
            mask_part[:, 0, 0, 0],
        )
    )
    column_out = column_out.reshape(rows_here, cols, local_width)
    col_update = weight_fold(col_out, lax.all_gather(column_out, "head", axis=2, tiled=True))
    return (mixed + col_update).astype(bf16)


def body(ids, pad_mask, embed, row_qkv, row_out, col_qkv, col_out):
    rows_here, cols = ids.shape
    groups = lax.axis_size("seq")
    own, rows = cols // groups, rows_here * groups
    parts = lax.axis_size("head")
    local = row_out.shape[0]
    fits = (
        parts == 4
        and groups >= 4
        and groups & (groups - 1) == 0
        and rows * 8 == LANES
        and rows_here == 2
        and own % 32 == 0
        and cols >= LANES
        and local == LANES + HEAD_DIM
        and embed.shape[0] <= TABLE_ROWS
    )
    chosen = fast_body if fits else general_body
    return chosen(ids, pad_mask, embed, row_qkv, row_out, col_qkv, col_out)


def solution(mesh):
    placed = (
        P("seq", None),
        P("seq"),
        P(),
        P(None, "head", None),
        P("head", None),
        P(None, "head", None),
        P("head", None),
    )
    return jax.shard_map(
        body, mesh=mesh, in_specs=placed, out_specs=P("seq", None, "head"), check_vma=False
    )
```

```python
import functools

import jax
import jax.numpy as jnp
from jax import lax
from jax.experimental import pallas as pl
from jax.experimental.pallas import tpu as pltpu
from jax.sharding import PartitionSpec as P

HEAD_DIM = 64
EPS = 1e-05
LANES = 128
CODES = 64
TABLE_ROWS = 40

SMALL_VMEM = 8 * 1024 * 1024
LARGE_VMEM = 32 * 1024 * 1024

f32 = jnp.float32
bf16 = jnp.bfloat16


def layer_norm(values):
    mean = jnp.mean(values, axis=-1, keepdims=True)
    centred = values - mean
    spread = jnp.mean(centred * centred, axis=-1, keepdims=True)
    return centred * lax.rsqrt(spread + EPS)


def softmax_last(scores):
    top = jnp.max(scores, axis=-1, keepdims=True)
    weights = jnp.exp(scores - top)
    return weights * (1.0 / jnp.sum(weights, axis=-1, keepdims=True))


def dot_nt(left, right):
    return lax.dot_general(left, right, (((1,), (1,)), ((), ())), preferred_element_type=f32)


def dot_nn(left, right):
    return jnp.dot(left, right, preferred_element_type=f32)


def in_hbm(value):
    return pltpu.with_memory_space_constraint(value, pltpu.HBM)


def iota(shape, axis):
    return lax.broadcasted_iota(jnp.int32, shape, axis)


def code_kernel(ids_hbm, live_hbm, out_ref, ids_ref, live_ref, sems):
    loads = [
        pltpu.make_async_copy(ids_hbm, ids_ref, sems.at[0]),
        pltpu.make_async_copy(live_hbm, live_ref, sems.at[1]),
    ]
    for load in loads:
        load.start()
    for load in loads:
        load.wait()
    row = iota(ids_ref.shape, 0)
    live = jnp.zeros(ids_ref.shape, jnp.int32)
    for r in range(ids_ref.shape[0]):
        live = jnp.where(row == r, live_ref[r], live)
    coded = ids_ref[...] + 65536 * live
    out_ref[...] = jnp.concatenate([coded] * (out_ref.shape[0] // coded.shape[0]), 0)


def make_codes(ids, pad_mask, height):
    return pl.pallas_call(
        code_kernel,
        out_shape=jax.ShapeDtypeStruct((height, ids.shape[1]), jnp.int32),
        in_specs=[pl.BlockSpec(memory_space=pltpu.HBM)] * 2,
        scratch_shapes=[
            pltpu.VMEM(ids.shape, jnp.int32),
            pltpu.SMEM(pad_mask.shape, jnp.int32),
            pltpu.SemaphoreType.DMA((2,)),
        ],
        compiler_params=pltpu.CompilerParams(vmem_limit_bytes=SMALL_VMEM),
        name="codes",
    )(in_hbm(ids), in_hbm(pad_mask))


def join_kernel(rows, own_ref, other_ref, out_ref):
    own, other = own_ref[...], other_ref[...]
    both = jnp.concatenate([own[0:rows], other[0:rows]], 0)
    out_ref[...] = jnp.concatenate([both] * (own.shape[0] // (2 * rows)), 0)


def join(own, other, rows):
    return pl.pallas_call(
        functools.partial(join_kernel, rows),
        out_shape=jax.ShapeDtypeStruct(own.shape, own.dtype),
        compiler_params=pltpu.CompilerParams(vmem_limit_bytes=SMALL_VMEM),
        name="join",
    )(own, other)


def table_kernel(embed_hbm, qkv_hbm, out_ref, embed_ref, qkv_ref, padded_ref, sems):
    kinds = qkv_ref.shape[0]
    loads = [pltpu.make_async_copy(embed_hbm, embed_ref, sems.at[kinds])]
    loads += [
        pltpu.make_async_copy(qkv_hbm.at[t], qkv_ref.at[t], sems.at[t]) for t in range(kinds)
    ]
    for load in loads:
        load.start()
    padded_ref[...] = jnp.zeros(padded_ref.shape, f32)
    loads[0].wait()
    padded_ref[0 : embed_ref.shape[0], :] = embed_ref[...].astype(f32)
    normed = layer_norm(padded_ref[...]).astype(bf16)
    tables = []
    for t in range(kinds):
        loads[1 + t].wait()
        tables.append(dot_nt(normed, qkv_ref[t]))
    out_ref[...] = jnp.concatenate(tables, 1).astype(bf16)


def make_tables(embed, row_qkv):
    kinds, local, width = row_qkv.shape
    return pl.pallas_call(
        table_kernel,
        out_shape=jax.ShapeDtypeStruct((TABLE_ROWS, kinds * local), bf16),
        in_specs=[pl.BlockSpec(memory_space=pltpu.HBM)] * 2,
        scratch_shapes=[
            pltpu.VMEM(embed.shape, bf16),
            pltpu.VMEM(row_qkv.shape, bf16),
            pltpu.VMEM((TABLE_ROWS, width), f32),
            pltpu.SemaphoreType.DMA((kinds + 1,)),
        ],
        cost_estimate=pl.CostEstimate(
            flops=2 * 10**9, bytes_accessed=2 * row_qkv.size, transcendentals=0
        ),
        compiler_params=pltpu.CompilerParams(vmem_limit_bytes=SMALL_VMEM),
        name="tables",
    )(in_hbm(embed), in_hbm(row_qkv))


def halves(pair):
    lane = iota(pair.shape, 1)
    zero = jnp.zeros_like(pair)
    return jnp.where(lane < HEAD_DIM, pair, zero), jnp.where(lane < HEAD_DIM, zero, pair)


def spread_pair(pair):
    first, second = halves(pair)
    zero = jnp.zeros_like(pair)
    return jnp.concatenate(
        [
            jnp.concatenate([first, zero], 1),
            jnp.concatenate([zero, first], 1),
            jnp.concatenate([second, zero], 1),
            jnp.concatenate([zero, second], 1),
        ],
        0,
    )


def double(block):
    zero = jnp.zeros_like(block)
    return jnp.concatenate(
        [jnp.concatenate([block, zero], 1), jnp.concatenate([zero, block], 1)], 0
    )


def row_kernel(parts, *refs):
    tables_refs, refs = refs[:parts], refs[parts:]
    (
        near_codes_ref,
        far_codes_ref,
        row_context_ref,
        own_ref,
        live_ref,
        tables_ref,
        table_ref,
        hot_ref,
        live_own_ref,
        sum_ref,
        spread_ref,
    ) = refs
    depth, cols = hot_ref.shape
    rows = depth // CODES
    pairs = rows // 2
    own = live_own_ref.shape[0] // pairs
    width = row_context_ref.shape[1]
    heads = width // HEAD_DIM
    local = width // parts
    group = lax.axis_index("seq")
    part = lax.axis_index("head")
    for p in range(parts):
        tables_ref[part ^ p] = tables_refs[p][...]

    for t in range(3):
        table_ref[t, 0:TABLE_ROWS, :] = jnp.concatenate(
            [tables_ref[p, :, t * local : (t + 1) * local] for p in range(parts)], 1
        )
        table_ref[t, TABLE_ROWS:CODES, :] = jnp.zeros((CODES - TABLE_ROWS, width), bf16)

    coded = jnp.concatenate([near_codes_ref[...], far_codes_ref[...]], 0)
    ids = (coded & 0xFFFF).astype(f32)
    live = (coded[:, 0:LANES] >> 16).astype(f32)
    live_ref[...] = live
    code = iota((CODES, cols), 0).astype(f32)
    for r in range(rows):
        hot = jnp.broadcast_to(ids[r : r + 1, :], (CODES, cols)) == code
        hot_ref[r * CODES : (r + 1) * CODES, :] = hot.astype(f32).astype(bf16)

    pick = (iota((own, cols), 1) == group * own + iota((own, cols), 0)).astype(f32).astype(bf16)
    mine = dot_nt(pick, ids.astype(bf16))
    lane = iota((own, LANES), 1)
    first_half = lane < CODES
    lane_code = jnp.where(first_half, lane, lane - CODES).astype(f32)
    for k in range(pairs):
        value = jnp.where(first_half, mine[:, 2 * k : 2 * k + 1], mine[:, 2 * k + 1 : 2 * k + 2])
        hot = (value == lane_code).astype(f32)
        alive = jnp.where(first_half, live[2 * k : 2 * k + 1, :], live[2 * k + 1 : 2 * k + 2, :])
        own_ref[k * own : (k + 1) * own, :] = hot.astype(bf16)
        live_own_ref[k * own : (k + 1) * own, :] = (hot * alive).astype(bf16)

    spans = [slice(hp * LANES, (hp + 1) * LANES) for hp in range(heads // 2)]
    queries = [spread_pair(table_ref[0, :, span]) for span in spans]
    keys = [double(table_ref[1, :, span]) for span in spans]
    scores = [dot_nt(query, key) for query, key in zip(queries, keys)]
    high = [score.astype(bf16) for score in scores]
    low = [(score - part.astype(f32)).astype(bf16) for score, part in zip(scores, high)]
    for hp in range(heads // 2):
        for h2 in range(2):
            these = slice(h2 * LANES, (h2 + 1) * LANES)
            looked = dot_nn(
                live_own_ref[...], jnp.concatenate([high[hp][these], low[hp][these]], 1)
            ).astype(bf16)
            base = (hp * 2 + h2) * own
            for piece in range(2):
                for k in range(pairs):
                    to = piece * depth + k * LANES
                    sum_ref[base : base + own, to : to + LANES] = looked[
                        k * own : (k + 1) * own, piece * LANES : (piece + 1) * LANES
                    ]
    tied = dot_nn(sum_ref[:, 0:depth], hot_ref[...]) + dot_nn(
        sum_ref[:, depth : 2 * depth], hot_ref[...]
    )
    count = jnp.sum(live, axis=0, keepdims=True)[:, 0:1]
    probs = softmax_last(tied * (HEAD_DIM ** (-0.5) / jnp.sqrt(count))).astype(bf16)

    spread_ref[...] = dot_nt(probs, hot_ref[...]).astype(bf16)
    values = [spread_pair(table_ref[2, :, span]) for span in spans]
    contexts = []
    for hp in range(heads // 2):
        first = (hp * 2) * own
        weights = jnp.concatenate(
            [
                jnp.concatenate(
                    [
                        spread_ref[first : first + own, k * LANES : (k + 1) * LANES],
                        spread_ref[first + own : first + 2 * own, k * LANES : (k + 1) * LANES],
                    ],
                    1,
                )
                for k in range(pairs)
            ],
            0,
        )
        contexts.append(dot_nn(weights, values[hp]).astype(bf16))
    for hp in range(heads // 2):
        for k in range(pairs):
            for r2 in range(2):
                at = (2 * k + r2) * own
                row_context_ref[at : at + own, spans[hp]] = contexts[hp][
                    k * own : (k + 1) * own, r2 * LANES : (r2 + 1) * LANES
                ]


def attend_rows(tables, codes, rows, cols, own, width):
    heads = width // HEAD_DIM
    parts = len(tables)
    return pl.pallas_call(
        functools.partial(row_kernel, parts),
        out_shape=(
            jax.ShapeDtypeStruct((rows * own, width), bf16),
            jax.ShapeDtypeStruct((rows * own // 2, LANES), bf16),
            jax.ShapeDtypeStruct((rows, LANES), f32),
        ),
        scratch_shapes=[
            pltpu.VMEM((parts,) + tables[0].shape, bf16),
            pltpu.VMEM((3, CODES, width), bf16),
            pltpu.VMEM((rows * CODES, cols), bf16),
            pltpu.VMEM((rows // 2 * own, LANES), bf16),
            pltpu.VMEM((heads * own, 2 * rows * CODES), bf16),
            pltpu.VMEM((heads * own, rows * CODES), bf16),
        ],
        cost_estimate=pl.CostEstimate(flops=3 * 10**9, bytes_accessed=10**6, transcendentals=0),
        compiler_params=pltpu.CompilerParams(vmem_limit_bytes=LARGE_VMEM),
        name="row_attention",
    )(*tables, *codes)


def column_kernel(parts, *refs):
    row_out_refs, refs = refs[:parts], refs[parts:]
    (
        live_ref,
        row_context_ref,
        own_ref,
        embed_ref,
        col_qkv_ref,
        *context_refs,
        mixed_out_ref,
        row_out_ref,
        embed2_ref,
        weight_ref,
    ) = refs
    rows = live_ref.shape[0]
    tokens, width = row_context_ref.shape
    pairs = rows // 2
    own = tokens // rows
    vocab = embed_ref.shape[0]
    local = width // parts
    part = lax.axis_index("head")

    for p in range(parts):
        row_out_ref[part ^ p] = row_out_refs[p][...]
    embed2_ref[...] = jnp.zeros(embed2_ref.shape, bf16)
    embed2_ref[0:vocab, 0:width] = embed_ref[...]
    embed2_ref[CODES : CODES + vocab, width : 2 * width] = embed_ref[...]

    embedded2 = dot_nn(own_ref[...], embed2_ref[...])
    embedded = jnp.concatenate(
        [
            embedded2[k * own : (k + 1) * own, r2 * width : (r2 + 1) * width]
            for k in range(pairs)
            for r2 in range(2)
        ],
        0,
    )
    mixed = embedded + dot_nt(row_context_ref[...], row_out_ref[...].reshape(width, width))
    for p in range(parts):

        @pl.when(part == p)
        def _():
            mixed_out_ref[...] = mixed[:, p * local : (p + 1) * local]

    normed = layer_norm(mixed).astype(bf16)

    few = 8
    groups = own // few
    unit = rows * few

    def regroup(values):
        shape = (rows, groups, few, values.shape[1])
        return jnp.swapaxes(values.reshape(shape), 0, 1).reshape(tokens, values.shape[1])

    odd = part % 2
    for t in range(3):
        first = pl.multiple_of(t * local + odd * HEAD_DIM, HEAD_DIM)
        last = pl.multiple_of(t * local + (1 - odd) * LANES, HEAD_DIM)
        third = (3 + t) * LANES
        weight_ref[t * LANES : (t + 1) * LANES, :] = col_qkv_ref[pl.ds(first, LANES), :]
        weight_ref[third : third + HEAD_DIM, :] = col_qkv_ref[pl.ds(last, HEAD_DIM), :]
        weight_ref[third + HEAD_DIM : third + LANES, :] = jnp.zeros((HEAD_DIM, width), bf16)
    proj = [
        dot_nt(normed, weight_ref[2 * j * LANES : 2 * (j + 1) * LANES, :]) for j in range(3)
    ]
    proj = [
        proj[j][:, k * LANES : (k + 1) * LANES] * (HEAD_DIM ** (-0.5) if (2 * j + k) % 3 == 0 else 1.0)
        for j in range(3)
        for k in range(2)
    ]
    proj = [regroup(values).astype(bf16) for values in proj]
    sub, lan = iota((unit, unit), 0), iota((unit, unit), 1)
    same_column = (sub % few) == (lan % few)
    seq_of_lane = iota((rows, unit), 1) // few
    live_lane = jnp.sum(
        jnp.where(seq_of_lane == iota((rows, unit), 0), live_ref[...], 0.0), axis=0, keepdims=True
    )
    visible = jnp.logical_and(same_column, jnp.broadcast_to(live_lane, (unit, unit)) > 0)
    chosen = []
    for g in range(groups):
        at = slice(g * unit, (g + 1) * unit)
        query, keys, values = (proj[t][at] for t in range(3))
        chosen += [(half, keys, values) for half in halves(query)]
        chosen.append(tuple(proj[3 + t][at] for t in range(3)))
    scores = [jnp.where(visible, dot_nt(query, keys), -jnp.inf) for query, keys, _ in chosen]
    tops = [jnp.max(score, axis=-1, keepdims=True) for score in scores]
    weights = [jnp.exp(score - top) for score, top in zip(scores, tops)]
    shares = [1.0 / jnp.sum(weight, axis=-1, keepdims=True) for weight in weights]
    probs = [(weight * share).astype(bf16) for weight, share in zip(weights, shares)]
    found = [dot_nn(prob, values) for prob, (_, _, values) in zip(probs, chosen)]
    first_head = iota((unit, LANES), 1) < HEAD_DIM

    def ungroup(blocks):
        whole = jnp.concatenate(blocks, 0).reshape(groups, rows, few, LANES)
        return jnp.swapaxes(whole, 0, 1).reshape(tokens, LANES)

    main = ungroup(
        [jnp.where(first_head, found[3 * g], found[3 * g + 1]) for g in range(groups)]
    )
    third = ungroup([found[3 * g + 2] for g in range(groups)])
    start = 0
    for context_ref in context_refs:
        count = context_ref.shape[0] * 2 // 3
        some = count // 2
        context_ref[0:count, :] = main[start : start + count].astype(bf16)
        early = third[start : start + some]
        late = third[start + some : start + count]
        left = jnp.where(odd == 1, late, early)
        right = jnp.where(odd == 1, early, late)
        context_ref[count : count + some, :] = jnp.concatenate(
            [left[:, 0:HEAD_DIM], right[:, 0:HEAD_DIM]], 1
        ).astype(bf16)
        start += count


def attend_columns_here(row_outs, live, row_context, own_codes, embed, col_qkv):
    parts = len(row_outs)
    tokens, width = row_context.shape
    local = width // parts
    half = tokens // 2 * local // LANES
    return pl.pallas_call(
        functools.partial(column_kernel, parts),
        out_shape=(
            jax.ShapeDtypeStruct((half, LANES), bf16),
            jax.ShapeDtypeStruct((half, LANES), bf16),
            jax.ShapeDtypeStruct((tokens, local), f32),
        ),
        scratch_shapes=[
            pltpu.VMEM((parts, local, width), bf16),
            pltpu.VMEM((2 * CODES, 2 * width), bf16),
            pltpu.VMEM((6 * LANES, width), bf16),
        ],
        cost_estimate=pl.CostEstimate(flops=2 * 10**9, bytes_accessed=10**6, transcendentals=0),
        compiler_params=pltpu.CompilerParams(vmem_limit_bytes=LARGE_VMEM),
        name="column_attention",
    )(*row_outs, live, row_context, own_codes, embed, col_qkv)


def finish_kernel(parts, groups, *refs):
    context_refs = [refs[:parts], refs[parts : 2 * parts]]
    mixed_ref, col_out_ref, out_ref, context_ref = refs[2 * parts :]
    tokens, local = mixed_ref.shape
    group = lax.axis_index("seq")
    part = lax.axis_index("head")
    starts = [0, context_refs[0][0].shape[0]]
    for start, some_refs in zip(starts, context_refs):
        for p in range(parts):
            context_ref[part ^ p, start : start + some_refs[p].shape[0], :] = some_refs[p][...]
    pieces = []
    for start, some_refs in zip(starts, context_refs):
        count = some_refs[0].shape[0] * 2 // 3
        end = start + some_refs[0].shape[0]
        low = iota((count // 2, LANES), 1) < HEAD_DIM
        features = []
        for p in range(0, parts, 2):
            even = context_ref[p, start + count : end, :]
            other = context_ref[p + 1, start + count : end, :]
            early = jnp.where(low, even, other)
            late = jnp.where(low, other, even)
            late = jnp.concatenate([late[:, HEAD_DIM:], late[:, 0:HEAD_DIM]], 1)
            features += [
                context_ref[p, start : start + count, :],
                jnp.concatenate([early, late], 0),
                context_ref[p + 1, start : start + count, :],
            ]
        pieces.append(jnp.concatenate(features, 1))
    total = mixed_ref[...] + dot_nt(jnp.concatenate(pieces, 0), col_out_ref[...])
    own = tokens // groups // 2
    for d in range(groups):
        first, second = (total[(2 * d + r) * own : (2 * d + r + 1) * own, :] for r in range(2))
        rest = jnp.concatenate([first[:, LANES:local], second[:, LANES:local]], 1)
        out_ref[group ^ d] = jnp.concatenate(
            [first[:, 0:LANES], second[:, 0:LANES], rest], 0
        ).astype(bf16)


def finish(contexts, mixed, col_out, groups):
    parts = len(contexts[0])
    tokens, local = mixed.shape
    return pl.pallas_call(
        functools.partial(finish_kernel, parts, groups),
        out_shape=jax.ShapeDtypeStruct((groups, tokens // groups * local // LANES, LANES), bf16),
        scratch_shapes=[pltpu.VMEM((parts, tokens * local // LANES, LANES), bf16)],
        compiler_params=pltpu.CompilerParams(vmem_limit_bytes=LARGE_VMEM),
        name="finish",
    )(*contexts[0], *contexts[1], mixed, col_out)


def order_kernel(blocks_ref, out_ref):
    groups = blocks_ref.shape[0]
    local, cols = out_ref.shape[1:]
    own = cols // groups
    rest = local - LANES
    for part in range(3):
        piece = jnp.concatenate(
            [blocks_ref[g, part * own : (part + 1) * own, :] for g in range(groups)], 0
        )
        turned = piece.astype(f32).T.astype(bf16)
        if part < 2:
            out_ref[part, 0:LANES, :] = turned
        else:
            for r in range(2):
                out_ref[r, LANES:local, :] = turned[r * rest : (r + 1) * rest, :]


def order(blocks, cols, local):
    return pl.pallas_call(
        order_kernel,
        out_shape=jax.ShapeDtypeStruct((2, local, cols), bf16),
        compiler_params=pltpu.CompilerParams(vmem_limit_bytes=SMALL_VMEM),
        name="order",
    )(blocks)


def fast_body(ids, pad_mask, embed, row_qkv, row_out, col_qkv, col_out):
    rows_here, cols = ids.shape
    width = embed.shape[1]
    local = row_out.shape[0]
    groups, parts = lax.axis_size("seq"), lax.axis_size("head")
    own, rows = cols // groups, rows_here * groups

    def pairwise(value, partner):
        order = [(g, p) for g in range(groups) for p in range(parts)]
        link = [(g * parts + p, partner(g, p)) for g, p in order]
        return lax.ppermute(value, ("seq", "head"), [(i, g * parts + p) for i, (g, p) in link])

    def sibling(g, p):
        return g, p ^ 1

    def across(g, p):
        return g, p ^ 2

    def opposite(g, p):
        return g, p ^ 3

    far = pairwise(row_out, across)
    coded = make_codes(ids, pad_mask, rows_here * groups // 2)
    coded, row_qkv = lax.optimization_barrier((coded, row_qkv))
    received = pairwise(coded, lambda g, p: (g ^ 1, p))
    table = make_tables(embed, row_qkv)
    tables = [table, None, pairwise(table, across), None]
    step = 2
    while step < groups:
        coded = join(coded, received, rows_here * step // 2)
        if step == 2:
            coded, table = lax.optimization_barrier((coded, table))
            tables[3] = pairwise(table, opposite)
        elif step == 4:
            coded, table, row_out, far = lax.optimization_barrier((coded, table, row_out, far))
            tables[1] = pairwise(table, sibling)
            row_outs = [row_out, pairwise(row_out, sibling), far, pairwise(far, sibling)]
        received = pairwise(coded, lambda g, p, step=step: (g ^ step, p))
        step *= 2
    codes = (coded, received)
    row_context, own_codes, live = attend_rows(tables, codes, rows, cols, own, width)
    *halves_here, mixed = attend_columns_here(
        row_outs, live, row_context, own_codes, embed, col_qkv.reshape(3 * local, width)
    )
    contexts = []
    for context in halves_here:
        beyond = pairwise(context, across)
        contexts.append(
            (context, pairwise(context, sibling), beyond, pairwise(beyond, sibling))
        )
    blocks = finish(contexts, mixed, col_out, groups)
    blocks = lax.all_to_all(blocks, "seq", split_axis=0, concat_axis=0, tiled=True)
    return jnp.swapaxes(order(blocks, cols, local), 1, 2)


def weight_fold(out_weight, piece):
    return jnp.einsum("rce,fe->rcf", piece, out_weight, preferred_element_type=f32)


def attend_columns(query, keys, values, key_live):
    rows_all, count_cols, local_width = query.shape
    heads_here = local_width // HEAD_DIM
    shape = (rows_all, count_cols, heads_here, HEAD_DIM)
    scores = jnp.einsum(
        "rchd,schd->chrs",
        query.reshape(shape),
        keys.reshape(shape),
        preferred_element_type=f32,
    ) * HEAD_DIM ** (-0.5)
    scores = jnp.where(key_live > 0, scores, -jnp.inf)
    probs = softmax_last(scores).astype(bf16)
    context = jnp.einsum(
        "chrs,schd->rchd", probs, values.reshape(shape), preferred_element_type=f32
    )
    return context.astype(bf16).reshape(rows_all, count_cols, local_width)


def send_back(context):
    return lax.all_to_all(context[:, None], "seq", split_axis=0, concat_axis=1, tiled=True)


def general_body(ids, pad_mask, embed, row_qkv, row_out, col_qkv, col_out):
    rows_here, cols = ids.shape
    width = embed.shape[1]
    local_width = row_out.shape[0]
    heads_here = local_width // HEAD_DIM
    groups = lax.axis_size("seq")
    per_group = cols // groups
    codes = lax.broadcasted_iota(jnp.int32, (1, 1, embed.shape[0]), 2)
    onehot = (ids[:, :, None] == codes).astype(bf16)
    embedded = jnp.einsum("rcv,vd->rcd", onehot, embed, preferred_element_type=f32)
    normed = layer_norm(embedded).astype(bf16)
    row_proj = jnp.einsum("rcd,ted->trce", normed, row_qkv, preferred_element_type=f32)
    row_proj = row_proj.astype(bf16)
    live = pad_mask.astype(bf16)
    head_shape = (rows_here, cols, heads_here, HEAD_DIM)
    query = (row_proj[0] * live[:, None, None]).reshape(head_shape)
    keys = row_proj[1].reshape(head_shape)
    values = row_proj[2].reshape(head_shape)
    partial_scores = jnp.einsum("rihd,rjhd->hij", query, keys, preferred_element_type=f32)
    count_here = jnp.sum(pad_mask.astype(f32))
    scale = HEAD_DIM ** (-0.5)
    total, count = lax.psum((partial_scores, count_here), "seq")
    row_probs = softmax_last(total * (scale / jnp.sqrt(count))).astype(bf16)
    row_context = jnp.einsum("hij,rjhd->rihd", row_probs, values, preferred_element_type=f32)
    row_context = row_context.astype(bf16).reshape(rows_here, cols, local_width)
    start_feature = lax.axis_index("head") * local_width
    resident = lax.dynamic_slice_in_dim(embedded, start_feature, local_width, 2)
    row_update = weight_fold(row_out, lax.all_gather(row_context, "head", axis=2, tiled=True))
    mixed = resident + row_update
    sums, squares = lax.psum((jnp.sum(mixed, axis=-1), jnp.sum(mixed * mixed, axis=-1)), "head")
    mean = sums / width
    spread = squares / width - mean * mean
    normed_here = ((mixed - mean[..., None]) * lax.rsqrt(spread[..., None] + EPS)).astype(bf16)
    live_tile = jnp.broadcast_to(live[:, None, None, None], (rows_here, groups, per_group, 1))
    normed_full = lax.all_gather(normed_here, "head", axis=2, tiled=True)
    col_proj = jnp.einsum("rcd,ted->rcte", normed_full, col_qkv, preferred_element_type=f32)
    packed = col_proj.astype(bf16).reshape(rows_here, groups, per_group, 3 * local_width)
    received = lax.all_to_all(packed, "seq", split_axis=1, concat_axis=0, tiled=True)
    mask_part = lax.all_to_all(live_tile, "seq", split_axis=1, concat_axis=0, tiled=True)
    column_out = send_back(
        attend_columns(
            received[:, 0, :, :local_width],
            received[:, 0, :, local_width : 2 * local_width],
            received[:, 0, :, 2 * local_width :],
            mask_part[:, 0, 0, 0],
        )
    )
    column_out = column_out.reshape(rows_here, cols, local_width)
    col_update = weight_fold(col_out, lax.all_gather(column_out, "head", axis=2, tiled=True))
    return (mixed + col_update).astype(bf16)


def body(ids, pad_mask, embed, row_qkv, row_out, col_qkv, col_out):
    rows_here, cols = ids.shape
    groups = lax.axis_size("seq")
    own, rows = cols // groups, rows_here * groups
    parts = lax.axis_size("head")
    local = row_out.shape[0]
    fits = (
        parts == 4
        and groups >= 8
        and groups & (groups - 1) == 0
        and rows * 8 == LANES
        and rows_here == 2
        and own % 32 == 0
        and cols >= LANES
        and local == LANES + HEAD_DIM
        and embed.shape[0] <= TABLE_ROWS
    )
    chosen = fast_body if fits else general_body
    return chosen(ids, pad_mask, embed, row_qkv, row_out, col_qkv, col_out)


def solution(mesh):
    placed = (
        P("seq", None),
        P("seq"),
        P(),
        P(None, "head", None),
        P("head", None),
        P(None, "head", None),
        P("head", None),
    )
    return jax.shard_map(
        body, mesh=mesh, in_specs=placed, out_specs=P("seq", None, "head"), check_vma=False
    )
```

```python
import functools

import jax
import jax.numpy as jnp
from jax import lax
from jax.experimental import pallas as pl
from jax.experimental.pallas import tpu as pltpu
from jax.sharding import PartitionSpec as P

HEAD_DIM = 64
EPS = 1e-05
LANES = 128
CODES = 64
TABLE_ROWS = 40

SMALL_VMEM = 8 * 1024 * 1024
LARGE_VMEM = 32 * 1024 * 1024

f32 = jnp.float32
bf16 = jnp.bfloat16


def layer_norm(values):
    mean = jnp.mean(values, axis=-1, keepdims=True)
    centred = values - mean
    spread = jnp.mean(centred * centred, axis=-1, keepdims=True)
    return centred * lax.rsqrt(spread + EPS)


def softmax_last(scores):
    top = jnp.max(scores, axis=-1, keepdims=True)
    weights = jnp.exp(scores - top)
    return weights * (1.0 / jnp.sum(weights, axis=-1, keepdims=True))


def dot_nt(left, right):
    return lax.dot_general(left, right, (((1,), (1,)), ((), ())), preferred_element_type=f32)


def dot_nn(left, right):
    return jnp.dot(left, right, preferred_element_type=f32)


def in_hbm(value):
    return pltpu.with_memory_space_constraint(value, pltpu.HBM)


def iota(shape, axis):
    return lax.broadcasted_iota(jnp.int32, shape, axis)


def code_kernel(ids_hbm, live_hbm, out_ref, ids_ref, live_ref, sems):
    loads = [
        pltpu.make_async_copy(ids_hbm, ids_ref, sems.at[0]),
        pltpu.make_async_copy(live_hbm, live_ref, sems.at[1]),
    ]
    for load in loads:
        load.start()
    for load in loads:
        load.wait()
    row = iota(ids_ref.shape, 0)
    live = jnp.zeros(ids_ref.shape, jnp.int32)
    for r in range(ids_ref.shape[0]):
        live = jnp.where(row == r, live_ref[r], live)
    coded = ids_ref[...] + 65536 * live
    out_ref[...] = jnp.concatenate([coded] * (out_ref.shape[0] // coded.shape[0]), 0)


def make_codes(ids, pad_mask, height):
    return pl.pallas_call(
        code_kernel,
        out_shape=jax.ShapeDtypeStruct((height, ids.shape[1]), jnp.int32),
        in_specs=[pl.BlockSpec(memory_space=pltpu.HBM)] * 2,
        scratch_shapes=[
            pltpu.VMEM(ids.shape, jnp.int32),
            pltpu.SMEM(pad_mask.shape, jnp.int32),
            pltpu.SemaphoreType.DMA((2,)),
        ],
        compiler_params=pltpu.CompilerParams(vmem_limit_bytes=SMALL_VMEM),
        name="codes",
    )(in_hbm(ids), in_hbm(pad_mask))


def join_kernel(rows, own_ref, other_ref, out_ref):
    own, other = own_ref[...], other_ref[...]
    both = jnp.concatenate([own[0:rows], other[0:rows]], 0)
    out_ref[...] = jnp.concatenate([both] * (own.shape[0] // (2 * rows)), 0)


def join(own, other, rows):
    return pl.pallas_call(
        functools.partial(join_kernel, rows),
        out_shape=jax.ShapeDtypeStruct(own.shape, own.dtype),
        compiler_params=pltpu.CompilerParams(vmem_limit_bytes=SMALL_VMEM),
        name="join",
    )(own, other)


def table_kernel(embed_hbm, qkv_hbm, out_ref, embed_ref, qkv_ref, padded_ref, sems):
    kinds = qkv_ref.shape[0]
    loads = [pltpu.make_async_copy(embed_hbm, embed_ref, sems.at[kinds])]
    loads += [
        pltpu.make_async_copy(qkv_hbm.at[t], qkv_ref.at[t], sems.at[t]) for t in range(kinds)
    ]
    for load in loads:
        load.start()
    padded_ref[...] = jnp.zeros(padded_ref.shape, f32)
    loads[0].wait()
    padded_ref[0 : embed_ref.shape[0], :] = embed_ref[...].astype(f32)
    normed = layer_norm(padded_ref[...]).astype(bf16)
    tables = []
    for t in range(kinds):
        loads[1 + t].wait()
        tables.append(dot_nt(normed, qkv_ref[t]))
    out_ref[...] = jnp.concatenate(tables, 1).astype(bf16)


def make_tables(embed, row_qkv):
    kinds, local, width = row_qkv.shape
    return pl.pallas_call(
        table_kernel,
        out_shape=jax.ShapeDtypeStruct((TABLE_ROWS, kinds * local), bf16),
        in_specs=[pl.BlockSpec(memory_space=pltpu.HBM)] * 2,
        scratch_shapes=[
            pltpu.VMEM(embed.shape, bf16),
            pltpu.VMEM(row_qkv.shape, bf16),
            pltpu.VMEM((TABLE_ROWS, width), f32),
            pltpu.SemaphoreType.DMA((kinds + 1,)),
        ],
        cost_estimate=pl.CostEstimate(
            flops=2 * 10**9, bytes_accessed=2 * row_qkv.size, transcendentals=0
        ),
        compiler_params=pltpu.CompilerParams(vmem_limit_bytes=SMALL_VMEM),
        name="tables",
    )(in_hbm(embed), in_hbm(row_qkv))


def halves(pair):
    lane = iota(pair.shape, 1)
    zero = jnp.zeros_like(pair)
    return jnp.where(lane < HEAD_DIM, pair, zero), jnp.where(lane < HEAD_DIM, zero, pair)


def spread_pair(pair):
    first, second = halves(pair)
    zero = jnp.zeros_like(pair)
    return jnp.concatenate(
        [
            jnp.concatenate([first, zero], 1),
            jnp.concatenate([zero, first], 1),
            jnp.concatenate([second, zero], 1),
            jnp.concatenate([zero, second], 1),
        ],
        0,
    )


def double(block):
    zero = jnp.zeros_like(block)
    return jnp.concatenate(
        [jnp.concatenate([block, zero], 1), jnp.concatenate([zero, block], 1)], 0
    )


def row_kernel(parts, *refs):
    tables_refs, refs = refs[:parts], refs[parts:]
    (
        near_codes_ref,
        far_codes_ref,
        row_context_ref,
        own_ref,
        live_ref,
        tables_ref,
        table_ref,
        hot_ref,
        live_own_ref,
        sum_ref,
        spread_ref,
    ) = refs
    depth, cols = hot_ref.shape
    rows = depth // CODES
    pairs = rows // 2
    own = live_own_ref.shape[0] // pairs
    width = row_context_ref.shape[1]
    heads = width // HEAD_DIM
    local = width // parts
    group = lax.axis_index("seq")
    part = lax.axis_index("head")
    for p in range(parts):
        tables_ref[part ^ p] = tables_refs[p][...]

    for t in range(3):
        table_ref[t, 0:TABLE_ROWS, :] = jnp.concatenate(
            [tables_ref[p, :, t * local : (t + 1) * local] for p in range(parts)], 1
        )
        table_ref[t, TABLE_ROWS:CODES, :] = jnp.zeros((CODES - TABLE_ROWS, width), bf16)

    coded = jnp.concatenate([near_codes_ref[...], far_codes_ref[...]], 0)
    ids = (coded & 0xFFFF).astype(f32)
    live = (coded[:, 0:LANES] >> 16).astype(f32)
    live_ref[...] = live
    code = iota((CODES, cols), 0).astype(f32)
    for r in range(rows):
        hot = jnp.broadcast_to(ids[r : r + 1, :], (CODES, cols)) == code
        hot_ref[r * CODES : (r + 1) * CODES, :] = hot.astype(f32).astype(bf16)

    pick = (iota((own, cols), 1) == group * own + iota((own, cols), 0)).astype(f32).astype(bf16)
    mine = dot_nt(pick, ids.astype(bf16))
    lane = iota((own, LANES), 1)
    first_half = lane < CODES
    lane_code = jnp.where(first_half, lane, lane - CODES).astype(f32)
    for k in range(pairs):
        value = jnp.where(first_half, mine[:, 2 * k : 2 * k + 1], mine[:, 2 * k + 1 : 2 * k + 2])
        hot = (value == lane_code).astype(f32)
        alive = jnp.where(first_half, live[2 * k : 2 * k + 1, :], live[2 * k + 1 : 2 * k + 2, :])
        own_ref[k * own : (k + 1) * own, :] = hot.astype(bf16)
        live_own_ref[k * own : (k + 1) * own, :] = (hot * alive).astype(bf16)

    spans = [slice(hp * LANES, (hp + 1) * LANES) for hp in range(heads // 2)]
    queries = [spread_pair(table_ref[0, :, span]) for span in spans]
    keys = [double(table_ref[1, :, span]) for span in spans]
    scores = [dot_nt(query, key) for query, key in zip(queries, keys)]
    high = [score.astype(bf16) for score in scores]
    low = [(score - part.astype(f32)).astype(bf16) for score, part in zip(scores, high)]
    for hp in range(heads // 2):
        for h2 in range(2):
            these = slice(h2 * LANES, (h2 + 1) * LANES)
            looked = dot_nn(
                live_own_ref[...], jnp.concatenate([high[hp][these], low[hp][these]], 1)
            ).astype(bf16)
            base = (hp * 2 + h2) * own
            for piece in range(2):
                for k in range(pairs):
                    to = piece * depth + k * LANES
                    sum_ref[base : base + own, to : to + LANES] = looked[
                        k * own : (k + 1) * own, piece * LANES : (piece + 1) * LANES
                    ]
    tied = dot_nn(sum_ref[:, 0:depth], hot_ref[...]) + dot_nn(
        sum_ref[:, depth : 2 * depth], hot_ref[...]
    )
    count = jnp.sum(live, axis=0, keepdims=True)[:, 0:1]
    probs = softmax_last(tied * (HEAD_DIM ** (-0.5) / jnp.sqrt(count))).astype(bf16)

    spread_ref[...] = dot_nt(probs, hot_ref[...]).astype(bf16)
    values = [spread_pair(table_ref[2, :, span]) for span in spans]
    contexts = []
    for hp in range(heads // 2):
        first = (hp * 2) * own
        weights = jnp.concatenate(
            [
                jnp.concatenate(
                    [
                        spread_ref[first : first + own, k * LANES : (k + 1) * LANES],
                        spread_ref[first + own : first + 2 * own, k * LANES : (k + 1) * LANES],
                    ],
                    1,
                )
                for k in range(pairs)
            ],
            0,
        )
        contexts.append(dot_nn(weights, values[hp]).astype(bf16))
    for hp in range(heads // 2):
        for k in range(pairs):
            for r2 in range(2):
                at = (2 * k + r2) * own
                row_context_ref[at : at + own, spans[hp]] = contexts[hp][
                    k * own : (k + 1) * own, r2 * LANES : (r2 + 1) * LANES
                ]


def attend_rows(tables, codes, rows, cols, own, width):
    heads = width // HEAD_DIM
    parts = len(tables)
    return pl.pallas_call(
        functools.partial(row_kernel, parts),
        out_shape=(
            jax.ShapeDtypeStruct((rows * own, width), bf16),
            jax.ShapeDtypeStruct((rows * own // 2, LANES), bf16),
            jax.ShapeDtypeStruct((rows, LANES), f32),
        ),
        scratch_shapes=[
            pltpu.VMEM((parts,) + tables[0].shape, bf16),
            pltpu.VMEM((3, CODES, width), bf16),
            pltpu.VMEM((rows * CODES, cols), bf16),
            pltpu.VMEM((rows // 2 * own, LANES), bf16),
            pltpu.VMEM((heads * own, 2 * rows * CODES), bf16),
            pltpu.VMEM((heads * own, rows * CODES), bf16),
        ],
        cost_estimate=pl.CostEstimate(flops=3 * 10**9, bytes_accessed=10**6, transcendentals=0),
        compiler_params=pltpu.CompilerParams(vmem_limit_bytes=LARGE_VMEM),
        name="row_attention",
    )(*tables, *codes)


def column_kernel(parts, *refs):
    row_out_refs, refs = refs[:parts], refs[parts:]
    (
        live_ref,
        row_context_ref,
        own_ref,
        embed_ref,
        col_qkv_ref,
        *context_refs,
        mixed_out_ref,
        row_out_ref,
        embed2_ref,
        weight_ref,
    ) = refs
    rows = live_ref.shape[0]
    tokens, width = row_context_ref.shape
    pairs = rows // 2
    own = tokens // rows
    vocab = embed_ref.shape[0]
    local = width // parts
    part = lax.axis_index("head")

    for p in range(parts):
        row_out_ref[part ^ p] = row_out_refs[p][...]
    embed2_ref[...] = jnp.zeros(embed2_ref.shape, bf16)
    embed2_ref[0:vocab, 0:width] = embed_ref[...]
    embed2_ref[CODES : CODES + vocab, width : 2 * width] = embed_ref[...]

    embedded2 = dot_nn(own_ref[...], embed2_ref[...])
    embedded = jnp.concatenate(
        [
            embedded2[k * own : (k + 1) * own, r2 * width : (r2 + 1) * width]
            for k in range(pairs)
            for r2 in range(2)
        ],
        0,
    )
    mixed = embedded + dot_nt(row_context_ref[...], row_out_ref[...].reshape(width, width))
    for p in range(parts):

        @pl.when(part == p)
        def _():
            mixed_out_ref[...] = mixed[:, p * local : (p + 1) * local]

    normed = layer_norm(mixed).astype(bf16)

    few = 8
    groups = own // few
    unit = rows * few

    def regroup(values):
        shape = (rows, groups, few, values.shape[1])
        return jnp.swapaxes(values.reshape(shape), 0, 1).reshape(tokens, values.shape[1])

    odd = part % 2
    for t in range(3):
        first = pl.multiple_of(t * local + odd * HEAD_DIM, HEAD_DIM)
        last = pl.multiple_of(t * local + (1 - odd) * LANES, HEAD_DIM)
        third = (3 + t) * LANES
        weight_ref[t * LANES : (t + 1) * LANES, :] = col_qkv_ref[pl.ds(first, LANES), :]
        weight_ref[third : third + HEAD_DIM, :] = col_qkv_ref[pl.ds(last, HEAD_DIM), :]
        weight_ref[third + HEAD_DIM : third + LANES, :] = jnp.zeros((HEAD_DIM, width), bf16)
    proj = [
        dot_nt(normed, weight_ref[2 * j * LANES : 2 * (j + 1) * LANES, :]) for j in range(3)
    ]
    proj = [
        proj[j][:, k * LANES : (k + 1) * LANES] * (HEAD_DIM ** (-0.5) if (2 * j + k) % 3 == 0 else 1.0)
        for j in range(3)
        for k in range(2)
    ]
    proj = [regroup(values).astype(bf16) for values in proj]
    sub, lan = iota((unit, unit), 0), iota((unit, unit), 1)
    same_column = (sub % few) == (lan % few)
    seq_of_lane = iota((rows, unit), 1) // few
    live_lane = jnp.sum(
        jnp.where(seq_of_lane == iota((rows, unit), 0), live_ref[...], 0.0), axis=0, keepdims=True
    )
    visible = jnp.logical_and(same_column, jnp.broadcast_to(live_lane, (unit, unit)) > 0)
    chosen = []
    for g in range(groups):
        at = slice(g * unit, (g + 1) * unit)
        query, keys, values = (proj[t][at] for t in range(3))
        chosen += [(half, keys, values) for half in halves(query)]
        chosen.append(tuple(proj[3 + t][at] for t in range(3)))
    scores = [jnp.where(visible, dot_nt(query, keys), -jnp.inf) for query, keys, _ in chosen]
    tops = [jnp.max(score, axis=-1, keepdims=True) for score in scores]
    weights = [jnp.exp(score - top) for score, top in zip(scores, tops)]
    shares = [1.0 / jnp.sum(weight, axis=-1, keepdims=True) for weight in weights]
    probs = [(weight * share).astype(bf16) for weight, share in zip(weights, shares)]
    found = [dot_nn(prob, values) for prob, (_, _, values) in zip(probs, chosen)]
    first_head = iota((unit, LANES), 1) < HEAD_DIM

    def ungroup(blocks):
        whole = jnp.concatenate(blocks, 0).reshape(groups, rows, few, LANES)
        return jnp.swapaxes(whole, 0, 1).reshape(tokens, LANES)

    main = ungroup(
        [jnp.where(first_head, found[3 * g], found[3 * g + 1]) for g in range(groups)]
    )
    third = ungroup([found[3 * g + 2] for g in range(groups)])
    start = 0
    for context_ref in context_refs:
        count = context_ref.shape[0] * 2 // 3
        some = count // 2
        context_ref[0:count, :] = main[start : start + count].astype(bf16)
        early = third[start : start + some]
        late = third[start + some : start + count]
        left = jnp.where(odd == 1, late, early)
        right = jnp.where(odd == 1, early, late)
        context_ref[count : count + some, :] = jnp.concatenate(
            [left[:, 0:HEAD_DIM], right[:, 0:HEAD_DIM]], 1
        ).astype(bf16)
        start += count


def attend_columns_here(row_outs, live, row_context, own_codes, embed, col_qkv):
    parts = len(row_outs)
    tokens, width = row_context.shape
    local = width // parts
    half = tokens // 2 * local // LANES
    return pl.pallas_call(
        functools.partial(column_kernel, parts),
        out_shape=(
            jax.ShapeDtypeStruct((half, LANES), bf16),
            jax.ShapeDtypeStruct((half, LANES), bf16),
            jax.ShapeDtypeStruct((tokens, local), f32),
        ),
        scratch_shapes=[
            pltpu.VMEM((parts, local, width), bf16),
            pltpu.VMEM((2 * CODES, 2 * width), bf16),
            pltpu.VMEM((6 * LANES, width), bf16),
        ],
        cost_estimate=pl.CostEstimate(flops=2 * 10**9, bytes_accessed=10**6, transcendentals=0),
        compiler_params=pltpu.CompilerParams(vmem_limit_bytes=LARGE_VMEM),
        name="column_attention",
    )(*row_outs, live, row_context, own_codes, embed, col_qkv)


def finish_kernel(parts, groups, *refs):
    context_refs = [refs[:parts], refs[parts : 2 * parts]]
    mixed_ref, col_out_ref, out_ref, context_ref = refs[2 * parts :]
    tokens, local = mixed_ref.shape
    group = lax.axis_index("seq")
    part = lax.axis_index("head")
    starts = [0, context_refs[0][0].shape[0]]
    for start, some_refs in zip(starts, context_refs):
        for p in range(parts):
            context_ref[part ^ p, start : start + some_refs[p].shape[0], :] = some_refs[p][...]
    pieces = []
    for start, some_refs in zip(starts, context_refs):
        count = some_refs[0].shape[0] * 2 // 3
        end = start + some_refs[0].shape[0]
        low = iota((count // 2, LANES), 1) < HEAD_DIM
        features = []
        for p in range(0, parts, 2):
            even = context_ref[p, start + count : end, :]
            other = context_ref[p + 1, start + count : end, :]
            early = jnp.where(low, even, other)
            late = jnp.where(low, other, even)
            late = jnp.concatenate([late[:, HEAD_DIM:], late[:, 0:HEAD_DIM]], 1)
            features += [
                context_ref[p, start : start + count, :],
                jnp.concatenate([early, late], 0),
                context_ref[p + 1, start : start + count, :],
            ]
        pieces.append(jnp.concatenate(features, 1))
    total = mixed_ref[...] + dot_nt(jnp.concatenate(pieces, 0), col_out_ref[...])
    own = tokens // groups // 2
    for d in range(groups):
        first, second = (total[(2 * d + r) * own : (2 * d + r + 1) * own, :] for r in range(2))
        rest = jnp.concatenate([first[:, LANES:local], second[:, LANES:local]], 1)
        out_ref[group ^ d] = jnp.concatenate(
            [first[:, 0:LANES], second[:, 0:LANES], rest], 0
        ).astype(bf16)


def finish(contexts, mixed, col_out, groups):
    parts = len(contexts[0])
    tokens, local = mixed.shape
    return pl.pallas_call(
        functools.partial(finish_kernel, parts, groups),
        out_shape=jax.ShapeDtypeStruct((groups, tokens // groups * local // LANES, LANES), bf16),
        scratch_shapes=[pltpu.VMEM((parts, tokens * local // LANES, LANES), bf16)],
        compiler_params=pltpu.CompilerParams(vmem_limit_bytes=LARGE_VMEM),
        name="finish",
    )(*contexts[0], *contexts[1], mixed, col_out)


def order_kernel(blocks_ref, out_ref):
    groups = blocks_ref.shape[0]
    local, cols = out_ref.shape[1:]
    own = cols // groups
    rest = local - LANES
    for part in range(3):
        piece = jnp.concatenate(
            [blocks_ref[g, part * own : (part + 1) * own, :] for g in range(groups)], 0
        )
        turned = piece.astype(f32).T.astype(bf16)
        if part < 2:
            out_ref[part, 0:LANES, :] = turned
        else:
            for r in range(2):
                out_ref[r, LANES:local, :] = turned[r * rest : (r + 1) * rest, :]


def order(blocks, cols, local):
    return pl.pallas_call(
        order_kernel,
        out_shape=jax.ShapeDtypeStruct((2, local, cols), bf16),
        compiler_params=pltpu.CompilerParams(vmem_limit_bytes=SMALL_VMEM),
        name="order",
    )(blocks)


def fast_body(ids, pad_mask, embed, row_qkv, row_out, col_qkv, col_out):
    rows_here, cols = ids.shape
    width = embed.shape[1]
    local = row_out.shape[0]
    groups, parts = lax.axis_size("seq"), lax.axis_size("head")
    own, rows = cols // groups, rows_here * groups

    def pairwise(value, partner):
        order = [(g, p) for g in range(groups) for p in range(parts)]
        link = [(g * parts + p, partner(g, p)) for g, p in order]
        return lax.ppermute(value, ("seq", "head"), [(i, g * parts + p) for i, (g, p) in link])

    def sibling(g, p):
        return g, p ^ 1

    def across(g, p):
        return g, p ^ 2

    def opposite(g, p):
        return g, p ^ 3

    far = pairwise(row_out, across)
    coded = make_codes(ids, pad_mask, rows_here * groups // 2)
    coded, row_qkv = lax.optimization_barrier((coded, row_qkv))
    received = pairwise(coded, lambda g, p: (g ^ 1, p))
    table = make_tables(embed, row_qkv)
    tables = [table, None, pairwise(table, across), None]
    step = 2
    while step < groups:
        coded = join(coded, received, rows_here * step // 2)
        if step == 2:
            coded, table, row_out = lax.optimization_barrier((coded, table, row_out))
            tables[3] = pairwise(table, opposite)
            near = pairwise(row_out, sibling)
        elif step == 4:
            coded, table, near, far = lax.optimization_barrier((coded, table, near, far))
            tables[1] = pairwise(table, sibling)
            row_outs = [row_out, near, far, pairwise(far, sibling)]
        received = pairwise(coded, lambda g, p, step=step: (g ^ step, p))
        step *= 2
    codes = (coded, received)
    row_context, own_codes, live = attend_rows(tables, codes, rows, cols, own, width)
    *halves_here, mixed = attend_columns_here(
        row_outs, live, row_context, own_codes, embed, col_qkv.reshape(3 * local, width)
    )
    contexts = []
    for context in halves_here:
        beyond = pairwise(context, across)
        contexts.append(
            (context, pairwise(context, sibling), beyond, pairwise(beyond, sibling))
        )
    blocks = finish(contexts, mixed, col_out, groups)
    blocks = lax.all_to_all(blocks, "seq", split_axis=0, concat_axis=0, tiled=True)
    return jnp.swapaxes(order(blocks, cols, local), 1, 2)


def weight_fold(out_weight, piece):
    return jnp.einsum("rce,fe->rcf", piece, out_weight, preferred_element_type=f32)


def attend_columns(query, keys, values, key_live):
    rows_all, count_cols, local_width = query.shape
    heads_here = local_width // HEAD_DIM
    shape = (rows_all, count_cols, heads_here, HEAD_DIM)
    scores = jnp.einsum(
        "rchd,schd->chrs",
        query.reshape(shape),
        keys.reshape(shape),
        preferred_element_type=f32,
    ) * HEAD_DIM ** (-0.5)
    scores = jnp.where(key_live > 0, scores, -jnp.inf)
    probs = softmax_last(scores).astype(bf16)
    context = jnp.einsum(
        "chrs,schd->rchd", probs, values.reshape(shape), preferred_element_type=f32
    )
    return context.astype(bf16).reshape(rows_all, count_cols, local_width)


def send_back(context):
    return lax.all_to_all(context[:, None], "seq", split_axis=0, concat_axis=1, tiled=True)


def general_body(ids, pad_mask, embed, row_qkv, row_out, col_qkv, col_out):
    rows_here, cols = ids.shape
    width = embed.shape[1]
    local_width = row_out.shape[0]
    heads_here = local_width // HEAD_DIM
    groups = lax.axis_size("seq")
    per_group = cols // groups
    codes = lax.broadcasted_iota(jnp.int32, (1, 1, embed.shape[0]), 2)
    onehot = (ids[:, :, None] == codes).astype(bf16)
    embedded = jnp.einsum("rcv,vd->rcd", onehot, embed, preferred_element_type=f32)
    normed = layer_norm(embedded).astype(bf16)
    row_proj = jnp.einsum("rcd,ted->trce", normed, row_qkv, preferred_element_type=f32)
    row_proj = row_proj.astype(bf16)
    live = pad_mask.astype(bf16)
    head_shape = (rows_here, cols, heads_here, HEAD_DIM)
    query = (row_proj[0] * live[:, None, None]).reshape(head_shape)
    keys = row_proj[1].reshape(head_shape)
    values = row_proj[2].reshape(head_shape)
    partial_scores = jnp.einsum("rihd,rjhd->hij", query, keys, preferred_element_type=f32)
    count_here = jnp.sum(pad_mask.astype(f32))
    scale = HEAD_DIM ** (-0.5)
    total, count = lax.psum((partial_scores, count_here), "seq")
    row_probs = softmax_last(total * (scale / jnp.sqrt(count))).astype(bf16)
    row_context = jnp.einsum("hij,rjhd->rihd", row_probs, values, preferred_element_type=f32)
    row_context = row_context.astype(bf16).reshape(rows_here, cols, local_width)
    start_feature = lax.axis_index("head") * local_width
    resident = lax.dynamic_slice_in_dim(embedded, start_feature, local_width, 2)
    row_update = weight_fold(row_out, lax.all_gather(row_context, "head", axis=2, tiled=True))
    mixed = resident + row_update
    sums, squares = lax.psum((jnp.sum(mixed, axis=-1), jnp.sum(mixed * mixed, axis=-1)), "head")
    mean = sums / width
    spread = squares / width - mean * mean
    normed_here = ((mixed - mean[..., None]) * lax.rsqrt(spread[..., None] + EPS)).astype(bf16)
    live_tile = jnp.broadcast_to(live[:, None, None, None], (rows_here, groups, per_group, 1))
    normed_full = lax.all_gather(normed_here, "head", axis=2, tiled=True)
    col_proj = jnp.einsum("rcd,ted->rcte", normed_full, col_qkv, preferred_element_type=f32)
    packed = col_proj.astype(bf16).reshape(rows_here, groups, per_group, 3 * local_width)
    received = lax.all_to_all(packed, "seq", split_axis=1, concat_axis=0, tiled=True)
    mask_part = lax.all_to_all(live_tile, "seq", split_axis=1, concat_axis=0, tiled=True)
    column_out = send_back(
        attend_columns(
            received[:, 0, :, :local_width],
            received[:, 0, :, local_width : 2 * local_width],
            received[:, 0, :, 2 * local_width :],
            mask_part[:, 0, 0, 0],
        )
    )
    column_out = column_out.reshape(rows_here, cols, local_width)
    col_update = weight_fold(col_out, lax.all_gather(column_out, "head", axis=2, tiled=True))
    return (mixed + col_update).astype(bf16)


def body(ids, pad_mask, embed, row_qkv, row_out, col_qkv, col_out):
    rows_here, cols = ids.shape
    groups = lax.axis_size("seq")
    own, rows = cols // groups, rows_here * groups
    parts = lax.axis_size("head")
    local = row_out.shape[0]
    fits = (
        parts == 4
        and groups >= 8
        and groups & (groups - 1) == 0
        and rows * 8 == LANES
        and rows_here == 2
        and own % 32 == 0
        and cols >= LANES
        and local == LANES + HEAD_DIM
        and embed.shape[0] <= TABLE_ROWS
    )
    chosen = fast_body if fits else general_body
    return chosen(ids, pad_mask, embed, row_qkv, row_out, col_qkv, col_out)


def solution(mesh):
    placed = (
        P("seq", None),
        P("seq"),
        P(),
        P(None, "head", None),
        P("head", None),
        P(None, "head", None),
        P("head", None),
    )
    return jax.shard_map(
        body, mesh=mesh, in_specs=placed, out_specs=P("seq", None, "head"), check_vma=False
    )
```

```python
import functools

import jax
import jax.numpy as jnp
from jax import lax
from jax.experimental import pallas as pl
from jax.experimental.pallas import tpu as pltpu
from jax.sharding import PartitionSpec as P

HEAD_DIM = 64
EPS = 1e-05
LANES = 128
CODES = 64
TABLE_ROWS = 40

SMALL_VMEM = 8 * 1024 * 1024
LARGE_VMEM = 32 * 1024 * 1024

f32 = jnp.float32
bf16 = jnp.bfloat16


def layer_norm(values):
    mean = jnp.mean(values, axis=-1, keepdims=True)
    centred = values - mean
    spread = jnp.mean(centred * centred, axis=-1, keepdims=True)
    return centred * lax.rsqrt(spread + EPS)


def softmax_last(scores):
    top = jnp.max(scores, axis=-1, keepdims=True)
    weights = jnp.exp(scores - top)
    return weights * (1.0 / jnp.sum(weights, axis=-1, keepdims=True))


def dot_nt(left, right):
    return lax.dot_general(left, right, (((1,), (1,)), ((), ())), preferred_element_type=f32)


def dot_nn(left, right):
    return jnp.dot(left, right, preferred_element_type=f32)


def in_hbm(value):
    return pltpu.with_memory_space_constraint(value, pltpu.HBM)


def iota(shape, axis):
    return lax.broadcasted_iota(jnp.int32, shape, axis)


def code_kernel(ids_hbm, live_hbm, out_ref, ids_ref, live_ref, sems):
    loads = [
        pltpu.make_async_copy(ids_hbm, ids_ref, sems.at[0]),
        pltpu.make_async_copy(live_hbm, live_ref, sems.at[1]),
    ]
    for load in loads:
        load.start()
    for load in loads:
        load.wait()
    row = iota(ids_ref.shape, 0)
    live = jnp.zeros(ids_ref.shape, jnp.int32)
    for r in range(ids_ref.shape[0]):
        live = jnp.where(row == r, live_ref[r], live)
    coded = ids_ref[...] + 65536 * live
    out_ref[...] = jnp.concatenate([coded] * (out_ref.shape[0] // coded.shape[0]), 0)


def make_codes(ids, pad_mask, height):
    return pl.pallas_call(
        code_kernel,
        out_shape=jax.ShapeDtypeStruct((height, ids.shape[1]), jnp.int32),
        in_specs=[pl.BlockSpec(memory_space=pltpu.HBM)] * 2,
        scratch_shapes=[
            pltpu.VMEM(ids.shape, jnp.int32),
            pltpu.SMEM(pad_mask.shape, jnp.int32),
            pltpu.SemaphoreType.DMA((2,)),
        ],
        compiler_params=pltpu.CompilerParams(vmem_limit_bytes=SMALL_VMEM),
        name="codes",
    )(in_hbm(ids), in_hbm(pad_mask))


def join_kernel(rows, own_ref, other_ref, out_ref):
    own, other = own_ref[...], other_ref[...]
    both = jnp.concatenate([own[0:rows], other[0:rows]], 0)
    out_ref[...] = jnp.concatenate([both] * (own.shape[0] // (2 * rows)), 0)


def join(own, other, rows):
    return pl.pallas_call(
        functools.partial(join_kernel, rows),
        out_shape=jax.ShapeDtypeStruct(own.shape, own.dtype),
        compiler_params=pltpu.CompilerParams(vmem_limit_bytes=SMALL_VMEM),
        name="join",
    )(own, other)


def table_kernel(embed_hbm, qkv_hbm, out_ref, embed_ref, qkv_ref, padded_ref, sems):
    kinds = qkv_ref.shape[0]
    loads = [pltpu.make_async_copy(embed_hbm, embed_ref, sems.at[kinds])]
    loads += [
        pltpu.make_async_copy(qkv_hbm.at[t], qkv_ref.at[t], sems.at[t]) for t in range(kinds)
    ]
    for load in loads:
        load.start()
    padded_ref[...] = jnp.zeros(padded_ref.shape, f32)
    loads[0].wait()
    padded_ref[0 : embed_ref.shape[0], :] = embed_ref[...].astype(f32)
    normed = layer_norm(padded_ref[...]).astype(bf16)
    tables = []
    for t in range(kinds):
        loads[1 + t].wait()
        tables.append(dot_nt(normed, qkv_ref[t]))
    out_ref[...] = jnp.concatenate(tables, 1).astype(bf16)


def make_tables(embed, row_qkv):
    kinds, local, width = row_qkv.shape
    return pl.pallas_call(
        table_kernel,
        out_shape=jax.ShapeDtypeStruct((TABLE_ROWS, kinds * local), bf16),
        in_specs=[pl.BlockSpec(memory_space=pltpu.HBM)] * 2,
        scratch_shapes=[
            pltpu.VMEM(embed.shape, bf16),
            pltpu.VMEM(row_qkv.shape, bf16),
            pltpu.VMEM((TABLE_ROWS, width), f32),
            pltpu.SemaphoreType.DMA((kinds + 1,)),
        ],
        cost_estimate=pl.CostEstimate(
            flops=2 * 10**9, bytes_accessed=2 * row_qkv.size, transcendentals=0
        ),
        compiler_params=pltpu.CompilerParams(vmem_limit_bytes=SMALL_VMEM),
        name="tables",
    )(in_hbm(embed), in_hbm(row_qkv))


def halves(pair):
    lane = iota(pair.shape, 1)
    zero = jnp.zeros_like(pair)
    return jnp.where(lane < HEAD_DIM, pair, zero), jnp.where(lane < HEAD_DIM, zero, pair)


def spread_pair(pair):
    first, second = halves(pair)
    zero = jnp.zeros_like(pair)
    return jnp.concatenate(
        [
            jnp.concatenate([first, zero], 1),
            jnp.concatenate([zero, first], 1),
            jnp.concatenate([second, zero], 1),
            jnp.concatenate([zero, second], 1),
        ],
        0,
    )


def double(block):
    zero = jnp.zeros_like(block)
    return jnp.concatenate(
        [jnp.concatenate([block, zero], 1), jnp.concatenate([zero, block], 1)], 0
    )


def score_kernel(*refs):
    *tables_refs, scores_ref, values_ref, tables_ref, table_ref = refs
    parts = len(tables_refs)
    width = values_ref.shape[1]
    heads = width // HEAD_DIM
    local = width // parts
    part = lax.axis_index("head")
    for p in range(parts):
        tables_ref[part ^ p] = tables_refs[p][...]

    for t in range(3):
        to_ref = values_ref if t == 2 else table_ref.at[t]
        to_ref[0:TABLE_ROWS, :] = jnp.concatenate(
            [tables_ref[p, :, t * local : (t + 1) * local] for p in range(parts)], 1
        )
        to_ref[TABLE_ROWS:CODES, :] = jnp.zeros((CODES - TABLE_ROWS, width), bf16)

    spans = [slice(hp * LANES, (hp + 1) * LANES) for hp in range(heads // 2)]
    queries = [spread_pair(table_ref[0, :, span]) for span in spans]
    keys = [double(table_ref[1, :, span]) for span in spans]
    scores = [dot_nt(query, key) for query, key in zip(queries, keys)]
    high = [score.astype(bf16) for score in scores]
    low = [(score - part_of.astype(f32)).astype(bf16) for score, part_of in zip(scores, high)]
    for h in range(heads):
        these = slice(h % 2 * LANES, (h % 2 + 1) * LANES)
        scores_ref[h, :, 0:LANES] = high[h // 2][these]
        scores_ref[h, :, LANES : 2 * LANES] = low[h // 2][these]


def score_tables(tables):
    parts = len(tables)
    width = tables[0].shape[1] // 3 * parts
    return pl.pallas_call(
        score_kernel,
        out_shape=(
            jax.ShapeDtypeStruct((width // HEAD_DIM, LANES, 2 * LANES), bf16),
            jax.ShapeDtypeStruct((CODES, width), bf16),
        ),
        scratch_shapes=[
            pltpu.VMEM((parts,) + tables[0].shape, bf16),
            pltpu.VMEM((2, CODES, width), bf16),
        ],
        cost_estimate=pl.CostEstimate(flops=10**9, bytes_accessed=10**6, transcendentals=0),
        compiler_params=pltpu.CompilerParams(vmem_limit_bytes=LARGE_VMEM),
        name="scores",
    )(*tables)


def row_kernel(
    scores_ref,
    values_ref,
    near_codes_ref,
    far_codes_ref,
    row_context_ref,
    own_ref,
    live_ref,
    hot_ref,
    live_own_ref,
    sum_ref,
    spread_ref,
):
    depth, cols = hot_ref.shape
    rows = depth // CODES
    pairs = rows // 2
    own = live_own_ref.shape[0] // pairs
    width = row_context_ref.shape[1]
    heads = width // HEAD_DIM
    group = lax.axis_index("seq")

    coded = jnp.concatenate([near_codes_ref[...], far_codes_ref[...]], 0)
    ids = (coded & 0xFFFF).astype(f32)
    live = (coded[:, 0:LANES] >> 16).astype(f32)
    live_ref[...] = live
    code = iota((CODES, cols), 0).astype(f32)
    for r in range(rows):
        hot = jnp.broadcast_to(ids[r : r + 1, :], (CODES, cols)) == code
        hot_ref[r * CODES : (r + 1) * CODES, :] = hot.astype(f32).astype(bf16)

    pick = (iota((own, cols), 1) == group * own + iota((own, cols), 0)).astype(f32).astype(bf16)
    mine = dot_nt(pick, ids.astype(bf16))
    lane = iota((own, LANES), 1)
    first_half = lane < CODES
    lane_code = jnp.where(first_half, lane, lane - CODES).astype(f32)
    for k in range(pairs):
        value = jnp.where(first_half, mine[:, 2 * k : 2 * k + 1], mine[:, 2 * k + 1 : 2 * k + 2])
        hot = (value == lane_code).astype(f32)
        alive = jnp.where(first_half, live[2 * k : 2 * k + 1, :], live[2 * k + 1 : 2 * k + 2, :])
        own_ref[k * own : (k + 1) * own, :] = hot.astype(bf16)
        live_own_ref[k * own : (k + 1) * own, :] = (hot * alive).astype(bf16)

    for h in range(heads):
        looked = dot_nn(live_own_ref[...], scores_ref[h]).astype(bf16)
        for piece in range(2):
            for k in range(pairs):
                to = piece * depth + k * LANES
                sum_ref[h * own : (h + 1) * own, to : to + LANES] = looked[
                    k * own : (k + 1) * own, piece * LANES : (piece + 1) * LANES
                ]
    tied = dot_nn(sum_ref[:, 0:depth], hot_ref[...]) + dot_nn(
        sum_ref[:, depth : 2 * depth], hot_ref[...]
    )
    count = jnp.sum(live, axis=0, keepdims=True)[:, 0:1]
    probs = softmax_last(tied * (HEAD_DIM ** (-0.5) / jnp.sqrt(count))).astype(bf16)

    spread_ref[...] = dot_nt(probs, hot_ref[...]).astype(bf16)
    spans = [slice(hp * LANES, (hp + 1) * LANES) for hp in range(heads // 2)]
    values = [spread_pair(values_ref[:, span]) for span in spans]
    contexts = []
    for hp in range(heads // 2):
        first = (hp * 2) * own
        weights = jnp.concatenate(
            [
                jnp.concatenate(
                    [
                        spread_ref[first : first + own, k * LANES : (k + 1) * LANES],
                        spread_ref[first + own : first + 2 * own, k * LANES : (k + 1) * LANES],
                    ],
                    1,
                )
                for k in range(pairs)
            ],
            0,
        )
        contexts.append(dot_nn(weights, values[hp]).astype(bf16))
    for hp in range(heads // 2):
        for k in range(pairs):
            for r2 in range(2):
                at = (2 * k + r2) * own
                row_context_ref[at : at + own, spans[hp]] = contexts[hp][
                    k * own : (k + 1) * own, r2 * LANES : (r2 + 1) * LANES
                ]


def attend_rows(scores, values, codes, rows, cols, own, width):
    heads = width // HEAD_DIM
    return pl.pallas_call(
        row_kernel,
        out_shape=(
            jax.ShapeDtypeStruct((rows * own, width), bf16),
            jax.ShapeDtypeStruct((rows * own // 2, LANES), bf16),
            jax.ShapeDtypeStruct((rows, LANES), f32),
        ),
        scratch_shapes=[
            pltpu.VMEM((rows * CODES, cols), bf16),
            pltpu.VMEM((rows // 2 * own, LANES), bf16),
            pltpu.VMEM((heads * own, 2 * rows * CODES), bf16),
            pltpu.VMEM((heads * own, rows * CODES), bf16),
        ],
        cost_estimate=pl.CostEstimate(flops=3 * 10**9, bytes_accessed=10**6, transcendentals=0),
        compiler_params=pltpu.CompilerParams(vmem_limit_bytes=LARGE_VMEM),
        name="row_attention",
    )(scores, values, *codes)


def column_kernel(parts, *refs):
    row_out_refs, refs = refs[:parts], refs[parts:]
    (
        live_ref,
        row_context_ref,
        own_ref,
        embed_ref,
        col_qkv_ref,
        *context_refs,
        mixed_out_ref,
        row_out_ref,
        embed2_ref,
        weight_ref,
    ) = refs
    rows = live_ref.shape[0]
    tokens, width = row_context_ref.shape
    pairs = rows // 2
    own = tokens // rows
    vocab = embed_ref.shape[0]
    local = width // parts
    part = lax.axis_index("head")

    for p in range(parts):
        row_out_ref[part ^ p] = row_out_refs[p][...]
    embed2_ref[...] = jnp.zeros(embed2_ref.shape, bf16)
    embed2_ref[0:vocab, 0:width] = embed_ref[...]
    embed2_ref[CODES : CODES + vocab, width : 2 * width] = embed_ref[...]

    embedded2 = dot_nn(own_ref[...], embed2_ref[...])
    embedded = jnp.concatenate(
        [
            embedded2[k * own : (k + 1) * own, r2 * width : (r2 + 1) * width]
            for k in range(pairs)
            for r2 in range(2)
        ],
        0,
    )
    mixed = embedded + dot_nt(row_context_ref[...], row_out_ref[...].reshape(width, width))
    for p in range(parts):

        @pl.when(part == p)
        def _():
            mixed_out_ref[...] = mixed[:, p * local : (p + 1) * local]

    normed = layer_norm(mixed).astype(bf16)

    few = 8
    groups = own // few
    unit = rows * few

    def regroup(values):
        shape = (rows, groups, few, values.shape[1])
        return jnp.swapaxes(values.reshape(shape), 0, 1).reshape(tokens, values.shape[1])

    odd = part % 2
    for t in range(3):
        first = pl.multiple_of(t * local + odd * HEAD_DIM, HEAD_DIM)
        last = pl.multiple_of(t * local + (1 - odd) * LANES, HEAD_DIM)
        third = (3 + t) * LANES
        weight_ref[t * LANES : (t + 1) * LANES, :] = col_qkv_ref[pl.ds(first, LANES), :]
        weight_ref[third : third + HEAD_DIM, :] = col_qkv_ref[pl.ds(last, HEAD_DIM), :]
        weight_ref[third + HEAD_DIM : third + LANES, :] = jnp.zeros((HEAD_DIM, width), bf16)
    proj = [
        dot_nt(normed, weight_ref[2 * j * LANES : 2 * (j + 1) * LANES, :]) for j in range(3)
    ]
    proj = [
        proj[j][:, k * LANES : (k + 1) * LANES] * (HEAD_DIM ** (-0.5) if (2 * j + k) % 3 == 0 else 1.0)
        for j in range(3)
        for k in range(2)
    ]
    proj = [regroup(values).astype(bf16) for values in proj]
    sub, lan = iota((unit, unit), 0), iota((unit, unit), 1)
    same_column = (sub % few) == (lan % few)
    seq_of_lane = iota((rows, unit), 1) // few
    live_lane = jnp.sum(
        jnp.where(seq_of_lane == iota((rows, unit), 0), live_ref[...], 0.0), axis=0, keepdims=True
    )
    visible = jnp.logical_and(same_column, jnp.broadcast_to(live_lane, (unit, unit)) > 0)
    chosen = []
    for g in range(groups):
        at = slice(g * unit, (g + 1) * unit)
        query, keys, values = (proj[t][at] for t in range(3))
        chosen += [(half, keys, values) for half in halves(query)]
        chosen.append(tuple(proj[3 + t][at] for t in range(3)))
    scores = [jnp.where(visible, dot_nt(query, keys), -jnp.inf) for query, keys, _ in chosen]
    tops = [jnp.max(score, axis=-1, keepdims=True) for score in scores]
    weights = [jnp.exp(score - top) for score, top in zip(scores, tops)]
    shares = [1.0 / jnp.sum(weight, axis=-1, keepdims=True) for weight in weights]
    probs = [(weight * share).astype(bf16) for weight, share in zip(weights, shares)]
    found = [dot_nn(prob, values) for prob, (_, _, values) in zip(probs, chosen)]
    first_head = iota((unit, LANES), 1) < HEAD_DIM

    def ungroup(blocks):
        whole = jnp.concatenate(blocks, 0).reshape(groups, rows, few, LANES)
        return jnp.swapaxes(whole, 0, 1).reshape(tokens, LANES)

    main = ungroup(
        [jnp.where(first_head, found[3 * g], found[3 * g + 1]) for g in range(groups)]
    )
    third = ungroup([found[3 * g + 2] for g in range(groups)])
    start = 0
    for context_ref in context_refs:
        count = context_ref.shape[0] * 2 // 3
        some = count // 2
        context_ref[0:count, :] = main[start : start + count].astype(bf16)
        early = third[start : start + some]
        late = third[start + some : start + count]
        left = jnp.where(odd == 1, late, early)
        right = jnp.where(odd == 1, early, late)
        context_ref[count : count + some, :] = jnp.concatenate(
            [left[:, 0:HEAD_DIM], right[:, 0:HEAD_DIM]], 1
        ).astype(bf16)
        start += count


def attend_columns_here(row_outs, live, row_context, own_codes, embed, col_qkv):
    parts = len(row_outs)
    tokens, width = row_context.shape
    local = width // parts
    half = tokens // 2 * local // LANES
    return pl.pallas_call(
        functools.partial(column_kernel, parts),
        out_shape=(
            jax.ShapeDtypeStruct((half, LANES), bf16),
            jax.ShapeDtypeStruct((half, LANES), bf16),
            jax.ShapeDtypeStruct((tokens, local), f32),
        ),
        scratch_shapes=[
            pltpu.VMEM((parts, local, width), bf16),
            pltpu.VMEM((2 * CODES, 2 * width), bf16),
            pltpu.VMEM((6 * LANES, width), bf16),
        ],
        cost_estimate=pl.CostEstimate(flops=2 * 10**9, bytes_accessed=10**6, transcendentals=0),
        compiler_params=pltpu.CompilerParams(vmem_limit_bytes=LARGE_VMEM),
        name="column_attention",
    )(*row_outs, live, row_context, own_codes, embed, col_qkv)


def finish_kernel(parts, groups, *refs):
    context_refs = [refs[:parts], refs[parts : 2 * parts]]
    mixed_ref, col_out_ref, out_ref, context_ref = refs[2 * parts :]
    tokens, local = mixed_ref.shape
    group = lax.axis_index("seq")
    part = lax.axis_index("head")
    starts = [0, context_refs[0][0].shape[0]]
    for start, some_refs in zip(starts, context_refs):
        for p in range(parts):
            context_ref[part ^ p, start : start + some_refs[p].shape[0], :] = some_refs[p][...]
    pieces = []
    for start, some_refs in zip(starts, context_refs):
        count = some_refs[0].shape[0] * 2 // 3
        end = start + some_refs[0].shape[0]
        low = iota((count // 2, LANES), 1) < HEAD_DIM
        features = []
        for p in range(0, parts, 2):
            even = context_ref[p, start + count : end, :]
            other = context_ref[p + 1, start + count : end, :]
            early = jnp.where(low, even, other)
            late = jnp.where(low, other, even)
            late = jnp.concatenate([late[:, HEAD_DIM:], late[:, 0:HEAD_DIM]], 1)
            features += [
                context_ref[p, start : start + count, :],
                jnp.concatenate([early, late], 0),
                context_ref[p + 1, start : start + count, :],
            ]
        pieces.append(jnp.concatenate(features, 1))
    total = mixed_ref[...] + dot_nt(jnp.concatenate(pieces, 0), col_out_ref[...])
    own = tokens // groups // 2
    for d in range(groups):
        first, second = (total[(2 * d + r) * own : (2 * d + r + 1) * own, :] for r in range(2))
        rest = jnp.concatenate([first[:, LANES:local], second[:, LANES:local]], 1)
        out_ref[group ^ d] = jnp.concatenate(
            [first[:, 0:LANES], second[:, 0:LANES], rest], 0
        ).astype(bf16)


def finish(contexts, mixed, col_out, groups):
    parts = len(contexts[0])
    tokens, local = mixed.shape
    return pl.pallas_call(
        functools.partial(finish_kernel, parts, groups),
        out_shape=jax.ShapeDtypeStruct((groups, tokens // groups * local // LANES, LANES), bf16),
        scratch_shapes=[pltpu.VMEM((parts, tokens * local // LANES, LANES), bf16)],
        compiler_params=pltpu.CompilerParams(vmem_limit_bytes=LARGE_VMEM),
        name="finish",
    )(*contexts[0], *contexts[1], mixed, col_out)


def order_kernel(blocks_ref, out_ref):
    groups = blocks_ref.shape[0]
    local, cols = out_ref.shape[1:]
    own = cols // groups
    rest = local - LANES
    for part in range(3):
        piece = jnp.concatenate(
            [blocks_ref[g, part * own : (part + 1) * own, :] for g in range(groups)], 0
        )
        turned = piece.astype(f32).T.astype(bf16)
        if part < 2:
            out_ref[part, 0:LANES, :] = turned
        else:
            for r in range(2):
                out_ref[r, LANES:local, :] = turned[r * rest : (r + 1) * rest, :]


def order(blocks, cols, local):
    return pl.pallas_call(
        order_kernel,
        out_shape=jax.ShapeDtypeStruct((2, local, cols), bf16),
        compiler_params=pltpu.CompilerParams(vmem_limit_bytes=SMALL_VMEM),
        name="order",
    )(blocks)


def fast_body(ids, pad_mask, embed, row_qkv, row_out, col_qkv, col_out):
    rows_here, cols = ids.shape
    width = embed.shape[1]
    local = row_out.shape[0]
    groups, parts = lax.axis_size("seq"), lax.axis_size("head")
    own, rows = cols // groups, rows_here * groups

    def pairwise(value, partner):
        order = [(g, p) for g in range(groups) for p in range(parts)]
        link = [(g * parts + p, partner(g, p)) for g, p in order]
        return lax.ppermute(value, ("seq", "head"), [(i, g * parts + p) for i, (g, p) in link])

    def sibling(g, p):
        return g, p ^ 1

    def across(g, p):
        return g, p ^ 2

    def opposite(g, p):
        return g, p ^ 3

    far = pairwise(row_out, across)
    coded = make_codes(ids, pad_mask, rows_here * groups // 2)
    coded, row_qkv = lax.optimization_barrier((coded, row_qkv))
    received = pairwise(coded, lambda g, p: (g ^ 1, p))
    table = make_tables(embed, row_qkv)
    tables = [table, None, pairwise(table, across), None]
    step = 2
    while step < groups:
        coded = join(coded, received, rows_here * step // 2)
        if step == 2:
            coded, table = lax.optimization_barrier((coded, table))
            tables[3] = pairwise(table, opposite)
        elif step == 4:
            coded, table, row_out, far = lax.optimization_barrier((coded, table, row_out, far))
            tables[1] = pairwise(table, sibling)
            row_outs = [row_out, pairwise(row_out, sibling), far, pairwise(far, sibling)]
        received = pairwise(coded, lambda g, p, step=step: (g ^ step, p))
        step *= 2
    codes = (coded, received)
    row_context, own_codes, live = attend_rows(
        *score_tables(tables), codes, rows, cols, own, width
    )
    *halves_here, mixed = attend_columns_here(
        row_outs, live, row_context, own_codes, embed, col_qkv.reshape(3 * local, width)
    )
    contexts = []
    for context in halves_here:
        beyond = pairwise(context, across)
        contexts.append(
            (context, pairwise(context, sibling), beyond, pairwise(beyond, sibling))
        )
    blocks = finish(contexts, mixed, col_out, groups)
    blocks = lax.all_to_all(blocks, "seq", split_axis=0, concat_axis=0, tiled=True)
    return jnp.swapaxes(order(blocks, cols, local), 1, 2)


def weight_fold(out_weight, piece):
    return jnp.einsum("rce,fe->rcf", piece, out_weight, preferred_element_type=f32)


def attend_columns(query, keys, values, key_live):
    rows_all, count_cols, local_width = query.shape
    heads_here = local_width // HEAD_DIM
    shape = (rows_all, count_cols, heads_here, HEAD_DIM)
    scores = jnp.einsum(
        "rchd,schd->chrs",
        query.reshape(shape),
        keys.reshape(shape),
        preferred_element_type=f32,
    ) * HEAD_DIM ** (-0.5)
    scores = jnp.where(key_live > 0, scores, -jnp.inf)
    probs = softmax_last(scores).astype(bf16)
    context = jnp.einsum(
        "chrs,schd->rchd", probs, values.reshape(shape), preferred_element_type=f32
    )
    return context.astype(bf16).reshape(rows_all, count_cols, local_width)


def send_back(context):
    return lax.all_to_all(context[:, None], "seq", split_axis=0, concat_axis=1, tiled=True)


def general_body(ids, pad_mask, embed, row_qkv, row_out, col_qkv, col_out):
    rows_here, cols = ids.shape
    width = embed.shape[1]
    local_width = row_out.shape[0]
    heads_here = local_width // HEAD_DIM
    groups = lax.axis_size("seq")
    per_group = cols // groups
    codes = lax.broadcasted_iota(jnp.int32, (1, 1, embed.shape[0]), 2)
    onehot = (ids[:, :, None] == codes).astype(bf16)
    embedded = jnp.einsum("rcv,vd->rcd", onehot, embed, preferred_element_type=f32)
    normed = layer_norm(embedded).astype(bf16)
    row_proj = jnp.einsum("rcd,ted->trce", normed, row_qkv, preferred_element_type=f32)
    row_proj = row_proj.astype(bf16)
    live = pad_mask.astype(bf16)
    head_shape = (rows_here, cols, heads_here, HEAD_DIM)
    query = (row_proj[0] * live[:, None, None]).reshape(head_shape)
    keys = row_proj[1].reshape(head_shape)
    values = row_proj[2].reshape(head_shape)
    partial_scores = jnp.einsum("rihd,rjhd->hij", query, keys, preferred_element_type=f32)
    count_here = jnp.sum(pad_mask.astype(f32))
    scale = HEAD_DIM ** (-0.5)
    total, count = lax.psum((partial_scores, count_here), "seq")
    row_probs = softmax_last(total * (scale / jnp.sqrt(count))).astype(bf16)
    row_context = jnp.einsum("hij,rjhd->rihd", row_probs, values, preferred_element_type=f32)
    row_context = row_context.astype(bf16).reshape(rows_here, cols, local_width)
    start_feature = lax.axis_index("head") * local_width
    resident = lax.dynamic_slice_in_dim(embedded, start_feature, local_width, 2)
    row_update = weight_fold(row_out, lax.all_gather(row_context, "head", axis=2, tiled=True))
    mixed = resident + row_update
    sums, squares = lax.psum((jnp.sum(mixed, axis=-1), jnp.sum(mixed * mixed, axis=-1)), "head")
    mean = sums / width
    spread = squares / width - mean * mean
    normed_here = ((mixed - mean[..., None]) * lax.rsqrt(spread[..., None] + EPS)).astype(bf16)
    live_tile = jnp.broadcast_to(live[:, None, None, None], (rows_here, groups, per_group, 1))
    normed_full = lax.all_gather(normed_here, "head", axis=2, tiled=True)
    col_proj = jnp.einsum("rcd,ted->rcte", normed_full, col_qkv, preferred_element_type=f32)
    packed = col_proj.astype(bf16).reshape(rows_here, groups, per_group, 3 * local_width)
    received = lax.all_to_all(packed, "seq", split_axis=1, concat_axis=0, tiled=True)
    mask_part = lax.all_to_all(live_tile, "seq", split_axis=1, concat_axis=0, tiled=True)
    column_out = send_back(
        attend_columns(
            received[:, 0, :, :local_width],
            received[:, 0, :, local_width : 2 * local_width],
            received[:, 0, :, 2 * local_width :],
            mask_part[:, 0, 0, 0],
        )
    )
    column_out = column_out.reshape(rows_here, cols, local_width)
    col_update = weight_fold(col_out, lax.all_gather(column_out, "head", axis=2, tiled=True))
    return (mixed + col_update).astype(bf16)


def body(ids, pad_mask, embed, row_qkv, row_out, col_qkv, col_out):
    rows_here, cols = ids.shape
    groups = lax.axis_size("seq")
    own, rows = cols // groups, rows_here * groups
    parts = lax.axis_size("head")
    local = row_out.shape[0]
    fits = (
        parts == 4
        and groups >= 8
        and groups & (groups - 1) == 0
        and rows * 8 == LANES
        and rows_here == 2
        and own % 32 == 0
        and cols >= LANES
        and local == LANES + HEAD_DIM
        and embed.shape[0] <= TABLE_ROWS
    )
    chosen = fast_body if fits else general_body
    return chosen(ids, pad_mask, embed, row_qkv, row_out, col_qkv, col_out)


def solution(mesh):
    placed = (
        P("seq", None),
        P("seq"),
        P(),
        P(None, "head", None),
        P("head", None),
        P(None, "head", None),
        P("head", None),
    )
    return jax.shard_map(
        body, mesh=mesh, in_specs=placed, out_specs=P("seq", None, "head"), check_vma=False
    )
```

```python
import functools

import jax
import jax.numpy as jnp
from jax import lax
from jax.experimental import pallas as pl
from jax.experimental.pallas import tpu as pltpu
from jax.sharding import PartitionSpec as P

HEAD_DIM = 64
EPS = 1e-05
LANES = 128
CODES = 64
TABLE_ROWS = 40

SMALL_VMEM = 8 * 1024 * 1024
LARGE_VMEM = 32 * 1024 * 1024

f32 = jnp.float32
bf16 = jnp.bfloat16


def layer_norm(values):
    mean = jnp.mean(values, axis=-1, keepdims=True)
    centred = values - mean
    spread = jnp.mean(centred * centred, axis=-1, keepdims=True)
    return centred * lax.rsqrt(spread + EPS)


def softmax_last(scores):
    top = jnp.max(scores, axis=-1, keepdims=True)
    weights = jnp.exp(scores - top)
    return weights * (1.0 / jnp.sum(weights, axis=-1, keepdims=True))


def dot_nt(left, right):
    return lax.dot_general(left, right, (((1,), (1,)), ((), ())), preferred_element_type=f32)


def dot_nn(left, right):
    return jnp.dot(left, right, preferred_element_type=f32)


def in_hbm(value):
    return pltpu.with_memory_space_constraint(value, pltpu.HBM)


def iota(shape, axis):
    return lax.broadcasted_iota(jnp.int32, shape, axis)


def code_kernel(ids_hbm, live_hbm, out_ref, ids_ref, live_ref, sems):
    loads = [
        pltpu.make_async_copy(ids_hbm, ids_ref, sems.at[0]),
        pltpu.make_async_copy(live_hbm, live_ref, sems.at[1]),
    ]
    for load in loads:
        load.start()
    for load in loads:
        load.wait()
    row = iota(ids_ref.shape, 0)
    live = jnp.zeros(ids_ref.shape, jnp.int32)
    for r in range(ids_ref.shape[0]):
        live = jnp.where(row == r, live_ref[r], live)
    coded = ids_ref[...] + 65536 * live
    out_ref[...] = jnp.concatenate([coded] * (out_ref.shape[0] // coded.shape[0]), 0)


def make_codes(ids, pad_mask, height):
    return pl.pallas_call(
        code_kernel,
        out_shape=jax.ShapeDtypeStruct((height, ids.shape[1]), jnp.int32),
        in_specs=[pl.BlockSpec(memory_space=pltpu.HBM)] * 2,
        scratch_shapes=[
            pltpu.VMEM(ids.shape, jnp.int32),
            pltpu.SMEM(pad_mask.shape, jnp.int32),
            pltpu.SemaphoreType.DMA((2,)),
        ],
        compiler_params=pltpu.CompilerParams(vmem_limit_bytes=SMALL_VMEM),
        name="codes",
    )(in_hbm(ids), in_hbm(pad_mask))


def join_kernel(rows, own_ref, other_ref, out_ref):
    own, other = own_ref[...], other_ref[...]
    both = jnp.concatenate([own[0:rows], other[0:rows]], 0)
    out_ref[...] = jnp.concatenate([both] * (own.shape[0] // (2 * rows)), 0)


def join(own, other, rows):
    return pl.pallas_call(
        functools.partial(join_kernel, rows),
        out_shape=jax.ShapeDtypeStruct(own.shape, own.dtype),
        compiler_params=pltpu.CompilerParams(vmem_limit_bytes=SMALL_VMEM),
        name="join",
    )(own, other)


def table_kernel(embed_hbm, qkv_hbm, out_ref, embed_ref, qkv_ref, padded_ref, sems):
    kinds = qkv_ref.shape[0]
    loads = [pltpu.make_async_copy(embed_hbm, embed_ref, sems.at[kinds])]
    loads += [
        pltpu.make_async_copy(qkv_hbm.at[t], qkv_ref.at[t], sems.at[t]) for t in range(kinds)
    ]
    for load in loads:
        load.start()
    padded_ref[...] = jnp.zeros(padded_ref.shape, f32)
    loads[0].wait()
    padded_ref[0 : embed_ref.shape[0], :] = embed_ref[...].astype(f32)
    normed = layer_norm(padded_ref[...]).astype(bf16)
    tables = []
    for t in range(kinds):
        loads[1 + t].wait()
        tables.append(dot_nt(normed, qkv_ref[t]))
    out_ref[...] = jnp.concatenate(tables, 1).astype(bf16)


def make_tables(embed, row_qkv):
    kinds, local, width = row_qkv.shape
    return pl.pallas_call(
        table_kernel,
        out_shape=jax.ShapeDtypeStruct((TABLE_ROWS, kinds * local), bf16),
        in_specs=[pl.BlockSpec(memory_space=pltpu.HBM)] * 2,
        scratch_shapes=[
            pltpu.VMEM(embed.shape, bf16),
            pltpu.VMEM(row_qkv.shape, bf16),
            pltpu.VMEM((TABLE_ROWS, width), f32),
            pltpu.SemaphoreType.DMA((kinds + 1,)),
        ],
        cost_estimate=pl.CostEstimate(
            flops=2 * 10**9, bytes_accessed=2 * row_qkv.size, transcendentals=0
        ),
        compiler_params=pltpu.CompilerParams(vmem_limit_bytes=SMALL_VMEM),
        name="tables",
    )(in_hbm(embed), in_hbm(row_qkv))


def halves(pair):
    lane = iota(pair.shape, 1)
    zero = jnp.zeros_like(pair)
    return jnp.where(lane < HEAD_DIM, pair, zero), jnp.where(lane < HEAD_DIM, zero, pair)


def spread_pair(pair):
    first, second = halves(pair)
    zero = jnp.zeros_like(pair)
    return jnp.concatenate(
        [
            jnp.concatenate([first, zero], 1),
            jnp.concatenate([zero, first], 1),
            jnp.concatenate([second, zero], 1),
            jnp.concatenate([zero, second], 1),
        ],
        0,
    )


def double(block):
    zero = jnp.zeros_like(block)
    return jnp.concatenate(
        [jnp.concatenate([block, zero], 1), jnp.concatenate([zero, block], 1)], 0
    )


def one_hots(coded, group, hot_ref, own_ref, live_own_ref):
    depth, cols = hot_ref.shape
    rows = depth // CODES
    pairs = rows // 2
    own = own_ref.shape[0] // pairs
    ids = (coded & 0xFFFF).astype(f32)
    live = (coded[:, 0:LANES] >> 16).astype(f32)

    code = iota((CODES, cols), 0).astype(f32)
    for r in range(rows):
        hot = jnp.broadcast_to(ids[r : r + 1, :], (CODES, cols)) == code
        hot_ref[r * CODES : (r + 1) * CODES, :] = hot.astype(f32).astype(bf16)

    pick = (iota((own, cols), 1) == group * own + iota((own, cols), 0)).astype(f32).astype(bf16)
    mine = dot_nt(pick, ids.astype(bf16))
    lane = iota((own, LANES), 1)
    first_half = lane < CODES
    lane_code = jnp.where(first_half, lane, lane - CODES).astype(f32)
    for k in range(pairs):
        value = jnp.where(first_half, mine[:, 2 * k : 2 * k + 1], mine[:, 2 * k + 1 : 2 * k + 2])
        hot = (value == lane_code).astype(f32)
        alive = jnp.where(first_half, live[2 * k : 2 * k + 1, :], live[2 * k + 1 : 2 * k + 2, :])
        own_ref[k * own : (k + 1) * own, :] = hot.astype(bf16)
        live_own_ref[k * own : (k + 1) * own, :] = (hot * alive).astype(bf16)
    return live


def tied_sum(scores_ref, live_own_ref, hot_ref, sum_ref):
    heads = scores_ref.shape[0]
    own = sum_ref.shape[0] // heads
    depth = hot_ref.shape[0]
    pairs = depth // CODES // 2
    for h in range(heads):
        looked = dot_nn(live_own_ref[...], scores_ref[h]).astype(bf16)
        for piece in range(2):
            for k in range(pairs):
                to = piece * depth + k * LANES
                sum_ref[h * own : (h + 1) * own, to : to + LANES] = looked[
                    k * own : (k + 1) * own, piece * LANES : (piece + 1) * LANES
                ]
    return dot_nn(sum_ref[:, 0:depth], hot_ref[...]) + dot_nn(
        sum_ref[:, depth : 2 * depth], hot_ref[...]
    )


def near_kernel(parts, *refs):
    tables_refs, refs = refs[:parts], refs[parts:]
    (
        codes_ref,
        scores_ref,
        values_ref,
        tied_ref,
        hot_ref,
        own_ref,
        tables_ref,
        table_ref,
        live_own_ref,
        sum_ref,
    ) = refs
    width = values_ref.shape[1]
    heads = width // HEAD_DIM
    local = width // parts
    group = lax.axis_index("seq")
    part = lax.axis_index("head")
    for p in range(parts):
        tables_ref[part ^ p] = tables_refs[p][...]

    for t in range(3):
        to_ref = values_ref if t == 2 else table_ref.at[t]
        to_ref[0:TABLE_ROWS, :] = jnp.concatenate(
            [tables_ref[p, :, t * local : (t + 1) * local] for p in range(parts)], 1
        )
        to_ref[TABLE_ROWS:CODES, :] = jnp.zeros((CODES - TABLE_ROWS, width), bf16)

    spans = [slice(hp * LANES, (hp + 1) * LANES) for hp in range(heads // 2)]
    queries = [spread_pair(table_ref[0, :, span]) for span in spans]
    keys = [double(table_ref[1, :, span]) for span in spans]
    scores = [dot_nt(query, key) for query, key in zip(queries, keys)]
    high = [score.astype(bf16) for score in scores]
    low = [(score - part_of.astype(f32)).astype(bf16) for score, part_of in zip(scores, high)]
    for h in range(heads):
        these = slice(h % 2 * LANES, (h % 2 + 1) * LANES)
        scores_ref[h, :, 0:LANES] = high[h // 2][these]
        scores_ref[h, :, LANES : 2 * LANES] = low[h // 2][these]

    one_hots(codes_ref[...], group, hot_ref, own_ref, live_own_ref)
    tied_ref[...] = tied_sum(scores_ref, live_own_ref, hot_ref, sum_ref)


def attend_near(tables, codes, own):
    parts = len(tables)
    width = tables[0].shape[1] // 3 * parts
    heads = width // HEAD_DIM
    rows, cols = codes.shape
    return pl.pallas_call(
        functools.partial(near_kernel, parts),
        out_shape=(
            jax.ShapeDtypeStruct((heads, LANES, 2 * LANES), bf16),
            jax.ShapeDtypeStruct((CODES, width), bf16),
            jax.ShapeDtypeStruct((heads * own, cols), f32),
            jax.ShapeDtypeStruct((rows * CODES, cols), bf16),
            jax.ShapeDtypeStruct((rows // 2 * own, LANES), bf16),
        ),
        scratch_shapes=[
            pltpu.VMEM((parts,) + tables[0].shape, bf16),
            pltpu.VMEM((2, CODES, width), bf16),
            pltpu.VMEM((rows // 2 * own, LANES), bf16),
            pltpu.VMEM((heads * own, 2 * rows * CODES), bf16),
        ],
        cost_estimate=pl.CostEstimate(flops=10**9, bytes_accessed=10**6, transcendentals=0),
        compiler_params=pltpu.CompilerParams(vmem_limit_bytes=LARGE_VMEM),
        name="near_scores",
    )(*tables, codes)


def row_kernel(
    scores_ref,
    values_ref,
    near_tied_ref,
    near_hot_ref,
    near_codes_ref,
    far_codes_ref,
    row_context_ref,
    own_ref,
    live_ref,
    hot_ref,
    live_own_ref,
    sum_ref,
    spread_ref,
):
    depth = hot_ref.shape[0]
    rows = 2 * depth // CODES
    pairs = rows // 2
    width = row_context_ref.shape[1]
    heads = width // HEAD_DIM
    own = spread_ref.shape[0] // heads
    group = lax.axis_index("seq")

    live = one_hots(far_codes_ref[...], group, hot_ref, own_ref, live_own_ref)
    live = jnp.concatenate([(near_codes_ref[:, 0:LANES] >> 16).astype(f32), live], 0)
    live_ref[...] = live
    tied = near_tied_ref[...] + tied_sum(scores_ref, live_own_ref, hot_ref, sum_ref)
    count = jnp.sum(live, axis=0, keepdims=True)[:, 0:1]
    probs = softmax_last(tied * (HEAD_DIM ** (-0.5) / jnp.sqrt(count))).astype(bf16)

    spread_ref[:, 0:depth] = dot_nt(probs, near_hot_ref[...]).astype(bf16)
    spread_ref[:, depth : 2 * depth] = dot_nt(probs, hot_ref[...]).astype(bf16)
    spans = [slice(hp * LANES, (hp + 1) * LANES) for hp in range(heads // 2)]
    values = [spread_pair(values_ref[:, span]) for span in spans]
    contexts = []
    for hp in range(heads // 2):
        first = (hp * 2) * own
        weights = jnp.concatenate(
            [
                jnp.concatenate(
                    [
                        spread_ref[first : first + own, k * LANES : (k + 1) * LANES],
                        spread_ref[first + own : first + 2 * own, k * LANES : (k + 1) * LANES],
                    ],
                    1,
                )
                for k in range(pairs)
            ],
            0,
        )
        contexts.append(dot_nn(weights, values[hp]).astype(bf16))
    for hp in range(heads // 2):
        for k in range(pairs):
            for r2 in range(2):
                at = (2 * k + r2) * own
                row_context_ref[at : at + own, spans[hp]] = contexts[hp][
                    k * own : (k + 1) * own, r2 * LANES : (r2 + 1) * LANES
                ]


def attend_rows(near, near_codes, far_codes, own):
    scores, values, near_tied, near_hot = near
    heads, width = scores.shape[0], values.shape[1]
    half, cols = near_codes.shape
    return pl.pallas_call(
        row_kernel,
        out_shape=(
            jax.ShapeDtypeStruct((2 * half * own, width), bf16),
            jax.ShapeDtypeStruct((half // 2 * own, LANES), bf16),
            jax.ShapeDtypeStruct((2 * half, LANES), f32),
        ),
        scratch_shapes=[
            pltpu.VMEM((half * CODES, cols), bf16),
            pltpu.VMEM((half // 2 * own, LANES), bf16),
            pltpu.VMEM((heads * own, 2 * half * CODES), bf16),
            pltpu.VMEM((heads * own, 2 * half * CODES), bf16),
        ],
        cost_estimate=pl.CostEstimate(flops=3 * 10**9, bytes_accessed=10**6, transcendentals=0),
        compiler_params=pltpu.CompilerParams(vmem_limit_bytes=LARGE_VMEM),
        name="row_attention",
    )(scores, values, near_tied, near_hot, near_codes, far_codes)


def column_kernel(parts, *refs):
    row_out_refs, refs = refs[:parts], refs[parts:]
    (
        live_ref,
        row_context_ref,
        near_own_ref,
        far_own_ref,
        embed_ref,
        col_qkv_ref,
        *context_refs,
        mixed_out_ref,
        row_out_ref,
        embed2_ref,
        weight_ref,
    ) = refs
    rows = live_ref.shape[0]
    tokens, width = row_context_ref.shape
    pairs = rows // 2
    own = tokens // rows
    vocab = embed_ref.shape[0]
    local = width // parts
    part = lax.axis_index("head")

    for p in range(parts):
        row_out_ref[part ^ p] = row_out_refs[p][...]
    embed2_ref[...] = jnp.zeros(embed2_ref.shape, bf16)
    embed2_ref[0:vocab, 0:width] = embed_ref[...]
    embed2_ref[CODES : CODES + vocab, width : 2 * width] = embed_ref[...]

    own_codes = jnp.concatenate([near_own_ref[...], far_own_ref[...]], 0)
    embedded2 = dot_nn(own_codes, embed2_ref[...])
    embedded = jnp.concatenate(
        [
            embedded2[k * own : (k + 1) * own, r2 * width : (r2 + 1) * width]
            for k in range(pairs)
            for r2 in range(2)
        ],
        0,
    )
    mixed = embedded + dot_nt(row_context_ref[...], row_out_ref[...].reshape(width, width))
    for p in range(parts):

        @pl.when(part == p)
        def _():
            mixed_out_ref[...] = mixed[:, p * local : (p + 1) * local]

    normed = layer_norm(mixed).astype(bf16)

    few = 8
    groups = own // few
    unit = rows * few

    def regroup(values):
        shape = (rows, groups, few, values.shape[1])
        return jnp.swapaxes(values.reshape(shape), 0, 1).reshape(tokens, values.shape[1])

    odd = part % 2
    for t in range(3):
        first = pl.multiple_of(t * local + odd * HEAD_DIM, HEAD_DIM)
        last = pl.multiple_of(t * local + (1 - odd) * LANES, HEAD_DIM)
        third = (3 + t) * LANES
        weight_ref[t * LANES : (t + 1) * LANES, :] = col_qkv_ref[pl.ds(first, LANES), :]
        weight_ref[third : third + HEAD_DIM, :] = col_qkv_ref[pl.ds(last, HEAD_DIM), :]
        weight_ref[third + HEAD_DIM : third + LANES, :] = jnp.zeros((HEAD_DIM, width), bf16)
    proj = [
        dot_nt(normed, weight_ref[2 * j * LANES : 2 * (j + 1) * LANES, :]) for j in range(3)
    ]
    proj = [
        proj[j][:, k * LANES : (k + 1) * LANES] * (HEAD_DIM ** (-0.5) if (2 * j + k) % 3 == 0 else 1.0)
        for j in range(3)
        for k in range(2)
    ]
    proj = [regroup(values).astype(bf16) for values in proj]
    sub, lan = iota((unit, unit), 0), iota((unit, unit), 1)
    same_column = (sub % few) == (lan % few)
    seq_of_lane = iota((rows, unit), 1) // few
    live_lane = jnp.sum(
        jnp.where(seq_of_lane == iota((rows, unit), 0), live_ref[...], 0.0), axis=0, keepdims=True
    )
    visible = jnp.logical_and(same_column, jnp.broadcast_to(live_lane, (unit, unit)) > 0)
    chosen = []
    for g in range(groups):
        at = slice(g * unit, (g + 1) * unit)
        query, keys, values = (proj[t][at] for t in range(3))
        chosen += [(half, keys, values) for half in halves(query)]
        chosen.append(tuple(proj[3 + t][at] for t in range(3)))
    scores = [jnp.where(visible, dot_nt(query, keys), -jnp.inf) for query, keys, _ in chosen]
    tops = [jnp.max(score, axis=-1, keepdims=True) for score in scores]
    weights = [jnp.exp(score - top) for score, top in zip(scores, tops)]
    shares = [1.0 / jnp.sum(weight, axis=-1, keepdims=True) for weight in weights]
    probs = [(weight * share).astype(bf16) for weight, share in zip(weights, shares)]
    found = [dot_nn(prob, values) for prob, (_, _, values) in zip(probs, chosen)]
    first_head = iota((unit, LANES), 1) < HEAD_DIM

    def ungroup(blocks):
        whole = jnp.concatenate(blocks, 0).reshape(groups, rows, few, LANES)
        return jnp.swapaxes(whole, 0, 1).reshape(tokens, LANES)

    main = ungroup(
        [jnp.where(first_head, found[3 * g], found[3 * g + 1]) for g in range(groups)]
    )
    third = ungroup([found[3 * g + 2] for g in range(groups)])
    start = 0
    for context_ref in context_refs:
        count = context_ref.shape[0] * 2 // 3
        some = count // 2
        context_ref[0:count, :] = main[start : start + count].astype(bf16)
        early = third[start : start + some]
        late = third[start + some : start + count]
        left = jnp.where(odd == 1, late, early)
        right = jnp.where(odd == 1, early, late)
        context_ref[count : count + some, :] = jnp.concatenate(
            [left[:, 0:HEAD_DIM], right[:, 0:HEAD_DIM]], 1
        ).astype(bf16)
        start += count


def attend_columns_here(row_outs, live, row_context, near_own, far_own, embed, col_qkv):
    parts = len(row_outs)
    tokens, width = row_context.shape
    local = width // parts
    half = tokens // 2 * local // LANES
    return pl.pallas_call(
        functools.partial(column_kernel, parts),
        out_shape=(
            jax.ShapeDtypeStruct((half, LANES), bf16),
            jax.ShapeDtypeStruct((half, LANES), bf16),
            jax.ShapeDtypeStruct((tokens, local), f32),
        ),
        scratch_shapes=[
            pltpu.VMEM((parts, local, width), bf16),
            pltpu.VMEM((2 * CODES, 2 * width), bf16),
            pltpu.VMEM((6 * LANES, width), bf16),
        ],
        cost_estimate=pl.CostEstimate(flops=2 * 10**9, bytes_accessed=10**6, transcendentals=0),
        compiler_params=pltpu.CompilerParams(vmem_limit_bytes=LARGE_VMEM),
        name="column_attention",
    )(*row_outs, live, row_context, near_own, far_own, embed, col_qkv)


def finish_kernel(parts, groups, *refs):
    context_refs = [refs[:parts], refs[parts : 2 * parts]]
    mixed_ref, col_out_ref, out_ref, context_ref = refs[2 * parts :]
    tokens, local = mixed_ref.shape
    group = lax.axis_index("seq")
    part = lax.axis_index("head")
    starts = [0, context_refs[0][0].shape[0]]
    for start, some_refs in zip(starts, context_refs):
        for p in range(parts):
            context_ref[part ^ p, start : start + some_refs[p].shape[0], :] = some_refs[p][...]
    pieces = []
    for start, some_refs in zip(starts, context_refs):
        count = some_refs[0].shape[0] * 2 // 3
        end = start + some_refs[0].shape[0]
        low = iota((count // 2, LANES), 1) < HEAD_DIM
        features = []
        for p in range(0, parts, 2):
            even = context_ref[p, start + count : end, :]
            other = context_ref[p + 1, start + count : end, :]
            early = jnp.where(low, even, other)
            late = jnp.where(low, other, even)
            late = jnp.concatenate([late[:, HEAD_DIM:], late[:, 0:HEAD_DIM]], 1)
            features += [
                context_ref[p, start : start + count, :],
                jnp.concatenate([early, late], 0),
                context_ref[p + 1, start : start + count, :],
            ]
        pieces.append(jnp.concatenate(features, 1))
    total = mixed_ref[...] + dot_nt(jnp.concatenate(pieces, 0), col_out_ref[...])
    own = tokens // groups // 2
    for d in range(groups):
        first, second = (total[(2 * d + r) * own : (2 * d + r + 1) * own, :] for r in range(2))
        rest = jnp.concatenate([first[:, LANES:local], second[:, LANES:local]], 1)
        out_ref[group ^ d] = jnp.concatenate(
            [first[:, 0:LANES], second[:, 0:LANES], rest], 0
        ).astype(bf16)


def finish(contexts, mixed, col_out, groups):
    parts = len(contexts[0])
    tokens, local = mixed.shape
    return pl.pallas_call(
        functools.partial(finish_kernel, parts, groups),
        out_shape=jax.ShapeDtypeStruct((groups, tokens // groups * local // LANES, LANES), bf16),
        scratch_shapes=[pltpu.VMEM((parts, tokens * local // LANES, LANES), bf16)],
        compiler_params=pltpu.CompilerParams(vmem_limit_bytes=LARGE_VMEM),
        name="finish",
    )(*contexts[0], *contexts[1], mixed, col_out)


def order_kernel(blocks_ref, out_ref):
    groups = blocks_ref.shape[0]
    local, cols = out_ref.shape[1:]
    own = cols // groups
    rest = local - LANES
    for part in range(3):
        piece = jnp.concatenate(
            [blocks_ref[g, part * own : (part + 1) * own, :] for g in range(groups)], 0
        )
        turned = piece.astype(f32).T.astype(bf16)
        if part < 2:
            out_ref[part, 0:LANES, :] = turned
        else:
            for r in range(2):
                out_ref[r, LANES:local, :] = turned[r * rest : (r + 1) * rest, :]


def order(blocks, cols, local):
    return pl.pallas_call(
        order_kernel,
        out_shape=jax.ShapeDtypeStruct((2, local, cols), bf16),
        compiler_params=pltpu.CompilerParams(vmem_limit_bytes=SMALL_VMEM),
        name="order",
    )(blocks)


def fast_body(ids, pad_mask, embed, row_qkv, row_out, col_qkv, col_out):
    rows_here, cols = ids.shape
    width = embed.shape[1]
    local = row_out.shape[0]
    groups, parts = lax.axis_size("seq"), lax.axis_size("head")
    own, rows = cols // groups, rows_here * groups

    def pairwise(value, partner):
        order = [(g, p) for g in range(groups) for p in range(parts)]
        link = [(g * parts + p, partner(g, p)) for g, p in order]
        return lax.ppermute(value, ("seq", "head"), [(i, g * parts + p) for i, (g, p) in link])

    def sibling(g, p):
        return g, p ^ 1

    def across(g, p):
        return g, p ^ 2

    def opposite(g, p):
        return g, p ^ 3

    far = pairwise(row_out, across)
    coded = make_codes(ids, pad_mask, rows_here * groups // 2)
    coded, row_qkv = lax.optimization_barrier((coded, row_qkv))
    received = pairwise(coded, lambda g, p: (g ^ 1, p))
    table = make_tables(embed, row_qkv)
    tables = [table, None, pairwise(table, across), None]
    step = 2
    while step < groups:
        coded = join(coded, received, rows_here * step // 2)
        if step == 2:
            coded, table = lax.optimization_barrier((coded, table))
            tables[3] = pairwise(table, opposite)
        elif step == 4:
            coded, table, row_out, far = lax.optimization_barrier((coded, table, row_out, far))
            tables[1] = pairwise(table, sibling)
            row_outs = [row_out, pairwise(row_out, sibling), far, pairwise(far, sibling)]
        received = pairwise(coded, lambda g, p, step=step: (g ^ step, p))
        step *= 2
    codes = (coded, received)
    *near_scores, near_own = attend_near(tables, codes[0], own)
    row_context, far_own, live = attend_rows(near_scores, *codes, own)
    *halves_here, mixed = attend_columns_here(
        row_outs,
        live,
        row_context,
        near_own,
        far_own,
        embed,
        col_qkv.reshape(3 * local, width),
    )
    contexts = []
    for context in halves_here:
        beyond = pairwise(context, across)
        contexts.append(
            (context, pairwise(context, sibling), beyond, pairwise(beyond, sibling))
        )
    blocks = finish(contexts, mixed, col_out, groups)
    blocks = lax.all_to_all(blocks, "seq", split_axis=0, concat_axis=0, tiled=True)
    return jnp.swapaxes(order(blocks, cols, local), 1, 2)


def weight_fold(out_weight, piece):
    return jnp.einsum("rce,fe->rcf", piece, out_weight, preferred_element_type=f32)


def attend_columns(query, keys, values, key_live):
    rows_all, count_cols, local_width = query.shape
    heads_here = local_width // HEAD_DIM
    shape = (rows_all, count_cols, heads_here, HEAD_DIM)
    scores = jnp.einsum(
        "rchd,schd->chrs",
        query.reshape(shape),
        keys.reshape(shape),
        preferred_element_type=f32,
    ) * HEAD_DIM ** (-0.5)
    scores = jnp.where(key_live > 0, scores, -jnp.inf)
    probs = softmax_last(scores).astype(bf16)
    context = jnp.einsum(
        "chrs,schd->rchd", probs, values.reshape(shape), preferred_element_type=f32
    )
    return context.astype(bf16).reshape(rows_all, count_cols, local_width)


def send_back(context):
    return lax.all_to_all(context[:, None], "seq", split_axis=0, concat_axis=1, tiled=True)


def general_body(ids, pad_mask, embed, row_qkv, row_out, col_qkv, col_out):
    rows_here, cols = ids.shape
    width = embed.shape[1]
    local_width = row_out.shape[0]
    heads_here = local_width // HEAD_DIM
    groups = lax.axis_size("seq")
    per_group = cols // groups
    codes = lax.broadcasted_iota(jnp.int32, (1, 1, embed.shape[0]), 2)
    onehot = (ids[:, :, None] == codes).astype(bf16)
    embedded = jnp.einsum("rcv,vd->rcd", onehot, embed, preferred_element_type=f32)
    normed = layer_norm(embedded).astype(bf16)
    row_proj = jnp.einsum("rcd,ted->trce", normed, row_qkv, preferred_element_type=f32)
    row_proj = row_proj.astype(bf16)
    live = pad_mask.astype(bf16)
    head_shape = (rows_here, cols, heads_here, HEAD_DIM)
    query = (row_proj[0] * live[:, None, None]).reshape(head_shape)
    keys = row_proj[1].reshape(head_shape)
    values = row_proj[2].reshape(head_shape)
    partial_scores = jnp.einsum("rihd,rjhd->hij", query, keys, preferred_element_type=f32)
    count_here = jnp.sum(pad_mask.astype(f32))
    scale = HEAD_DIM ** (-0.5)
    total, count = lax.psum((partial_scores, count_here), "seq")
    row_probs = softmax_last(total * (scale / jnp.sqrt(count))).astype(bf16)
    row_context = jnp.einsum("hij,rjhd->rihd", row_probs, values, preferred_element_type=f32)
    row_context = row_context.astype(bf16).reshape(rows_here, cols, local_width)
    start_feature = lax.axis_index("head") * local_width
    resident = lax.dynamic_slice_in_dim(embedded, start_feature, local_width, 2)
    row_update = weight_fold(row_out, lax.all_gather(row_context, "head", axis=2, tiled=True))
    mixed = resident + row_update
    sums, squares = lax.psum((jnp.sum(mixed, axis=-1), jnp.sum(mixed * mixed, axis=-1)), "head")
    mean = sums / width
    spread = squares / width - mean * mean
    normed_here = ((mixed - mean[..., None]) * lax.rsqrt(spread[..., None] + EPS)).astype(bf16)
    live_tile = jnp.broadcast_to(live[:, None, None, None], (rows_here, groups, per_group, 1))
    normed_full = lax.all_gather(normed_here, "head", axis=2, tiled=True)
    col_proj = jnp.einsum("rcd,ted->rcte", normed_full, col_qkv, preferred_element_type=f32)
    packed = col_proj.astype(bf16).reshape(rows_here, groups, per_group, 3 * local_width)
    received = lax.all_to_all(packed, "seq", split_axis=1, concat_axis=0, tiled=True)
    mask_part = lax.all_to_all(live_tile, "seq", split_axis=1, concat_axis=0, tiled=True)
    column_out = send_back(
        attend_columns(
            received[:, 0, :, :local_width],
            received[:, 0, :, local_width : 2 * local_width],
            received[:, 0, :, 2 * local_width :],
            mask_part[:, 0, 0, 0],
        )
    )
    column_out = column_out.reshape(rows_here, cols, local_width)
    col_update = weight_fold(col_out, lax.all_gather(column_out, "head", axis=2, tiled=True))
    return (mixed + col_update).astype(bf16)


def body(ids, pad_mask, embed, row_qkv, row_out, col_qkv, col_out):
    rows_here, cols = ids.shape
    groups = lax.axis_size("seq")
    own, rows = cols // groups, rows_here * groups
    parts = lax.axis_size("head")
    local = row_out.shape[0]
    fits = (
        parts == 4
        and groups >= 8
        and groups & (groups - 1) == 0
        and rows * 8 == LANES
        and rows_here == 2
        and own % 32 == 0
        and cols >= LANES
        and local == LANES + HEAD_DIM
        and embed.shape[0] <= TABLE_ROWS
    )
    chosen = fast_body if fits else general_body
    return chosen(ids, pad_mask, embed, row_qkv, row_out, col_qkv, col_out)


def solution(mesh):
    placed = (
        P("seq", None),
        P("seq"),
        P(),
        P(None, "head", None),
        P("head", None),
        P(None, "head", None),
        P("head", None),
    )
    return jax.shard_map(
        body, mesh=mesh, in_specs=placed, out_specs=P("seq", None, "head"), check_vma=False
    )
```

```python
import functools

import jax
import jax.numpy as jnp
from jax import lax
from jax.experimental import pallas as pl
from jax.experimental.pallas import tpu as pltpu
from jax.sharding import PartitionSpec as P

HEAD_DIM = 64
EPS = 1e-05
LANES = 128
CODES = 64
TABLE_ROWS = 40

SMALL_VMEM = 8 * 1024 * 1024
LARGE_VMEM = 32 * 1024 * 1024

f32 = jnp.float32
bf16 = jnp.bfloat16


def layer_norm(values):
    mean = jnp.mean(values, axis=-1, keepdims=True)
    centred = values - mean
    spread = jnp.mean(centred * centred, axis=-1, keepdims=True)
    return centred * lax.rsqrt(spread + EPS)


def softmax_last(scores):
    top = jnp.max(scores, axis=-1, keepdims=True)
    weights = jnp.exp(scores - top)
    return weights * (1.0 / jnp.sum(weights, axis=-1, keepdims=True))


def dot_nt(left, right):
    return lax.dot_general(left, right, (((1,), (1,)), ((), ())), preferred_element_type=f32)


def dot_nn(left, right):
    return jnp.dot(left, right, preferred_element_type=f32)


def in_hbm(value):
    return pltpu.with_memory_space_constraint(value, pltpu.HBM)


def iota(shape, axis):
    return lax.broadcasted_iota(jnp.int32, shape, axis)


def code_kernel(ids_hbm, live_hbm, out_ref, ids_ref, live_ref, sems):
    loads = [
        pltpu.make_async_copy(ids_hbm, ids_ref, sems.at[0]),
        pltpu.make_async_copy(live_hbm, live_ref, sems.at[1]),
    ]
    for load in loads:
        load.start()
    for load in loads:
        load.wait()
    row = iota(ids_ref.shape, 0)
    live = jnp.zeros(ids_ref.shape, jnp.int32)
    for r in range(ids_ref.shape[0]):
        live = jnp.where(row == r, live_ref[r], live)
    coded = ids_ref[...] + 65536 * live
    out_ref[...] = jnp.concatenate([coded] * (out_ref.shape[0] // coded.shape[0]), 0)


def make_codes(ids, pad_mask, height):
    return pl.pallas_call(
        code_kernel,
        out_shape=jax.ShapeDtypeStruct((height, ids.shape[1]), jnp.int32),
        in_specs=[pl.BlockSpec(memory_space=pltpu.HBM)] * 2,
        scratch_shapes=[
            pltpu.VMEM(ids.shape, jnp.int32),
            pltpu.SMEM(pad_mask.shape, jnp.int32),
            pltpu.SemaphoreType.DMA((2,)),
        ],
        compiler_params=pltpu.CompilerParams(vmem_limit_bytes=SMALL_VMEM),
        name="codes",
    )(in_hbm(ids), in_hbm(pad_mask))


def join_kernel(rows, own_ref, other_ref, out_ref):
    own, other = own_ref[...], other_ref[...]
    both = jnp.concatenate([own[0:rows], other[0:rows]], 0)
    out_ref[...] = jnp.concatenate([both] * (own.shape[0] // (2 * rows)), 0)


def join(own, other, rows):
    return pl.pallas_call(
        functools.partial(join_kernel, rows),
        out_shape=jax.ShapeDtypeStruct(own.shape, own.dtype),
        compiler_params=pltpu.CompilerParams(vmem_limit_bytes=SMALL_VMEM),
        name="join",
    )(own, other)


def table_kernel(embed_hbm, qkv_hbm, out_ref, embed_ref, qkv_ref, padded_ref, sems):
    kinds = qkv_ref.shape[0]
    loads = [pltpu.make_async_copy(embed_hbm, embed_ref, sems.at[kinds])]
    loads += [
        pltpu.make_async_copy(qkv_hbm.at[t], qkv_ref.at[t], sems.at[t]) for t in range(kinds)
    ]
    for load in loads:
        load.start()
    padded_ref[...] = jnp.zeros(padded_ref.shape, f32)
    loads[0].wait()
    padded_ref[0 : embed_ref.shape[0], :] = embed_ref[...].astype(f32)
    normed = layer_norm(padded_ref[...]).astype(bf16)
    tables = []
    for t in range(kinds):
        loads[1 + t].wait()
        tables.append(dot_nt(normed, qkv_ref[t]))
    out_ref[...] = jnp.concatenate(tables, 1).astype(bf16)


def make_tables(embed, row_qkv):
    kinds, local, width = row_qkv.shape
    return pl.pallas_call(
        table_kernel,
        out_shape=jax.ShapeDtypeStruct((TABLE_ROWS, kinds * local), bf16),
        in_specs=[pl.BlockSpec(memory_space=pltpu.HBM)] * 2,
        scratch_shapes=[
            pltpu.VMEM(embed.shape, bf16),
            pltpu.VMEM(row_qkv.shape, bf16),
            pltpu.VMEM((TABLE_ROWS, width), f32),
            pltpu.SemaphoreType.DMA((kinds + 1,)),
        ],
        cost_estimate=pl.CostEstimate(
            flops=2 * 10**9, bytes_accessed=2 * row_qkv.size, transcendentals=0
        ),
        compiler_params=pltpu.CompilerParams(vmem_limit_bytes=SMALL_VMEM),
        name="tables",
    )(in_hbm(embed), in_hbm(row_qkv))


def halves(pair):
    lane = iota(pair.shape, 1)
    zero = jnp.zeros_like(pair)
    return jnp.where(lane < HEAD_DIM, pair, zero), jnp.where(lane < HEAD_DIM, zero, pair)


def spread_pair(pair):
    first, second = halves(pair)
    zero = jnp.zeros_like(pair)
    return jnp.concatenate(
        [
            jnp.concatenate([first, zero], 1),
            jnp.concatenate([zero, first], 1),
            jnp.concatenate([second, zero], 1),
            jnp.concatenate([zero, second], 1),
        ],
        0,
    )


def double(block):
    zero = jnp.zeros_like(block)
    return jnp.concatenate(
        [jnp.concatenate([block, zero], 1), jnp.concatenate([zero, block], 1)], 0
    )


def one_hots(coded, group, hot_ref, own_ref, live_own_ref):
    depth, cols = hot_ref.shape
    rows = depth // CODES
    pairs = rows // 2
    own = own_ref.shape[0] // pairs
    ids = (coded & 0xFFFF).astype(f32)
    live = (coded[:, 0:LANES] >> 16).astype(f32)

    code = iota((CODES, cols), 0).astype(f32)
    for r in range(rows):
        hot = jnp.broadcast_to(ids[r : r + 1, :], (CODES, cols)) == code
        hot_ref[r * CODES : (r + 1) * CODES, :] = hot.astype(f32).astype(bf16)

    pick = (iota((own, cols), 1) == group * own + iota((own, cols), 0)).astype(f32).astype(bf16)
    mine = dot_nt(pick, ids.astype(bf16))
    lane = iota((own, LANES), 1)
    first_half = lane < CODES
    lane_code = jnp.where(first_half, lane, lane - CODES).astype(f32)
    for k in range(pairs):
        value = jnp.where(first_half, mine[:, 2 * k : 2 * k + 1], mine[:, 2 * k + 1 : 2 * k + 2])
        hot = (value == lane_code).astype(f32)
        alive = jnp.where(first_half, live[2 * k : 2 * k + 1, :], live[2 * k + 1 : 2 * k + 2, :])
        own_ref[k * own : (k + 1) * own, :] = hot.astype(bf16)
        live_own_ref[k * own : (k + 1) * own, :] = (hot * alive).astype(bf16)
    return live


def tied_sum(scores_ref, live_own_ref, hot_ref, sum_ref):
    heads = scores_ref.shape[0]
    own = sum_ref.shape[0] // heads
    depth = hot_ref.shape[0]
    pairs = depth // CODES // 2
    for h in range(heads):
        looked = dot_nn(live_own_ref[...], scores_ref[h]).astype(bf16)
        for piece in range(2):
            for k in range(pairs):
                to = piece * depth + k * LANES
                sum_ref[h * own : (h + 1) * own, to : to + LANES] = looked[
                    k * own : (k + 1) * own, piece * LANES : (piece + 1) * LANES
                ]
    return dot_nn(sum_ref[:, 0:depth], hot_ref[...]) + dot_nn(
        sum_ref[:, depth : 2 * depth], hot_ref[...]
    )


def embed_own(own_ref, embed2_ref, own):
    width = embed2_ref.shape[1] // 2
    both = dot_nn(own_ref[...], embed2_ref[...])
    return jnp.concatenate(
        [
            both[k * own : (k + 1) * own, r2 * width : (r2 + 1) * width]
            for k in range(both.shape[0] // own)
            for r2 in range(2)
        ],
        0,
    )


def near_kernel(parts, *refs):
    tables_refs, refs = refs[:parts], refs[parts:]
    (
        codes_ref,
        embed_ref,
        col_qkv_hbm,
        scores_ref,
        values_ref,
        tied_ref,
        hot_ref,
        embed2_ref,
        embedded_ref,
        weight_ref,
        tables_ref,
        table_ref,
        own_ref,
        live_own_ref,
        sum_ref,
        sems,
    ) = refs
    width = values_ref.shape[1]
    heads = width // HEAD_DIM
    local = width // parts
    vocab = embed_ref.shape[0]
    group = lax.axis_index("seq")
    part = lax.axis_index("head")

    odd = part % 2
    loads = []
    for t in range(3):
        first = pl.multiple_of(t * local + odd * HEAD_DIM, HEAD_DIM)
        last = pl.multiple_of(t * local + (1 - odd) * LANES, HEAD_DIM)
        third = (3 + t) * LANES
        loads += [
            pltpu.make_async_copy(
                col_qkv_hbm.at[pl.ds(first, LANES)],
                weight_ref.at[pl.ds(t * LANES, LANES)],
                sems.at[2 * t],
            ),
            pltpu.make_async_copy(
                col_qkv_hbm.at[pl.ds(last, HEAD_DIM)],
                weight_ref.at[pl.ds(third, HEAD_DIM)],
                sems.at[2 * t + 1],
            ),
        ]
        weight_ref[third + HEAD_DIM : third + LANES, :] = jnp.zeros((HEAD_DIM, width), bf16)
    for load in loads:
        load.start()
    embed2_ref[...] = jnp.zeros(embed2_ref.shape, bf16)
    embed2_ref[0:vocab, 0:width] = embed_ref[...]
    embed2_ref[CODES : CODES + vocab, width : 2 * width] = embed_ref[...]
    for p in range(parts):
        tables_ref[part ^ p] = tables_refs[p][...]

    for t in range(3):
        to_ref = values_ref if t == 2 else table_ref.at[t]
        to_ref[0:TABLE_ROWS, :] = jnp.concatenate(
            [tables_ref[p, :, t * local : (t + 1) * local] for p in range(parts)], 1
        )
        to_ref[TABLE_ROWS:CODES, :] = jnp.zeros((CODES - TABLE_ROWS, width), bf16)

    spans = [slice(hp * LANES, (hp + 1) * LANES) for hp in range(heads // 2)]
    queries = [spread_pair(table_ref[0, :, span]) for span in spans]
    keys = [double(table_ref[1, :, span]) for span in spans]
    scores = [dot_nt(query, key) for query, key in zip(queries, keys)]
    high = [score.astype(bf16) for score in scores]
    low = [(score - part_of.astype(f32)).astype(bf16) for score, part_of in zip(scores, high)]
    for h in range(heads):
        these = slice(h % 2 * LANES, (h % 2 + 1) * LANES)
        scores_ref[h, :, 0:LANES] = high[h // 2][these]
        scores_ref[h, :, LANES : 2 * LANES] = low[h // 2][these]

    one_hots(codes_ref[...], group, hot_ref, own_ref, live_own_ref)
    tied_ref[...] = tied_sum(scores_ref, live_own_ref, hot_ref, sum_ref)
    embedded_ref[...] = embed_own(own_ref, embed2_ref, own_ref.shape[0] // (hot_ref.shape[0] // LANES))
    for load in loads:
        load.wait()


def attend_near(tables, codes, embed, col_qkv, own):
    parts = len(tables)
    width = tables[0].shape[1] // 3 * parts
    heads = width // HEAD_DIM
    rows, cols = codes.shape
    return pl.pallas_call(
        functools.partial(near_kernel, parts),
        out_shape=(
            jax.ShapeDtypeStruct((heads, LANES, 2 * LANES), bf16),
            jax.ShapeDtypeStruct((CODES, width), bf16),
            jax.ShapeDtypeStruct((heads * own, cols), f32),
            jax.ShapeDtypeStruct((rows * CODES, cols), bf16),
            jax.ShapeDtypeStruct((2 * CODES, 2 * width), bf16),
            jax.ShapeDtypeStruct((rows * own, width), f32),
            jax.ShapeDtypeStruct((6 * LANES, width), bf16),
        ),
        in_specs=[pl.BlockSpec(memory_space=pltpu.VMEM)] * (parts + 2)
        + [pl.BlockSpec(memory_space=pltpu.HBM)],
        scratch_shapes=[
            pltpu.VMEM((parts,) + tables[0].shape, bf16),
            pltpu.VMEM((2, CODES, width), bf16),
            pltpu.VMEM((rows // 2 * own, LANES), bf16),
            pltpu.VMEM((rows // 2 * own, LANES), bf16),
            pltpu.VMEM((heads * own, 2 * rows * CODES), bf16),
            pltpu.SemaphoreType.DMA((6,)),
        ],
        cost_estimate=pl.CostEstimate(flops=10**9, bytes_accessed=10**6, transcendentals=0),
        compiler_params=pltpu.CompilerParams(vmem_limit_bytes=LARGE_VMEM),
        name="near_scores",
    )(*tables, codes, embed, in_hbm(col_qkv))


def row_kernel(
    scores_ref,
    values_ref,
    near_tied_ref,
    near_hot_ref,
    near_codes_ref,
    far_codes_ref,
    row_context_ref,
    own_ref,
    live_ref,
    hot_ref,
    live_own_ref,
    sum_ref,
    spread_ref,
):
    depth = hot_ref.shape[0]
    rows = 2 * depth // CODES
    pairs = rows // 2
    width = row_context_ref.shape[1]
    heads = width // HEAD_DIM
    own = spread_ref.shape[0] // heads
    group = lax.axis_index("seq")

    live = one_hots(far_codes_ref[...], group, hot_ref, own_ref, live_own_ref)
    live = jnp.concatenate([(near_codes_ref[:, 0:LANES] >> 16).astype(f32), live], 0)
    live_ref[...] = live
    tied = near_tied_ref[...] + tied_sum(scores_ref, live_own_ref, hot_ref, sum_ref)
    count = jnp.sum(live, axis=0, keepdims=True)[:, 0:1]
    probs = softmax_last(tied * (HEAD_DIM ** (-0.5) / jnp.sqrt(count))).astype(bf16)

    spread_ref[:, 0:depth] = dot_nt(probs, near_hot_ref[...]).astype(bf16)
    spread_ref[:, depth : 2 * depth] = dot_nt(probs, hot_ref[...]).astype(bf16)
    spans = [slice(hp * LANES, (hp + 1) * LANES) for hp in range(heads // 2)]
    values = [spread_pair(values_ref[:, span]) for span in spans]
    contexts = []
    for hp in range(heads // 2):
        first = (hp * 2) * own
        weights = jnp.concatenate(
            [
                jnp.concatenate(
                    [
                        spread_ref[first : first + own, k * LANES : (k + 1) * LANES],
                        spread_ref[first + own : first + 2 * own, k * LANES : (k + 1) * LANES],
                    ],
                    1,
                )
                for k in range(pairs)
            ],
            0,
        )
        contexts.append(dot_nn(weights, values[hp]).astype(bf16))
    for hp in range(heads // 2):
        for k in range(pairs):
            for r2 in range(2):
                at = (2 * k + r2) * own
                row_context_ref[at : at + own, spans[hp]] = contexts[hp][
                    k * own : (k + 1) * own, r2 * LANES : (r2 + 1) * LANES
                ]


def attend_rows(near, near_codes, far_codes, own):
    scores, values, near_tied, near_hot = near
    heads, width = scores.shape[0], values.shape[1]
    half, cols = near_codes.shape
    return pl.pallas_call(
        row_kernel,
        out_shape=(
            jax.ShapeDtypeStruct((2 * half * own, width), bf16),
            jax.ShapeDtypeStruct((half // 2 * own, LANES), bf16),
            jax.ShapeDtypeStruct((2 * half, LANES), f32),
        ),
        scratch_shapes=[
            pltpu.VMEM((half * CODES, cols), bf16),
            pltpu.VMEM((half // 2 * own, LANES), bf16),
            pltpu.VMEM((heads * own, 2 * half * CODES), bf16),
            pltpu.VMEM((heads * own, 2 * half * CODES), bf16),
        ],
        cost_estimate=pl.CostEstimate(flops=3 * 10**9, bytes_accessed=10**6, transcendentals=0),
        compiler_params=pltpu.CompilerParams(vmem_limit_bytes=LARGE_VMEM),
        name="row_attention",
    )(scores, values, near_tied, near_hot, near_codes, far_codes)


def column_kernel(parts, *refs):
    row_out_refs, refs = refs[:parts], refs[parts:]
    (
        live_ref,
        row_context_ref,
        embedded_ref,
        far_own_ref,
        embed2_ref,
        weight_ref,
        *context_refs,
        mixed_out_ref,
        row_out_ref,
    ) = refs
    rows = live_ref.shape[0]
    tokens, width = row_context_ref.shape
    pairs = rows // 2
    own = tokens // rows
    local = width // parts
    part = lax.axis_index("head")

    for p in range(parts):
        row_out_ref[part ^ p] = row_out_refs[p][...]

    embedded = jnp.concatenate([embedded_ref[...], embed_own(far_own_ref, embed2_ref, own)], 0)
    mixed = embedded + dot_nt(row_context_ref[...], row_out_ref[...].reshape(width, width))
    for p in range(parts):

        @pl.when(part == p)
        def _():
            mixed_out_ref[...] = mixed[:, p * local : (p + 1) * local]

    normed = layer_norm(mixed).astype(bf16)

    few = 8
    groups = own // few
    unit = rows * few

    def regroup(values):
        shape = (rows, groups, few, values.shape[1])
        return jnp.swapaxes(values.reshape(shape), 0, 1).reshape(tokens, values.shape[1])

    odd = part % 2
    proj = [
        dot_nt(normed, weight_ref[2 * j * LANES : 2 * (j + 1) * LANES, :]) for j in range(3)
    ]
    proj = [
        proj[j][:, k * LANES : (k + 1) * LANES] * (HEAD_DIM ** (-0.5) if (2 * j + k) % 3 == 0 else 1.0)
        for j in range(3)
        for k in range(2)
    ]
    proj = [regroup(values).astype(bf16) for values in proj]
    sub, lan = iota((unit, unit), 0), iota((unit, unit), 1)
    same_column = (sub % few) == (lan % few)
    seq_of_lane = iota((rows, unit), 1) // few
    live_lane = jnp.sum(
        jnp.where(seq_of_lane == iota((rows, unit), 0), live_ref[...], 0.0), axis=0, keepdims=True
    )
    visible = jnp.logical_and(same_column, jnp.broadcast_to(live_lane, (unit, unit)) > 0)
    chosen = []
    for g in range(groups):
        at = slice(g * unit, (g + 1) * unit)
        query, keys, values = (proj[t][at] for t in range(3))
        chosen += [(half, keys, values) for half in halves(query)]
        chosen.append(tuple(proj[3 + t][at] for t in range(3)))
    scores = [jnp.where(visible, dot_nt(query, keys), -jnp.inf) for query, keys, _ in chosen]
    tops = [jnp.max(score, axis=-1, keepdims=True) for score in scores]
    weights = [jnp.exp(score - top) for score, top in zip(scores, tops)]
    shares = [1.0 / jnp.sum(weight, axis=-1, keepdims=True) for weight in weights]
    probs = [(weight * share).astype(bf16) for weight, share in zip(weights, shares)]
    found = [dot_nn(prob, values) for prob, (_, _, values) in zip(probs, chosen)]
    first_head = iota((unit, LANES), 1) < HEAD_DIM

    def ungroup(blocks):
        whole = jnp.concatenate(blocks, 0).reshape(groups, rows, few, LANES)
        return jnp.swapaxes(whole, 0, 1).reshape(tokens, LANES)

    main = ungroup(
        [jnp.where(first_head, found[3 * g], found[3 * g + 1]) for g in range(groups)]
    )
    third = ungroup([found[3 * g + 2] for g in range(groups)])
    start = 0
    for context_ref in context_refs:
        count = context_ref.shape[0] * 2 // 3
        some = count // 2
        context_ref[0:count, :] = main[start : start + count].astype(bf16)
        early = third[start : start + some]
        late = third[start + some : start + count]
        left = jnp.where(odd == 1, late, early)
        right = jnp.where(odd == 1, early, late)
        context_ref[count : count + some, :] = jnp.concatenate(
            [left[:, 0:HEAD_DIM], right[:, 0:HEAD_DIM]], 1
        ).astype(bf16)
        start += count


def attend_columns_here(row_outs, live, row_context, embedded, far_own, embed2, weights):
    parts = len(row_outs)
    tokens, width = row_context.shape
    local = width // parts
    half = tokens // 2 * local // LANES
    return pl.pallas_call(
        functools.partial(column_kernel, parts),
        out_shape=(
            jax.ShapeDtypeStruct((half, LANES), bf16),
            jax.ShapeDtypeStruct((half, LANES), bf16),
            jax.ShapeDtypeStruct((tokens, local), f32),
        ),
        scratch_shapes=[
            pltpu.VMEM((parts, local, width), bf16),
        ],
        cost_estimate=pl.CostEstimate(flops=2 * 10**9, bytes_accessed=10**6, transcendentals=0),
        compiler_params=pltpu.CompilerParams(vmem_limit_bytes=LARGE_VMEM),
        name="column_attention",
    )(*row_outs, live, row_context, embedded, far_own, embed2, weights)


def finish_kernel(parts, groups, *refs):
    context_refs = [refs[:parts], refs[parts : 2 * parts]]
    mixed_ref, col_out_ref, out_ref, context_ref = refs[2 * parts :]
    tokens, local = mixed_ref.shape
    group = lax.axis_index("seq")
    part = lax.axis_index("head")
    starts = [0, context_refs[0][0].shape[0]]
    for start, some_refs in zip(starts, context_refs):
        for p in range(parts):
            context_ref[part ^ p, start : start + some_refs[p].shape[0], :] = some_refs[p][...]
    pieces = []
    for start, some_refs in zip(starts, context_refs):
        count = some_refs[0].shape[0] * 2 // 3
        end = start + some_refs[0].shape[0]
        low = iota((count // 2, LANES), 1) < HEAD_DIM
        features = []
        for p in range(0, parts, 2):
            even = context_ref[p, start + count : end, :]
            other = context_ref[p + 1, start + count : end, :]
            early = jnp.where(low, even, other)
            late = jnp.where(low, other, even)
            late = jnp.concatenate([late[:, HEAD_DIM:], late[:, 0:HEAD_DIM]], 1)
            features += [
                context_ref[p, start : start + count, :],
                jnp.concatenate([early, late], 0),
                context_ref[p + 1, start : start + count, :],
            ]
        pieces.append(jnp.concatenate(features, 1))
    total = mixed_ref[...] + dot_nt(jnp.concatenate(pieces, 0), col_out_ref[...])
    own = tokens // groups // 2
    for d in range(groups):
        first, second = (total[(2 * d + r) * own : (2 * d + r + 1) * own, :] for r in range(2))
        rest = jnp.concatenate([first[:, LANES:local], second[:, LANES:local]], 1)
        out_ref[group ^ d] = jnp.concatenate(
            [first[:, 0:LANES], second[:, 0:LANES], rest], 0
        ).astype(bf16)


def finish(contexts, mixed, col_out, groups):
    parts = len(contexts[0])
    tokens, local = mixed.shape
    return pl.pallas_call(
        functools.partial(finish_kernel, parts, groups),
        out_shape=jax.ShapeDtypeStruct((groups, tokens // groups * local // LANES, LANES), bf16),
        scratch_shapes=[pltpu.VMEM((parts, tokens * local // LANES, LANES), bf16)],
        compiler_params=pltpu.CompilerParams(vmem_limit_bytes=LARGE_VMEM),
        name="finish",
    )(*contexts[0], *contexts[1], mixed, col_out)


def order_kernel(blocks_ref, out_ref):
    groups = blocks_ref.shape[0]
    local, cols = out_ref.shape[1:]
    own = cols // groups
    rest = local - LANES
    for part in range(3):
        piece = jnp.concatenate(
            [blocks_ref[g, part * own : (part + 1) * own, :] for g in range(groups)], 0
        )
        turned = piece.astype(f32).T.astype(bf16)
        if part < 2:
            out_ref[part, 0:LANES, :] = turned
        else:
            for r in range(2):
                out_ref[r, LANES:local, :] = turned[r * rest : (r + 1) * rest, :]


def order(blocks, cols, local):
    return pl.pallas_call(
        order_kernel,
        out_shape=jax.ShapeDtypeStruct((2, local, cols), bf16),
        compiler_params=pltpu.CompilerParams(vmem_limit_bytes=SMALL_VMEM),
        name="order",
    )(blocks)


def fast_body(ids, pad_mask, embed, row_qkv, row_out, col_qkv, col_out):
    rows_here, cols = ids.shape
    width = embed.shape[1]
    local = row_out.shape[0]
    groups, parts = lax.axis_size("seq"), lax.axis_size("head")
    own, rows = cols // groups, rows_here * groups

    def pairwise(value, partner):
        order = [(g, p) for g in range(groups) for p in range(parts)]
        link = [(g * parts + p, partner(g, p)) for g, p in order]
        return lax.ppermute(value, ("seq", "head"), [(i, g * parts + p) for i, (g, p) in link])

    def sibling(g, p):
        return g, p ^ 1

    def across(g, p):
        return g, p ^ 2

    def opposite(g, p):
        return g, p ^ 3

    far = pairwise(row_out, across)
    coded = make_codes(ids, pad_mask, rows_here * groups // 2)
    coded, row_qkv = lax.optimization_barrier((coded, row_qkv))
    received = pairwise(coded, lambda g, p: (g ^ 1, p))
    table = make_tables(embed, row_qkv)
    tables = [table, None, pairwise(table, across), None]
    step = 2
    while step < groups:
        coded = join(coded, received, rows_here * step // 2)
        if step == 2:
            coded, table = lax.optimization_barrier((coded, table))
            tables[3] = pairwise(table, opposite)
        elif step == 4:
            coded, table, row_out, far = lax.optimization_barrier((coded, table, row_out, far))
            tables[1] = pairwise(table, sibling)
            row_outs = [row_out, pairwise(row_out, sibling), far, pairwise(far, sibling)]
        received = pairwise(coded, lambda g, p, step=step: (g ^ step, p))
        step *= 2
    codes = (coded, received)
    *near_scores, embed2, embedded, weights = attend_near(
        tables, coded, embed, col_qkv.reshape(3 * local, width), own
    )
    row_context, far_own, live = attend_rows(near_scores, *codes, own)
    *halves_here, mixed = attend_columns_here(
        row_outs, live, row_context, embedded, far_own, embed2, weights
    )
    contexts = []
    for context in halves_here:
        beyond = pairwise(context, across)
        contexts.append(
            (context, pairwise(context, sibling), beyond, pairwise(beyond, sibling))
        )
    blocks = finish(contexts, mixed, col_out, groups)
    blocks = lax.all_to_all(blocks, "seq", split_axis=0, concat_axis=0, tiled=True)
    return jnp.swapaxes(order(blocks, cols, local), 1, 2)


def weight_fold(out_weight, piece):
    return jnp.einsum("rce,fe->rcf", piece, out_weight, preferred_element_type=f32)


def attend_columns(query, keys, values, key_live):
    rows_all, count_cols, local_width = query.shape
    heads_here = local_width // HEAD_DIM
    shape = (rows_all, count_cols, heads_here, HEAD_DIM)
    scores = jnp.einsum(
        "rchd,schd->chrs",
        query.reshape(shape),
        keys.reshape(shape),
        preferred_element_type=f32,
    ) * HEAD_DIM ** (-0.5)
    scores = jnp.where(key_live > 0, scores, -jnp.inf)
    probs = softmax_last(scores).astype(bf16)
    context = jnp.einsum(
        "chrs,schd->rchd", probs, values.reshape(shape), preferred_element_type=f32
    )
    return context.astype(bf16).reshape(rows_all, count_cols, local_width)


def send_back(context):
    return lax.all_to_all(context[:, None], "seq", split_axis=0, concat_axis=1, tiled=True)


def general_body(ids, pad_mask, embed, row_qkv, row_out, col_qkv, col_out):
    rows_here, cols = ids.shape
    width = embed.shape[1]
    local_width = row_out.shape[0]
    heads_here = local_width // HEAD_DIM
    groups = lax.axis_size("seq")
    per_group = cols // groups
    codes = lax.broadcasted_iota(jnp.int32, (1, 1, embed.shape[0]), 2)
    onehot = (ids[:, :, None] == codes).astype(bf16)
    embedded = jnp.einsum("rcv,vd->rcd", onehot, embed, preferred_element_type=f32)
    normed = layer_norm(embedded).astype(bf16)
    row_proj = jnp.einsum("rcd,ted->trce", normed, row_qkv, preferred_element_type=f32)
    row_proj = row_proj.astype(bf16)
    live = pad_mask.astype(bf16)
    head_shape = (rows_here, cols, heads_here, HEAD_DIM)
    query = (row_proj[0] * live[:, None, None]).reshape(head_shape)
    keys = row_proj[1].reshape(head_shape)
    values = row_proj[2].reshape(head_shape)
    partial_scores = jnp.einsum("rihd,rjhd->hij", query, keys, preferred_element_type=f32)
    count_here = jnp.sum(pad_mask.astype(f32))
    scale = HEAD_DIM ** (-0.5)
    total, count = lax.psum((partial_scores, count_here), "seq")
    row_probs = softmax_last(total * (scale / jnp.sqrt(count))).astype(bf16)
    row_context = jnp.einsum("hij,rjhd->rihd", row_probs, values, preferred_element_type=f32)
    row_context = row_context.astype(bf16).reshape(rows_here, cols, local_width)
    start_feature = lax.axis_index("head") * local_width
    resident = lax.dynamic_slice_in_dim(embedded, start_feature, local_width, 2)
    row_update = weight_fold(row_out, lax.all_gather(row_context, "head", axis=2, tiled=True))
    mixed = resident + row_update
    sums, squares = lax.psum((jnp.sum(mixed, axis=-1), jnp.sum(mixed * mixed, axis=-1)), "head")
    mean = sums / width
    spread = squares / width - mean * mean
    normed_here = ((mixed - mean[..., None]) * lax.rsqrt(spread[..., None] + EPS)).astype(bf16)
    live_tile = jnp.broadcast_to(live[:, None, None, None], (rows_here, groups, per_group, 1))
    normed_full = lax.all_gather(normed_here, "head", axis=2, tiled=True)
    col_proj = jnp.einsum("rcd,ted->rcte", normed_full, col_qkv, preferred_element_type=f32)
    packed = col_proj.astype(bf16).reshape(rows_here, groups, per_group, 3 * local_width)
    received = lax.all_to_all(packed, "seq", split_axis=1, concat_axis=0, tiled=True)
    mask_part = lax.all_to_all(live_tile, "seq", split_axis=1, concat_axis=0, tiled=True)
    column_out = send_back(
        attend_columns(
            received[:, 0, :, :local_width],
            received[:, 0, :, local_width : 2 * local_width],
            received[:, 0, :, 2 * local_width :],
            mask_part[:, 0, 0, 0],
        )
    )
    column_out = column_out.reshape(rows_here, cols, local_width)
    col_update = weight_fold(col_out, lax.all_gather(column_out, "head", axis=2, tiled=True))
    return (mixed + col_update).astype(bf16)


def body(ids, pad_mask, embed, row_qkv, row_out, col_qkv, col_out):
    rows_here, cols = ids.shape
    groups = lax.axis_size("seq")
    own, rows = cols // groups, rows_here * groups
    parts = lax.axis_size("head")
    local = row_out.shape[0]
    fits = (
        parts == 4
        and groups >= 8
        and groups & (groups - 1) == 0
        and rows * 8 == LANES
        and rows_here == 2
        and own % 32 == 0
        and cols >= LANES
        and local == LANES + HEAD_DIM
        and embed.shape[0] <= TABLE_ROWS
    )
    chosen = fast_body if fits else general_body
    return chosen(ids, pad_mask, embed, row_qkv, row_out, col_qkv, col_out)


def solution(mesh):
    placed = (
        P("seq", None),
        P("seq"),
        P(),
        P(None, "head", None),
        P("head", None),
        P(None, "head", None),
        P("head", None),
    )
    return jax.shard_map(
        body, mesh=mesh, in_specs=placed, out_specs=P("seq", None, "head"), check_vma=False
    )
```

```python
import functools

import jax
import jax.numpy as jnp
from jax import lax
from jax.experimental import pallas as pl
from jax.experimental.pallas import tpu as pltpu
from jax.sharding import PartitionSpec as P

HEAD_DIM = 64
EPS = 1e-05
LANES = 128
CODES = 64
TABLE_ROWS = 40

SMALL_VMEM = 8 * 1024 * 1024
LARGE_VMEM = 32 * 1024 * 1024

f32 = jnp.float32
bf16 = jnp.bfloat16


def layer_norm(values):
    mean = jnp.mean(values, axis=-1, keepdims=True)
    centred = values - mean
    spread = jnp.mean(centred * centred, axis=-1, keepdims=True)
    return centred * lax.rsqrt(spread + EPS)


def softmax_last(scores):
    top = jnp.max(scores, axis=-1, keepdims=True)
    weights = jnp.exp(scores - top)
    return weights * (1.0 / jnp.sum(weights, axis=-1, keepdims=True))


def dot_nt(left, right):
    return lax.dot_general(left, right, (((1,), (1,)), ((), ())), preferred_element_type=f32)


def dot_nn(left, right):
    return jnp.dot(left, right, preferred_element_type=f32)


def in_hbm(value):
    return pltpu.with_memory_space_constraint(value, pltpu.HBM)


def iota(shape, axis):
    return lax.broadcasted_iota(jnp.int32, shape, axis)


def join_kernel(rows, own_ref, other_ref, out_ref):
    own, other = own_ref[...], other_ref[...]
    both = jnp.concatenate([own[0:rows], other[0:rows]], 0)
    out_ref[...] = jnp.concatenate([both] * (own.shape[0] // (2 * rows)), 0)


def join(own, other, rows):
    return pl.pallas_call(
        functools.partial(join_kernel, rows),
        out_shape=jax.ShapeDtypeStruct(own.shape, own.dtype),
        compiler_params=pltpu.CompilerParams(vmem_limit_bytes=SMALL_VMEM),
        name="join",
    )(own, other)


def join_raw_kernel(own_ref, ids_ref, live_ref, out_ref):
    rows = ids_ref.shape[0]
    live = live_ref[...]
    other = ids_ref[...] + 65536 * jnp.concatenate(
        [jnp.broadcast_to(live[:, r : r + 1], (1, ids_ref.shape[1])) for r in range(rows)], 0
    )
    both = jnp.concatenate([own_ref[0:rows], other], 0)
    out_ref[...] = jnp.concatenate([both] * (out_ref.shape[0] // (2 * rows)), 0)


def join_raw(own, ids, pad_mask):
    return pl.pallas_call(
        join_raw_kernel,
        out_shape=jax.ShapeDtypeStruct(own.shape, own.dtype),
        compiler_params=pltpu.CompilerParams(vmem_limit_bytes=SMALL_VMEM),
        name="join_raw",
    )(own, ids, pad_mask)


def table_kernel(
    ids_hbm,
    live_hbm,
    embed_hbm,
    qkv_hbm,
    out_ref,
    coded_ref,
    ids_ref,
    live_ref,
    embed_ref,
    qkv_ref,
    padded_ref,
    sems,
):
    kinds = qkv_ref.shape[0]
    loads = [
        pltpu.make_async_copy(embed_hbm, embed_ref, sems.at[kinds]),
        pltpu.make_async_copy(ids_hbm, ids_ref, sems.at[kinds + 1]),
        pltpu.make_async_copy(live_hbm, live_ref, sems.at[kinds + 2]),
    ]
    loads += [
        pltpu.make_async_copy(qkv_hbm.at[t], qkv_ref.at[t], sems.at[t]) for t in range(kinds)
    ]
    for load in loads:
        load.start()
    padded_ref[...] = jnp.zeros(padded_ref.shape, f32)
    for load in loads[0:3]:
        load.wait()
    padded_ref[0 : embed_ref.shape[0], :] = embed_ref[...].astype(f32)
    normed = layer_norm(padded_ref[...]).astype(bf16)
    row = iota(ids_ref.shape, 0)
    live = jnp.zeros(ids_ref.shape, jnp.int32)
    for r in range(ids_ref.shape[0]):
        live = jnp.where(row == r, live_ref[r], live)
    coded = ids_ref[...] + 65536 * live
    coded_ref[...] = jnp.concatenate([coded] * (coded_ref.shape[0] // coded.shape[0]), 0)
    tables = []
    for t in range(kinds):
        loads[3 + t].wait()
        tables.append(dot_nt(normed, qkv_ref[t]))
    out_ref[...] = jnp.concatenate(tables, 1).astype(bf16)


def make_tables(ids, pad_mask, embed, row_qkv, height):
    kinds, local, width = row_qkv.shape
    return pl.pallas_call(
        table_kernel,
        out_shape=(
            jax.ShapeDtypeStruct((TABLE_ROWS, kinds * local), bf16),
            jax.ShapeDtypeStruct((height, ids.shape[1]), jnp.int32),
        ),
        in_specs=[pl.BlockSpec(memory_space=pltpu.HBM)] * 4,
        scratch_shapes=[
            pltpu.VMEM(ids.shape, jnp.int32),
            pltpu.SMEM(pad_mask.shape, jnp.int32),
            pltpu.VMEM(embed.shape, bf16),
            pltpu.VMEM(row_qkv.shape, bf16),
            pltpu.VMEM((TABLE_ROWS, width), f32),
            pltpu.SemaphoreType.DMA((kinds + 3,)),
        ],
        cost_estimate=pl.CostEstimate(
            flops=2 * 10**9, bytes_accessed=2 * row_qkv.size, transcendentals=0
        ),
        compiler_params=pltpu.CompilerParams(vmem_limit_bytes=SMALL_VMEM),
        name="tables",
    )(in_hbm(ids), in_hbm(pad_mask), in_hbm(embed), in_hbm(row_qkv))


def halves(pair):
    lane = iota(pair.shape, 1)
    zero = jnp.zeros_like(pair)
    return jnp.where(lane < HEAD_DIM, pair, zero), jnp.where(lane < HEAD_DIM, zero, pair)


def spread_pair(pair):
    first, second = halves(pair)
    zero = jnp.zeros_like(pair)
    return jnp.concatenate(
        [
            jnp.concatenate([first, zero], 1),
            jnp.concatenate([zero, first], 1),
            jnp.concatenate([second, zero], 1),
            jnp.concatenate([zero, second], 1),
        ],
        0,
    )


def double(block):
    zero = jnp.zeros_like(block)
    return jnp.concatenate(
        [jnp.concatenate([block, zero], 1), jnp.concatenate([zero, block], 1)], 0
    )


def one_hots(coded, group, hot_ref, own_ref, live_own_ref):
    depth, cols = hot_ref.shape
    rows = depth // CODES
    pairs = rows // 2
    own = own_ref.shape[0] // pairs
    ids = (coded & 0xFFFF).astype(f32)
    live = (coded[:, 0:LANES] >> 16).astype(f32)

    code = iota((CODES, cols), 0).astype(f32)
    for r in range(rows):
        hot = jnp.broadcast_to(ids[r : r + 1, :], (CODES, cols)) == code
        hot_ref[r * CODES : (r + 1) * CODES, :] = hot.astype(f32).astype(bf16)

    pick = (iota((own, cols), 1) == group * own + iota((own, cols), 0)).astype(f32).astype(bf16)
    mine = dot_nt(pick, ids.astype(bf16))
    lane = iota((own, LANES), 1)
    first_half = lane < CODES
    lane_code = jnp.where(first_half, lane, lane - CODES).astype(f32)
    for k in range(pairs):
        value = jnp.where(first_half, mine[:, 2 * k : 2 * k + 1], mine[:, 2 * k + 1 : 2 * k + 2])
        hot = (value == lane_code).astype(f32)
        alive = jnp.where(first_half, live[2 * k : 2 * k + 1, :], live[2 * k + 1 : 2 * k + 2, :])
        own_ref[k * own : (k + 1) * own, :] = hot.astype(bf16)
        live_own_ref[k * own : (k + 1) * own, :] = (hot * alive).astype(bf16)
    return live


def tied_sum(scores_ref, live_own_ref, hot_ref, sum_ref):
    heads = scores_ref.shape[0]
    own = sum_ref.shape[0] // heads
    depth = hot_ref.shape[0]
    pairs = depth // CODES // 2
    for h in range(heads):
        looked = dot_nn(live_own_ref[...], scores_ref[h]).astype(bf16)
        for piece in range(2):
            for k in range(pairs):
                to = piece * depth + k * LANES
                sum_ref[h * own : (h + 1) * own, to : to + LANES] = looked[
                    k * own : (k + 1) * own, piece * LANES : (piece + 1) * LANES
                ]
    return dot_nn(sum_ref[:, 0:depth], hot_ref[...]) + dot_nn(
        sum_ref[:, depth : 2 * depth], hot_ref[...]
    )


def near_kernel(parts, *refs):
    tables_refs, refs = refs[:parts], refs[parts:]
    (
        codes_ref,
        scores_ref,
        values_ref,
        tied_ref,
        hot_ref,
        own_ref,
        tables_ref,
        table_ref,
        live_own_ref,
        sum_ref,
    ) = refs
    width = values_ref.shape[1]
    heads = width // HEAD_DIM
    local = width // parts
    group = lax.axis_index("seq")
    part = lax.axis_index("head")
    for p in range(parts):
        tables_ref[part ^ p] = tables_refs[p][...]

    for t in range(3):
        to_ref = values_ref if t == 2 else table_ref.at[t]
        to_ref[0:TABLE_ROWS, :] = jnp.concatenate(
            [tables_ref[p, :, t * local : (t + 1) * local] for p in range(parts)], 1
        )
        to_ref[TABLE_ROWS:CODES, :] = jnp.zeros((CODES - TABLE_ROWS, width), bf16)

    spans = [slice(hp * LANES, (hp + 1) * LANES) for hp in range(heads // 2)]
    queries = [spread_pair(table_ref[0, :, span]) for span in spans]
    keys = [double(table_ref[1, :, span]) for span in spans]
    scores = [dot_nt(query, key) for query, key in zip(queries, keys)]
    high = [score.astype(bf16) for score in scores]
    low = [(score - part_of.astype(f32)).astype(bf16) for score, part_of in zip(scores, high)]
    for h in range(heads):
        these = slice(h % 2 * LANES, (h % 2 + 1) * LANES)
        scores_ref[h, :, 0:LANES] = high[h // 2][these]
        scores_ref[h, :, LANES : 2 * LANES] = low[h // 2][these]

    one_hots(codes_ref[...], group, hot_ref, own_ref, live_own_ref)
    tied_ref[...] = tied_sum(scores_ref, live_own_ref, hot_ref, sum_ref)


def attend_near(tables, codes, own):
    parts = len(tables)
    width = tables[0].shape[1] // 3 * parts
    heads = width // HEAD_DIM
    rows, cols = codes.shape
    return pl.pallas_call(
        functools.partial(near_kernel, parts),
        out_shape=(
            jax.ShapeDtypeStruct((heads, LANES, 2 * LANES), bf16),
            jax.ShapeDtypeStruct((CODES, width), bf16),
            jax.ShapeDtypeStruct((heads * own, cols), f32),
            jax.ShapeDtypeStruct((rows * CODES, cols), bf16),
            jax.ShapeDtypeStruct((rows // 2 * own, LANES), bf16),
        ),
        scratch_shapes=[
            pltpu.VMEM((parts,) + tables[0].shape, bf16),
            pltpu.VMEM((2, CODES, width), bf16),
            pltpu.VMEM((rows // 2 * own, LANES), bf16),
            pltpu.VMEM((heads * own, 2 * rows * CODES), bf16),
        ],
        cost_estimate=pl.CostEstimate(flops=10**9, bytes_accessed=10**6, transcendentals=0),
        compiler_params=pltpu.CompilerParams(vmem_limit_bytes=LARGE_VMEM),
        name="near_scores",
    )(*tables, codes)


def row_kernel(
    scores_ref,
    values_ref,
    near_tied_ref,
    near_hot_ref,
    near_codes_ref,
    far_codes_ref,
    row_context_ref,
    own_ref,
    live_ref,
    hot_ref,
    live_own_ref,
    sum_ref,
    spread_ref,
):
    depth = hot_ref.shape[0]
    rows = 2 * depth // CODES
    pairs = rows // 2
    width = row_context_ref.shape[1]
    heads = width // HEAD_DIM
    own = spread_ref.shape[0] // heads
    group = lax.axis_index("seq")

    live = one_hots(far_codes_ref[...], group, hot_ref, own_ref, live_own_ref)
    live = jnp.concatenate([(near_codes_ref[:, 0:LANES] >> 16).astype(f32), live], 0)
    live_ref[...] = live
    tied = near_tied_ref[...] + tied_sum(scores_ref, live_own_ref, hot_ref, sum_ref)
    count = jnp.sum(live, axis=0, keepdims=True)[:, 0:1]
    probs = softmax_last(tied * (HEAD_DIM ** (-0.5) / jnp.sqrt(count))).astype(bf16)

    spread_ref[:, 0:depth] = dot_nt(probs, near_hot_ref[...]).astype(bf16)
    spread_ref[:, depth : 2 * depth] = dot_nt(probs, hot_ref[...]).astype(bf16)
    spans = [slice(hp * LANES, (hp + 1) * LANES) for hp in range(heads // 2)]
    values = [spread_pair(values_ref[:, span]) for span in spans]
    contexts = []
    for hp in range(heads // 2):
        first = (hp * 2) * own
        weights = jnp.concatenate(
            [
                jnp.concatenate(
                    [
                        spread_ref[first : first + own, k * LANES : (k + 1) * LANES],
                        spread_ref[first + own : first + 2 * own, k * LANES : (k + 1) * LANES],
                    ],
                    1,
                )
                for k in range(pairs)
            ],
            0,
        )
        contexts.append(dot_nn(weights, values[hp]).astype(bf16))
    for hp in range(heads // 2):
        for k in range(pairs):
            for r2 in range(2):
                at = (2 * k + r2) * own
                row_context_ref[at : at + own, spans[hp]] = contexts[hp][
                    k * own : (k + 1) * own, r2 * LANES : (r2 + 1) * LANES
                ]


def attend_rows(near, near_codes, far_codes, own):
    scores, values, near_tied, near_hot = near
    heads, width = scores.shape[0], values.shape[1]
    half, cols = near_codes.shape
    return pl.pallas_call(
        row_kernel,
        out_shape=(
            jax.ShapeDtypeStruct((2 * half * own, width), bf16),
            jax.ShapeDtypeStruct((half // 2 * own, LANES), bf16),
            jax.ShapeDtypeStruct((2 * half, LANES), f32),
        ),
        scratch_shapes=[
            pltpu.VMEM((half * CODES, cols), bf16),
            pltpu.VMEM((half // 2 * own, LANES), bf16),
            pltpu.VMEM((heads * own, 2 * half * CODES), bf16),
            pltpu.VMEM((heads * own, 2 * half * CODES), bf16),
        ],
        cost_estimate=pl.CostEstimate(flops=3 * 10**9, bytes_accessed=10**6, transcendentals=0),
        compiler_params=pltpu.CompilerParams(vmem_limit_bytes=LARGE_VMEM),
        name="row_attention",
    )(scores, values, near_tied, near_hot, near_codes, far_codes)


def column_kernel(parts, *refs):
    row_out_refs, refs = refs[:parts], refs[parts:]
    (
        live_ref,
        row_context_ref,
        near_own_ref,
        far_own_ref,
        embed_ref,
        col_qkv_ref,
        *context_refs,
        mixed_out_ref,
        row_out_ref,
        embed2_ref,
        weight_ref,
    ) = refs
    rows = live_ref.shape[0]
    tokens, width = row_context_ref.shape
    pairs = rows // 2
    own = tokens // rows
    vocab = embed_ref.shape[0]
    local = width // parts
    part = lax.axis_index("head")

    for p in range(parts):
        row_out_ref[part ^ p] = row_out_refs[p][...]
    embed2_ref[...] = jnp.zeros(embed2_ref.shape, bf16)
    embed2_ref[0:vocab, 0:width] = embed_ref[...]
    embed2_ref[CODES : CODES + vocab, width : 2 * width] = embed_ref[...]

    own_codes = jnp.concatenate([near_own_ref[...], far_own_ref[...]], 0)
    embedded2 = dot_nn(own_codes, embed2_ref[...])
    embedded = jnp.concatenate(
        [
            embedded2[k * own : (k + 1) * own, r2 * width : (r2 + 1) * width]
            for k in range(pairs)
            for r2 in range(2)
        ],
        0,
    )
    mixed = embedded + dot_nt(row_context_ref[...], row_out_ref[...].reshape(width, width))
    for p in range(parts):

        @pl.when(part == p)
        def _():
            mixed_out_ref[...] = mixed[:, p * local : (p + 1) * local]

    normed = layer_norm(mixed).astype(bf16)

    few = 8
    groups = own // few
    unit = rows * few

    def regroup(values):
        shape = (rows, groups, few, values.shape[1])
        return jnp.swapaxes(values.reshape(shape), 0, 1).reshape(tokens, values.shape[1])

    odd = part % 2
    for t in range(3):
        first = pl.multiple_of(t * local + odd * HEAD_DIM, HEAD_DIM)
        last = pl.multiple_of(t * local + (1 - odd) * LANES, HEAD_DIM)
        third = (3 + t) * LANES
        weight_ref[t * LANES : (t + 1) * LANES, :] = col_qkv_ref[pl.ds(first, LANES), :]
        weight_ref[third : third + HEAD_DIM, :] = col_qkv_ref[pl.ds(last, HEAD_DIM), :]
        weight_ref[third + HEAD_DIM : third + LANES, :] = jnp.zeros((HEAD_DIM, width), bf16)
    proj = [
        dot_nt(normed, weight_ref[2 * j * LANES : 2 * (j + 1) * LANES, :]) for j in range(3)
    ]
    proj = [
        proj[j][:, k * LANES : (k + 1) * LANES] * (HEAD_DIM ** (-0.5) if (2 * j + k) % 3 == 0 else 1.0)
        for j in range(3)
        for k in range(2)
    ]
    proj = [regroup(values).astype(bf16) for values in proj]
    sub, lan = iota((unit, unit), 0), iota((unit, unit), 1)
    same_column = (sub % few) == (lan % few)
    seq_of_lane = iota((rows, unit), 1) // few
    live_lane = jnp.sum(
        jnp.where(seq_of_lane == iota((rows, unit), 0), live_ref[...], 0.0), axis=0, keepdims=True
    )
    visible = jnp.logical_and(same_column, jnp.broadcast_to(live_lane, (unit, unit)) > 0)
    chosen = []
    for g in range(groups):
        at = slice(g * unit, (g + 1) * unit)
        query, keys, values = (proj[t][at] for t in range(3))
        chosen += [(half, keys, values) for half in halves(query)]
        chosen.append(tuple(proj[3 + t][at] for t in range(3)))
    scores = [jnp.where(visible, dot_nt(query, keys), -jnp.inf) for query, keys, _ in chosen]
    tops = [jnp.max(score, axis=-1, keepdims=True) for score in scores]
    weights = [jnp.exp(score - top) for score, top in zip(scores, tops)]
    shares = [1.0 / jnp.sum(weight, axis=-1, keepdims=True) for weight in weights]
    probs = [(weight * share).astype(bf16) for weight, share in zip(weights, shares)]
    found = [dot_nn(prob, values) for prob, (_, _, values) in zip(probs, chosen)]
    first_head = iota((unit, LANES), 1) < HEAD_DIM

    def ungroup(blocks):
        whole = jnp.concatenate(blocks, 0).reshape(groups, rows, few, LANES)
        return jnp.swapaxes(whole, 0, 1).reshape(tokens, LANES)

    main = ungroup(
        [jnp.where(first_head, found[3 * g], found[3 * g + 1]) for g in range(groups)]
    )
    third = ungroup([found[3 * g + 2] for g in range(groups)])
    start = 0
    for context_ref in context_refs:
        count = context_ref.shape[0] * 2 // 3
        some = count // 2
        context_ref[0:count, :] = main[start : start + count].astype(bf16)
        early = third[start : start + some]
        late = third[start + some : start + count]
        left = jnp.where(odd == 1, late, early)
        right = jnp.where(odd == 1, early, late)
        context_ref[count : count + some, :] = jnp.concatenate(
            [left[:, 0:HEAD_DIM], right[:, 0:HEAD_DIM]], 1
        ).astype(bf16)
        start += count


def attend_columns_here(row_outs, live, row_context, near_own, far_own, embed, col_qkv):
    parts = len(row_outs)
    tokens, width = row_context.shape
    local = width // parts
    half = tokens // 2 * local // LANES
    return pl.pallas_call(
        functools.partial(column_kernel, parts),
        out_shape=(
            jax.ShapeDtypeStruct((half, LANES), bf16),
            jax.ShapeDtypeStruct((half, LANES), bf16),
            jax.ShapeDtypeStruct((tokens, local), f32),
        ),
        scratch_shapes=[
            pltpu.VMEM((parts, local, width), bf16),
            pltpu.VMEM((2 * CODES, 2 * width), bf16),
            pltpu.VMEM((6 * LANES, width), bf16),
        ],
        cost_estimate=pl.CostEstimate(flops=2 * 10**9, bytes_accessed=10**6, transcendentals=0),
        compiler_params=pltpu.CompilerParams(vmem_limit_bytes=LARGE_VMEM),
        name="column_attention",
    )(*row_outs, live, row_context, near_own, far_own, embed, col_qkv)


def finish_kernel(parts, groups, *refs):
    context_refs = [refs[:parts], refs[parts : 2 * parts]]
    mixed_ref, col_out_ref, out_ref, context_ref = refs[2 * parts :]
    tokens, local = mixed_ref.shape
    group = lax.axis_index("seq")
    part = lax.axis_index("head")
    starts = [0, context_refs[0][0].shape[0]]
    for start, some_refs in zip(starts, context_refs):
        for p in range(parts):
            context_ref[part ^ p, start : start + some_refs[p].shape[0], :] = some_refs[p][...]
    pieces = []
    for start, some_refs in zip(starts, context_refs):
        count = some_refs[0].shape[0] * 2 // 3
        end = start + some_refs[0].shape[0]
        low = iota((count // 2, LANES), 1) < HEAD_DIM
        features = []
        for p in range(0, parts, 2):
            even = context_ref[p, start + count : end, :]
            other = context_ref[p + 1, start + count : end, :]
            early = jnp.where(low, even, other)
            late = jnp.where(low, other, even)
            late = jnp.concatenate([late[:, HEAD_DIM:], late[:, 0:HEAD_DIM]], 1)
            features += [
                context_ref[p, start : start + count, :],
                jnp.concatenate([early, late], 0),
                context_ref[p + 1, start : start + count, :],
            ]
        pieces.append(jnp.concatenate(features, 1))
    total = mixed_ref[...] + dot_nt(jnp.concatenate(pieces, 0), col_out_ref[...])
    own = tokens // groups // 2
    for d in range(groups):
        first, second = (total[(2 * d + r) * own : (2 * d + r + 1) * own, :] for r in range(2))
        rest = jnp.concatenate([first[:, LANES:local], second[:, LANES:local]], 1)
        out_ref[group ^ d] = jnp.concatenate(
            [first[:, 0:LANES], second[:, 0:LANES], rest], 0
        ).astype(bf16)


def finish(contexts, mixed, col_out, groups):
    parts = len(contexts[0])
    tokens, local = mixed.shape
    return pl.pallas_call(
        functools.partial(finish_kernel, parts, groups),
        out_shape=jax.ShapeDtypeStruct((groups, tokens // groups * local // LANES, LANES), bf16),
        scratch_shapes=[pltpu.VMEM((parts, tokens * local // LANES, LANES), bf16)],
        compiler_params=pltpu.CompilerParams(vmem_limit_bytes=LARGE_VMEM),
        name="finish",
    )(*contexts[0], *contexts[1], mixed, col_out)


def order_kernel(blocks_ref, out_ref):
    groups = blocks_ref.shape[0]
    local, cols = out_ref.shape[1:]
    own = cols // groups
    rest = local - LANES
    for part in range(3):
        piece = jnp.concatenate(
            [blocks_ref[g, part * own : (part + 1) * own, :] for g in range(groups)], 0
        )
        turned = piece.astype(f32).T.astype(bf16)
        if part < 2:
            out_ref[part, 0:LANES, :] = turned
        else:
            for r in range(2):
                out_ref[r, LANES:local, :] = turned[r * rest : (r + 1) * rest, :]


def order(blocks, cols, local):
    return pl.pallas_call(
        order_kernel,
        out_shape=jax.ShapeDtypeStruct((2, local, cols), bf16),
        compiler_params=pltpu.CompilerParams(vmem_limit_bytes=SMALL_VMEM),
        name="order",
    )(blocks)


def fast_body(ids, pad_mask, embed, row_qkv, row_out, col_qkv, col_out):
    rows_here, cols = ids.shape
    width = embed.shape[1]
    local = row_out.shape[0]
    groups, parts = lax.axis_size("seq"), lax.axis_size("head")
    own, rows = cols // groups, rows_here * groups

    def pairwise(value, partner):
        order = [(g, p) for g in range(groups) for p in range(parts)]
        link = [(g * parts + p, partner(g, p)) for g, p in order]
        return lax.ppermute(value, ("seq", "head"), [(i, g * parts + p) for i, (g, p) in link])

    def sibling(g, p):
        return g, p ^ 1

    def across(g, p):
        return g, p ^ 2

    def opposite(g, p):
        return g, p ^ 3

    far = pairwise(row_out, across)
    other_ids = pairwise(ids, lambda g, p: (g ^ 1, p))
    other_mask = pairwise(pad_mask.reshape(1, rows_here), lambda g, p: (g ^ 1, p))
    table, coded = make_tables(ids, pad_mask, embed, row_qkv, rows_here * groups // 2)
    tables = [table, None, pairwise(table, across), None]
    step = 2
    while step < groups:
        if step == 2:
            coded = join_raw(coded, other_ids, other_mask)
        else:
            coded = join(coded, received, rows_here * step // 2)
        if step == 2:
            coded, table = lax.optimization_barrier((coded, table))
            tables[3] = pairwise(table, opposite)
        elif step == 4:
            coded, table, row_out, far = lax.optimization_barrier((coded, table, row_out, far))
            tables[1] = pairwise(table, sibling)
            row_outs = [row_out, pairwise(row_out, sibling), far, pairwise(far, sibling)]
        received = pairwise(coded, lambda g, p, step=step: (g ^ step, p))
        step *= 2
    codes = (coded, received)
    *near_scores, near_own = attend_near(tables, codes[0], own)
    row_context, far_own, live = attend_rows(near_scores, *codes, own)
    *halves_here, mixed = attend_columns_here(
        row_outs,
        live,
        row_context,
        near_own,
        far_own,
        embed,
        col_qkv.reshape(3 * local, width),
    )
    contexts = []
    for context in halves_here:
        beyond = pairwise(context, across)
        contexts.append(
            (context, pairwise(context, sibling), beyond, pairwise(beyond, sibling))
        )
    blocks = finish(contexts, mixed, col_out, groups)
    blocks = lax.all_to_all(blocks, "seq", split_axis=0, concat_axis=0, tiled=True)
    return jnp.swapaxes(order(blocks, cols, local), 1, 2)


def weight_fold(out_weight, piece):
    return jnp.einsum("rce,fe->rcf", piece, out_weight, preferred_element_type=f32)


def attend_columns(query, keys, values, key_live):
    rows_all, count_cols, local_width = query.shape
    heads_here = local_width // HEAD_DIM
    shape = (rows_all, count_cols, heads_here, HEAD_DIM)
    scores = jnp.einsum(
        "rchd,schd->chrs",
        query.reshape(shape),
        keys.reshape(shape),
        preferred_element_type=f32,
    ) * HEAD_DIM ** (-0.5)
    scores = jnp.where(key_live > 0, scores, -jnp.inf)
    probs = softmax_last(scores).astype(bf16)
    context = jnp.einsum(
        "chrs,schd->rchd", probs, values.reshape(shape), preferred_element_type=f32
    )
    return context.astype(bf16).reshape(rows_all, count_cols, local_width)


def send_back(context):
    return lax.all_to_all(context[:, None], "seq", split_axis=0, concat_axis=1, tiled=True)


def general_body(ids, pad_mask, embed, row_qkv, row_out, col_qkv, col_out):
    rows_here, cols = ids.shape
    width = embed.shape[1]
    local_width = row_out.shape[0]
    heads_here = local_width // HEAD_DIM
    groups = lax.axis_size("seq")
    per_group = cols // groups
    codes = lax.broadcasted_iota(jnp.int32, (1, 1, embed.shape[0]), 2)
    onehot = (ids[:, :, None] == codes).astype(bf16)
    embedded = jnp.einsum("rcv,vd->rcd", onehot, embed, preferred_element_type=f32)
    normed = layer_norm(embedded).astype(bf16)
    row_proj = jnp.einsum("rcd,ted->trce", normed, row_qkv, preferred_element_type=f32)
    row_proj = row_proj.astype(bf16)
    live = pad_mask.astype(bf16)
    head_shape = (rows_here, cols, heads_here, HEAD_DIM)
    query = (row_proj[0] * live[:, None, None]).reshape(head_shape)
    keys = row_proj[1].reshape(head_shape)
    values = row_proj[2].reshape(head_shape)
    partial_scores = jnp.einsum("rihd,rjhd->hij", query, keys, preferred_element_type=f32)
    count_here = jnp.sum(pad_mask.astype(f32))
    scale = HEAD_DIM ** (-0.5)
    total, count = lax.psum((partial_scores, count_here), "seq")
    row_probs = softmax_last(total * (scale / jnp.sqrt(count))).astype(bf16)
    row_context = jnp.einsum("hij,rjhd->rihd", row_probs, values, preferred_element_type=f32)
    row_context = row_context.astype(bf16).reshape(rows_here, cols, local_width)
    start_feature = lax.axis_index("head") * local_width
    resident = lax.dynamic_slice_in_dim(embedded, start_feature, local_width, 2)
    row_update = weight_fold(row_out, lax.all_gather(row_context, "head", axis=2, tiled=True))
    mixed = resident + row_update
    sums, squares = lax.psum((jnp.sum(mixed, axis=-1), jnp.sum(mixed * mixed, axis=-1)), "head")
    mean = sums / width
    spread = squares / width - mean * mean
    normed_here = ((mixed - mean[..., None]) * lax.rsqrt(spread[..., None] + EPS)).astype(bf16)
    live_tile = jnp.broadcast_to(live[:, None, None, None], (rows_here, groups, per_group, 1))
    normed_full = lax.all_gather(normed_here, "head", axis=2, tiled=True)
    col_proj = jnp.einsum("rcd,ted->rcte", normed_full, col_qkv, preferred_element_type=f32)
    packed = col_proj.astype(bf16).reshape(rows_here, groups, per_group, 3 * local_width)
    received = lax.all_to_all(packed, "seq", split_axis=1, concat_axis=0, tiled=True)
    mask_part = lax.all_to_all(live_tile, "seq", split_axis=1, concat_axis=0, tiled=True)
    column_out = send_back(
        attend_columns(
            received[:, 0, :, :local_width],
            received[:, 0, :, local_width : 2 * local_width],
            received[:, 0, :, 2 * local_width :],
            mask_part[:, 0, 0, 0],
        )
    )
    column_out = column_out.reshape(rows_here, cols, local_width)
    col_update = weight_fold(col_out, lax.all_gather(column_out, "head", axis=2, tiled=True))
    return (mixed + col_update).astype(bf16)


def body(ids, pad_mask, embed, row_qkv, row_out, col_qkv, col_out):
    rows_here, cols = ids.shape
    groups = lax.axis_size("seq")
    own, rows = cols // groups, rows_here * groups
    parts = lax.axis_size("head")
    local = row_out.shape[0]
    fits = (
        parts == 4
        and groups >= 8
        and groups & (groups - 1) == 0
        and rows * 8 == LANES
        and rows_here == 2
        and own % 32 == 0
        and cols >= LANES
        and local == LANES + HEAD_DIM
        and embed.shape[0] <= TABLE_ROWS
    )
    chosen = fast_body if fits else general_body
    return chosen(ids, pad_mask, embed, row_qkv, row_out, col_qkv, col_out)


def solution(mesh):
    placed = (
        P("seq", None),
        P("seq"),
        P(),
        P(None, "head", None),
        P("head", None),
        P(None, "head", None),
        P("head", None),
    )
    return jax.shard_map(
        body, mesh=mesh, in_specs=placed, out_specs=P("seq", None, "head"), check_vma=False
    )
```

```python
import functools

import jax
import jax.numpy as jnp
from jax import lax
from jax.experimental import pallas as pl
from jax.experimental.pallas import tpu as pltpu
from jax.sharding import PartitionSpec as P

HEAD_DIM = 64
EPS = 1e-05
LANES = 128
CODES = 64
TABLE_ROWS = 40

SMALL_VMEM = 8 * 1024 * 1024
LARGE_VMEM = 32 * 1024 * 1024

f32 = jnp.float32
bf16 = jnp.bfloat16


def layer_norm(values):
    mean = jnp.mean(values, axis=-1, keepdims=True)
    centred = values - mean
    spread = jnp.mean(centred * centred, axis=-1, keepdims=True)
    return centred * lax.rsqrt(spread + EPS)


def softmax_last(scores):
    top = jnp.max(scores, axis=-1, keepdims=True)
    weights = jnp.exp(scores - top)
    return weights * (1.0 / jnp.sum(weights, axis=-1, keepdims=True))


def dot_nt(left, right):
    return lax.dot_general(left, right, (((1,), (1,)), ((), ())), preferred_element_type=f32)


def dot_nn(left, right):
    return jnp.dot(left, right, preferred_element_type=f32)


def in_hbm(value):
    return pltpu.with_memory_space_constraint(value, pltpu.HBM)


def iota(shape, axis):
    return lax.broadcasted_iota(jnp.int32, shape, axis)


def join_kernel(rows, own_ref, other_ref, out_ref):
    own, other = own_ref[...], other_ref[...]
    both = jnp.concatenate([own[0:rows], other[0:rows]], 0)
    out_ref[...] = jnp.concatenate([both] * (own.shape[0] // (2 * rows)), 0)


def join(own, other, rows):
    return pl.pallas_call(
        functools.partial(join_kernel, rows),
        out_shape=jax.ShapeDtypeStruct(own.shape, own.dtype),
        compiler_params=pltpu.CompilerParams(vmem_limit_bytes=SMALL_VMEM),
        name="join",
    )(own, other)


def join_raw_kernel(own_ref, ids_ref, live_ref, out_ref):
    rows = ids_ref.shape[0]
    live = live_ref[...]
    other = ids_ref[...] + 65536 * jnp.concatenate(
        [jnp.broadcast_to(live[:, r : r + 1], (1, ids_ref.shape[1])) for r in range(rows)], 0
    )
    both = jnp.concatenate([own_ref[0:rows], other], 0)
    out_ref[...] = jnp.concatenate([both] * (out_ref.shape[0] // (2 * rows)), 0)


def join_raw(own, ids, pad_mask):
    return pl.pallas_call(
        join_raw_kernel,
        out_shape=jax.ShapeDtypeStruct(own.shape, own.dtype),
        compiler_params=pltpu.CompilerParams(vmem_limit_bytes=SMALL_VMEM),
        name="join_raw",
    )(own, ids, pad_mask)


def table_kernel(
    ids_hbm,
    live_hbm,
    embed_hbm,
    qkv_hbm,
    out_ref,
    coded_ref,
    ids_ref,
    live_ref,
    embed_ref,
    qkv_ref,
    padded_ref,
    sems,
):
    kinds = qkv_ref.shape[0]
    loads = [
        pltpu.make_async_copy(embed_hbm, embed_ref, sems.at[kinds]),
        pltpu.make_async_copy(ids_hbm, ids_ref, sems.at[kinds + 1]),
        pltpu.make_async_copy(live_hbm, live_ref, sems.at[kinds + 2]),
    ]
    loads += [
        pltpu.make_async_copy(qkv_hbm.at[t], qkv_ref.at[t], sems.at[t]) for t in range(kinds)
    ]
    for load in loads:
        load.start()
    padded_ref[...] = jnp.zeros(padded_ref.shape, f32)
    for load in loads[0:3]:
        load.wait()
    padded_ref[0 : embed_ref.shape[0], :] = embed_ref[...].astype(f32)
    normed = layer_norm(padded_ref[...]).astype(bf16)
    row = iota(ids_ref.shape, 0)
    live = jnp.zeros(ids_ref.shape, jnp.int32)
    for r in range(ids_ref.shape[0]):
        live = jnp.where(row == r, live_ref[r], live)
    coded = ids_ref[...] + 65536 * live
    coded_ref[...] = jnp.concatenate([coded] * (coded_ref.shape[0] // coded.shape[0]), 0)
    tables = []
    for t in range(kinds):
        loads[3 + t].wait()
        tables.append(dot_nt(normed, qkv_ref[t]))
    out_ref[...] = jnp.concatenate(tables, 1).astype(bf16)


def make_tables(ids, pad_mask, embed, row_qkv, height):
    kinds, local, width = row_qkv.shape
    return pl.pallas_call(
        table_kernel,
        out_shape=(
            jax.ShapeDtypeStruct((TABLE_ROWS, kinds * local), bf16),
            jax.ShapeDtypeStruct((height, ids.shape[1]), jnp.int32),
        ),
        in_specs=[pl.BlockSpec(memory_space=pltpu.HBM)] * 4,
        scratch_shapes=[
            pltpu.VMEM(ids.shape, jnp.int32),
            pltpu.SMEM(pad_mask.shape, jnp.int32),
            pltpu.VMEM(embed.shape, bf16),
            pltpu.VMEM(row_qkv.shape, bf16),
            pltpu.VMEM((TABLE_ROWS, width), f32),
            pltpu.SemaphoreType.DMA((kinds + 3,)),
        ],
        cost_estimate=pl.CostEstimate(
            flops=2 * 10**9, bytes_accessed=2 * row_qkv.size, transcendentals=0
        ),
        compiler_params=pltpu.CompilerParams(vmem_limit_bytes=SMALL_VMEM),
        name="tables",
    )(in_hbm(ids), in_hbm(pad_mask), in_hbm(embed), in_hbm(row_qkv))


def halves(pair):
    lane = iota(pair.shape, 1)
    zero = jnp.zeros_like(pair)
    return jnp.where(lane < HEAD_DIM, pair, zero), jnp.where(lane < HEAD_DIM, zero, pair)


def spread_pair(pair):
    first, second = halves(pair)
    zero = jnp.zeros_like(pair)
    return jnp.concatenate(
        [
            jnp.concatenate([first, zero], 1),
            jnp.concatenate([zero, first], 1),
            jnp.concatenate([second, zero], 1),
            jnp.concatenate([zero, second], 1),
        ],
        0,
    )


def double(block):
    zero = jnp.zeros_like(block)
    return jnp.concatenate(
        [jnp.concatenate([block, zero], 1), jnp.concatenate([zero, block], 1)], 0
    )


def one_hots(coded, group, hot_ref, own_ref, live_own_ref):
    depth, cols = hot_ref.shape
    rows = depth // CODES
    pairs = rows // 2
    own = own_ref.shape[0] // pairs
    ids = (coded & 0xFFFF).astype(f32)
    live = (coded[:, 0:LANES] >> 16).astype(f32)

    code = iota((CODES, cols), 0).astype(f32)
    for r in range(rows):
        hot = jnp.broadcast_to(ids[r : r + 1, :], (CODES, cols)) == code
        hot_ref[r * CODES : (r + 1) * CODES, :] = hot.astype(f32).astype(bf16)

    pick = (iota((own, cols), 1) == group * own + iota((own, cols), 0)).astype(f32).astype(bf16)
    mine = dot_nt(pick, ids.astype(bf16))
    lane = iota((own, LANES), 1)
    first_half = lane < CODES
    lane_code = jnp.where(first_half, lane, lane - CODES).astype(f32)
    for k in range(pairs):
        value = jnp.where(first_half, mine[:, 2 * k : 2 * k + 1], mine[:, 2 * k + 1 : 2 * k + 2])
        hot = (value == lane_code).astype(f32)
        alive = jnp.where(first_half, live[2 * k : 2 * k + 1, :], live[2 * k + 1 : 2 * k + 2, :])
        own_ref[k * own : (k + 1) * own, :] = hot.astype(bf16)
        live_own_ref[k * own : (k + 1) * own, :] = (hot * alive).astype(bf16)
    return live


def tied_sum(scores_ref, live_own_ref, hot_ref, sum_ref):
    heads = scores_ref.shape[0]
    own = sum_ref.shape[0] // heads
    depth = hot_ref.shape[0]
    pairs = depth // CODES // 2
    for h in range(heads):
        looked = dot_nn(live_own_ref[...], scores_ref[h]).astype(bf16)
        for piece in range(2):
            for k in range(pairs):
                to = piece * depth + k * LANES
                sum_ref[h * own : (h + 1) * own, to : to + LANES] = looked[
                    k * own : (k + 1) * own, piece * LANES : (piece + 1) * LANES
                ]
    return dot_nn(sum_ref[:, 0:depth], hot_ref[...]) + dot_nn(
        sum_ref[:, depth : 2 * depth], hot_ref[...]
    )


def near_kernel(parts, *refs):
    tables_refs, refs = refs[:parts], refs[parts:]
    (
        codes_ref,
        scores_ref,
        values_ref,
        tied_ref,
        hot_ref,
        own_ref,
        tables_ref,
        table_ref,
        live_own_ref,
        sum_ref,
    ) = refs
    width = values_ref.shape[1]
    heads = width // HEAD_DIM
    local = width // parts
    group = lax.axis_index("seq")
    part = lax.axis_index("head")
    for p in range(parts):
        tables_ref[part ^ p] = tables_refs[p][...]

    for t in range(3):
        to_ref = values_ref if t == 2 else table_ref.at[t]
        to_ref[0:TABLE_ROWS, :] = jnp.concatenate(
            [tables_ref[p, :, t * local : (t + 1) * local] for p in range(parts)], 1
        )
        to_ref[TABLE_ROWS:CODES, :] = jnp.zeros((CODES - TABLE_ROWS, width), bf16)

    spans = [slice(hp * LANES, (hp + 1) * LANES) for hp in range(heads // 2)]
    queries = [spread_pair(table_ref[0, :, span]) for span in spans]
    keys = [double(table_ref[1, :, span]) for span in spans]
    scores = [dot_nt(query, key) for query, key in zip(queries, keys)]
    high = [score.astype(bf16) for score in scores]
    low = [(score - part_of.astype(f32)).astype(bf16) for score, part_of in zip(scores, high)]
    for h in range(heads):
        these = slice(h % 2 * LANES, (h % 2 + 1) * LANES)
        scores_ref[h, :, 0:LANES] = high[h // 2][these]
        scores_ref[h, :, LANES : 2 * LANES] = low[h // 2][these]

    one_hots(codes_ref[...], group, hot_ref, own_ref, live_own_ref)
    tied_ref[...] = tied_sum(scores_ref, live_own_ref, hot_ref, sum_ref)


def attend_near(tables, codes, own):
    parts = len(tables)
    width = tables[0].shape[1] // 3 * parts
    heads = width // HEAD_DIM
    rows, cols = codes.shape
    return pl.pallas_call(
        functools.partial(near_kernel, parts),
        out_shape=(
            jax.ShapeDtypeStruct((heads, LANES, 2 * LANES), bf16),
            jax.ShapeDtypeStruct((CODES, width), bf16),
            jax.ShapeDtypeStruct((heads * own, cols), f32),
            jax.ShapeDtypeStruct((rows * CODES, cols), bf16),
            jax.ShapeDtypeStruct((rows // 2 * own, LANES), bf16),
        ),
        scratch_shapes=[
            pltpu.VMEM((parts,) + tables[0].shape, bf16),
            pltpu.VMEM((2, CODES, width), bf16),
            pltpu.VMEM((rows // 2 * own, LANES), bf16),
            pltpu.VMEM((heads * own, 2 * rows * CODES), bf16),
        ],
        cost_estimate=pl.CostEstimate(flops=10**9, bytes_accessed=10**6, transcendentals=0),
        compiler_params=pltpu.CompilerParams(vmem_limit_bytes=LARGE_VMEM),
        name="near_scores",
    )(*tables, codes)


def row_kernel(
    scores_ref,
    values_ref,
    near_tied_ref,
    near_hot_ref,
    near_codes_ref,
    far_codes_ref,
    row_context_ref,
    own_ref,
    live_ref,
    hot_ref,
    live_own_ref,
    sum_ref,
    spread_ref,
):
    depth = hot_ref.shape[0]
    rows = 2 * depth // CODES
    pairs = rows // 2
    width = row_context_ref.shape[1]
    heads = width // HEAD_DIM
    own = spread_ref.shape[0] // heads
    group = lax.axis_index("seq")

    live = one_hots(far_codes_ref[...], group, hot_ref, own_ref, live_own_ref)
    live = jnp.concatenate([(near_codes_ref[:, 0:LANES] >> 16).astype(f32), live], 0)
    live_ref[...] = live
    tied = near_tied_ref[...] + tied_sum(scores_ref, live_own_ref, hot_ref, sum_ref)
    count = jnp.sum(live, axis=0, keepdims=True)[:, 0:1]
    probs = softmax_last(tied * (HEAD_DIM ** (-0.5) / jnp.sqrt(count))).astype(bf16)

    spread_ref[:, 0:depth] = dot_nt(probs, near_hot_ref[...]).astype(bf16)
    spread_ref[:, depth : 2 * depth] = dot_nt(probs, hot_ref[...]).astype(bf16)
    spans = [slice(hp * LANES, (hp + 1) * LANES) for hp in range(heads // 2)]
    values = [spread_pair(values_ref[:, span]) for span in spans]
    contexts = []
    for hp in range(heads // 2):
        first = (hp * 2) * own
        weights = jnp.concatenate(
            [
                jnp.concatenate(
                    [
                        spread_ref[first : first + own, k * LANES : (k + 1) * LANES],
                        spread_ref[first + own : first + 2 * own, k * LANES : (k + 1) * LANES],
                    ],
                    1,
                )
                for k in range(pairs)
            ],
            0,
        )
        contexts.append(dot_nn(weights, values[hp]).astype(bf16))
    for hp in range(heads // 2):
        for k in range(pairs):
            for r2 in range(2):
                at = (2 * k + r2) * own
                row_context_ref[at : at + own, spans[hp]] = contexts[hp][
                    k * own : (k + 1) * own, r2 * LANES : (r2 + 1) * LANES
                ]


def attend_rows(near, near_codes, far_codes, own):
    scores, values, near_tied, near_hot = near
    heads, width = scores.shape[0], values.shape[1]
    half, cols = near_codes.shape
    return pl.pallas_call(
        row_kernel,
        out_shape=(
            jax.ShapeDtypeStruct((2 * half * own, width), bf16),
            jax.ShapeDtypeStruct((half // 2 * own, LANES), bf16),
            jax.ShapeDtypeStruct((2 * half, LANES), f32),
        ),
        scratch_shapes=[
            pltpu.VMEM((half * CODES, cols), bf16),
            pltpu.VMEM((half // 2 * own, LANES), bf16),
            pltpu.VMEM((heads * own, 2 * half * CODES), bf16),
            pltpu.VMEM((heads * own, 2 * half * CODES), bf16),
        ],
        cost_estimate=pl.CostEstimate(flops=3 * 10**9, bytes_accessed=10**6, transcendentals=0),
        compiler_params=pltpu.CompilerParams(vmem_limit_bytes=LARGE_VMEM),
        name="row_attention",
    )(scores, values, near_tied, near_hot, near_codes, far_codes)


def column_kernel(parts, *refs):
    row_out_refs, refs = refs[:parts], refs[parts:]
    (
        live_ref,
        row_context_ref,
        near_own_ref,
        far_own_ref,
        embed_ref,
        col_qkv_ref,
        *context_refs,
        mixed_out_ref,
        row_out_ref,
        embed2_ref,
        weight_ref,
        mixed_ref,
    ) = refs
    rows = live_ref.shape[0]
    tokens, width = row_context_ref.shape
    pairs = rows // 2
    own = tokens // rows
    vocab = embed_ref.shape[0]
    local = width // parts
    part = lax.axis_index("head")

    for p in range(parts):
        row_out_ref[part ^ p] = row_out_refs[p][...]
    embed2_ref[...] = jnp.zeros(embed2_ref.shape, bf16)
    embed2_ref[0:vocab, 0:width] = embed_ref[...]
    embed2_ref[CODES : CODES + vocab, width : 2 * width] = embed_ref[...]

    own_codes = jnp.concatenate([near_own_ref[...], far_own_ref[...]], 0)
    embedded2 = dot_nn(own_codes, embed2_ref[...])
    embedded = jnp.concatenate(
        [
            embedded2[k * own : (k + 1) * own, r2 * width : (r2 + 1) * width]
            for k in range(pairs)
            for r2 in range(2)
        ],
        0,
    )
    row_out = row_out_ref[...].reshape(width, width)
    halves_at = [slice(c * tokens // 2, (c + 1) * tokens // 2) for c in range(2)]
    normed = []
    for at in halves_at:
        mixed = embedded[at] + dot_nt(row_context_ref[at, :], row_out)
        mixed_ref[at, :] = mixed
        normed.append(layer_norm(mixed).astype(bf16))

    few = 8
    groups = own // few
    unit = rows * few

    def regroup(values):
        shape = (rows, groups, few, values.shape[1])
        return jnp.swapaxes(values.reshape(shape), 0, 1).reshape(tokens, values.shape[1])

    odd = part % 2
    for t in range(3):
        first = pl.multiple_of(t * local + odd * HEAD_DIM, HEAD_DIM)
        last = pl.multiple_of(t * local + (1 - odd) * LANES, HEAD_DIM)
        third = (3 + t) * LANES
        weight_ref[t * LANES : (t + 1) * LANES, :] = col_qkv_ref[pl.ds(first, LANES), :]
        weight_ref[third : third + HEAD_DIM, :] = col_qkv_ref[pl.ds(last, HEAD_DIM), :]
        weight_ref[third + HEAD_DIM : third + LANES, :] = jnp.zeros((HEAD_DIM, width), bf16)
    proj = [
        jnp.concatenate(
            [dot_nt(part_of, weight_ref[2 * j * LANES : 2 * (j + 1) * LANES, :]) for part_of in normed],
            0,
        )
        for j in range(3)
    ]
    proj = [
        proj[j][:, k * LANES : (k + 1) * LANES] * (HEAD_DIM ** (-0.5) if (2 * j + k) % 3 == 0 else 1.0)
        for j in range(3)
        for k in range(2)
    ]
    proj = [regroup(values).astype(bf16) for values in proj]
    sub, lan = iota((unit, unit), 0), iota((unit, unit), 1)
    same_column = (sub % few) == (lan % few)
    seq_of_lane = iota((rows, unit), 1) // few
    live_lane = jnp.sum(
        jnp.where(seq_of_lane == iota((rows, unit), 0), live_ref[...], 0.0), axis=0, keepdims=True
    )
    visible = jnp.logical_and(same_column, jnp.broadcast_to(live_lane, (unit, unit)) > 0)
    chosen = []
    for g in range(groups):
        at = slice(g * unit, (g + 1) * unit)
        query, keys, values = (proj[t][at] for t in range(3))
        chosen += [(half, keys, values) for half in halves(query)]
        chosen.append(tuple(proj[3 + t][at] for t in range(3)))
    scores = [jnp.where(visible, dot_nt(query, keys), -jnp.inf) for query, keys, _ in chosen]
    tops = [jnp.max(score, axis=-1, keepdims=True) for score in scores]
    weights = [jnp.exp(score - top) for score, top in zip(scores, tops)]
    shares = [1.0 / jnp.sum(weight, axis=-1, keepdims=True) for weight in weights]
    probs = [(weight * share).astype(bf16) for weight, share in zip(weights, shares)]
    found = [dot_nn(prob, values) for prob, (_, _, values) in zip(probs, chosen)]
    first_head = iota((unit, LANES), 1) < HEAD_DIM

    def ungroup(blocks):
        whole = jnp.concatenate(blocks, 0).reshape(groups, rows, few, LANES)
        return jnp.swapaxes(whole, 0, 1).reshape(tokens, LANES)

    main = ungroup(
        [jnp.where(first_head, found[3 * g], found[3 * g + 1]) for g in range(groups)]
    )
    third = ungroup([found[3 * g + 2] for g in range(groups)])
    start = 0
    for context_ref in context_refs:
        count = context_ref.shape[0] * 2 // 3
        some = count // 2
        context_ref[0:count, :] = main[start : start + count].astype(bf16)
        early = third[start : start + some]
        late = third[start + some : start + count]
        left = jnp.where(odd == 1, late, early)
        right = jnp.where(odd == 1, early, late)
        context_ref[count : count + some, :] = jnp.concatenate(
            [left[:, 0:HEAD_DIM], right[:, 0:HEAD_DIM]], 1
        ).astype(bf16)
        start += count
    for p in range(parts):

        @pl.when(part == p)
        def _():
            mixed_out_ref[...] = mixed_ref[:, p * local : (p + 1) * local]


def attend_columns_here(row_outs, live, row_context, near_own, far_own, embed, col_qkv):
    parts = len(row_outs)
    tokens, width = row_context.shape
    local = width // parts
    half = tokens // 2 * local // LANES
    return pl.pallas_call(
        functools.partial(column_kernel, parts),
        out_shape=(
            jax.ShapeDtypeStruct((half, LANES), bf16),
            jax.ShapeDtypeStruct((half, LANES), bf16),
            jax.ShapeDtypeStruct((tokens, local), f32),
        ),
        scratch_shapes=[
            pltpu.VMEM((parts, local, width), bf16),
            pltpu.VMEM((2 * CODES, 2 * width), bf16),
            pltpu.VMEM((6 * LANES, width), bf16),
            pltpu.VMEM((tokens, width), f32),
        ],
        cost_estimate=pl.CostEstimate(flops=2 * 10**9, bytes_accessed=10**6, transcendentals=0),
        compiler_params=pltpu.CompilerParams(vmem_limit_bytes=LARGE_VMEM),
        name="column_attention",
    )(*row_outs, live, row_context, near_own, far_own, embed, col_qkv)


def finish_kernel(parts, groups, *refs):
    context_refs = [refs[:parts], refs[parts : 2 * parts]]
    mixed_ref, col_out_ref, out_ref, context_ref = refs[2 * parts :]
    tokens, local = mixed_ref.shape
    group = lax.axis_index("seq")
    part = lax.axis_index("head")
    starts = [0, context_refs[0][0].shape[0]]
    for start, some_refs in zip(starts, context_refs):
        for p in range(parts):
            context_ref[part ^ p, start : start + some_refs[p].shape[0], :] = some_refs[p][...]
    pieces = []
    for start, some_refs in zip(starts, context_refs):
        count = some_refs[0].shape[0] * 2 // 3
        end = start + some_refs[0].shape[0]
        low = iota((count // 2, LANES), 1) < HEAD_DIM
        features = []
        for p in range(0, parts, 2):
            even = context_ref[p, start + count : end, :]
            other = context_ref[p + 1, start + count : end, :]
            early = jnp.where(low, even, other)
            late = jnp.where(low, other, even)
            late = jnp.concatenate([late[:, HEAD_DIM:], late[:, 0:HEAD_DIM]], 1)
            features += [
                context_ref[p, start : start + count, :],
                jnp.concatenate([early, late], 0),
                context_ref[p + 1, start : start + count, :],
            ]
        pieces.append(jnp.concatenate(features, 1))
    total = mixed_ref[...] + dot_nt(jnp.concatenate(pieces, 0), col_out_ref[...])
    own = tokens // groups // 2
    for d in range(groups):
        first, second = (total[(2 * d + r) * own : (2 * d + r + 1) * own, :] for r in range(2))
        rest = jnp.concatenate([first[:, LANES:local], second[:, LANES:local]], 1)
        out_ref[group ^ d] = jnp.concatenate(
            [first[:, 0:LANES], second[:, 0:LANES], rest], 0
        ).astype(bf16)


def finish(contexts, mixed, col_out, groups):
    parts = len(contexts[0])
    tokens, local = mixed.shape
    return pl.pallas_call(
        functools.partial(finish_kernel, parts, groups),
        out_shape=jax.ShapeDtypeStruct((groups, tokens // groups * local // LANES, LANES), bf16),
        scratch_shapes=[pltpu.VMEM((parts, tokens * local // LANES, LANES), bf16)],
        compiler_params=pltpu.CompilerParams(vmem_limit_bytes=LARGE_VMEM),
        name="finish",
    )(*contexts[0], *contexts[1], mixed, col_out)


def order_kernel(blocks_ref, out_ref):
    groups = blocks_ref.shape[0]
    local, cols = out_ref.shape[1:]
    own = cols // groups
    rest = local - LANES
    for part in range(3):
        piece = jnp.concatenate(
            [blocks_ref[g, part * own : (part + 1) * own, :] for g in range(groups)], 0
        )
        turned = piece.astype(f32).T.astype(bf16)
        if part < 2:
            out_ref[part, 0:LANES, :] = turned
        else:
            for r in range(2):
                out_ref[r, LANES:local, :] = turned[r * rest : (r + 1) * rest, :]


def order(blocks, cols, local):
    return pl.pallas_call(
        order_kernel,
        out_shape=jax.ShapeDtypeStruct((2, local, cols), bf16),
        compiler_params=pltpu.CompilerParams(vmem_limit_bytes=SMALL_VMEM),
        name="order",
    )(blocks)


def fast_body(ids, pad_mask, embed, row_qkv, row_out, col_qkv, col_out):
    rows_here, cols = ids.shape
    width = embed.shape[1]
    local = row_out.shape[0]
    groups, parts = lax.axis_size("seq"), lax.axis_size("head")
    own, rows = cols // groups, rows_here * groups

    def pairwise(value, partner):
        order = [(g, p) for g in range(groups) for p in range(parts)]
        link = [(g * parts + p, partner(g, p)) for g, p in order]
        return lax.ppermute(value, ("seq", "head"), [(i, g * parts + p) for i, (g, p) in link])

    def sibling(g, p):
        return g, p ^ 1

    def across(g, p):
        return g, p ^ 2

    def opposite(g, p):
        return g, p ^ 3

    far = pairwise(row_out, across)
    other_ids = pairwise(ids, lambda g, p: (g ^ 1, p))
    other_mask = pairwise(pad_mask.reshape(1, rows_here), lambda g, p: (g ^ 1, p))
    table, coded = make_tables(ids, pad_mask, embed, row_qkv, rows_here * groups // 2)
    tables = [table, None, pairwise(table, across), None]
    step = 2
    while step < groups:
        if step == 2:
            coded = join_raw(coded, other_ids, other_mask)
        else:
            coded = join(coded, received, rows_here * step // 2)
        if step == 2:
            coded, table = lax.optimization_barrier((coded, table))
            tables[3] = pairwise(table, opposite)
        elif step == 4:
            coded, table, row_out, far = lax.optimization_barrier((coded, table, row_out, far))
            tables[1] = pairwise(table, sibling)
            row_outs = [row_out, pairwise(row_out, sibling), far, pairwise(far, sibling)]
        received = pairwise(coded, lambda g, p, step=step: (g ^ step, p))
        step *= 2
    codes = (coded, received)
    *near_scores, near_own = attend_near(tables, codes[0], own)
    row_context, far_own, live = attend_rows(near_scores, *codes, own)
    *halves_here, mixed = attend_columns_here(
        row_outs,
        live,
        row_context,
        near_own,
        far_own,
        embed,
        col_qkv.reshape(3 * local, width),
    )
    contexts = []
    for context in halves_here:
        beyond = pairwise(context, across)
        contexts.append(
            (context, pairwise(context, sibling), beyond, pairwise(beyond, sibling))
        )
    blocks = finish(contexts, mixed, col_out, groups)
    blocks = lax.all_to_all(blocks, "seq", split_axis=0, concat_axis=0, tiled=True)
    return jnp.swapaxes(order(blocks, cols, local), 1, 2)


def weight_fold(out_weight, piece):
    return jnp.einsum("rce,fe->rcf", piece, out_weight, preferred_element_type=f32)


def attend_columns(query, keys, values, key_live):
    rows_all, count_cols, local_width = query.shape
    heads_here = local_width // HEAD_DIM
    shape = (rows_all, count_cols, heads_here, HEAD_DIM)
    scores = jnp.einsum(
        "rchd,schd->chrs",
        query.reshape(shape),
        keys.reshape(shape),
        preferred_element_type=f32,
    ) * HEAD_DIM ** (-0.5)
    scores = jnp.where(key_live > 0, scores, -jnp.inf)
    probs = softmax_last(scores).astype(bf16)
    context = jnp.einsum(
        "chrs,schd->rchd", probs, values.reshape(shape), preferred_element_type=f32
    )
    return context.astype(bf16).reshape(rows_all, count_cols, local_width)


def send_back(context):
    return lax.all_to_all(context[:, None], "seq", split_axis=0, concat_axis=1, tiled=True)


def general_body(ids, pad_mask, embed, row_qkv, row_out, col_qkv, col_out):
    rows_here, cols = ids.shape
    width = embed.shape[1]
    local_width = row_out.shape[0]
    heads_here = local_width // HEAD_DIM
    groups = lax.axis_size("seq")
    per_group = cols // groups
    codes = lax.broadcasted_iota(jnp.int32, (1, 1, embed.shape[0]), 2)
    onehot = (ids[:, :, None] == codes).astype(bf16)
    embedded = jnp.einsum("rcv,vd->rcd", onehot, embed, preferred_element_type=f32)
    normed = layer_norm(embedded).astype(bf16)
    row_proj = jnp.einsum("rcd,ted->trce", normed, row_qkv, preferred_element_type=f32)
    row_proj = row_proj.astype(bf16)
    live = pad_mask.astype(bf16)
    head_shape = (rows_here, cols, heads_here, HEAD_DIM)
    query = (row_proj[0] * live[:, None, None]).reshape(head_shape)
    keys = row_proj[1].reshape(head_shape)
    values = row_proj[2].reshape(head_shape)
    partial_scores = jnp.einsum("rihd,rjhd->hij", query, keys, preferred_element_type=f32)
    count_here = jnp.sum(pad_mask.astype(f32))
    scale = HEAD_DIM ** (-0.5)
    total, count = lax.psum((partial_scores, count_here), "seq")
    row_probs = softmax_last(total * (scale / jnp.sqrt(count))).astype(bf16)
    row_context = jnp.einsum("hij,rjhd->rihd", row_probs, values, preferred_element_type=f32)
    row_context = row_context.astype(bf16).reshape(rows_here, cols, local_width)
    start_feature = lax.axis_index("head") * local_width
    resident = lax.dynamic_slice_in_dim(embedded, start_feature, local_width, 2)
    row_update = weight_fold(row_out, lax.all_gather(row_context, "head", axis=2, tiled=True))
    mixed = resident + row_update
    sums, squares = lax.psum((jnp.sum(mixed, axis=-1), jnp.sum(mixed * mixed, axis=-1)), "head")
    mean = sums / width
    spread = squares / width - mean * mean
    normed_here = ((mixed - mean[..., None]) * lax.rsqrt(spread[..., None] + EPS)).astype(bf16)
    live_tile = jnp.broadcast_to(live[:, None, None, None], (rows_here, groups, per_group, 1))
    normed_full = lax.all_gather(normed_here, "head", axis=2, tiled=True)
    col_proj = jnp.einsum("rcd,ted->rcte", normed_full, col_qkv, preferred_element_type=f32)
    packed = col_proj.astype(bf16).reshape(rows_here, groups, per_group, 3 * local_width)
    received = lax.all_to_all(packed, "seq", split_axis=1, concat_axis=0, tiled=True)
    mask_part = lax.all_to_all(live_tile, "seq", split_axis=1, concat_axis=0, tiled=True)
    column_out = send_back(
        attend_columns(
            received[:, 0, :, :local_width],
            received[:, 0, :, local_width : 2 * local_width],
            received[:, 0, :, 2 * local_width :],
            mask_part[:, 0, 0, 0],
        )
    )
    column_out = column_out.reshape(rows_here, cols, local_width)
    col_update = weight_fold(col_out, lax.all_gather(column_out, "head", axis=2, tiled=True))
    return (mixed + col_update).astype(bf16)


def body(ids, pad_mask, embed, row_qkv, row_out, col_qkv, col_out):
    rows_here, cols = ids.shape
    groups = lax.axis_size("seq")
    own, rows = cols // groups, rows_here * groups
    parts = lax.axis_size("head")
    local = row_out.shape[0]
    fits = (
        parts == 4
        and groups >= 8
        and groups & (groups - 1) == 0
        and rows * 8 == LANES
        and rows_here == 2
        and own % 32 == 0
        and cols >= LANES
        and local == LANES + HEAD_DIM
        and embed.shape[0] <= TABLE_ROWS
    )
    chosen = fast_body if fits else general_body
    return chosen(ids, pad_mask, embed, row_qkv, row_out, col_qkv, col_out)


def solution(mesh):
    placed = (
        P("seq", None),
        P("seq"),
        P(),
        P(None, "head", None),
        P("head", None),
        P(None, "head", None),
        P("head", None),
    )
    return jax.shard_map(
        body, mesh=mesh, in_specs=placed, out_specs=P("seq", None, "head"), check_vma=False
    )
```

```python
import functools

import jax
import jax.numpy as jnp
from jax import lax
from jax.experimental import pallas as pl
from jax.experimental.pallas import tpu as pltpu
from jax.sharding import PartitionSpec as P

HEAD_DIM = 64
EPS = 1e-05
LANES = 128
CODES = 64
TABLE_ROWS = 40

SMALL_VMEM = 8 * 1024 * 1024
LARGE_VMEM = 32 * 1024 * 1024

f32 = jnp.float32
bf16 = jnp.bfloat16


def layer_norm(values):
    mean = jnp.mean(values, axis=-1, keepdims=True)
    centred = values - mean
    spread = jnp.mean(centred * centred, axis=-1, keepdims=True)
    return centred * lax.rsqrt(spread + EPS)


def softmax_last(scores):
    top = jnp.max(scores, axis=-1, keepdims=True)
    weights = jnp.exp(scores - top)
    return weights * (1.0 / jnp.sum(weights, axis=-1, keepdims=True))


def dot_nt(left, right):
    return lax.dot_general(left, right, (((1,), (1,)), ((), ())), preferred_element_type=f32)


def dot_nn(left, right):
    return jnp.dot(left, right, preferred_element_type=f32)


def in_hbm(value):
    return pltpu.with_memory_space_constraint(value, pltpu.HBM)


def iota(shape, axis):
    return lax.broadcasted_iota(jnp.int32, shape, axis)


def join_kernel(rows, own_ref, other_ref, out_ref):
    own, other = own_ref[...], other_ref[...]
    both = jnp.concatenate([own[0:rows], other[0:rows]], 0)
    out_ref[...] = jnp.concatenate([both] * (own.shape[0] // (2 * rows)), 0)


def join(own, other, rows):
    return pl.pallas_call(
        functools.partial(join_kernel, rows),
        out_shape=jax.ShapeDtypeStruct(own.shape, own.dtype),
        compiler_params=pltpu.CompilerParams(vmem_limit_bytes=SMALL_VMEM),
        name="join",
    )(own, other)


def join_raw_kernel(own_ref, ids_ref, live_ref, out_ref):
    rows = ids_ref.shape[0]
    live = live_ref[...]
    other = ids_ref[...] + 65536 * jnp.concatenate(
        [jnp.broadcast_to(live[:, r : r + 1], (1, ids_ref.shape[1])) for r in range(rows)], 0
    )
    both = jnp.concatenate([own_ref[0:rows], other], 0)
    out_ref[...] = jnp.concatenate([both] * (out_ref.shape[0] // (2 * rows)), 0)


def join_raw(own, ids, pad_mask):
    return pl.pallas_call(
        join_raw_kernel,
        out_shape=jax.ShapeDtypeStruct(own.shape, own.dtype),
        compiler_params=pltpu.CompilerParams(vmem_limit_bytes=SMALL_VMEM),
        name="join_raw",
    )(own, ids, pad_mask)


def table_kernel(
    ids_hbm,
    live_hbm,
    embed_hbm,
    qkv_hbm,
    out_ref,
    coded_ref,
    ids_ref,
    live_ref,
    embed_ref,
    qkv_ref,
    padded_ref,
    sems,
):
    kinds = qkv_ref.shape[0]
    loads = [
        pltpu.make_async_copy(embed_hbm, embed_ref, sems.at[kinds]),
        pltpu.make_async_copy(ids_hbm, ids_ref, sems.at[kinds + 1]),
        pltpu.make_async_copy(live_hbm, live_ref, sems.at[kinds + 2]),
    ]
    loads += [
        pltpu.make_async_copy(qkv_hbm.at[t], qkv_ref.at[t], sems.at[t]) for t in range(kinds)
    ]
    for load in loads:
        load.start()
    padded_ref[...] = jnp.zeros(padded_ref.shape, f32)
    for load in loads[0:3]:
        load.wait()
    padded_ref[0 : embed_ref.shape[0], :] = embed_ref[...].astype(f32)
    normed = layer_norm(padded_ref[...]).astype(bf16)
    row = iota(ids_ref.shape, 0)
    live = jnp.zeros(ids_ref.shape, jnp.int32)
    for r in range(ids_ref.shape[0]):
        live = jnp.where(row == r, live_ref[r], live)
    coded = ids_ref[...] + 65536 * live
    coded_ref[...] = jnp.concatenate([coded] * (coded_ref.shape[0] // coded.shape[0]), 0)
    tables = []
    for t in range(kinds):
        loads[3 + t].wait()
        tables.append(dot_nt(normed, qkv_ref[t]))
    out_ref[...] = jnp.concatenate(tables, 1).astype(bf16)


def make_tables(ids, pad_mask, embed, row_qkv, height):
    kinds, local, width = row_qkv.shape
    return pl.pallas_call(
        table_kernel,
        out_shape=(
            jax.ShapeDtypeStruct((TABLE_ROWS, kinds * local), bf16),
            jax.ShapeDtypeStruct((height, ids.shape[1]), jnp.int32),
        ),
        in_specs=[pl.BlockSpec(memory_space=pltpu.HBM)] * 4,
        scratch_shapes=[
            pltpu.VMEM(ids.shape, jnp.int32),
            pltpu.SMEM(pad_mask.shape, jnp.int32),
            pltpu.VMEM(embed.shape, bf16),
            pltpu.VMEM(row_qkv.shape, bf16),
            pltpu.VMEM((TABLE_ROWS, width), f32),
            pltpu.SemaphoreType.DMA((kinds + 3,)),
        ],
        cost_estimate=pl.CostEstimate(
            flops=2 * 10**9, bytes_accessed=2 * row_qkv.size, transcendentals=0
        ),
        compiler_params=pltpu.CompilerParams(vmem_limit_bytes=SMALL_VMEM),
        name="tables",
    )(in_hbm(ids), in_hbm(pad_mask), in_hbm(embed), in_hbm(row_qkv))


def halves(pair):
    lane = iota(pair.shape, 1)
    zero = jnp.zeros_like(pair)
    return jnp.where(lane < HEAD_DIM, pair, zero), jnp.where(lane < HEAD_DIM, zero, pair)


def spread_pair(pair):
    first, second = halves(pair)
    zero = jnp.zeros_like(pair)
    return jnp.concatenate(
        [
            jnp.concatenate([first, zero], 1),
            jnp.concatenate([zero, first], 1),
            jnp.concatenate([second, zero], 1),
            jnp.concatenate([zero, second], 1),
        ],
        0,
    )


def double(block):
    zero = jnp.zeros_like(block)
    return jnp.concatenate(
        [jnp.concatenate([block, zero], 1), jnp.concatenate([zero, block], 1)], 0
    )


def one_hots(coded, group, hot_ref, own_ref, live_own_ref):
    depth, cols = hot_ref.shape
    rows = depth // CODES
    pairs = rows // 2
    own = own_ref.shape[0] // pairs
    ids = (coded & 0xFFFF).astype(f32)
    live = (coded[:, 0:LANES] >> 16).astype(f32)

    code = iota((CODES, cols), 0).astype(f32)
    for r in range(rows):
        hot = jnp.broadcast_to(ids[r : r + 1, :], (CODES, cols)) == code
        hot_ref[r * CODES : (r + 1) * CODES, :] = hot.astype(f32).astype(bf16)

    pick = (iota((own, cols), 1) == group * own + iota((own, cols), 0)).astype(f32).astype(bf16)
    mine = dot_nt(pick, ids.astype(bf16))
    lane = iota((own, LANES), 1)
    first_half = lane < CODES
    lane_code = jnp.where(first_half, lane, lane - CODES).astype(f32)
    for k in range(pairs):
        value = jnp.where(first_half, mine[:, 2 * k : 2 * k + 1], mine[:, 2 * k + 1 : 2 * k + 2])
        hot = (value == lane_code).astype(f32)
        alive = jnp.where(first_half, live[2 * k : 2 * k + 1, :], live[2 * k + 1 : 2 * k + 2, :])
        own_ref[k * own : (k + 1) * own, :] = hot.astype(bf16)
        live_own_ref[k * own : (k + 1) * own, :] = (hot * alive).astype(bf16)
    return live


def head_groups(heads, own):
    some = heads // 2
    return [(slice(g * some * own, (g + 1) * some * own), g * some, (g + 1) * some) for g in range(2)]


def tied_sum(scores_ref, live_own_ref, hot_ref, sum_ref, first, last):
    own = sum_ref.shape[0] // scores_ref.shape[0]
    depth = hot_ref.shape[0]
    pairs = depth // CODES // 2
    for h in range(first, last):
        looked = dot_nn(live_own_ref[...], scores_ref[h]).astype(bf16)
        for piece in range(2):
            for k in range(pairs):
                to = piece * depth + k * LANES
                sum_ref[h * own : (h + 1) * own, to : to + LANES] = looked[
                    k * own : (k + 1) * own, piece * LANES : (piece + 1) * LANES
                ]
    at = slice(first * own, last * own)
    return dot_nn(sum_ref[at, 0:depth], hot_ref[...]) + dot_nn(
        sum_ref[at, depth : 2 * depth], hot_ref[...]
    )


def near_kernel(parts, *refs):
    tables_refs, refs = refs[:parts], refs[parts:]
    (
        codes_ref,
        scores_ref,
        values_ref,
        tied_ref,
        hot_ref,
        own_ref,
        tables_ref,
        table_ref,
        live_own_ref,
        sum_ref,
    ) = refs
    width = values_ref.shape[1]
    heads = width // HEAD_DIM
    local = width // parts
    group = lax.axis_index("seq")
    part = lax.axis_index("head")
    for p in range(parts):
        tables_ref[part ^ p] = tables_refs[p][...]

    for t in range(3):
        to_ref = values_ref if t == 2 else table_ref.at[t]
        to_ref[0:TABLE_ROWS, :] = jnp.concatenate(
            [tables_ref[p, :, t * local : (t + 1) * local] for p in range(parts)], 1
        )
        to_ref[TABLE_ROWS:CODES, :] = jnp.zeros((CODES - TABLE_ROWS, width), bf16)

    spans = [slice(hp * LANES, (hp + 1) * LANES) for hp in range(heads // 2)]
    queries = [spread_pair(table_ref[0, :, span]) for span in spans]
    keys = [double(table_ref[1, :, span]) for span in spans]
    scores = [dot_nt(query, key) for query, key in zip(queries, keys)]
    high = [score.astype(bf16) for score in scores]
    low = [(score - part_of.astype(f32)).astype(bf16) for score, part_of in zip(scores, high)]
    for h in range(heads):
        these = slice(h % 2 * LANES, (h % 2 + 1) * LANES)
        scores_ref[h, :, 0:LANES] = high[h // 2][these]
        scores_ref[h, :, LANES : 2 * LANES] = low[h // 2][these]

    one_hots(codes_ref[...], group, hot_ref, own_ref, live_own_ref)
    for at, first, last in head_groups(heads, sum_ref.shape[0] // heads):
        tied_ref[at, :] = tied_sum(scores_ref, live_own_ref, hot_ref, sum_ref, first, last)


def attend_near(tables, codes, own):
    parts = len(tables)
    width = tables[0].shape[1] // 3 * parts
    heads = width // HEAD_DIM
    rows, cols = codes.shape
    return pl.pallas_call(
        functools.partial(near_kernel, parts),
        out_shape=(
            jax.ShapeDtypeStruct((heads, LANES, 2 * LANES), bf16),
            jax.ShapeDtypeStruct((CODES, width), bf16),
            jax.ShapeDtypeStruct((heads * own, cols), f32),
            jax.ShapeDtypeStruct((rows * CODES, cols), bf16),
            jax.ShapeDtypeStruct((rows // 2 * own, LANES), bf16),
        ),
        scratch_shapes=[
            pltpu.VMEM((parts,) + tables[0].shape, bf16),
            pltpu.VMEM((2, CODES, width), bf16),
            pltpu.VMEM((rows // 2 * own, LANES), bf16),
            pltpu.VMEM((heads * own, 2 * rows * CODES), bf16),
        ],
        cost_estimate=pl.CostEstimate(flops=10**9, bytes_accessed=10**6, transcendentals=0),
        compiler_params=pltpu.CompilerParams(vmem_limit_bytes=LARGE_VMEM),
        name="near_scores",
    )(*tables, codes)


def row_kernel(
    scores_ref,
    values_ref,
    near_tied_ref,
    near_hot_ref,
    near_codes_ref,
    far_codes_ref,
    row_context_ref,
    own_ref,
    live_ref,
    hot_ref,
    live_own_ref,
    sum_ref,
    spread_ref,
):
    depth = hot_ref.shape[0]
    rows = 2 * depth // CODES
    pairs = rows // 2
    width = row_context_ref.shape[1]
    heads = width // HEAD_DIM
    own = spread_ref.shape[0] // heads
    group = lax.axis_index("seq")

    live = one_hots(far_codes_ref[...], group, hot_ref, own_ref, live_own_ref)
    live = jnp.concatenate([(near_codes_ref[:, 0:LANES] >> 16).astype(f32), live], 0)
    live_ref[...] = live
    count = jnp.sum(live, axis=0, keepdims=True)[:, 0:1]
    scale = HEAD_DIM ** (-0.5) / jnp.sqrt(count)
    groups = head_groups(heads, own)
    tied = [
        near_tied_ref[at, :] + tied_sum(scores_ref, live_own_ref, hot_ref, sum_ref, first, last)
        for at, first, last in groups
    ]
    probs = [softmax_last(some * scale).astype(bf16) for some in tied]

    for (at, _, _), some in zip(groups, probs):
        spread_ref[at, 0:depth] = dot_nt(some, near_hot_ref[...]).astype(bf16)
        spread_ref[at, depth : 2 * depth] = dot_nt(some, hot_ref[...]).astype(bf16)
    spans = [slice(hp * LANES, (hp + 1) * LANES) for hp in range(heads // 2)]
    values = [spread_pair(values_ref[:, span]) for span in spans]
    contexts = []
    for hp in range(heads // 2):
        first = (hp * 2) * own
        weights = jnp.concatenate(
            [
                jnp.concatenate(
                    [
                        spread_ref[first : first + own, k * LANES : (k + 1) * LANES],
                        spread_ref[first + own : first + 2 * own, k * LANES : (k + 1) * LANES],
                    ],
                    1,
                )
                for k in range(pairs)
            ],
            0,
        )
        contexts.append(dot_nn(weights, values[hp]).astype(bf16))
    for hp in range(heads // 2):
        for k in range(pairs):
            for r2 in range(2):
                at = (2 * k + r2) * own
                row_context_ref[at : at + own, spans[hp]] = contexts[hp][
                    k * own : (k + 1) * own, r2 * LANES : (r2 + 1) * LANES
                ]


def attend_rows(near, near_codes, far_codes, own):
    scores, values, near_tied, near_hot = near
    heads, width = scores.shape[0], values.shape[1]
    half, cols = near_codes.shape
    return pl.pallas_call(
        row_kernel,
        out_shape=(
            jax.ShapeDtypeStruct((2 * half * own, width), bf16),
            jax.ShapeDtypeStruct((half // 2 * own, LANES), bf16),
            jax.ShapeDtypeStruct((2 * half, LANES), f32),
        ),
        scratch_shapes=[
            pltpu.VMEM((half * CODES, cols), bf16),
            pltpu.VMEM((half // 2 * own, LANES), bf16),
            pltpu.VMEM((heads * own, 2 * half * CODES), bf16),
            pltpu.VMEM((heads * own, 2 * half * CODES), bf16),
        ],
        cost_estimate=pl.CostEstimate(flops=3 * 10**9, bytes_accessed=10**6, transcendentals=0),
        compiler_params=pltpu.CompilerParams(vmem_limit_bytes=LARGE_VMEM),
        name="row_attention",
    )(scores, values, near_tied, near_hot, near_codes, far_codes)


def column_kernel(parts, *refs):
    row_out_refs, refs = refs[:parts], refs[parts:]
    (
        live_ref,
        row_context_ref,
        near_own_ref,
        far_own_ref,
        embed_ref,
        col_qkv_ref,
        *context_refs,
        mixed_out_ref,
        row_out_ref,
        embed2_ref,
        weight_ref,
        mixed_ref,
    ) = refs
    rows = live_ref.shape[0]
    tokens, width = row_context_ref.shape
    pairs = rows // 2
    own = tokens // rows
    vocab = embed_ref.shape[0]
    local = width // parts
    part = lax.axis_index("head")

    for p in range(parts):
        row_out_ref[part ^ p] = row_out_refs[p][...]
    embed2_ref[...] = jnp.zeros(embed2_ref.shape, bf16)
    embed2_ref[0:vocab, 0:width] = embed_ref[...]
    embed2_ref[CODES : CODES + vocab, width : 2 * width] = embed_ref[...]

    own_codes = jnp.concatenate([near_own_ref[...], far_own_ref[...]], 0)
    embedded2 = dot_nn(own_codes, embed2_ref[...])
    embedded = jnp.concatenate(
        [
            embedded2[k * own : (k + 1) * own, r2 * width : (r2 + 1) * width]
            for k in range(pairs)
            for r2 in range(2)
        ],
        0,
    )
    row_out = row_out_ref[...].reshape(width, width)
    halves_at = [slice(c * tokens // 2, (c + 1) * tokens // 2) for c in range(2)]
    normed = []
    for at in halves_at:
        mixed = embedded[at] + dot_nt(row_context_ref[at, :], row_out)
        mixed_ref[at, :] = mixed
        normed.append(layer_norm(mixed).astype(bf16))

    few = 8
    groups = own // few
    unit = rows * few

    def regroup(values):
        shape = (rows, groups, few, values.shape[1])
        return jnp.swapaxes(values.reshape(shape), 0, 1).reshape(tokens, values.shape[1])

    odd = part % 2
    for t in range(3):
        first = pl.multiple_of(t * local + odd * HEAD_DIM, HEAD_DIM)
        last = pl.multiple_of(t * local + (1 - odd) * LANES, HEAD_DIM)
        third = (3 + t) * LANES
        weight_ref[t * LANES : (t + 1) * LANES, :] = col_qkv_ref[pl.ds(first, LANES), :]
        weight_ref[third : third + HEAD_DIM, :] = col_qkv_ref[pl.ds(last, HEAD_DIM), :]
        weight_ref[third + HEAD_DIM : third + LANES, :] = jnp.zeros((HEAD_DIM, width), bf16)
    proj = [
        jnp.concatenate(
            [dot_nt(part_of, weight_ref[2 * j * LANES : 2 * (j + 1) * LANES, :]) for part_of in normed],
            0,
        )
        for j in range(3)
    ]
    proj = [
        proj[j][:, k * LANES : (k + 1) * LANES] * (HEAD_DIM ** (-0.5) if (2 * j + k) % 3 == 0 else 1.0)
        for j in range(3)
        for k in range(2)
    ]
    proj = [regroup(values).astype(bf16) for values in proj]
    sub, lan = iota((unit, unit), 0), iota((unit, unit), 1)
    same_column = (sub % few) == (lan % few)
    seq_of_lane = iota((rows, unit), 1) // few
    live_lane = jnp.sum(
        jnp.where(seq_of_lane == iota((rows, unit), 0), live_ref[...], 0.0), axis=0, keepdims=True
    )
    visible = jnp.logical_and(same_column, jnp.broadcast_to(live_lane, (unit, unit)) > 0)
    chosen = []
    for g in range(groups):
        at = slice(g * unit, (g + 1) * unit)
        query, keys, values = (proj[t][at] for t in range(3))
        chosen += [(half, keys, values) for half in halves(query)]
        chosen.append(tuple(proj[3 + t][at] for t in range(3)))
    scores = [jnp.where(visible, dot_nt(query, keys), -jnp.inf) for query, keys, _ in chosen]
    tops = [jnp.max(score, axis=-1, keepdims=True) for score in scores]
    weights = [jnp.exp(score - top) for score, top in zip(scores, tops)]
    shares = [1.0 / jnp.sum(weight, axis=-1, keepdims=True) for weight in weights]
    probs = [(weight * share).astype(bf16) for weight, share in zip(weights, shares)]
    found = [dot_nn(prob, values) for prob, (_, _, values) in zip(probs, chosen)]
    first_head = iota((unit, LANES), 1) < HEAD_DIM

    def ungroup(blocks):
        whole = jnp.concatenate(blocks, 0).reshape(groups, rows, few, LANES)
        return jnp.swapaxes(whole, 0, 1).reshape(tokens, LANES)

    main = ungroup(
        [jnp.where(first_head, found[3 * g], found[3 * g + 1]) for g in range(groups)]
    )
    third = ungroup([found[3 * g + 2] for g in range(groups)])
    start = 0
    for context_ref in context_refs:
        count = context_ref.shape[0] * 2 // 3
        some = count // 2
        context_ref[0:count, :] = main[start : start + count].astype(bf16)
        early = third[start : start + some]
        late = third[start + some : start + count]
        left = jnp.where(odd == 1, late, early)
        right = jnp.where(odd == 1, early, late)
        context_ref[count : count + some, :] = jnp.concatenate(
            [left[:, 0:HEAD_DIM], right[:, 0:HEAD_DIM]], 1
        ).astype(bf16)
        start += count
    for p in range(parts):

        @pl.when(part == p)
        def _():
            mixed_out_ref[...] = mixed_ref[:, p * local : (p + 1) * local]


def attend_columns_here(row_outs, live, row_context, near_own, far_own, embed, col_qkv):
    parts = len(row_outs)
    tokens, width = row_context.shape
    local = width // parts
    half = tokens // 2 * local // LANES
    return pl.pallas_call(
        functools.partial(column_kernel, parts),
        out_shape=(
            jax.ShapeDtypeStruct((half, LANES), bf16),
            jax.ShapeDtypeStruct((half, LANES), bf16),
            jax.ShapeDtypeStruct((tokens, local), f32),
        ),
        scratch_shapes=[
            pltpu.VMEM((parts, local, width), bf16),
            pltpu.VMEM((2 * CODES, 2 * width), bf16),
            pltpu.VMEM((6 * LANES, width), bf16),
            pltpu.VMEM((tokens, width), f32),
        ],
        cost_estimate=pl.CostEstimate(flops=2 * 10**9, bytes_accessed=10**6, transcendentals=0),
        compiler_params=pltpu.CompilerParams(vmem_limit_bytes=LARGE_VMEM),
        name="column_attention",
    )(*row_outs, live, row_context, near_own, far_own, embed, col_qkv)


def finish_kernel(parts, groups, *refs):
    context_refs = [refs[:parts], refs[parts : 2 * parts]]
    mixed_ref, col_out_ref, out_ref, context_ref = refs[2 * parts :]
    tokens, local = mixed_ref.shape
    group = lax.axis_index("seq")
    part = lax.axis_index("head")
    starts = [0, context_refs[0][0].shape[0]]
    for start, some_refs in zip(starts, context_refs):
        for p in range(parts):
            context_ref[part ^ p, start : start + some_refs[p].shape[0], :] = some_refs[p][...]
    pieces = []
    for start, some_refs in zip(starts, context_refs):
        count = some_refs[0].shape[0] * 2 // 3
        end = start + some_refs[0].shape[0]
        low = iota((count // 2, LANES), 1) < HEAD_DIM
        features = []
        for p in range(0, parts, 2):
            even = context_ref[p, start + count : end, :]
            other = context_ref[p + 1, start + count : end, :]
            early = jnp.where(low, even, other)
            late = jnp.where(low, other, even)
            late = jnp.concatenate([late[:, HEAD_DIM:], late[:, 0:HEAD_DIM]], 1)
            features += [
                context_ref[p, start : start + count, :],
                jnp.concatenate([early, late], 0),
                context_ref[p + 1, start : start + count, :],
            ]
        pieces.append(jnp.concatenate(features, 1))
    total = mixed_ref[...] + dot_nt(jnp.concatenate(pieces, 0), col_out_ref[...])
    own = tokens // groups // 2
    for d in range(groups):
        first, second = (total[(2 * d + r) * own : (2 * d + r + 1) * own, :] for r in range(2))
        rest = jnp.concatenate([first[:, LANES:local], second[:, LANES:local]], 1)
        out_ref[group ^ d] = jnp.concatenate(
            [first[:, 0:LANES], second[:, 0:LANES], rest], 0
        ).astype(bf16)


def finish(contexts, mixed, col_out, groups):
    parts = len(contexts[0])
    tokens, local = mixed.shape
    return pl.pallas_call(
        functools.partial(finish_kernel, parts, groups),
        out_shape=jax.ShapeDtypeStruct((groups, tokens // groups * local // LANES, LANES), bf16),
        scratch_shapes=[pltpu.VMEM((parts, tokens * local // LANES, LANES), bf16)],
        compiler_params=pltpu.CompilerParams(vmem_limit_bytes=LARGE_VMEM),
        name="finish",
    )(*contexts[0], *contexts[1], mixed, col_out)


def order_kernel(blocks_ref, out_hbm, out_ref, sems):
    groups = blocks_ref.shape[0]
    local, cols = out_ref.shape[1:]
    own = cols // groups
    rest = local - LANES
    stores = []

    def store(row, first, last, values):
        out_ref[row, first:last, :] = values
        stores.append(
            pltpu.make_async_copy(
                out_ref.at[row, first:last], out_hbm.at[row, first:last], sems.at[len(stores)]
            )
        )
        stores[-1].start()

    for part in range(3):
        piece = jnp.concatenate(
            [blocks_ref[g, part * own : (part + 1) * own, :] for g in range(groups)], 0
        )
        turned = piece.astype(f32).T.astype(bf16)
        if part < 2:
            store(part, 0, LANES, turned)
        else:
            for r in range(2):
                store(r, LANES, local, turned[r * rest : (r + 1) * rest, :])
    for started in stores:
        started.wait()


def order(blocks, cols, local):
    return pl.pallas_call(
        order_kernel,
        out_shape=jax.ShapeDtypeStruct((2, local, cols), bf16),
        out_specs=pl.BlockSpec(memory_space=pl.ANY),
        scratch_shapes=[pltpu.VMEM((2, local, cols), bf16), pltpu.SemaphoreType.DMA((4,))],
        compiler_params=pltpu.CompilerParams(vmem_limit_bytes=SMALL_VMEM),
        name="order",
    )(blocks)


def fast_body(ids, pad_mask, embed, row_qkv, row_out, col_qkv, col_out):
    rows_here, cols = ids.shape
    width = embed.shape[1]
    local = row_out.shape[0]
    groups, parts = lax.axis_size("seq"), lax.axis_size("head")
    own, rows = cols // groups, rows_here * groups

    def pairwise(value, partner):
        order = [(g, p) for g in range(groups) for p in range(parts)]
        link = [(g * parts + p, partner(g, p)) for g, p in order]
        return lax.ppermute(value, ("seq", "head"), [(i, g * parts + p) for i, (g, p) in link])

    def sibling(g, p):
        return g, p ^ 1

    def across(g, p):
        return g, p ^ 2

    def opposite(g, p):
        return g, p ^ 3

    far = pairwise(row_out, across)
    other_ids = pairwise(ids, lambda g, p: (g ^ 1, p))
    other_mask = pairwise(pad_mask.reshape(1, rows_here), lambda g, p: (g ^ 1, p))
    table, coded = make_tables(ids, pad_mask, embed, row_qkv, rows_here * groups // 2)
    tables = [table, None, pairwise(table, across), None]
    step = 2
    while step < groups:
        if step == 2:
            coded = join_raw(coded, other_ids, other_mask)
        else:
            coded = join(coded, received, rows_here * step // 2)
        if step == 2:
            coded, table = lax.optimization_barrier((coded, table))
            tables[3] = pairwise(table, opposite)
        elif step == 4:
            coded, table, row_out, far = lax.optimization_barrier((coded, table, row_out, far))
            tables[1] = pairwise(table, sibling)
            row_outs = [row_out, pairwise(row_out, sibling), far, pairwise(far, sibling)]
        received = pairwise(coded, lambda g, p, step=step: (g ^ step, p))
        step *= 2
    codes = (coded, received)
    *near_scores, near_own = attend_near(tables, codes[0], own)
    row_context, far_own, live = attend_rows(near_scores, *codes, own)
    *halves_here, mixed = attend_columns_here(
        row_outs,
        live,
        row_context,
        near_own,
        far_own,
        embed,
        col_qkv.reshape(3 * local, width),
    )
    contexts = []
    for context in halves_here:
        beyond = pairwise(context, across)
        contexts.append(
            (context, pairwise(context, sibling), beyond, pairwise(beyond, sibling))
        )
    blocks = finish(contexts, mixed, col_out, groups)
    blocks = lax.all_to_all(blocks, "seq", split_axis=0, concat_axis=0, tiled=True)
    return jnp.swapaxes(order(blocks, cols, local), 1, 2)


def weight_fold(out_weight, piece):
    return jnp.einsum("rce,fe->rcf", piece, out_weight, preferred_element_type=f32)


def attend_columns(query, keys, values, key_live):
    rows_all, count_cols, local_width = query.shape
    heads_here = local_width // HEAD_DIM
    shape = (rows_all, count_cols, heads_here, HEAD_DIM)
    scores = jnp.einsum(
        "rchd,schd->chrs",
        query.reshape(shape),
        keys.reshape(shape),
        preferred_element_type=f32,
    ) * HEAD_DIM ** (-0.5)
    scores = jnp.where(key_live > 0, scores, -jnp.inf)
    probs = softmax_last(scores).astype(bf16)
    context = jnp.einsum(
        "chrs,schd->rchd", probs, values.reshape(shape), preferred_element_type=f32
    )
    return context.astype(bf16).reshape(rows_all, count_cols, local_width)


def send_back(context):
    return lax.all_to_all(context[:, None], "seq", split_axis=0, concat_axis=1, tiled=True)


def general_body(ids, pad_mask, embed, row_qkv, row_out, col_qkv, col_out):
    rows_here, cols = ids.shape
    width = embed.shape[1]
    local_width = row_out.shape[0]
    heads_here = local_width // HEAD_DIM
    groups = lax.axis_size("seq")
    per_group = cols // groups
    codes = lax.broadcasted_iota(jnp.int32, (1, 1, embed.shape[0]), 2)
    onehot = (ids[:, :, None] == codes).astype(bf16)
    embedded = jnp.einsum("rcv,vd->rcd", onehot, embed, preferred_element_type=f32)
    normed = layer_norm(embedded).astype(bf16)
    row_proj = jnp.einsum("rcd,ted->trce", normed, row_qkv, preferred_element_type=f32)
    row_proj = row_proj.astype(bf16)
    live = pad_mask.astype(bf16)
    head_shape = (rows_here, cols, heads_here, HEAD_DIM)
    query = (row_proj[0] * live[:, None, None]).reshape(head_shape)
    keys = row_proj[1].reshape(head_shape)
    values = row_proj[2].reshape(head_shape)
    partial_scores = jnp.einsum("rihd,rjhd->hij", query, keys, preferred_element_type=f32)
    count_here = jnp.sum(pad_mask.astype(f32))
    scale = HEAD_DIM ** (-0.5)
    total, count = lax.psum((partial_scores, count_here), "seq")
    row_probs = softmax_last(total * (scale / jnp.sqrt(count))).astype(bf16)
    row_context = jnp.einsum("hij,rjhd->rihd", row_probs, values, preferred_element_type=f32)
    row_context = row_context.astype(bf16).reshape(rows_here, cols, local_width)
    start_feature = lax.axis_index("head") * local_width
    resident = lax.dynamic_slice_in_dim(embedded, start_feature, local_width, 2)
    row_update = weight_fold(row_out, lax.all_gather(row_context, "head", axis=2, tiled=True))
    mixed = resident + row_update
    sums, squares = lax.psum((jnp.sum(mixed, axis=-1), jnp.sum(mixed * mixed, axis=-1)), "head")
    mean = sums / width
    spread = squares / width - mean * mean
    normed_here = ((mixed - mean[..., None]) * lax.rsqrt(spread[..., None] + EPS)).astype(bf16)
    live_tile = jnp.broadcast_to(live[:, None, None, None], (rows_here, groups, per_group, 1))
    normed_full = lax.all_gather(normed_here, "head", axis=2, tiled=True)
    col_proj = jnp.einsum("rcd,ted->rcte", normed_full, col_qkv, preferred_element_type=f32)
    packed = col_proj.astype(bf16).reshape(rows_here, groups, per_group, 3 * local_width)
    received = lax.all_to_all(packed, "seq", split_axis=1, concat_axis=0, tiled=True)
    mask_part = lax.all_to_all(live_tile, "seq", split_axis=1, concat_axis=0, tiled=True)
    column_out = send_back(
        attend_columns(
            received[:, 0, :, :local_width],
            received[:, 0, :, local_width : 2 * local_width],
            received[:, 0, :, 2 * local_width :],
            mask_part[:, 0, 0, 0],
        )
    )
    column_out = column_out.reshape(rows_here, cols, local_width)
    col_update = weight_fold(col_out, lax.all_gather(column_out, "head", axis=2, tiled=True))
    return (mixed + col_update).astype(bf16)


def body(ids, pad_mask, embed, row_qkv, row_out, col_qkv, col_out):
    rows_here, cols = ids.shape
    groups = lax.axis_size("seq")
    own, rows = cols // groups, rows_here * groups
    parts = lax.axis_size("head")
    local = row_out.shape[0]
    fits = (
        parts == 4
        and groups >= 8
        and groups & (groups - 1) == 0
        and rows * 8 == LANES
        and rows_here == 2
        and own % 32 == 0
        and cols >= LANES
        and local == LANES + HEAD_DIM
        and embed.shape[0] <= TABLE_ROWS
    )
    chosen = fast_body if fits else general_body
    return chosen(ids, pad_mask, embed, row_qkv, row_out, col_qkv, col_out)


def solution(mesh):
    placed = (
        P("seq", None),
        P("seq"),
        P(),
        P(None, "head", None),
        P("head", None),
        P(None, "head", None),
        P("head", None),
    )
    return jax.shard_map(
        body, mesh=mesh, in_specs=placed, out_specs=P("seq", None, "head"), check_vma=False
    )
```

```python
import functools

import jax
import jax.numpy as jnp
from jax import lax
from jax.experimental import pallas as pl
from jax.experimental.pallas import tpu as pltpu
from jax.sharding import PartitionSpec as P

HEAD_DIM = 64
EPS = 1e-05
LANES = 128
CODES = 64
TABLE_ROWS = 40

SMALL_VMEM = 8 * 1024 * 1024
LARGE_VMEM = 32 * 1024 * 1024

f32 = jnp.float32
bf16 = jnp.bfloat16


def layer_norm(values):
    mean = jnp.mean(values, axis=-1, keepdims=True)
    centred = values - mean
    spread = jnp.mean(centred * centred, axis=-1, keepdims=True)
    return centred * lax.rsqrt(spread + EPS)


def softmax_last(scores):
    top = jnp.max(scores, axis=-1, keepdims=True)
    weights = jnp.exp(scores - top)
    return weights * (1.0 / jnp.sum(weights, axis=-1, keepdims=True))


def dot_nt(left, right):
    return lax.dot_general(left, right, (((1,), (1,)), ((), ())), preferred_element_type=f32)


def dot_nn(left, right):
    return jnp.dot(left, right, preferred_element_type=f32)


def in_hbm(value):
    return pltpu.with_memory_space_constraint(value, pltpu.HBM)


def iota(shape, axis):
    return lax.broadcasted_iota(jnp.int32, shape, axis)


def join_kernel(rows, own_ref, other_ref, out_ref):
    own, other = own_ref[...], other_ref[...]
    both = jnp.concatenate([own[0:rows], other[0:rows]], 0)
    out_ref[...] = jnp.concatenate([both] * (own.shape[0] // (2 * rows)), 0)


def join(own, other, rows):
    return pl.pallas_call(
        functools.partial(join_kernel, rows),
        out_shape=jax.ShapeDtypeStruct(own.shape, own.dtype),
        compiler_params=pltpu.CompilerParams(vmem_limit_bytes=SMALL_VMEM),
        name="join",
    )(own, other)


def join_raw_kernel(own_ref, ids_ref, live_ref, out_ref):
    rows = ids_ref.shape[0]
    live = live_ref[...]
    other = ids_ref[...] + 65536 * jnp.concatenate(
        [jnp.broadcast_to(live[:, r : r + 1], (1, ids_ref.shape[1])) for r in range(rows)], 0
    )
    both = jnp.concatenate([own_ref[0:rows], other], 0)
    out_ref[...] = jnp.concatenate([both] * (out_ref.shape[0] // (2 * rows)), 0)


def join_raw(own, ids, pad_mask):
    return pl.pallas_call(
        join_raw_kernel,
        out_shape=jax.ShapeDtypeStruct(own.shape, own.dtype),
        compiler_params=pltpu.CompilerParams(vmem_limit_bytes=SMALL_VMEM),
        name="join_raw",
    )(own, ids, pad_mask)


def table_kernel(
    ids_hbm,
    live_hbm,
    embed_hbm,
    qkv_hbm,
    out_ref,
    coded_ref,
    ids_ref,
    live_ref,
    embed_ref,
    qkv_ref,
    padded_ref,
    sems,
):
    kinds = qkv_ref.shape[0]
    loads = [
        pltpu.make_async_copy(embed_hbm, embed_ref, sems.at[kinds]),
        pltpu.make_async_copy(ids_hbm, ids_ref, sems.at[kinds + 1]),
        pltpu.make_async_copy(live_hbm, live_ref, sems.at[kinds + 2]),
    ]
    loads += [
        pltpu.make_async_copy(qkv_hbm.at[t], qkv_ref.at[t], sems.at[t]) for t in range(kinds)
    ]
    for load in loads:
        load.start()
    padded_ref[...] = jnp.zeros(padded_ref.shape, f32)
    for load in loads[0:3]:
        load.wait()
    padded_ref[0 : embed_ref.shape[0], :] = embed_ref[...].astype(f32)
    normed = layer_norm(padded_ref[...]).astype(bf16)
    row = iota(ids_ref.shape, 0)
    live = jnp.zeros(ids_ref.shape, jnp.int32)
    for r in range(ids_ref.shape[0]):
        live = jnp.where(row == r, live_ref[r], live)
    coded = ids_ref[...] + 65536 * live
    coded_ref[...] = jnp.concatenate([coded] * (coded_ref.shape[0] // coded.shape[0]), 0)
    tables = []
    for t in range(kinds):
        loads[3 + t].wait()
        tables.append(dot_nt(normed, qkv_ref[t]))
    out_ref[...] = jnp.concatenate(tables, 1).astype(bf16)


def make_tables(ids, pad_mask, embed, row_qkv, height):
    kinds, local, width = row_qkv.shape
    return pl.pallas_call(
        table_kernel,
        out_shape=(
            jax.ShapeDtypeStruct((TABLE_ROWS, kinds * local), bf16),
            jax.ShapeDtypeStruct((height, ids.shape[1]), jnp.int32),
        ),
        in_specs=[pl.BlockSpec(memory_space=pltpu.HBM)] * 4,
        scratch_shapes=[
            pltpu.VMEM(ids.shape, jnp.int32),
            pltpu.SMEM(pad_mask.shape, jnp.int32),
            pltpu.VMEM(embed.shape, bf16),
            pltpu.VMEM(row_qkv.shape, bf16),
            pltpu.VMEM((TABLE_ROWS, width), f32),
            pltpu.SemaphoreType.DMA((kinds + 3,)),
        ],
        cost_estimate=pl.CostEstimate(
            flops=2 * 10**9, bytes_accessed=2 * row_qkv.size, transcendentals=0
        ),
        compiler_params=pltpu.CompilerParams(vmem_limit_bytes=SMALL_VMEM),
        name="tables",
    )(in_hbm(ids), in_hbm(pad_mask), in_hbm(embed), in_hbm(row_qkv))


def halves(pair):
    lane = iota(pair.shape, 1)
    zero = jnp.zeros_like(pair)
    return jnp.where(lane < HEAD_DIM, pair, zero), jnp.where(lane < HEAD_DIM, zero, pair)


def spread_pair(pair):
    first, second = halves(pair)
    zero = jnp.zeros_like(pair)
    return jnp.concatenate(
        [
            jnp.concatenate([first, zero], 1),
            jnp.concatenate([zero, first], 1),
            jnp.concatenate([second, zero], 1),
            jnp.concatenate([zero, second], 1),
        ],
        0,
    )


def double(block):
    zero = jnp.zeros_like(block)
    return jnp.concatenate(
        [jnp.concatenate([block, zero], 1), jnp.concatenate([zero, block], 1)], 0
    )


def one_hots(coded, group, hot_ref, own_ref, live_own_ref):
    depth, cols = hot_ref.shape
    rows = depth // CODES
    pairs = rows // 2
    own = own_ref.shape[0] // pairs
    ids = (coded & 0xFFFF).astype(f32)
    live = (coded[:, 0:LANES] >> 16).astype(f32)

    code = iota((CODES, cols), 0).astype(f32)
    for r in range(rows):
        hot = jnp.broadcast_to(ids[r : r + 1, :], (CODES, cols)) == code
        hot_ref[r * CODES : (r + 1) * CODES, :] = hot.astype(f32).astype(bf16)

    pick = (iota((own, cols), 1) == group * own + iota((own, cols), 0)).astype(f32).astype(bf16)
    mine = dot_nt(pick, ids.astype(bf16))
    lane = iota((own, LANES), 1)
    first_half = lane < CODES
    lane_code = jnp.where(first_half, lane, lane - CODES).astype(f32)
    for k in range(pairs):
        value = jnp.where(first_half, mine[:, 2 * k : 2 * k + 1], mine[:, 2 * k + 1 : 2 * k + 2])
        hot = (value == lane_code).astype(f32)
        alive = jnp.where(first_half, live[2 * k : 2 * k + 1, :], live[2 * k + 1 : 2 * k + 2, :])
        own_ref[k * own : (k + 1) * own, :] = hot.astype(bf16)
        live_own_ref[k * own : (k + 1) * own, :] = (hot * alive).astype(bf16)
    return live


def head_groups(heads, own):
    some = heads // 2
    return [(slice(g * some * own, (g + 1) * some * own), g * some, (g + 1) * some) for g in range(2)]


def tied_sum(scores_ref, live_own_ref, hot_ref, sum_ref, first, last):
    own = sum_ref.shape[0] // scores_ref.shape[0]
    depth = hot_ref.shape[0]
    pairs = depth // CODES // 2
    for h in range(first, last):
        looked = dot_nn(live_own_ref[...], scores_ref[h]).astype(bf16)
        for piece in range(2):
            for k in range(pairs):
                to = piece * depth + k * LANES
                sum_ref[h * own : (h + 1) * own, to : to + LANES] = looked[
                    k * own : (k + 1) * own, piece * LANES : (piece + 1) * LANES
                ]
    at = slice(first * own, last * own)
    return dot_nn(sum_ref[at, 0:depth], hot_ref[...]) + dot_nn(
        sum_ref[at, depth : 2 * depth], hot_ref[...]
    )


def near_kernel(parts, *refs):
    tables_refs, refs = refs[:parts], refs[parts:]
    (
        codes_ref,
        scores_ref,
        values_ref,
        tied_ref,
        hot_ref,
        own_ref,
        tables_ref,
        table_ref,
        live_own_ref,
        sum_ref,
    ) = refs
    width = values_ref.shape[1]
    heads = width // HEAD_DIM
    local = width // parts
    group = lax.axis_index("seq")
    part = lax.axis_index("head")
    for p in range(parts):
        tables_ref[part ^ p] = tables_refs[p][...]

    for t in range(3):
        to_ref = values_ref if t == 2 else table_ref.at[t]
        to_ref[0:TABLE_ROWS, :] = jnp.concatenate(
            [tables_ref[p, :, t * local : (t + 1) * local] for p in range(parts)], 1
        )
        to_ref[TABLE_ROWS:CODES, :] = jnp.zeros((CODES - TABLE_ROWS, width), bf16)

    spans = [slice(hp * LANES, (hp + 1) * LANES) for hp in range(heads // 2)]
    queries = [spread_pair(table_ref[0, :, span]) for span in spans]
    keys = [double(table_ref[1, :, span]) for span in spans]
    scores = [dot_nt(query, key) for query, key in zip(queries, keys)]
    high = [score.astype(bf16) for score in scores]
    low = [(score - part_of.astype(f32)).astype(bf16) for score, part_of in zip(scores, high)]
    for h in range(heads):
        these = slice(h % 2 * LANES, (h % 2 + 1) * LANES)
        scores_ref[h, :, 0:LANES] = high[h // 2][these]
        scores_ref[h, :, LANES : 2 * LANES] = low[h // 2][these]

    one_hots(codes_ref[...], group, hot_ref, own_ref, live_own_ref)
    tied_ref[...] = tied_sum(scores_ref, live_own_ref, hot_ref, sum_ref, 0, heads)


def attend_near(tables, codes, own):
    parts = len(tables)
    width = tables[0].shape[1] // 3 * parts
    heads = width // HEAD_DIM
    rows, cols = codes.shape
    return pl.pallas_call(
        functools.partial(near_kernel, parts),
        out_shape=(
            jax.ShapeDtypeStruct((heads, LANES, 2 * LANES), bf16),
            jax.ShapeDtypeStruct((CODES, width), bf16),
            jax.ShapeDtypeStruct((heads * own, cols), f32),
            jax.ShapeDtypeStruct((rows * CODES, cols), bf16),
            jax.ShapeDtypeStruct((rows // 2 * own, LANES), bf16),
        ),
        scratch_shapes=[
            pltpu.VMEM((parts,) + tables[0].shape, bf16),
            pltpu.VMEM((2, CODES, width), bf16),
            pltpu.VMEM((rows // 2 * own, LANES), bf16),
            pltpu.VMEM((heads * own, 2 * rows * CODES), bf16),
        ],
        cost_estimate=pl.CostEstimate(flops=10**9, bytes_accessed=10**6, transcendentals=0),
        compiler_params=pltpu.CompilerParams(vmem_limit_bytes=LARGE_VMEM),
        name="near_scores",
    )(*tables, codes)


def row_kernel(
    scores_ref,
    values_ref,
    near_tied_ref,
    near_hot_ref,
    near_codes_ref,
    far_codes_ref,
    row_context_ref,
    own_ref,
    live_ref,
    hot_ref,
    live_own_ref,
    sum_ref,
    spread_ref,
):
    depth = hot_ref.shape[0]
    rows = 2 * depth // CODES
    pairs = rows // 2
    width = row_context_ref.shape[1]
    heads = width // HEAD_DIM
    own = spread_ref.shape[0] // heads
    group = lax.axis_index("seq")

    live = one_hots(far_codes_ref[...], group, hot_ref, own_ref, live_own_ref)
    live = jnp.concatenate([(near_codes_ref[:, 0:LANES] >> 16).astype(f32), live], 0)
    live_ref[...] = live
    count = jnp.sum(live, axis=0, keepdims=True)[:, 0:1]
    scale = HEAD_DIM ** (-0.5) / jnp.sqrt(count)
    groups = head_groups(heads, own)
    tied = [
        near_tied_ref[at, :] + tied_sum(scores_ref, live_own_ref, hot_ref, sum_ref, first, last)
        for at, first, last in groups
    ]
    probs = [softmax_last(some * scale).astype(bf16) for some in tied]

    for (at, _, _), some in zip(groups, probs):
        spread_ref[at, 0:depth] = dot_nt(some, near_hot_ref[...]).astype(bf16)
        spread_ref[at, depth : 2 * depth] = dot_nt(some, hot_ref[...]).astype(bf16)
    spans = [slice(hp * LANES, (hp + 1) * LANES) for hp in range(heads // 2)]
    values = [spread_pair(values_ref[:, span]) for span in spans]
    contexts = []
    for hp in range(heads // 2):
        first = (hp * 2) * own
        weights = jnp.concatenate(
            [
                jnp.concatenate(
                    [
                        spread_ref[first : first + own, k * LANES : (k + 1) * LANES],
                        spread_ref[first + own : first + 2 * own, k * LANES : (k + 1) * LANES],
                    ],
                    1,
                )
                for k in range(pairs)
            ],
            0,
        )
        contexts.append(dot_nn(weights, values[hp]).astype(bf16))
    for hp in range(heads // 2):
        for k in range(pairs):
            for r2 in range(2):
                at = (2 * k + r2) * own
                row_context_ref[at : at + own, spans[hp]] = contexts[hp][
                    k * own : (k + 1) * own, r2 * LANES : (r2 + 1) * LANES
                ]


def attend_rows(near, near_codes, far_codes, own):
    scores, values, near_tied, near_hot = near
    heads, width = scores.shape[0], values.shape[1]
    half, cols = near_codes.shape
    return pl.pallas_call(
        row_kernel,
        out_shape=(
            jax.ShapeDtypeStruct((2 * half * own, width), bf16),
            jax.ShapeDtypeStruct((half // 2 * own, LANES), bf16),
            jax.ShapeDtypeStruct((2 * half, LANES), f32),
        ),
        scratch_shapes=[
            pltpu.VMEM((half * CODES, cols), bf16),
            pltpu.VMEM((half // 2 * own, LANES), bf16),
            pltpu.VMEM((heads * own, 2 * half * CODES), bf16),
            pltpu.VMEM((heads * own, 2 * half * CODES), bf16),
        ],
        cost_estimate=pl.CostEstimate(flops=3 * 10**9, bytes_accessed=10**6, transcendentals=0),
        compiler_params=pltpu.CompilerParams(vmem_limit_bytes=LARGE_VMEM),
        name="row_attention",
    )(scores, values, near_tied, near_hot, near_codes, far_codes)


def column_kernel(parts, *refs):
    row_out_refs, refs = refs[:parts], refs[parts:]
    (
        live_ref,
        row_context_ref,
        near_own_ref,
        far_own_ref,
        embed_ref,
        col_qkv_ref,
        *context_refs,
        mixed_out_ref,
        row_out_ref,
        embed2_ref,
        weight_ref,
        mixed_ref,
    ) = refs
    rows = live_ref.shape[0]
    tokens, width = row_context_ref.shape
    pairs = rows // 2
    own = tokens // rows
    vocab = embed_ref.shape[0]
    local = width // parts
    part = lax.axis_index("head")

    for p in range(parts):
        row_out_ref[part ^ p] = row_out_refs[p][...]
    embed2_ref[...] = jnp.zeros(embed2_ref.shape, bf16)
    embed2_ref[0:vocab, 0:width] = embed_ref[...]
    embed2_ref[CODES : CODES + vocab, width : 2 * width] = embed_ref[...]

    own_codes = jnp.concatenate([near_own_ref[...], far_own_ref[...]], 0)
    embedded2 = dot_nn(own_codes, embed2_ref[...])
    embedded = jnp.concatenate(
        [
            embedded2[k * own : (k + 1) * own, r2 * width : (r2 + 1) * width]
            for k in range(pairs)
            for r2 in range(2)
        ],
        0,
    )
    row_out = row_out_ref[...].reshape(width, width)
    quarters = [slice(c * tokens // 4, (c + 1) * tokens // 4) for c in range(4)]
    normed = []
    for at in quarters:
        mixed = embedded[at] + dot_nt(row_context_ref[at, :], row_out)
        mixed_ref[at, :] = mixed
        normed.append(layer_norm(mixed).astype(bf16))

    few = 8
    groups = own // few
    unit = rows * few

    def regroup(values):
        shape = (rows, groups, few, values.shape[1])
        return jnp.swapaxes(values.reshape(shape), 0, 1).reshape(tokens, values.shape[1])

    odd = part % 2
    for t in range(3):
        first = pl.multiple_of(t * local + odd * HEAD_DIM, HEAD_DIM)
        last = pl.multiple_of(t * local + (1 - odd) * LANES, HEAD_DIM)
        third = (3 + t) * LANES
        weight_ref[t * LANES : (t + 1) * LANES, :] = col_qkv_ref[pl.ds(first, LANES), :]
        weight_ref[third : third + HEAD_DIM, :] = col_qkv_ref[pl.ds(last, HEAD_DIM), :]
        weight_ref[third + HEAD_DIM : third + LANES, :] = jnp.zeros((HEAD_DIM, width), bf16)
    proj = [
        jnp.concatenate(
            [dot_nt(part_of, weight_ref[2 * j * LANES : 2 * (j + 1) * LANES, :]) for part_of in normed],
            0,
        )
        for j in range(3)
    ]
    proj = [
        proj[j][:, k * LANES : (k + 1) * LANES] * (HEAD_DIM ** (-0.5) if (2 * j + k) % 3 == 0 else 1.0)
        for j in range(3)
        for k in range(2)
    ]
    proj = [regroup(values).astype(bf16) for values in proj]
    sub, lan = iota((unit, unit), 0), iota((unit, unit), 1)
    same_column = (sub % few) == (lan % few)
    seq_of_lane = iota((rows, unit), 1) // few
    live_lane = jnp.sum(
        jnp.where(seq_of_lane == iota((rows, unit), 0), live_ref[...], 0.0), axis=0, keepdims=True
    )
    visible = jnp.logical_and(same_column, jnp.broadcast_to(live_lane, (unit, unit)) > 0)
    chosen = []
    for g in range(groups):
        at = slice(g * unit, (g + 1) * unit)
        query, keys, values = (proj[t][at] for t in range(3))
        chosen += [(half, keys, values) for half in halves(query)]
        chosen.append(tuple(proj[3 + t][at] for t in range(3)))
    scores = [jnp.where(visible, dot_nt(query, keys), -jnp.inf) for query, keys, _ in chosen]
    tops = [jnp.max(score, axis=-1, keepdims=True) for score in scores]
    weights = [jnp.exp(score - top) for score, top in zip(scores, tops)]
    shares = [1.0 / jnp.sum(weight, axis=-1, keepdims=True) for weight in weights]
    probs = [(weight * share).astype(bf16) for weight, share in zip(weights, shares)]
    found = [dot_nn(prob, values) for prob, (_, _, values) in zip(probs, chosen)]
    first_head = iota((unit, LANES), 1) < HEAD_DIM

    def ungroup(blocks):
        whole = jnp.concatenate(blocks, 0).reshape(groups, rows, few, LANES)
        return jnp.swapaxes(whole, 0, 1).reshape(tokens, LANES)

    main = ungroup(
        [jnp.where(first_head, found[3 * g], found[3 * g + 1]) for g in range(groups)]
    )
    third = ungroup([found[3 * g + 2] for g in range(groups)])
    start = 0
    for context_ref in context_refs:
        count = context_ref.shape[0] * 2 // 3
        some = count // 2
        context_ref[0:count, :] = main[start : start + count].astype(bf16)
        early = third[start : start + some]
        late = third[start + some : start + count]
        left = jnp.where(odd == 1, late, early)
        right = jnp.where(odd == 1, early, late)
        context_ref[count : count + some, :] = jnp.concatenate(
            [left[:, 0:HEAD_DIM], right[:, 0:HEAD_DIM]], 1
        ).astype(bf16)
        start += count
    for p in range(parts):

        @pl.when(part == p)
        def _():
            mixed_out_ref[...] = mixed_ref[:, p * local : (p + 1) * local]


def attend_columns_here(row_outs, live, row_context, near_own, far_own, embed, col_qkv):
    parts = len(row_outs)
    tokens, width = row_context.shape
    local = width // parts
    half = tokens // 2 * local // LANES
    return pl.pallas_call(
        functools.partial(column_kernel, parts),
        out_shape=(
            jax.ShapeDtypeStruct((half, LANES), bf16),
            jax.ShapeDtypeStruct((half, LANES), bf16),
            jax.ShapeDtypeStruct((tokens, local), f32),
        ),
        scratch_shapes=[
            pltpu.VMEM((parts, local, width), bf16),
            pltpu.VMEM((2 * CODES, 2 * width), bf16),
            pltpu.VMEM((6 * LANES, width), bf16),
            pltpu.VMEM((tokens, width), f32),
        ],
        cost_estimate=pl.CostEstimate(flops=2 * 10**9, bytes_accessed=10**6, transcendentals=0),
        compiler_params=pltpu.CompilerParams(vmem_limit_bytes=LARGE_VMEM),
        name="column_attention",
    )(*row_outs, live, row_context, near_own, far_own, embed, col_qkv)


def finish_kernel(parts, groups, *refs):
    context_refs = [refs[:parts], refs[parts : 2 * parts]]
    mixed_ref, col_out_ref, out_ref, context_ref = refs[2 * parts :]
    tokens, local = mixed_ref.shape
    group = lax.axis_index("seq")
    part = lax.axis_index("head")
    starts = [0, context_refs[0][0].shape[0]]
    for start, some_refs in zip(starts, context_refs):
        for p in range(parts):
            context_ref[part ^ p, start : start + some_refs[p].shape[0], :] = some_refs[p][...]
    pieces = []
    for start, some_refs in zip(starts, context_refs):
        count = some_refs[0].shape[0] * 2 // 3
        end = start + some_refs[0].shape[0]
        low = iota((count // 2, LANES), 1) < HEAD_DIM
        features = []
        for p in range(0, parts, 2):
            even = context_ref[p, start + count : end, :]
            other = context_ref[p + 1, start + count : end, :]
            early = jnp.where(low, even, other)
            late = jnp.where(low, other, even)
            late = jnp.concatenate([late[:, HEAD_DIM:], late[:, 0:HEAD_DIM]], 1)
            features += [
                context_ref[p, start : start + count, :],
                jnp.concatenate([early, late], 0),
                context_ref[p + 1, start : start + count, :],
            ]
        pieces.append(jnp.concatenate(features, 1))
    total = mixed_ref[...] + dot_nt(jnp.concatenate(pieces, 0), col_out_ref[...])
    own = tokens // groups // 2
    for d in range(groups):
        first, second = (total[(2 * d + r) * own : (2 * d + r + 1) * own, :] for r in range(2))
        rest = jnp.concatenate([first[:, LANES:local], second[:, LANES:local]], 1)
        out_ref[group ^ d] = jnp.concatenate(
            [first[:, 0:LANES], second[:, 0:LANES], rest], 0
        ).astype(bf16)


def finish(contexts, mixed, col_out, groups):
    parts = len(contexts[0])
    tokens, local = mixed.shape
    return pl.pallas_call(
        functools.partial(finish_kernel, parts, groups),
        out_shape=jax.ShapeDtypeStruct((groups, tokens // groups * local // LANES, LANES), bf16),
        scratch_shapes=[pltpu.VMEM((parts, tokens * local // LANES, LANES), bf16)],
        compiler_params=pltpu.CompilerParams(vmem_limit_bytes=LARGE_VMEM),
        name="finish",
    )(*contexts[0], *contexts[1], mixed, col_out)


def order_kernel(blocks_ref, out_ref):
    groups = blocks_ref.shape[0]
    local, cols = out_ref.shape[1:]
    own = cols // groups
    rest = local - LANES
    one = (iota((LANES, LANES), 0) == iota((LANES, LANES), 1)).astype(f32).astype(bf16)
    for part in range(3):
        piece = jnp.concatenate(
            [blocks_ref[g, part * own : (part + 1) * own, :] for g in range(groups)], 0
        )
        turned = dot_nt(one, piece).astype(bf16)
        if part < 2:
            out_ref[part, 0:LANES, :] = turned
        else:
            for r in range(2):
                out_ref[r, LANES:local, :] = turned[r * rest : (r + 1) * rest, :]


def order(blocks, cols, local):
    return pl.pallas_call(
        order_kernel,
        out_shape=jax.ShapeDtypeStruct((2, local, cols), bf16),
        compiler_params=pltpu.CompilerParams(vmem_limit_bytes=SMALL_VMEM),
        name="order",
    )(blocks)


def fast_body(ids, pad_mask, embed, row_qkv, row_out, col_qkv, col_out):
    rows_here, cols = ids.shape
    width = embed.shape[1]
    local = row_out.shape[0]
    groups, parts = lax.axis_size("seq"), lax.axis_size("head")
    own, rows = cols // groups, rows_here * groups

    def pairwise(value, partner):
        order = [(g, p) for g in range(groups) for p in range(parts)]
        link = [(g * parts + p, partner(g, p)) for g, p in order]
        return lax.ppermute(value, ("seq", "head"), [(i, g * parts + p) for i, (g, p) in link])

    def sibling(g, p):
        return g, p ^ 1

    def across(g, p):
        return g, p ^ 2

    def opposite(g, p):
        return g, p ^ 3

    far = pairwise(row_out, across)
    other_ids = pairwise(ids, lambda g, p: (g ^ 1, p))
    other_mask = pairwise(pad_mask.reshape(1, rows_here), lambda g, p: (g ^ 1, p))
    table, coded = make_tables(ids, pad_mask, embed, row_qkv, rows_here * groups // 2)
    tables = [table, None, pairwise(table, across), None]
    step = 2
    while step < groups:
        if step == 2:
            coded = join_raw(coded, other_ids, other_mask)
        else:
            coded = join(coded, received, rows_here * step // 2)
        if step == 2:
            coded, table = lax.optimization_barrier((coded, table))
            tables[3] = pairwise(table, opposite)
        elif step == 4:
            coded, table, row_out, far = lax.optimization_barrier((coded, table, row_out, far))
            tables[1] = pairwise(table, sibling)
            row_outs = [row_out, pairwise(row_out, sibling), far, pairwise(far, sibling)]
        received = pairwise(coded, lambda g, p, step=step: (g ^ step, p))
        step *= 2
    codes = (coded, received)
    *near_scores, near_own = attend_near(tables, codes[0], own)
    row_context, far_own, live = attend_rows(near_scores, *codes, own)
    *halves_here, mixed = attend_columns_here(
        row_outs,
        live,
        row_context,
        near_own,
        far_own,
        embed,
        col_qkv.reshape(3 * local, width),
    )
    contexts = []
    for context in halves_here:
        beyond = pairwise(context, across)
        contexts.append(
            (context, pairwise(context, sibling), beyond, pairwise(beyond, sibling))
        )
    blocks = finish(contexts, mixed, col_out, groups)
    blocks = lax.all_to_all(blocks, "seq", split_axis=0, concat_axis=0, tiled=True)
    return jnp.swapaxes(order(blocks, cols, local), 1, 2)


def weight_fold(out_weight, piece):
    return jnp.einsum("rce,fe->rcf", piece, out_weight, preferred_element_type=f32)


def attend_columns(query, keys, values, key_live):
    rows_all, count_cols, local_width = query.shape
    heads_here = local_width // HEAD_DIM
    shape = (rows_all, count_cols, heads_here, HEAD_DIM)
    scores = jnp.einsum(
        "rchd,schd->chrs",
        query.reshape(shape),
        keys.reshape(shape),
        preferred_element_type=f32,
    ) * HEAD_DIM ** (-0.5)
    scores = jnp.where(key_live > 0, scores, -jnp.inf)
    probs = softmax_last(scores).astype(bf16)
    context = jnp.einsum(
        "chrs,schd->rchd", probs, values.reshape(shape), preferred_element_type=f32
    )
    return context.astype(bf16).reshape(rows_all, count_cols, local_width)


def send_back(context):
    return lax.all_to_all(context[:, None], "seq", split_axis=0, concat_axis=1, tiled=True)


def general_body(ids, pad_mask, embed, row_qkv, row_out, col_qkv, col_out):
    rows_here, cols = ids.shape
    width = embed.shape[1]
    local_width = row_out.shape[0]
    heads_here = local_width // HEAD_DIM
    groups = lax.axis_size("seq")
    per_group = cols // groups
    codes = lax.broadcasted_iota(jnp.int32, (1, 1, embed.shape[0]), 2)
    onehot = (ids[:, :, None] == codes).astype(bf16)
    embedded = jnp.einsum("rcv,vd->rcd", onehot, embed, preferred_element_type=f32)
    normed = layer_norm(embedded).astype(bf16)
    row_proj = jnp.einsum("rcd,ted->trce", normed, row_qkv, preferred_element_type=f32)
    row_proj = row_proj.astype(bf16)
    live = pad_mask.astype(bf16)
    head_shape = (rows_here, cols, heads_here, HEAD_DIM)
    query = (row_proj[0] * live[:, None, None]).reshape(head_shape)
    keys = row_proj[1].reshape(head_shape)
    values = row_proj[2].reshape(head_shape)
    partial_scores = jnp.einsum("rihd,rjhd->hij", query, keys, preferred_element_type=f32)
    count_here = jnp.sum(pad_mask.astype(f32))
    scale = HEAD_DIM ** (-0.5)
    total, count = lax.psum((partial_scores, count_here), "seq")
    row_probs = softmax_last(total * (scale / jnp.sqrt(count))).astype(bf16)
    row_context = jnp.einsum("hij,rjhd->rihd", row_probs, values, preferred_element_type=f32)
    row_context = row_context.astype(bf16).reshape(rows_here, cols, local_width)
    start_feature = lax.axis_index("head") * local_width
    resident = lax.dynamic_slice_in_dim(embedded, start_feature, local_width, 2)
    row_update = weight_fold(row_out, lax.all_gather(row_context, "head", axis=2, tiled=True))
    mixed = resident + row_update
    sums, squares = lax.psum((jnp.sum(mixed, axis=-1), jnp.sum(mixed * mixed, axis=-1)), "head")
    mean = sums / width
    spread = squares / width - mean * mean
    normed_here = ((mixed - mean[..., None]) * lax.rsqrt(spread[..., None] + EPS)).astype(bf16)
    live_tile = jnp.broadcast_to(live[:, None, None, None], (rows_here, groups, per_group, 1))
    normed_full = lax.all_gather(normed_here, "head", axis=2, tiled=True)
    col_proj = jnp.einsum("rcd,ted->rcte", normed_full, col_qkv, preferred_element_type=f32)
    packed = col_proj.astype(bf16).reshape(rows_here, groups, per_group, 3 * local_width)
    received = lax.all_to_all(packed, "seq", split_axis=1, concat_axis=0, tiled=True)
    mask_part = lax.all_to_all(live_tile, "seq", split_axis=1, concat_axis=0, tiled=True)
    column_out = send_back(
        attend_columns(
            received[:, 0, :, :local_width],
            received[:, 0, :, local_width : 2 * local_width],
            received[:, 0, :, 2 * local_width :],
            mask_part[:, 0, 0, 0],
        )
    )
    column_out = column_out.reshape(rows_here, cols, local_width)
    col_update = weight_fold(col_out, lax.all_gather(column_out, "head", axis=2, tiled=True))
    return (mixed + col_update).astype(bf16)


def body(ids, pad_mask, embed, row_qkv, row_out, col_qkv, col_out):
    rows_here, cols = ids.shape
    groups = lax.axis_size("seq")
    own, rows = cols // groups, rows_here * groups
    parts = lax.axis_size("head")
    local = row_out.shape[0]
    fits = (
        parts == 4
        and groups >= 8
        and groups & (groups - 1) == 0
        and rows * 8 == LANES
        and rows_here == 2
        and own % 32 == 0
        and cols >= LANES
        and local == LANES + HEAD_DIM
        and embed.shape[0] <= TABLE_ROWS
    )
    chosen = fast_body if fits else general_body
    return chosen(ids, pad_mask, embed, row_qkv, row_out, col_qkv, col_out)


def solution(mesh):
    placed = (
        P("seq", None),
        P("seq"),
        P(),
        P(None, "head", None),
        P("head", None),
        P(None, "head", None),
        P("head", None),
    )
    return jax.shard_map(
        body, mesh=mesh, in_specs=placed, out_specs=P("seq", None, "head"), check_vma=False
    )
```

```python
import functools

import jax
import jax.numpy as jnp
from jax import lax
from jax.experimental import pallas as pl
from jax.experimental.pallas import tpu as pltpu
from jax.sharding import PartitionSpec as P

HEAD_DIM = 64
EPS = 1e-05
LANES = 128
CODES = 64
TABLE_ROWS = 40

SMALL_VMEM = 8 * 1024 * 1024
LARGE_VMEM = 32 * 1024 * 1024

f32 = jnp.float32
bf16 = jnp.bfloat16


def layer_norm(values):
    mean = jnp.mean(values, axis=-1, keepdims=True)
    centred = values - mean
    spread = jnp.mean(centred * centred, axis=-1, keepdims=True)
    return centred * lax.rsqrt(spread + EPS)


def softmax_last(scores):
    top = jnp.max(scores, axis=-1, keepdims=True)
    weights = jnp.exp(scores - top)
    return weights * (1.0 / jnp.sum(weights, axis=-1, keepdims=True))


def dot_nt(left, right):
    return lax.dot_general(left, right, (((1,), (1,)), ((), ())), preferred_element_type=f32)


def dot_nn(left, right):
    return jnp.dot(left, right, preferred_element_type=f32)


def in_hbm(value):
    return pltpu.with_memory_space_constraint(value, pltpu.HBM)


def iota(shape, axis):
    return lax.broadcasted_iota(jnp.int32, shape, axis)


def join_kernel(rows, own_ref, other_ref, out_ref):
    own, other = own_ref[...], other_ref[...]
    both = jnp.concatenate([own[0:rows], other[0:rows]], 0)
    out_ref[...] = jnp.concatenate([both] * (own.shape[0] // (2 * rows)), 0)


def join(own, other, rows):
    return pl.pallas_call(
        functools.partial(join_kernel, rows),
        out_shape=jax.ShapeDtypeStruct(own.shape, own.dtype),
        compiler_params=pltpu.CompilerParams(vmem_limit_bytes=SMALL_VMEM),
        name="join",
    )(own, other)


def join_raw_kernel(own_ref, ids_ref, live_ref, out_ref):
    rows = ids_ref.shape[0]
    live = live_ref[...]
    other = ids_ref[...] + 65536 * jnp.concatenate(
        [jnp.broadcast_to(live[:, r : r + 1], (1, ids_ref.shape[1])) for r in range(rows)], 0
    )
    both = jnp.concatenate([own_ref[0:rows], other], 0)
    out_ref[...] = jnp.concatenate([both] * (out_ref.shape[0] // (2 * rows)), 0)


def join_raw(own, ids, pad_mask):
    return pl.pallas_call(
        join_raw_kernel,
        out_shape=jax.ShapeDtypeStruct(own.shape, own.dtype),
        compiler_params=pltpu.CompilerParams(vmem_limit_bytes=SMALL_VMEM),
        name="join_raw",
    )(own, ids, pad_mask)


def table_kernel(
    ids_hbm,
    live_hbm,
    embed_hbm,
    qkv_hbm,
    out_ref,
    coded_ref,
    ids_ref,
    live_ref,
    embed_ref,
    qkv_ref,
    padded_ref,
    sems,
):
    kinds = qkv_ref.shape[0]
    loads = [
        pltpu.make_async_copy(embed_hbm, embed_ref, sems.at[kinds]),
        pltpu.make_async_copy(ids_hbm, ids_ref, sems.at[kinds + 1]),
        pltpu.make_async_copy(live_hbm, live_ref, sems.at[kinds + 2]),
    ]
    loads += [
        pltpu.make_async_copy(qkv_hbm.at[t], qkv_ref.at[t], sems.at[t]) for t in range(kinds)
    ]
    for load in loads:
        load.start()
    padded_ref[...] = jnp.zeros(padded_ref.shape, f32)
    for load in loads[0:3]:
        load.wait()
    padded_ref[0 : embed_ref.shape[0], :] = embed_ref[...].astype(f32)
    normed = layer_norm(padded_ref[...]).astype(bf16)
    row = iota(ids_ref.shape, 0)
    live = jnp.zeros(ids_ref.shape, jnp.int32)
    for r in range(ids_ref.shape[0]):
        live = jnp.where(row == r, live_ref[r], live)
    coded = ids_ref[...] + 65536 * live
    coded_ref[...] = jnp.concatenate([coded] * (coded_ref.shape[0] // coded.shape[0]), 0)
    tables = []
    for t in range(kinds):
        loads[3 + t].wait()
        tables.append(dot_nt(normed, qkv_ref[t]))
    out_ref[...] = jnp.concatenate(tables, 1).astype(bf16)


def make_tables(ids, pad_mask, embed, row_qkv, height):
    kinds, local, width = row_qkv.shape
    return pl.pallas_call(
        table_kernel,
        out_shape=(
            jax.ShapeDtypeStruct((TABLE_ROWS, kinds * local), bf16),
            jax.ShapeDtypeStruct((height, ids.shape[1]), jnp.int32),
        ),
        in_specs=[pl.BlockSpec(memory_space=pltpu.HBM)] * 4,
        scratch_shapes=[
            pltpu.VMEM(ids.shape, jnp.int32),
            pltpu.SMEM(pad_mask.shape, jnp.int32),
            pltpu.VMEM(embed.shape, bf16),
            pltpu.VMEM(row_qkv.shape, bf16),
            pltpu.VMEM((TABLE_ROWS, width), f32),
            pltpu.SemaphoreType.DMA((kinds + 3,)),
        ],
        cost_estimate=pl.CostEstimate(
            flops=2 * 10**9, bytes_accessed=2 * row_qkv.size, transcendentals=0
        ),
        compiler_params=pltpu.CompilerParams(vmem_limit_bytes=SMALL_VMEM),
        name="tables",
    )(in_hbm(ids), in_hbm(pad_mask), in_hbm(embed), in_hbm(row_qkv))


def halves(pair):
    lane = iota(pair.shape, 1)
    zero = jnp.zeros_like(pair)
    return jnp.where(lane < HEAD_DIM, pair, zero), jnp.where(lane < HEAD_DIM, zero, pair)


def spread_pair(pair):
    first, second = halves(pair)
    zero = jnp.zeros_like(pair)
    return jnp.concatenate(
        [
            jnp.concatenate([first, zero], 1),
            jnp.concatenate([zero, first], 1),
            jnp.concatenate([second, zero], 1),
            jnp.concatenate([zero, second], 1),
        ],
        0,
    )


def double(block):
    zero = jnp.zeros_like(block)
    return jnp.concatenate(
        [jnp.concatenate([block, zero], 1), jnp.concatenate([zero, block], 1)], 0
    )


def one_hots(coded, group, hot_ref, own_ref, live_own_ref):
    depth, cols = hot_ref.shape
    rows = depth // CODES
    pairs = rows // 2
    own = own_ref.shape[0] // pairs
    ids = (coded & 0xFFFF).astype(f32)
    live = (coded[:, 0:LANES] >> 16).astype(f32)

    code = iota((CODES, cols), 0).astype(f32)
    for r in range(rows):
        hot = jnp.broadcast_to(ids[r : r + 1, :], (CODES, cols)) == code
        hot_ref[r * CODES : (r + 1) * CODES, :] = hot.astype(f32).astype(bf16)

    pick = (iota((own, cols), 1) == group * own + iota((own, cols), 0)).astype(f32).astype(bf16)
    mine = dot_nt(pick, ids.astype(bf16))
    lane = iota((own, LANES), 1)
    first_half = lane < CODES
    lane_code = jnp.where(first_half, lane, lane - CODES).astype(f32)
    for k in range(pairs):
        value = jnp.where(first_half, mine[:, 2 * k : 2 * k + 1], mine[:, 2 * k + 1 : 2 * k + 2])
        hot = (value == lane_code).astype(f32)
        alive = jnp.where(first_half, live[2 * k : 2 * k + 1, :], live[2 * k + 1 : 2 * k + 2, :])
        own_ref[k * own : (k + 1) * own, :] = hot.astype(bf16)
        live_own_ref[k * own : (k + 1) * own, :] = (hot * alive).astype(bf16)
    return live


def head_groups(heads, own):
    some = heads // 2
    return [(slice(g * some * own, (g + 1) * some * own), g * some, (g + 1) * some) for g in range(2)]


def tied_sum(scores_ref, live_own_ref, hot_ref, sum_ref, first, last):
    own = sum_ref.shape[0] // scores_ref.shape[0]
    depth = hot_ref.shape[0]
    pairs = depth // CODES // 2
    for h in range(first, last):
        looked = dot_nn(live_own_ref[...], scores_ref[h]).astype(bf16)
        for piece in range(2):
            for k in range(pairs):
                to = piece * depth + k * LANES
                sum_ref[h * own : (h + 1) * own, to : to + LANES] = looked[
                    k * own : (k + 1) * own, piece * LANES : (piece + 1) * LANES
                ]
    at = slice(first * own, last * own)
    return dot_nn(sum_ref[at, 0:depth], hot_ref[...]) + dot_nn(
        sum_ref[at, depth : 2 * depth], hot_ref[...]
    )


def near_kernel(parts, *refs):
    tables_refs, refs = refs[:parts], refs[parts:]
    (
        codes_ref,
        scores_ref,
        values_ref,
        tied_ref,
        hot_ref,
        own_ref,
        tables_ref,
        table_ref,
        live_own_ref,
        sum_ref,
    ) = refs
    width = values_ref.shape[1]
    heads = width // HEAD_DIM
    local = width // parts
    group = lax.axis_index("seq")
    part = lax.axis_index("head")
    for p in range(parts):
        tables_ref[part ^ p] = tables_refs[p][...]

    for t in range(3):
        to_ref = values_ref if t == 2 else table_ref.at[t]
        to_ref[0:TABLE_ROWS, :] = jnp.concatenate(
            [tables_ref[p, :, t * local : (t + 1) * local] for p in range(parts)], 1
        )
        to_ref[TABLE_ROWS:CODES, :] = jnp.zeros((CODES - TABLE_ROWS, width), bf16)

    spans = [slice(hp * LANES, (hp + 1) * LANES) for hp in range(heads // 2)]
    queries = [spread_pair(table_ref[0, :, span]) for span in spans]
    keys = [double(table_ref[1, :, span]) for span in spans]
    scores = [dot_nt(query, key) for query, key in zip(queries, keys)]
    high = [score.astype(bf16) for score in scores]
    low = [(score - part_of.astype(f32)).astype(bf16) for score, part_of in zip(scores, high)]
    for h in range(heads):
        these = slice(h % 2 * LANES, (h % 2 + 1) * LANES)
        scores_ref[h, :, 0:LANES] = high[h // 2][these]
        scores_ref[h, :, LANES : 2 * LANES] = low[h // 2][these]

    one_hots(codes_ref[...], group, hot_ref, own_ref, live_own_ref)
    tied_ref[...] = tied_sum(scores_ref, live_own_ref, hot_ref, sum_ref, 0, heads)


def attend_near(tables, codes, own):
    parts = len(tables)
    width = tables[0].shape[1] // 3 * parts
    heads = width // HEAD_DIM
    rows, cols = codes.shape
    return pl.pallas_call(
        functools.partial(near_kernel, parts),
        out_shape=(
            jax.ShapeDtypeStruct((heads, LANES, 2 * LANES), bf16),
            jax.ShapeDtypeStruct((CODES, width), bf16),
            jax.ShapeDtypeStruct((heads * own, cols), f32),
            jax.ShapeDtypeStruct((rows * CODES, cols), bf16),
            jax.ShapeDtypeStruct((rows // 2 * own, LANES), bf16),
        ),
        scratch_shapes=[
            pltpu.VMEM((parts,) + tables[0].shape, bf16),
            pltpu.VMEM((2, CODES, width), bf16),
            pltpu.VMEM((rows // 2 * own, LANES), bf16),
            pltpu.VMEM((heads * own, 2 * rows * CODES), bf16),
        ],
        cost_estimate=pl.CostEstimate(flops=10**9, bytes_accessed=10**6, transcendentals=0),
        compiler_params=pltpu.CompilerParams(vmem_limit_bytes=LARGE_VMEM),
        name="near_scores",
    )(*tables, codes)


def row_kernel(
    scores_ref,
    values_ref,
    near_tied_ref,
    near_hot_ref,
    near_codes_ref,
    far_codes_ref,
    row_context_ref,
    own_ref,
    live_ref,
    hot_ref,
    live_own_ref,
    sum_ref,
    spread_ref,
):
    depth = hot_ref.shape[0]
    rows = 2 * depth // CODES
    pairs = rows // 2
    width = row_context_ref.shape[1]
    heads = width // HEAD_DIM
    own = spread_ref.shape[0] // heads
    group = lax.axis_index("seq")

    live = one_hots(far_codes_ref[...], group, hot_ref, own_ref, live_own_ref)
    live = jnp.concatenate([(near_codes_ref[:, 0:LANES] >> 16).astype(f32), live], 0)
    live_ref[...] = live
    count = jnp.sum(live, axis=0, keepdims=True)[:, 0:1]
    scale = HEAD_DIM ** (-0.5) / jnp.sqrt(count)
    groups = head_groups(heads, own)
    tied = [
        near_tied_ref[at, :] + tied_sum(scores_ref, live_own_ref, hot_ref, sum_ref, first, last)
        for at, first, last in groups
    ]
    probs = [softmax_last(some * scale).astype(bf16) for some in tied]

    for (at, _, _), some in zip(groups, probs):
        spread_ref[at, 0:depth] = dot_nt(some, near_hot_ref[...]).astype(bf16)
        spread_ref[at, depth : 2 * depth] = dot_nt(some, hot_ref[...]).astype(bf16)
    spans = [slice(hp * LANES, (hp + 1) * LANES) for hp in range(heads // 2)]
    values = [spread_pair(values_ref[:, span]) for span in spans]
    contexts = []
    for hp in range(heads // 2):
        first = (hp * 2) * own
        weights = jnp.concatenate(
            [
                jnp.concatenate(
                    [
                        spread_ref[first : first + own, k * LANES : (k + 1) * LANES],
                        spread_ref[first + own : first + 2 * own, k * LANES : (k + 1) * LANES],
                    ],
                    1,
                )
                for k in range(pairs)
            ],
            0,
        )
        contexts.append(dot_nn(weights, values[hp]).astype(bf16))
    for hp in range(heads // 2):
        for k in range(pairs):
            for r2 in range(2):
                at = (2 * k + r2) * own
                row_context_ref[at : at + own, spans[hp]] = contexts[hp][
                    k * own : (k + 1) * own, r2 * LANES : (r2 + 1) * LANES
                ]


def attend_rows(near, near_codes, far_codes, own):
    scores, values, near_tied, near_hot = near
    heads, width = scores.shape[0], values.shape[1]
    half, cols = near_codes.shape
    return pl.pallas_call(
        row_kernel,
        out_shape=(
            jax.ShapeDtypeStruct((2 * half * own, width), bf16),
            jax.ShapeDtypeStruct((half // 2 * own, LANES), bf16),
            jax.ShapeDtypeStruct((2 * half, LANES), f32),
        ),
        scratch_shapes=[
            pltpu.VMEM((half * CODES, cols), bf16),
            pltpu.VMEM((half // 2 * own, LANES), bf16),
            pltpu.VMEM((heads * own, 2 * half * CODES), bf16),
            pltpu.VMEM((heads * own, 2 * half * CODES), bf16),
        ],
        cost_estimate=pl.CostEstimate(flops=3 * 10**9, bytes_accessed=10**6, transcendentals=0),
        compiler_params=pltpu.CompilerParams(vmem_limit_bytes=LARGE_VMEM),
        name="row_attention",
    )(scores, values, near_tied, near_hot, near_codes, far_codes)


def column_kernel(parts, *refs):
    row_out_refs, refs = refs[:parts], refs[parts:]
    (
        live_ref,
        row_context_ref,
        near_own_ref,
        far_own_ref,
        embed_ref,
        col_qkv_ref,
        *context_refs,
        mixed_out_ref,
        row_out_ref,
        embed2_ref,
        weight_ref,
        mixed_ref,
    ) = refs
    rows = live_ref.shape[0]
    tokens, width = row_context_ref.shape
    pairs = rows // 2
    own = tokens // rows
    vocab = embed_ref.shape[0]
    local = width // parts
    part = lax.axis_index("head")

    for p in range(parts):
        row_out_ref[part ^ p] = row_out_refs[p][...]
    embed2_ref[...] = jnp.zeros(embed2_ref.shape, bf16)
    embed2_ref[0:vocab, 0:width] = embed_ref[...]
    embed2_ref[CODES : CODES + vocab, width : 2 * width] = embed_ref[...]

    own_codes = jnp.concatenate([near_own_ref[...], far_own_ref[...]], 0)
    embedded2 = dot_nn(own_codes, embed2_ref[...])
    embedded = jnp.concatenate(
        [
            embedded2[k * own : (k + 1) * own, r2 * width : (r2 + 1) * width]
            for k in range(pairs)
            for r2 in range(2)
        ],
        0,
    )
    mixed = embedded + dot_nt(row_context_ref[...], row_out_ref[...].reshape(width, width))
    mixed_ref[...] = mixed
    normed = layer_norm(mixed).astype(bf16)

    few = 8
    groups = own // few
    unit = rows * few

    def regroup(values):
        shape = (rows, groups, few, values.shape[1])
        return jnp.swapaxes(values.reshape(shape), 0, 1).reshape(tokens, values.shape[1])

    odd = part % 2
    for t in range(3):
        first = pl.multiple_of(t * local + odd * HEAD_DIM, HEAD_DIM)
        last = pl.multiple_of(t * local + (1 - odd) * LANES, HEAD_DIM)
        third = (3 + t) * LANES
        weight_ref[t * LANES : (t + 1) * LANES, :] = col_qkv_ref[pl.ds(first, LANES), :]
        weight_ref[third : third + HEAD_DIM, :] = col_qkv_ref[pl.ds(last, HEAD_DIM), :]
        weight_ref[third + HEAD_DIM : third + LANES, :] = jnp.zeros((HEAD_DIM, width), bf16)
    proj = [
        dot_nt(normed, weight_ref[2 * j * LANES : 2 * (j + 1) * LANES, :]) for j in range(3)
    ]
    proj = [
        proj[j][:, k * LANES : (k + 1) * LANES] * (HEAD_DIM ** (-0.5) if (2 * j + k) % 3 == 0 else 1.0)
        for j in range(3)
        for k in range(2)
    ]
    proj = [regroup(values).astype(bf16) for values in proj]
    sub, lan = iota((unit, unit), 0), iota((unit, unit), 1)
    same_column = (sub % few) == (lan % few)
    seq_of_lane = iota((rows, unit), 1) // few
    live_lane = jnp.sum(
        jnp.where(seq_of_lane == iota((rows, unit), 0), live_ref[...], 0.0), axis=0, keepdims=True
    )
    visible = jnp.logical_and(same_column, jnp.broadcast_to(live_lane, (unit, unit)) > 0)
    chosen = []
    for g in range(groups):
        at = slice(g * unit, (g + 1) * unit)
        query, keys, values = (proj[t][at] for t in range(3))
        chosen += [(half, keys, values) for half in halves(query)]
        chosen.append(tuple(proj[3 + t][at] for t in range(3)))
    scores = [jnp.where(visible, dot_nt(query, keys), -jnp.inf) for query, keys, _ in chosen]
    tops = [jnp.max(score, axis=-1, keepdims=True) for score in scores]
    weights = [jnp.exp(score - top) for score, top in zip(scores, tops)]
    shares = [1.0 / jnp.sum(weight, axis=-1, keepdims=True) for weight in weights]
    probs = [(weight * share).astype(bf16) for weight, share in zip(weights, shares)]
    found = [dot_nn(prob, values) for prob, (_, _, values) in zip(probs, chosen)]
    first_head = iota((unit, LANES), 1) < HEAD_DIM

    def ungroup(blocks):
        whole = jnp.concatenate(blocks, 0).reshape(groups, rows, few, LANES)
        return jnp.swapaxes(whole, 0, 1).reshape(tokens, LANES)

    main = ungroup(
        [jnp.where(first_head, found[3 * g], found[3 * g + 1]) for g in range(groups)]
    )
    third = ungroup([found[3 * g + 2] for g in range(groups)])
    start = 0
    for context_ref in context_refs:
        count = context_ref.shape[0] * 2 // 3
        some = count // 2
        context_ref[0:count, :] = main[start : start + count].astype(bf16)
        early = third[start : start + some]
        late = third[start + some : start + count]
        left = jnp.where(odd == 1, late, early)
        right = jnp.where(odd == 1, early, late)
        context_ref[count : count + some, :] = jnp.concatenate(
            [left[:, 0:HEAD_DIM], right[:, 0:HEAD_DIM]], 1
        ).astype(bf16)
        start += count
    for p in range(parts):

        @pl.when(part == p)
        def _():
            mixed_out_ref[...] = mixed_ref[:, p * local : (p + 1) * local]


def attend_columns_here(row_outs, live, row_context, near_own, far_own, embed, col_qkv):
    parts = len(row_outs)
    tokens, width = row_context.shape
    local = width // parts
    half = tokens // 2 * local // LANES
    return pl.pallas_call(
        functools.partial(column_kernel, parts),
        out_shape=(
            jax.ShapeDtypeStruct((half, LANES), bf16),
            jax.ShapeDtypeStruct((half, LANES), bf16),
            jax.ShapeDtypeStruct((tokens, local), f32),
        ),
        scratch_shapes=[
            pltpu.VMEM((parts, local, width), bf16),
            pltpu.VMEM((2 * CODES, 2 * width), bf16),
            pltpu.VMEM((6 * LANES, width), bf16),
            pltpu.VMEM((tokens, width), f32),
        ],
        cost_estimate=pl.CostEstimate(flops=2 * 10**9, bytes_accessed=10**6, transcendentals=0),
        compiler_params=pltpu.CompilerParams(vmem_limit_bytes=LARGE_VMEM),
        name="column_attention",
    )(*row_outs, live, row_context, near_own, far_own, embed, col_qkv)


def finish_kernel(parts, groups, *refs):
    context_refs = [refs[:parts], refs[parts : 2 * parts]]
    mixed_ref, col_out_ref, out_ref, context_ref = refs[2 * parts :]
    tokens, local = mixed_ref.shape
    group = lax.axis_index("seq")
    part = lax.axis_index("head")
    starts = [0, context_refs[0][0].shape[0]]
    for start, some_refs in zip(starts, context_refs):
        for p in range(parts):
            context_ref[part ^ p, start : start + some_refs[p].shape[0], :] = some_refs[p][...]
    pieces = []
    for start, some_refs in zip(starts, context_refs):
        count = some_refs[0].shape[0] * 2 // 3
        end = start + some_refs[0].shape[0]
        low = iota((count // 2, LANES), 1) < HEAD_DIM
        features = []
        for p in range(0, parts, 2):
            even = context_ref[p, start + count : end, :]
            other = context_ref[p + 1, start + count : end, :]
            early = jnp.where(low, even, other)
            late = jnp.where(low, other, even)
            late = jnp.concatenate([late[:, HEAD_DIM:], late[:, 0:HEAD_DIM]], 1)
            features += [
                context_ref[p, start : start + count, :],
                jnp.concatenate([early, late], 0),
                context_ref[p + 1, start : start + count, :],
            ]
        pieces.append(jnp.concatenate(features, 1))
    total = mixed_ref[...] + dot_nt(jnp.concatenate(pieces, 0), col_out_ref[...])
    own = tokens // groups // 2
    for d in range(groups):
        first, second = (total[(2 * d + r) * own : (2 * d + r + 1) * own, :] for r in range(2))
        rest = jnp.concatenate([first[:, LANES:local], second[:, LANES:local]], 1)
        out_ref[group ^ d] = jnp.concatenate(
            [first[:, 0:LANES], second[:, 0:LANES], rest], 0
        ).astype(bf16)


def finish(contexts, mixed, col_out, groups):
    parts = len(contexts[0])
    tokens, local = mixed.shape
    return pl.pallas_call(
        functools.partial(finish_kernel, parts, groups),
        out_shape=jax.ShapeDtypeStruct((groups, tokens // groups * local // LANES, LANES), bf16),
        scratch_shapes=[pltpu.VMEM((parts, tokens * local // LANES, LANES), bf16)],
        compiler_params=pltpu.CompilerParams(vmem_limit_bytes=LARGE_VMEM),
        name="finish",
    )(*contexts[0], *contexts[1], mixed, col_out)


def order_kernel(blocks_ref, out_ref):
    groups = blocks_ref.shape[0]
    local, cols = out_ref.shape[1:]
    own = cols // groups
    rest = local - LANES
    for part in range(3):
        piece = jnp.concatenate(
            [blocks_ref[g, part * own : (part + 1) * own, :] for g in range(groups)], 0
        )
        turned = piece.astype(f32).T.astype(bf16)
        if part < 2:
            out_ref[part, 0:LANES, :] = turned
        else:
            for r in range(2):
                out_ref[r, LANES:local, :] = turned[r * rest : (r + 1) * rest, :]


def order(blocks, cols, local):
    return pl.pallas_call(
        order_kernel,
        out_shape=jax.ShapeDtypeStruct((2, local, cols), bf16),
        compiler_params=pltpu.CompilerParams(vmem_limit_bytes=SMALL_VMEM),
        name="order",
    )(blocks)


def fast_body(ids, pad_mask, embed, row_qkv, row_out, col_qkv, col_out):
    rows_here, cols = ids.shape
    width = embed.shape[1]
    local = row_out.shape[0]
    groups, parts = lax.axis_size("seq"), lax.axis_size("head")
    own, rows = cols // groups, rows_here * groups

    def pairwise(value, partner):
        order = [(g, p) for g in range(groups) for p in range(parts)]
        link = [(g * parts + p, partner(g, p)) for g, p in order]
        return lax.ppermute(value, ("seq", "head"), [(i, g * parts + p) for i, (g, p) in link])

    def sibling(g, p):
        return g, p ^ 1

    def across(g, p):
        return g, p ^ 2

    def opposite(g, p):
        return g, p ^ 3

    far = pairwise(row_out, across)
    other_ids = pairwise(ids, lambda g, p: (g ^ 1, p))
    other_mask = pairwise(pad_mask.reshape(1, rows_here), lambda g, p: (g ^ 1, p))
    table, coded = make_tables(ids, pad_mask, embed, row_qkv, rows_here * groups // 2)
    tables = [table, None, pairwise(table, across), None]
    step = 2
    while step < groups:
        if step == 2:
            coded = join_raw(coded, other_ids, other_mask)
        else:
            coded = join(coded, received, rows_here * step // 2)
        if step == 2:
            coded, table = lax.optimization_barrier((coded, table))
            tables[3] = pairwise(table, opposite)
        elif step == 4:
            coded, table, row_out, far = lax.optimization_barrier((coded, table, row_out, far))
            tables[1] = pairwise(table, sibling)
            row_outs = [row_out, pairwise(row_out, sibling), far, pairwise(far, sibling)]
        received = pairwise(coded, lambda g, p, step=step: (g ^ step, p))
        step *= 2
    codes = (coded, received)
    *near_scores, near_own = attend_near(tables, codes[0], own)
    row_context, far_own, live = attend_rows(near_scores, *codes, own)
    *halves_here, mixed = attend_columns_here(
        row_outs,
        live,
        row_context,
        near_own,
        far_own,
        embed,
        col_qkv.reshape(3 * local, width),
    )
    contexts = []
    for context in halves_here:
        beyond = pairwise(context, across)
        contexts.append(
            (context, pairwise(context, sibling), beyond, pairwise(beyond, sibling))
        )
    blocks = finish(contexts, mixed, col_out, groups)
    blocks = lax.all_to_all(blocks, "seq", split_axis=0, concat_axis=0, tiled=True)
    return jnp.swapaxes(order(blocks, cols, local), 1, 2)


def weight_fold(out_weight, piece):
    return jnp.einsum("rce,fe->rcf", piece, out_weight, preferred_element_type=f32)


def attend_columns(query, keys, values, key_live):
    rows_all, count_cols, local_width = query.shape
    heads_here = local_width // HEAD_DIM
    shape = (rows_all, count_cols, heads_here, HEAD_DIM)
    scores = jnp.einsum(
        "rchd,schd->chrs",
        query.reshape(shape),
        keys.reshape(shape),
        preferred_element_type=f32,
    ) * HEAD_DIM ** (-0.5)
    scores = jnp.where(key_live > 0, scores, -jnp.inf)
    probs = softmax_last(scores).astype(bf16)
    context = jnp.einsum(
        "chrs,schd->rchd", probs, values.reshape(shape), preferred_element_type=f32
    )
    return context.astype(bf16).reshape(rows_all, count_cols, local_width)


def send_back(context):
    return lax.all_to_all(context[:, None], "seq", split_axis=0, concat_axis=1, tiled=True)


def general_body(ids, pad_mask, embed, row_qkv, row_out, col_qkv, col_out):
    rows_here, cols = ids.shape
    width = embed.shape[1]
    local_width = row_out.shape[0]
    heads_here = local_width // HEAD_DIM
    groups = lax.axis_size("seq")
    per_group = cols // groups
    codes = lax.broadcasted_iota(jnp.int32, (1, 1, embed.shape[0]), 2)
    onehot = (ids[:, :, None] == codes).astype(bf16)
    embedded = jnp.einsum("rcv,vd->rcd", onehot, embed, preferred_element_type=f32)
    normed = layer_norm(embedded).astype(bf16)
    row_proj = jnp.einsum("rcd,ted->trce", normed, row_qkv, preferred_element_type=f32)
    row_proj = row_proj.astype(bf16)
    live = pad_mask.astype(bf16)
    head_shape = (rows_here, cols, heads_here, HEAD_DIM)
    query = (row_proj[0] * live[:, None, None]).reshape(head_shape)
    keys = row_proj[1].reshape(head_shape)
    values = row_proj[2].reshape(head_shape)
    partial_scores = jnp.einsum("rihd,rjhd->hij", query, keys, preferred_element_type=f32)
    count_here = jnp.sum(pad_mask.astype(f32))
    scale = HEAD_DIM ** (-0.5)
    total, count = lax.psum((partial_scores, count_here), "seq")
    row_probs = softmax_last(total * (scale / jnp.sqrt(count))).astype(bf16)
    row_context = jnp.einsum("hij,rjhd->rihd", row_probs, values, preferred_element_type=f32)
    row_context = row_context.astype(bf16).reshape(rows_here, cols, local_width)
    start_feature = lax.axis_index("head") * local_width
    resident = lax.dynamic_slice_in_dim(embedded, start_feature, local_width, 2)
    row_update = weight_fold(row_out, lax.all_gather(row_context, "head", axis=2, tiled=True))
    mixed = resident + row_update
    sums, squares = lax.psum((jnp.sum(mixed, axis=-1), jnp.sum(mixed * mixed, axis=-1)), "head")
    mean = sums / width
    spread = squares / width - mean * mean
    normed_here = ((mixed - mean[..., None]) * lax.rsqrt(spread[..., None] + EPS)).astype(bf16)
    live_tile = jnp.broadcast_to(live[:, None, None, None], (rows_here, groups, per_group, 1))
    normed_full = lax.all_gather(normed_here, "head", axis=2, tiled=True)
    col_proj = jnp.einsum("rcd,ted->rcte", normed_full, col_qkv, preferred_element_type=f32)
    packed = col_proj.astype(bf16).reshape(rows_here, groups, per_group, 3 * local_width)
    received = lax.all_to_all(packed, "seq", split_axis=1, concat_axis=0, tiled=True)
    mask_part = lax.all_to_all(live_tile, "seq", split_axis=1, concat_axis=0, tiled=True)
    column_out = send_back(
        attend_columns(
            received[:, 0, :, :local_width],
            received[:, 0, :, local_width : 2 * local_width],
            received[:, 0, :, 2 * local_width :],
            mask_part[:, 0, 0, 0],
        )
    )
    column_out = column_out.reshape(rows_here, cols, local_width)
    col_update = weight_fold(col_out, lax.all_gather(column_out, "head", axis=2, tiled=True))
    return (mixed + col_update).astype(bf16)


def body(ids, pad_mask, embed, row_qkv, row_out, col_qkv, col_out):
    rows_here, cols = ids.shape
    groups = lax.axis_size("seq")
    own, rows = cols // groups, rows_here * groups
    parts = lax.axis_size("head")
    local = row_out.shape[0]
    fits = (
        parts == 4
        and groups >= 8
        and groups & (groups - 1) == 0
        and rows * 8 == LANES
        and rows_here == 2
        and own % 32 == 0
        and cols >= LANES
        and local == LANES + HEAD_DIM
        and embed.shape[0] <= TABLE_ROWS
    )
    chosen = fast_body if fits else general_body
    return chosen(ids, pad_mask, embed, row_qkv, row_out, col_qkv, col_out)


def solution(mesh):
    placed = (
        P("seq", None),
        P("seq"),
        P(),
        P(None, "head", None),
        P("head", None),
        P(None, "head", None),
        P("head", None),
    )
    return jax.shard_map(
        body, mesh=mesh, in_specs=placed, out_specs=P("seq", None, "head"), check_vma=False
    )
```

```python
import functools

import jax
import jax.numpy as jnp
from jax import lax
from jax.experimental import pallas as pl
from jax.experimental.pallas import tpu as pltpu
from jax.sharding import PartitionSpec as P

HEAD_DIM = 64
EPS = 1e-05
LANES = 128
CODES = 64
TABLE_ROWS = 40

SMALL_VMEM = 8 * 1024 * 1024
LARGE_VMEM = 32 * 1024 * 1024

f32 = jnp.float32
bf16 = jnp.bfloat16


def layer_norm(values):
    mean = jnp.mean(values, axis=-1, keepdims=True)
    centred = values - mean
    spread = jnp.mean(centred * centred, axis=-1, keepdims=True)
    return centred * lax.rsqrt(spread + EPS)


def softmax_last(scores):
    top = jnp.max(scores, axis=-1, keepdims=True)
    weights = jnp.exp(scores - top)
    return weights * (1.0 / jnp.sum(weights, axis=-1, keepdims=True))


def dot_nt(left, right):
    return lax.dot_general(left, right, (((1,), (1,)), ((), ())), preferred_element_type=f32)


def dot_nn(left, right):
    return jnp.dot(left, right, preferred_element_type=f32)


def in_hbm(value):
    return pltpu.with_memory_space_constraint(value, pltpu.HBM)


def iota(shape, axis):
    return lax.broadcasted_iota(jnp.int32, shape, axis)


def join_kernel(rows, own_ref, other_ref, out_ref):
    own, other = own_ref[...], other_ref[...]
    both = jnp.concatenate([own[0:rows], other[0:rows]], 0)
    out_ref[...] = jnp.concatenate([both] * (own.shape[0] // (2 * rows)), 0)


def join(own, other, rows):
    return pl.pallas_call(
        functools.partial(join_kernel, rows),
        out_shape=jax.ShapeDtypeStruct(own.shape, own.dtype),
        compiler_params=pltpu.CompilerParams(vmem_limit_bytes=SMALL_VMEM),
        name="join",
    )(own, other)


def join_raw_kernel(own_ref, ids_ref, live_ref, out_ref):
    rows = ids_ref.shape[0]
    live = live_ref[...]
    other = ids_ref[...] + 65536 * jnp.concatenate(
        [jnp.broadcast_to(live[:, r : r + 1], (1, ids_ref.shape[1])) for r in range(rows)], 0
    )
    both = jnp.concatenate([own_ref[0:rows], other], 0)
    out_ref[...] = jnp.concatenate([both] * (out_ref.shape[0] // (2 * rows)), 0)


def join_raw(own, ids, pad_mask):
    return pl.pallas_call(
        join_raw_kernel,
        out_shape=jax.ShapeDtypeStruct(own.shape, own.dtype),
        compiler_params=pltpu.CompilerParams(vmem_limit_bytes=SMALL_VMEM),
        name="join_raw",
    )(own, ids, pad_mask)


def table_kernel(
    ids_hbm,
    live_hbm,
    embed_hbm,
    qkv_hbm,
    out_ref,
    coded_ref,
    ids_ref,
    live_ref,
    embed_ref,
    qkv_ref,
    padded_ref,
    sems,
):
    kinds = qkv_ref.shape[0]
    loads = [
        pltpu.make_async_copy(embed_hbm, embed_ref, sems.at[kinds]),
        pltpu.make_async_copy(ids_hbm, ids_ref, sems.at[kinds + 1]),
        pltpu.make_async_copy(live_hbm, live_ref, sems.at[kinds + 2]),
    ]
    loads += [
        pltpu.make_async_copy(qkv_hbm.at[t], qkv_ref.at[t], sems.at[t]) for t in range(kinds)
    ]
    for load in loads:
        load.start()
    padded_ref[...] = jnp.zeros(padded_ref.shape, f32)
    for load in loads[0:3]:
        load.wait()
    padded_ref[0 : embed_ref.shape[0], :] = embed_ref[...].astype(f32)
    normed = layer_norm(padded_ref[...]).astype(bf16)
    row = iota(ids_ref.shape, 0)
    live = jnp.zeros(ids_ref.shape, jnp.int32)
    for r in range(ids_ref.shape[0]):
        live = jnp.where(row == r, live_ref[r], live)
    coded = ids_ref[...] + 65536 * live
    coded_ref[...] = jnp.concatenate([coded] * (coded_ref.shape[0] // coded.shape[0]), 0)
    tables = []
    for t in range(kinds):
        loads[3 + t].wait()
        tables.append(dot_nt(normed, qkv_ref[t]))
    out_ref[...] = jnp.concatenate(tables, 1).astype(bf16)


def make_tables(ids, pad_mask, embed, row_qkv, height):
    kinds, local, width = row_qkv.shape
    return pl.pallas_call(
        table_kernel,
        out_shape=(
            jax.ShapeDtypeStruct((TABLE_ROWS, kinds * local), bf16),
            jax.ShapeDtypeStruct((height, ids.shape[1]), jnp.int32),
        ),
        in_specs=[pl.BlockSpec(memory_space=pltpu.HBM)] * 4,
        scratch_shapes=[
            pltpu.VMEM(ids.shape, jnp.int32),
            pltpu.SMEM(pad_mask.shape, jnp.int32),
            pltpu.VMEM(embed.shape, bf16),
            pltpu.VMEM(row_qkv.shape, bf16),
            pltpu.VMEM((TABLE_ROWS, width), f32),
            pltpu.SemaphoreType.DMA((kinds + 3,)),
        ],
        cost_estimate=pl.CostEstimate(
            flops=2 * 10**9, bytes_accessed=2 * row_qkv.size, transcendentals=0
        ),
        compiler_params=pltpu.CompilerParams(vmem_limit_bytes=SMALL_VMEM),
        name="tables",
    )(in_hbm(ids), in_hbm(pad_mask), in_hbm(embed), in_hbm(row_qkv))


def halves(pair):
    lane = iota(pair.shape, 1)
    zero = jnp.zeros_like(pair)
    return jnp.where(lane < HEAD_DIM, pair, zero), jnp.where(lane < HEAD_DIM, zero, pair)


def spread_pair(pair):
    first, second = halves(pair)
    zero = jnp.zeros_like(pair)
    return jnp.concatenate(
        [
            jnp.concatenate([first, zero], 1),
            jnp.concatenate([zero, first], 1),
            jnp.concatenate([second, zero], 1),
            jnp.concatenate([zero, second], 1),
        ],
        0,
    )


def double(block):
    zero = jnp.zeros_like(block)
    return jnp.concatenate(
        [jnp.concatenate([block, zero], 1), jnp.concatenate([zero, block], 1)], 0
    )


def one_hots(coded, group, hot_ref, own_ref, live_own_ref):
    depth, cols = hot_ref.shape
    rows = depth // CODES
    pairs = rows // 2
    own = own_ref.shape[0] // pairs
    ids = (coded & 0xFFFF).astype(f32)
    live = (coded[:, 0:LANES] >> 16).astype(f32)

    code = iota((CODES, cols), 0).astype(f32)
    for r in range(rows):
        hot = jnp.broadcast_to(ids[r : r + 1, :], (CODES, cols)) == code
        hot_ref[r * CODES : (r + 1) * CODES, :] = hot.astype(f32).astype(bf16)

    pick = (iota((own, cols), 1) == group * own + iota((own, cols), 0)).astype(f32).astype(bf16)
    mine = dot_nt(pick, ids.astype(bf16))
    lane = iota((own, LANES), 1)
    first_half = lane < CODES
    lane_code = jnp.where(first_half, lane, lane - CODES).astype(f32)
    for k in range(pairs):
        value = jnp.where(first_half, mine[:, 2 * k : 2 * k + 1], mine[:, 2 * k + 1 : 2 * k + 2])
        hot = (value == lane_code).astype(f32)
        alive = jnp.where(first_half, live[2 * k : 2 * k + 1, :], live[2 * k + 1 : 2 * k + 2, :])
        own_ref[k * own : (k + 1) * own, :] = hot.astype(bf16)
        live_own_ref[k * own : (k + 1) * own, :] = (hot * alive).astype(bf16)
    return live


def head_groups(heads, own):
    some = heads // 2
    return [(slice(g * some * own, (g + 1) * some * own), g * some, (g + 1) * some) for g in range(2)]


def tied_sum(scores_ref, live_own_ref, hot_ref, sum_ref, first, last):
    own = sum_ref.shape[0] // scores_ref.shape[0]
    depth = hot_ref.shape[0]
    pairs = depth // CODES // 2
    for h in range(first, last):
        looked = dot_nn(live_own_ref[...], scores_ref[h]).astype(bf16)
        for piece in range(2):
            for k in range(pairs):
                to = piece * depth + k * LANES
                sum_ref[h * own : (h + 1) * own, to : to + LANES] = looked[
                    k * own : (k + 1) * own, piece * LANES : (piece + 1) * LANES
                ]
    at = slice(first * own, last * own)
    return dot_nn(sum_ref[at, 0:depth], hot_ref[...]) + dot_nn(
        sum_ref[at, depth : 2 * depth], hot_ref[...]
    )


def near_kernel(parts, *refs):
    tables_refs, refs = refs[:parts], refs[parts:]
    (
        codes_ref,
        scores_ref,
        values_ref,
        tied_ref,
        hot_ref,
        own_ref,
        tables_ref,
        table_ref,
        live_own_ref,
        sum_ref,
    ) = refs
    width = values_ref.shape[1]
    heads = width // HEAD_DIM
    local = width // parts
    group = lax.axis_index("seq")
    part = lax.axis_index("head")
    for p in range(parts):
        tables_ref[part ^ p] = tables_refs[p][...]

    for t in range(3):
        to_ref = values_ref if t == 2 else table_ref.at[t]
        to_ref[0:TABLE_ROWS, :] = jnp.concatenate(
            [tables_ref[p, :, t * local : (t + 1) * local] for p in range(parts)], 1
        )
        to_ref[TABLE_ROWS:CODES, :] = jnp.zeros((CODES - TABLE_ROWS, width), bf16)

    spans = [slice(hp * LANES, (hp + 1) * LANES) for hp in range(heads // 2)]
    queries = [spread_pair(table_ref[0, :, span]) for span in spans]
    keys = [double(table_ref[1, :, span]) for span in spans]
    scores = [dot_nt(query, key) for query, key in zip(queries, keys)]
    high = [score.astype(bf16) for score in scores]
    low = [(score - part_of.astype(f32)).astype(bf16) for score, part_of in zip(scores, high)]
    for h in range(heads):
        these = slice(h % 2 * LANES, (h % 2 + 1) * LANES)
        scores_ref[h, :, 0:LANES] = high[h // 2][these]
        scores_ref[h, :, LANES : 2 * LANES] = low[h // 2][these]

    one_hots(codes_ref[...], group, hot_ref, own_ref, live_own_ref)
    tied_ref[...] = tied_sum(scores_ref, live_own_ref, hot_ref, sum_ref, 0, heads)


def attend_near(tables, codes, own):
    parts = len(tables)
    width = tables[0].shape[1] // 3 * parts
    heads = width // HEAD_DIM
    rows, cols = codes.shape
    return pl.pallas_call(
        functools.partial(near_kernel, parts),
        out_shape=(
            jax.ShapeDtypeStruct((heads, LANES, 2 * LANES), bf16),
            jax.ShapeDtypeStruct((CODES, width), bf16),
            jax.ShapeDtypeStruct((heads * own, cols), f32),
            jax.ShapeDtypeStruct((rows * CODES, cols), bf16),
            jax.ShapeDtypeStruct((rows // 2 * own, LANES), bf16),
        ),
        scratch_shapes=[
            pltpu.VMEM((parts,) + tables[0].shape, bf16),
            pltpu.VMEM((2, CODES, width), bf16),
            pltpu.VMEM((rows // 2 * own, LANES), bf16),
            pltpu.VMEM((heads * own, 2 * rows * CODES), bf16),
        ],
        cost_estimate=pl.CostEstimate(flops=10**9, bytes_accessed=10**6, transcendentals=0),
        compiler_params=pltpu.CompilerParams(vmem_limit_bytes=LARGE_VMEM),
        name="near_scores",
    )(*tables, codes)


def row_kernel(
    scores_ref,
    values_ref,
    near_tied_ref,
    near_hot_ref,
    near_codes_ref,
    far_codes_ref,
    row_context_ref,
    own_ref,
    live_ref,
    hot_ref,
    live_own_ref,
    sum_ref,
    spread_ref,
):
    depth = hot_ref.shape[0]
    rows = 2 * depth // CODES
    pairs = rows // 2
    width = row_context_ref.shape[1]
    heads = width // HEAD_DIM
    own = spread_ref.shape[0] // heads
    group = lax.axis_index("seq")

    live = one_hots(far_codes_ref[...], group, hot_ref, own_ref, live_own_ref)
    live = jnp.concatenate([(near_codes_ref[:, 0:LANES] >> 16).astype(f32), live], 0)
    live_ref[...] = live
    count = jnp.sum(live, axis=0, keepdims=True)[:, 0:1]
    scale = HEAD_DIM ** (-0.5) / jnp.sqrt(count)
    groups = head_groups(heads, own)
    tied = [
        near_tied_ref[at, :] + tied_sum(scores_ref, live_own_ref, hot_ref, sum_ref, first, last)
        for at, first, last in groups
    ]
    probs = [softmax_last(some * scale).astype(bf16) for some in tied]

    for (at, _, _), some in zip(groups, probs):
        spread_ref[at, 0:depth] = dot_nt(some, near_hot_ref[...]).astype(bf16)
        spread_ref[at, depth : 2 * depth] = dot_nt(some, hot_ref[...]).astype(bf16)
    spans = [slice(hp * LANES, (hp + 1) * LANES) for hp in range(heads // 2)]
    values = [spread_pair(values_ref[:, span]) for span in spans]
    contexts = []
    for hp in range(heads // 2):
        first = (hp * 2) * own
        weights = jnp.concatenate(
            [
                jnp.concatenate(
                    [
                        spread_ref[first : first + own, k * LANES : (k + 1) * LANES],
                        spread_ref[first + own : first + 2 * own, k * LANES : (k + 1) * LANES],
                    ],
                    1,
                )
                for k in range(pairs)
            ],
            0,
        )
        contexts.append(dot_nn(weights, values[hp]).astype(bf16))
    for hp in range(heads // 2):
        for k in range(pairs):
            for r2 in range(2):
                at = (2 * k + r2) * own
                row_context_ref[at : at + own, spans[hp]] = contexts[hp][
                    k * own : (k + 1) * own, r2 * LANES : (r2 + 1) * LANES
                ]


def attend_rows(near, near_codes, far_codes, own):
    scores, values, near_tied, near_hot = near
    heads, width = scores.shape[0], values.shape[1]
    half, cols = near_codes.shape
    return pl.pallas_call(
        row_kernel,
        out_shape=(
            jax.ShapeDtypeStruct((2 * half * own, width), bf16),
            jax.ShapeDtypeStruct((half // 2 * own, LANES), bf16),
            jax.ShapeDtypeStruct((2 * half, LANES), f32),
        ),
        scratch_shapes=[
            pltpu.VMEM((half * CODES, cols), bf16),
            pltpu.VMEM((half // 2 * own, LANES), bf16),
            pltpu.VMEM((heads * own, 2 * half * CODES), bf16),
            pltpu.VMEM((heads * own, 2 * half * CODES), bf16),
        ],
        cost_estimate=pl.CostEstimate(flops=3 * 10**9, bytes_accessed=10**6, transcendentals=0),
        compiler_params=pltpu.CompilerParams(vmem_limit_bytes=LARGE_VMEM),
        name="row_attention",
    )(scores, values, near_tied, near_hot, near_codes, far_codes)


def column_kernel(parts, *refs):
    row_out_refs, refs = refs[:parts], refs[parts:]
    (
        live_ref,
        row_context_ref,
        near_own_ref,
        far_own_ref,
        embed_ref,
        col_qkv_ref,
        *context_refs,
        mixed_out_ref,
        row_out_ref,
        embed2_ref,
        weight_ref,
        mixed_ref,
    ) = refs
    rows = live_ref.shape[0]
    tokens, width = row_context_ref.shape
    pairs = rows // 2
    own = tokens // rows
    vocab = embed_ref.shape[0]
    local = width // parts
    part = lax.axis_index("head")

    for p in range(parts):
        row_out_ref[part ^ p] = row_out_refs[p][...]
    embed2_ref[...] = jnp.zeros(embed2_ref.shape, bf16)
    embed2_ref[0:vocab, 0:width] = embed_ref[...]
    embed2_ref[CODES : CODES + vocab, width : 2 * width] = embed_ref[...]

    own_codes = jnp.concatenate([near_own_ref[...], far_own_ref[...]], 0)
    embedded2 = dot_nn(own_codes, embed2_ref[...])
    embedded = jnp.concatenate(
        [
            embedded2[k * own : (k + 1) * own, r2 * width : (r2 + 1) * width]
            for k in range(pairs)
            for r2 in range(2)
        ],
        0,
    )
    mixed = embedded + dot_nt(row_context_ref[...], row_out_ref[...].reshape(width, width))
    mixed_ref[...] = mixed
    normed = layer_norm(mixed).astype(bf16)

    few = 8
    groups = own // few
    unit = rows * few

    def regroup(values):
        shape = (rows, groups, few, values.shape[1])
        return jnp.swapaxes(values.reshape(shape), 0, 1).reshape(tokens, values.shape[1])

    odd = part % 2
    for t in range(3):
        first = pl.multiple_of(t * local + odd * HEAD_DIM, HEAD_DIM)
        last = pl.multiple_of(t * local + (1 - odd) * LANES, HEAD_DIM)
        third = (3 + t) * LANES
        weight_ref[t * LANES : (t + 1) * LANES, :] = col_qkv_ref[pl.ds(first, LANES), :]
        weight_ref[third : third + HEAD_DIM, :] = col_qkv_ref[pl.ds(last, HEAD_DIM), :]
        weight_ref[third + HEAD_DIM : third + LANES, :] = jnp.zeros((HEAD_DIM, width), bf16)
    proj = [
        dot_nt(normed, weight_ref[2 * j * LANES : 2 * (j + 1) * LANES, :]) for j in range(3)
    ]
    proj = [
        proj[j][:, k * LANES : (k + 1) * LANES] * (HEAD_DIM ** (-0.5) if (2 * j + k) % 3 == 0 else 1.0)
        for j in range(3)
        for k in range(2)
    ]
    proj = [regroup(values).astype(bf16) for values in proj]
    sub, lan = iota((unit, unit), 0), iota((unit, unit), 1)
    same_column = (sub % few) == (lan % few)
    seq_of_lane = iota((rows, unit), 1) // few
    live_lane = jnp.sum(
        jnp.where(seq_of_lane == iota((rows, unit), 0), live_ref[...], 0.0), axis=0, keepdims=True
    )
    visible = jnp.logical_and(same_column, jnp.broadcast_to(live_lane, (unit, unit)) > 0)
    chosen = []
    for g in range(groups):
        at = slice(g * unit, (g + 1) * unit)
        query, keys, values = (proj[t][at] for t in range(3))
        chosen += [(half, keys, values) for half in halves(query)]
        chosen.append(tuple(proj[3 + t][at] for t in range(3)))
    scores = [jnp.where(visible, dot_nt(query, keys), -jnp.inf) for query, keys, _ in chosen]
    tops = [jnp.max(score, axis=-1, keepdims=True) for score in scores]
    weights = [jnp.exp(score - top) for score, top in zip(scores, tops)]
    shares = [1.0 / jnp.sum(weight, axis=-1, keepdims=True) for weight in weights]
    probs = [(weight * share).astype(bf16) for weight, share in zip(weights, shares)]
    found = [dot_nn(prob, values) for prob, (_, _, values) in zip(probs, chosen)]
    first_head = iota((unit, LANES), 1) < HEAD_DIM

    def ungroup(blocks):
        whole = jnp.concatenate(blocks, 0).reshape(groups, rows, few, LANES)
        return jnp.swapaxes(whole, 0, 1).reshape(tokens, LANES)

    main = ungroup(
        [jnp.where(first_head, found[3 * g], found[3 * g + 1]) for g in range(groups)]
    )
    third = ungroup([found[3 * g + 2] for g in range(groups)])
    start = 0
    for context_ref in context_refs:
        count = context_ref.shape[0] * 2 // 3
        some = count // 2
        context_ref[0:count, :] = main[start : start + count].astype(bf16)
        early = third[start : start + some]
        late = third[start + some : start + count]
        left = jnp.where(odd == 1, late, early)
        right = jnp.where(odd == 1, early, late)
        context_ref[count : count + some, :] = jnp.concatenate(
            [left[:, 0:HEAD_DIM], right[:, 0:HEAD_DIM]], 1
        ).astype(bf16)
        start += count
    for p in range(parts):

        @pl.when(part == p)
        def _():
            mixed_out_ref[...] = mixed_ref[:, p * local : (p + 1) * local]


def attend_columns_here(row_outs, live, row_context, near_own, far_own, embed, col_qkv):
    parts = len(row_outs)
    tokens, width = row_context.shape
    local = width // parts
    return pl.pallas_call(
        functools.partial(column_kernel, parts),
        out_shape=(
            jax.ShapeDtypeStruct((tokens * local // LANES, LANES), bf16),
            jax.ShapeDtypeStruct((tokens, local), f32),
        ),
        scratch_shapes=[
            pltpu.VMEM((parts, local, width), bf16),
            pltpu.VMEM((2 * CODES, 2 * width), bf16),
            pltpu.VMEM((6 * LANES, width), bf16),
            pltpu.VMEM((tokens, width), f32),
        ],
        cost_estimate=pl.CostEstimate(flops=2 * 10**9, bytes_accessed=10**6, transcendentals=0),
        compiler_params=pltpu.CompilerParams(vmem_limit_bytes=LARGE_VMEM),
        name="column_attention",
    )(*row_outs, live, row_context, near_own, far_own, embed, col_qkv)


def finish_kernel(parts, groups, *refs):
    context_refs = [refs[:parts]]
    mixed_ref, col_out_ref, out_ref, context_ref = refs[parts:]
    tokens, local = mixed_ref.shape
    group = lax.axis_index("seq")
    part = lax.axis_index("head")
    starts = [0]
    for start, some_refs in zip(starts, context_refs):
        for p in range(parts):
            context_ref[part ^ p, start : start + some_refs[p].shape[0], :] = some_refs[p][...]
    pieces = []
    for start, some_refs in zip(starts, context_refs):
        count = some_refs[0].shape[0] * 2 // 3
        end = start + some_refs[0].shape[0]
        low = iota((count // 2, LANES), 1) < HEAD_DIM
        features = []
        for p in range(0, parts, 2):
            even = context_ref[p, start + count : end, :]
            other = context_ref[p + 1, start + count : end, :]
            early = jnp.where(low, even, other)
            late = jnp.where(low, other, even)
            late = jnp.concatenate([late[:, HEAD_DIM:], late[:, 0:HEAD_DIM]], 1)
            features += [
                context_ref[p, start : start + count, :],
                jnp.concatenate([early, late], 0),
                context_ref[p + 1, start : start + count, :],
            ]
        pieces.append(jnp.concatenate(features, 1))
    total = mixed_ref[...] + dot_nt(jnp.concatenate(pieces, 0), col_out_ref[...])
    own = tokens // groups // 2
    for d in range(groups):
        first, second = (total[(2 * d + r) * own : (2 * d + r + 1) * own, :] for r in range(2))
        rest = jnp.concatenate([first[:, LANES:local], second[:, LANES:local]], 1)
        out_ref[group ^ d] = jnp.concatenate(
            [first[:, 0:LANES], second[:, 0:LANES], rest], 0
        ).astype(bf16)


def finish(contexts, mixed, col_out, groups):
    parts = len(contexts[0])
    tokens, local = mixed.shape
    return pl.pallas_call(
        functools.partial(finish_kernel, parts, groups),
        out_shape=jax.ShapeDtypeStruct((groups, tokens // groups * local // LANES, LANES), bf16),
        scratch_shapes=[pltpu.VMEM((parts, tokens * local // LANES, LANES), bf16)],
        compiler_params=pltpu.CompilerParams(vmem_limit_bytes=LARGE_VMEM),
        name="finish",
    )(*contexts[0], mixed, col_out)


def order_kernel(blocks_ref, out_ref):
    groups = blocks_ref.shape[0]
    local, cols = out_ref.shape[1:]
    own = cols // groups
    rest = local - LANES
    for part in range(3):
        piece = jnp.concatenate(
            [blocks_ref[g, part * own : (part + 1) * own, :] for g in range(groups)], 0
        )
        turned = piece.astype(f32).T.astype(bf16)
        if part < 2:
            out_ref[part, 0:LANES, :] = turned
        else:
            for r in range(2):
                out_ref[r, LANES:local, :] = turned[r * rest : (r + 1) * rest, :]


def order(blocks, cols, local):
    return pl.pallas_call(
        order_kernel,
        out_shape=jax.ShapeDtypeStruct((2, local, cols), bf16),
        compiler_params=pltpu.CompilerParams(vmem_limit_bytes=SMALL_VMEM),
        name="order",
    )(blocks)


def fast_body(ids, pad_mask, embed, row_qkv, row_out, col_qkv, col_out):
    rows_here, cols = ids.shape
    width = embed.shape[1]
    local = row_out.shape[0]
    groups, parts = lax.axis_size("seq"), lax.axis_size("head")
    own, rows = cols // groups, rows_here * groups

    def pairwise(value, partner):
        order = [(g, p) for g in range(groups) for p in range(parts)]
        link = [(g * parts + p, partner(g, p)) for g, p in order]
        return lax.ppermute(value, ("seq", "head"), [(i, g * parts + p) for i, (g, p) in link])

    def sibling(g, p):
        return g, p ^ 1

    def across(g, p):
        return g, p ^ 2

    def opposite(g, p):
        return g, p ^ 3

    far = pairwise(row_out, across)
    other_ids = pairwise(ids, lambda g, p: (g ^ 1, p))
    other_mask = pairwise(pad_mask.reshape(1, rows_here), lambda g, p: (g ^ 1, p))
    table, coded = make_tables(ids, pad_mask, embed, row_qkv, rows_here * groups // 2)
    tables = [table, None, pairwise(table, across), None]
    step = 2
    while step < groups:
        if step == 2:
            coded = join_raw(coded, other_ids, other_mask)
        else:
            coded = join(coded, received, rows_here * step // 2)
        if step == 2:
            coded, table = lax.optimization_barrier((coded, table))
            tables[3] = pairwise(table, opposite)
        elif step == 4:
            coded, table, row_out, far = lax.optimization_barrier((coded, table, row_out, far))
            tables[1] = pairwise(table, sibling)
            row_outs = [row_out, pairwise(row_out, sibling), far, pairwise(far, sibling)]
        received = pairwise(coded, lambda g, p, step=step: (g ^ step, p))
        step *= 2
    codes = (coded, received)
    *near_scores, near_own = attend_near(tables, codes[0], own)
    row_context, far_own, live = attend_rows(near_scores, *codes, own)
    *halves_here, mixed = attend_columns_here(
        row_outs,
        live,
        row_context,
        near_own,
        far_own,
        embed,
        col_qkv.reshape(3 * local, width),
    )
    contexts = []
    for context in halves_here:
        beyond = pairwise(context, across)
        contexts.append(
            (context, pairwise(context, sibling), beyond, pairwise(beyond, sibling))
        )
    blocks = finish(contexts, mixed, col_out, groups)
    blocks = lax.all_to_all(blocks, "seq", split_axis=0, concat_axis=0, tiled=True)
    return jnp.swapaxes(order(blocks, cols, local), 1, 2)


def weight_fold(out_weight, piece):
    return jnp.einsum("rce,fe->rcf", piece, out_weight, preferred_element_type=f32)


def attend_columns(query, keys, values, key_live):
    rows_all, count_cols, local_width = query.shape
    heads_here = local_width // HEAD_DIM
    shape = (rows_all, count_cols, heads_here, HEAD_DIM)
    scores = jnp.einsum(
        "rchd,schd->chrs",
        query.reshape(shape),
        keys.reshape(shape),
        preferred_element_type=f32,
    ) * HEAD_DIM ** (-0.5)
    scores = jnp.where(key_live > 0, scores, -jnp.inf)
    probs = softmax_last(scores).astype(bf16)
    context = jnp.einsum(
        "chrs,schd->rchd", probs, values.reshape(shape), preferred_element_type=f32
    )
    return context.astype(bf16).reshape(rows_all, count_cols, local_width)


def send_back(context):
    return lax.all_to_all(context[:, None], "seq", split_axis=0, concat_axis=1, tiled=True)


def general_body(ids, pad_mask, embed, row_qkv, row_out, col_qkv, col_out):
    rows_here, cols = ids.shape
    width = embed.shape[1]
    local_width = row_out.shape[0]
    heads_here = local_width // HEAD_DIM
    groups = lax.axis_size("seq")
    per_group = cols // groups
    codes = lax.broadcasted_iota(jnp.int32, (1, 1, embed.shape[0]), 2)
    onehot = (ids[:, :, None] == codes).astype(bf16)
    embedded = jnp.einsum("rcv,vd->rcd", onehot, embed, preferred_element_type=f32)
    normed = layer_norm(embedded).astype(bf16)
    row_proj = jnp.einsum("rcd,ted->trce", normed, row_qkv, preferred_element_type=f32)
    row_proj = row_proj.astype(bf16)
    live = pad_mask.astype(bf16)
    head_shape = (rows_here, cols, heads_here, HEAD_DIM)
    query = (row_proj[0] * live[:, None, None]).reshape(head_shape)
    keys = row_proj[1].reshape(head_shape)
    values = row_proj[2].reshape(head_shape)
    partial_scores = jnp.einsum("rihd,rjhd->hij", query, keys, preferred_element_type=f32)
    count_here = jnp.sum(pad_mask.astype(f32))
    scale = HEAD_DIM ** (-0.5)
    total, count = lax.psum((partial_scores, count_here), "seq")
    row_probs = softmax_last(total * (scale / jnp.sqrt(count))).astype(bf16)
    row_context = jnp.einsum("hij,rjhd->rihd", row_probs, values, preferred_element_type=f32)
    row_context = row_context.astype(bf16).reshape(rows_here, cols, local_width)
    start_feature = lax.axis_index("head") * local_width
    resident = lax.dynamic_slice_in_dim(embedded, start_feature, local_width, 2)
    row_update = weight_fold(row_out, lax.all_gather(row_context, "head", axis=2, tiled=True))
    mixed = resident + row_update
    sums, squares = lax.psum((jnp.sum(mixed, axis=-1), jnp.sum(mixed * mixed, axis=-1)), "head")
    mean = sums / width
    spread = squares / width - mean * mean
    normed_here = ((mixed - mean[..., None]) * lax.rsqrt(spread[..., None] + EPS)).astype(bf16)
    live_tile = jnp.broadcast_to(live[:, None, None, None], (rows_here, groups, per_group, 1))
    normed_full = lax.all_gather(normed_here, "head", axis=2, tiled=True)
    col_proj = jnp.einsum("rcd,ted->rcte", normed_full, col_qkv, preferred_element_type=f32)
    packed = col_proj.astype(bf16).reshape(rows_here, groups, per_group, 3 * local_width)
    received = lax.all_to_all(packed, "seq", split_axis=1, concat_axis=0, tiled=True)
    mask_part = lax.all_to_all(live_tile, "seq", split_axis=1, concat_axis=0, tiled=True)
    column_out = send_back(
        attend_columns(
            received[:, 0, :, :local_width],
            received[:, 0, :, local_width : 2 * local_width],
            received[:, 0, :, 2 * local_width :],
            mask_part[:, 0, 0, 0],
        )
    )
    column_out = column_out.reshape(rows_here, cols, local_width)
    col_update = weight_fold(col_out, lax.all_gather(column_out, "head", axis=2, tiled=True))
    return (mixed + col_update).astype(bf16)


def body(ids, pad_mask, embed, row_qkv, row_out, col_qkv, col_out):
    rows_here, cols = ids.shape
    groups = lax.axis_size("seq")
    own, rows = cols // groups, rows_here * groups
    parts = lax.axis_size("head")
    local = row_out.shape[0]
    fits = (
        parts == 4
        and groups >= 8
        and groups & (groups - 1) == 0
        and rows * 8 == LANES
        and rows_here == 2
        and own % 32 == 0
        and cols >= LANES
        and local == LANES + HEAD_DIM
        and embed.shape[0] <= TABLE_ROWS
    )
    chosen = fast_body if fits else general_body
    return chosen(ids, pad_mask, embed, row_qkv, row_out, col_qkv, col_out)


def solution(mesh):
    placed = (
        P("seq", None),
        P("seq"),
        P(),
        P(None, "head", None),
        P("head", None),
        P(None, "head", None),
        P("head", None),
    )
    return jax.shard_map(
        body, mesh=mesh, in_specs=placed, out_specs=P("seq", None, "head"), check_vma=False
    )
```

```python
import functools

import jax
import jax.numpy as jnp
from jax import lax
from jax.experimental import pallas as pl
from jax.experimental.pallas import tpu as pltpu
from jax.sharding import PartitionSpec as P

HEAD_DIM = 64
EPS = 1e-05
LANES = 128
CODES = 64
TABLE_ROWS = 40

SMALL_VMEM = 8 * 1024 * 1024
LARGE_VMEM = 32 * 1024 * 1024

f32 = jnp.float32
bf16 = jnp.bfloat16


def layer_norm(values):
    mean = jnp.mean(values, axis=-1, keepdims=True)
    centred = values - mean
    spread = jnp.mean(centred * centred, axis=-1, keepdims=True)
    return centred * lax.rsqrt(spread + EPS)


def softmax_last(scores):
    top = jnp.max(scores, axis=-1, keepdims=True)
    weights = jnp.exp(scores - top)
    return weights * (1.0 / jnp.sum(weights, axis=-1, keepdims=True))


def dot_nt(left, right):
    return lax.dot_general(left, right, (((1,), (1,)), ((), ())), preferred_element_type=f32)


def dot_nn(left, right):
    return jnp.dot(left, right, preferred_element_type=f32)


def in_hbm(value):
    return pltpu.with_memory_space_constraint(value, pltpu.HBM)


def iota(shape, axis):
    return lax.broadcasted_iota(jnp.int32, shape, axis)


def join_kernel(rows, own_ref, other_ref, out_ref):
    own, other = own_ref[...], other_ref[...]
    both = jnp.concatenate([own[0:rows], other[0:rows]], 0)
    out_ref[...] = jnp.concatenate([both] * (own.shape[0] // (2 * rows)), 0)


def join(own, other, rows):
    return pl.pallas_call(
        functools.partial(join_kernel, rows),
        out_shape=jax.ShapeDtypeStruct(own.shape, own.dtype),
        compiler_params=pltpu.CompilerParams(vmem_limit_bytes=SMALL_VMEM),
        name="join",
    )(own, other)


def join_raw_kernel(own_ref, ids_ref, live_ref, out_ref):
    rows = ids_ref.shape[0]
    live = live_ref[...]
    other = ids_ref[...] + 65536 * jnp.concatenate(
        [jnp.broadcast_to(live[:, r : r + 1], (1, ids_ref.shape[1])) for r in range(rows)], 0
    )
    both = jnp.concatenate([own_ref[0:rows], other], 0)
    out_ref[...] = jnp.concatenate([both] * (out_ref.shape[0] // (2 * rows)), 0)


def join_raw(own, ids, pad_mask):
    return pl.pallas_call(
        join_raw_kernel,
        out_shape=jax.ShapeDtypeStruct(own.shape, own.dtype),
        compiler_params=pltpu.CompilerParams(vmem_limit_bytes=SMALL_VMEM),
        name="join_raw",
    )(own, ids, pad_mask)


def table_kernel(
    ids_hbm,
    live_hbm,
    embed_hbm,
    qkv_hbm,
    out_ref,
    coded_ref,
    ids_ref,
    live_ref,
    embed_ref,
    qkv_ref,
    padded_ref,
    sems,
):
    kinds = qkv_ref.shape[0]
    loads = [
        pltpu.make_async_copy(embed_hbm, embed_ref, sems.at[kinds]),
        pltpu.make_async_copy(ids_hbm, ids_ref, sems.at[kinds + 1]),
        pltpu.make_async_copy(live_hbm, live_ref, sems.at[kinds + 2]),
    ]
    loads += [
        pltpu.make_async_copy(qkv_hbm.at[t], qkv_ref.at[t], sems.at[t]) for t in range(kinds)
    ]
    for load in loads:
        load.start()
    padded_ref[...] = jnp.zeros(padded_ref.shape, f32)
    for load in loads[0:3]:
        load.wait()
    padded_ref[0 : embed_ref.shape[0], :] = embed_ref[...].astype(f32)
    normed = layer_norm(padded_ref[...]).astype(bf16)
    row = iota(ids_ref.shape, 0)
    live = jnp.zeros(ids_ref.shape, jnp.int32)
    for r in range(ids_ref.shape[0]):
        live = jnp.where(row == r, live_ref[r], live)
    coded = ids_ref[...] + 65536 * live
    coded_ref[...] = jnp.concatenate([coded] * (coded_ref.shape[0] // coded.shape[0]), 0)
    tables = []
    for t in range(kinds):
        loads[3 + t].wait()
        tables.append(dot_nt(normed, qkv_ref[t]))
    out_ref[...] = jnp.concatenate(tables, 1).astype(bf16)


def make_tables(ids, pad_mask, embed, row_qkv, height):
    kinds, local, width = row_qkv.shape
    return pl.pallas_call(
        table_kernel,
        out_shape=(
            jax.ShapeDtypeStruct((TABLE_ROWS, kinds * local), bf16),
            jax.ShapeDtypeStruct((height, ids.shape[1]), jnp.int32),
        ),
        in_specs=[pl.BlockSpec(memory_space=pltpu.HBM)] * 4,
        scratch_shapes=[
            pltpu.VMEM(ids.shape, jnp.int32),
            pltpu.SMEM(pad_mask.shape, jnp.int32),
            pltpu.VMEM(embed.shape, bf16),
            pltpu.VMEM(row_qkv.shape, bf16),
            pltpu.VMEM((TABLE_ROWS, width), f32),
            pltpu.SemaphoreType.DMA((kinds + 3,)),
        ],
        cost_estimate=pl.CostEstimate(
            flops=2 * 10**9, bytes_accessed=2 * row_qkv.size, transcendentals=0
        ),
        compiler_params=pltpu.CompilerParams(vmem_limit_bytes=SMALL_VMEM),
        name="tables",
    )(in_hbm(ids), in_hbm(pad_mask), in_hbm(embed), in_hbm(row_qkv))


def halves(pair):
    lane = iota(pair.shape, 1)
    zero = jnp.zeros_like(pair)
    return jnp.where(lane < HEAD_DIM, pair, zero), jnp.where(lane < HEAD_DIM, zero, pair)


def spread_pair(pair):
    first, second = halves(pair)
    zero = jnp.zeros_like(pair)
    return jnp.concatenate(
        [
            jnp.concatenate([first, zero], 1),
            jnp.concatenate([zero, first], 1),
            jnp.concatenate([second, zero], 1),
            jnp.concatenate([zero, second], 1),
        ],
        0,
    )


def double(block):
    zero = jnp.zeros_like(block)
    return jnp.concatenate(
        [jnp.concatenate([block, zero], 1), jnp.concatenate([zero, block], 1)], 0
    )


def one_hots(coded, group, hot_ref, own_ref, live_own_ref):
    depth, cols = hot_ref.shape
    rows = depth // CODES
    pairs = rows // 2
    own = own_ref.shape[0] // pairs
    ids = (coded & 0xFFFF).astype(f32)
    live = (coded[:, 0:LANES] >> 16).astype(f32)

    code = iota((CODES, cols), 0).astype(f32)
    for r in range(rows):
        hot = jnp.broadcast_to(ids[r : r + 1, :], (CODES, cols)) == code
        hot_ref[r * CODES : (r + 1) * CODES, :] = hot.astype(f32).astype(bf16)

    pick = (iota((own, cols), 1) == group * own + iota((own, cols), 0)).astype(f32).astype(bf16)
    mine = dot_nt(pick, ids.astype(bf16))
    lane = iota((own, LANES), 1)
    first_half = lane < CODES
    lane_code = jnp.where(first_half, lane, lane - CODES).astype(f32)
    for k in range(pairs):
        value = jnp.where(first_half, mine[:, 2 * k : 2 * k + 1], mine[:, 2 * k + 1 : 2 * k + 2])
        hot = (value == lane_code).astype(f32)
        alive = jnp.where(first_half, live[2 * k : 2 * k + 1, :], live[2 * k + 1 : 2 * k + 2, :])
        own_ref[k * own : (k + 1) * own, :] = hot.astype(bf16)
        live_own_ref[k * own : (k + 1) * own, :] = (hot * alive).astype(bf16)
    return live


def head_groups(heads, own):
    some = heads // 2
    return [(slice(g * some * own, (g + 1) * some * own), g * some, (g + 1) * some) for g in range(2)]


def tied_sum(scores_ref, live_own_ref, hot_ref, sum_ref, first, last):
    own = sum_ref.shape[0] // scores_ref.shape[0]
    depth = hot_ref.shape[0]
    pairs = depth // CODES // 2
    for h in range(first, last):
        looked = dot_nn(live_own_ref[...], scores_ref[h]).astype(bf16)
        for piece in range(2):
            for k in range(pairs):
                to = piece * depth + k * LANES
                sum_ref[h * own : (h + 1) * own, to : to + LANES] = looked[
                    k * own : (k + 1) * own, piece * LANES : (piece + 1) * LANES
                ]
    at = slice(first * own, last * own)
    return dot_nn(sum_ref[at, 0:depth], hot_ref[...]) + dot_nn(
        sum_ref[at, depth : 2 * depth], hot_ref[...]
    )


def near_kernel(parts, *refs):
    tables_refs, refs = refs[:parts], refs[parts:]
    (
        codes_ref,
        scores_ref,
        values_ref,
        tied_ref,
        hot_ref,
        own_ref,
        tables_ref,
        table_ref,
        live_own_ref,
        sum_ref,
    ) = refs
    width = values_ref.shape[1]
    heads = width // HEAD_DIM
    local = width // parts
    group = lax.axis_index("seq")
    part = lax.axis_index("head")
    for p in range(parts):
        tables_ref[part ^ p] = tables_refs[p][...]

    for t in range(3):
        to_ref = values_ref if t == 2 else table_ref.at[t]
        to_ref[0:TABLE_ROWS, :] = jnp.concatenate(
            [tables_ref[p, :, t * local : (t + 1) * local] for p in range(parts)], 1
        )
        to_ref[TABLE_ROWS:CODES, :] = jnp.zeros((CODES - TABLE_ROWS, width), bf16)

    spans = [slice(hp * LANES, (hp + 1) * LANES) for hp in range(heads // 2)]
    queries = [spread_pair(table_ref[0, :, span]) for span in spans]
    keys = [double(table_ref[1, :, span]) for span in spans]
    scores = [dot_nt(query, key) for query, key in zip(queries, keys)]
    high = [score.astype(bf16) for score in scores]
    low = [(score - part_of.astype(f32)).astype(bf16) for score, part_of in zip(scores, high)]
    for h in range(heads):
        these = slice(h % 2 * LANES, (h % 2 + 1) * LANES)
        scores_ref[h, :, 0:LANES] = high[h // 2][these]
        scores_ref[h, :, LANES : 2 * LANES] = low[h // 2][these]

    one_hots(codes_ref[...], group, hot_ref, own_ref, live_own_ref)
    tied_ref[...] = tied_sum(scores_ref, live_own_ref, hot_ref, sum_ref, 0, heads)


def attend_near(tables, codes, own):
    parts = len(tables)
    width = tables[0].shape[1] // 3 * parts
    heads = width // HEAD_DIM
    rows, cols = codes.shape
    return pl.pallas_call(
        functools.partial(near_kernel, parts),
        out_shape=(
            jax.ShapeDtypeStruct((heads, LANES, 2 * LANES), bf16),
            jax.ShapeDtypeStruct((CODES, width), bf16),
            jax.ShapeDtypeStruct((heads * own, cols), f32),
            jax.ShapeDtypeStruct((rows * CODES, cols), bf16),
            jax.ShapeDtypeStruct((rows // 2 * own, LANES), bf16),
        ),
        scratch_shapes=[
            pltpu.VMEM((parts,) + tables[0].shape, bf16),
            pltpu.VMEM((2, CODES, width), bf16),
            pltpu.VMEM((rows // 2 * own, LANES), bf16),
            pltpu.VMEM((heads * own, 2 * rows * CODES), bf16),
        ],
        cost_estimate=pl.CostEstimate(flops=10**9, bytes_accessed=10**6, transcendentals=0),
        compiler_params=pltpu.CompilerParams(vmem_limit_bytes=LARGE_VMEM),
        name="near_scores",
    )(*tables, codes)


def row_kernel(
    scores_ref,
    values_ref,
    near_tied_ref,
    near_hot_ref,
    near_codes_ref,
    far_codes_ref,
    row_context_ref,
    own_ref,
    live_ref,
    hot_ref,
    live_own_ref,
    sum_ref,
    spread_ref,
):
    depth = hot_ref.shape[0]
    rows = 2 * depth // CODES
    pairs = rows // 2
    width = row_context_ref.shape[1]
    heads = width // HEAD_DIM
    own = spread_ref.shape[0] // heads
    group = lax.axis_index("seq")

    live = one_hots(far_codes_ref[...], group, hot_ref, own_ref, live_own_ref)
    live = jnp.concatenate([(near_codes_ref[:, 0:LANES] >> 16).astype(f32), live], 0)
    live_ref[...] = live
    count = jnp.sum(live, axis=0, keepdims=True)[:, 0:1]
    scale = HEAD_DIM ** (-0.5) / jnp.sqrt(count)
    groups = head_groups(heads, own)
    tied = [
        near_tied_ref[at, :] + tied_sum(scores_ref, live_own_ref, hot_ref, sum_ref, first, last)
        for at, first, last in groups
    ]
    probs = [softmax_last(some * scale).astype(bf16) for some in tied]

    for (at, _, _), some in zip(groups, probs):
        spread_ref[at, 0:depth] = dot_nt(some, near_hot_ref[...]).astype(bf16)
        spread_ref[at, depth : 2 * depth] = dot_nt(some, hot_ref[...]).astype(bf16)
    spans = [slice(hp * LANES, (hp + 1) * LANES) for hp in range(heads // 2)]
    values = [spread_pair(values_ref[:, span]) for span in spans]
    contexts = []
    for hp in range(heads // 2):
        first = (hp * 2) * own
        weights = jnp.concatenate(
            [
                jnp.concatenate(
                    [
                        spread_ref[first : first + own, k * LANES : (k + 1) * LANES],
                        spread_ref[first + own : first + 2 * own, k * LANES : (k + 1) * LANES],
                    ],
                    1,
                )
                for k in range(pairs)
            ],
            0,
        )
        contexts.append(dot_nn(weights, values[hp]).astype(bf16))
    for hp in range(heads // 2):
        for k in range(pairs):
            for r2 in range(2):
                at = (2 * k + r2) * own
                row_context_ref[at : at + own, spans[hp]] = contexts[hp][
                    k * own : (k + 1) * own, r2 * LANES : (r2 + 1) * LANES
                ]


def attend_rows(near, near_codes, far_codes, own):
    scores, values, near_tied, near_hot = near
    heads, width = scores.shape[0], values.shape[1]
    half, cols = near_codes.shape
    return pl.pallas_call(
        row_kernel,
        out_shape=(
            jax.ShapeDtypeStruct((2 * half * own, width), bf16),
            jax.ShapeDtypeStruct((half // 2 * own, LANES), bf16),
            jax.ShapeDtypeStruct((2 * half, LANES), f32),
        ),
        scratch_shapes=[
            pltpu.VMEM((half * CODES, cols), bf16),
            pltpu.VMEM((half // 2 * own, LANES), bf16),
            pltpu.VMEM((heads * own, 2 * half * CODES), bf16),
            pltpu.VMEM((heads * own, 2 * half * CODES), bf16),
        ],
        cost_estimate=pl.CostEstimate(flops=3 * 10**9, bytes_accessed=10**6, transcendentals=0),
        compiler_params=pltpu.CompilerParams(vmem_limit_bytes=LARGE_VMEM),
        name="row_attention",
    )(scores, values, near_tied, near_hot, near_codes, far_codes)


def column_kernel(parts, *refs):
    row_out_refs, refs = refs[:parts], refs[parts:]
    (
        live_ref,
        row_context_ref,
        near_own_ref,
        far_own_ref,
        embed_ref,
        col_qkv_ref,
        *context_refs,
        mixed_out_ref,
        row_out_ref,
        embed2_ref,
        weight_ref,
        mixed_ref,
    ) = refs
    rows = live_ref.shape[0]
    tokens, width = row_context_ref.shape
    pairs = rows // 2
    own = tokens // rows
    vocab = embed_ref.shape[0]
    local = width // parts
    part = lax.axis_index("head")

    for p in range(parts):
        row_out_ref[part ^ p] = row_out_refs[p][...]
    embed2_ref[...] = jnp.zeros(embed2_ref.shape, bf16)
    embed2_ref[0:vocab, 0:width] = embed_ref[...]
    embed2_ref[CODES : CODES + vocab, width : 2 * width] = embed_ref[...]

    own_codes = jnp.concatenate([near_own_ref[...], far_own_ref[...]], 0)
    embedded2 = dot_nn(own_codes, embed2_ref[...])
    embedded = jnp.concatenate(
        [
            embedded2[k * own : (k + 1) * own, r2 * width : (r2 + 1) * width]
            for k in range(pairs)
            for r2 in range(2)
        ],
        0,
    )
    mixed = embedded + dot_nt(row_context_ref[...], row_out_ref[...].reshape(width, width))
    mixed_ref[...] = mixed
    normed = layer_norm(mixed).astype(bf16)

    few = 8
    groups = own // few
    unit = rows * few

    def regroup(values):
        shape = (rows, groups, few, values.shape[1])
        return jnp.swapaxes(values.reshape(shape), 0, 1).reshape(tokens, values.shape[1])

    odd = part % 2
    for t in range(3):
        first = pl.multiple_of(t * local + odd * HEAD_DIM, HEAD_DIM)
        last = pl.multiple_of(t * local + (1 - odd) * LANES, HEAD_DIM)
        third = (3 + t) * LANES
        weight_ref[t * LANES : (t + 1) * LANES, :] = col_qkv_ref[pl.ds(first, LANES), :]
        weight_ref[third : third + HEAD_DIM, :] = col_qkv_ref[pl.ds(last, HEAD_DIM), :]
        weight_ref[third + HEAD_DIM : third + LANES, :] = jnp.zeros((HEAD_DIM, width), bf16)
    proj = [
        dot_nt(normed, weight_ref[2 * j * LANES : 2 * (j + 1) * LANES, :]) for j in range(3)
    ]
    proj = [
        proj[j][:, k * LANES : (k + 1) * LANES] * (HEAD_DIM ** (-0.5) if (2 * j + k) % 3 == 0 else 1.0)
        for j in range(3)
        for k in range(2)
    ]
    proj = [regroup(values).astype(bf16) for values in proj]
    sub, lan = iota((unit, unit), 0), iota((unit, unit), 1)
    same_column = (sub % few) == (lan % few)
    seq_of_lane = iota((rows, unit), 1) // few
    live_lane = jnp.sum(
        jnp.where(seq_of_lane == iota((rows, unit), 0), live_ref[...], 0.0), axis=0, keepdims=True
    )
    visible = jnp.logical_and(same_column, jnp.broadcast_to(live_lane, (unit, unit)) > 0)
    chosen = []
    for g in range(groups):
        at = slice(g * unit, (g + 1) * unit)
        query, keys, values = (proj[t][at] for t in range(3))
        chosen += [(half, keys, values) for half in halves(query)]
        chosen.append(tuple(proj[3 + t][at] for t in range(3)))
    scores = [jnp.where(visible, dot_nt(query, keys), -jnp.inf) for query, keys, _ in chosen]
    tops = [jnp.max(score, axis=-1, keepdims=True) for score in scores]
    weights = [jnp.exp(score - top) for score, top in zip(scores, tops)]
    shares = [1.0 / jnp.sum(weight, axis=-1, keepdims=True) for weight in weights]
    probs = [(weight * share).astype(bf16) for weight, share in zip(weights, shares)]
    found = [dot_nn(prob, values) for prob, (_, _, values) in zip(probs, chosen)]
    first_head = iota((unit, LANES), 1) < HEAD_DIM

    def ungroup(blocks):
        whole = jnp.concatenate(blocks, 0).reshape(groups, rows, few, LANES)
        return jnp.swapaxes(whole, 0, 1).reshape(tokens, LANES)

    main = ungroup(
        [jnp.where(first_head, found[3 * g], found[3 * g + 1]) for g in range(groups)]
    )
    third = ungroup([found[3 * g + 2] for g in range(groups)])
    start = 0
    for context_ref in context_refs:
        count = context_ref.shape[0] * 2 // 3
        some = count // 2
        context_ref[0:count, :] = main[start : start + count].astype(bf16)
        early = third[start : start + some]
        late = third[start + some : start + count]
        left = jnp.where(odd == 1, late, early)
        right = jnp.where(odd == 1, early, late)
        context_ref[count : count + some, :] = jnp.concatenate(
            [left[:, 0:HEAD_DIM], right[:, 0:HEAD_DIM]], 1
        ).astype(bf16)
        start += count
    for p in range(parts):

        @pl.when(part == p)
        def _():
            mixed_out_ref[...] = mixed_ref[:, p * local : (p + 1) * local]


def attend_columns_here(row_outs, live, row_context, near_own, far_own, embed, col_qkv):
    parts = len(row_outs)
    tokens, width = row_context.shape
    local = width // parts
    half = tokens // 2 * local // LANES
    return pl.pallas_call(
        functools.partial(column_kernel, parts),
        out_shape=(
            jax.ShapeDtypeStruct((half, LANES), bf16),
            jax.ShapeDtypeStruct((half, LANES), bf16),
            jax.ShapeDtypeStruct((tokens, local), f32),
        ),
        scratch_shapes=[
            pltpu.VMEM((parts, local, width), bf16),
            pltpu.VMEM((2 * CODES, 2 * width), bf16),
            pltpu.VMEM((6 * LANES, width), bf16),
            pltpu.VMEM((tokens, width), f32),
        ],
        cost_estimate=pl.CostEstimate(flops=2 * 10**9, bytes_accessed=10**6, transcendentals=0),
        compiler_params=pltpu.CompilerParams(vmem_limit_bytes=LARGE_VMEM),
        name="column_attention",
    )(*row_outs, live, row_context, near_own, far_own, embed, col_qkv)


def steps_of(groups):
    return [1] + [1 << k for k in range(groups.bit_length() - 2, 0, -1)]


def slot_order(groups):
    order = [0]
    for step in steps_of(groups):
        order += [slot ^ step for slot in order]
    return order


def finish_kernel(parts, groups, *refs):
    context_refs = [refs[:parts], refs[parts : 2 * parts]]
    mixed_ref, col_out_ref, out_ref, context_ref = refs[2 * parts :]
    tokens, local = mixed_ref.shape
    group = lax.axis_index("seq")
    part = lax.axis_index("head")
    starts = [0, context_refs[0][0].shape[0]]
    for start, some_refs in zip(starts, context_refs):
        for p in range(parts):
            context_ref[part ^ p, start : start + some_refs[p].shape[0], :] = some_refs[p][...]
    pieces = []
    for start, some_refs in zip(starts, context_refs):
        count = some_refs[0].shape[0] * 2 // 3
        end = start + some_refs[0].shape[0]
        low = iota((count // 2, LANES), 1) < HEAD_DIM
        features = []
        for p in range(0, parts, 2):
            even = context_ref[p, start + count : end, :]
            other = context_ref[p + 1, start + count : end, :]
            early = jnp.where(low, even, other)
            late = jnp.where(low, other, even)
            late = jnp.concatenate([late[:, HEAD_DIM:], late[:, 0:HEAD_DIM]], 1)
            features += [
                context_ref[p, start : start + count, :],
                jnp.concatenate([early, late], 0),
                context_ref[p + 1, start : start + count, :],
            ]
        pieces.append(jnp.concatenate(features, 1))
    total = mixed_ref[...] + dot_nt(jnp.concatenate(pieces, 0), col_out_ref[...])
    own = tokens // groups // 2
    for d, slot in enumerate(slot_order(groups)):
        first, second = (total[(2 * d + r) * own : (2 * d + r + 1) * own, :] for r in range(2))
        rest = jnp.concatenate([first[:, LANES:local], second[:, LANES:local]], 1)
        out_ref[group ^ slot] = jnp.concatenate(
            [first[:, 0:LANES], second[:, 0:LANES], rest], 0
        ).astype(bf16)


def finish(contexts, mixed, col_out, groups):
    parts = len(contexts[0])
    tokens, local = mixed.shape
    return pl.pallas_call(
        functools.partial(finish_kernel, parts, groups),
        out_shape=jax.ShapeDtypeStruct((groups, tokens // groups * local // LANES, LANES), bf16),
        scratch_shapes=[pltpu.VMEM((parts, tokens * local // LANES, LANES), bf16)],
        compiler_params=pltpu.CompilerParams(vmem_limit_bytes=LARGE_VMEM),
        name="finish",
    )(*contexts[0], *contexts[1], mixed, col_out)


def order_kernel(blocks_ref, out_ref):
    groups = blocks_ref.shape[0]
    local, cols = out_ref.shape[1:]
    own = cols // groups
    rest = local - LANES
    for part in range(3):
        piece = jnp.concatenate(
            [blocks_ref[g, part * own : (part + 1) * own, :] for g in range(groups)], 0
        )
        turned = piece.astype(f32).T.astype(bf16)
        if part < 2:
            out_ref[part, 0:LANES, :] = turned
        else:
            for r in range(2):
                out_ref[r, LANES:local, :] = turned[r * rest : (r + 1) * rest, :]


def order(blocks, cols, local):
    return pl.pallas_call(
        order_kernel,
        out_shape=jax.ShapeDtypeStruct((2, local, cols), bf16),
        compiler_params=pltpu.CompilerParams(vmem_limit_bytes=SMALL_VMEM),
        name="order",
    )(blocks)


def fast_body(ids, pad_mask, embed, row_qkv, row_out, col_qkv, col_out):
    rows_here, cols = ids.shape
    width = embed.shape[1]
    local = row_out.shape[0]
    groups, parts = lax.axis_size("seq"), lax.axis_size("head")
    own, rows = cols // groups, rows_here * groups

    def pairwise(value, partner):
        order = [(g, p) for g in range(groups) for p in range(parts)]
        link = [(g * parts + p, partner(g, p)) for g, p in order]
        return lax.ppermute(value, ("seq", "head"), [(i, g * parts + p) for i, (g, p) in link])

    def sibling(g, p):
        return g, p ^ 1

    def across(g, p):
        return g, p ^ 2

    def opposite(g, p):
        return g, p ^ 3

    far = pairwise(row_out, across)
    other_ids = pairwise(ids, lambda g, p: (g ^ 1, p))
    other_mask = pairwise(pad_mask.reshape(1, rows_here), lambda g, p: (g ^ 1, p))
    table, coded = make_tables(ids, pad_mask, embed, row_qkv, rows_here * groups // 2)
    tables = [table, None, pairwise(table, across), None]
    for count, step in enumerate(steps_of(groups)[1:], 1):
        if count == 1:
            coded = join_raw(coded, other_ids, other_mask)
            coded, table = lax.optimization_barrier((coded, table))
            tables[3] = pairwise(table, opposite)
        else:
            coded = join(coded, received, rows_here << (count - 1))
        if count == 2:
            coded, table, row_out, far = lax.optimization_barrier((coded, table, row_out, far))
            tables[1] = pairwise(table, sibling)
            row_outs = [row_out, pairwise(row_out, sibling), far, pairwise(far, sibling)]
        received = pairwise(coded, lambda g, p, step=step: (g ^ step, p))
    codes = (coded, received)
    *near_scores, near_own = attend_near(tables, codes[0], own)
    row_context, far_own, live = attend_rows(near_scores, *codes, own)
    *halves_here, mixed = attend_columns_here(
        row_outs,
        live,
        row_context,
        near_own,
        far_own,
        embed,
        col_qkv.reshape(3 * local, width),
    )
    contexts = []
    for context in halves_here:
        beyond = pairwise(context, across)
        contexts.append(
            (context, pairwise(context, sibling), beyond, pairwise(beyond, sibling))
        )
    blocks = finish(contexts, mixed, col_out, groups)
    blocks = lax.all_to_all(blocks, "seq", split_axis=0, concat_axis=0, tiled=True)
    return jnp.swapaxes(order(blocks, cols, local), 1, 2)


def weight_fold(out_weight, piece):
    return jnp.einsum("rce,fe->rcf", piece, out_weight, preferred_element_type=f32)


def attend_columns(query, keys, values, key_live):
    rows_all, count_cols, local_width = query.shape
    heads_here = local_width // HEAD_DIM
    shape = (rows_all, count_cols, heads_here, HEAD_DIM)
    scores = jnp.einsum(
        "rchd,schd->chrs",
        query.reshape(shape),
        keys.reshape(shape),
        preferred_element_type=f32,
    ) * HEAD_DIM ** (-0.5)
    scores = jnp.where(key_live > 0, scores, -jnp.inf)
    probs = softmax_last(scores).astype(bf16)
    context = jnp.einsum(
        "chrs,schd->rchd", probs, values.reshape(shape), preferred_element_type=f32
    )
    return context.astype(bf16).reshape(rows_all, count_cols, local_width)


def send_back(context):
    return lax.all_to_all(context[:, None], "seq", split_axis=0, concat_axis=1, tiled=True)


def general_body(ids, pad_mask, embed, row_qkv, row_out, col_qkv, col_out):
    rows_here, cols = ids.shape
    width = embed.shape[1]
    local_width = row_out.shape[0]
    heads_here = local_width // HEAD_DIM
    groups = lax.axis_size("seq")
    per_group = cols // groups
    codes = lax.broadcasted_iota(jnp.int32, (1, 1, embed.shape[0]), 2)
    onehot = (ids[:, :, None] == codes).astype(bf16)
    embedded = jnp.einsum("rcv,vd->rcd", onehot, embed, preferred_element_type=f32)
    normed = layer_norm(embedded).astype(bf16)
    row_proj = jnp.einsum("rcd,ted->trce", normed, row_qkv, preferred_element_type=f32)
    row_proj = row_proj.astype(bf16)
    live = pad_mask.astype(bf16)
    head_shape = (rows_here, cols, heads_here, HEAD_DIM)
    query = (row_proj[0] * live[:, None, None]).reshape(head_shape)
    keys = row_proj[1].reshape(head_shape)
    values = row_proj[2].reshape(head_shape)
    partial_scores = jnp.einsum("rihd,rjhd->hij", query, keys, preferred_element_type=f32)
    count_here = jnp.sum(pad_mask.astype(f32))
    scale = HEAD_DIM ** (-0.5)
    total, count = lax.psum((partial_scores, count_here), "seq")
    row_probs = softmax_last(total * (scale / jnp.sqrt(count))).astype(bf16)
    row_context = jnp.einsum("hij,rjhd->rihd", row_probs, values, preferred_element_type=f32)
    row_context = row_context.astype(bf16).reshape(rows_here, cols, local_width)
    start_feature = lax.axis_index("head") * local_width
    resident = lax.dynamic_slice_in_dim(embedded, start_feature, local_width, 2)
    row_update = weight_fold(row_out, lax.all_gather(row_context, "head", axis=2, tiled=True))
    mixed = resident + row_update
    sums, squares = lax.psum((jnp.sum(mixed, axis=-1), jnp.sum(mixed * mixed, axis=-1)), "head")
    mean = sums / width
    spread = squares / width - mean * mean
    normed_here = ((mixed - mean[..., None]) * lax.rsqrt(spread[..., None] + EPS)).astype(bf16)
    live_tile = jnp.broadcast_to(live[:, None, None, None], (rows_here, groups, per_group, 1))
    normed_full = lax.all_gather(normed_here, "head", axis=2, tiled=True)
    col_proj = jnp.einsum("rcd,ted->rcte", normed_full, col_qkv, preferred_element_type=f32)
    packed = col_proj.astype(bf16).reshape(rows_here, groups, per_group, 3 * local_width)
    received = lax.all_to_all(packed, "seq", split_axis=1, concat_axis=0, tiled=True)
    mask_part = lax.all_to_all(live_tile, "seq", split_axis=1, concat_axis=0, tiled=True)
    column_out = send_back(
        attend_columns(
            received[:, 0, :, :local_width],
            received[:, 0, :, local_width : 2 * local_width],
            received[:, 0, :, 2 * local_width :],
            mask_part[:, 0, 0, 0],
        )
    )
    column_out = column_out.reshape(rows_here, cols, local_width)
    col_update = weight_fold(col_out, lax.all_gather(column_out, "head", axis=2, tiled=True))
    return (mixed + col_update).astype(bf16)


def body(ids, pad_mask, embed, row_qkv, row_out, col_qkv, col_out):
    rows_here, cols = ids.shape
    groups = lax.axis_size("seq")
    own, rows = cols // groups, rows_here * groups
    parts = lax.axis_size("head")
    local = row_out.shape[0]
    fits = (
        parts == 4
        and groups >= 8
        and groups & (groups - 1) == 0
        and rows * 8 == LANES
        and rows_here == 2
        and own % 32 == 0
        and cols >= LANES
        and local == LANES + HEAD_DIM
        and embed.shape[0] <= TABLE_ROWS
    )
    chosen = fast_body if fits else general_body
    return chosen(ids, pad_mask, embed, row_qkv, row_out, col_qkv, col_out)


def solution(mesh):
    placed = (
        P("seq", None),
        P("seq"),
        P(),
        P(None, "head", None),
        P("head", None),
        P(None, "head", None),
        P("head", None),
    )
    return jax.shard_map(
        body, mesh=mesh, in_specs=placed, out_specs=P("seq", None, "head"), check_vma=False
    )
```

```python
import functools

import jax
import jax.numpy as jnp
from jax import lax
from jax.experimental import pallas as pl
from jax.experimental.pallas import tpu as pltpu
from jax.sharding import PartitionSpec as P

HEAD_DIM = 64
EPS = 1e-05
LANES = 128
CODES = 64
TABLE_ROWS = 40

SMALL_VMEM = 8 * 1024 * 1024
LARGE_VMEM = 32 * 1024 * 1024

f32 = jnp.float32
bf16 = jnp.bfloat16


def layer_norm(values):
    mean = jnp.mean(values, axis=-1, keepdims=True)
    centred = values - mean
    spread = jnp.mean(centred * centred, axis=-1, keepdims=True)
    return centred * lax.rsqrt(spread + EPS)


def softmax_last(scores):
    top = jnp.max(scores, axis=-1, keepdims=True)
    weights = jnp.exp(scores - top)
    return weights * (1.0 / jnp.sum(weights, axis=-1, keepdims=True))


def dot_nt(left, right):
    return lax.dot_general(left, right, (((1,), (1,)), ((), ())), preferred_element_type=f32)


def dot_nn(left, right):
    return jnp.dot(left, right, preferred_element_type=f32)


def in_hbm(value):
    return pltpu.with_memory_space_constraint(value, pltpu.HBM)


def iota(shape, axis):
    return lax.broadcasted_iota(jnp.int32, shape, axis)


def join_kernel(rows, own_ref, other_ref, out_ref):
    own, other = own_ref[...], other_ref[...]
    both = jnp.concatenate([own[0:rows], other[0:rows]], 0)
    out_ref[...] = jnp.concatenate([both] * (own.shape[0] // (2 * rows)), 0)


def join(own, other, rows):
    return pl.pallas_call(
        functools.partial(join_kernel, rows),
        out_shape=jax.ShapeDtypeStruct(own.shape, own.dtype),
        compiler_params=pltpu.CompilerParams(vmem_limit_bytes=SMALL_VMEM),
        name="join",
    )(own, other)


def join_raw_kernel(own_ref, ids_ref, live_ref, out_ref):
    rows = ids_ref.shape[0]
    live = live_ref[...]
    other = ids_ref[...] + 65536 * jnp.concatenate(
        [jnp.broadcast_to(live[:, r : r + 1], (1, ids_ref.shape[1])) for r in range(rows)], 0
    )
    both = jnp.concatenate([own_ref[0:rows], other], 0)
    out_ref[...] = jnp.concatenate([both] * (out_ref.shape[0] // (2 * rows)), 0)


def join_raw(own, ids, pad_mask):
    return pl.pallas_call(
        join_raw_kernel,
        out_shape=jax.ShapeDtypeStruct(own.shape, own.dtype),
        compiler_params=pltpu.CompilerParams(vmem_limit_bytes=SMALL_VMEM),
        name="join_raw",
    )(own, ids, pad_mask)


def table_kernel(
    ids_hbm,
    live_hbm,
    embed_hbm,
    qkv_hbm,
    out_ref,
    coded_ref,
    ids_ref,
    live_ref,
    embed_ref,
    qkv_ref,
    padded_ref,
    sems,
):
    kinds = qkv_ref.shape[0]
    loads = [
        pltpu.make_async_copy(embed_hbm, embed_ref, sems.at[kinds]),
        pltpu.make_async_copy(ids_hbm, ids_ref, sems.at[kinds + 1]),
        pltpu.make_async_copy(live_hbm, live_ref, sems.at[kinds + 2]),
    ]
    loads += [
        pltpu.make_async_copy(qkv_hbm.at[t], qkv_ref.at[t], sems.at[t]) for t in range(kinds)
    ]
    for load in loads:
        load.start()
    padded_ref[...] = jnp.zeros(padded_ref.shape, f32)
    for load in loads[0:3]:
        load.wait()
    padded_ref[0 : embed_ref.shape[0], :] = embed_ref[...].astype(f32)
    normed = layer_norm(padded_ref[...]).astype(bf16)
    row = iota(ids_ref.shape, 0)
    live = jnp.zeros(ids_ref.shape, jnp.int32)
    for r in range(ids_ref.shape[0]):
        live = jnp.where(row == r, live_ref[r], live)
    coded = ids_ref[...] + 65536 * live
    coded_ref[...] = jnp.concatenate([coded] * (coded_ref.shape[0] // coded.shape[0]), 0)
    tables = []
    for t in range(kinds):
        loads[3 + t].wait()
        tables.append(dot_nt(normed, qkv_ref[t]))
    out_ref[...] = jnp.concatenate(tables, 1).astype(bf16)


def make_tables(ids, pad_mask, embed, row_qkv, height):
    kinds, local, width = row_qkv.shape
    return pl.pallas_call(
        table_kernel,
        out_shape=(
            jax.ShapeDtypeStruct((TABLE_ROWS, kinds * local), bf16),
            jax.ShapeDtypeStruct((height, ids.shape[1]), jnp.int32),
        ),
        in_specs=[pl.BlockSpec(memory_space=pltpu.HBM)] * 4,
        scratch_shapes=[
            pltpu.VMEM(ids.shape, jnp.int32),
            pltpu.SMEM(pad_mask.shape, jnp.int32),
            pltpu.VMEM(embed.shape, bf16),
            pltpu.VMEM(row_qkv.shape, bf16),
            pltpu.VMEM((TABLE_ROWS, width), f32),
            pltpu.SemaphoreType.DMA((kinds + 3,)),
        ],
        cost_estimate=pl.CostEstimate(
            flops=2 * 10**9, bytes_accessed=2 * row_qkv.size, transcendentals=0
        ),
        compiler_params=pltpu.CompilerParams(vmem_limit_bytes=SMALL_VMEM),
        name="tables",
    )(in_hbm(ids), in_hbm(pad_mask), in_hbm(embed), in_hbm(row_qkv))


def halves(pair):
    lane = iota(pair.shape, 1)
    zero = jnp.zeros_like(pair)
    return jnp.where(lane < HEAD_DIM, pair, zero), jnp.where(lane < HEAD_DIM, zero, pair)


def spread_pair(pair):
    first, second = halves(pair)
    zero = jnp.zeros_like(pair)
    return jnp.concatenate(
        [
            jnp.concatenate([first, zero], 1),
            jnp.concatenate([zero, first], 1),
            jnp.concatenate([second, zero], 1),
            jnp.concatenate([zero, second], 1),
        ],
        0,
    )


def double(block):
    zero = jnp.zeros_like(block)
    return jnp.concatenate(
        [jnp.concatenate([block, zero], 1), jnp.concatenate([zero, block], 1)], 0
    )


def one_hots(coded, group, hot_ref, own_ref, live_own_ref):
    depth, cols = hot_ref.shape
    rows = depth // CODES
    pairs = rows // 2
    own = own_ref.shape[0] // pairs
    ids = (coded & 0xFFFF).astype(f32)
    live = (coded[:, 0:LANES] >> 16).astype(f32)

    code = iota((CODES, cols), 0).astype(f32)
    for r in range(rows):
        hot = jnp.broadcast_to(ids[r : r + 1, :], (CODES, cols)) == code
        hot_ref[r * CODES : (r + 1) * CODES, :] = hot.astype(f32).astype(bf16)

    pick = (iota((own, cols), 1) == group * own + iota((own, cols), 0)).astype(f32).astype(bf16)
    mine = dot_nt(pick, ids.astype(bf16))
    lane = iota((own, LANES), 1)
    first_half = lane < CODES
    lane_code = jnp.where(first_half, lane, lane - CODES).astype(f32)
    for k in range(pairs):
        value = jnp.where(first_half, mine[:, 2 * k : 2 * k + 1], mine[:, 2 * k + 1 : 2 * k + 2])
        hot = (value == lane_code).astype(f32)
        alive = jnp.where(first_half, live[2 * k : 2 * k + 1, :], live[2 * k + 1 : 2 * k + 2, :])
        own_ref[k * own : (k + 1) * own, :] = hot.astype(bf16)
        live_own_ref[k * own : (k + 1) * own, :] = (hot * alive).astype(bf16)
    return live


def head_groups(heads, own):
    some = heads // 2
    return [(slice(g * some * own, (g + 1) * some * own), g * some, (g + 1) * some) for g in range(2)]


def tied_sum(scores_ref, live_own_ref, hot_ref, sum_ref, first, last):
    own = sum_ref.shape[0] // scores_ref.shape[0]
    depth = hot_ref.shape[0]
    pairs = depth // CODES // 2
    for h in range(first, last):
        looked = dot_nn(live_own_ref[...], scores_ref[h]).astype(bf16)
        for piece in range(2):
            for k in range(pairs):
                to = piece * depth + k * LANES
                sum_ref[h * own : (h + 1) * own, to : to + LANES] = looked[
                    k * own : (k + 1) * own, piece * LANES : (piece + 1) * LANES
                ]
    at = slice(first * own, last * own)
    return dot_nn(sum_ref[at, 0:depth], hot_ref[...]) + dot_nn(
        sum_ref[at, depth : 2 * depth], hot_ref[...]
    )


def near_kernel(parts, *refs):
    tables_refs, refs = refs[:parts], refs[parts:]
    (
        codes_ref,
        scores_ref,
        values_ref,
        tied_ref,
        hot_ref,
        own_ref,
        tables_ref,
        table_ref,
        live_own_ref,
        sum_ref,
    ) = refs
    width = values_ref.shape[1]
    heads = width // HEAD_DIM
    local = width // parts
    group = lax.axis_index("seq")
    part = lax.axis_index("head")
    for p in range(parts):
        tables_ref[part ^ p] = tables_refs[p][...]

    for t in range(3):
        to_ref = values_ref if t == 2 else table_ref.at[t]
        to_ref[0:TABLE_ROWS, :] = jnp.concatenate(
            [tables_ref[p, :, t * local : (t + 1) * local] for p in range(parts)], 1
        )
        to_ref[TABLE_ROWS:CODES, :] = jnp.zeros((CODES - TABLE_ROWS, width), bf16)

    spans = [slice(hp * LANES, (hp + 1) * LANES) for hp in range(heads // 2)]
    queries = [spread_pair(table_ref[0, :, span]) for span in spans]
    keys = [double(table_ref[1, :, span]) for span in spans]
    scores = [dot_nt(query, key) for query, key in zip(queries, keys)]
    high = [score.astype(bf16) for score in scores]
    low = [(score - part_of.astype(f32)).astype(bf16) for score, part_of in zip(scores, high)]
    for h in range(heads):
        these = slice(h % 2 * LANES, (h % 2 + 1) * LANES)
        scores_ref[h, :, 0:LANES] = high[h // 2][these]
        scores_ref[h, :, LANES : 2 * LANES] = low[h // 2][these]

    one_hots(codes_ref[...], group, hot_ref, own_ref, live_own_ref)
    tied_ref[...] = tied_sum(scores_ref, live_own_ref, hot_ref, sum_ref, 0, heads)


def attend_near(tables, codes, own):
    parts = len(tables)
    width = tables[0].shape[1] // 3 * parts
    heads = width // HEAD_DIM
    rows, cols = codes.shape
    return pl.pallas_call(
        functools.partial(near_kernel, parts),
        out_shape=(
            jax.ShapeDtypeStruct((heads, LANES, 2 * LANES), bf16),
            jax.ShapeDtypeStruct((CODES, width), bf16),
            jax.ShapeDtypeStruct((heads * own, cols), f32),
            jax.ShapeDtypeStruct((rows * CODES, cols), bf16),
            jax.ShapeDtypeStruct((rows // 2 * own, LANES), bf16),
        ),
        scratch_shapes=[
            pltpu.VMEM((parts,) + tables[0].shape, bf16),
            pltpu.VMEM((2, CODES, width), bf16),
            pltpu.VMEM((rows // 2 * own, LANES), bf16),
            pltpu.VMEM((heads * own, 2 * rows * CODES), bf16),
        ],
        cost_estimate=pl.CostEstimate(flops=10**9, bytes_accessed=10**6, transcendentals=0),
        compiler_params=pltpu.CompilerParams(vmem_limit_bytes=LARGE_VMEM),
        name="near_scores",
    )(*tables, codes)


def row_kernel(
    scores_ref,
    values_ref,
    near_tied_ref,
    near_hot_ref,
    near_codes_ref,
    far_codes_ref,
    row_context_ref,
    own_ref,
    live_ref,
    hot_ref,
    live_own_ref,
    sum_ref,
    spread_ref,
):
    depth = hot_ref.shape[0]
    rows = 2 * depth // CODES
    pairs = rows // 2
    width = row_context_ref.shape[1]
    heads = width // HEAD_DIM
    own = spread_ref.shape[0] // heads
    group = lax.axis_index("seq")

    live = one_hots(far_codes_ref[...], group, hot_ref, own_ref, live_own_ref)
    live = jnp.concatenate([(near_codes_ref[:, 0:LANES] >> 16).astype(f32), live], 0)
    live_ref[...] = live
    count = jnp.sum(live, axis=0, keepdims=True)[:, 0:1]
    scale = HEAD_DIM ** (-0.5) / jnp.sqrt(count)
    groups = head_groups(heads, own)
    tied = [
        near_tied_ref[at, :] + tied_sum(scores_ref, live_own_ref, hot_ref, sum_ref, first, last)
        for at, first, last in groups
    ]
    probs = [softmax_last(some * scale).astype(bf16) for some in tied]

    for (at, _, _), some in zip(groups, probs):
        spread_ref[at, 0:depth] = dot_nt(some, near_hot_ref[...]).astype(bf16)
        spread_ref[at, depth : 2 * depth] = dot_nt(some, hot_ref[...]).astype(bf16)
    spans = [slice(hp * LANES, (hp + 1) * LANES) for hp in range(heads // 2)]
    values = [spread_pair(values_ref[:, span]) for span in spans]
    contexts = []
    for hp in range(heads // 2):
        first = (hp * 2) * own
        weights = jnp.concatenate(
            [
                jnp.concatenate(
                    [
                        spread_ref[first : first + own, k * LANES : (k + 1) * LANES],
                        spread_ref[first + own : first + 2 * own, k * LANES : (k + 1) * LANES],
                    ],
                    1,
                )
                for k in range(pairs)
            ],
            0,
        )
        contexts.append(dot_nn(weights, values[hp]).astype(bf16))
    for hp in range(heads // 2):
        for k in range(pairs):
            for r2 in range(2):
                at = (2 * k + r2) * own
                row_context_ref[at : at + own, spans[hp]] = contexts[hp][
                    k * own : (k + 1) * own, r2 * LANES : (r2 + 1) * LANES
                ]


def attend_rows(near, near_codes, far_codes, own):
    scores, values, near_tied, near_hot = near
    heads, width = scores.shape[0], values.shape[1]
    half, cols = near_codes.shape
    return pl.pallas_call(
        row_kernel,
        out_shape=(
            jax.ShapeDtypeStruct((2 * half * own, width), bf16),
            jax.ShapeDtypeStruct((half // 2 * own, LANES), bf16),
            jax.ShapeDtypeStruct((2 * half, LANES), f32),
        ),
        scratch_shapes=[
            pltpu.VMEM((half * CODES, cols), bf16),
            pltpu.VMEM((half // 2 * own, LANES), bf16),
            pltpu.VMEM((heads * own, 2 * half * CODES), bf16),
            pltpu.VMEM((heads * own, 2 * half * CODES), bf16),
        ],
        cost_estimate=pl.CostEstimate(flops=3 * 10**9, bytes_accessed=10**6, transcendentals=0),
        compiler_params=pltpu.CompilerParams(vmem_limit_bytes=LARGE_VMEM),
        name="row_attention",
    )(scores, values, near_tied, near_hot, near_codes, far_codes)


def column_kernel(parts, *refs):
    row_out_refs, refs = refs[:parts], refs[parts:]
    (
        live_ref,
        row_context_ref,
        near_own_ref,
        far_own_ref,
        embed_ref,
        col_qkv_ref,
        *context_refs,
        mixed_out_ref,
        row_out_ref,
        embed2_ref,
        weight_ref,
        mixed_ref,
    ) = refs
    rows = live_ref.shape[0]
    tokens, width = row_context_ref.shape
    pairs = rows // 2
    own = tokens // rows
    vocab = embed_ref.shape[0]
    local = width // parts
    part = lax.axis_index("head")

    for p in range(parts):
        row_out_ref[part ^ p] = row_out_refs[p][...]
    embed2_ref[...] = jnp.zeros(embed2_ref.shape, bf16)
    embed2_ref[0:vocab, 0:width] = embed_ref[...]
    embed2_ref[CODES : CODES + vocab, width : 2 * width] = embed_ref[...]

    own_codes = jnp.concatenate([near_own_ref[...], far_own_ref[...]], 0)
    embedded2 = dot_nn(own_codes, embed2_ref[...])
    embedded = jnp.concatenate(
        [
            embedded2[k * own : (k + 1) * own, r2 * width : (r2 + 1) * width]
            for k in range(pairs)
            for r2 in range(2)
        ],
        0,
    )
    mixed = embedded + dot_nt(row_context_ref[...], row_out_ref[...].reshape(width, width))
    mixed_ref[...] = mixed
    normed = layer_norm(mixed).astype(bf16)

    few = 8
    groups = own // few
    unit = rows * few

    def regroup(values):
        shape = (rows, groups, few, values.shape[1])
        return jnp.swapaxes(values.reshape(shape), 0, 1).reshape(tokens, values.shape[1])

    odd = part % 2
    for t in range(3):
        first = pl.multiple_of(t * local + odd * HEAD_DIM, HEAD_DIM)
        last = pl.multiple_of(t * local + (1 - odd) * LANES, HEAD_DIM)
        third = (3 + t) * LANES
        weight_ref[t * LANES : (t + 1) * LANES, :] = col_qkv_ref[pl.ds(first, LANES), :]
        weight_ref[third : third + HEAD_DIM, :] = col_qkv_ref[pl.ds(last, HEAD_DIM), :]
        weight_ref[third + HEAD_DIM : third + LANES, :] = jnp.zeros((HEAD_DIM, width), bf16)
    proj = [
        dot_nt(normed, weight_ref[2 * j * LANES : 2 * (j + 1) * LANES, :]) for j in range(3)
    ]
    proj = [
        proj[j][:, k * LANES : (k + 1) * LANES] * (HEAD_DIM ** (-0.5) if (2 * j + k) % 3 == 0 else 1.0)
        for j in range(3)
        for k in range(2)
    ]
    proj = [regroup(values).astype(bf16) for values in proj]
    sub, lan = iota((unit, unit), 0), iota((unit, unit), 1)
    same_column = (sub % few) == (lan % few)
    seq_of_lane = iota((rows, unit), 1) // few
    live_lane = jnp.sum(
        jnp.where(seq_of_lane == iota((rows, unit), 0), live_ref[...], 0.0), axis=0, keepdims=True
    )
    visible = jnp.logical_and(same_column, jnp.broadcast_to(live_lane, (unit, unit)) > 0)
    chosen = []
    for g in range(groups):
        at = slice(g * unit, (g + 1) * unit)
        query, keys, values = (proj[t][at] for t in range(3))
        chosen += [(half, keys, values) for half in halves(query)]
        chosen.append(tuple(proj[3 + t][at] for t in range(3)))
    scores = [jnp.where(visible, dot_nt(query, keys), -jnp.inf) for query, keys, _ in chosen]
    tops = [jnp.max(score, axis=-1, keepdims=True) for score in scores]
    weights = [jnp.exp(score - top) for score, top in zip(scores, tops)]
    shares = [1.0 / jnp.sum(weight, axis=-1, keepdims=True) for weight in weights]
    probs = [(weight * share).astype(bf16) for weight, share in zip(weights, shares)]
    found = [dot_nn(prob, values) for prob, (_, _, values) in zip(probs, chosen)]
    first_head = iota((unit, LANES), 1) < HEAD_DIM

    def ungroup(blocks):
        whole = jnp.concatenate(blocks, 0).reshape(groups, rows, few, LANES)
        return jnp.swapaxes(whole, 0, 1).reshape(tokens, LANES)

    main = ungroup(
        [jnp.where(first_head, found[3 * g], found[3 * g + 1]) for g in range(groups)]
    )
    third = ungroup([found[3 * g + 2] for g in range(groups)])
    start = 0
    for context_ref in context_refs:
        count = context_ref.shape[0] * 2 // 3
        some = count // 2
        context_ref[0:count, :] = main[start : start + count].astype(bf16)
        early = third[start : start + some]
        late = third[start + some : start + count]
        left = jnp.where(odd == 1, late, early)
        right = jnp.where(odd == 1, early, late)
        context_ref[count : count + some, :] = jnp.concatenate(
            [left[:, 0:HEAD_DIM], right[:, 0:HEAD_DIM]], 1
        ).astype(bf16)
        start += count
    for p in range(parts):

        @pl.when(part == p)
        def _():
            mixed_out_ref[...] = mixed_ref[:, p * local : (p + 1) * local]


def attend_columns_here(row_outs, live, row_context, near_own, far_own, embed, col_qkv):
    parts = len(row_outs)
    tokens, width = row_context.shape
    local = width // parts
    half = tokens // 2 * local // LANES
    return pl.pallas_call(
        functools.partial(column_kernel, parts),
        out_shape=(
            jax.ShapeDtypeStruct((half, LANES), bf16),
            jax.ShapeDtypeStruct((half, LANES), bf16),
            jax.ShapeDtypeStruct((tokens, local), f32),
        ),
        scratch_shapes=[
            pltpu.VMEM((parts, local, width), bf16),
            pltpu.VMEM((2 * CODES, 2 * width), bf16),
            pltpu.VMEM((6 * LANES, width), bf16),
            pltpu.VMEM((tokens, width), f32),
        ],
        cost_estimate=pl.CostEstimate(flops=2 * 10**9, bytes_accessed=10**6, transcendentals=0),
        compiler_params=pltpu.CompilerParams(vmem_limit_bytes=LARGE_VMEM),
        name="column_attention",
    )(*row_outs, live, row_context, near_own, far_own, embed, col_qkv)


def steps_of(groups):
    return [1] + [1 << k for k in range(groups.bit_length() - 2, 0, -1)]


def slot_order(groups):
    order = [0]
    for step in steps_of(groups):
        order += [slot ^ step for slot in order]
    return order


def finish_kernel(parts, groups, *refs):
    context_refs = [refs[:parts], refs[parts : 2 * parts]]
    mixed_ref, col_out_ref, out_ref, context_ref = refs[2 * parts :]
    tokens, local = mixed_ref.shape
    group = lax.axis_index("seq")
    part = lax.axis_index("head")
    starts = [0, context_refs[0][0].shape[0]]
    for start, some_refs in zip(starts, context_refs):
        for p in range(parts):
            context_ref[part ^ p, start : start + some_refs[p].shape[0], :] = some_refs[p][...]
    pieces = []
    for start, some_refs in zip(starts, context_refs):
        count = some_refs[0].shape[0] * 2 // 3
        end = start + some_refs[0].shape[0]
        low = iota((count // 2, LANES), 1) < HEAD_DIM
        features = []
        for p in range(0, parts, 2):
            even = context_ref[p, start + count : end, :]
            other = context_ref[p + 1, start + count : end, :]
            early = jnp.where(low, even, other)
            late = jnp.where(low, other, even)
            late = jnp.concatenate([late[:, HEAD_DIM:], late[:, 0:HEAD_DIM]], 1)
            features += [
                context_ref[p, start : start + count, :],
                jnp.concatenate([early, late], 0),
                context_ref[p + 1, start : start + count, :],
            ]
        pieces.append(jnp.concatenate(features, 1))
    total = mixed_ref[...] + dot_nt(jnp.concatenate(pieces, 0), col_out_ref[...])
    own = tokens // groups // 2
    for d, slot in enumerate(slot_order(groups)):
        first, second = (total[(2 * d + r) * own : (2 * d + r + 1) * own, :] for r in range(2))
        rest = jnp.concatenate([first[:, LANES:local], second[:, LANES:local]], 1)
        out_ref[group ^ slot] = jnp.concatenate(
            [first[:, 0:LANES], second[:, 0:LANES], rest], 0
        ).astype(bf16)


def finish(contexts, mixed, col_out, groups):
    parts = len(contexts[0])
    tokens, local = mixed.shape
    return pl.pallas_call(
        functools.partial(finish_kernel, parts, groups),
        out_shape=jax.ShapeDtypeStruct((groups, tokens // groups * local // LANES, LANES), bf16),
        scratch_shapes=[pltpu.VMEM((parts, tokens * local // LANES, LANES), bf16)],
        compiler_params=pltpu.CompilerParams(vmem_limit_bytes=LARGE_VMEM),
        name="finish",
    )(*contexts[0], *contexts[1], mixed, col_out)


def order_kernel(blocks_ref, out_ref):
    groups = blocks_ref.shape[0]
    local, cols = out_ref.shape[1:]
    own = cols // groups
    rest = local - LANES
    for part in range(3):
        piece = jnp.concatenate(
            [blocks_ref[g, part * own : (part + 1) * own, :] for g in range(groups)], 0
        )
        turned = piece.astype(f32).T.astype(bf16)
        if part < 2:
            out_ref[part, 0:LANES, :] = turned
        else:
            for r in range(2):
                out_ref[r, LANES:local, :] = turned[r * rest : (r + 1) * rest, :]


def order(blocks, cols, local):
    return pl.pallas_call(
        order_kernel,
        out_shape=jax.ShapeDtypeStruct((2, local, cols), bf16),
        compiler_params=pltpu.CompilerParams(vmem_limit_bytes=SMALL_VMEM),
        name="order",
    )(blocks)


def fast_body(ids, pad_mask, embed, row_qkv, row_out, col_qkv, col_out):
    rows_here, cols = ids.shape
    width = embed.shape[1]
    local = row_out.shape[0]
    groups, parts = lax.axis_size("seq"), lax.axis_size("head")
    own, rows = cols // groups, rows_here * groups

    def pairwise(value, partner):
        order = [(g, p) for g in range(groups) for p in range(parts)]
        link = [(g * parts + p, partner(g, p)) for g, p in order]
        return lax.ppermute(value, ("seq", "head"), [(i, g * parts + p) for i, (g, p) in link])

    def sibling(g, p):
        return g, p ^ 1

    def across(g, p):
        return g, p ^ 2

    far = pairwise(row_out, across)
    other_ids = pairwise(ids, lambda g, p: (g ^ 1, p))
    other_mask = pairwise(pad_mask.reshape(1, rows_here), lambda g, p: (g ^ 1, p))
    table, coded = make_tables(ids, pad_mask, embed, row_qkv, rows_here * groups // 2)
    tables = [table, None, None, None]
    for count, step in enumerate(steps_of(groups)[1:], 1):
        if count == 1:
            coded = join_raw(coded, other_ids, other_mask)
            coded, table = lax.optimization_barrier((coded, table))
            tables[2] = pairwise(table, across)
        else:
            coded = join(coded, received, rows_here << (count - 1))
        if count == 2:
            coded, table, row_out, far = lax.optimization_barrier((coded, table, row_out, far))
            tables[1], tables[3] = pairwise(table, sibling), pairwise(tables[2], sibling)
            row_outs = [row_out, pairwise(row_out, sibling), far, pairwise(far, sibling)]
        received = pairwise(coded, lambda g, p, step=step: (g ^ step, p))
    codes = (coded, received)
    *near_scores, near_own = attend_near(tables, codes[0], own)
    row_context, far_own, live = attend_rows(near_scores, *codes, own)
    *halves_here, mixed = attend_columns_here(
        row_outs,
        live,
        row_context,
        near_own,
        far_own,
        embed,
        col_qkv.reshape(3 * local, width),
    )
    contexts = []
    for context in halves_here:
        beyond = pairwise(context, across)
        contexts.append(
            (context, pairwise(context, sibling), beyond, pairwise(beyond, sibling))
        )
    blocks = finish(contexts, mixed, col_out, groups)
    blocks = lax.all_to_all(blocks, "seq", split_axis=0, concat_axis=0, tiled=True)
    return jnp.swapaxes(order(blocks, cols, local), 1, 2)


def weight_fold(out_weight, piece):
    return jnp.einsum("rce,fe->rcf", piece, out_weight, preferred_element_type=f32)


def attend_columns(query, keys, values, key_live):
    rows_all, count_cols, local_width = query.shape
    heads_here = local_width // HEAD_DIM
    shape = (rows_all, count_cols, heads_here, HEAD_DIM)
    scores = jnp.einsum(
        "rchd,schd->chrs",
        query.reshape(shape),
        keys.reshape(shape),
        preferred_element_type=f32,
    ) * HEAD_DIM ** (-0.5)
    scores = jnp.where(key_live > 0, scores, -jnp.inf)
    probs = softmax_last(scores).astype(bf16)
    context = jnp.einsum(
        "chrs,schd->rchd", probs, values.reshape(shape), preferred_element_type=f32
    )
    return context.astype(bf16).reshape(rows_all, count_cols, local_width)


def send_back(context):
    return lax.all_to_all(context[:, None], "seq", split_axis=0, concat_axis=1, tiled=True)


def general_body(ids, pad_mask, embed, row_qkv, row_out, col_qkv, col_out):
    rows_here, cols = ids.shape
    width = embed.shape[1]
    local_width = row_out.shape[0]
    heads_here = local_width // HEAD_DIM
    groups = lax.axis_size("seq")
    per_group = cols // groups
    codes = lax.broadcasted_iota(jnp.int32, (1, 1, embed.shape[0]), 2)
    onehot = (ids[:, :, None] == codes).astype(bf16)
    embedded = jnp.einsum("rcv,vd->rcd", onehot, embed, preferred_element_type=f32)
    normed = layer_norm(embedded).astype(bf16)
    row_proj = jnp.einsum("rcd,ted->trce", normed, row_qkv, preferred_element_type=f32)
    row_proj = row_proj.astype(bf16)
    live = pad_mask.astype(bf16)
    head_shape = (rows_here, cols, heads_here, HEAD_DIM)
    query = (row_proj[0] * live[:, None, None]).reshape(head_shape)
    keys = row_proj[1].reshape(head_shape)
    values = row_proj[2].reshape(head_shape)
    partial_scores = jnp.einsum("rihd,rjhd->hij", query, keys, preferred_element_type=f32)
    count_here = jnp.sum(pad_mask.astype(f32))
    scale = HEAD_DIM ** (-0.5)
    total, count = lax.psum((partial_scores, count_here), "seq")
    row_probs = softmax_last(total * (scale / jnp.sqrt(count))).astype(bf16)
    row_context = jnp.einsum("hij,rjhd->rihd", row_probs, values, preferred_element_type=f32)
    row_context = row_context.astype(bf16).reshape(rows_here, cols, local_width)
    start_feature = lax.axis_index("head") * local_width
    resident = lax.dynamic_slice_in_dim(embedded, start_feature, local_width, 2)
    row_update = weight_fold(row_out, lax.all_gather(row_context, "head", axis=2, tiled=True))
    mixed = resident + row_update
    sums, squares = lax.psum((jnp.sum(mixed, axis=-1), jnp.sum(mixed * mixed, axis=-1)), "head")
    mean = sums / width
    spread = squares / width - mean * mean
    normed_here = ((mixed - mean[..., None]) * lax.rsqrt(spread[..., None] + EPS)).astype(bf16)
    live_tile = jnp.broadcast_to(live[:, None, None, None], (rows_here, groups, per_group, 1))
    normed_full = lax.all_gather(normed_here, "head", axis=2, tiled=True)
    col_proj = jnp.einsum("rcd,ted->rcte", normed_full, col_qkv, preferred_element_type=f32)
    packed = col_proj.astype(bf16).reshape(rows_here, groups, per_group, 3 * local_width)
    received = lax.all_to_all(packed, "seq", split_axis=1, concat_axis=0, tiled=True)
    mask_part = lax.all_to_all(live_tile, "seq", split_axis=1, concat_axis=0, tiled=True)
    column_out = send_back(
        attend_columns(
            received[:, 0, :, :local_width],
            received[:, 0, :, local_width : 2 * local_width],
            received[:, 0, :, 2 * local_width :],
            mask_part[:, 0, 0, 0],
        )
    )
    column_out = column_out.reshape(rows_here, cols, local_width)
    col_update = weight_fold(col_out, lax.all_gather(column_out, "head", axis=2, tiled=True))
    return (mixed + col_update).astype(bf16)


def body(ids, pad_mask, embed, row_qkv, row_out, col_qkv, col_out):
    rows_here, cols = ids.shape
    groups = lax.axis_size("seq")
    own, rows = cols // groups, rows_here * groups
    parts = lax.axis_size("head")
    local = row_out.shape[0]
    fits = (
        parts == 4
        and groups >= 8
        and groups & (groups - 1) == 0
        and rows * 8 == LANES
        and rows_here == 2
        and own % 32 == 0
        and cols >= LANES
        and local == LANES + HEAD_DIM
        and embed.shape[0] <= TABLE_ROWS
    )
    chosen = fast_body if fits else general_body
    return chosen(ids, pad_mask, embed, row_qkv, row_out, col_qkv, col_out)


def solution(mesh):
    placed = (
        P("seq", None),
        P("seq"),
        P(),
        P(None, "head", None),
        P("head", None),
        P(None, "head", None),
        P("head", None),
    )
    return jax.shard_map(
        body, mesh=mesh, in_specs=placed, out_specs=P("seq", None, "head"), check_vma=False
    )
```

```python
import functools

import jax
import jax.numpy as jnp
from jax import lax
from jax.experimental import pallas as pl
from jax.experimental.pallas import tpu as pltpu
from jax.sharding import PartitionSpec as P

HEAD_DIM = 64
EPS = 1e-05
LANES = 128
CODES = 64
TABLE_ROWS = 40

SMALL_VMEM = 8 * 1024 * 1024
LARGE_VMEM = 32 * 1024 * 1024

f32 = jnp.float32
bf16 = jnp.bfloat16


def layer_norm(values):
    mean = jnp.mean(values, axis=-1, keepdims=True)
    centred = values - mean
    spread = jnp.mean(centred * centred, axis=-1, keepdims=True)
    return centred * lax.rsqrt(spread + EPS)


def softmax_last(scores):
    top = jnp.max(scores, axis=-1, keepdims=True)
    weights = jnp.exp(scores - top)
    return weights * (1.0 / jnp.sum(weights, axis=-1, keepdims=True))


def dot_nt(left, right):
    return lax.dot_general(left, right, (((1,), (1,)), ((), ())), preferred_element_type=f32)


def dot_nn(left, right):
    return jnp.dot(left, right, preferred_element_type=f32)


def in_hbm(value):
    return pltpu.with_memory_space_constraint(value, pltpu.HBM)


def iota(shape, axis):
    return lax.broadcasted_iota(jnp.int32, shape, axis)


def join_kernel(rows, own_ref, other_ref, out_ref):
    own, other = own_ref[...], other_ref[...]
    both = jnp.concatenate([own[0:rows], other[0:rows]], 0)
    out_ref[...] = jnp.concatenate([both] * (own.shape[0] // (2 * rows)), 0)


def join(own, other, rows):
    return pl.pallas_call(
        functools.partial(join_kernel, rows),
        out_shape=jax.ShapeDtypeStruct(own.shape, own.dtype),
        compiler_params=pltpu.CompilerParams(vmem_limit_bytes=SMALL_VMEM),
        name="join",
    )(own, other)


def join_raw_kernel(own_ref, ids_ref, live_ref, out_ref):
    rows = ids_ref.shape[0]
    live = live_ref[...]
    other = ids_ref[...] + 65536 * jnp.concatenate(
        [jnp.broadcast_to(live[:, r : r + 1], (1, ids_ref.shape[1])) for r in range(rows)], 0
    )
    both = jnp.concatenate([own_ref[0:rows], other], 0)
    out_ref[...] = jnp.concatenate([both] * (out_ref.shape[0] // (2 * rows)), 0)


def join_raw(own, ids, pad_mask):
    return pl.pallas_call(
        join_raw_kernel,
        out_shape=jax.ShapeDtypeStruct(own.shape, own.dtype),
        compiler_params=pltpu.CompilerParams(vmem_limit_bytes=SMALL_VMEM),
        name="join_raw",
    )(own, ids, pad_mask)


def table_kernel(
    ids_hbm,
    live_hbm,
    embed_hbm,
    qkv_hbm,
    out_ref,
    coded_ref,
    ids_ref,
    live_ref,
    embed_ref,
    qkv_ref,
    padded_ref,
    sems,
):
    kinds = qkv_ref.shape[0]
    loads = [
        pltpu.make_async_copy(embed_hbm, embed_ref, sems.at[kinds]),
        pltpu.make_async_copy(ids_hbm, ids_ref, sems.at[kinds + 1]),
        pltpu.make_async_copy(live_hbm, live_ref, sems.at[kinds + 2]),
    ]
    loads += [
        pltpu.make_async_copy(qkv_hbm.at[t], qkv_ref.at[t], sems.at[t]) for t in range(kinds)
    ]
    for load in loads:
        load.start()
    padded_ref[...] = jnp.zeros(padded_ref.shape, f32)
    for load in loads[0:3]:
        load.wait()
    padded_ref[0 : embed_ref.shape[0], :] = embed_ref[...].astype(f32)
    normed = layer_norm(padded_ref[...]).astype(bf16)
    row = iota(ids_ref.shape, 0)
    live = jnp.zeros(ids_ref.shape, jnp.int32)
    for r in range(ids_ref.shape[0]):
        live = jnp.where(row == r, live_ref[r], live)
    coded = ids_ref[...] + 65536 * live
    coded_ref[...] = jnp.concatenate([coded] * (coded_ref.shape[0] // coded.shape[0]), 0)
    tables = []
    for t in range(kinds):
        loads[3 + t].wait()
        tables.append(dot_nt(normed, qkv_ref[t]))
    out_ref[...] = jnp.concatenate(tables, 1).astype(bf16)


def make_tables(ids, pad_mask, embed, row_qkv, height):
    kinds, local, width = row_qkv.shape
    return pl.pallas_call(
        table_kernel,
        out_shape=(
            jax.ShapeDtypeStruct((TABLE_ROWS, kinds * local), bf16),
            jax.ShapeDtypeStruct((height, ids.shape[1]), jnp.int32),
        ),
        in_specs=[pl.BlockSpec(memory_space=pltpu.HBM)] * 4,
        scratch_shapes=[
            pltpu.VMEM(ids.shape, jnp.int32),
            pltpu.SMEM(pad_mask.shape, jnp.int32),
            pltpu.VMEM(embed.shape, bf16),
            pltpu.VMEM(row_qkv.shape, bf16),
            pltpu.VMEM((TABLE_ROWS, width), f32),
            pltpu.SemaphoreType.DMA((kinds + 3,)),
        ],
        cost_estimate=pl.CostEstimate(
            flops=2 * 10**9, bytes_accessed=2 * row_qkv.size, transcendentals=0
        ),
        compiler_params=pltpu.CompilerParams(vmem_limit_bytes=SMALL_VMEM),
        name="tables",
    )(in_hbm(ids), in_hbm(pad_mask), in_hbm(embed), in_hbm(row_qkv))


def halves(pair):
    lane = iota(pair.shape, 1)
    zero = jnp.zeros_like(pair)
    return jnp.where(lane < HEAD_DIM, pair, zero), jnp.where(lane < HEAD_DIM, zero, pair)


def spread_pair(pair):
    first, second = halves(pair)
    zero = jnp.zeros_like(pair)
    return jnp.concatenate(
        [
            jnp.concatenate([first, zero], 1),
            jnp.concatenate([zero, first], 1),
            jnp.concatenate([second, zero], 1),
            jnp.concatenate([zero, second], 1),
        ],
        0,
    )


def double(block):
    zero = jnp.zeros_like(block)
    return jnp.concatenate(
        [jnp.concatenate([block, zero], 1), jnp.concatenate([zero, block], 1)], 0
    )


def one_hots(coded, group, hot_ref, own_ref, live_own_ref):
    depth, cols = hot_ref.shape
    rows = depth // CODES
    pairs = rows // 2
    own = own_ref.shape[0] // pairs
    ids = (coded & 0xFFFF).astype(f32)
    live = (coded[:, 0:LANES] >> 16).astype(f32)

    code = iota((CODES, cols), 0).astype(f32)
    for r in range(rows):
        hot = jnp.broadcast_to(ids[r : r + 1, :], (CODES, cols)) == code
        hot_ref[r * CODES : (r + 1) * CODES, :] = hot.astype(f32).astype(bf16)

    pick = (iota((own, cols), 1) == group * own + iota((own, cols), 0)).astype(f32).astype(bf16)
    mine = dot_nt(pick, ids.astype(bf16))
    lane = iota((own, LANES), 1)
    first_half = lane < CODES
    lane_code = jnp.where(first_half, lane, lane - CODES).astype(f32)
    for k in range(pairs):
        value = jnp.where(first_half, mine[:, 2 * k : 2 * k + 1], mine[:, 2 * k + 1 : 2 * k + 2])
        hot = (value == lane_code).astype(f32)
        alive = jnp.where(first_half, live[2 * k : 2 * k + 1, :], live[2 * k + 1 : 2 * k + 2, :])
        own_ref[k * own : (k + 1) * own, :] = hot.astype(bf16)
        live_own_ref[k * own : (k + 1) * own, :] = (hot * alive).astype(bf16)
    return live


def head_groups(heads, own):
    some = heads // 2
    return [(slice(g * some * own, (g + 1) * some * own), g * some, (g + 1) * some) for g in range(2)]


def tied_sum(scores_ref, live_own_ref, hot_ref, sum_ref, first, last):
    own = sum_ref.shape[0] // scores_ref.shape[0]
    depth = hot_ref.shape[0]
    pairs = depth // CODES // 2
    for h in range(first, last):
        looked = dot_nn(live_own_ref[...], scores_ref[h]).astype(bf16)
        for piece in range(2):
            for k in range(pairs):
                to = piece * depth + k * LANES
                sum_ref[h * own : (h + 1) * own, to : to + LANES] = looked[
                    k * own : (k + 1) * own, piece * LANES : (piece + 1) * LANES
                ]
    at = slice(first * own, last * own)
    return dot_nn(sum_ref[at, 0:depth], hot_ref[...]) + dot_nn(
        sum_ref[at, depth : 2 * depth], hot_ref[...]
    )


def near_kernel(parts, *refs):
    tables_refs, refs = refs[:parts], refs[parts:]
    (
        codes_ref,
        scores_ref,
        values_ref,
        tied_ref,
        hot_ref,
        own_ref,
        tables_ref,
        table_ref,
        live_own_ref,
        sum_ref,
    ) = refs
    width = values_ref.shape[1]
    heads = width // HEAD_DIM
    local = width // parts
    group = lax.axis_index("seq")
    part = lax.axis_index("head")
    for p in range(parts):
        tables_ref[part ^ p] = tables_refs[p][...]

    for t in range(3):
        to_ref = values_ref if t == 2 else table_ref.at[t]
        to_ref[0:TABLE_ROWS, :] = jnp.concatenate(
            [tables_ref[p, :, t * local : (t + 1) * local] for p in range(parts)], 1
        )
        to_ref[TABLE_ROWS:CODES, :] = jnp.zeros((CODES - TABLE_ROWS, width), bf16)

    spans = [slice(hp * LANES, (hp + 1) * LANES) for hp in range(heads // 2)]
    queries = [spread_pair(table_ref[0, :, span]) for span in spans]
    keys = [double(table_ref[1, :, span]) for span in spans]
    scores = [dot_nt(query, key) for query, key in zip(queries, keys)]
    high = [score.astype(bf16) for score in scores]
    low = [(score - part_of.astype(f32)).astype(bf16) for score, part_of in zip(scores, high)]
    for h in range(heads):
        these = slice(h % 2 * LANES, (h % 2 + 1) * LANES)
        scores_ref[h, :, 0:LANES] = high[h // 2][these]
        scores_ref[h, :, LANES : 2 * LANES] = low[h // 2][these]

    one_hots(codes_ref[...], group, hot_ref, own_ref, live_own_ref)
    tied_ref[...] = tied_sum(scores_ref, live_own_ref, hot_ref, sum_ref, 0, heads)


def attend_near(tables, codes, own):
    parts = len(tables)
    width = tables[0].shape[1] // 3 * parts
    heads = width // HEAD_DIM
    rows, cols = codes.shape
    return pl.pallas_call(
        functools.partial(near_kernel, parts),
        out_shape=(
            jax.ShapeDtypeStruct((heads, LANES, 2 * LANES), bf16),
            jax.ShapeDtypeStruct((CODES, width), bf16),
            jax.ShapeDtypeStruct((heads * own, cols), f32),
            jax.ShapeDtypeStruct((rows * CODES, cols), bf16),
            jax.ShapeDtypeStruct((rows // 2 * own, LANES), bf16),
        ),
        scratch_shapes=[
            pltpu.VMEM((parts,) + tables[0].shape, bf16),
            pltpu.VMEM((2, CODES, width), bf16),
            pltpu.VMEM((rows // 2 * own, LANES), bf16),
            pltpu.VMEM((heads * own, 2 * rows * CODES), bf16),
        ],
        cost_estimate=pl.CostEstimate(flops=10**9, bytes_accessed=10**6, transcendentals=0),
        compiler_params=pltpu.CompilerParams(vmem_limit_bytes=LARGE_VMEM),
        name="near_scores",
    )(*tables, codes)


def row_kernel(
    scores_ref,
    values_ref,
    near_tied_ref,
    near_hot_ref,
    near_codes_ref,
    far_codes_ref,
    row_context_ref,
    own_ref,
    live_ref,
    hot_ref,
    live_own_ref,
    sum_ref,
    spread_ref,
):
    depth = hot_ref.shape[0]
    rows = 2 * depth // CODES
    pairs = rows // 2
    width = row_context_ref.shape[1]
    heads = width // HEAD_DIM
    own = spread_ref.shape[0] // heads
    group = lax.axis_index("seq")

    live = one_hots(far_codes_ref[...], group, hot_ref, own_ref, live_own_ref)
    live = jnp.concatenate([(near_codes_ref[:, 0:LANES] >> 16).astype(f32), live], 0)
    live_ref[...] = live
    count = jnp.sum(live, axis=0, keepdims=True)[:, 0:1]
    scale = HEAD_DIM ** (-0.5) / jnp.sqrt(count)
    groups = head_groups(heads, own)
    tied = [
        near_tied_ref[at, :] + tied_sum(scores_ref, live_own_ref, hot_ref, sum_ref, first, last)
        for at, first, last in groups
    ]
    probs = [softmax_last(some * scale).astype(bf16) for some in tied]

    for (at, _, _), some in zip(groups, probs):
        spread_ref[at, 0:depth] = dot_nt(some, near_hot_ref[...]).astype(bf16)
        spread_ref[at, depth : 2 * depth] = dot_nt(some, hot_ref[...]).astype(bf16)
    spans = [slice(hp * LANES, (hp + 1) * LANES) for hp in range(heads // 2)]
    values = [spread_pair(values_ref[:, span]) for span in spans]
    contexts = []
    for hp in range(heads // 2):
        first = (hp * 2) * own
        weights = jnp.concatenate(
            [
                jnp.concatenate(
                    [
                        spread_ref[first : first + own, k * LANES : (k + 1) * LANES],
                        spread_ref[first + own : first + 2 * own, k * LANES : (k + 1) * LANES],
                    ],
                    1,
                )
                for k in range(pairs)
            ],
            0,
        )
        contexts.append(dot_nn(weights, values[hp]).astype(bf16))
    for hp in range(heads // 2):
        for k in range(pairs):
            for r2 in range(2):
                at = (2 * k + r2) * own
                row_context_ref[at : at + own, spans[hp]] = contexts[hp][
                    k * own : (k + 1) * own, r2 * LANES : (r2 + 1) * LANES
                ]


def attend_rows(near, near_codes, far_codes, own):
    scores, values, near_tied, near_hot = near
    heads, width = scores.shape[0], values.shape[1]
    half, cols = near_codes.shape
    return pl.pallas_call(
        row_kernel,
        out_shape=(
            jax.ShapeDtypeStruct((2 * half * own, width), bf16),
            jax.ShapeDtypeStruct((half // 2 * own, LANES), bf16),
            jax.ShapeDtypeStruct((2 * half, LANES), f32),
        ),
        scratch_shapes=[
            pltpu.VMEM((half * CODES, cols), bf16),
            pltpu.VMEM((half // 2 * own, LANES), bf16),
            pltpu.VMEM((heads * own, 2 * half * CODES), bf16),
            pltpu.VMEM((heads * own, 2 * half * CODES), bf16),
        ],
        cost_estimate=pl.CostEstimate(flops=3 * 10**9, bytes_accessed=10**6, transcendentals=0),
        compiler_params=pltpu.CompilerParams(vmem_limit_bytes=LARGE_VMEM),
        name="row_attention",
    )(scores, values, near_tied, near_hot, near_codes, far_codes)


def column_kernel(parts, *refs):
    row_out_refs, refs = refs[:parts], refs[parts:]
    (
        live_ref,
        row_context_ref,
        near_own_ref,
        far_own_ref,
        embed_ref,
        col_qkv_ref,
        *context_refs,
        mixed_out_ref,
        row_out_ref,
        embed2_ref,
        weight_ref,
        mixed_ref,
    ) = refs
    rows = live_ref.shape[0]
    tokens, width = row_context_ref.shape
    pairs = rows // 2
    own = tokens // rows
    vocab = embed_ref.shape[0]
    local = width // parts
    part = lax.axis_index("head")

    for p in range(parts):
        row_out_ref[part ^ p] = row_out_refs[p][...]
    embed2_ref[...] = jnp.zeros(embed2_ref.shape, bf16)
    embed2_ref[0:vocab, 0:width] = embed_ref[...]
    embed2_ref[CODES : CODES + vocab, width : 2 * width] = embed_ref[...]

    own_codes = jnp.concatenate([near_own_ref[...], far_own_ref[...]], 0)
    embedded2 = dot_nn(own_codes, embed2_ref[...])
    embedded = jnp.concatenate(
        [
            embedded2[k * own : (k + 1) * own, r2 * width : (r2 + 1) * width]
            for k in range(pairs)
            for r2 in range(2)
        ],
        0,
    )
    mixed = embedded + dot_nt(row_context_ref[...], row_out_ref[...].reshape(width, width))
    mixed_ref[...] = mixed
    normed = layer_norm(mixed).astype(bf16)

    few = 8
    groups = own // few
    unit = rows * few

    def regroup(values):
        shape = (rows, groups, few, values.shape[1])
        return jnp.swapaxes(values.reshape(shape), 0, 1).reshape(tokens, values.shape[1])

    odd = part % 2
    for t in range(3):
        first = pl.multiple_of(t * local + odd * HEAD_DIM, HEAD_DIM)
        last = pl.multiple_of(t * local + (1 - odd) * LANES, HEAD_DIM)
        third = (3 + t) * LANES
        weight_ref[t * LANES : (t + 1) * LANES, :] = col_qkv_ref[pl.ds(first, LANES), :]
        weight_ref[third : third + HEAD_DIM, :] = col_qkv_ref[pl.ds(last, HEAD_DIM), :]
        weight_ref[third + HEAD_DIM : third + LANES, :] = jnp.zeros((HEAD_DIM, width), bf16)
    proj = [
        dot_nt(normed, weight_ref[2 * j * LANES : 2 * (j + 1) * LANES, :]) for j in range(3)
    ]
    proj = [
        proj[j][:, k * LANES : (k + 1) * LANES] * (HEAD_DIM ** (-0.5) if (2 * j + k) % 3 == 0 else 1.0)
        for j in range(3)
        for k in range(2)
    ]
    proj = [regroup(values).astype(bf16) for values in proj]
    sub, lan = iota((unit, unit), 0), iota((unit, unit), 1)
    same_column = (sub % few) == (lan % few)
    seq_of_lane = iota((rows, unit), 1) // few
    live_lane = jnp.sum(
        jnp.where(seq_of_lane == iota((rows, unit), 0), live_ref[...], 0.0), axis=0, keepdims=True
    )
    visible = jnp.logical_and(same_column, jnp.broadcast_to(live_lane, (unit, unit)) > 0)
    chosen = []
    for g in range(groups):
        at = slice(g * unit, (g + 1) * unit)
        query, keys, values = (proj[t][at] for t in range(3))
        chosen += [(half, keys, values) for half in halves(query)]
        chosen.append(tuple(proj[3 + t][at] for t in range(3)))
    scores = [jnp.where(visible, dot_nt(query, keys), -jnp.inf) for query, keys, _ in chosen]
    tops = [jnp.max(score, axis=-1, keepdims=True) for score in scores]
    weights = [jnp.exp(score - top) for score, top in zip(scores, tops)]
    shares = [1.0 / jnp.sum(weight, axis=-1, keepdims=True) for weight in weights]
    probs = [(weight * share).astype(bf16) for weight, share in zip(weights, shares)]
    found = [dot_nn(prob, values) for prob, (_, _, values) in zip(probs, chosen)]
    first_head = iota((unit, LANES), 1) < HEAD_DIM

    def ungroup(blocks):
        whole = jnp.concatenate(blocks, 0).reshape(groups, rows, few, LANES)
        return jnp.swapaxes(whole, 0, 1).reshape(tokens, LANES)

    main = ungroup(
        [jnp.where(first_head, found[3 * g], found[3 * g + 1]) for g in range(groups)]
    )
    third = ungroup([found[3 * g + 2] for g in range(groups)])
    start = 0
    for context_ref in context_refs:
        count = context_ref.shape[0] * 2 // 3
        some = count // 2
        context_ref[0:count, :] = main[start : start + count].astype(bf16)
        early = third[start : start + some]
        late = third[start + some : start + count]
        left = jnp.where(odd == 1, late, early)
        right = jnp.where(odd == 1, early, late)
        context_ref[count : count + some, :] = jnp.concatenate(
            [left[:, 0:HEAD_DIM], right[:, 0:HEAD_DIM]], 1
        ).astype(bf16)
        start += count
    for p in range(parts):

        @pl.when(part == p)
        def _():
            mixed_out_ref[...] = mixed_ref[:, p * local : (p + 1) * local]


def attend_columns_here(row_outs, live, row_context, near_own, far_own, embed, col_qkv):
    parts = len(row_outs)
    tokens, width = row_context.shape
    local = width // parts
    return pl.pallas_call(
        functools.partial(column_kernel, parts),
        out_shape=(
            jax.ShapeDtypeStruct((tokens * local // LANES, LANES), bf16),
            jax.ShapeDtypeStruct((tokens, local), f32),
        ),
        scratch_shapes=[
            pltpu.VMEM((parts, local, width), bf16),
            pltpu.VMEM((2 * CODES, 2 * width), bf16),
            pltpu.VMEM((6 * LANES, width), bf16),
            pltpu.VMEM((tokens, width), f32),
        ],
        cost_estimate=pl.CostEstimate(flops=2 * 10**9, bytes_accessed=10**6, transcendentals=0),
        compiler_params=pltpu.CompilerParams(vmem_limit_bytes=LARGE_VMEM),
        name="column_attention",
    )(*row_outs, live, row_context, near_own, far_own, embed, col_qkv)


def steps_of(groups):
    return [1] + [1 << k for k in range(groups.bit_length() - 2, 0, -1)]


def slot_order(groups):
    order = [0]
    for step in steps_of(groups):
        order += [slot ^ step for slot in order]
    return order


def finish_kernel(parts, groups, *refs):
    context_refs = [refs[:parts]]
    mixed_ref, col_out_ref, out_ref, context_ref = refs[parts:]
    tokens, local = mixed_ref.shape
    group = lax.axis_index("seq")
    part = lax.axis_index("head")
    starts = [0]
    for start, some_refs in zip(starts, context_refs):
        for p in range(parts):
            context_ref[part ^ p, start : start + some_refs[p].shape[0], :] = some_refs[p][...]
    pieces = []
    for start, some_refs in zip(starts, context_refs):
        count = some_refs[0].shape[0] * 2 // 3
        end = start + some_refs[0].shape[0]
        low = iota((count // 2, LANES), 1) < HEAD_DIM
        features = []
        for p in range(0, parts, 2):
            even = context_ref[p, start + count : end, :]
            other = context_ref[p + 1, start + count : end, :]
            early = jnp.where(low, even, other)
            late = jnp.where(low, other, even)
            late = jnp.concatenate([late[:, HEAD_DIM:], late[:, 0:HEAD_DIM]], 1)
            features += [
                context_ref[p, start : start + count, :],
                jnp.concatenate([early, late], 0),
                context_ref[p + 1, start : start + count, :],
            ]
        pieces.append(jnp.concatenate(features, 1))
    total = mixed_ref[...] + dot_nt(jnp.concatenate(pieces, 0), col_out_ref[...])
    own = tokens // groups // 2
    for d, slot in enumerate(slot_order(groups)):
        first, second = (total[(2 * d + r) * own : (2 * d + r + 1) * own, :] for r in range(2))
        rest = jnp.concatenate([first[:, LANES:local], second[:, LANES:local]], 1)
        out_ref[group ^ slot] = jnp.concatenate(
            [first[:, 0:LANES], second[:, 0:LANES], rest], 0
        ).astype(bf16)


def finish(contexts, mixed, col_out, groups):
    parts = len(contexts[0])
    tokens, local = mixed.shape
    return pl.pallas_call(
        functools.partial(finish_kernel, parts, groups),
        out_shape=jax.ShapeDtypeStruct((groups, tokens // groups * local // LANES, LANES), bf16),
        scratch_shapes=[pltpu.VMEM((parts, tokens * local // LANES, LANES), bf16)],
        compiler_params=pltpu.CompilerParams(vmem_limit_bytes=LARGE_VMEM),
        name="finish",
    )(*contexts[0], mixed, col_out)


def order_kernel(blocks_ref, out_ref):
    groups = blocks_ref.shape[0]
    local, cols = out_ref.shape[1:]
    own = cols // groups
    rest = local - LANES
    for part in range(3):
        piece = jnp.concatenate(
            [blocks_ref[g, part * own : (part + 1) * own, :] for g in range(groups)], 0
        )
        turned = piece.astype(f32).T.astype(bf16)
        if part < 2:
            out_ref[part, 0:LANES, :] = turned
        else:
            for r in range(2):
                out_ref[r, LANES:local, :] = turned[r * rest : (r + 1) * rest, :]


def order(blocks, cols, local):
    return pl.pallas_call(
        order_kernel,
        out_shape=jax.ShapeDtypeStruct((2, local, cols), bf16),
        compiler_params=pltpu.CompilerParams(vmem_limit_bytes=SMALL_VMEM),
        name="order",
    )(blocks)


def fast_body(ids, pad_mask, embed, row_qkv, row_out, col_qkv, col_out):
    rows_here, cols = ids.shape
    width = embed.shape[1]
    local = row_out.shape[0]
    groups, parts = lax.axis_size("seq"), lax.axis_size("head")
    own, rows = cols // groups, rows_here * groups

    def pairwise(value, partner):
        order = [(g, p) for g in range(groups) for p in range(parts)]
        link = [(g * parts + p, partner(g, p)) for g, p in order]
        return lax.ppermute(value, ("seq", "head"), [(i, g * parts + p) for i, (g, p) in link])

    def sibling(g, p):
        return g, p ^ 1

    def across(g, p):
        return g, p ^ 2

    def opposite(g, p):
        return g, p ^ 3

    far = pairwise(row_out, across)
    other_ids = pairwise(ids, lambda g, p: (g ^ 1, p))
    other_mask = pairwise(pad_mask.reshape(1, rows_here), lambda g, p: (g ^ 1, p))
    table, coded = make_tables(ids, pad_mask, embed, row_qkv, rows_here * groups // 2)
    tables = [table, None, pairwise(table, across), None]
    for count, step in enumerate(steps_of(groups)[1:], 1):
        if count == 1:
            coded = join_raw(coded, other_ids, other_mask)
            coded, table = lax.optimization_barrier((coded, table))
            tables[3] = pairwise(table, opposite)
        else:
            coded = join(coded, received, rows_here << (count - 1))
        if count == 2:
            coded, table, row_out, far = lax.optimization_barrier((coded, table, row_out, far))
            tables[1] = pairwise(table, sibling)
            row_outs = [row_out, pairwise(row_out, sibling), far, pairwise(far, sibling)]
        received = pairwise(coded, lambda g, p, step=step: (g ^ step, p))
    codes = (coded, received)
    *near_scores, near_own = attend_near(tables, codes[0], own)
    row_context, far_own, live = attend_rows(near_scores, *codes, own)
    *halves_here, mixed = attend_columns_here(
        row_outs,
        live,
        row_context,
        near_own,
        far_own,
        embed,
        col_qkv.reshape(3 * local, width),
    )
    contexts = []
    for context in halves_here:
        beyond = pairwise(context, across)
        contexts.append(
            (context, pairwise(context, sibling), beyond, pairwise(beyond, sibling))
        )
    blocks = finish(contexts, mixed, col_out, groups)
    blocks = lax.all_to_all(blocks, "seq", split_axis=0, concat_axis=0, tiled=True)
    return jnp.swapaxes(order(blocks, cols, local), 1, 2)


def weight_fold(out_weight, piece):
    return jnp.einsum("rce,fe->rcf", piece, out_weight, preferred_element_type=f32)


def attend_columns(query, keys, values, key_live):
    rows_all, count_cols, local_width = query.shape
    heads_here = local_width // HEAD_DIM
    shape = (rows_all, count_cols, heads_here, HEAD_DIM)
    scores = jnp.einsum(
        "rchd,schd->chrs",
        query.reshape(shape),
        keys.reshape(shape),
        preferred_element_type=f32,
    ) * HEAD_DIM ** (-0.5)
    scores = jnp.where(key_live > 0, scores, -jnp.inf)
    probs = softmax_last(scores).astype(bf16)
    context = jnp.einsum(
        "chrs,schd->rchd", probs, values.reshape(shape), preferred_element_type=f32
    )
    return context.astype(bf16).reshape(rows_all, count_cols, local_width)


def send_back(context):
    return lax.all_to_all(context[:, None], "seq", split_axis=0, concat_axis=1, tiled=True)


def general_body(ids, pad_mask, embed, row_qkv, row_out, col_qkv, col_out):
    rows_here, cols = ids.shape
    width = embed.shape[1]
    local_width = row_out.shape[0]
    heads_here = local_width // HEAD_DIM
    groups = lax.axis_size("seq")
    per_group = cols // groups
    codes = lax.broadcasted_iota(jnp.int32, (1, 1, embed.shape[0]), 2)
    onehot = (ids[:, :, None] == codes).astype(bf16)
    embedded = jnp.einsum("rcv,vd->rcd", onehot, embed, preferred_element_type=f32)
    normed = layer_norm(embedded).astype(bf16)
    row_proj = jnp.einsum("rcd,ted->trce", normed, row_qkv, preferred_element_type=f32)
    row_proj = row_proj.astype(bf16)
    live = pad_mask.astype(bf16)
    head_shape = (rows_here, cols, heads_here, HEAD_DIM)
    query = (row_proj[0] * live[:, None, None]).reshape(head_shape)
    keys = row_proj[1].reshape(head_shape)
    values = row_proj[2].reshape(head_shape)
    partial_scores = jnp.einsum("rihd,rjhd->hij", query, keys, preferred_element_type=f32)
    count_here = jnp.sum(pad_mask.astype(f32))
    scale = HEAD_DIM ** (-0.5)
    total, count = lax.psum((partial_scores, count_here), "seq")
    row_probs = softmax_last(total * (scale / jnp.sqrt(count))).astype(bf16)
    row_context = jnp.einsum("hij,rjhd->rihd", row_probs, values, preferred_element_type=f32)
    row_context = row_context.astype(bf16).reshape(rows_here, cols, local_width)
    start_feature = lax.axis_index("head") * local_width
    resident = lax.dynamic_slice_in_dim(embedded, start_feature, local_width, 2)
    row_update = weight_fold(row_out, lax.all_gather(row_context, "head", axis=2, tiled=True))
    mixed = resident + row_update
    sums, squares = lax.psum((jnp.sum(mixed, axis=-1), jnp.sum(mixed * mixed, axis=-1)), "head")
    mean = sums / width
    spread = squares / width - mean * mean
    normed_here = ((mixed - mean[..., None]) * lax.rsqrt(spread[..., None] + EPS)).astype(bf16)
    live_tile = jnp.broadcast_to(live[:, None, None, None], (rows_here, groups, per_group, 1))
    normed_full = lax.all_gather(normed_here, "head", axis=2, tiled=True)
    col_proj = jnp.einsum("rcd,ted->rcte", normed_full, col_qkv, preferred_element_type=f32)
    packed = col_proj.astype(bf16).reshape(rows_here, groups, per_group, 3 * local_width)
    received = lax.all_to_all(packed, "seq", split_axis=1, concat_axis=0, tiled=True)
    mask_part = lax.all_to_all(live_tile, "seq", split_axis=1, concat_axis=0, tiled=True)
    column_out = send_back(
        attend_columns(
            received[:, 0, :, :local_width],
            received[:, 0, :, local_width : 2 * local_width],
            received[:, 0, :, 2 * local_width :],
            mask_part[:, 0, 0, 0],
        )
    )
    column_out = column_out.reshape(rows_here, cols, local_width)
    col_update = weight_fold(col_out, lax.all_gather(column_out, "head", axis=2, tiled=True))
    return (mixed + col_update).astype(bf16)


def body(ids, pad_mask, embed, row_qkv, row_out, col_qkv, col_out):
    rows_here, cols = ids.shape
    groups = lax.axis_size("seq")
    own, rows = cols // groups, rows_here * groups
    parts = lax.axis_size("head")
    local = row_out.shape[0]
    fits = (
        parts == 4
        and groups >= 8
        and groups & (groups - 1) == 0
        and rows * 8 == LANES
        and rows_here == 2
        and own % 32 == 0
        and cols >= LANES
        and local == LANES + HEAD_DIM
        and embed.shape[0] <= TABLE_ROWS
    )
    chosen = fast_body if fits else general_body
    return chosen(ids, pad_mask, embed, row_qkv, row_out, col_qkv, col_out)


def solution(mesh):
    placed = (
        P("seq", None),
        P("seq"),
        P(),
        P(None, "head", None),
        P("head", None),
        P(None, "head", None),
        P("head", None),
    )
    return jax.shard_map(
        body, mesh=mesh, in_specs=placed, out_specs=P("seq", None, "head"), check_vma=False
    )
```
